32 devices in a mesh: dp: 8 (over z, core), seq: 4 (over y, x).
Axes of the slice: x: 2, y: 2, z: 4, core: 2. Of those that a mesh axis runs over, the one named last changes fastest.
Arguments:
- segment: bfloat16 [24, 768, 1024], P('dp', 'seq'), may hold values from -6 to 6
- memory: bfloat16 [24, 768, 1024], P('dp', 'seq'), may hold values from -6 to 6
- compressed: bfloat16 [24, 256, 1024], P('dp', 'seq'), may hold values from -6 to 6
- eob: int32 [24, 768], P('dp'), may hold values from 0 to 1, as said below
- reset: int32 [24], P('dp'), may hold values 0 or 1
- ln1_gain: bfloat16 [1024], P('seq'), may hold values from 0.5 to 1.5
- ln1_bias: bfloat16 [1024], P('seq'), may hold values from -1 to 1
- w_query: bfloat16 [1024, 1024], P('seq'), may hold values from -0.1875 to 0.1875
- w_key: bfloat16 [1024, 1024], P('seq'), may hold values from -0.1875 to 0.1875
- w_value: bfloat16 [1024, 1024], P('seq'), may hold values from -0.1875 to 0.1875
- w_out: bfloat16 [1024, 1024], P('seq'), may hold values from -1 to 1
- out_bias: bfloat16 [1024], P('seq'), may hold values from -1.5 to 1.5
- w_rel: bfloat16 [1024, 1024], P('seq'), may hold values from -0.1875 to 0.1875
- bias_content: bfloat16 [1024], P('seq'), may hold values from -2.5 to 2.5
- bias_position: bfloat16 [1024], P('seq'), may hold values from -2.5 to 2.5
- ln2_gain: bfloat16 [1024], P('seq'), may hold values from 0.5 to 1.5
- ln2_bias: bfloat16 [1024], P('seq'), may hold values from -1 to 1
- w_up: bfloat16 [1024, 4096], P('seq'), may hold values from -0.1875 to 0.1875
- up_bias: bfloat16 [4096], P('seq'), may hold values from -2.5 to 2.5
- w_down: bfloat16 [4096, 1024], P('seq'), may hold values from -0.1875 to 0.1875
- down_bias: bfloat16 [1024], P('seq'), may hold values from -1.5 to 1.5
- conv_weight: bfloat16 [3, 1024, 1024], P(None, 'seq'), may hold values from -0.109375 to 0.109375
- conv_bias: bfloat16 [1024], P('seq'), may hold values from -1.5 to 1.5
- cotangent: bfloat16 [24, 768, 1024], P('dp', 'seq'), may hold values from -6 to 6
Outputs:
- mixed: bfloat16 [24, 768, 1024], P('dp', 'seq')
- segment_grad: float32 [24, 768, 1024], P('dp', 'seq')
- ln1_gain_grad: float32 [1024], P('seq')
- ln1_bias_grad: float32 [1024], P('seq')
- w_query_grad: float32 [1024, 1024], P('seq')
- w_key_grad: float32 [1024, 1024], P('seq')
- w_value_grad: float32 [1024, 1024], P('seq')
- w_out_grad: float32 [1024, 1024], P('seq')
- out_bias_grad: float32 [1024], P('seq')
- w_rel_grad: float32 [1024, 1024], P('seq')
- bias_content_grad: float32 [1024], P('seq')
- bias_position_grad: float32 [1024], P('seq')
- ln2_gain_grad: float32 [1024], P('seq')
- ln2_bias_grad: float32 [1024], P('seq')
- w_up_grad: float32 [1024, 4096], P('seq')
- up_bias_grad: float32 [4096], P('seq')
- w_down_grad: float32 [4096, 1024], P('seq')
- down_bias_grad: float32 [1024], P('seq')
- new_compressed: bfloat16 [24, 256, 1024], P('dp', 'seq')
The draws below stay inside these ranges and needn't reach their ends.
Inputs may be any that keep to these rules, and one draw needn't show every extreme that they name: `eob`: in each aligned block of 3 streams at least one stream has no 1.
All inputs are finite; a program needn't handle non-finite values. No bound on the sum of `reset` on one device may be relied on, other than what follows from the above.
Results may differ from the reference program's by a relative error of at most 0.02.
Values may be sent and summed in bfloat16 or wider, within the bound.
No kernel may reach another device: no remote copies, remote signals or barrier semaphores. Data moves between devices by JAX's collectives and lax.ppermute only.
A program may use at most 384 MiB of HBM per device.

```python
import math
import jax
import jax.numpy as jnp
from jax import lax

D = 1024
HEADS = 8
DH = 128
FF = 4096
SEG = 768
GROUP = 3
MEM = 768
CMEM = 256
KEYS = 1792
STREAMS = 24


def draw_eob(key, part):
    key = jax.random.fold_in(key, 11)
    first, second = jax.random.split(key)
    marks = (jax.random.randint(first, (STREAMS, SEG), 0, SEG) < 3).astype(jnp.int32)
    chosen = jax.random.randint(second, (STREAMS // GROUP,), 0, GROUP)
    spared = jnp.arange(STREAMS) % GROUP == jnp.repeat(chosen, GROUP, total_repeat_length=STREAMS)
    return jnp.where(spared[:, None], 0, marks).astype(jnp.int32)


def set_ends(array, key, smallest, largest):
    shape = array.shape
    spot = [jax.random.randint(jax.random.fold_in(key, axis), (), 0, shape[axis]) for axis in range(len(shape))]
    array = array.at[tuple(spot)].set(smallest)
    longest = shape.index(max(shape))
    spot[longest] = (spot[longest] + 1) % shape[longest]
    return array.at[tuple(spot)].set(largest)


def level_of(stream_key, shape, cuts, low, largest):
    def one(position, parts):
        heights = jax.random.uniform(jax.random.fold_in(jax.random.fold_in(stream_key, 6), position), (parts,), jnp.float32, low / len(cuts), largest / len(cuts))
        return jnp.repeat(jnp.exp(heights), shape[position] // parts).reshape((-1,) + (1,) * (len(shape) - position - 1))

    loudness = one(*cuts[0])
    for cut in cuts[1:]:
        loudness = loudness * one(*cut)
    return loudness


def gaussian(rng, dims, scale, limit, cuts=(), held_as=jnp.bfloat16):
    drawn = scale * jax.random.normal(rng, dims, jnp.float32)
    if cuts:
        drawn = drawn * level_of(rng, dims, cuts, -0.22, 0.18)
    return jnp.clip(drawn, -limit, limit).astype(held_as)


def setup_inputs(seed: int = 0) -> dict:
    seeds = jax.random.split(jax.random.key(seed), 25)
    return {
        "segment": gaussian(seeds[0], (STREAMS, SEG, D), 1.0, 6.0, ((0, 8), (1, 4))),
        "memory": gaussian(seeds[1], (STREAMS, MEM, D), 1.0, 6.0, ((0, 8), (1, 4))),
        "compressed": gaussian(seeds[2], (STREAMS, CMEM, D), 1.0, 6.0, ((0, 8), (1, 4))),
        "eob": draw_eob(jax.random.fold_in(seeds[24], 71), 0),
        "reset": set_ends((jax.random.randint(seeds[4], (STREAMS,), 0, 3) < 1).astype(jnp.int32), jax.random.fold_in(seeds[4], 1), 0, 1),
        "ln1_gain": jnp.clip(1.0 + 0.1 * jax.random.normal(seeds[5], (D,), jnp.float32), 0.5, 1.5).astype(jnp.bfloat16),
        "ln1_bias": gaussian(seeds[6], (D,), 0.2, 1.0, ((0, 4),)),
        "w_query": gaussian(seeds[7], (D, D), D ** -0.5, 0.1875, ((0, 4),)),
        "w_key": gaussian(seeds[8], (D, D), D ** -0.5, 0.1875, ((0, 4),)),
        "w_value": gaussian(seeds[9], (D, D), D ** -0.5, 0.1875, ((0, 4),)),
        "w_out": gaussian(seeds[10], (D, D), (D // 32) ** -0.5, 1.0, ((0, 4),)),
        "out_bias": gaussian(seeds[11], (D,), 0.3, 1.5, ((0, 4),)),
        "w_rel": gaussian(seeds[12], (D, D), D ** -0.5, 0.1875, ((0, 4),)),
        "bias_content": gaussian(seeds[13], (D,), 0.5, 2.5, ((0, 4),)),
        "bias_position": gaussian(seeds[14], (D,), 0.5, 2.5, ((0, 4),)),
        "ln2_gain": jnp.clip(1.0 + 0.1 * jax.random.normal(seeds[15], (D,), jnp.float32), 0.5, 1.5).astype(jnp.bfloat16),
        "ln2_bias": gaussian(seeds[16], (D,), 0.2, 1.0, ((0, 4),)),
        "w_up": gaussian(seeds[17], (D, FF), D ** -0.5, 0.1875, ((0, 4),)),
        "up_bias": gaussian(seeds[18], (FF,), 0.5, 2.5, ((0, 4),)),
        "w_down": gaussian(seeds[19], (FF, D), (FF // 4) ** -0.5, 0.1875, ((0, 4),)),
        "down_bias": gaussian(seeds[20], (D,), 0.3, 1.5, ((0, 4),)),
        "conv_weight": gaussian(seeds[21], (3, D, D), (3 * D) ** -0.5, 0.109375, ((1, 4),)),
        "conv_bias": gaussian(seeds[22], (D,), 0.3, 1.5, ((0, 4),)),
        "cotangent": gaussian(seeds[23], (STREAMS, SEG, D), 1.0, 6.0, ((0, 8), (1, 4))),
    }


@jax.custom_vjp
def low(v):
    return lax.optimization_barrier(v.astype(jnp.bfloat16)).astype(jnp.float32)

@jax.custom_vjp
def low_back(v):
    return v

def low_keep(v):
    return (low(v), None)

def low_pass(kept, grad):
    return (grad,)

def back_keep(v):
    return (v, None)

def back_low(kept, grad):
    return (low(grad),)
low.defvjp(low_keep, low_pass)
low_back.defvjp(back_keep, back_low)
EPSILON = 1e-05

def layer_norm(values, norm_gain, norm_shift):
    row_mean = lax.optimization_barrier(jnp.mean(values, axis=-1, keepdims=True))
    centred = values - row_mean
    row_var = lax.optimization_barrier(jnp.mean(centred * centred, axis=-1, keepdims=True))
    return centred * lax.rsqrt(row_var + EPSILON) * norm_gain + norm_shift

def sinusoid(table_rows, table_width):
    positions = jnp.arange(table_rows, dtype=jnp.float32)[:, None]
    half_width = table_width // 2
    frequency = jnp.exp(jnp.arange(half_width, dtype=jnp.float32) * (-2.0 * math.log(10000.0) / table_width))
    angles = positions * frequency[None, :]
    return jnp.concatenate([jnp.sin(angles), jnp.cos(angles)], axis=1)

def matmul(left, right):
    return jnp.dot(left, right, precision=lax.Precision.HIGHEST)

def gelu_exact(values):
    return jax.nn.gelu(values, approximate=False)

def split_heads(matrix):
    return matrix.reshape(matrix.shape[0], HEADS, DH).transpose(1, 0, 2)

def head_attention(content_q, position_q, head_keys, head_values, head_table, visible, distance):
    content = matmul(content_q, head_keys.T)
    positional = matmul(position_q, head_table.T)
    shifted = jnp.take_along_axis(positional, distance, axis=1)
    raw_score = low_back(content + shifted)
    scores = jnp.where(visible, raw_score * (1.0 / math.sqrt(DH)), -1e+30)
    row_top = lax.optimization_barrier(jnp.max(scores, axis=1, keepdims=True))
    weights = jnp.exp(scores - row_top)
    probability = weights / lax.optimization_barrier(jnp.sum(weights, axis=1, keepdims=True))
    return matmul(low(probability), head_values)

def stream_forward(weights, proj_table, seg_rows, old_memory, packed, eob_row, reset_flag):
    ln1_gain, ln1_bias, w_query, w_key, w_value, w_out, out_bias, w_rel, bias_content, bias_position, ln2_gain, ln2_bias, w_up, up_bias, w_down, down_bias = weights
    all_rows = jnp.concatenate([packed, old_memory, seg_rows], axis=0)
    normed = low(layer_norm(all_rows, ln1_gain, ln1_bias))
    query_rows = low_back(matmul(normed[CMEM + MEM:], w_query))
    key_rows = low_back(low(matmul(normed, w_key)))
    value_rows = low_back(low(matmul(normed, w_value)))
    content_q = low_back(low(query_rows + bias_content))
    position_q = low_back(low(query_rows + bias_position))
    book_index = jnp.cumsum(eob_row) - eob_row
    query_place = CMEM + MEM + jnp.arange(SEG, dtype=jnp.int32)
    key_place = jnp.arange(KEYS, dtype=jnp.int32)
    key_book = jnp.concatenate([jnp.zeros((CMEM + MEM,), book_index.dtype), book_index])
    in_segment = key_place >= CMEM + MEM
    visible = jnp.where(in_segment[None, :], (key_place[None, :] <= query_place[:, None]) & (key_book[None, :] == book_index[:, None]), (book_index[:, None] == 0) & (reset_flag == 0))
    distance = jnp.clip(query_place[:, None] - key_place[None, :], 0, KEYS - 1).astype(jnp.int32)

    def one_head(pieces):
        return head_attention(pieces[0], pieces[1], pieces[2], pieces[3], pieces[4], visible, distance)
    head_out = lax.map(jax.checkpoint(one_head), (split_heads(content_q), split_heads(position_q), split_heads(key_rows), split_heads(value_rows), split_heads(proj_table)))
    attended = low_back(low(head_out.transpose(1, 0, 2).reshape(SEG, D)))
    branch = low_back(matmul(attended, w_out) + out_bias)
    middle = seg_rows + branch
    normed_two = low(layer_norm(middle, ln2_gain, ln2_bias))
    pre_act = low_back(matmul(normed_two, w_up) + up_bias)
    hidden = low(gelu_exact(pre_act))
    result = low_back(matmul(hidden, w_down) + down_bias)
    return middle + result

def reference(segment, memory, compressed, eob, reset, ln1_gain, ln1_bias, w_query, w_key, w_value, w_out, out_bias, w_rel, bias_content, bias_position, ln2_gain, ln2_bias, w_up, up_bias, w_down, down_bias, conv_weight, conv_bias, cotangent):
    weights = tuple((item.astype(jnp.float32) for item in (ln1_gain, ln1_bias, w_query, w_key, w_value, w_out, out_bias, w_rel, bias_content, bias_position, ln2_gain, ln2_bias, w_up, up_bias, w_down, down_bias)))
    memories = memory.astype(jnp.float32)
    packed_all = compressed.astype(jnp.float32)

    def run(segments, params):
        proj_table = low(matmul(low(sinusoid(KEYS, D)), params[7]))

        def stream_step(carry, stream_item):
            seg_rows, old_memory, packed, eob_row, reset_flag = stream_item
            return (carry, stream_forward(params, proj_table, seg_rows, old_memory, packed, eob_row, reset_flag))
        unused, outputs = lax.scan(jax.checkpoint(stream_step), jnp.zeros((), jnp.float32), (segments, memories, packed_all, eob, reset))
        return outputs
    outputs, pull_back = jax.vjp(run, segment.astype(jnp.float32), weights)
    segment_grad, grads = pull_back(cotangent.astype(jnp.float32))
    merged = memories.reshape(STREAMS * (MEM // 3), 3 * D)
    new_compressed = (matmul(merged, conv_weight.astype(jnp.float32).reshape(3 * D, D)) + conv_bias.astype(jnp.float32)).astype(jnp.bfloat16).reshape(STREAMS, CMEM, D)
    return (outputs.astype(jnp.bfloat16), segment_grad, grads[0], grads[1], grads[2], grads[3], grads[4], grads[5], grads[6], grads[7], grads[8], grads[9], grads[10], grads[11], grads[12], grads[13], grads[14], grads[15], new_compressed)
```

```python
import functools
import math

import jax
import jax.numpy as jnp
from jax import lax
from jax.experimental import pallas as pl
from jax.experimental.pallas import tpu as pltpu
from jax.sharding import PartitionSpec as P

HEADS = 8
DH = 128
EPSILON = 1e-05
MASKED = -1e30
LANES = 128
BLOCK = 256
CHUNK = 16
SCALE = 1.0 / math.sqrt(DH)
LOG2E = 1.4426950408889634
BF16 = jnp.bfloat16
F32 = jnp.float32


def mm(left, right, dims):
    return lax.dot_general(left, right, (dims, ((), ())), preferred_element_type=F32)


NN = ((1,), (0,))
NT = ((1,), (1,))
TN = ((0,), (0,))


def lean_left(block, first_row, fill_columns):
    columns = block.shape[1] // LANES
    far = BLOCK - 1 - first_row
    whole, part = far // LANES, far % LANES
    turned = [
        pltpu.roll(
            block[:, LANES * t : LANES * (t + 1)], LANES - part, 1, stride=1, stride_axis=0
        )
        for t in range(columns)
    ]
    rows = lax.broadcasted_iota(jnp.int32, (block.shape[0], LANES), 0)
    lanes = lax.broadcasted_iota(jnp.int32, (block.shape[0], LANES), 1)
    near = lanes - rows < LANES - part
    out = []
    for t in range(fill_columns):
        a = turned[(t + whole) % columns]
        b = turned[(t + whole + 1) % columns]
        out.append(jnp.where(near, a, b))
    return jnp.concatenate(out, axis=1)


def lean_right(block, first_row):
    columns = block.shape[1] // LANES
    whole, part = first_row // LANES, first_row % LANES
    turned = [
        pltpu.roll(block[:, LANES * t : LANES * (t + 1)], part, 1, stride=1, stride_axis=0)
        for t in range(columns)
    ]
    rows = lax.broadcasted_iota(jnp.int32, (block.shape[0], LANES), 0)
    lanes = lax.broadcasted_iota(jnp.int32, (block.shape[0], LANES), 1)
    wrapped = lanes - rows < part
    out = []
    for t in range(columns):
        a = turned[(t - whole) % columns]
        b = turned[(t - whole - 1) % columns]
        out.append(jnp.where(wrapped, b, a))
    return jnp.concatenate(out, axis=1)


def flip_matrix(kind):
    rows = lax.broadcasted_iota(jnp.int32, (BLOCK, BLOCK), 0)
    lanes = lax.broadcasted_iota(jnp.int32, (BLOCK, BLOCK), 1)
    return (rows + lanes == BLOCK - 1).astype(F32).astype(kind)


def in_place_order(parts_ref, out_ref, cuts):
    parts = parts_ref.shape[0]
    low, base = 0, 0
    for size in cuts:
        for part in range(parts):
            out_ref[base + part * size : base + (part + 1) * size, :] = parts_ref[
                part, low : low + size, :
            ]
        low += size
        base += parts * size


def attend_kernel(
    cuts, q_ref, cb_ref, pb_ref, k_ref, v_ref, t_ref, info_ref,
    e_ref, inv_ref, o_ref, cq_ref, pq_ref,
    keys, values, raw, lean, mix,
):
    parts, seg, _ = q_ref.shape
    queries = parts * seg
    old = parts * (cuts[0] + cuts[1])
    in_place_order(k_ref, keys, cuts)
    in_place_order(v_ref, values, cuts)
    q = q_ref[...].reshape(queries, DH)
    content_q = (q + cb_ref[...]).astype(BF16)
    position_q = (q + pb_ref[...]).astype(BF16)
    cq_ref[...] = content_q.reshape(parts, seg, DH)
    pq_ref[...] = position_q.reshape(parts, seg, DH)
    for block in range(queries // BLOCK):
        row0 = block * BLOCK
        width = old + row0 + BLOCK
        skip = queries - BLOCK - row0
        raw[:, :width] = mm(content_q[row0 : row0 + BLOCK], keys[:width, :], NT)
        lean[:, :width] = mm(position_q[row0 : row0 + BLOCK], t_ref[skip : skip + width, :], NT)
        for chunk in range(BLOCK // CHUNK):
            r0 = chunk * CHUNK
            turned = lean_left(lean[r0 : r0 + CHUNK, :width], r0, width // LANES)
            score = raw[r0 : r0 + CHUNK, :width] + turned
            start = info_ref[row0 + r0 : row0 + r0 + CHUNK, 0:1]
            shade = info_ref[row0 + r0 : row0 + r0 + CHUNK, 1:2]
            past = score[:, :old] + shade
            place = lax.broadcasted_iota(jnp.int32, (CHUNK, row0 + BLOCK), 1)
            own = lax.broadcasted_iota(jnp.int32, (CHUNK, row0 + BLOCK), 0) + (row0 + r0)
            seen = (place <= own) & (place >= start.astype(jnp.int32))
            now = jnp.where(seen, score[:, old:], MASKED)
            top = jnp.maximum(
                jnp.max(past, axis=1, keepdims=True), jnp.max(now, axis=1, keepdims=True)
            )
            past = jnp.exp2((past - top) * (SCALE * LOG2E))
            now = jnp.exp2((now - top) * (SCALE * LOG2E))
            total = jnp.sum(past, axis=1, keepdims=True) + jnp.sum(now, axis=1, keepdims=True)
            inv = jnp.broadcast_to(1.0 / total, (CHUNK, DH))
            inv_ref[row0 + r0 : row0 + r0 + CHUNK, :] = inv
            e_ref[row0 + r0 : row0 + r0 + CHUNK, :old] = past.astype(BF16)
            e_ref[row0 + r0 : row0 + r0 + CHUNK, old:width] = now.astype(BF16)
        mix[row0 : row0 + BLOCK, :] = mm(
            e_ref[row0 : row0 + BLOCK, :width], values[:width, :], NN
        )
    o_ref[...] = (mix[...] * inv_ref[...]).astype(BF16).reshape(parts, seg, DH)


def attend(query, content_shift, position_shift, keys, values, table_rev, info, cuts):
    parts, group, seg, cols = query.shape
    rows = keys.shape[2]
    queries, key_count, heads = parts * seg, parts * rows, cols // DH
    by_head = lambda size: pl.BlockSpec((parts, None, size, DH), lambda s, h: (0, s, 0, h))
    grid_spec = pl.GridSpec(
        grid=(group, heads),
        in_specs=[
            by_head(seg),
            pl.BlockSpec((1, DH), lambda s, h: (0, h)),
            pl.BlockSpec((1, DH), lambda s, h: (0, h)),
            by_head(rows),
            by_head(rows),
            pl.BlockSpec((key_count, DH), lambda s, h: (0, h)),
            pl.BlockSpec((None, queries, LANES), lambda s, h: (s, 0, 0)),
        ],
        out_specs=[
            pl.BlockSpec((None, None, queries, key_count), lambda s, h: (s, h, 0, 0)),
            pl.BlockSpec((None, None, queries, DH), lambda s, h: (s, h, 0, 0)),
            by_head(seg),
            by_head(seg),
            by_head(seg),
        ],
        scratch_shapes=[
            pltpu.VMEM((key_count, DH), BF16),
            pltpu.VMEM((key_count, DH), BF16),
            pltpu.VMEM((BLOCK, key_count), F32),
            pltpu.VMEM((BLOCK, key_count), F32),
            pltpu.VMEM((queries, DH), F32),
        ],
    )
    small = jax.ShapeDtypeStruct((parts, group, seg, cols), BF16)
    return pl.pallas_call(
        functools.partial(attend_kernel, cuts),
        grid_spec=grid_spec,
        out_shape=[
            jax.ShapeDtypeStruct((group, heads, queries, key_count), BF16),
            jax.ShapeDtypeStruct((group, heads, queries, DH), F32),
            small,
            small,
            small,
        ],
        compiler_params=pltpu.CompilerParams(
            dimension_semantics=("arbitrary", "arbitrary"), vmem_limit_bytes=50 * 2**20
        ),
        cost_estimate=pl.CostEstimate(
            flops=6 * group * heads * queries * key_count * DH,
            bytes_accessed=2 * group * heads * queries * key_count,
            transcendentals=group * heads * queries * key_count,
        ),
        name="attend",
    )(query, content_shift, position_shift, keys, values, table_rev, info)


def pull_kernel(
    cuts, e_ref, inv_ref, o_ref, g_ref, cq_ref, pq_ref, k_ref, v_ref, t_ref,
    dq_ref, dk_ref, dv_ref, dt_ref, sums_ref,
    keys, values, grad, prob, part, score, lean, key_sum, value_sum,
):
    stream = pl.program_id(1)
    parts, seg, _ = g_ref.shape
    queries = parts * seg
    old = parts * (cuts[0] + cuts[1])
    in_place_order(k_ref, keys, cuts)
    in_place_order(v_ref, values, cuts)
    out_grad = g_ref[...].reshape(queries, DH).astype(F32)
    attended = o_ref[...].reshape(queries, DH).astype(F32)
    inv = inv_ref[...]
    grad[...] = (out_grad * inv).astype(BF16)
    dots = jnp.sum(out_grad * attended, axis=1, keepdims=True) * inv
    content_q = cq_ref[...].reshape(queries, DH)
    position_q = pq_ref[...].reshape(queries, DH)

    @pl.when(stream == 0)
    def _():
        dt_ref[...] = jnp.zeros_like(dt_ref)
        sums_ref[...] = jnp.zeros_like(sums_ref)

    key_sum[...] = jnp.zeros_like(key_sum)
    value_sum[...] = jnp.zeros_like(value_sum)
    content_total = jnp.zeros((1, DH), F32)
    position_total = jnp.zeros((1, DH), F32)
    query_total = jnp.zeros((1, DH), F32)
    flip = flip_matrix(BF16)
    flip_wide = flip_matrix(F32)
    turn = lambda rows: mm(flip, rows, NN).astype(BF16)
    for block in range(queries // BLOCK):
        row0 = block * BLOCK
        width = old + row0 + BLOCK
        skip = queries - BLOCK - row0
        rows = slice(row0, row0 + BLOCK)
        dots_back = lax.dot_general(
            flip_wide,
            jnp.broadcast_to(dots[rows], (BLOCK, DH)),
            (NN, ((), ())),
            precision=lax.Precision.HIGHEST,
            preferred_element_type=F32,
        )
        content_back = turn(content_q[rows])
        position_back = turn(position_q[rows])
        prob[:, :width] = mm(turn(grad[rows, :]), values[:width, :], NT)
        part[:, :width] = mm(flip, e_ref[rows, :width], NN)
        value_sum[:, :width] += mm(grad[rows, :], e_ref[rows, :width], TN)
        for chunk in range(BLOCK // CHUNK):
            r0 = chunk * CHUNK
            mean = dots_back[r0 : r0 + CHUNK, 0:1]
            change = part[r0 : r0 + CHUNK, :width] * (prob[r0 : r0 + CHUNK, :width] - mean)
            score[r0 : r0 + CHUNK, :width] = change.astype(BF16)
            lean[r0 : r0 + CHUNK, :width] = lean_right(change, r0).astype(BF16)
        content_grad = (mm(score[:, :width], keys[:width, :], NN) * SCALE).astype(BF16).astype(F32)
        position_grad = (
            (mm(lean[:, :width], t_ref[skip : skip + width, :], NN) * SCALE)
            .astype(BF16)
            .astype(F32)
        )
        query_grad = turn((content_grad + position_grad).astype(BF16))
        content_total += jnp.sum(content_grad, axis=0, keepdims=True)
        position_total += jnp.sum(position_grad, axis=0, keepdims=True)
        query_total += jnp.sum(query_grad.astype(F32), axis=0, keepdims=True)
        low = row0
        while low < row0 + BLOCK:
            part_at, part_row = low // seg, low % seg
            size = min(seg - part_row, row0 + BLOCK - low)
            dq_ref[part_at, part_row : part_row + size, :] = query_grad[
                low - row0 : low - row0 + size
            ]
            low += size
        key_sum[:, :width] += mm(content_back, score[:, :width], TN)
        dt_ref[:, skip : skip + width] += mm(position_back, lean[:, :width], TN) * SCALE
    key_rows = (key_sum[...] * SCALE).T.astype(BF16)
    value_rows = value_sum[...].T.astype(BF16)
    low, base = 0, 0
    for size in cuts:
        for at in range(parts):
            span = slice(base + at * size, base + (at + 1) * size)
            dk_ref[at, low : low + size, :] = key_rows[span]
            dv_ref[at, low : low + size, :] = value_rows[span]
        low += size
        base += parts * size
    key_total = jnp.sum(key_rows.astype(F32), axis=0, keepdims=True)
    value_total = jnp.sum(value_rows.astype(F32), axis=0, keepdims=True)
    sums_ref[...] += jnp.concatenate(
        [
            content_total,
            position_total,
            query_total,
            key_total,
            value_total,
            jnp.zeros((3, DH), F32),
        ],
        axis=0,
    )


def pull(weights, inverse, attended, out_grad, content_q, position_q, keys, values, table_rev, cuts):
    parts, group, seg, cols = out_grad.shape
    rows = keys.shape[2]
    queries, key_count, heads = parts * seg, parts * rows, cols // DH
    by_head = lambda size: pl.BlockSpec((parts, None, size, DH), lambda h, s: (0, s, 0, h))
    grid_spec = pl.GridSpec(
        grid=(heads, group),
        in_specs=[
            pl.BlockSpec((None, None, queries, key_count), lambda h, s: (s, h, 0, 0)),
            pl.BlockSpec((None, None, queries, DH), lambda h, s: (s, h, 0, 0)),
            by_head(seg),
            by_head(seg),
            by_head(seg),
            by_head(seg),
            by_head(rows),
            by_head(rows),
            pl.BlockSpec((key_count, DH), lambda h, s: (0, h)),
        ],
        out_specs=[
            by_head(seg),
            by_head(rows),
            by_head(rows),
            pl.BlockSpec((None, DH, key_count), lambda h, s: (h, 0, 0)),
            pl.BlockSpec((None, 8, DH), lambda h, s: (h, 0, 0)),
        ],
        scratch_shapes=[
            pltpu.VMEM((key_count, DH), BF16),
            pltpu.VMEM((key_count, DH), BF16),
            pltpu.VMEM((queries, DH), BF16),
            pltpu.VMEM((BLOCK, key_count), F32),
            pltpu.VMEM((BLOCK, key_count), F32),
            pltpu.VMEM((BLOCK, key_count), BF16),
            pltpu.VMEM((BLOCK, key_count), BF16),
            pltpu.VMEM((DH, key_count), F32),
            pltpu.VMEM((DH, key_count), F32),
        ],
    )
    return pl.pallas_call(
        functools.partial(pull_kernel, cuts),
        grid_spec=grid_spec,
        out_shape=[
            jax.ShapeDtypeStruct((parts, group, seg, cols), BF16),
            jax.ShapeDtypeStruct((parts, group, rows, cols), BF16),
            jax.ShapeDtypeStruct((parts, group, rows, cols), BF16),
            jax.ShapeDtypeStruct((heads, DH, key_count), F32),
            jax.ShapeDtypeStruct((heads, 8, DH), F32),
        ],
        compiler_params=pltpu.CompilerParams(
            dimension_semantics=("arbitrary", "arbitrary"), vmem_limit_bytes=50 * 2**20
        ),
        cost_estimate=pl.CostEstimate(
            flops=12 * group * heads * queries * key_count * DH,
            bytes_accessed=2 * group * heads * queries * key_count,
            transcendentals=0,
        ),
        name="pull",
    )(weights, inverse, attended, out_grad, content_q, position_q, keys, values, table_rev)


def standardise(rows):
    mean = jnp.mean(rows, axis=-1, keepdims=True)
    centred = rows - mean
    rate = lax.rsqrt(jnp.mean(centred * centred, axis=-1, keepdims=True) + EPSILON)
    return centred * rate, rate


def standardise_back(unit, rate, grad, gain):
    scaled = grad * gain
    mean = jnp.mean(scaled, axis=-1, keepdims=True)
    along = jnp.mean(scaled * unit, axis=-1, keepdims=True)
    return rate * (scaled - mean - unit * along)


def sinusoid_reversed(rows, width):
    positions = (rows - 1 - jnp.arange(rows, dtype=jnp.int32)).astype(F32)[:, None]
    frequency = jnp.exp(
        jnp.arange(width // 2, dtype=F32) * (-2.0 * math.log(10000.0) / width)
    )
    angles = positions * frequency[None, :]
    return jnp.concatenate([jnp.sin(angles), jnp.cos(angles)], axis=1).astype(BF16)


def dot(left, right):
    return mm(left, right, NN)


def swap(value):
    return lax.ppermute(value, "core", [(0, 1), (1, 0)])


def body(
    segment, memory, compressed, eob, reset, ln1_gain, ln1_bias, w_query, w_key, w_value,
    w_out, out_bias, w_rel, bias_content, bias_position, ln2_gain, ln2_bias, w_up, up_bias,
    w_down, down_bias, conv_weight, conv_bias, cotangent,
):
    parts = lax.axis_size("seq")
    core = lax.axis_index("core")
    group, seg, width = segment.shape
    mem, old = memory.shape[1], compressed.shape[1]
    cuts = (old, mem, seg)
    each = old + mem + seg
    keys_in_all = parts * each
    cols = width // parts
    own = group * seg
    units = w_up.shape[1] // 2
    unit_shard = units // parts

    rows_all = lax.all_gather(jnp.concatenate([compressed, memory, segment], axis=1), "seq")
    square = jnp.stack([w_query, w_key, w_value, w_rel, conv_weight[0], conv_weight[1], conv_weight[2]])
    count = square.shape[0]
    sent = square.reshape(count, cols, parts, cols).transpose(2, 1, 0, 3)
    sent = sent.reshape(parts, cols, count * cols)
    columns = lax.all_to_all(sent, "seq", 0, 0, tiled=True).reshape(width, count * cols)
    up_bias_half = lax.dynamic_slice_in_dim(up_bias, core * unit_shard, unit_shard, 0)
    vectors = jnp.concatenate(
        [ln1_gain, ln1_bias, out_bias, ln2_gain, ln2_bias, down_bias, up_bias_half]
    )
    vectors = lax.all_gather(vectors, "seq").astype(F32)
    gain_one, shift_one, out_shift, gain_two, shift_two, down_shift = (
        vectors[:, cols * i : cols * (i + 1)].reshape(width) for i in range(6)
    )
    up_shift = vectors[:, 6 * cols :].reshape(units)
    up_half = lax.dynamic_slice_in_dim(
        w_up.reshape(cols, parts, 2, unit_shard), core, 1, 2
    ).reshape(cols, 2, width)
    down_half = lax.dynamic_slice_in_dim(w_down, core * unit_shard, unit_shard, 0)
    wide = jnp.concatenate([up_half[:, 0], up_half[:, 1], down_half, w_out], axis=0)
    wide, rows_all = lax.optimization_barrier((wide, rows_all))
    wide = lax.all_gather(wide, "seq")
    up_cols = [wide[:, cols * i : cols * (i + 1)].reshape(width, width) for i in range(2)]
    down_rows = wide[:, 2 * cols : 2 * cols + unit_shard].reshape(units, width)
    out_full = wide[:, 2 * cols + unit_shard :].reshape(width, width)
    cot_own = cotangent.reshape(own, width)
    cot_both = jnp.concatenate([cot_own, swap(cot_own)], axis=0)

    table_rev = sinusoid_reversed(keys_in_all, width)
    proj_rev = dot(table_rev, columns[:, 3 * cols : 4 * cols]).astype(BF16)
    index = jnp.arange(eob.shape[1], dtype=jnp.int32)[None, :]
    first = jnp.pad(eob, ((0, 0), (1, 0)))[:, :-1] == 1
    start = lax.cummax(jnp.where(first, index, 0), axis=1)
    shade = jnp.where((start == 0) & (reset[:, None] == 0), 0.0, MASKED)
    info = jnp.stack([start.astype(F32), shade], axis=2)
    info = jnp.pad(info, ((0, 0), (0, 0), (0, LANES - 2)))

    unit_all, _ = standardise(rows_all.reshape(parts * group * each, width).astype(F32))
    normed = (unit_all * gain_one + shift_one).astype(BF16)
    normed_seg = normed.reshape(parts, group, each, width)[:, :, old + mem :]
    normed_seg = normed_seg.reshape(parts * own, width)
    query = dot(normed_seg, columns[:, :cols]).reshape(parts, group, seg, cols)
    keys = dot(normed, columns[:, cols : 2 * cols]).astype(BF16)
    values = dot(normed, columns[:, 2 * cols : 3 * cols]).astype(BF16)
    keys = keys.reshape(parts, group, each, cols)
    values = values.reshape(parts, group, each, cols)
    weights, inverse, mixed_heads, content_q, position_q = attend(
        query,
        bias_content.astype(F32).reshape(1, cols),
        bias_position.astype(F32).reshape(1, cols),
        keys,
        values,
        proj_rev,
        info,
        cuts,
    )
    attended = lax.all_to_all(mixed_heads, "seq", 0, 0, tiled=True)
    attended = attended.transpose(1, 2, 0, 3).reshape(own, width)

    merged = rows_all[:, :, old : old + mem].reshape(parts * group * mem // 3, 3 * width)
    conv_cols = columns[:, 4 * cols :].reshape(width, 3, cols).transpose(1, 0, 2)
    packed = dot(merged, conv_cols.reshape(3 * width, cols)) + conv_bias.astype(F32)
    packed = packed.astype(BF16).reshape(parts, group, mem // 3, cols)
    packed = lax.all_to_all(packed, "seq", 0, 0, tiled=True)
    new_compressed = packed.transpose(1, 2, 0, 3).reshape(group, mem // 3, width)

    segment_own = segment.reshape(own, width).astype(F32)
    middle = segment_own + (dot(attended, out_full) + out_shift)
    unit_two, rate_two = standardise(middle)
    normed_two = (unit_two * gain_two + shift_two).astype(BF16)
    both = jnp.concatenate([normed_two, swap(normed_two)], axis=0)
    hidden, act_grad, up_grads = [], [], []
    for i in range(2):
        down_part = down_rows[i * width : (i + 1) * width]
        pre = dot(both, up_cols[i]) + up_shift[i * width : (i + 1) * width]
        below = 0.5 * (1.0 + lax.erf(pre * math.sqrt(0.5)))
        slope = below + pre * (jnp.exp(-0.5 * pre * pre) * (1.0 / math.sqrt(2.0 * math.pi)))
        hidden.append((pre * below).astype(BF16))
        act_grad.append((slope * mm(cot_both, down_part, NT)).astype(BF16))
        up_grads.append(mm(both, act_grad[i], TN).astype(BF16))
    hidden = jnp.concatenate(hidden, axis=1)
    part = dot(hidden, down_rows)
    result = part[:own] + swap(part[own:].astype(BF16)).astype(F32) + down_shift
    output = (middle + result).astype(BF16).reshape(group, seg, width)
    down_grad = mm(hidden, cot_both, TN).astype(BF16)
    part = mm(act_grad[0], up_cols[0], NT) + mm(act_grad[1], up_cols[1], NT)
    normed_two_grad = part[:own] + swap(part[own:].astype(BF16)).astype(F32)
    up_shift_grad = jnp.concatenate([jnp.sum(a.astype(F32), axis=0) for a in act_grad])

    cot_wide = cot_own.astype(F32)
    gain_two_grad = jnp.sum(normed_two_grad * unit_two, axis=0)
    shift_two_grad = jnp.sum(normed_two_grad, axis=0)
    middle_grad = cot_wide + standardise_back(unit_two, rate_two, normed_two_grad, gain_two)
    branch_grad = middle_grad.astype(BF16)
    attended_grad = mm(branch_grad, out_full, NT).astype(BF16)
    attended_grad = attended_grad.reshape(group, seg, parts, cols).transpose(2, 0, 1, 3)
    head_grad = lax.all_to_all(attended_grad, "seq", 0, 0, tiled=True)
    out_grad = mm(attended, branch_grad, TN).astype(BF16)
    down_shift_grad = jnp.sum(cot_wide, axis=0)
    out_shift_grad = jnp.sum(branch_grad.astype(F32), axis=0)
    shifts = jnp.stack([out_shift_grad, gain_two_grad, shift_two_grad, down_shift_grad])
    shifts = shifts.reshape(4, parts, cols).transpose(1, 0, 2).reshape(parts, 1, 4 * cols)
    shifts = jnp.pad(shifts, ((0, 0), (0, 0), (0, width - 4 * cols)))
    unit_row = up_shift_grad.reshape(parts, 1, unit_shard)
    unit_row = jnp.pad(unit_row, ((0, 0), (0, 0), (0, width - unit_shard)))
    shifts = jnp.concatenate([unit_row, shifts], axis=1).astype(BF16)
    shifts = jnp.pad(shifts, ((0, 0), (0, 62), (0, 0)))
    block = lambda grad: grad.reshape(parts, grad.shape[0] // parts, width)
    late = jnp.concatenate(
        [block(up_grads[0]), block(up_grads[1]), block(down_grad), block(out_grad), shifts], axis=1
    )
    late = lax.psum_scatter(
        late.reshape(-1, width), "seq", scatter_dimension=0, tiled=True
    )
    ff_rows = 2 * cols + unit_shard
    ff_own = lax.psum(late[:ff_rows], "z")
    ff_other = swap(ff_own)
    unit_sum = lax.psum(late[ff_rows + cols, :unit_shard], "z")

    query_grad, key_grad, value_grad, table_grad, sums = pull(
        weights, inverse, mixed_heads, head_grad, content_q, position_q, keys, values, proj_rev, cuts
    )
    seg_grads = jnp.concatenate(
        [query_grad, key_grad[:, :, old + mem :], value_grad[:, :, old + mem :]], axis=3
    )
    seg_part = mm(seg_grads.reshape(parts * own, 3 * cols), columns[:, : 3 * cols], NT)
    seg_grad = lax.psum_scatter(
        seg_part.astype(BF16), "seq", scatter_dimension=0, tiled=True
    ).astype(F32)
    unit_seg, rate_seg = standardise(segment_own)
    rows_grad = standardise_back(unit_seg, rate_seg, seg_grad, gain_one)
    segment_grad = (middle_grad + rows_grad).reshape(group, seg, width)

    query_w = mm(normed_seg, query_grad.reshape(parts * own, cols), TN)
    key_w = mm(normed, key_grad.reshape(parts * group * each, cols), TN)
    value_w = mm(normed, value_grad.reshape(parts * group * each, cols), TN)
    rel_w = mm(table_rev, table_grad.reshape(cols, keys_in_all).astype(BF16), ((0,), (1,)))
    sums = sums.transpose(1, 0, 2).reshape(8, cols)
    weight_cols = columns[:, : 3 * cols].astype(F32)
    row_sums = sums[2:5].reshape(1, 3 * cols)
    three = jnp.concatenate([query_w, key_w, value_w], axis=1)
    shift_one_grad = jnp.sum(weight_cols * row_sums, axis=1)
    gain_one_grad = jnp.sum(weight_cols * (three - shift_one[:, None] * row_sums), axis=1) / gain_one
    ones = jnp.stack([gain_one_grad, shift_one_grad], axis=0)
    ones = ones.reshape(2, parts, cols).transpose(1, 0, 2).reshape(parts, 1, 2 * cols)
    ones = jnp.pad(ones.astype(BF16), ((0, 0), (0, 15), (0, 2 * cols)))
    square_grads = jnp.concatenate([three.astype(BF16), rel_w.astype(BF16)], axis=1)
    square_grads = jnp.concatenate(
        [square_grads.reshape(parts, cols, 4 * cols), ones], axis=1
    )
    got = lax.all_to_all(square_grads, "seq", 0, 0, tiled=True)
    squares = got[:, :cols].reshape(parts, cols, 4, cols).transpose(2, 1, 0, 3)
    squares = squares.reshape(4 * cols, width)
    ones = jnp.sum(got[:, cols : cols + 1].astype(F32), axis=0)
    ones = jnp.pad(ones, ((0, 0), (0, width - 4 * cols)))
    heads_row = jnp.pad(sums[:2].reshape(1, 2 * cols), ((0, 0), (0, width - 2 * cols)))
    rows = jnp.concatenate([ones, heads_row], axis=0).astype(BF16)
    rows = jnp.pad(rows, ((0, 14), (0, 0)))
    rest = jnp.concatenate([late[ff_rows:], squares, rows], axis=0)
    rest = lax.psum(rest, ("z", "core")).astype(F32)

    out_w = rest[:cols]
    shift_row = rest[cols + 1]
    base = cols + 64
    query_w, key_w, value_w, rel_w = (
        rest[base + cols * i : base + cols * (i + 1)] for i in range(4)
    )
    base += 4 * cols
    both_halves = lambda mine, other: (
        jnp.where(core == 0, mine, other),
        jnp.where(core == 0, other, mine),
    )
    ff = both_halves(ff_own, ff_other)
    up_w = jnp.stack(
        [
            jnp.concatenate([half[:cols], half[cols : 2 * cols]], axis=1).reshape(
                cols, parts, unit_shard
            )
            for half in ff
        ],
        axis=2,
    )
    up_w = up_w.reshape(cols, 2 * units).astype(F32)
    down_w = jnp.concatenate([half[2 * cols :] for half in ff], axis=0).astype(F32)
    unit_w = jnp.concatenate(both_halves(unit_sum, swap(unit_sum))).astype(F32)
    piece = lambda row, i: row[cols * i : cols * (i + 1)]
    return (
        output,
        segment_grad,
        piece(rest[base], 0),
        piece(rest[base], 1),
        query_w,
        key_w,
        value_w,
        out_w,
        piece(shift_row, 0),
        rel_w,
        piece(rest[base + 1], 0),
        piece(rest[base + 1], 1),
        piece(shift_row, 1),
        piece(shift_row, 2),
        up_w,
        unit_w,
        down_w,
        piece(shift_row, 3),
        new_compressed,
    )


def solution(mesh):
    dp = mesh.shape["dp"]
    cores = jax.sharding.Mesh(
        mesh.devices.reshape(dp // 2, 2, mesh.shape["seq"]), ("z", "core", "seq")
    )
    rows = P(("z", "core"), "seq", None)
    shard, matrix = P("seq"), P("seq", None)
    return jax.shard_map(
        body,
        mesh=cores,
        in_specs=(
            rows, rows, rows, P(("z", "core"), None), P(("z", "core")), shard, shard, matrix,
            matrix, matrix, matrix, shard, matrix, shard, shard, shard, shard, matrix, shard,
            matrix, shard, P(None, "seq", None), shard, rows,
        ),
        out_specs=(
            rows, rows, shard, shard, matrix, matrix, matrix, matrix, shard, matrix, shard,
            shard, shard, shard, matrix, shard, matrix, shard, rows,
        ),
        check_vma=False,
    )
```

```python
import functools
import math

import jax
import jax.numpy as jnp
from jax import lax
from jax.experimental import pallas as pl
from jax.experimental.pallas import tpu as pltpu
from jax.sharding import PartitionSpec as P

HEADS = 8
DH = 128
EPSILON = 1e-05
MASKED = -1e30
LANES = 128
BLOCK = 256
CHUNK = 16
SCALE = 1.0 / math.sqrt(DH)
LOG2E = 1.4426950408889634
BF16 = jnp.bfloat16
F32 = jnp.float32


def mm(left, right, dims):
    return lax.dot_general(left, right, (dims, ((), ())), preferred_element_type=F32)


NN = ((1,), (0,))
NT = ((1,), (1,))
TN = ((0,), (0,))


def lean_left(block, first_row, fill_columns):
    columns = block.shape[1] // LANES
    far = BLOCK - 1 - first_row
    whole, part = far // LANES, far % LANES
    turned = [
        pltpu.roll(
            block[:, LANES * t : LANES * (t + 1)], LANES - part, 1, stride=1, stride_axis=0
        )
        for t in range(columns)
    ]
    rows = lax.broadcasted_iota(jnp.int32, (block.shape[0], LANES), 0)
    lanes = lax.broadcasted_iota(jnp.int32, (block.shape[0], LANES), 1)
    near = lanes - rows < LANES - part
    out = []
    for t in range(fill_columns):
        a = turned[(t + whole) % columns]
        b = turned[(t + whole + 1) % columns]
        out.append(jnp.where(near, a, b))
    return jnp.concatenate(out, axis=1)


def lean_right(block, first_row):
    columns = block.shape[1] // LANES
    whole, part = first_row // LANES, first_row % LANES
    turned = [
        pltpu.roll(block[:, LANES * t : LANES * (t + 1)], part, 1, stride=1, stride_axis=0)
        for t in range(columns)
    ]
    rows = lax.broadcasted_iota(jnp.int32, (block.shape[0], LANES), 0)
    lanes = lax.broadcasted_iota(jnp.int32, (block.shape[0], LANES), 1)
    wrapped = lanes - rows < part
    out = []
    for t in range(columns):
        a = turned[(t - whole) % columns]
        b = turned[(t - whole - 1) % columns]
        out.append(jnp.where(wrapped, b, a))
    return jnp.concatenate(out, axis=1)


def flip_matrix(kind):
    rows = lax.broadcasted_iota(jnp.int32, (BLOCK, BLOCK), 0)
    lanes = lax.broadcasted_iota(jnp.int32, (BLOCK, BLOCK), 1)
    return (rows + lanes == BLOCK - 1).astype(F32).astype(kind)


def in_place_order(parts_ref, out_ref, cuts):
    parts = parts_ref.shape[0]
    low, base = 0, 0
    for size in cuts:
        for part in range(parts):
            out_ref[base + part * size : base + (part + 1) * size, :] = parts_ref[
                part, low : low + size, :
            ]
        low += size
        base += parts * size


def attend_kernel(
    cuts, q_ref, cb_ref, pb_ref, k_ref, v_ref, t_ref, info_ref,
    e_ref, inv_ref, o_ref, cq_ref, pq_ref,
    keys, values, raw, lean, mix,
):
    parts, seg, _ = q_ref.shape
    queries = parts * seg
    old = parts * (cuts[0] + cuts[1])
    in_place_order(k_ref, keys, cuts)
    in_place_order(v_ref, values, cuts)
    q = q_ref[...].reshape(queries, DH)
    content_q = (q + cb_ref[...]).astype(BF16)
    position_q = (q + pb_ref[...]).astype(BF16)
    cq_ref[...] = content_q.reshape(parts, seg, DH)
    pq_ref[...] = position_q.reshape(parts, seg, DH)
    for block in range(queries // BLOCK):
        row0 = block * BLOCK
        width = old + row0 + BLOCK
        skip = queries - BLOCK - row0
        raw[:, :width] = mm(content_q[row0 : row0 + BLOCK], keys[:width, :], NT)
        lean[:, :width] = mm(position_q[row0 : row0 + BLOCK], t_ref[skip : skip + width, :], NT)
        for chunk in range(BLOCK // CHUNK):
            r0 = chunk * CHUNK
            turned = lean_left(lean[r0 : r0 + CHUNK, :width], r0, width // LANES)
            score = raw[r0 : r0 + CHUNK, :width] + turned
            start = info_ref[row0 + r0 : row0 + r0 + CHUNK, 0:1]
            shade = info_ref[row0 + r0 : row0 + r0 + CHUNK, 1:2]
            past = score[:, :old] + shade
            place = lax.broadcasted_iota(jnp.int32, (CHUNK, row0 + BLOCK), 1)
            own = lax.broadcasted_iota(jnp.int32, (CHUNK, row0 + BLOCK), 0) + (row0 + r0)
            seen = (place <= own) & (place >= start.astype(jnp.int32))
            now = jnp.where(seen, score[:, old:], MASKED)
            top = jnp.maximum(
                jnp.max(past, axis=1, keepdims=True), jnp.max(now, axis=1, keepdims=True)
            )
            past = jnp.exp2((past - top) * (SCALE * LOG2E))
            now = jnp.exp2((now - top) * (SCALE * LOG2E))
            total = jnp.sum(past, axis=1, keepdims=True) + jnp.sum(now, axis=1, keepdims=True)
            inv = jnp.broadcast_to(1.0 / total, (CHUNK, DH))
            inv_ref[row0 + r0 : row0 + r0 + CHUNK, :] = inv
            e_ref[row0 + r0 : row0 + r0 + CHUNK, :old] = past.astype(BF16)
            e_ref[row0 + r0 : row0 + r0 + CHUNK, old:width] = now.astype(BF16)
        mix[row0 : row0 + BLOCK, :] = mm(
            e_ref[row0 : row0 + BLOCK, :width], values[:width, :], NN
        )
    o_ref[...] = (mix[...] * inv_ref[...]).astype(BF16).reshape(parts, seg, DH)


def attend(query, content_shift, position_shift, keys, values, table_rev, info, cuts):
    parts, group, seg, cols = query.shape
    rows = keys.shape[2]
    queries, key_count, heads = parts * seg, parts * rows, cols // DH
    by_head = lambda size: pl.BlockSpec((parts, None, size, DH), lambda s, h: (0, s, 0, h))
    grid_spec = pl.GridSpec(
        grid=(group, heads),
        in_specs=[
            by_head(seg),
            pl.BlockSpec((1, DH), lambda s, h: (0, h)),
            pl.BlockSpec((1, DH), lambda s, h: (0, h)),
            by_head(rows),
            by_head(rows),
            pl.BlockSpec((key_count, DH), lambda s, h: (0, h)),
            pl.BlockSpec((None, queries, LANES), lambda s, h: (s, 0, 0)),
        ],
        out_specs=[
            pl.BlockSpec((None, None, queries, key_count), lambda s, h: (s, h, 0, 0)),
            pl.BlockSpec((None, None, queries, DH), lambda s, h: (s, h, 0, 0)),
            by_head(seg),
            by_head(seg),
            by_head(seg),
        ],
        scratch_shapes=[
            pltpu.VMEM((key_count, DH), BF16),
            pltpu.VMEM((key_count, DH), BF16),
            pltpu.VMEM((BLOCK, key_count), F32),
            pltpu.VMEM((BLOCK, key_count), F32),
            pltpu.VMEM((queries, DH), F32),
        ],
    )
    small = jax.ShapeDtypeStruct((parts, group, seg, cols), BF16)
    return pl.pallas_call(
        functools.partial(attend_kernel, cuts),
        grid_spec=grid_spec,
        out_shape=[
            jax.ShapeDtypeStruct((group, heads, queries, key_count), BF16),
            jax.ShapeDtypeStruct((group, heads, queries, DH), F32),
            small,
            small,
            small,
        ],
        compiler_params=pltpu.CompilerParams(
            dimension_semantics=("arbitrary", "arbitrary"), vmem_limit_bytes=50 * 2**20
        ),
        cost_estimate=pl.CostEstimate(
            flops=6 * group * heads * queries * key_count * DH,
            bytes_accessed=2 * group * heads * queries * key_count,
            transcendentals=group * heads * queries * key_count,
        ),
        name="attend",
    )(query, content_shift, position_shift, keys, values, table_rev, info)


def pull_kernel(
    cuts, e_ref, inv_ref, o_ref, g_ref, cq_ref, pq_ref, k_ref, v_ref, t_ref,
    dq_ref, dk_ref, dv_ref, dt_ref, sums_ref,
    keys, values, grad, prob, part, score, lean, key_sum, value_sum,
):
    stream = pl.program_id(1)
    parts, seg, _ = g_ref.shape
    queries = parts * seg
    old = parts * (cuts[0] + cuts[1])
    in_place_order(k_ref, keys, cuts)
    in_place_order(v_ref, values, cuts)
    out_grad = g_ref[...].reshape(queries, DH).astype(F32)
    attended = o_ref[...].reshape(queries, DH).astype(F32)
    inv = inv_ref[...]
    grad[...] = (out_grad * inv).astype(BF16)
    dots = jnp.sum(out_grad * attended, axis=1, keepdims=True) * inv
    content_q = cq_ref[...].reshape(queries, DH)
    position_q = pq_ref[...].reshape(queries, DH)

    @pl.when(stream == 0)
    def _():
        dt_ref[...] = jnp.zeros_like(dt_ref)
        sums_ref[...] = jnp.zeros_like(sums_ref)

    key_sum[...] = jnp.zeros_like(key_sum)
    value_sum[...] = jnp.zeros_like(value_sum)
    content_total = jnp.zeros((1, DH), F32)
    position_total = jnp.zeros((1, DH), F32)
    query_total = jnp.zeros((1, DH), F32)
    flip = flip_matrix(BF16)
    flip_wide = flip_matrix(F32)
    turn = lambda rows: mm(flip, rows, NN).astype(BF16)
    for block in range(queries // BLOCK):
        row0 = block * BLOCK
        width = old + row0 + BLOCK
        skip = queries - BLOCK - row0
        rows = slice(row0, row0 + BLOCK)
        dots_back = lax.dot_general(
            flip_wide,
            jnp.broadcast_to(dots[rows], (BLOCK, DH)),
            (NN, ((), ())),
            precision=lax.Precision.HIGHEST,
            preferred_element_type=F32,
        )
        content_back = turn(content_q[rows])
        position_back = turn(position_q[rows])
        prob[:, :width] = mm(turn(grad[rows, :]), values[:width, :], NT)
        part[:, :width] = mm(flip, e_ref[rows, :width], NN)
        value_sum[:, :width] += mm(grad[rows, :], e_ref[rows, :width], TN)
        for chunk in range(BLOCK // CHUNK):
            r0 = chunk * CHUNK
            mean = dots_back[r0 : r0 + CHUNK, 0:1]
            change = part[r0 : r0 + CHUNK, :width] * (prob[r0 : r0 + CHUNK, :width] - mean)
            score[r0 : r0 + CHUNK, :width] = change.astype(BF16)
            lean[r0 : r0 + CHUNK, :width] = lean_right(change, r0).astype(BF16)
        content_grad = (mm(score[:, :width], keys[:width, :], NN) * SCALE).astype(BF16).astype(F32)
        position_grad = (
            (mm(lean[:, :width], t_ref[skip : skip + width, :], NN) * SCALE)
            .astype(BF16)
            .astype(F32)
        )
        query_grad = turn((content_grad + position_grad).astype(BF16))
        content_total += jnp.sum(content_grad, axis=0, keepdims=True)
        position_total += jnp.sum(position_grad, axis=0, keepdims=True)
        query_total += jnp.sum(query_grad.astype(F32), axis=0, keepdims=True)
        low = row0
        while low < row0 + BLOCK:
            part_at, part_row = low // seg, low % seg
            size = min(seg - part_row, row0 + BLOCK - low)
            dq_ref[part_at, part_row : part_row + size, :] = query_grad[
                low - row0 : low - row0 + size
            ]
            low += size
        key_sum[:, :width] += mm(content_back, score[:, :width], TN)
        dt_ref[:, skip : skip + width] += mm(position_back, lean[:, :width], TN) * SCALE
    key_rows = (key_sum[...] * SCALE).T.astype(BF16)
    value_rows = value_sum[...].T.astype(BF16)
    low, base = 0, 0
    for size in cuts:
        for at in range(parts):
            span = slice(base + at * size, base + (at + 1) * size)
            dk_ref[at, low : low + size, :] = key_rows[span]
            dv_ref[at, low : low + size, :] = value_rows[span]
        low += size
        base += parts * size
    key_total = jnp.sum(key_rows.astype(F32), axis=0, keepdims=True)
    value_total = jnp.sum(value_rows.astype(F32), axis=0, keepdims=True)
    sums_ref[...] += jnp.concatenate(
        [
            content_total,
            position_total,
            query_total,
            key_total,
            value_total,
            jnp.zeros((3, DH), F32),
        ],
        axis=0,
    )


def pull(weights, inverse, attended, out_grad, content_q, position_q, keys, values, table_rev, cuts):
    parts, group, seg, cols = out_grad.shape
    rows = keys.shape[2]
    queries, key_count, heads = parts * seg, parts * rows, cols // DH
    by_head = lambda size: pl.BlockSpec((parts, None, size, DH), lambda h, s: (0, s, 0, h))
    grid_spec = pl.GridSpec(
        grid=(heads, group),
        in_specs=[
            pl.BlockSpec((None, None, queries, key_count), lambda h, s: (s, h, 0, 0)),
            pl.BlockSpec((None, None, queries, DH), lambda h, s: (s, h, 0, 0)),
            by_head(seg),
            by_head(seg),
            by_head(seg),
            by_head(seg),
            by_head(rows),
            by_head(rows),
            pl.BlockSpec((key_count, DH), lambda h, s: (0, h)),
        ],
        out_specs=[
            by_head(seg),
            by_head(rows),
            by_head(rows),
            pl.BlockSpec((None, DH, key_count), lambda h, s: (h, 0, 0)),
            pl.BlockSpec((None, 8, DH), lambda h, s: (h, 0, 0)),
        ],
        scratch_shapes=[
            pltpu.VMEM((key_count, DH), BF16),
            pltpu.VMEM((key_count, DH), BF16),
            pltpu.VMEM((queries, DH), BF16),
            pltpu.VMEM((BLOCK, key_count), F32),
            pltpu.VMEM((BLOCK, key_count), F32),
            pltpu.VMEM((BLOCK, key_count), BF16),
            pltpu.VMEM((BLOCK, key_count), BF16),
            pltpu.VMEM((DH, key_count), F32),
            pltpu.VMEM((DH, key_count), F32),
        ],
    )
    return pl.pallas_call(
        functools.partial(pull_kernel, cuts),
        grid_spec=grid_spec,
        out_shape=[
            jax.ShapeDtypeStruct((parts, group, seg, cols), BF16),
            jax.ShapeDtypeStruct((parts, group, rows, cols), BF16),
            jax.ShapeDtypeStruct((parts, group, rows, cols), BF16),
            jax.ShapeDtypeStruct((heads, DH, key_count), F32),
            jax.ShapeDtypeStruct((heads, 8, DH), F32),
        ],
        compiler_params=pltpu.CompilerParams(
            dimension_semantics=("arbitrary", "arbitrary"), vmem_limit_bytes=50 * 2**20
        ),
        cost_estimate=pl.CostEstimate(
            flops=12 * group * heads * queries * key_count * DH,
            bytes_accessed=2 * group * heads * queries * key_count,
            transcendentals=0,
        ),
        name="pull",
    )(weights, inverse, attended, out_grad, content_q, position_q, keys, values, table_rev)


def project_kernel(cut, rows_ref, gain_ref, shift_ref, w_ref, n_ref, ns_ref, q_ref, k_ref, v_ref):
    rows, width = rows_ref.shape
    cols = k_ref.shape[1]
    step = 64 if rows % 64 == 0 else 32
    for low in range(0, rows, step):
        wide = rows_ref[low : low + step, :].astype(F32)
        centred = wide - jnp.mean(wide, axis=1, keepdims=True)
        rate = lax.rsqrt(jnp.mean(centred * centred, axis=1, keepdims=True) + EPSILON)
        normed = (centred * rate * gain_ref[...] + shift_ref[...]).astype(BF16)
        n_ref[low : low + step, :] = normed
    ns_ref[...] = n_ref[cut:, :]
    q_ref[...] = mm(n_ref[cut:, :], w_ref[:, :cols], NN)
    k_ref[...] = mm(n_ref[...], w_ref[:, cols : 2 * cols], NN).astype(BF16)
    v_ref[...] = mm(n_ref[...], w_ref[:, 2 * cols : 3 * cols], NN).astype(BF16)


def project(rows_all, gain, shift, columns, cut):
    parts, group, each, width = rows_all.shape
    cols = columns.shape[1] // 4
    seg = each - cut
    block = lambda size, wide: pl.BlockSpec((None, None, size, wide), lambda p, s: (p, s, 0, 0))
    whole = lambda *shape: pl.BlockSpec(shape, lambda p, s: (0,) * len(shape))
    shape = lambda size, wide, kind: jax.ShapeDtypeStruct((parts, group, size, wide), kind)
    return pl.pallas_call(
        functools.partial(project_kernel, cut),
        grid_spec=pl.GridSpec(
            grid=(parts, group),
            in_specs=[
                block(each, width),
                whole(1, width),
                whole(1, width),
                whole(width, 4 * cols),
            ],
            out_specs=[
                block(each, width),
                block(seg, width),
                block(seg, cols),
                block(each, cols),
                block(each, cols),
            ],
        ),
        out_shape=[
            shape(each, width, BF16),
            shape(seg, width, BF16),
            shape(seg, cols, F32),
            shape(each, cols, BF16),
            shape(each, cols, BF16),
        ],
        compiler_params=pltpu.CompilerParams(
            dimension_semantics=("arbitrary", "arbitrary"), vmem_limit_bytes=40 * 2**20
        ),
        cost_estimate=pl.CostEstimate(
            flops=5 * parts * group * each * width * cols,
            bytes_accessed=5 * parts * group * each * width,
            transcendentals=0,
        ),
        name="project",
    )(rows_all, gain, shift, columns)


def gelu_both(x):
    near = jnp.abs(x)
    t = 1.0 / (1.0 + (0.3275911 * math.sqrt(0.5)) * near)
    bell = jnp.exp2((x * x) * (-0.5 * LOG2E))
    tail = 0.5 * 1.061405429
    for factor in (-1.453152027, 1.421413741, -0.284496736, 0.254829592):
        tail = tail * t + 0.5 * factor
    tail = tail * t * bell
    below = jnp.where(x < 0.0, tail, 1.0 - tail)
    return x * below, below + x * bell * (1.0 / math.sqrt(2.0 * math.pi))


def forward_back_kernel(
    carried, n_ref, c_ref, up_ref, down_ref, shift_ref, *rest,
):
    if carried:
        part_in, grad_in, part_ref, grad_ref, late_ref, sums_ref = rest[:6]
    else:
        part_ref, grad_ref, late_ref, sums_ref = rest[:4]
    pre, slope, hidden, act, up_out, down_out, sems = rest[6 if carried else 4 :]
    tile = pl.program_id(0)
    tiles = pl.num_programs(0)
    parts, cols, units = up_ref.shape
    width = parts * cols
    rows = n_ref.shape[0]
    layers, up_low, down_low = up_out.shape[2], up_out.shape[3], down_out.shape[2]
    slot = lax.rem(tile, 2)
    up_weight = up_ref[...].reshape(width, units)
    down_weight = down_ref[...]

    def copies(at, index):
        return (
            pltpu.make_async_copy(
                up_out.at[at],
                late_ref.at[
                    :, :, pl.ds(0, up_low), pl.ds(pl.multiple_of(index * units, units), units)
                ],
                sems.at[at, 0],
            ),
            pltpu.make_async_copy(
                down_out.at[at],
                late_ref.at[index, :, pl.ds(up_low, down_low), :],
                sems.at[at, 1],
            ),
        )

    @pl.when(tile == 0)
    def _():
        if carried:
            part_ref[...] = part_in[...]
            grad_ref[...] = grad_in[...]
        else:
            part_ref[...] = jnp.zeros_like(part_ref)
            grad_ref[...] = jnp.zeros_like(grad_ref)

    pre[...] = mm(n_ref[...], up_weight, NN)
    slope[...] = mm(c_ref[...], down_weight, NT)
    step = 64
    for low in range(0, rows, step):
        value, change = gelu_both(pre[low : low + step, :] + shift_ref[...])
        hidden[low : low + step, :] = value.astype(BF16)
        act[low : low + step, :] = (change * slope[low : low + step, :]).astype(BF16)
    part_ref[...] += mm(hidden[...], down_weight, NN)
    grad_ref[...] += mm(act[...], up_weight, NT)
    sums_ref[...] = jnp.sum(act[...].astype(F32), axis=0, keepdims=True)

    @pl.when(tile >= 2)
    def _():
        for copy in copies(slot, tile - 2):
            copy.wait()

    up_out[slot] = mm(n_ref[...], act[...], TN).astype(BF16).reshape(
        parts, layers, up_low, units
    )
    down_out[slot] = mm(hidden[...], c_ref[...], TN).astype(BF16).reshape(layers, down_low, width)
    for copy in copies(slot, tile):
        copy.start()

    @pl.when(tile == tiles - 1)
    def _():
        for copy in copies(1 - slot, tile - 1) + copies(slot, tile):
            copy.wait()


def forward_back(normed, cot, gathered, shift, layers, late_rows, carry):
    parts, _, width = gathered.shape
    rows = normed.shape[0]
    cols = width // parts
    units = shift.shape[1] // parts
    one = pl.Buffered(1)
    whole = lambda *shape: pl.BlockSpec(shape, lambda t: (0,) * len(shape), pipeline_mode=one)
    wide = jax.ShapeDtypeStruct((rows, width), F32)
    return pl.pallas_call(
        functools.partial(forward_back_kernel, len(carry) > 0),
        grid_spec=pl.GridSpec(
            grid=(parts,),
            in_specs=[
                whole(rows, width),
                whole(rows, width),
                pl.BlockSpec((parts, cols, units), lambda t: (0, 0, t)),
                pl.BlockSpec((None, units, width), lambda t: (t, cols // units, 0)),
                pl.BlockSpec((1, units), lambda t: (0, t)),
            ]
            + [whole(rows, width) for _ in carry],
            out_specs=[
                whole(rows, width),
                whole(rows, width),
                pl.BlockSpec(memory_space=pl.ANY),
                pl.BlockSpec((1, units), lambda t: (0, t)),
            ],
            scratch_shapes=[
                pltpu.VMEM((rows, units), F32),
                pltpu.VMEM((rows, units), F32),
                pltpu.VMEM((rows, units), BF16),
                pltpu.VMEM((rows, units), BF16),
                pltpu.VMEM((2, parts, layers, cols // layers, units), BF16),
                pltpu.VMEM((2, layers, units // layers, width), BF16),
                pltpu.SemaphoreType.DMA((2, 2)),
            ],
        ),
        out_shape=[
            wide,
            wide,
            jax.ShapeDtypeStruct((parts, layers, late_rows, width), BF16),
            jax.ShapeDtypeStruct((1, parts * units), F32),
        ],
        compiler_params=pltpu.CompilerParams(
            dimension_semantics=("arbitrary",), vmem_limit_bytes=56 * 2**20
        ),
        cost_estimate=pl.CostEstimate(
            flops=12 * rows * width * parts * units,
            bytes_accessed=12 * rows * width + 8 * parts * units * width,
            transcendentals=2 * rows * parts * units,
        ),
        name="forward_back",
    )(normed, cot, gathered, gathered, shift, *carry)


def compress_kernel(low, rows_ref, w_ref, shift_ref, out_ref, wide):
    count = out_ref.shape[0]
    cols = out_ref.shape[1]
    blocks = wide.shape[0]
    for at in range(blocks):
        wide[at] = rows_ref[low : low + 3 * count, at * LANES : (at + 1) * LANES].astype(F32)
    total = jnp.broadcast_to(shift_ref[...], (count, cols))
    for k in range(3):
        every = jnp.concatenate(
            [wide[at, pl.ds(k, count, stride=3), :] for at in range(blocks)], axis=1
        ).astype(BF16)
        total = total + mm(every, w_ref[:, k * cols : (k + 1) * cols], NN)
    out_ref[...] = total.astype(BF16)


def compress(rows_all, columns, shift, low, count):
    parts, group, each, width = rows_all.shape
    cols = columns.shape[1] // 3
    return pl.pallas_call(
        functools.partial(compress_kernel, low),
        grid_spec=pl.GridSpec(
            grid=(parts, group),
            in_specs=[
                pl.BlockSpec((None, None, each, width), lambda p, s: (p, s, 0, 0)),
                pl.BlockSpec((width, 3 * cols), lambda p, s: (0, 0)),
                pl.BlockSpec((1, cols), lambda p, s: (0, 0)),
            ],
            out_specs=pl.BlockSpec((None, None, count, cols), lambda p, s: (p, s, 0, 0)),
            scratch_shapes=[pltpu.VMEM((width // LANES, 3 * count, LANES), F32)],
        ),
        out_shape=jax.ShapeDtypeStruct((parts, group, count, cols), BF16),
        compiler_params=pltpu.CompilerParams(
            dimension_semantics=("arbitrary", "arbitrary"), vmem_limit_bytes=32 * 2**20
        ),
        cost_estimate=pl.CostEstimate(
            flops=6 * parts * group * count * width * cols,
            bytes_accessed=2 * parts * group * each * width,
            transcendentals=0,
        ),
        name="compress",
    )(rows_all, columns, shift)


def lay_out_kernel(sizes, parts, all_ref, up_ref, down_ref, out_ref):
    up_low, down_low, unit_cols, cols = sizes
    lows = (0, up_low + down_low)
    for half in range(2):
        for core in range(2):
            low = lows[half]
            for part in range(parts):
                at = ((part * 2 + core) * 2 + half) * unit_cols
                up_ref[:, at : at + unit_cols] = all_ref[
                    core, low : low + up_low, part * unit_cols : (part + 1) * unit_cols
                ].astype(F32)
            down_ref[2 * core + half] = all_ref[
                core, low + up_low : low + up_low + down_low, :
            ].astype(F32)
    low = 2 * (up_low + down_low)
    out_ref[...] = all_ref[0, low:, :].astype(F32) + all_ref[1, low:, :].astype(F32)


def lay_out(gathered, parts, unit_cols):
    layers, _, rows, width = gathered.shape
    cols = width // parts
    up_low, down_low = cols // layers, unit_cols // layers
    units = 4 * unit_cols * parts
    return pl.pallas_call(
        functools.partial(lay_out_kernel, (up_low, down_low, unit_cols, cols), parts),
        grid_spec=pl.GridSpec(
            grid=(layers,),
            in_specs=[pl.BlockSpec((None, 2, rows, width), lambda z: (z, 0, 0, 0))],
            out_specs=[
                pl.BlockSpec((up_low, units), lambda z: (z, 0)),
                pl.BlockSpec((4, down_low, width), lambda z: (0, z, 0)),
                pl.BlockSpec((up_low, width), lambda z: (z, 0)),
            ],
        ),
        out_shape=[
            jax.ShapeDtypeStruct((cols, units), F32),
            jax.ShapeDtypeStruct((4, unit_cols, width), F32),
            jax.ShapeDtypeStruct((cols, width), F32),
        ],
        compiler_params=pltpu.CompilerParams(vmem_limit_bytes=32 * 2**20),
        cost_estimate=pl.CostEstimate(
            flops=0, bytes_accessed=6 * cols * units * 2, transcendentals=0
        ),
        name="lay_out",
    )(gathered)


def lay_squares_kernel(in_ref, *out_refs):
    parts = in_ref.shape[0]
    cols = in_ref.shape[2] // len(out_refs)
    for at, out_ref in enumerate(out_refs):
        for part in range(parts):
            out_ref[:, part * cols : (part + 1) * cols] = in_ref[
                part, :, at * cols : (at + 1) * cols
            ].astype(F32)


def lay_squares(summed, rows):
    parts, _, wide = summed.shape
    width = parts * wide // 4
    step = rows // 2
    return pl.pallas_call(
        lay_squares_kernel,
        grid_spec=pl.GridSpec(
            grid=(2,),
            in_specs=[pl.BlockSpec((parts, step, wide), lambda i: (0, i, 0))],
            out_specs=[pl.BlockSpec((step, width), lambda i: (i, 0)) for _ in range(4)],
        ),
        out_shape=[jax.ShapeDtypeStruct((rows, width), F32) for _ in range(4)],
        compiler_params=pltpu.CompilerParams(vmem_limit_bytes=32 * 2**20),
        cost_estimate=pl.CostEstimate(
            flops=0, bytes_accessed=24 * rows * width, transcendentals=0
        ),
        name="lay_squares",
    )(summed)


def standardise(rows):
    mean = jnp.mean(rows, axis=-1, keepdims=True)
    centred = rows - mean
    rate = lax.rsqrt(jnp.mean(centred * centred, axis=-1, keepdims=True) + EPSILON)
    return centred * rate, rate


def standardise_back(unit, rate, grad, gain):
    scaled = grad * gain
    mean = jnp.mean(scaled, axis=-1, keepdims=True)
    along = jnp.mean(scaled * unit, axis=-1, keepdims=True)
    return rate * (scaled - mean - unit * along)


def sinusoid_reversed(rows, width):
    positions = (rows - 1 - jnp.arange(rows, dtype=jnp.int32)).astype(F32)[:, None]
    frequency = jnp.exp(
        jnp.arange(width // 2, dtype=F32) * (-2.0 * math.log(10000.0) / width)
    )
    angles = positions * frequency[None, :]
    return jnp.concatenate([jnp.sin(angles), jnp.cos(angles)], axis=1).astype(BF16)


def dot(left, right):
    return mm(left, right, NN)


def swap(value):
    return lax.ppermute(value, "core", [(0, 1), (1, 0)])


def body(
    segment, memory, compressed, eob, reset, ln1_gain, ln1_bias, w_query, w_key, w_value,
    w_out, out_bias, w_rel, bias_content, bias_position, ln2_gain, ln2_bias, w_up, up_bias,
    w_down, down_bias, conv_weight, conv_bias, cotangent,
):
    parts = lax.axis_size("seq")
    layers = lax.axis_size("z")
    core = lax.axis_index("core")
    me = lax.axis_index("seq")
    group, seg, width = segment.shape
    mem, old = memory.shape[1], compressed.shape[1]
    cuts = (old, mem, seg)
    each = old + mem + seg
    keys_in_all = parts * each
    cols = width // parts
    wide = 4 * cols
    own = group * seg
    unit_cols = w_up.shape[1] // (4 * parts)
    barrier = lax.optimization_barrier

    def by_columns(matrices):
        count = matrices.shape[0]
        sent = matrices.reshape(count, cols, parts, cols).transpose(2, 1, 0, 3)
        return sent.reshape(parts, cols, count * cols)

    up_bias_own = lax.dynamic_slice_in_dim(up_bias, core * 2 * unit_cols, 2 * unit_cols, 0)
    vectors = jnp.concatenate(
        [ln1_gain, ln1_bias, out_bias, ln2_gain, ln2_bias, down_bias, up_bias_own]
    )
    vectors = jnp.pad(vectors.reshape(2, wide), ((0, 14), (0, 0)))
    sent = jnp.concatenate(
        [
            by_columns(jnp.stack([w_query, w_key, w_value, w_rel])),
            jnp.broadcast_to(vectors, (parts, 16, wide)),
        ],
        axis=1,
    )
    got = lax.all_to_all(sent, "seq", 0, 0, tiled=True)
    rows_all = lax.all_gather(jnp.concatenate([compressed, memory, segment], axis=1), "seq")
    columns = got[:, :cols].reshape(width, wide)
    vectors = got[:, cols : cols + 2].reshape(parts, 2 * wide).astype(F32)
    gain_one, shift_one, out_shift, gain_two, shift_two, down_shift = (
        vectors[:, cols * i : cols * (i + 1)].reshape(1, width) for i in range(6)
    )
    up_shift = vectors[:, 6 * cols :].reshape(parts, 2, unit_cols).transpose(1, 0, 2)
    up_shift = up_shift.reshape(2, 1, parts * unit_cols)
    up_quarters = lax.dynamic_slice_in_dim(
        w_up.reshape(cols, parts, 2, 2, unit_cols), core, 1, 2
    ).reshape(cols, parts, 2, unit_cols)
    up_quarters = [up_quarters[:, :, i].reshape(cols, width) for i in range(2)]
    down_half = lax.dynamic_slice_in_dim(w_down, core * 2 * unit_cols, 2 * unit_cols, 0)
    down_quarters = [down_half[unit_cols * i : unit_cols * (i + 1)] for i in range(2)]
    first = jnp.concatenate([up_quarters[0], down_quarters[0], w_out], axis=0)
    second = jnp.concatenate([up_quarters[1], down_quarters[1]], axis=0)
    first, rows_all = barrier((first, rows_all))
    first = lax.all_gather(first, "seq")
    second, first = barrier((second, first))
    second = lax.all_gather(second, "seq")
    out_full = first[:, cols + unit_cols :].reshape(width, width)
    cot_own = cotangent.reshape(own, width)
    cot_both = jnp.concatenate([cot_own, swap(cot_own)], axis=0)

    table_rev = sinusoid_reversed(keys_in_all, width)
    proj_rev = dot(table_rev, columns[:, 3 * cols :]).astype(BF16)
    index = jnp.arange(eob.shape[1], dtype=jnp.int32)[None, :]
    opens = jnp.pad(eob, ((0, 0), (1, 0)))[:, :-1] == 1
    start = lax.cummax(jnp.where(opens, index, 0), axis=1)
    shade = jnp.where((start == 0) & (reset[:, None] == 0), 0.0, MASKED)
    info = jnp.stack([start.astype(F32), shade], axis=2)
    info = jnp.pad(info, ((0, 0), (0, 0), (0, LANES - 2)))
    rows_all, proj_rev, info, cot_both, table_rev = barrier(
        (rows_all, proj_rev, info, cot_both, table_rev)
    )

    normed, normed_seg, query, keys, values = project(
        rows_all, gain_one, shift_one, columns, old + mem
    )
    weights, inverse, mixed_heads, content_q, position_q = attend(
        query,
        bias_content.astype(F32).reshape(1, cols),
        bias_position.astype(F32).reshape(1, cols),
        keys,
        values,
        proj_rev,
        info,
        cuts,
    )
    attended = lax.all_to_all(mixed_heads, "seq", 0, 0, tiled=True)
    attended = attended.transpose(1, 2, 0, 3).reshape(own, width)
    conv_sent, attended = barrier((by_columns(conv_weight), attended))
    conv_columns = lax.all_to_all(conv_sent, "seq", 0, 0, tiled=True).reshape(width, 3 * cols)

    segment_own = segment.reshape(own, width).astype(F32)
    middle = segment_own + (dot(attended, out_full) + out_shift)
    unit_two, rate_two = standardise(middle)
    normed_two = (unit_two * gain_two + shift_two).astype(BF16)
    both = jnp.concatenate([normed_two, swap(normed_two)], axis=0)
    low = (cols + unit_cols) // layers
    part, part_grad, late_one, unit_one = forward_back(
        both, cot_both, first, up_shift[0], layers, low, ()
    )
    early = lax.psum_scatter(
        late_one.reshape(-1, width), ("seq", "z"), scatter_dimension=0, tiled=True
    )
    part, part_grad, late_two, unit_two_sums = forward_back(
        both, cot_both, second, up_shift[1], layers, low + cols // layers, (part, part_grad)
    )
    normed_two_grad = part_grad[:own] + swap(part_grad[own:].astype(BF16)).astype(F32)
    result = part[:own] + swap(part[own:].astype(BF16)).astype(F32) + down_shift
    output = (middle + result).astype(BF16).reshape(group, seg, width)

    cot_wide = cot_own.astype(F32)
    middle_grad = cot_wide + standardise_back(unit_two, rate_two, normed_two_grad, gain_two)
    branch_grad = middle_grad.astype(BF16)
    attended_grad = mm(branch_grad, out_full, NT).astype(BF16)
    attended_grad = attended_grad.reshape(group, seg, parts, cols).transpose(2, 0, 1, 3)
    head_grad = lax.all_to_all(attended_grad, "seq", 0, 0, tiled=True)
    out_grad = mm(attended, branch_grad, TN).astype(BF16)
    late_two = late_two.at[:, :, low:, :].set(
        out_grad.reshape(parts, layers, cols // layers, width)
    )
    later = lax.psum_scatter(
        late_two.reshape(-1, width), ("seq", "z"), scatter_dimension=0, tiled=True
    )

    query_grad, key_grad, value_grad, table_grad, sums = pull(
        weights, inverse, mixed_heads, head_grad, content_q, position_q, keys, values, proj_rev, cuts
    )
    seg_grads = jnp.concatenate(
        [query_grad, key_grad[:, :, old + mem :], value_grad[:, :, old + mem :]], axis=3
    )
    seg_part = mm(seg_grads.reshape(parts * own, 3 * cols), columns[:, : 3 * cols], NT)
    seg_part = lax.all_to_all(
        seg_part.astype(BF16).reshape(parts, own, width), "seq", 0, 0, tiled=True
    )
    early, later, query_grad = barrier((early, later, query_grad))
    gathered = lax.all_gather(jnp.concatenate([early, later], axis=0), ("z", "core"))
    gathered = gathered.reshape(layers, 2, 2 * low + cols // layers, width)

    query_w = mm(normed_seg.reshape(parts * own, width), query_grad.reshape(parts * own, cols), TN)
    normed = normed.reshape(parts * group * each, width)
    key_w = mm(normed, key_grad.reshape(parts * group * each, cols), TN)
    value_w = mm(normed, value_grad.reshape(parts * group * each, cols), TN)
    rel_w = mm(table_rev, table_grad.reshape(cols, keys_in_all).astype(BF16), ((0,), (1,)))
    sums = sums.transpose(1, 0, 2).reshape(8, cols)
    weight_cols = columns[:, : 3 * cols].astype(F32)
    row_sums = sums[2:5].reshape(1, 3 * cols)
    three = jnp.concatenate([query_w, key_w, value_w], axis=1)
    shift_one_grad = jnp.sum(weight_cols * row_sums, axis=1)
    gain_one_grad = jnp.sum(
        weight_cols * (three - shift_one.reshape(width, 1) * row_sums), axis=1
    ) / gain_one.reshape(width)
    gain_two_grad = jnp.sum(normed_two_grad * unit_two, axis=0)
    shift_two_grad = jnp.sum(normed_two_grad, axis=0)
    down_shift_grad = jnp.sum(cot_wide, axis=0)
    out_shift_grad = jnp.sum(branch_grad.astype(F32), axis=0)
    chunk = lambda vector: vector.reshape(parts, cols)
    mine = (jnp.arange(parts) == me).astype(F32)[:, None]
    unit_sums = jnp.stack(
        [unit_one.reshape(parts, unit_cols), unit_two_sums.reshape(parts, unit_cols)], axis=1
    ).reshape(parts, 2 * unit_cols)
    small = jnp.stack(
        [
            jnp.concatenate(
                [chunk(gain_one_grad), chunk(shift_one_grad), chunk(out_shift_grad), chunk(gain_two_grad)],
                axis=1,
            ),
            jnp.concatenate(
                [chunk(shift_two_grad), chunk(down_shift_grad), mine * sums[0:1], mine * sums[1:2]],
                axis=1,
            ),
            jnp.concatenate(
                [jnp.where(core == 0, unit_sums, 0.0), jnp.where(core == 1, unit_sums, 0.0)], axis=1
            ),
        ],
        axis=1,
    )
    small = jnp.pad(small, ((0, 0), (0, 13), (0, 0))).astype(BF16)
    square_grads = jnp.concatenate([three.astype(BF16), rel_w.astype(BF16)], axis=1)
    square_grads = jnp.concatenate([square_grads.reshape(parts, cols, wide), small], axis=1)
    summed = lax.all_to_all(square_grads, "seq", 0, 0, tiled=True)
    summed = lax.psum(summed, ("z", "core"))

    conv_columns, query_grad = barrier((conv_columns, query_grad))
    packed = compress(
        rows_all, conv_columns, conv_bias.astype(F32).reshape(1, cols), old, mem // 3
    )
    packed = lax.all_to_all(packed, "seq", 0, 0, tiled=True)
    new_compressed = packed.transpose(1, 2, 0, 3).reshape(group, mem // 3, width)

    seg_grad = jnp.sum(seg_part.astype(F32), axis=0)
    unit_seg, rate_seg = standardise(segment_own)
    rows_grad = standardise_back(unit_seg, rate_seg, seg_grad, gain_one)
    segment_grad = (middle_grad + rows_grad).reshape(group, seg, width)

    up_w, down_w, out_w = lay_out(gathered, parts, unit_cols)
    down_w = down_w.reshape(4 * unit_cols, width)
    query_w, key_w, value_w, rel_w = lay_squares(summed, cols)
    small = jnp.sum(summed[:, cols : cols + 3].astype(F32), axis=0)
    piece = lambda row, i: small[row, cols * i : cols * (i + 1)]
    return (
        output,
        segment_grad,
        piece(0, 0),
        piece(0, 1),
        query_w,
        key_w,
        value_w,
        out_w,
        piece(0, 2),
        rel_w,
        piece(1, 2),
        piece(1, 3),
        piece(0, 3),
        piece(1, 0),
        up_w,
        small[2],
        down_w,
        piece(1, 1),
        new_compressed,
    )


def solution(mesh):
    dp = mesh.shape["dp"]
    cores = jax.sharding.Mesh(
        mesh.devices.reshape(dp // 2, 2, mesh.shape["seq"]), ("z", "core", "seq")
    )
    rows = P(("z", "core"), "seq", None)
    shard, matrix = P("seq"), P("seq", None)
    return jax.shard_map(
        body,
        mesh=cores,
        in_specs=(
            rows, rows, rows, P(("z", "core"), None), P(("z", "core")), shard, shard, matrix,
            matrix, matrix, matrix, shard, matrix, shard, shard, shard, shard, matrix, shard,
            matrix, shard, P(None, "seq", None), shard, rows,
        ),
        out_specs=(
            rows, rows, shard, shard, matrix, matrix, matrix, matrix, shard, matrix, shard,
            shard, shard, shard, matrix, shard, matrix, shard, rows,
        ),
        check_vma=False,
    )
```

```python
import functools
import math

import jax
import jax.numpy as jnp
from jax import lax
from jax.experimental import pallas as pl
from jax.experimental.pallas import tpu as pltpu
from jax.sharding import PartitionSpec as P

HEADS = 8
DH = 128
EPSILON = 1e-05
MASKED = -1e30
LANES = 128
BLOCK = 256
CHUNK = 16
SCALE = 1.0 / math.sqrt(DH)
LOG2E = 1.4426950408889634
BF16 = jnp.bfloat16
F32 = jnp.float32


def cost(microseconds):
    return pl.CostEstimate(flops=int(microseconds * 1.15e7), bytes_accessed=0, transcendentals=0)


def mm(left, right, dims):
    return lax.dot_general(left, right, (dims, ((), ())), preferred_element_type=F32)


NN = ((1,), (0,))
NT = ((1,), (1,))
TN = ((0,), (0,))


def lean_left(block, first_row, fill_columns):
    columns = block.shape[1] // LANES
    far = BLOCK - 1 - first_row
    whole, part = far // LANES, far % LANES
    turned = [
        pltpu.roll(
            block[:, LANES * t : LANES * (t + 1)], LANES - part, 1, stride=1, stride_axis=0
        )
        for t in range(columns)
    ]
    rows = lax.broadcasted_iota(jnp.int32, (block.shape[0], LANES), 0)
    lanes = lax.broadcasted_iota(jnp.int32, (block.shape[0], LANES), 1)
    near = lanes - rows < LANES - part
    out = []
    for t in range(fill_columns):
        a = turned[(t + whole) % columns]
        b = turned[(t + whole + 1) % columns]
        out.append(jnp.where(near, a, b))
    return jnp.concatenate(out, axis=1)


def lean_right(block, first_row):
    columns = block.shape[1] // LANES
    whole, part = first_row // LANES, first_row % LANES
    turned = [
        pltpu.roll(block[:, LANES * t : LANES * (t + 1)], part, 1, stride=1, stride_axis=0)
        for t in range(columns)
    ]
    rows = lax.broadcasted_iota(jnp.int32, (block.shape[0], LANES), 0)
    lanes = lax.broadcasted_iota(jnp.int32, (block.shape[0], LANES), 1)
    wrapped = lanes - rows < part
    out = []
    for t in range(columns):
        a = turned[(t - whole) % columns]
        b = turned[(t - whole - 1) % columns]
        out.append(jnp.where(wrapped, b, a))
    return jnp.concatenate(out, axis=1)


def flip_matrix(kind):
    rows = lax.broadcasted_iota(jnp.int32, (BLOCK, BLOCK), 0)
    lanes = lax.broadcasted_iota(jnp.int32, (BLOCK, BLOCK), 1)
    return (rows + lanes == BLOCK - 1).astype(F32).astype(kind)


def in_place_order(parts_ref, out_ref, cuts):
    parts = parts_ref.shape[0]
    low, base = 0, 0
    for size in cuts:
        for part in range(parts):
            out_ref[base + part * size : base + (part + 1) * size, :] = parts_ref[
                part, low : low + size, :
            ]
        low += size
        base += parts * size


def attend_kernel(
    cuts, q_ref, cb_ref, pb_ref, k_ref, v_ref, t_ref, info_ref,
    e_ref, inv_ref, o_ref, cq_ref, pq_ref,
    keys, values, raw, lean, mix,
):
    parts, seg, _ = q_ref.shape
    queries = parts * seg
    old = parts * (cuts[0] + cuts[1])
    in_place_order(k_ref, keys, cuts)
    in_place_order(v_ref, values, cuts)
    q = q_ref[...].reshape(queries, DH)
    content_q = (q + cb_ref[...]).astype(BF16)
    position_q = (q + pb_ref[...]).astype(BF16)
    cq_ref[...] = content_q.reshape(parts, seg, DH)
    pq_ref[...] = position_q.reshape(parts, seg, DH)
    for block in range(queries // BLOCK):
        row0 = block * BLOCK
        width = old + row0 + BLOCK
        skip = queries - BLOCK - row0
        raw[:, :width] = mm(content_q[row0 : row0 + BLOCK], keys[:width, :], NT)
        lean[:, :width] = mm(position_q[row0 : row0 + BLOCK], t_ref[skip : skip + width, :], NT)
        for chunk in range(BLOCK // CHUNK):
            r0 = chunk * CHUNK
            turned = lean_left(lean[r0 : r0 + CHUNK, :width], r0, width // LANES)
            score = raw[r0 : r0 + CHUNK, :width] + turned
            start = info_ref[row0 + r0 : row0 + r0 + CHUNK, 0:1]
            shade = info_ref[row0 + r0 : row0 + r0 + CHUNK, 1:2]
            past = score[:, :old] + shade
            place = lax.broadcasted_iota(jnp.int32, (CHUNK, row0 + BLOCK), 1)
            own = lax.broadcasted_iota(jnp.int32, (CHUNK, row0 + BLOCK), 0) + (row0 + r0)
            seen = (place <= own) & (place >= start.astype(jnp.int32))
            now = jnp.where(seen, score[:, old:], MASKED)
            top = jnp.maximum(
                jnp.max(past, axis=1, keepdims=True), jnp.max(now, axis=1, keepdims=True)
            )
            past = jnp.exp2((past - top) * (SCALE * LOG2E))
            now = jnp.exp2((now - top) * (SCALE * LOG2E))
            total = jnp.sum(past, axis=1, keepdims=True) + jnp.sum(now, axis=1, keepdims=True)
            inv = jnp.broadcast_to(1.0 / total, (CHUNK, DH))
            inv_ref[row0 + r0 : row0 + r0 + CHUNK, :] = inv
            e_ref[row0 + r0 : row0 + r0 + CHUNK, :old] = past.astype(BF16)
            e_ref[row0 + r0 : row0 + r0 + CHUNK, old:width] = now.astype(BF16)
        mix[row0 : row0 + BLOCK, :] = mm(
            e_ref[row0 : row0 + BLOCK, :width], values[:width, :], NN
        )
    o_ref[...] = (mix[...] * inv_ref[...]).astype(BF16).reshape(parts, seg, DH)


def attend(query, content_shift, position_shift, keys, values, table_rev, info, cuts):
    parts, group, seg, cols = query.shape
    rows = keys.shape[2]
    queries, key_count, heads = parts * seg, parts * rows, cols // DH
    by_head = lambda size: pl.BlockSpec((parts, None, size, DH), lambda s, h: (0, s, 0, h))
    grid_spec = pl.GridSpec(
        grid=(group, heads),
        in_specs=[
            by_head(seg),
            pl.BlockSpec((1, DH), lambda s, h: (0, h)),
            pl.BlockSpec((1, DH), lambda s, h: (0, h)),
            by_head(rows),
            by_head(rows),
            pl.BlockSpec((key_count, DH), lambda s, h: (0, h)),
            pl.BlockSpec((None, queries, LANES), lambda s, h: (s, 0, 0)),
        ],
        out_specs=[
            pl.BlockSpec((None, None, queries, key_count), lambda s, h: (s, h, 0, 0)),
            pl.BlockSpec((None, None, queries, DH), lambda s, h: (s, h, 0, 0)),
            by_head(seg),
            by_head(seg),
            by_head(seg),
        ],
        scratch_shapes=[
            pltpu.VMEM((key_count, DH), BF16),
            pltpu.VMEM((key_count, DH), BF16),
            pltpu.VMEM((BLOCK, key_count), F32),
            pltpu.VMEM((BLOCK, key_count), F32),
            pltpu.VMEM((queries, DH), F32),
        ],
    )
    small = jax.ShapeDtypeStruct((parts, group, seg, cols), BF16)
    return pl.pallas_call(
        functools.partial(attend_kernel, cuts),
        grid_spec=grid_spec,
        out_shape=[
            jax.ShapeDtypeStruct((group, heads, queries, key_count), BF16),
            jax.ShapeDtypeStruct((group, heads, queries, DH), F32),
            small,
            small,
            small,
        ],
        compiler_params=pltpu.CompilerParams(
            dimension_semantics=("arbitrary", "arbitrary"), vmem_limit_bytes=50 * 2**20
        ),
        cost_estimate=cost(40),
        name="attend",
    )(query, content_shift, position_shift, keys, values, table_rev, info)


def pull_kernel(
    cuts, e_ref, inv_ref, o_ref, g_ref, cq_ref, pq_ref, k_ref, v_ref, t_ref,
    dq_ref, dk_ref, dv_ref, dt_ref, sums_ref,
    keys, values, grad, prob, part, score, lean, key_sum, value_sum,
):
    stream = pl.program_id(1)
    parts, seg, _ = g_ref.shape
    queries = parts * seg
    old = parts * (cuts[0] + cuts[1])
    in_place_order(k_ref, keys, cuts)
    in_place_order(v_ref, values, cuts)
    out_grad = g_ref[...].reshape(queries, DH).astype(F32)
    attended = o_ref[...].reshape(queries, DH).astype(F32)
    inv = inv_ref[...]
    grad[...] = (out_grad * inv).astype(BF16)
    dots = jnp.sum(out_grad * attended, axis=1, keepdims=True) * inv
    content_q = cq_ref[...].reshape(queries, DH)
    position_q = pq_ref[...].reshape(queries, DH)

    @pl.when(stream == 0)
    def _():
        dt_ref[...] = jnp.zeros_like(dt_ref)
        sums_ref[...] = jnp.zeros_like(sums_ref)

    key_sum[...] = jnp.zeros_like(key_sum)
    value_sum[...] = jnp.zeros_like(value_sum)
    content_total = jnp.zeros((1, DH), F32)
    position_total = jnp.zeros((1, DH), F32)
    query_total = jnp.zeros((1, DH), F32)
    flip = flip_matrix(BF16)
    flip_wide = flip_matrix(F32)
    turn = lambda rows: mm(flip, rows, NN).astype(BF16)
    for block in range(queries // BLOCK):
        row0 = block * BLOCK
        width = old + row0 + BLOCK
        skip = queries - BLOCK - row0
        rows = slice(row0, row0 + BLOCK)
        dots_back = lax.dot_general(
            flip_wide,
            jnp.broadcast_to(dots[rows], (BLOCK, DH)),
            (NN, ((), ())),
            precision=lax.Precision.HIGHEST,
            preferred_element_type=F32,
        )
        content_back = turn(content_q[rows])
        position_back = turn(position_q[rows])
        prob[:, :width] = mm(turn(grad[rows, :]), values[:width, :], NT)
        part[:, :width] = mm(flip, e_ref[rows, :width], NN)
        value_sum[:, :width] += mm(grad[rows, :], e_ref[rows, :width], TN)
        for chunk in range(BLOCK // CHUNK):
            r0 = chunk * CHUNK
            mean = dots_back[r0 : r0 + CHUNK, 0:1]
            change = part[r0 : r0 + CHUNK, :width] * (prob[r0 : r0 + CHUNK, :width] - mean)
            score[r0 : r0 + CHUNK, :width] = change.astype(BF16)
            lean[r0 : r0 + CHUNK, :width] = lean_right(change, r0).astype(BF16)
        content_grad = (mm(score[:, :width], keys[:width, :], NN) * SCALE).astype(BF16).astype(F32)
        position_grad = (
            (mm(lean[:, :width], t_ref[skip : skip + width, :], NN) * SCALE)
            .astype(BF16)
            .astype(F32)
        )
        query_grad = turn((content_grad + position_grad).astype(BF16))
        content_total += jnp.sum(content_grad, axis=0, keepdims=True)
        position_total += jnp.sum(position_grad, axis=0, keepdims=True)
        query_total += jnp.sum(query_grad.astype(F32), axis=0, keepdims=True)
        low = row0
        while low < row0 + BLOCK:
            part_at, part_row = low // seg, low % seg
            size = min(seg - part_row, row0 + BLOCK - low)
            dq_ref[part_at, part_row : part_row + size, :] = query_grad[
                low - row0 : low - row0 + size
            ]
            low += size
        key_sum[:, :width] += mm(content_back, score[:, :width], TN)
        dt_ref[:, skip : skip + width] += mm(position_back, lean[:, :width], TN) * SCALE
    key_rows = (key_sum[...] * SCALE).T.astype(BF16)
    value_rows = value_sum[...].T.astype(BF16)
    low, base = 0, 0
    for size in cuts:
        for at in range(parts):
            span = slice(base + at * size, base + (at + 1) * size)
            dk_ref[at, low : low + size, :] = key_rows[span]
            dv_ref[at, low : low + size, :] = value_rows[span]
        low += size
        base += parts * size
    key_total = jnp.sum(key_rows.astype(F32), axis=0, keepdims=True)
    value_total = jnp.sum(value_rows.astype(F32), axis=0, keepdims=True)
    sums_ref[...] += jnp.concatenate(
        [
            content_total,
            position_total,
            query_total,
            key_total,
            value_total,
            jnp.zeros((3, DH), F32),
        ],
        axis=0,
    )


def pull(weights, inverse, attended, out_grad, content_q, position_q, keys, values, table_rev, cuts):
    parts, group, seg, cols = out_grad.shape
    rows = keys.shape[2]
    queries, key_count, heads = parts * seg, parts * rows, cols // DH
    by_head = lambda size: pl.BlockSpec((parts, None, size, DH), lambda h, s: (0, s, 0, h))
    grid_spec = pl.GridSpec(
        grid=(heads, group),
        in_specs=[
            pl.BlockSpec((None, None, queries, key_count), lambda h, s: (s, h, 0, 0)),
            pl.BlockSpec((None, None, queries, DH), lambda h, s: (s, h, 0, 0)),
            by_head(seg),
            by_head(seg),
            by_head(seg),
            by_head(seg),
            by_head(rows),
            by_head(rows),
            pl.BlockSpec((key_count, DH), lambda h, s: (0, h)),
        ],
        out_specs=[
            by_head(seg),
            by_head(rows),
            by_head(rows),
            pl.BlockSpec((None, DH, key_count), lambda h, s: (h, 0, 0)),
            pl.BlockSpec((None, 8, DH), lambda h, s: (h, 0, 0)),
        ],
        scratch_shapes=[
            pltpu.VMEM((key_count, DH), BF16),
            pltpu.VMEM((key_count, DH), BF16),
            pltpu.VMEM((queries, DH), BF16),
            pltpu.VMEM((BLOCK, key_count), F32),
            pltpu.VMEM((BLOCK, key_count), F32),
            pltpu.VMEM((BLOCK, key_count), BF16),
            pltpu.VMEM((BLOCK, key_count), BF16),
            pltpu.VMEM((DH, key_count), F32),
            pltpu.VMEM((DH, key_count), F32),
        ],
    )
    return pl.pallas_call(
        functools.partial(pull_kernel, cuts),
        grid_spec=grid_spec,
        out_shape=[
            jax.ShapeDtypeStruct((parts, group, seg, cols), BF16),
            jax.ShapeDtypeStruct((parts, group, rows, cols), BF16),
            jax.ShapeDtypeStruct((parts, group, rows, cols), BF16),
            jax.ShapeDtypeStruct((heads, DH, key_count), F32),
            jax.ShapeDtypeStruct((heads, 8, DH), F32),
        ],
        compiler_params=pltpu.CompilerParams(
            dimension_semantics=("arbitrary", "arbitrary"), vmem_limit_bytes=50 * 2**20
        ),
        cost_estimate=cost(39),
        name="pull",
    )(weights, inverse, attended, out_grad, content_q, position_q, keys, values, table_rev)


def project_kernel(cut, rows_ref, gain_ref, shift_ref, w_ref, n_ref, ns_ref, q_ref, k_ref, v_ref):
    rows, width = rows_ref.shape
    cols = k_ref.shape[1]
    step = 64 if rows % 64 == 0 else 32
    for low in range(0, rows, step):
        wide = rows_ref[low : low + step, :].astype(F32)
        centred = wide - jnp.mean(wide, axis=1, keepdims=True)
        rate = lax.rsqrt(jnp.mean(centred * centred, axis=1, keepdims=True) + EPSILON)
        normed = (centred * rate * gain_ref[...] + shift_ref[...]).astype(BF16)
        n_ref[low : low + step, :] = normed
    ns_ref[...] = n_ref[cut:, :]
    q_ref[...] = mm(n_ref[cut:, :], w_ref[:, :cols], NN)
    k_ref[...] = mm(n_ref[...], w_ref[:, cols : 2 * cols], NN).astype(BF16)
    v_ref[...] = mm(n_ref[...], w_ref[:, 2 * cols : 3 * cols], NN).astype(BF16)


def project(rows_all, gain, shift, columns, cut):
    parts, group, each, width = rows_all.shape
    cols = columns.shape[1] // 4
    seg = each - cut
    block = lambda size, wide: pl.BlockSpec((None, None, size, wide), lambda p, s: (p, s, 0, 0))
    whole = lambda *shape: pl.BlockSpec(shape, lambda p, s: (0,) * len(shape))
    shape = lambda size, wide, kind: jax.ShapeDtypeStruct((parts, group, size, wide), kind)
    return pl.pallas_call(
        functools.partial(project_kernel, cut),
        grid_spec=pl.GridSpec(
            grid=(parts, group),
            in_specs=[
                block(each, width),
                whole(1, width),
                whole(1, width),
                whole(width, 4 * cols),
            ],
            out_specs=[
                block(each, width),
                block(seg, width),
                block(seg, cols),
                block(each, cols),
                block(each, cols),
            ],
        ),
        out_shape=[
            shape(each, width, BF16),
            shape(seg, width, BF16),
            shape(seg, cols, F32),
            shape(each, cols, BF16),
            shape(each, cols, BF16),
        ],
        compiler_params=pltpu.CompilerParams(
            dimension_semantics=("arbitrary", "arbitrary"), vmem_limit_bytes=40 * 2**20
        ),
        cost_estimate=cost(17),
        name="project",
    )(rows_all, gain, shift, columns)


def gelu_both(x):
    near = jnp.abs(x)
    t = 1.0 / (1.0 + (0.3275911 * math.sqrt(0.5)) * near)
    bell = jnp.exp2((x * x) * (-0.5 * LOG2E))
    tail = 0.5 * 1.061405429
    for factor in (-1.453152027, 1.421413741, -0.284496736, 0.254829592):
        tail = tail * t + 0.5 * factor
    tail = tail * t * bell
    below = jnp.where(x < 0.0, tail, 1.0 - tail)
    return x * below, below + x * bell * (1.0 / math.sqrt(2.0 * math.pi))


def forward_back_kernel(
    last, n_ref, c_ref, up_ref, down_ref, shift_ref, *rest,
):
    if last:
        part_in, grad_in, part_out, part_far, grad_out, grad_far, late_ref, sums_ref = rest[:8]
        pre, slope, hidden, act, up_out, down_out, sems, part_ref, grad_ref = rest[8:]
    else:
        part_ref, grad_ref, late_ref, sums_ref = rest[:4]
        pre, slope, hidden, act, up_out, down_out, sems = rest[4:]
    tile = pl.program_id(0)
    tiles = pl.num_programs(0)
    parts, cols, units = up_ref.shape
    width = parts * cols
    rows = n_ref.shape[0]
    slot = lax.rem(tile, 2)
    up_weight = up_ref[...].reshape(width, units)
    down_weight = down_ref[...]

    def copies(at, index):
        return (
            pltpu.make_async_copy(
                up_out.at[at],
                late_ref.at[:, pl.ds(0, cols), pl.ds(pl.multiple_of(index * units, units), units)],
                sems.at[at, 0],
            ),
            pltpu.make_async_copy(
                down_out.at[at], late_ref.at[index, pl.ds(cols, units), :], sems.at[at, 1]
            ),
        )

    @pl.when(tile == 0)
    def _():
        if last:
            part_ref[...] = part_in[...]
            grad_ref[...] = grad_in[...]
        else:
            part_ref[...] = jnp.zeros_like(part_ref)
            grad_ref[...] = jnp.zeros_like(grad_ref)

    pre[...] = mm(n_ref[...], up_weight, NN)
    slope[...] = mm(c_ref[...], down_weight, NT)
    step = 64
    for low in range(0, rows, step):
        value, change = gelu_both(pre[low : low + step, :] + shift_ref[...])
        hidden[low : low + step, :] = value.astype(BF16)
        act[low : low + step, :] = (change * slope[low : low + step, :]).astype(BF16)
    part_ref[...] += mm(hidden[...], down_weight, NN)
    grad_ref[...] += mm(act[...], up_weight, NT)
    sums_ref[...] = jnp.sum(act[...].astype(F32), axis=0, keepdims=True)

    @pl.when(tile >= 2)
    def _():
        for copy in copies(slot, tile - 2):
            copy.wait()

    up_out[slot] = mm(n_ref[...], act[...], TN).astype(BF16).reshape(parts, cols, units)
    down_out[slot] = mm(hidden[...], c_ref[...], TN).astype(BF16)
    for copy in copies(slot, tile):
        copy.start()

    @pl.when(tile == tiles - 1)
    def _():
        if last:
            part_out[...] = part_ref[: rows // 2, :]
            part_far[...] = part_ref[rows // 2 :, :].astype(BF16)
            grad_out[...] = grad_ref[: rows // 2, :]
            grad_far[...] = grad_ref[rows // 2 :, :].astype(BF16)
        for copy in copies(1 - slot, tile - 1) + copies(slot, tile):
            copy.wait()


def forward_back(normed, cot, gathered, shift, carry):
    parts, _, width = gathered.shape
    rows = normed.shape[0]
    cols = width // parts
    units = shift.shape[1] // parts
    last = len(carry) > 0
    one = pl.Buffered(1)
    whole = lambda *shape: pl.BlockSpec(shape, lambda t: (0,) * len(shape), pipeline_mode=one)
    if last:
        sums = [((rows // 2, width), F32), ((rows // 2, width), BF16)] * 2
    else:
        sums = [((rows, width), F32)] * 2
    return pl.pallas_call(
        functools.partial(forward_back_kernel, last),
        grid_spec=pl.GridSpec(
            grid=(parts,),
            in_specs=[
                whole(rows, width),
                whole(rows, width),
                pl.BlockSpec((parts, cols, units), lambda t: (0, 0, t)),
                pl.BlockSpec((None, units, width), lambda t: (t, cols // units, 0)),
                pl.BlockSpec((1, units), lambda t: (0, t)),
            ]
            + [whole(rows, width) for _ in carry],
            out_specs=[whole(*shape) for shape, _ in sums]
            + [
                pl.BlockSpec(memory_space=pl.ANY),
                pl.BlockSpec((1, units), lambda t: (0, t)),
            ],
            scratch_shapes=[
                pltpu.VMEM((rows, units), F32),
                pltpu.VMEM((rows, units), F32),
                pltpu.VMEM((rows, units), BF16),
                pltpu.VMEM((rows, units), BF16),
                pltpu.VMEM((2, parts, cols, units), BF16),
                pltpu.VMEM((2, units, width), BF16),
                pltpu.SemaphoreType.DMA((2, 2)),
            ]
            + [pltpu.VMEM((rows, width), F32) for _ in carry],
        ),
        out_shape=[jax.ShapeDtypeStruct(shape, kind) for shape, kind in sums]
        + [
            jax.ShapeDtypeStruct((parts, cols + units, width), BF16),
            jax.ShapeDtypeStruct((1, parts * units), F32),
        ],
        compiler_params=pltpu.CompilerParams(
            dimension_semantics=("arbitrary",), vmem_limit_bytes=56 * 2**20
        ),
        cost_estimate=cost(29),
        name="forward_back",
    )(normed, cot, gathered, gathered, shift, *carry)


def leave_kernel(a_ref, s_ref, w_ref, shift_ref, gain_ref, bias_ref, flat_ref, m_ref, n_ref):
    parts = a_ref.shape[0]
    flat_ref[...] = jnp.concatenate([a_ref[part] for part in range(parts)], axis=1)
    weight = w_ref[...].reshape(flat_ref.shape[1], flat_ref.shape[1])
    m_ref[...] = s_ref[...].astype(F32) + (mm(flat_ref[...], weight, NN) + shift_ref[...])
    step = 32
    for low in range(0, m_ref.shape[0], step):
        unit, _ = standardise(m_ref[low : low + step, :])
        n_ref[low : low + step, :] = (unit * gain_ref[...] + bias_ref[...]).astype(BF16)


def leave(mixed_heads, segment, gathered, shift, gain, bias):
    parts, group, seg, cols = mixed_heads.shape
    width = parts * cols
    at = gathered.shape[1] // cols - 1
    rows = lambda: pl.BlockSpec((None, seg, width), lambda s: (s, 0, 0))
    vector = lambda: pl.BlockSpec((1, width), lambda s: (0, 0))
    shape = lambda kind: jax.ShapeDtypeStruct((group, seg, width), kind)
    return pl.pallas_call(
        leave_kernel,
        grid_spec=pl.GridSpec(
            grid=(group,),
            in_specs=[
                pl.BlockSpec((parts, None, seg, cols), lambda s: (0, s, 0, 0)),
                rows(),
                pl.BlockSpec((parts, cols, width), lambda s: (0, at, 0)),
                vector(),
                vector(),
                vector(),
            ],
            out_specs=[rows(), rows(), rows()],
        ),
        out_shape=[shape(BF16), shape(F32), shape(BF16)],
        compiler_params=pltpu.CompilerParams(vmem_limit_bytes=32 * 2**20),
        cost_estimate=cost(6),
        name="leave",
    )(mixed_heads, segment, gathered, shift, gain, bias)


def enter_kernel(
    m_ref, g_ref, far_ref, c_ref, w_ref, gain_ref, mg_ref, b_ref, a_ref, sums_ref
):
    @pl.when(pl.program_id(0) == 0)
    def _():
        sums_ref[...] = jnp.zeros_like(sums_ref)

    parts = a_ref.shape[0]
    rows, width = m_ref.shape
    step = 32
    total = [jnp.zeros((1, width), F32) for _ in range(4)]
    for low in range(0, rows, step):
        at = slice(low, low + step)
        unit, rate = standardise(m_ref[at, :])
        grad = g_ref[at, :] + far_ref[at, :].astype(F32)
        cot = c_ref[at, :].astype(F32)
        middle_grad = cot + standardise_back(unit, rate, grad, gain_ref[...])
        branch = middle_grad.astype(BF16)
        mg_ref[at, :] = middle_grad
        b_ref[at, :] = branch
        for i, value in enumerate((branch.astype(F32), grad * unit, grad, cot)):
            total[i] = total[i] + jnp.sum(value, axis=0, keepdims=True)
    sums_ref[...] += jnp.concatenate(total + [jnp.zeros((4, width), F32)], axis=0)
    for part in range(parts):
        a_ref[part] = mm(b_ref[...], w_ref[part], NT).astype(BF16)


def enter(middle, grad, far, cot, gathered, gain):
    group, seg, width = middle.shape
    parts = gathered.shape[0]
    cols = width // parts
    at = gathered.shape[1] // cols - 1
    rows = lambda: pl.BlockSpec((None, seg, width), lambda s: (s, 0, 0))
    shape = lambda kind: jax.ShapeDtypeStruct((group, seg, width), kind)
    return pl.pallas_call(
        enter_kernel,
        grid_spec=pl.GridSpec(
            grid=(group,),
            in_specs=[
                rows(),
                rows(),
                rows(),
                rows(),
                pl.BlockSpec((parts, cols, width), lambda s: (0, at, 0)),
                pl.BlockSpec((1, width), lambda s: (0, 0)),
            ],
            out_specs=[
                rows(),
                rows(),
                pl.BlockSpec((parts, None, seg, cols), lambda s: (0, s, 0, 0)),
                pl.BlockSpec((8, width), lambda s: (0, 0)),
            ],
        ),
        out_shape=[
            shape(F32),
            shape(BF16),
            jax.ShapeDtypeStruct((parts, group, seg, cols), BF16),
            jax.ShapeDtypeStruct((8, width), F32),
        ],
        compiler_params=pltpu.CompilerParams(
            dimension_semantics=("arbitrary",), vmem_limit_bytes=32 * 2**20
        ),
        cost_estimate=cost(7),
        name="enter",
    )(middle, grad, far, cot, gathered, gain)


def compress_kernel(low, rows_ref, w_ref, shift_ref, out_ref, wide):
    count = out_ref.shape[0]
    cols = out_ref.shape[1]
    blocks = wide.shape[0]
    for at in range(blocks):
        wide[at] = rows_ref[low : low + 3 * count, at * LANES : (at + 1) * LANES].astype(F32)
    total = jnp.broadcast_to(shift_ref[...], (count, cols))
    for k in range(3):
        every = jnp.concatenate(
            [wide[at, pl.ds(k, count, stride=3), :] for at in range(blocks)], axis=1
        ).astype(BF16)
        total = total + mm(every, w_ref[:, k * cols : (k + 1) * cols], NN)
    out_ref[...] = total.astype(BF16)


def compress(rows_all, columns, shift, low, count):
    parts, group, each, width = rows_all.shape
    cols = columns.shape[1] // 3
    return pl.pallas_call(
        functools.partial(compress_kernel, low),
        grid_spec=pl.GridSpec(
            grid=(parts, group),
            in_specs=[
                pl.BlockSpec((None, None, each, width), lambda p, s: (p, s, 0, 0)),
                pl.BlockSpec((width, 3 * cols), lambda p, s: (0, 0)),
                pl.BlockSpec((1, cols), lambda p, s: (0, 0)),
            ],
            out_specs=pl.BlockSpec((None, None, count, cols), lambda p, s: (p, s, 0, 0)),
            scratch_shapes=[pltpu.VMEM((width // LANES, 3 * count, LANES), F32)],
        ),
        out_shape=jax.ShapeDtypeStruct((parts, group, count, cols), BF16),
        compiler_params=pltpu.CompilerParams(
            dimension_semantics=("arbitrary", "arbitrary"), vmem_limit_bytes=32 * 2**20
        ),
        cost_estimate=cost(6.5),
        name="compress",
    )(rows_all, columns, shift)


def lay_out_kernel(parts, unit_cols, core_ref, a_ref, b_ref, c_ref, d_ref, up_ref, down_ref):
    flipped = core_ref[0] == 1
    for half, (mine_ref, far_ref) in enumerate(((a_ref, c_ref), (b_ref, d_ref))):
        mine, far = mine_ref[...].astype(F32), far_ref[...].astype(F32)
        for core, value in enumerate(
            (jnp.where(flipped, far, mine), jnp.where(flipped, mine, far))
        ):
            for part in range(parts):
                at = ((part * 2 + core) * 2 + half) * unit_cols
                up_ref[:, at : at + unit_cols] = value[
                    0, :, part * unit_cols : (part + 1) * unit_cols
                ]
            down_ref[2 * core + half] = value[1]


def lay_out(core, mine, far, parts):
    _, _, rows, width = mine.shape
    step = rows // 4 if rows % 64 == 0 else rows
    half = lambda i: pl.BlockSpec((None, 2, step, width), lambda r, *_, i=i: (i, 0, r, 0))
    return pl.pallas_call(
        functools.partial(lay_out_kernel, parts, rows),
        grid_spec=pltpu.PrefetchScalarGridSpec(
            num_scalar_prefetch=1,
            grid=(rows // step,),
            in_specs=[half(0), half(1), half(0), half(1)],
            out_specs=[
                pl.BlockSpec((step, 4 * width), lambda r, *_: (r, 0)),
                pl.BlockSpec((4, step, width), lambda r, *_: (0, r, 0)),
            ],
        ),
        out_shape=[
            jax.ShapeDtypeStruct((rows, 4 * width), F32),
            jax.ShapeDtypeStruct((4, rows, width), F32),
        ],
        compiler_params=pltpu.CompilerParams(vmem_limit_bytes=32 * 2**20),
        cost_estimate=cost(4),
        name="lay_out",
    )(core.reshape(1), mine, mine, far, far)


def lay_squares_kernel(in_ref, *out_refs):
    parts = in_ref.shape[0]
    cols = in_ref.shape[2] // len(out_refs)
    for at, out_ref in enumerate(out_refs):
        for part in range(parts):
            out_ref[:, part * cols : (part + 1) * cols] = in_ref[
                part, :, at * cols : (at + 1) * cols
            ].astype(F32)


def lay_squares(summed, rows):
    parts, _, wide = summed.shape
    width = parts * wide // 4
    step = rows // 2
    return pl.pallas_call(
        lay_squares_kernel,
        grid_spec=pl.GridSpec(
            grid=(2,),
            in_specs=[pl.BlockSpec((parts, step, wide), lambda i: (0, i, 0))],
            out_specs=[pl.BlockSpec((step, width), lambda i: (i, 0)) for _ in range(4)],
        ),
        out_shape=[jax.ShapeDtypeStruct((rows, width), F32) for _ in range(4)],
        compiler_params=pltpu.CompilerParams(vmem_limit_bytes=32 * 2**20),
        cost_estimate=cost(2.5),
        name="lay_squares",
    )(summed)


def standardise(rows):
    mean = jnp.mean(rows, axis=-1, keepdims=True)
    centred = rows - mean
    rate = lax.rsqrt(jnp.mean(centred * centred, axis=-1, keepdims=True) + EPSILON)
    return centred * rate, rate


def standardise_back(unit, rate, grad, gain):
    scaled = grad * gain
    mean = jnp.mean(scaled, axis=-1, keepdims=True)
    along = jnp.mean(scaled * unit, axis=-1, keepdims=True)
    return rate * (scaled - mean - unit * along)


def sinusoid_reversed(rows, width):
    positions = (rows - 1 - jnp.arange(rows, dtype=jnp.int32)).astype(F32)[:, None]
    frequency = jnp.exp(
        jnp.arange(width // 2, dtype=F32) * (-2.0 * math.log(10000.0) / width)
    )
    angles = positions * frequency[None, :]
    return jnp.concatenate([jnp.sin(angles), jnp.cos(angles)], axis=1).astype(BF16)


def dot(left, right):
    return mm(left, right, NN)


def swap(value):
    return lax.ppermute(value, "core", [(0, 1), (1, 0)])


def exchange(blocks):
    parts = blocks.shape[0]
    me = lax.axis_index("seq")
    out = [lax.dynamic_index_in_dim(blocks, me, 0, keepdims=False)]
    for apart in range(1, parts):
        sent = lax.dynamic_index_in_dim(blocks, me ^ apart, 0, keepdims=False)
        out.append(lax.ppermute(sent, "seq", [(i, i ^ apart) for i in range(parts)]))
    return out


def add_up(arrays, kind=BF16):
    total = arrays[0].astype(F32)
    for array in arrays[1:]:
        total = total + array.astype(F32)
    return total.astype(kind)


def body(
    segment, memory, compressed, eob, reset, ln1_gain, ln1_bias, w_query, w_key, w_value,
    w_out, out_bias, w_rel, bias_content, bias_position, ln2_gain, ln2_bias, w_up, up_bias,
    w_down, down_bias, conv_weight, conv_bias, cotangent,
):
    parts = lax.axis_size("seq")
    core = lax.axis_index("core")
    me = lax.axis_index("seq")
    group, seg, width = segment.shape
    mem, old = memory.shape[1], compressed.shape[1]
    cuts = (old, mem, seg)
    each = old + mem + seg
    keys_in_all = parts * each
    cols = width // parts
    wide = 4 * cols
    own = group * seg
    unit_cols = w_up.shape[1] // (4 * parts)
    barrier = lax.optimization_barrier

    def by_columns(matrices):
        count = matrices.shape[0]
        sent = matrices.reshape(count, cols, parts, cols).transpose(2, 1, 0, 3)
        return sent.reshape(parts, cols, count * cols)

    up_bias_own = lax.dynamic_slice_in_dim(up_bias, core * 2 * unit_cols, 2 * unit_cols, 0)
    vectors = jnp.concatenate(
        [ln1_gain, ln1_bias, out_bias, ln2_gain, ln2_bias, down_bias, up_bias_own]
    )
    vectors = jnp.pad(vectors.reshape(2, wide), ((0, 14), (0, 0)))
    sent = jnp.concatenate(
        [
            by_columns(jnp.stack([w_query, w_key, w_value, w_rel])),
            jnp.broadcast_to(vectors, (parts, 16, wide)),
        ],
        axis=1,
    )
    got = lax.all_to_all(sent, "seq", 0, 0, tiled=True)
    rows_all = lax.all_gather(jnp.concatenate([compressed, memory, segment], axis=1), "seq")
    columns = got[:, :cols].reshape(width, wide)
    vectors = got[:, cols : cols + 2].reshape(parts, 2 * wide).astype(F32)
    gain_one, shift_one, out_shift, gain_two, shift_two, down_shift = (
        vectors[:, cols * i : cols * (i + 1)].reshape(1, width) for i in range(6)
    )
    up_shift = vectors[:, 6 * cols :].reshape(parts, 2, unit_cols).transpose(1, 0, 2)
    up_shift = up_shift.reshape(2, 1, parts * unit_cols)
    up_quarters = lax.dynamic_slice_in_dim(
        w_up.reshape(cols, parts, 2, 2, unit_cols), core, 1, 2
    ).reshape(cols, parts, 2, unit_cols)
    up_quarters = [up_quarters[:, :, i].reshape(cols, width) for i in range(2)]
    down_half = lax.dynamic_slice_in_dim(w_down, core * 2 * unit_cols, 2 * unit_cols, 0)
    down_quarters = [down_half[unit_cols * i : unit_cols * (i + 1)] for i in range(2)]
    first = jnp.concatenate([up_quarters[0], down_quarters[0], w_out], axis=0)
    second = jnp.concatenate([up_quarters[1], down_quarters[1]], axis=0)
    cot_own = cotangent.reshape(own, width)
    cot_both = jnp.concatenate([cot_own, swap(cot_own)], axis=0)

    table_rev = sinusoid_reversed(keys_in_all, width)
    proj_rev = dot(table_rev, columns[:, 3 * cols :]).astype(BF16)
    index = jnp.arange(eob.shape[1], dtype=jnp.int32)[None, :]
    opens = jnp.pad(eob, ((0, 0), (1, 0)))[:, :-1] == 1
    start = lax.cummax(jnp.where(opens, index, 0), axis=1)
    shade = jnp.where((start == 0) & (reset[:, None] == 0), 0.0, MASKED)
    info = jnp.stack([start.astype(F32), shade], axis=2)
    info = jnp.pad(info, ((0, 0), (0, 0), (0, LANES - 2)))
    rows_all, first, proj_rev, info, cot_both, table_rev, columns = barrier(
        (rows_all, first, proj_rev, info, cot_both, table_rev, columns)
    )
    first = lax.all_gather(first, "seq")

    normed, normed_seg, query, keys, values = project(
        rows_all, gain_one, shift_one, columns, old + mem
    )
    second, query = barrier((second, query))
    second = lax.all_gather(second, "seq")
    weights, inverse, mixed_heads, content_q, position_q = attend(
        query,
        bias_content.astype(F32).reshape(1, cols),
        bias_position.astype(F32).reshape(1, cols),
        keys,
        values,
        proj_rev,
        info,
        cuts,
    )
    attended = lax.all_to_all(mixed_heads, "seq", 0, 0, tiled=True)
    conv_sent, attended = barrier((by_columns(conv_weight), attended))
    conv_columns = lax.all_to_all(conv_sent, "seq", 0, 0, tiled=True)

    attended, middle, normed_two = leave(
        attended, segment, first, out_shift, gain_two, shift_two
    )
    normed_two = normed_two.reshape(own, width)
    both = jnp.concatenate([normed_two, swap(normed_two)], axis=0)
    part, part_grad, late_one, unit_one = forward_back(both, cot_both, first, up_shift[0], ())
    early = lax.psum_scatter(
        late_one.reshape(-1, width), "seq", scatter_dimension=0, tiled=True
    )
    part, part_far, part_grad, grad_far, late_two, unit_two = forward_back(
        both, cot_both, second, up_shift[1], (part, part_grad)
    )
    conv_columns, grad_far = barrier((conv_columns, grad_far))
    grad_far = swap(grad_far)
    by_stream = lambda rows: rows.reshape(group, seg, width)
    middle_grad, branch_grad, attended_grad, sums_two = enter(
        middle, by_stream(part_grad), by_stream(grad_far), cotangent, first, gain_two
    )
    head_grad = lax.all_to_all(attended_grad, "seq", 0, 0, tiled=True)
    late_two = exchange(late_two)
    out_grad = mm(attended.reshape(own, width), branch_grad.reshape(own, width), TN)
    out_grad = exchange(out_grad.astype(BF16).reshape(parts, cols, width))
    result = part + swap(part_far).astype(F32) + down_shift
    output = (middle.reshape(own, width) + result).astype(BF16).reshape(group, seg, width)
    early, late_two, out_grad, head_grad = barrier((early, late_two, out_grad, head_grad))
    ff = jnp.concatenate([early, add_up(late_two)], axis=0)
    out_sum = add_up(out_grad)
    ff, out_sum, head_grad = barrier((ff, out_sum, head_grad))
    ff = lax.psum(ff, "z")

    query_grad, key_grad, value_grad, table_grad, sums = pull(
        weights, inverse, mixed_heads, head_grad, content_q, position_q, keys, values, proj_rev, cuts
    )
    conv_columns, query_grad = barrier((conv_columns, query_grad))
    seg_grads = jnp.concatenate(
        [query_grad, key_grad[:, :, old + mem :], value_grad[:, :, old + mem :]], axis=3
    )
    seg_part = mm(seg_grads.reshape(parts * own, 3 * cols), columns[:, : 3 * cols], NT)
    seg_part = exchange(seg_part.astype(BF16).reshape(parts, own, width))
    query_w = mm(normed_seg.reshape(parts * own, width), query_grad.reshape(parts * own, cols), TN)
    normed = normed.reshape(parts * group * each, width)
    key_w = mm(normed, key_grad.reshape(parts * group * each, cols), TN)
    value_w = mm(normed, value_grad.reshape(parts * group * each, cols), TN)
    rel_w = mm(table_rev, table_grad.reshape(cols, keys_in_all).astype(BF16), ((0,), (1,)))
    sums = sums.transpose(1, 0, 2).reshape(8, cols)
    weight_cols = columns[:, : 3 * cols].astype(F32)
    row_sums = sums[2:5].reshape(1, 3 * cols)
    three = jnp.concatenate([query_w, key_w, value_w], axis=1)
    shift_one_grad = jnp.sum(weight_cols * row_sums, axis=1)
    gain_one_grad = jnp.sum(
        weight_cols * (three - shift_one.reshape(width, 1) * row_sums), axis=1
    ) / gain_one.reshape(width)
    out_shift_grad, gain_two_grad, shift_two_grad, down_shift_grad = (
        sums_two[i] for i in range(4)
    )
    chunk = lambda vector: vector.reshape(parts, cols)
    mine = (jnp.arange(parts) == me).astype(F32)[:, None]
    unit_sums = jnp.stack(
        [unit_one.reshape(parts, unit_cols), unit_two.reshape(parts, unit_cols)], axis=1
    ).reshape(parts, 2 * unit_cols)
    small = jnp.stack(
        [
            jnp.concatenate(
                [chunk(gain_one_grad), chunk(shift_one_grad), chunk(out_shift_grad), chunk(gain_two_grad)],
                axis=1,
            ),
            jnp.concatenate(
                [chunk(shift_two_grad), chunk(down_shift_grad), mine * sums[0:1], mine * sums[1:2]],
                axis=1,
            ),
            jnp.concatenate(
                [jnp.where(core == 0, unit_sums, 0.0), jnp.where(core == 1, unit_sums, 0.0)], axis=1
            ),
        ],
        axis=1,
    )
    small = jnp.pad(small, ((0, 0), (0, 13), (0, 0))).astype(BF16)
    square_grads = jnp.concatenate([three.astype(BF16), rel_w.astype(BF16)], axis=1)
    square_grads = jnp.concatenate([square_grads.reshape(parts, cols, wide), small], axis=1)
    summed = lax.all_to_all(square_grads, "seq", 0, 0, tiled=True)
    summed = jnp.concatenate([summed.reshape(-1, wide), out_sum.reshape(-1, wide)], axis=0)
    summed = lax.psum(summed, ("z", "core"))
    ff_far = swap(ff)
    squares = parts * (cols + 16)
    out_w = summed[squares:].reshape(cols, width).astype(F32)
    summed = summed[:squares].reshape(parts, cols + 16, wide)

    packed = compress(
        rows_all, conv_columns.reshape(width, 3 * cols), conv_bias.astype(F32).reshape(1, cols), old, mem // 3
    )
    packed = lax.all_to_all(packed, "seq", 0, 0, tiled=True)
    new_compressed = packed.transpose(1, 2, 0, 3).reshape(group, mem // 3, width)

    seg_grad = add_up(seg_part, F32)
    unit_seg, rate_seg = standardise(segment.reshape(own, width).astype(F32))
    rows_grad = standardise_back(unit_seg, rate_seg, seg_grad, gain_one)
    segment_grad = middle_grad + by_stream(rows_grad)

    up_w, down_w = lay_out(
        core,
        ff.reshape(2, 2, unit_cols, width),
        ff_far.reshape(2, 2, unit_cols, width),
        parts,
    )
    down_w = down_w.reshape(4 * unit_cols, width)
    query_w, key_w, value_w, rel_w = lay_squares(summed, cols)
    small = jnp.sum(summed[:, cols : cols + 3].astype(F32), axis=0)
    piece = lambda row, i: small[row, cols * i : cols * (i + 1)]
    return (
        output,
        segment_grad,
        piece(0, 0),
        piece(0, 1),
        query_w,
        key_w,
        value_w,
        out_w,
        piece(0, 2),
        rel_w,
        piece(1, 2),
        piece(1, 3),
        piece(0, 3),
        piece(1, 0),
        up_w,
        small[2],
        down_w,
        piece(1, 1),
        new_compressed,
    )


def solution(mesh):
    dp = mesh.shape["dp"]
    cores = jax.sharding.Mesh(
        mesh.devices.reshape(dp // 2, 2, mesh.shape["seq"]), ("z", "core", "seq")
    )
    rows = P(("z", "core"), "seq", None)
    shard, matrix = P("seq"), P("seq", None)
    return jax.shard_map(
        body,
        mesh=cores,
        in_specs=(
            rows, rows, rows, P(("z", "core"), None), P(("z", "core")), shard, shard, matrix,
            matrix, matrix, matrix, shard, matrix, shard, shard, shard, shard, matrix, shard,
            matrix, shard, P(None, "seq", None), shard, rows,
        ),
        out_specs=(
            rows, rows, shard, shard, matrix, matrix, matrix, matrix, shard, matrix, shard,
            shard, shard, shard, matrix, shard, matrix, shard, rows,
        ),
        check_vma=False,
    )
```

```python
import functools
import math

import jax
import jax.numpy as jnp
from jax import lax
from jax.experimental import pallas as pl
from jax.experimental.pallas import tpu as pltpu
from jax.sharding import PartitionSpec as P

HEADS = 8
DH = 128
EPSILON = 1e-05
MASKED = -1e30
LANES = 128
BLOCK = 256
CHUNK = 16
SCALE = 1.0 / math.sqrt(DH)
LOG2E = 1.4426950408889634
BF16 = jnp.bfloat16
F32 = jnp.float32


def cost(microseconds):
    return pl.CostEstimate(flops=int(microseconds * 1.15e7), bytes_accessed=0, transcendentals=0)


def mm(left, right, dims):
    return lax.dot_general(left, right, (dims, ((), ())), preferred_element_type=F32)


NN = ((1,), (0,))
NT = ((1,), (1,))
TN = ((0,), (0,))


def lean_left(block, first_row, fill_columns):
    columns = block.shape[1] // LANES
    far = BLOCK - 1 - first_row
    whole, part = far // LANES, far % LANES
    turned = [
        pltpu.roll(
            block[:, LANES * t : LANES * (t + 1)], LANES - part, 1, stride=1, stride_axis=0
        )
        for t in range(columns)
    ]
    rows = lax.broadcasted_iota(jnp.int32, (block.shape[0], LANES), 0)
    lanes = lax.broadcasted_iota(jnp.int32, (block.shape[0], LANES), 1)
    near = lanes - rows < LANES - part
    out = []
    for t in range(fill_columns):
        a = turned[(t + whole) % columns]
        b = turned[(t + whole + 1) % columns]
        out.append(jnp.where(near, a, b))
    return jnp.concatenate(out, axis=1)


def lean_right(block, first_row):
    columns = block.shape[1] // LANES
    whole, part = first_row // LANES, first_row % LANES
    turned = [
        pltpu.roll(block[:, LANES * t : LANES * (t + 1)], part, 1, stride=1, stride_axis=0)
        for t in range(columns)
    ]
    rows = lax.broadcasted_iota(jnp.int32, (block.shape[0], LANES), 0)
    lanes = lax.broadcasted_iota(jnp.int32, (block.shape[0], LANES), 1)
    wrapped = lanes - rows < part
    out = []
    for t in range(columns):
        a = turned[(t - whole) % columns]
        b = turned[(t - whole - 1) % columns]
        out.append(jnp.where(wrapped, b, a))
    return jnp.concatenate(out, axis=1)


def flip_matrix(kind):
    rows = lax.broadcasted_iota(jnp.int32, (BLOCK, BLOCK), 0)
    lanes = lax.broadcasted_iota(jnp.int32, (BLOCK, BLOCK), 1)
    return (rows + lanes == BLOCK - 1).astype(F32).astype(kind)


def in_place_order(parts_ref, out_ref, cuts):
    parts = parts_ref.shape[0]
    low, base = 0, 0
    for size in cuts:
        for part in range(parts):
            out_ref[base + part * size : base + (part + 1) * size, :] = parts_ref[
                part, low : low + size, :
            ]
        low += size
        base += parts * size


def attend_kernel(
    cuts, q_ref, cb_ref, pb_ref, k_ref, v_ref, t_ref, info_ref,
    e_ref, inv_ref, o_ref, cq_ref, pq_ref,
    keys, values, raw, lean, mix,
):
    parts, seg, _ = q_ref.shape
    queries = parts * seg
    old = parts * (cuts[0] + cuts[1])
    in_place_order(k_ref, keys, cuts)
    in_place_order(v_ref, values, cuts)
    q = q_ref[...].reshape(queries, DH)
    content_q = (q + cb_ref[...]).astype(BF16)
    position_q = (q + pb_ref[...]).astype(BF16)
    cq_ref[...] = content_q.reshape(parts, seg, DH)
    pq_ref[...] = position_q.reshape(parts, seg, DH)
    for block in range(queries // BLOCK):
        row0 = block * BLOCK
        width = old + row0 + BLOCK
        skip = queries - BLOCK - row0
        raw[:, :width] = mm(content_q[row0 : row0 + BLOCK], keys[:width, :], NT)
        lean[:, :width] = mm(position_q[row0 : row0 + BLOCK], t_ref[skip : skip + width, :], NT)
        for chunk in range(BLOCK // CHUNK):
            r0 = chunk * CHUNK
            turned = lean_left(lean[r0 : r0 + CHUNK, :width], r0, width // LANES)
            score = raw[r0 : r0 + CHUNK, :width] + turned
            start = info_ref[row0 + r0 : row0 + r0 + CHUNK, 0:1]
            shade = info_ref[row0 + r0 : row0 + r0 + CHUNK, 1:2]
            past = score[:, :old] + shade
            place = lax.broadcasted_iota(jnp.int32, (CHUNK, row0 + BLOCK), 1)
            own = lax.broadcasted_iota(jnp.int32, (CHUNK, row0 + BLOCK), 0) + (row0 + r0)
            seen = (place <= own) & (place >= start.astype(jnp.int32))
            now = jnp.where(seen, score[:, old:], MASKED)
            top = jnp.maximum(
                jnp.max(past, axis=1, keepdims=True), jnp.max(now, axis=1, keepdims=True)
            )
            past = jnp.exp2((past - top) * (SCALE * LOG2E))
            now = jnp.exp2((now - top) * (SCALE * LOG2E))
            total = jnp.sum(past, axis=1, keepdims=True) + jnp.sum(now, axis=1, keepdims=True)
            inv = jnp.broadcast_to(1.0 / total, (CHUNK, DH))
            inv_ref[row0 + r0 : row0 + r0 + CHUNK, :] = inv
            e_ref[row0 + r0 : row0 + r0 + CHUNK, :old] = past.astype(BF16)
            e_ref[row0 + r0 : row0 + r0 + CHUNK, old:width] = now.astype(BF16)
        mix[row0 : row0 + BLOCK, :] = mm(
            e_ref[row0 : row0 + BLOCK, :width], values[:width, :], NN
        )
    o_ref[...] = (mix[...] * inv_ref[...]).astype(BF16).reshape(parts, seg, DH)


def attend(query, content_shift, position_shift, keys, values, table_rev, info, cuts):
    parts, group, seg, cols = query.shape
    rows = keys.shape[2]
    queries, key_count, heads = parts * seg, parts * rows, cols // DH
    by_head = lambda size: pl.BlockSpec((parts, None, size, DH), lambda s, h: (0, s, 0, h))
    grid_spec = pl.GridSpec(
        grid=(group, heads),
        in_specs=[
            by_head(seg),
            pl.BlockSpec((1, DH), lambda s, h: (0, h)),
            pl.BlockSpec((1, DH), lambda s, h: (0, h)),
            by_head(rows),
            by_head(rows),
            pl.BlockSpec((key_count, DH), lambda s, h: (0, h)),
            pl.BlockSpec((None, queries, LANES), lambda s, h: (s, 0, 0)),
        ],
        out_specs=[
            pl.BlockSpec((None, None, queries, key_count), lambda s, h: (s, h, 0, 0)),
            pl.BlockSpec((None, None, queries, DH), lambda s, h: (s, h, 0, 0)),
            by_head(seg),
            by_head(seg),
            by_head(seg),
        ],
        scratch_shapes=[
            pltpu.VMEM((key_count, DH), BF16),
            pltpu.VMEM((key_count, DH), BF16),
            pltpu.VMEM((BLOCK, key_count), F32),
            pltpu.VMEM((BLOCK, key_count), F32),
            pltpu.VMEM((queries, DH), F32),
        ],
    )
    small = jax.ShapeDtypeStruct((parts, group, seg, cols), BF16)
    return pl.pallas_call(
        functools.partial(attend_kernel, cuts),
        grid_spec=grid_spec,
        out_shape=[
            jax.ShapeDtypeStruct((group, heads, queries, key_count), BF16),
            jax.ShapeDtypeStruct((group, heads, queries, DH), F32),
            small,
            small,
            small,
        ],
        compiler_params=pltpu.CompilerParams(
            dimension_semantics=("arbitrary", "arbitrary"), vmem_limit_bytes=50 * 2**20
        ),
        cost_estimate=cost(40),
        name="attend",
    )(query, content_shift, position_shift, keys, values, table_rev, info)


def pull_kernel(
    cuts, e_ref, inv_ref, o_ref, g_ref, cq_ref, pq_ref, k_ref, v_ref, t_ref,
    dq_ref, dk_ref, dv_ref, dt_ref, sums_ref,
    keys, values, grad, prob, part, score, lean, key_sum, value_sum,
):
    stream = pl.program_id(1)
    parts, seg, _ = g_ref.shape
    queries = parts * seg
    old = parts * (cuts[0] + cuts[1])
    in_place_order(k_ref, keys, cuts)
    in_place_order(v_ref, values, cuts)
    out_grad = g_ref[...].reshape(queries, DH).astype(F32)
    attended = o_ref[...].reshape(queries, DH).astype(F32)
    inv = inv_ref[...]
    grad[...] = (out_grad * inv).astype(BF16)
    dots = jnp.sum(out_grad * attended, axis=1, keepdims=True) * inv
    content_q = cq_ref[...].reshape(queries, DH)
    position_q = pq_ref[...].reshape(queries, DH)

    @pl.when(stream == 0)
    def _():
        dt_ref[...] = jnp.zeros_like(dt_ref)
        sums_ref[...] = jnp.zeros_like(sums_ref)

    key_sum[...] = jnp.zeros_like(key_sum)
    value_sum[...] = jnp.zeros_like(value_sum)
    content_total = jnp.zeros((1, DH), F32)
    position_total = jnp.zeros((1, DH), F32)
    query_total = jnp.zeros((1, DH), F32)
    flip = flip_matrix(BF16)
    flip_wide = flip_matrix(F32)
    turn = lambda rows: mm(flip, rows, NN).astype(BF16)
    for block in range(queries // BLOCK):
        row0 = block * BLOCK
        width = old + row0 + BLOCK
        skip = queries - BLOCK - row0
        rows = slice(row0, row0 + BLOCK)
        dots_back = lax.dot_general(
            flip_wide,
            jnp.broadcast_to(dots[rows], (BLOCK, DH)),
            (NN, ((), ())),
            precision=lax.Precision.HIGHEST,
            preferred_element_type=F32,
        )
        content_back = turn(content_q[rows])
        position_back = turn(position_q[rows])
        prob[:, :width] = mm(turn(grad[rows, :]), values[:width, :], NT)
        part[:, :width] = mm(flip, e_ref[rows, :width], NN)
        value_sum[:, :width] += mm(grad[rows, :], e_ref[rows, :width], TN)
        for chunk in range(BLOCK // CHUNK):
            r0 = chunk * CHUNK
            mean = dots_back[r0 : r0 + CHUNK, 0:1]
            change = part[r0 : r0 + CHUNK, :width] * (prob[r0 : r0 + CHUNK, :width] - mean)
            score[r0 : r0 + CHUNK, :width] = change.astype(BF16)
            lean[r0 : r0 + CHUNK, :width] = lean_right(change, r0).astype(BF16)
        content_grad = (mm(score[:, :width], keys[:width, :], NN) * SCALE).astype(BF16).astype(F32)
        position_grad = (
            (mm(lean[:, :width], t_ref[skip : skip + width, :], NN) * SCALE)
            .astype(BF16)
            .astype(F32)
        )
        query_grad = turn((content_grad + position_grad).astype(BF16))
        content_total += jnp.sum(content_grad, axis=0, keepdims=True)
        position_total += jnp.sum(position_grad, axis=0, keepdims=True)
        query_total += jnp.sum(query_grad.astype(F32), axis=0, keepdims=True)
        low = row0
        while low < row0 + BLOCK:
            part_at, part_row = low // seg, low % seg
            size = min(seg - part_row, row0 + BLOCK - low)
            dq_ref[part_at, part_row : part_row + size, :] = query_grad[
                low - row0 : low - row0 + size
            ]
            low += size
        key_sum[:, :width] += mm(content_back, score[:, :width], TN)
        dt_ref[:, skip : skip + width] += mm(position_back, lean[:, :width], TN) * SCALE
    key_rows = (key_sum[...] * SCALE).T.astype(BF16)
    value_rows = value_sum[...].T.astype(BF16)
    low, base = 0, 0
    for size in cuts:
        for at in range(parts):
            span = slice(base + at * size, base + (at + 1) * size)
            dk_ref[at, low : low + size, :] = key_rows[span]
            dv_ref[at, low : low + size, :] = value_rows[span]
        low += size
        base += parts * size
    key_total = jnp.sum(key_rows.astype(F32), axis=0, keepdims=True)
    value_total = jnp.sum(value_rows.astype(F32), axis=0, keepdims=True)
    sums_ref[...] += jnp.concatenate(
        [
            content_total,
            position_total,
            query_total,
            key_total,
            value_total,
            jnp.zeros((3, DH), F32),
        ],
        axis=0,
    )


def pull(weights, inverse, attended, out_grad, content_q, position_q, keys, values, table_rev, cuts):
    parts, group, seg, cols = out_grad.shape
    rows = keys.shape[2]
    queries, key_count, heads = parts * seg, parts * rows, cols // DH
    by_head = lambda size: pl.BlockSpec((parts, None, size, DH), lambda h, s: (0, s, 0, h))
    grid_spec = pl.GridSpec(
        grid=(heads, group),
        in_specs=[
            pl.BlockSpec((None, None, queries, key_count), lambda h, s: (s, h, 0, 0)),
            pl.BlockSpec((None, None, queries, DH), lambda h, s: (s, h, 0, 0)),
            by_head(seg),
            by_head(seg),
            by_head(seg),
            by_head(seg),
            by_head(rows),
            by_head(rows),
            pl.BlockSpec((key_count, DH), lambda h, s: (0, h)),
        ],
        out_specs=[
            by_head(seg),
            by_head(rows),
            by_head(rows),
            pl.BlockSpec((None, DH, key_count), lambda h, s: (h, 0, 0)),
            pl.BlockSpec((None, 8, DH), lambda h, s: (h, 0, 0)),
        ],
        scratch_shapes=[
            pltpu.VMEM((key_count, DH), BF16),
            pltpu.VMEM((key_count, DH), BF16),
            pltpu.VMEM((queries, DH), BF16),
            pltpu.VMEM((BLOCK, key_count), F32),
            pltpu.VMEM((BLOCK, key_count), F32),
            pltpu.VMEM((BLOCK, key_count), BF16),
            pltpu.VMEM((BLOCK, key_count), BF16),
            pltpu.VMEM((DH, key_count), F32),
            pltpu.VMEM((DH, key_count), F32),
        ],
    )
    return pl.pallas_call(
        functools.partial(pull_kernel, cuts),
        grid_spec=grid_spec,
        out_shape=[
            jax.ShapeDtypeStruct((parts, group, seg, cols), BF16),
            jax.ShapeDtypeStruct((parts, group, rows, cols), BF16),
            jax.ShapeDtypeStruct((parts, group, rows, cols), BF16),
            jax.ShapeDtypeStruct((heads, DH, key_count), F32),
            jax.ShapeDtypeStruct((heads, 8, DH), F32),
        ],
        compiler_params=pltpu.CompilerParams(
            dimension_semantics=("arbitrary", "arbitrary"), vmem_limit_bytes=50 * 2**20
        ),
        cost_estimate=cost(39),
        name="pull",
    )(weights, inverse, attended, out_grad, content_q, position_q, keys, values, table_rev)


def project_kernel(cut, rows_ref, gain_ref, shift_ref, w_ref, n_ref, ns_ref, q_ref, k_ref, v_ref):
    rows, width = rows_ref.shape
    cols = k_ref.shape[1]
    step = 64 if rows % 64 == 0 else 32
    for low in range(0, rows, step):
        wide = rows_ref[low : low + step, :].astype(F32)
        centred = wide - jnp.mean(wide, axis=1, keepdims=True)
        rate = lax.rsqrt(jnp.mean(centred * centred, axis=1, keepdims=True) + EPSILON)
        normed = (centred * rate * gain_ref[...] + shift_ref[...]).astype(BF16)
        n_ref[low : low + step, :] = normed
    ns_ref[...] = n_ref[cut:, :]
    q_ref[...] = mm(n_ref[cut:, :], w_ref[:, :cols], NN)
    k_ref[...] = mm(n_ref[...], w_ref[:, cols : 2 * cols], NN).astype(BF16)
    v_ref[...] = mm(n_ref[...], w_ref[:, 2 * cols : 3 * cols], NN).astype(BF16)


def project(rows_all, gain, shift, columns, cut):
    parts, group, each, width = rows_all.shape
    cols = columns.shape[1] // 4
    seg = each - cut
    block = lambda size, wide: pl.BlockSpec((None, None, size, wide), lambda p, s: (p, s, 0, 0))
    whole = lambda *shape: pl.BlockSpec(shape, lambda p, s: (0,) * len(shape))
    shape = lambda size, wide, kind: jax.ShapeDtypeStruct((parts, group, size, wide), kind)
    return pl.pallas_call(
        functools.partial(project_kernel, cut),
        grid_spec=pl.GridSpec(
            grid=(parts, group),
            in_specs=[
                block(each, width),
                whole(1, width),
                whole(1, width),
                whole(width, 4 * cols),
            ],
            out_specs=[
                block(each, width),
                block(seg, width),
                block(seg, cols),
                block(each, cols),
                block(each, cols),
            ],
        ),
        out_shape=[
            shape(each, width, BF16),
            shape(seg, width, BF16),
            shape(seg, cols, F32),
            shape(each, cols, BF16),
            shape(each, cols, BF16),
        ],
        compiler_params=pltpu.CompilerParams(
            dimension_semantics=("arbitrary", "arbitrary"), vmem_limit_bytes=40 * 2**20
        ),
        cost_estimate=cost(17),
        name="project",
    )(rows_all, gain, shift, columns)


def gelu_both(x):
    near = jnp.abs(x)
    t = 1.0 / (1.0 + (0.3275911 * math.sqrt(0.5)) * near)
    bell = jnp.exp2((x * x) * (-0.5 * LOG2E))
    tail = 0.5 * 1.061405429
    for factor in (-1.453152027, 1.421413741, -0.284496736, 0.254829592):
        tail = tail * t + 0.5 * factor
    tail = tail * t * bell
    below = jnp.where(x < 0.0, tail, 1.0 - tail)
    return x * below, below + x * bell * (1.0 / math.sqrt(2.0 * math.pi))


def forward_back_kernel(
    last, n_ref, c_ref, up_ref, down_ref, shift_ref, *rest,
):
    if last:
        part_in, grad_in, part_out, part_far, grad_out, grad_far, late_ref, sums_ref = rest[:8]
        pre, slope, hidden, act, up_out, down_out, sems, part_ref, grad_ref = rest[8:]
    else:
        part_ref, grad_ref, late_ref, sums_ref = rest[:4]
        pre, slope, hidden, act, up_out, down_out, sems = rest[4:]
    tile = pl.program_id(0)
    tiles = pl.num_programs(0)
    parts, cols, units = up_ref.shape
    width = parts * cols
    rows = n_ref.shape[0]
    slot = lax.rem(tile, 2)
    up_weight = up_ref[...].reshape(width, units)
    down_weight = down_ref[...]

    def copies(at, index):
        return (
            pltpu.make_async_copy(
                up_out.at[at],
                late_ref.at[:, pl.ds(0, cols), pl.ds(pl.multiple_of(index * units, units), units)],
                sems.at[at, 0],
            ),
            pltpu.make_async_copy(
                down_out.at[at], late_ref.at[index, pl.ds(cols, units), :], sems.at[at, 1]
            ),
        )

    @pl.when(tile == 0)
    def _():
        if last:
            part_ref[...] = part_in[...]
            grad_ref[...] = grad_in[...]
        else:
            part_ref[...] = jnp.zeros_like(part_ref)
            grad_ref[...] = jnp.zeros_like(grad_ref)

    pre[...] = mm(n_ref[...], up_weight, NN)
    slope[...] = mm(c_ref[...], down_weight, NT)
    step = 64
    for low in range(0, rows, step):
        value, change = gelu_both(pre[low : low + step, :] + shift_ref[...])
        hidden[low : low + step, :] = value.astype(BF16)
        act[low : low + step, :] = (change * slope[low : low + step, :]).astype(BF16)
    part_ref[...] += mm(hidden[...], down_weight, NN)
    grad_ref[...] += mm(act[...], up_weight, NT)
    sums_ref[...] = jnp.sum(act[...].astype(F32), axis=0, keepdims=True)

    @pl.when(tile >= 2)
    def _():
        for copy in copies(slot, tile - 2):
            copy.wait()

    up_out[slot] = mm(n_ref[...], act[...], TN).astype(BF16).reshape(parts, cols, units)
    down_out[slot] = mm(hidden[...], c_ref[...], TN).astype(BF16)
    for copy in copies(slot, tile):
        copy.start()

    @pl.when(tile == tiles - 1)
    def _():
        if last:
            part_out[...] = part_ref[: rows // 2, :]
            part_far[...] = part_ref[rows // 2 :, :].astype(BF16)
            grad_out[...] = grad_ref[: rows // 2, :]
            grad_far[...] = grad_ref[rows // 2 :, :].astype(BF16)
        for copy in copies(1 - slot, tile - 1) + copies(slot, tile):
            copy.wait()


def forward_back(normed, cot, gathered, shift, carry):
    parts, _, width = gathered.shape
    rows = normed.shape[0]
    cols = width // parts
    units = shift.shape[1] // parts
    last = len(carry) > 0
    one = pl.Buffered(1)
    whole = lambda *shape: pl.BlockSpec(shape, lambda t: (0,) * len(shape), pipeline_mode=one)
    if last:
        sums = [((rows // 2, width), F32), ((rows // 2, width), BF16)] * 2
    else:
        sums = [((rows, width), F32)] * 2
    return pl.pallas_call(
        functools.partial(forward_back_kernel, last),
        grid_spec=pl.GridSpec(
            grid=(parts,),
            in_specs=[
                whole(rows, width),
                whole(rows, width),
                pl.BlockSpec((parts, cols, units), lambda t: (0, 0, t)),
                pl.BlockSpec((None, units, width), lambda t: (t, cols // units, 0)),
                pl.BlockSpec((1, units), lambda t: (0, t)),
            ]
            + [whole(rows, width) for _ in carry],
            out_specs=[whole(*shape) for shape, _ in sums]
            + [
                pl.BlockSpec(memory_space=pl.ANY),
                pl.BlockSpec((1, units), lambda t: (0, t)),
            ],
            scratch_shapes=[
                pltpu.VMEM((rows, units), F32),
                pltpu.VMEM((rows, units), F32),
                pltpu.VMEM((rows, units), BF16),
                pltpu.VMEM((rows, units), BF16),
                pltpu.VMEM((2, parts, cols, units), BF16),
                pltpu.VMEM((2, units, width), BF16),
                pltpu.SemaphoreType.DMA((2, 2)),
            ]
            + [pltpu.VMEM((rows, width), F32) for _ in carry],
        ),
        out_shape=[jax.ShapeDtypeStruct(shape, kind) for shape, kind in sums]
        + [
            jax.ShapeDtypeStruct((parts, cols + units, width), BF16),
            jax.ShapeDtypeStruct((1, parts * units), F32),
        ],
        compiler_params=pltpu.CompilerParams(
            dimension_semantics=("arbitrary",), vmem_limit_bytes=56 * 2**20
        ),
        cost_estimate=cost(29),
        name="forward_back",
    )(normed, cot, gathered, gathered, shift, *carry)


def leave_kernel(a_ref, s_ref, w_ref, shift_ref, gain_ref, bias_ref, flat_ref, m_ref, n_ref):
    parts = a_ref.shape[0]
    flat_ref[...] = jnp.concatenate([a_ref[part] for part in range(parts)], axis=1)
    weight = w_ref[...].reshape(flat_ref.shape[1], flat_ref.shape[1])
    m_ref[...] = s_ref[...].astype(F32) + (mm(flat_ref[...], weight, NN) + shift_ref[...])
    step = 32
    for low in range(0, m_ref.shape[0], step):
        unit, _ = standardise(m_ref[low : low + step, :])
        n_ref[low : low + step, :] = (unit * gain_ref[...] + bias_ref[...]).astype(BF16)


def leave(mixed_heads, segment, base, gathered, shift, gain, bias):
    parts, group, seg, cols = mixed_heads.shape
    width = parts * cols
    at = gathered.shape[1] // cols - 1
    rows = lambda: pl.BlockSpec((None, seg, width), lambda s: (s, 0, 0))
    vector = lambda: pl.BlockSpec((1, width), lambda s: (0, 0))
    shape = lambda kind: jax.ShapeDtypeStruct((group, seg, width), kind)
    return pl.pallas_call(
        leave_kernel,
        grid_spec=pl.GridSpec(
            grid=(group,),
            in_specs=[
                pl.BlockSpec((parts, None, seg, cols), lambda s: (0, s, 0, 0)),
                pl.BlockSpec((None, seg, width), lambda s: (s + base, 0, 0)),
                pl.BlockSpec((parts, cols, width), lambda s: (0, at, 0)),
                vector(),
                vector(),
                vector(),
            ],
            out_specs=[rows(), rows(), rows()],
        ),
        out_shape=[shape(BF16), shape(F32), shape(BF16)],
        compiler_params=pltpu.CompilerParams(vmem_limit_bytes=32 * 2**20),
        cost_estimate=cost(6),
        name="leave",
    )(mixed_heads, segment, gathered, shift, gain, bias)


def enter_kernel(
    m_ref, g_ref, far_ref, c_ref, w_ref, gain_ref, mg_ref, b_ref, a_ref, sums_ref
):
    @pl.when(pl.program_id(0) == 0)
    def _():
        sums_ref[...] = jnp.zeros_like(sums_ref)

    parts = a_ref.shape[0]
    rows, width = m_ref.shape
    step = 32
    total = [jnp.zeros((1, width), F32) for _ in range(4)]
    for low in range(0, rows, step):
        at = slice(low, low + step)
        unit, rate = standardise(m_ref[at, :])
        grad = g_ref[at, :] + far_ref[at, :].astype(F32)
        cot = c_ref[at, :].astype(F32)
        middle_grad = cot + standardise_back(unit, rate, grad, gain_ref[...])
        branch = middle_grad.astype(BF16)
        mg_ref[at, :] = middle_grad
        b_ref[at, :] = branch
        for i, value in enumerate((branch.astype(F32), grad * unit, grad, cot)):
            total[i] = total[i] + jnp.sum(value, axis=0, keepdims=True)
    sums_ref[...] += jnp.concatenate(total + [jnp.zeros((4, width), F32)], axis=0)
    for part in range(parts):
        a_ref[part] = mm(b_ref[...], w_ref[part], NT).astype(BF16)


def enter(middle, grad, far, cot, base, gathered, gain):
    group, seg, width = middle.shape
    parts = gathered.shape[0]
    cols = width // parts
    at = gathered.shape[1] // cols - 1
    rows = lambda: pl.BlockSpec((None, seg, width), lambda s: (s, 0, 0))
    later = lambda: pl.BlockSpec((None, seg, width), lambda s: (s + base, 0, 0))
    shape = lambda kind: jax.ShapeDtypeStruct((group, seg, width), kind)
    return pl.pallas_call(
        enter_kernel,
        grid_spec=pl.GridSpec(
            grid=(group,),
            in_specs=[
                rows(),
                later(),
                later(),
                later(),
                pl.BlockSpec((parts, cols, width), lambda s: (0, at, 0)),
                pl.BlockSpec((1, width), lambda s: (0, 0)),
            ],
            out_specs=[
                rows(),
                rows(),
                pl.BlockSpec((parts, None, seg, cols), lambda s: (0, s, 0, 0)),
                pl.BlockSpec((8, width), lambda s: (0, 0)),
            ],
        ),
        out_shape=[
            shape(F32),
            shape(BF16),
            jax.ShapeDtypeStruct((parts, group, seg, cols), BF16),
            jax.ShapeDtypeStruct((8, width), F32),
        ],
        compiler_params=pltpu.CompilerParams(
            dimension_semantics=("arbitrary",), vmem_limit_bytes=32 * 2**20
        ),
        cost_estimate=cost(7),
        name="enter",
    )(middle, grad, far, cot, gathered, gain)


def compress_kernel(low, rows_ref, w_ref, shift_ref, out_ref, wide):
    count = out_ref.shape[0]
    cols = out_ref.shape[1]
    blocks = wide.shape[0]
    for at in range(blocks):
        wide[at] = rows_ref[low : low + 3 * count, at * LANES : (at + 1) * LANES].astype(F32)
    total = jnp.broadcast_to(shift_ref[...], (count, cols))
    for k in range(3):
        every = jnp.concatenate(
            [wide[at, pl.ds(k, count, stride=3), :] for at in range(blocks)], axis=1
        ).astype(BF16)
        total = total + mm(every, w_ref[:, k * cols : (k + 1) * cols], NN)
    out_ref[...] = total.astype(BF16)


def compress(rows_all, columns, shift, low, count):
    parts, group, each, width = rows_all.shape
    cols = columns.shape[1] // 3
    return pl.pallas_call(
        functools.partial(compress_kernel, low),
        grid_spec=pl.GridSpec(
            grid=(parts, group),
            in_specs=[
                pl.BlockSpec((None, None, each, width), lambda p, s: (p, s, 0, 0)),
                pl.BlockSpec((width, 3 * cols), lambda p, s: (0, 0)),
                pl.BlockSpec((1, cols), lambda p, s: (0, 0)),
            ],
            out_specs=pl.BlockSpec((None, None, count, cols), lambda p, s: (p, s, 0, 0)),
            scratch_shapes=[pltpu.VMEM((width // LANES, 3 * count, LANES), F32)],
        ),
        out_shape=jax.ShapeDtypeStruct((parts, group, count, cols), BF16),
        compiler_params=pltpu.CompilerParams(
            dimension_semantics=("arbitrary", "arbitrary"), vmem_limit_bytes=32 * 2**20
        ),
        cost_estimate=cost(6.5),
        name="compress",
    )(rows_all, columns, shift)


def lay_out_kernel(
    parts, unit_cols, core_ref, a_ref, b_ref, c_ref, d_ref, e_ref, f_ref, up_ref, down_ref, out_ref
):
    out_ref[...] = e_ref[...].astype(F32) + f_ref[...].astype(F32)
    flipped = core_ref[0] == 1
    for half, (mine_ref, far_ref) in enumerate(((a_ref, c_ref), (b_ref, d_ref))):
        mine, far = mine_ref[...].astype(F32), far_ref[...].astype(F32)
        for core, value in enumerate(
            (jnp.where(flipped, far, mine), jnp.where(flipped, mine, far))
        ):
            for part in range(parts):
                at = ((part * 2 + core) * 2 + half) * unit_cols
                up_ref[:, at : at + unit_cols] = value[
                    0, :, part * unit_cols : (part + 1) * unit_cols
                ]
            down_ref[2 * core + half] = value[1]


def lay_out(core, mine, far, parts):
    _, rows, width = mine.shape
    step = rows // 4 if rows % 64 == 0 else rows
    half = lambda i: pl.BlockSpec((2, step, width), lambda r, *_, i=i: (i, r, 0))
    final = lambda: pl.BlockSpec((None, step, width), lambda r, *_: (4, r, 0))
    return pl.pallas_call(
        functools.partial(lay_out_kernel, parts, rows),
        grid_spec=pltpu.PrefetchScalarGridSpec(
            num_scalar_prefetch=1,
            grid=(rows // step,),
            in_specs=[half(0), half(1), half(0), half(1), final(), final()],
            out_specs=[
                pl.BlockSpec((step, 4 * width), lambda r, *_: (r, 0)),
                pl.BlockSpec((4, step, width), lambda r, *_: (0, r, 0)),
                pl.BlockSpec((step, width), lambda r, *_: (r, 0)),
            ],
        ),
        out_shape=[
            jax.ShapeDtypeStruct((rows, 4 * width), F32),
            jax.ShapeDtypeStruct((4, rows, width), F32),
            jax.ShapeDtypeStruct((rows, width), F32),
        ],
        compiler_params=pltpu.CompilerParams(vmem_limit_bytes=32 * 2**20),
        cost_estimate=cost(4),
        name="lay_out",
    )(core.reshape(1), mine, mine, far, far, mine, far)


def lay_squares_kernel(in_ref, *out_refs):
    parts = in_ref.shape[0]
    cols = in_ref.shape[2] // len(out_refs)
    for at, out_ref in enumerate(out_refs):
        for part in range(parts):
            out_ref[:, part * cols : (part + 1) * cols] = in_ref[
                part, :, at * cols : (at + 1) * cols
            ].astype(F32)


def lay_squares(summed, rows):
    parts, _, wide = summed.shape
    width = parts * wide // 4
    step = rows // 2
    return pl.pallas_call(
        lay_squares_kernel,
        grid_spec=pl.GridSpec(
            grid=(2,),
            in_specs=[pl.BlockSpec((parts, step, wide), lambda i: (0, i, 0))],
            out_specs=[pl.BlockSpec((step, width), lambda i: (i, 0)) for _ in range(4)],
        ),
        out_shape=[jax.ShapeDtypeStruct((rows, width), F32) for _ in range(4)],
        compiler_params=pltpu.CompilerParams(vmem_limit_bytes=32 * 2**20),
        cost_estimate=cost(2.5),
        name="lay_squares",
    )(summed)


def standardise(rows):
    mean = jnp.mean(rows, axis=-1, keepdims=True)
    centred = rows - mean
    rate = lax.rsqrt(jnp.mean(centred * centred, axis=-1, keepdims=True) + EPSILON)
    return centred * rate, rate


def standardise_back(unit, rate, grad, gain):
    scaled = grad * gain
    mean = jnp.mean(scaled, axis=-1, keepdims=True)
    along = jnp.mean(scaled * unit, axis=-1, keepdims=True)
    return rate * (scaled - mean - unit * along)


def sinusoid_reversed(rows, width):
    positions = (rows - 1 - jnp.arange(rows, dtype=jnp.int32)).astype(F32)[:, None]
    frequency = jnp.exp(
        jnp.arange(width // 2, dtype=F32) * (-2.0 * math.log(10000.0) / width)
    )
    angles = positions * frequency[None, :]
    return jnp.concatenate([jnp.sin(angles), jnp.cos(angles)], axis=1).astype(BF16)


def dot(left, right):
    return mm(left, right, NN)


def swap(value):
    return lax.ppermute(value, "core", [(0, 1), (1, 0)])


def exchange(blocks):
    parts = blocks.shape[0]
    me = lax.axis_index("seq")
    out = [lax.dynamic_index_in_dim(blocks, me, 0, keepdims=False)]
    for apart in range(1, parts):
        sent = lax.dynamic_index_in_dim(blocks, me ^ apart, 0, keepdims=False)
        out.append(lax.ppermute(sent, "seq", [(i, i ^ apart) for i in range(parts)]))
    return out


def add_up(arrays, kind=BF16):
    total = arrays[0].astype(F32)
    for array in arrays[1:]:
        total = total + array.astype(F32)
    return total.astype(kind)


def body(
    segment, memory, compressed, eob, reset, ln1_gain, ln1_bias, w_query, w_key, w_value,
    w_out, out_bias, w_rel, bias_content, bias_position, ln2_gain, ln2_bias, w_up, up_bias,
    w_down, down_bias, conv_weight, conv_bias, cotangent,
):
    parts = lax.axis_size("seq")
    core = lax.axis_index("core")
    me = lax.axis_index("seq")
    group, seg, width = segment.shape
    mem, old = memory.shape[1], compressed.shape[1]
    cuts = (old, mem, seg)
    each = old + mem + seg
    keys_in_all = parts * each
    cols = width // parts
    wide = 4 * cols
    own = group * seg
    unit_cols = w_up.shape[1] // (4 * parts)
    barrier = lax.optimization_barrier

    def by_columns(matrices):
        count = matrices.shape[0]
        sent = matrices.reshape(count, cols, parts, cols).transpose(2, 1, 0, 3)
        return sent.reshape(parts, cols, count * cols)

    up_bias_own = lax.dynamic_slice_in_dim(up_bias, core * 2 * unit_cols, 2 * unit_cols, 0)
    vectors = jnp.concatenate(
        [ln1_gain, ln1_bias, out_bias, ln2_gain, ln2_bias, down_bias, up_bias_own]
    )
    vectors = jnp.pad(vectors.reshape(2, wide), ((0, 14), (0, 0)))
    sent = jnp.concatenate(
        [
            by_columns(jnp.stack([w_query, w_key, w_value, w_rel])),
            jnp.broadcast_to(vectors, (parts, 16, wide)),
        ],
        axis=1,
    )
    got = lax.all_to_all(sent, "seq", 0, 0, tiled=True)
    cut = max(group - 1, 1)
    spans = [(0, cut), (cut, group)] if cut < group else [(0, group)]
    local = [
        jnp.concatenate([compressed[low:high], memory[low:high], segment[low:high]], axis=1)
        for low, high in spans
    ]
    rows_all = [lax.all_gather(local[0], "seq")]
    columns = got[:, :cols].reshape(width, wide)
    vectors = got[:, cols : cols + 2].reshape(parts, 2 * wide).astype(F32)
    gain_one, shift_one, out_shift, gain_two, shift_two, down_shift = (
        vectors[:, cols * i : cols * (i + 1)].reshape(1, width) for i in range(6)
    )
    up_shift = vectors[:, 6 * cols :].reshape(parts, 2, unit_cols).transpose(1, 0, 2)
    up_shift = up_shift.reshape(2, 1, parts * unit_cols)
    up_quarters = lax.dynamic_slice_in_dim(
        w_up.reshape(cols, parts, 2, 2, unit_cols), core, 1, 2
    ).reshape(cols, parts, 2, unit_cols)
    up_quarters = [up_quarters[:, :, i].reshape(cols, width) for i in range(2)]
    down_half = lax.dynamic_slice_in_dim(w_down, core * 2 * unit_cols, 2 * unit_cols, 0)
    down_quarters = [down_half[unit_cols * i : unit_cols * (i + 1)] for i in range(2)]
    first = jnp.concatenate([up_quarters[0], down_quarters[0], w_out], axis=0)
    second = jnp.concatenate([up_quarters[1], down_quarters[1]], axis=0)
    cot_own = cotangent.reshape(own, width)
    cot_both = jnp.concatenate([cot_own, swap(cot_own)], axis=0)

    table_rev = sinusoid_reversed(keys_in_all, width)
    proj_rev = dot(table_rev, columns[:, 3 * cols :]).astype(BF16)
    index = jnp.arange(eob.shape[1], dtype=jnp.int32)[None, :]
    opens = jnp.pad(eob, ((0, 0), (1, 0)))[:, :-1] == 1
    start = lax.cummax(jnp.where(opens, index, 0), axis=1)
    shade = jnp.where((start == 0) & (reset[:, None] == 0), 0.0, MASKED)
    info = jnp.stack([start.astype(F32), shade], axis=2)
    info = jnp.pad(info, ((0, 0), (0, 0), (0, LANES - 2)))
    rows_all[0], proj_rev, info, cot_both, table_rev, columns, *local = barrier(
        (rows_all[0], proj_rev, info, cot_both, table_rev, columns, *local)
    )
    rows_all = [rows_all[0]] + [lax.all_gather(rows, "seq") for rows in local[1:]]

    normed, normed_seg, kept, heads = [], [], [], []
    for batch, (low, high) in enumerate(spans):
        if batch == len(spans) - 1:
            rows_all[batch], first, *heads = barrier((rows_all[batch], first, *heads))
            first = lax.all_gather(first, "seq")
        normed_batch, seg_batch, query, keys, values = project(
            rows_all[batch], gain_one, shift_one, columns, old + mem
        )
        if batch == len(spans) - 1:
            second, query = barrier((second, query))
            second = lax.all_gather(second, "seq")
        weights, inverse, mixed_heads, content_q, position_q = attend(
            query,
            bias_content.astype(F32).reshape(1, cols),
            bias_position.astype(F32).reshape(1, cols),
            keys,
            values,
            proj_rev,
            info[low:high],
            cuts,
        )
        normed.append(normed_batch)
        normed_seg.append(seg_batch)
        kept.append((weights, inverse, mixed_heads, content_q, position_q, keys, values))
        heads.append(lax.all_to_all(mixed_heads, "seq", 0, 0, tiled=True))
    conv_sent, *heads = barrier((by_columns(conv_weight), *heads))
    conv_columns = lax.all_to_all(conv_sent, "seq", 0, 0, tiled=True)

    attended, middle, normed_two = [], [], []
    for (low, high), batch in zip(spans, heads):
        one, two, three = leave(batch, segment, low, first, out_shift, gain_two, shift_two)
        attended.append(one.reshape(-1, width))
        middle.append(two)
        normed_two.append(three.reshape(-1, width))
    both = jnp.concatenate(normed_two + [swap(rows) for rows in normed_two], axis=0)
    part, part_grad, late_one, unit_one = forward_back(both, cot_both, first, up_shift[0], ())
    early = lax.psum_scatter(
        late_one.reshape(-1, width), "seq", scatter_dimension=0, tiled=True
    )
    part, part_far, part_grad, grad_far, late_two, unit_two = forward_back(
        both, cot_both, second, up_shift[1], (part, part_grad)
    )
    conv_columns, grad_far = barrier((conv_columns, grad_far))
    grad_far = swap(grad_far)
    by_stream = lambda rows: rows.reshape(group, seg, width)
    middle_grad, branch_grad, head_grad, sums_two = [], [], [], 0.0
    for (low, high), batch in zip(spans, middle):
        one, two, three, four = enter(
            batch, by_stream(part_grad), by_stream(grad_far), cotangent, low, first, gain_two
        )
        middle_grad.append(one)
        branch_grad.append(two.reshape(-1, width))
        three, part_grad = barrier((three, part_grad))
        head_grad.append(lax.all_to_all(three, "seq", 0, 0, tiled=True))
        sums_two = sums_two + four
    late_two, branch_grad[-1] = barrier((late_two, branch_grad[-1]))
    late_two = exchange(late_two)
    out_grad = mm(jnp.concatenate(attended), jnp.concatenate(branch_grad), TN)
    out_grad = exchange(out_grad.astype(BF16).reshape(parts, cols, width))
    result = part + swap(part_far).astype(F32) + down_shift
    output = (jnp.concatenate(middle).reshape(own, width) + result).astype(BF16)
    output = output.reshape(group, seg, width)

    query_w, key_w, value_w, table_grad, sums, seg_parts = 0.0, 0.0, 0.0, 0.0, 0.0, []
    for batch, (low, high) in enumerate(spans):
        weights, inverse, mixed_heads, content_q, position_q, keys, values = kept[batch]
        query_grad, key_grad, value_grad, table_part, sums_part = pull(
            weights, inverse, mixed_heads, head_grad[batch], content_q, position_q, keys, values,
            proj_rev, cuts,
        )
        if batch == 0:
            early, late_two, out_grad, query_grad = barrier((early, late_two, out_grad, query_grad))
            ff = jnp.concatenate([early, add_up(late_two), add_up(out_grad)], axis=0)
            ff, head_grad[-1] = barrier((ff, head_grad[-1]))
            ff = lax.psum(ff, "z")
        table_grad = table_grad + table_part
        sums = sums + sums_part
        flat = lambda rows: rows.reshape(-1, rows.shape[-1])
        query_w = query_w + mm(flat(normed_seg[batch]), flat(query_grad), TN)
        key_w = key_w + mm(flat(normed[batch]), flat(key_grad), TN)
        value_w = value_w + mm(flat(normed[batch]), flat(value_grad), TN)
        seg_grads = jnp.concatenate(
            [query_grad, key_grad[:, :, old + mem :], value_grad[:, :, old + mem :]], axis=3
        )
        seg_part = mm(flat(seg_grads), columns[:, : 3 * cols], NT)
        seg_parts.append(seg_part.astype(BF16).reshape(parts, -1, width))
    conv_columns, query_grad = barrier((conv_columns, query_grad))
    packed = [
        compress(
            rows, conv_columns.reshape(width, 3 * cols), conv_bias.astype(F32).reshape(1, cols),
            old, mem // 3,
        )
        for rows in rows_all
    ]
    packed = lax.all_to_all(jnp.concatenate(packed, axis=1), "seq", 0, 0, tiled=True)
    new_compressed = packed.transpose(1, 2, 0, 3).reshape(group, mem // 3, width)

    rel_w = mm(table_rev, table_grad.reshape(cols, keys_in_all).astype(BF16), ((0,), (1,)))
    sums = sums.transpose(1, 0, 2).reshape(8, cols)
    weight_cols = columns[:, : 3 * cols].astype(F32)
    row_sums = sums[2:5].reshape(1, 3 * cols)
    three = jnp.concatenate([query_w, key_w, value_w], axis=1)
    shift_one_grad = jnp.sum(weight_cols * row_sums, axis=1)
    gain_one_grad = jnp.sum(
        weight_cols * (three - shift_one.reshape(width, 1) * row_sums), axis=1
    ) / gain_one.reshape(width)
    out_shift_grad, gain_two_grad, shift_two_grad, down_shift_grad = (
        sums_two[i] for i in range(4)
    )
    chunk = lambda vector: vector.reshape(parts, cols)
    mine = (jnp.arange(parts) == me).astype(F32)[:, None]
    unit_sums = jnp.stack(
        [unit_one.reshape(parts, unit_cols), unit_two.reshape(parts, unit_cols)], axis=1
    ).reshape(parts, 2 * unit_cols)
    small = jnp.stack(
        [
            jnp.concatenate(
                [chunk(gain_one_grad), chunk(shift_one_grad), chunk(out_shift_grad), chunk(gain_two_grad)],
                axis=1,
            ),
            jnp.concatenate(
                [chunk(shift_two_grad), chunk(down_shift_grad), mine * sums[0:1], mine * sums[1:2]],
                axis=1,
            ),
            jnp.concatenate(
                [jnp.where(core == 0, unit_sums, 0.0), jnp.where(core == 1, unit_sums, 0.0)], axis=1
            ),
        ],
        axis=1,
    )
    small = jnp.pad(small, ((0, 0), (0, 13), (0, 0))).astype(BF16)
    square_grads = jnp.concatenate([three.astype(BF16), rel_w.astype(BF16)], axis=1)
    square_grads = jnp.concatenate([square_grads.reshape(parts, cols, wide), small], axis=1)
    summed = lax.all_to_all(square_grads, "seq", 0, 0, tiled=True)
    summed, *seg_parts = barrier((summed, *seg_parts))
    seg_grad = [add_up(exchange(rows), F32) for rows in seg_parts]
    summed = lax.psum(summed, ("z", "core"))
    ff_far = swap(ff)

    seg_grad = jnp.concatenate(seg_grad, axis=0)
    unit_seg, rate_seg = standardise(segment.reshape(own, width).astype(F32))
    rows_grad = standardise_back(unit_seg, rate_seg, seg_grad, gain_one)
    segment_grad = jnp.concatenate(middle_grad, axis=0) + by_stream(rows_grad)

    up_w, down_w, out_w = lay_out(
        core, ff.reshape(5, unit_cols, width), ff_far.reshape(5, unit_cols, width), parts
    )
    down_w = down_w.reshape(4 * unit_cols, width)
    query_w, key_w, value_w, rel_w = lay_squares(summed, cols)
    small = jnp.sum(summed[:, cols : cols + 3].astype(F32), axis=0)
    piece = lambda row, i: small[row, cols * i : cols * (i + 1)]
    return (
        output,
        segment_grad,
        piece(0, 0),
        piece(0, 1),
        query_w,
        key_w,
        value_w,
        out_w,
        piece(0, 2),
        rel_w,
        piece(1, 2),
        piece(1, 3),
        piece(0, 3),
        piece(1, 0),
        up_w,
        small[2],
        down_w,
        piece(1, 1),
        new_compressed,
    )


def solution(mesh):
    dp = mesh.shape["dp"]
    cores = jax.sharding.Mesh(
        mesh.devices.reshape(dp // 2, 2, mesh.shape["seq"]), ("z", "core", "seq")
    )
    rows = P(("z", "core"), "seq", None)
    shard, matrix = P("seq"), P("seq", None)
    return jax.shard_map(
        body,
        mesh=cores,
        in_specs=(
            rows, rows, rows, P(("z", "core"), None), P(("z", "core")), shard, shard, matrix,
            matrix, matrix, matrix, shard, matrix, shard, shard, shard, shard, matrix, shard,
            matrix, shard, P(None, "seq", None), shard, rows,
        ),
        out_specs=(
            rows, rows, shard, shard, matrix, matrix, matrix, matrix, shard, matrix, shard,
            shard, shard, shard, matrix, shard, matrix, shard, rows,
        ),
        check_vma=False,
    )
```

```python
import functools
import math

import jax
import jax.numpy as jnp
from jax import lax
from jax.experimental import pallas as pl
from jax.experimental.pallas import tpu as pltpu
from jax.sharding import PartitionSpec as P

HEADS = 8
DH = 128
EPSILON = 1e-05
MASKED = -1e30
LANES = 128
BLOCK = 256
CHUNK = 16
SCALE = 1.0 / math.sqrt(DH)
LOG2E = 1.4426950408889634
BF16 = jnp.bfloat16
F32 = jnp.float32


def cost(microseconds):
    return pl.CostEstimate(flops=int(microseconds * 1.15e7), bytes_accessed=0, transcendentals=0)


def mm(left, right, dims):
    return lax.dot_general(left, right, (dims, ((), ())), preferred_element_type=F32)


NN = ((1,), (0,))
NT = ((1,), (1,))
TN = ((0,), (0,))


def lean_left(block, first_row, fill_columns):
    columns = block.shape[1] // LANES
    far = BLOCK - 1 - first_row
    whole, part = far // LANES, far % LANES
    turned = [
        pltpu.roll(
            block[:, LANES * t : LANES * (t + 1)], LANES - part, 1, stride=1, stride_axis=0
        )
        for t in range(columns)
    ]
    rows = lax.broadcasted_iota(jnp.int32, (block.shape[0], LANES), 0)
    lanes = lax.broadcasted_iota(jnp.int32, (block.shape[0], LANES), 1)
    near = lanes - rows < LANES - part
    out = []
    for t in range(fill_columns):
        a = turned[(t + whole) % columns]
        b = turned[(t + whole + 1) % columns]
        out.append(jnp.where(near, a, b))
    return jnp.concatenate(out, axis=1)


def lean_right(block, first_row):
    columns = block.shape[1] // LANES
    whole, part = first_row // LANES, first_row % LANES
    turned = [
        pltpu.roll(block[:, LANES * t : LANES * (t + 1)], part, 1, stride=1, stride_axis=0)
        for t in range(columns)
    ]
    rows = lax.broadcasted_iota(jnp.int32, (block.shape[0], LANES), 0)
    lanes = lax.broadcasted_iota(jnp.int32, (block.shape[0], LANES), 1)
    wrapped = lanes - rows < part
    out = []
    for t in range(columns):
        a = turned[(t - whole) % columns]
        b = turned[(t - whole - 1) % columns]
        out.append(jnp.where(wrapped, b, a))
    return jnp.concatenate(out, axis=1)


def flip_matrix(kind):
    rows = lax.broadcasted_iota(jnp.int32, (BLOCK, BLOCK), 0)
    lanes = lax.broadcasted_iota(jnp.int32, (BLOCK, BLOCK), 1)
    return (rows + lanes == BLOCK - 1).astype(F32).astype(kind)


def in_place_order(parts_ref, out_ref, cuts):
    parts = parts_ref.shape[0]
    low, base = 0, 0
    for size in cuts:
        for part in range(parts):
            out_ref[base + part * size : base + (part + 1) * size, :] = parts_ref[
                part, low : low + size, :
            ]
        low += size
        base += parts * size


def attend_kernel(
    cuts, q_ref, cb_ref, pb_ref, k_ref, v_ref, t_ref, info_ref,
    e_ref, inv_ref, o_ref, cq_ref, pq_ref,
    keys, values, raw, lean, mix,
):
    parts, seg, _ = q_ref.shape
    queries = parts * seg
    old = parts * (cuts[0] + cuts[1])
    in_place_order(k_ref, keys, cuts)
    in_place_order(v_ref, values, cuts)
    q = q_ref[...].reshape(queries, DH)
    content_q = (q + cb_ref[...]).astype(BF16)
    position_q = (q + pb_ref[...]).astype(BF16)
    cq_ref[...] = content_q.reshape(parts, seg, DH)
    pq_ref[...] = position_q.reshape(parts, seg, DH)
    for block in range(queries // BLOCK):
        row0 = block * BLOCK
        width = old + row0 + BLOCK
        skip = queries - BLOCK - row0
        raw[block, :, :width] = mm(content_q[row0 : row0 + BLOCK], keys[:width, :], NT)
        lean[block, :, :width] = mm(
            position_q[row0 : row0 + BLOCK], t_ref[skip : skip + width, :], NT
        )
        for chunk in range(BLOCK // CHUNK):
            r0 = chunk * CHUNK
            rows = slice(row0 + r0, row0 + r0 + CHUNK)
            turned = lean_left(lean[block, r0 : r0 + CHUNK, :width], r0, width // LANES)
            score = raw[block, r0 : r0 + CHUNK, :width] + turned
            start = info_ref[rows, 0:1].astype(jnp.int32)
            shade = info_ref[rows, 1:2]
            edge = old + row0
            past = score[:, :old]
            place = lax.broadcasted_iota(jnp.int32, (CHUNK, BLOCK), 1) + row0
            own = lax.broadcasted_iota(jnp.int32, (CHUNK, BLOCK), 0) + (row0 + r0)
            now = [jnp.where((place <= own) & (place >= start), score[:, edge:], MASKED)]
            if row0 > 0:
                before = lax.broadcasted_iota(jnp.int32, (CHUNK, row0), 1)
                now = [jnp.where(before >= start, score[:, old:edge], MASKED)] + now
            top = jnp.max(past, axis=1, keepdims=True) + shade
            for piece in now:
                top = jnp.maximum(top, jnp.max(piece, axis=1, keepdims=True))
            past = jnp.exp2((past - (top - shade)) * (SCALE * LOG2E))
            now = [jnp.exp2((piece - top) * (SCALE * LOG2E)) for piece in now]
            total = jnp.sum(past, axis=1, keepdims=True)
            for piece in now:
                total = total + jnp.sum(piece, axis=1, keepdims=True)
            inv_ref[rows, :] = jnp.broadcast_to(1.0 / total, (CHUNK, DH))
            e_ref[rows, :old] = past.astype(BF16)
            low = old
            for piece in now:
                e_ref[rows, low : low + piece.shape[1]] = piece.astype(BF16)
                low += piece.shape[1]
        mix[row0 : row0 + BLOCK, :] = mm(
            e_ref[row0 : row0 + BLOCK, :width], values[:width, :], NN
        )
    o_ref[...] = (mix[...] * inv_ref[...]).astype(BF16).reshape(parts, seg, DH)


def attend(query, content_shift, position_shift, keys, values, table_rev, info, cuts):
    parts, group, seg, cols = query.shape
    rows = keys.shape[2]
    queries, key_count, heads = parts * seg, parts * rows, cols // DH
    by_head = lambda size: pl.BlockSpec((parts, None, size, DH), lambda s, h: (0, s, 0, h))
    grid_spec = pl.GridSpec(
        grid=(group, heads),
        in_specs=[
            by_head(seg),
            pl.BlockSpec((1, DH), lambda s, h: (0, h)),
            pl.BlockSpec((1, DH), lambda s, h: (0, h)),
            by_head(rows),
            by_head(rows),
            pl.BlockSpec((key_count, DH), lambda s, h: (0, h)),
            pl.BlockSpec((None, queries, LANES), lambda s, h: (s, 0, 0)),
        ],
        out_specs=[
            pl.BlockSpec((None, None, queries, key_count), lambda s, h: (s, h, 0, 0)),
            pl.BlockSpec((None, None, queries, DH), lambda s, h: (s, h, 0, 0)),
            by_head(seg),
            by_head(seg),
            by_head(seg),
        ],
        scratch_shapes=[
            pltpu.VMEM((key_count, DH), BF16),
            pltpu.VMEM((key_count, DH), BF16),
            pltpu.VMEM((queries // BLOCK, BLOCK, key_count), F32),
            pltpu.VMEM((queries // BLOCK, BLOCK, key_count), F32),
            pltpu.VMEM((queries, DH), F32),
        ],
    )
    small = jax.ShapeDtypeStruct((parts, group, seg, cols), BF16)
    return pl.pallas_call(
        functools.partial(attend_kernel, cuts),
        grid_spec=grid_spec,
        out_shape=[
            jax.ShapeDtypeStruct((group, heads, queries, key_count), BF16),
            jax.ShapeDtypeStruct((group, heads, queries, DH), F32),
            small,
            small,
            small,
        ],
        compiler_params=pltpu.CompilerParams(
            dimension_semantics=("arbitrary", "arbitrary"), vmem_limit_bytes=50 * 2**20
        ),
        cost_estimate=cost(40),
        name="attend",
    )(query, content_shift, position_shift, keys, values, table_rev, info)


def pull_kernel(
    cuts, e_ref, inv_ref, o_ref, g_ref, cq_ref, pq_ref, k_ref, v_ref, t_ref,
    dq_ref, dk_ref, dv_ref, dt_ref, sums_ref,
    keys, values, grad, prob, part, score, lean, key_sum, value_sum,
):
    stream = pl.program_id(1)
    parts, seg, _ = g_ref.shape
    queries = parts * seg
    old = parts * (cuts[0] + cuts[1])
    in_place_order(k_ref, keys, cuts)
    in_place_order(v_ref, values, cuts)
    out_grad = g_ref[...].reshape(queries, DH).astype(F32)
    attended = o_ref[...].reshape(queries, DH).astype(F32)
    inv = inv_ref[...]
    grad[...] = (out_grad * inv).astype(BF16)
    dots = jnp.sum(out_grad * attended, axis=1, keepdims=True) * inv
    content_q = cq_ref[...].reshape(queries, DH)
    position_q = pq_ref[...].reshape(queries, DH)

    @pl.when(stream == 0)
    def _():
        dt_ref[...] = jnp.zeros_like(dt_ref)
        sums_ref[...] = jnp.zeros_like(sums_ref)

    key_sum[...] = jnp.zeros_like(key_sum)
    value_sum[...] = jnp.zeros_like(value_sum)
    content_total = jnp.zeros((1, DH), F32)
    position_total = jnp.zeros((1, DH), F32)
    query_total = jnp.zeros((1, DH), F32)
    flip = flip_matrix(BF16)
    flip_wide = flip_matrix(F32)
    turn = lambda rows: mm(flip, rows, NN).astype(BF16)
    for block in range(queries // BLOCK):
        row0 = block * BLOCK
        width = old + row0 + BLOCK
        skip = queries - BLOCK - row0
        rows = slice(row0, row0 + BLOCK)
        dots_back = lax.dot_general(
            flip_wide,
            jnp.broadcast_to(dots[rows], (BLOCK, DH)),
            (NN, ((), ())),
            precision=lax.Precision.HIGHEST,
            preferred_element_type=F32,
        )
        content_back = turn(content_q[rows])
        position_back = turn(position_q[rows])
        prob[block, :, :width] = mm(turn(grad[rows, :]), values[:width, :], NT)
        part[block, :, :width] = mm(flip, e_ref[rows, :width], NN)
        value_sum[:, :width] += mm(grad[rows, :], e_ref[rows, :width], TN)
        for chunk in range(BLOCK // CHUNK):
            r0 = chunk * CHUNK
            mean = dots_back[r0 : r0 + CHUNK, 0:1]
            change = part[block, r0 : r0 + CHUNK, :width] * (prob[block, r0 : r0 + CHUNK, :width] - mean)
            score[block, r0 : r0 + CHUNK, :width] = change.astype(BF16)
            lean[block, r0 : r0 + CHUNK, :width] = lean_right(change, r0).astype(BF16)
        content_grad = (mm(score[block, :, :width], keys[:width, :], NN) * SCALE).astype(BF16).astype(F32)
        position_grad = (
            (mm(lean[block, :, :width], t_ref[skip : skip + width, :], NN) * SCALE)
            .astype(BF16)
            .astype(F32)
        )
        query_grad = turn((content_grad + position_grad).astype(BF16))
        content_total += jnp.sum(content_grad, axis=0, keepdims=True)
        position_total += jnp.sum(position_grad, axis=0, keepdims=True)
        query_total += jnp.sum(query_grad.astype(F32), axis=0, keepdims=True)
        low = row0
        while low < row0 + BLOCK:
            part_at, part_row = low // seg, low % seg
            size = min(seg - part_row, row0 + BLOCK - low)
            dq_ref[part_at, part_row : part_row + size, :] = query_grad[
                low - row0 : low - row0 + size
            ]
            low += size
        key_sum[:, :width] += mm(content_back, score[block, :, :width], TN)
        dt_ref[:, skip : skip + width] += mm(position_back, lean[block, :, :width], TN) * SCALE
    key_rows = (key_sum[...] * SCALE).T.astype(BF16)
    value_rows = value_sum[...].T.astype(BF16)
    low, base = 0, 0
    for size in cuts:
        for at in range(parts):
            span = slice(base + at * size, base + (at + 1) * size)
            dk_ref[at, low : low + size, :] = key_rows[span]
            dv_ref[at, low : low + size, :] = value_rows[span]
        low += size
        base += parts * size
    key_total = jnp.sum(key_rows.astype(F32), axis=0, keepdims=True)
    value_total = jnp.sum(value_rows.astype(F32), axis=0, keepdims=True)
    sums_ref[...] += jnp.concatenate(
        [
            content_total,
            position_total,
            query_total,
            key_total,
            value_total,
            jnp.zeros((3, DH), F32),
        ],
        axis=0,
    )


def pull(weights, inverse, attended, out_grad, content_q, position_q, keys, values, table_rev, cuts):
    parts, group, seg, cols = out_grad.shape
    rows = keys.shape[2]
    queries, key_count, heads = parts * seg, parts * rows, cols // DH
    by_head = lambda size: pl.BlockSpec((parts, None, size, DH), lambda h, s: (0, s, 0, h))
    grid_spec = pl.GridSpec(
        grid=(heads, group),
        in_specs=[
            pl.BlockSpec((None, None, queries, key_count), lambda h, s: (s, h, 0, 0)),
            pl.BlockSpec((None, None, queries, DH), lambda h, s: (s, h, 0, 0)),
            by_head(seg),
            by_head(seg),
            by_head(seg),
            by_head(seg),
            by_head(rows),
            by_head(rows),
            pl.BlockSpec((key_count, DH), lambda h, s: (0, h)),
        ],
        out_specs=[
            by_head(seg),
            by_head(rows),
            by_head(rows),
            pl.BlockSpec((None, DH, key_count), lambda h, s: (h, 0, 0)),
            pl.BlockSpec((None, 8, DH), lambda h, s: (h, 0, 0)),
        ],
        scratch_shapes=[
            pltpu.VMEM((key_count, DH), BF16),
            pltpu.VMEM((key_count, DH), BF16),
            pltpu.VMEM((queries, DH), BF16),
            pltpu.VMEM((queries // BLOCK, BLOCK, key_count), F32),
            pltpu.VMEM((queries // BLOCK, BLOCK, key_count), F32),
            pltpu.VMEM((queries // BLOCK, BLOCK, key_count), BF16),
            pltpu.VMEM((queries // BLOCK, BLOCK, key_count), BF16),
            pltpu.VMEM((DH, key_count), F32),
            pltpu.VMEM((DH, key_count), F32),
        ],
    )
    return pl.pallas_call(
        functools.partial(pull_kernel, cuts),
        grid_spec=grid_spec,
        out_shape=[
            jax.ShapeDtypeStruct((parts, group, seg, cols), BF16),
            jax.ShapeDtypeStruct((parts, group, rows, cols), BF16),
            jax.ShapeDtypeStruct((parts, group, rows, cols), BF16),
            jax.ShapeDtypeStruct((heads, DH, key_count), F32),
            jax.ShapeDtypeStruct((heads, 8, DH), F32),
        ],
        compiler_params=pltpu.CompilerParams(
            dimension_semantics=("arbitrary", "arbitrary"), vmem_limit_bytes=50 * 2**20
        ),
        cost_estimate=cost(39),
        name="pull",
    )(weights, inverse, attended, out_grad, content_q, position_q, keys, values, table_rev)


def project_kernel(cut, rows_ref, gain_ref, shift_ref, w_ref, n_ref, ns_ref, q_ref, k_ref, v_ref):
    rows, width = rows_ref.shape
    cols = k_ref.shape[1]
    step = 64 if rows % 64 == 0 else 32
    for low in range(0, rows, step):
        wide = rows_ref[low : low + step, :].astype(F32)
        centred = wide - jnp.mean(wide, axis=1, keepdims=True)
        rate = lax.rsqrt(jnp.mean(centred * centred, axis=1, keepdims=True) + EPSILON)
        normed = (centred * rate * gain_ref[...] + shift_ref[...]).astype(BF16)
        n_ref[low : low + step, :] = normed
    ns_ref[...] = n_ref[cut:, :]
    q_ref[...] = mm(n_ref[cut:, :], w_ref[:, :cols], NN)
    k_ref[...] = mm(n_ref[...], w_ref[:, cols : 2 * cols], NN).astype(BF16)
    v_ref[...] = mm(n_ref[...], w_ref[:, 2 * cols : 3 * cols], NN).astype(BF16)


def project(rows_all, gain, shift, columns, cut):
    parts, group, each, width = rows_all.shape
    cols = columns.shape[1] // 4
    seg = each - cut
    block = lambda size, wide: pl.BlockSpec((None, None, size, wide), lambda p, s: (p, s, 0, 0))
    whole = lambda *shape: pl.BlockSpec(shape, lambda p, s: (0,) * len(shape))
    shape = lambda size, wide, kind: jax.ShapeDtypeStruct((parts, group, size, wide), kind)
    return pl.pallas_call(
        functools.partial(project_kernel, cut),
        grid_spec=pl.GridSpec(
            grid=(parts, group),
            in_specs=[
                block(each, width),
                whole(1, width),
                whole(1, width),
                whole(width, 4 * cols),
            ],
            out_specs=[
                block(each, width),
                block(seg, width),
                block(seg, cols),
                block(each, cols),
                block(each, cols),
            ],
        ),
        out_shape=[
            shape(each, width, BF16),
            shape(seg, width, BF16),
            shape(seg, cols, F32),
            shape(each, cols, BF16),
            shape(each, cols, BF16),
        ],
        compiler_params=pltpu.CompilerParams(
            dimension_semantics=("arbitrary", "arbitrary"), vmem_limit_bytes=40 * 2**20
        ),
        cost_estimate=cost(17),
        name="project",
    )(rows_all, gain, shift, columns)


def gelu_both(x):
    near = jnp.abs(x)
    t = 1.0 / (1.0 + (0.3275911 * math.sqrt(0.5)) * near)
    bell = jnp.exp2((x * x) * (-0.5 * LOG2E))
    tail = 0.5 * 1.061405429
    for factor in (-1.453152027, 1.421413741, -0.284496736, 0.254829592):
        tail = tail * t + 0.5 * factor
    tail = tail * t * bell
    below = jnp.where(x < 0.0, tail, 1.0 - tail)
    return x * below, below + x * bell * (1.0 / math.sqrt(2.0 * math.pi))


def forward_back_kernel(
    last, n_ref, c_ref, up_ref, down_ref, shift_ref, *rest,
):
    if last:
        part_in, grad_in, part_out, part_far, grad_out, grad_far, late_ref, sums_ref = rest[:8]
        pre, slope, hidden, act, up_out, down_out, sems, part_ref, grad_ref = rest[8:]
    else:
        part_ref, grad_ref, late_ref, sums_ref = rest[:4]
        pre, slope, hidden, act, up_out, down_out, sems = rest[4:]
    tile = pl.program_id(0)
    tiles = pl.num_programs(0)
    parts, cols, units = up_ref.shape
    width = parts * cols
    rows = n_ref.shape[0]
    slot = lax.rem(tile, 2)
    up_weight = up_ref[...].reshape(width, units)
    down_weight = down_ref[...]

    def copies(at, index):
        return (
            pltpu.make_async_copy(
                up_out.at[at],
                late_ref.at[:, pl.ds(0, cols), pl.ds(pl.multiple_of(index * units, units), units)],
                sems.at[at, 0],
            ),
            pltpu.make_async_copy(
                down_out.at[at], late_ref.at[index, pl.ds(cols, units), :], sems.at[at, 1]
            ),
        )

    @pl.when(tile == 0)
    def _():
        if last:
            part_ref[...] = part_in[...]
            grad_ref[...] = grad_in[...]
        else:
            part_ref[...] = jnp.zeros_like(part_ref)
            grad_ref[...] = jnp.zeros_like(grad_ref)

    pre[...] = mm(n_ref[...], up_weight, NN)
    slope[...] = mm(c_ref[...], down_weight, NT)
    step = 64
    for low in range(0, rows, step):
        value, change = gelu_both(pre[low : low + step, :] + shift_ref[...])
        hidden[low : low + step, :] = value.astype(BF16)
        act[low : low + step, :] = (change * slope[low : low + step, :]).astype(BF16)
    part_ref[...] += mm(hidden[...], down_weight, NN)
    grad_ref[...] += mm(act[...], up_weight, NT)
    sums_ref[...] = jnp.sum(act[...].astype(F32), axis=0, keepdims=True)

    @pl.when(tile >= 2)
    def _():
        for copy in copies(slot, tile - 2):
            copy.wait()

    up_out[slot] = mm(n_ref[...], act[...], TN).astype(BF16).reshape(parts, cols, units)
    down_out[slot] = mm(hidden[...], c_ref[...], TN).astype(BF16)
    for copy in copies(slot, tile):
        copy.start()

    @pl.when(tile == tiles - 1)
    def _():
        if last:
            part_out[...] = part_ref[: rows // 2, :]
            part_far[...] = part_ref[rows // 2 :, :].astype(BF16)
            grad_out[...] = grad_ref[: rows // 2, :]
            grad_far[...] = grad_ref[rows // 2 :, :].astype(BF16)
        for copy in copies(1 - slot, tile - 1) + copies(slot, tile):
            copy.wait()


def forward_back(normed, cot, gathered, shift, carry):
    parts, _, width = gathered.shape
    rows = normed.shape[0]
    cols = width // parts
    units = shift.shape[1] // parts
    last = len(carry) > 0
    one = pl.Buffered(1)
    whole = lambda *shape: pl.BlockSpec(shape, lambda t: (0,) * len(shape), pipeline_mode=one)
    if last:
        sums = [((rows // 2, width), F32), ((rows // 2, width), BF16)] * 2
    else:
        sums = [((rows, width), F32)] * 2
    return pl.pallas_call(
        functools.partial(forward_back_kernel, last),
        grid_spec=pl.GridSpec(
            grid=(parts,),
            in_specs=[
                whole(rows, width),
                whole(rows, width),
                pl.BlockSpec((parts, cols, units), lambda t: (0, 0, t)),
                pl.BlockSpec((None, units, width), lambda t: (t, cols // units, 0)),
                pl.BlockSpec((1, units), lambda t: (0, t)),
            ]
            + [whole(rows, width) for _ in carry],
            out_specs=[whole(*shape) for shape, _ in sums]
            + [
                pl.BlockSpec(memory_space=pl.ANY),
                pl.BlockSpec((1, units), lambda t: (0, t)),
            ],
            scratch_shapes=[
                pltpu.VMEM((rows, units), F32),
                pltpu.VMEM((rows, units), F32),
                pltpu.VMEM((rows, units), BF16),
                pltpu.VMEM((rows, units), BF16),
                pltpu.VMEM((2, parts, cols, units), BF16),
                pltpu.VMEM((2, units, width), BF16),
                pltpu.SemaphoreType.DMA((2, 2)),
            ]
            + [pltpu.VMEM((rows, width), F32) for _ in carry],
        ),
        out_shape=[jax.ShapeDtypeStruct(shape, kind) for shape, kind in sums]
        + [
            jax.ShapeDtypeStruct((parts, cols + units, width), BF16),
            jax.ShapeDtypeStruct((1, parts * units), F32),
        ],
        compiler_params=pltpu.CompilerParams(
            dimension_semantics=("arbitrary",), vmem_limit_bytes=56 * 2**20
        ),
        cost_estimate=cost(29),
        name="forward_back",
    )(normed, cot, gathered, gathered, shift, *carry)


def leave_kernel(a_ref, s_ref, w_ref, shift_ref, gain_ref, bias_ref, flat_ref, m_ref, n_ref):
    parts = a_ref.shape[0]
    flat_ref[...] = jnp.concatenate([a_ref[part] for part in range(parts)], axis=1)
    weight = w_ref[...].reshape(flat_ref.shape[1], flat_ref.shape[1])
    m_ref[...] = s_ref[...].astype(F32) + (mm(flat_ref[...], weight, NN) + shift_ref[...])
    step = 32
    for low in range(0, m_ref.shape[0], step):
        unit, _ = standardise(m_ref[low : low + step, :])
        n_ref[low : low + step, :] = (unit * gain_ref[...] + bias_ref[...]).astype(BF16)


def leave(mixed_heads, segment, base, gathered, shift, gain, bias):
    parts, group, seg, cols = mixed_heads.shape
    width = parts * cols
    at = gathered.shape[1] // cols - 1
    rows = lambda: pl.BlockSpec((None, seg, width), lambda s: (s, 0, 0))
    vector = lambda: pl.BlockSpec((1, width), lambda s: (0, 0))
    shape = lambda kind: jax.ShapeDtypeStruct((group, seg, width), kind)
    return pl.pallas_call(
        leave_kernel,
        grid_spec=pl.GridSpec(
            grid=(group,),
            in_specs=[
                pl.BlockSpec((parts, None, seg, cols), lambda s: (0, s, 0, 0)),
                pl.BlockSpec((None, seg, width), lambda s: (s + base, 0, 0)),
                pl.BlockSpec((parts, cols, width), lambda s: (0, at, 0)),
                vector(),
                vector(),
                vector(),
            ],
            out_specs=[rows(), rows(), rows()],
        ),
        out_shape=[shape(BF16), shape(F32), shape(BF16)],
        compiler_params=pltpu.CompilerParams(vmem_limit_bytes=32 * 2**20),
        cost_estimate=cost(6),
        name="leave",
    )(mixed_heads, segment, gathered, shift, gain, bias)


def enter_kernel(
    m_ref, g_ref, far_ref, c_ref, w_ref, gain_ref, mg_ref, b_ref, a_ref, sums_ref
):
    @pl.when(pl.program_id(0) == 0)
    def _():
        sums_ref[...] = jnp.zeros_like(sums_ref)

    parts = a_ref.shape[0]
    rows, width = m_ref.shape
    step = 32
    total = [jnp.zeros((1, width), F32) for _ in range(4)]
    for low in range(0, rows, step):
        at = slice(low, low + step)
        unit, rate = standardise(m_ref[at, :])
        grad = g_ref[at, :] + far_ref[at, :].astype(F32)
        cot = c_ref[at, :].astype(F32)
        middle_grad = cot + standardise_back(unit, rate, grad, gain_ref[...])
        branch = middle_grad.astype(BF16)
        mg_ref[at, :] = middle_grad
        b_ref[at, :] = branch
        for i, value in enumerate((branch.astype(F32), grad * unit, grad, cot)):
            total[i] = total[i] + jnp.sum(value, axis=0, keepdims=True)
    sums_ref[...] += jnp.concatenate(total + [jnp.zeros((4, width), F32)], axis=0)
    for part in range(parts):
        a_ref[part] = mm(b_ref[...], w_ref[part], NT).astype(BF16)


def enter(middle, grad, far, cot, base, gathered, gain):
    group, seg, width = middle.shape
    parts = gathered.shape[0]
    cols = width // parts
    at = gathered.shape[1] // cols - 1
    rows = lambda: pl.BlockSpec((None, seg, width), lambda s: (s, 0, 0))
    later = lambda: pl.BlockSpec((None, seg, width), lambda s: (s + base, 0, 0))
    shape = lambda kind: jax.ShapeDtypeStruct((group, seg, width), kind)
    return pl.pallas_call(
        enter_kernel,
        grid_spec=pl.GridSpec(
            grid=(group,),
            in_specs=[
                rows(),
                later(),
                later(),
                later(),
                pl.BlockSpec((parts, cols, width), lambda s: (0, at, 0)),
                pl.BlockSpec((1, width), lambda s: (0, 0)),
            ],
            out_specs=[
                rows(),
                rows(),
                pl.BlockSpec((parts, None, seg, cols), lambda s: (0, s, 0, 0)),
                pl.BlockSpec((8, width), lambda s: (0, 0)),
            ],
        ),
        out_shape=[
            shape(F32),
            shape(BF16),
            jax.ShapeDtypeStruct((parts, group, seg, cols), BF16),
            jax.ShapeDtypeStruct((8, width), F32),
        ],
        compiler_params=pltpu.CompilerParams(
            dimension_semantics=("arbitrary",), vmem_limit_bytes=32 * 2**20
        ),
        cost_estimate=cost(7),
        name="enter",
    )(middle, grad, far, cot, gathered, gain)


def compress_kernel(low, rows_ref, w_ref, shift_ref, out_ref, wide):
    count = out_ref.shape[0]
    cols = out_ref.shape[1]
    blocks = wide.shape[0]
    for at in range(blocks):
        wide[at] = rows_ref[low : low + 3 * count, at * LANES : (at + 1) * LANES].astype(F32)
    total = jnp.broadcast_to(shift_ref[...], (count, cols))
    for k in range(3):
        every = jnp.concatenate(
            [wide[at, pl.ds(k, count, stride=3), :] for at in range(blocks)], axis=1
        ).astype(BF16)
        total = total + mm(every, w_ref[:, k * cols : (k + 1) * cols], NN)
    out_ref[...] = total.astype(BF16)


def compress(rows_all, columns, shift, low, count):
    parts, group, each, width = rows_all.shape
    cols = columns.shape[1] // 3
    return pl.pallas_call(
        functools.partial(compress_kernel, low),
        grid_spec=pl.GridSpec(
            grid=(parts, group),
            in_specs=[
                pl.BlockSpec((None, None, each, width), lambda p, s: (p, s, 0, 0)),
                pl.BlockSpec((width, 3 * cols), lambda p, s: (0, 0)),
                pl.BlockSpec((1, cols), lambda p, s: (0, 0)),
            ],
            out_specs=pl.BlockSpec((None, None, count, cols), lambda p, s: (p, s, 0, 0)),
            scratch_shapes=[pltpu.VMEM((width // LANES, 3 * count, LANES), F32)],
        ),
        out_shape=jax.ShapeDtypeStruct((parts, group, count, cols), BF16),
        compiler_params=pltpu.CompilerParams(
            dimension_semantics=("arbitrary", "arbitrary"), vmem_limit_bytes=32 * 2**20
        ),
        cost_estimate=cost(6.5),
        name="compress",
    )(rows_all, columns, shift)


def lay_out_kernel(
    parts, unit_cols, core_ref, a_ref, b_ref, c_ref, d_ref, e_ref, f_ref, up_ref, down_ref, out_ref
):
    out_ref[...] = e_ref[...].astype(F32) + f_ref[...].astype(F32)
    flipped = core_ref[0] == 1
    for half, (mine_ref, far_ref) in enumerate(((a_ref, c_ref), (b_ref, d_ref))):
        mine, far = mine_ref[...].astype(F32), far_ref[...].astype(F32)
        for core, value in enumerate(
            (jnp.where(flipped, far, mine), jnp.where(flipped, mine, far))
        ):
            for part in range(parts):
                at = ((part * 2 + core) * 2 + half) * unit_cols
                up_ref[:, at : at + unit_cols] = value[
                    0, :, part * unit_cols : (part + 1) * unit_cols
                ]
            down_ref[2 * core + half] = value[1]


def lay_out(core, mine, far, parts):
    _, rows, width = mine[0].shape
    step = rows // 4 if rows % 64 == 0 else rows
    half = lambda: pl.BlockSpec((2, step, width), lambda r, *_: (0, r, 0))
    final = lambda: pl.BlockSpec((None, step, width), lambda r, *_: (2, r, 0))
    return pl.pallas_call(
        functools.partial(lay_out_kernel, parts, rows),
        grid_spec=pltpu.PrefetchScalarGridSpec(
            num_scalar_prefetch=1,
            grid=(rows // step,),
            in_specs=[half(), half(), half(), half(), final(), final()],
            out_specs=[
                pl.BlockSpec((step, 4 * width), lambda r, *_: (r, 0)),
                pl.BlockSpec((4, step, width), lambda r, *_: (0, r, 0)),
                pl.BlockSpec((step, width), lambda r, *_: (r, 0)),
            ],
        ),
        out_shape=[
            jax.ShapeDtypeStruct((rows, 4 * width), F32),
            jax.ShapeDtypeStruct((4, rows, width), F32),
            jax.ShapeDtypeStruct((rows, width), F32),
        ],
        compiler_params=pltpu.CompilerParams(vmem_limit_bytes=32 * 2**20),
        cost_estimate=cost(4),
        name="lay_out",
    )(core.reshape(1), *mine, *far, mine[1], far[1])


def lay_squares_kernel(in_ref, *out_refs):
    parts = in_ref.shape[0]
    cols = in_ref.shape[2] // len(out_refs)
    for at, out_ref in enumerate(out_refs):
        for part in range(parts):
            out_ref[:, part * cols : (part + 1) * cols] = in_ref[
                part, :, at * cols : (at + 1) * cols
            ].astype(F32)


def lay_squares(summed, rows):
    parts, _, wide = summed.shape
    width = parts * wide // 4
    step = rows // 2
    return pl.pallas_call(
        lay_squares_kernel,
        grid_spec=pl.GridSpec(
            grid=(2,),
            in_specs=[pl.BlockSpec((parts, step, wide), lambda i: (0, i, 0))],
            out_specs=[pl.BlockSpec((step, width), lambda i: (i, 0)) for _ in range(4)],
        ),
        out_shape=[jax.ShapeDtypeStruct((rows, width), F32) for _ in range(4)],
        compiler_params=pltpu.CompilerParams(vmem_limit_bytes=32 * 2**20),
        cost_estimate=cost(2.5),
        name="lay_squares",
    )(summed)


def standardise(rows):
    mean = jnp.mean(rows, axis=-1, keepdims=True)
    centred = rows - mean
    rate = lax.rsqrt(jnp.mean(centred * centred, axis=-1, keepdims=True) + EPSILON)
    return centred * rate, rate


def standardise_back(unit, rate, grad, gain):
    scaled = grad * gain
    mean = jnp.mean(scaled, axis=-1, keepdims=True)
    along = jnp.mean(scaled * unit, axis=-1, keepdims=True)
    return rate * (scaled - mean - unit * along)


def sinusoid_reversed(rows, width):
    positions = (rows - 1 - jnp.arange(rows, dtype=jnp.int32)).astype(F32)[:, None]
    frequency = jnp.exp(
        jnp.arange(width // 2, dtype=F32) * (-2.0 * math.log(10000.0) / width)
    )
    angles = positions * frequency[None, :]
    return jnp.concatenate([jnp.sin(angles), jnp.cos(angles)], axis=1).astype(BF16)


def dot(left, right):
    return mm(left, right, NN)


def swap(value):
    return lax.ppermute(value, "core", [(0, 1), (1, 0)])


def exchange(blocks, name, axis=0):
    count = lax.axis_size(name)
    me = lax.axis_index(name)
    block = lambda at: lax.dynamic_index_in_dim(blocks, at, axis, keepdims=False)
    return [block(me)] + [
        lax.ppermute(block(me ^ apart), name, [(i, i ^ apart) for i in range(count)])
        for apart in range(1, count)
    ]


def collect(block, name):
    count = lax.axis_size(name)
    me = lax.axis_index(name)
    found = jnp.stack(
        [block]
        + [
            lax.ppermute(block, name, [(i, i ^ apart) for i in range(count)])
            for apart in range(1, count)
        ]
    )
    return jnp.concatenate(
        [lax.dynamic_index_in_dim(found, me ^ i, 0, keepdims=False) for i in range(count)]
    )


def add_up(arrays, kind=BF16):
    total = arrays[0].astype(F32)
    for array in arrays[1:]:
        total = total + array.astype(F32)
    return total.astype(kind)


def body(
    segment, memory, compressed, eob, reset, ln1_gain, ln1_bias, w_query, w_key, w_value,
    w_out, out_bias, w_rel, bias_content, bias_position, ln2_gain, ln2_bias, w_up, up_bias,
    w_down, down_bias, conv_weight, conv_bias, cotangent,
):
    parts = lax.axis_size("seq")
    layers = lax.axis_size("z")
    core = lax.axis_index("core")
    me = lax.axis_index("seq")
    group, seg, width = segment.shape
    mem, old = memory.shape[1], compressed.shape[1]
    cuts = (old, mem, seg)
    each = old + mem + seg
    keys_in_all = parts * each
    cols = width // parts
    wide = 4 * cols
    own = group * seg
    unit_cols = w_up.shape[1] // (4 * parts)
    barrier = lax.optimization_barrier

    def by_columns(matrices):
        count = matrices.shape[0]
        sent = matrices.reshape(count, cols, parts, cols).transpose(2, 1, 0, 3)
        return sent.reshape(parts, cols, count * cols)

    up_bias_own = lax.dynamic_slice_in_dim(up_bias, core * 2 * unit_cols, 2 * unit_cols, 0)
    vectors = jnp.concatenate(
        [ln1_gain, ln1_bias, out_bias, ln2_gain, ln2_bias, down_bias, up_bias_own]
    )
    vectors = jnp.pad(vectors.reshape(2, wide), ((0, 14), (0, 0)))
    sent = jnp.concatenate(
        [
            by_columns(jnp.stack([w_query, w_key, w_value, w_rel])),
            jnp.broadcast_to(vectors, (parts, 16, wide)),
        ],
        axis=1,
    )
    got = lax.all_to_all(sent, "seq", 0, 0, tiled=True)
    spans = [(0, group)]
    local = [
        jnp.concatenate([compressed[low:high], memory[low:high], segment[low:high]], axis=1)
        for low, high in spans
    ]
    rows_all = [lax.all_gather(local[0], "seq")]
    columns = got[:, :cols].reshape(width, wide)
    vectors = got[:, cols : cols + 2].reshape(parts, 2 * wide).astype(F32)
    gain_one, shift_one, out_shift, gain_two, shift_two, down_shift = (
        vectors[:, cols * i : cols * (i + 1)].reshape(1, width) for i in range(6)
    )
    up_shift = vectors[:, 6 * cols :].reshape(parts, 2, unit_cols).transpose(1, 0, 2)
    up_shift = up_shift.reshape(2, 1, parts * unit_cols)
    up_quarters = lax.dynamic_slice_in_dim(
        w_up.reshape(cols, parts, 2, 2, unit_cols), core, 1, 2
    ).reshape(cols, parts, 2, unit_cols)
    up_quarters = [up_quarters[:, :, i].reshape(cols, width) for i in range(2)]
    down_half = lax.dynamic_slice_in_dim(w_down, core * 2 * unit_cols, 2 * unit_cols, 0)
    down_quarters = [down_half[unit_cols * i : unit_cols * (i + 1)] for i in range(2)]
    first = jnp.concatenate([up_quarters[0], down_quarters[0], w_out], axis=0)
    second = jnp.concatenate([up_quarters[1], down_quarters[1]], axis=0)
    cot_own = cotangent.reshape(own, width)
    cot_both = jnp.concatenate([cot_own, swap(cot_own)], axis=0)

    table_rev = sinusoid_reversed(keys_in_all, width)
    proj_rev = dot(table_rev, columns[:, 3 * cols :]).astype(BF16)
    index = jnp.arange(eob.shape[1], dtype=jnp.int32)[None, :]
    opens = jnp.pad(eob, ((0, 0), (1, 0)))[:, :-1] == 1
    start = lax.cummax(jnp.where(opens, index, 0), axis=1)
    shade = jnp.where((start == 0) & (reset[:, None] == 0), 0.0, MASKED)
    info = jnp.stack([start.astype(F32), shade], axis=2)
    info = jnp.pad(info, ((0, 0), (0, 0), (0, LANES - 2)))
    rows_all[0], proj_rev, info, cot_both, table_rev, columns, *local = barrier(
        (rows_all[0], proj_rev, info, cot_both, table_rev, columns, *local)
    )
    rows_all = [rows_all[0]] + [lax.all_gather(rows, "seq") for rows in local[1:]]

    normed, normed_seg, kept, heads = [], [], [], []
    for batch, (low, high) in enumerate(spans):
        if batch == len(spans) - 1:
            rows_all[batch], first, *heads = barrier((rows_all[batch], first, *heads))
            first = lax.all_gather(first, "seq")
        normed_batch, seg_batch, query, keys, values = project(
            rows_all[batch], gain_one, shift_one, columns, old + mem
        )
        if batch == len(spans) - 1:
            second, query = barrier((second, query))
            second = lax.all_gather(second, "seq")
        weights, inverse, mixed_heads, content_q, position_q = attend(
            query,
            bias_content.astype(F32).reshape(1, cols),
            bias_position.astype(F32).reshape(1, cols),
            keys,
            values,
            proj_rev,
            info[low:high],
            cuts,
        )
        normed.append(normed_batch)
        normed_seg.append(seg_batch)
        kept.append((weights, inverse, mixed_heads, content_q, position_q, keys, values))
        heads.append(lax.all_to_all(mixed_heads, "seq", 0, 0, tiled=True))
    conv_sent, *heads = barrier((by_columns(conv_weight), *heads))
    conv_columns = lax.all_to_all(conv_sent, "seq", 0, 0, tiled=True)

    attended, middle, normed_two = [], [], []
    for (low, high), batch in zip(spans, heads):
        one, two, three = leave(batch, segment, low, first, out_shift, gain_two, shift_two)
        attended.append(one.reshape(-1, width))
        middle.append(two)
        normed_two.append(three.reshape(-1, width))
    both = jnp.concatenate(normed_two + [swap(rows) for rows in normed_two], axis=0)
    part, part_grad, late_one, unit_one = forward_back(both, cot_both, first, up_shift[0], ())
    early = exchange(late_one.reshape(parts, layers, -1, width), "z", 1)
    part, part_far, part_grad, grad_far, late_two, unit_two = forward_back(
        both, cot_both, second, up_shift[1], (part, part_grad)
    )
    late_two = lax.psum_scatter(
        late_two.reshape(-1, width), "seq", scatter_dimension=0, tiled=True
    )
    conv_columns, grad_far = barrier((conv_columns, grad_far))
    grad_far = swap(grad_far)
    by_stream = lambda rows: rows.reshape(group, seg, width)
    middle_grad, branch_grad, head_grad, sums_two = [], [], [], 0.0
    for (low, high), batch in zip(spans, middle):
        one, two, three, four = enter(
            batch, by_stream(part_grad), by_stream(grad_far), cotangent, low, first, gain_two
        )
        middle_grad.append(one)
        branch_grad.append(two.reshape(-1, width))
        three, part_grad = barrier((three, part_grad))
        head_grad.append(lax.all_to_all(three, "seq", 0, 0, tiled=True))
        sums_two = sums_two + four
    branch_grad[-1], head_grad = barrier((branch_grad[-1], head_grad))
    out_grad = mm(jnp.concatenate(attended), jnp.concatenate(branch_grad), TN)
    out_grad = exchange(out_grad.astype(BF16).reshape(parts, cols, width), "seq")
    result = part + swap(part_far).astype(F32) + down_shift
    output = (jnp.concatenate(middle).reshape(own, width) + result).astype(BF16)
    output = output.reshape(group, seg, width)

    query_w, key_w, value_w, table_grad, sums, seg_parts = 0.0, 0.0, 0.0, 0.0, 0.0, []
    for batch, (low, high) in enumerate(spans):
        weights, inverse, mixed_heads, content_q, position_q, keys, values = kept[batch]
        query_grad, key_grad, value_grad, table_part, sums_part = pull(
            weights, inverse, mixed_heads, head_grad[batch], content_q, position_q, keys, values,
            proj_rev, cuts,
        )
        if batch == 0:
            early, late_two, out_grad, query_grad = barrier((early, late_two, out_grad, query_grad))
            ff = lax.psum(jnp.concatenate([late_two, add_up(out_grad)], axis=0), "z")
            early = exchange(add_up(early), "seq")
        table_grad = table_grad + table_part
        sums = sums + sums_part
        flat = lambda rows: rows.reshape(-1, rows.shape[-1])
        query_w = query_w + mm(flat(normed_seg[batch]), flat(query_grad), TN)
        key_w = key_w + mm(flat(normed[batch]), flat(key_grad), TN)
        value_w = value_w + mm(flat(normed[batch]), flat(value_grad), TN)
        seg_grads = jnp.concatenate(
            [query_grad, key_grad[:, :, old + mem :], value_grad[:, :, old + mem :]], axis=3
        )
        seg_part = mm(flat(seg_grads), columns[:, : 3 * cols], NT)
        seg_parts.append(seg_part.astype(BF16).reshape(parts, -1, width))
    conv_columns, query_grad = barrier((conv_columns, query_grad))
    packed = [
        compress(
            rows, conv_columns.reshape(width, 3 * cols), conv_bias.astype(F32).reshape(1, cols),
            old, mem // 3,
        )
        for rows in rows_all
    ]
    packed = lax.all_to_all(jnp.concatenate(packed, axis=1), "seq", 0, 0, tiled=True)
    new_compressed = packed.transpose(1, 2, 0, 3).reshape(group, mem // 3, width)

    rel_w = mm(table_rev, table_grad.reshape(cols, keys_in_all).astype(BF16), ((0,), (1,)))
    sums = sums.transpose(1, 0, 2).reshape(8, cols)
    weight_cols = columns[:, : 3 * cols].astype(F32)
    row_sums = sums[2:5].reshape(1, 3 * cols)
    three = jnp.concatenate([query_w, key_w, value_w], axis=1)
    shift_one_grad = jnp.sum(weight_cols * row_sums, axis=1)
    gain_one_grad = jnp.sum(
        weight_cols * (three - shift_one.reshape(width, 1) * row_sums), axis=1
    ) / gain_one.reshape(width)
    out_shift_grad, gain_two_grad, shift_two_grad, down_shift_grad = (
        sums_two[i] for i in range(4)
    )
    chunk = lambda vector: vector.reshape(parts, cols)
    mine = (jnp.arange(parts) == me).astype(F32)[:, None]
    unit_sums = jnp.stack(
        [unit_one.reshape(parts, unit_cols), unit_two.reshape(parts, unit_cols)], axis=1
    ).reshape(parts, 2 * unit_cols)
    small = jnp.stack(
        [
            jnp.concatenate(
                [chunk(gain_one_grad), chunk(shift_one_grad), chunk(out_shift_grad), chunk(gain_two_grad)],
                axis=1,
            ),
            jnp.concatenate(
                [chunk(shift_two_grad), chunk(down_shift_grad), mine * sums[0:1], mine * sums[1:2]],
                axis=1,
            ),
            jnp.concatenate(
                [jnp.where(core == 0, unit_sums, 0.0), jnp.where(core == 1, unit_sums, 0.0)], axis=1
            ),
        ],
        axis=1,
    )
    small = jnp.pad(small, ((0, 0), (0, 13), (0, 0))).astype(BF16)
    square_grads = jnp.concatenate([three.astype(BF16), rel_w.astype(BF16)], axis=1)
    square_grads = jnp.concatenate([square_grads.reshape(parts, cols, wide), small], axis=1)
    summed = lax.all_to_all(square_grads, "seq", 0, 0, tiled=True)
    early, summed, *seg_parts = barrier((early, summed, *seg_parts))
    early = collect(add_up(early), "z")
    seg_grad = [add_up(exchange(rows, "seq"), F32) for rows in seg_parts]
    summed = lax.psum(summed, ("z", "core"))

    seg_grad = jnp.concatenate(seg_grad, axis=0)
    unit_seg, rate_seg = standardise(segment.reshape(own, width).astype(F32))
    rows_grad = standardise_back(unit_seg, rate_seg, seg_grad, gain_one)
    segment_grad = jnp.concatenate(middle_grad, axis=0) + by_stream(rows_grad)

    mine = (early.reshape(2, unit_cols, width), ff.reshape(3, unit_cols, width))
    up_w, down_w, out_w = lay_out(core, mine, [swap(rows) for rows in mine], parts)
    down_w = down_w.reshape(4 * unit_cols, width)
    query_w, key_w, value_w, rel_w = lay_squares(summed, cols)
    small = jnp.sum(summed[:, cols : cols + 3].astype(F32), axis=0)
    piece = lambda row, i: small[row, cols * i : cols * (i + 1)]
    return (
        output,
        segment_grad,
        piece(0, 0),
        piece(0, 1),
        query_w,
        key_w,
        value_w,
        out_w,
        piece(0, 2),
        rel_w,
        piece(1, 2),
        piece(1, 3),
        piece(0, 3),
        piece(1, 0),
        up_w,
        small[2],
        down_w,
        piece(1, 1),
        new_compressed,
    )


def solution(mesh):
    dp = mesh.shape["dp"]
    cores = jax.sharding.Mesh(
        mesh.devices.reshape(dp // 2, 2, mesh.shape["seq"]), ("z", "core", "seq")
    )
    rows = P(("z", "core"), "seq", None)
    shard, matrix = P("seq"), P("seq", None)
    return jax.shard_map(
        body,
        mesh=cores,
        in_specs=(
            rows, rows, rows, P(("z", "core"), None), P(("z", "core")), shard, shard, matrix,
            matrix, matrix, matrix, shard, matrix, shard, shard, shard, shard, matrix, shard,
            matrix, shard, P(None, "seq", None), shard, rows,
        ),
        out_specs=(
            rows, rows, shard, shard, matrix, matrix, matrix, matrix, shard, matrix, shard,
            shard, shard, shard, matrix, shard, matrix, shard, rows,
        ),
        check_vma=False,
    )
```

```python
import functools
import math

import jax
import jax.numpy as jnp
from jax import lax
from jax.experimental import pallas as pl
from jax.experimental.pallas import tpu as pltpu
from jax.sharding import PartitionSpec as P

HEADS = 8
DH = 128
EPSILON = 1e-05
MASKED = -1e30
LANES = 128
BLOCK = 256
CHUNK = 16
SCALE = 1.0 / math.sqrt(DH)
LOG2E = 1.4426950408889634
BF16 = jnp.bfloat16
F32 = jnp.float32


def cost(microseconds):
    return pl.CostEstimate(flops=int(microseconds * 1.15e7), bytes_accessed=0, transcendentals=0)


def mm(left, right, dims):
    return lax.dot_general(left, right, (dims, ((), ())), preferred_element_type=F32)


NN = ((1,), (0,))
NT = ((1,), (1,))
TN = ((0,), (0,))


def lean_left(block, first_row, fill_columns):
    columns = block.shape[1] // LANES
    far = BLOCK - 1 - first_row
    whole, part = far // LANES, far % LANES
    turned = [
        pltpu.roll(
            block[:, LANES * t : LANES * (t + 1)], LANES - part, 1, stride=1, stride_axis=0
        )
        for t in range(columns)
    ]
    rows = lax.broadcasted_iota(jnp.int32, (block.shape[0], LANES), 0)
    lanes = lax.broadcasted_iota(jnp.int32, (block.shape[0], LANES), 1)
    near = lanes - rows < LANES - part
    out = []
    for t in range(fill_columns):
        a = turned[(t + whole) % columns]
        b = turned[(t + whole + 1) % columns]
        out.append(jnp.where(near, a, b))
    return jnp.concatenate(out, axis=1)


def lean_right(block, first_row):
    columns = block.shape[1] // LANES
    whole, part = first_row // LANES, first_row % LANES
    turned = [
        pltpu.roll(block[:, LANES * t : LANES * (t + 1)], part, 1, stride=1, stride_axis=0)
        for t in range(columns)
    ]
    rows = lax.broadcasted_iota(jnp.int32, (block.shape[0], LANES), 0)
    lanes = lax.broadcasted_iota(jnp.int32, (block.shape[0], LANES), 1)
    wrapped = lanes - rows < part
    out = []
    for t in range(columns):
        a = turned[(t - whole) % columns]
        b = turned[(t - whole - 1) % columns]
        out.append(jnp.where(wrapped, b, a))
    return jnp.concatenate(out, axis=1)


def flip_matrix(kind):
    rows = lax.broadcasted_iota(jnp.int32, (BLOCK, BLOCK), 0)
    lanes = lax.broadcasted_iota(jnp.int32, (BLOCK, BLOCK), 1)
    return (rows + lanes == BLOCK - 1).astype(F32).astype(kind)


def in_place_order(parts_ref, out_ref, cuts):
    parts = parts_ref.shape[0]
    low, base = 0, 0
    for size in cuts:
        for part in range(parts):
            out_ref[base + part * size : base + (part + 1) * size, :] = parts_ref[
                part, low : low + size, :
            ]
        low += size
        base += parts * size


def attend_kernel(
    cuts, q_ref, cb_ref, pb_ref, k_ref, v_ref, t_ref, info_ref,
    e_ref, inv_ref, o_ref, cq_ref, pq_ref,
    keys, values, raw, lean, mix,
):
    parts, seg, _ = q_ref.shape
    queries = parts * seg
    old = parts * (cuts[0] + cuts[1])
    in_place_order(k_ref, keys, cuts)
    in_place_order(v_ref, values, cuts)
    q = q_ref[...].reshape(queries, DH)
    content_q = (q + cb_ref[...]).astype(BF16)
    position_q = (q + pb_ref[...]).astype(BF16)
    cq_ref[...] = content_q.reshape(parts, seg, DH)
    pq_ref[...] = position_q.reshape(parts, seg, DH)
    for block in range(queries // BLOCK):
        row0 = block * BLOCK
        width = old + row0 + BLOCK
        skip = queries - BLOCK - row0
        raw[:, :width] = mm(content_q[row0 : row0 + BLOCK], keys[:width, :], NT)
        lean[:, :width] = mm(position_q[row0 : row0 + BLOCK], t_ref[skip : skip + width, :], NT)
        for chunk in range(BLOCK // CHUNK):
            r0 = chunk * CHUNK
            turned = lean_left(lean[r0 : r0 + CHUNK, :width], r0, width // LANES)
            score = raw[r0 : r0 + CHUNK, :width] + turned
            start = info_ref[row0 + r0 : row0 + r0 + CHUNK, 0:1]
            shade = info_ref[row0 + r0 : row0 + r0 + CHUNK, 1:2]
            past = score[:, :old] + shade
            place = lax.broadcasted_iota(jnp.int32, (CHUNK, row0 + BLOCK), 1)
            own = lax.broadcasted_iota(jnp.int32, (CHUNK, row0 + BLOCK), 0) + (row0 + r0)
            seen = (place <= own) & (place >= start.astype(jnp.int32))
            now = jnp.where(seen, score[:, old:], MASKED)
            top = jnp.maximum(
                jnp.max(past, axis=1, keepdims=True), jnp.max(now, axis=1, keepdims=True)
            )
            past = jnp.exp2((past - top) * (SCALE * LOG2E))
            now = jnp.exp2((now - top) * (SCALE * LOG2E))
            total = jnp.sum(past, axis=1, keepdims=True) + jnp.sum(now, axis=1, keepdims=True)
            inv = jnp.broadcast_to(1.0 / total, (CHUNK, DH))
            inv_ref[row0 + r0 : row0 + r0 + CHUNK, :] = inv
            e_ref[row0 + r0 : row0 + r0 + CHUNK, :old] = past.astype(BF16)
            e_ref[row0 + r0 : row0 + r0 + CHUNK, old:width] = now.astype(BF16)
        mix[row0 : row0 + BLOCK, :] = mm(
            e_ref[row0 : row0 + BLOCK, :width], values[:width, :], NN
        )
    o_ref[...] = (mix[...] * inv_ref[...]).astype(BF16).reshape(parts, seg, DH)


def attend(query, content_shift, position_shift, keys, values, table_rev, info, cuts):
    parts, group, seg, cols = query.shape
    rows = keys.shape[2]
    queries, key_count, heads = parts * seg, parts * rows, cols // DH
    by_head = lambda size: pl.BlockSpec((parts, None, size, DH), lambda s, h: (0, s, 0, h))
    grid_spec = pl.GridSpec(
        grid=(group, heads),
        in_specs=[
            by_head(seg),
            pl.BlockSpec((1, DH), lambda s, h: (0, h)),
            pl.BlockSpec((1, DH), lambda s, h: (0, h)),
            by_head(rows),
            by_head(rows),
            pl.BlockSpec((key_count, DH), lambda s, h: (0, h)),
            pl.BlockSpec((None, queries, LANES), lambda s, h: (s, 0, 0)),
        ],
        out_specs=[
            pl.BlockSpec((None, None, queries, key_count), lambda s, h: (s, h, 0, 0)),
            pl.BlockSpec((None, None, queries, DH), lambda s, h: (s, h, 0, 0)),
            by_head(seg),
            by_head(seg),
            by_head(seg),
        ],
        scratch_shapes=[
            pltpu.VMEM((key_count, DH), BF16),
            pltpu.VMEM((key_count, DH), BF16),
            pltpu.VMEM((BLOCK, key_count), F32),
            pltpu.VMEM((BLOCK, key_count), F32),
            pltpu.VMEM((queries, DH), F32),
        ],
    )
    small = jax.ShapeDtypeStruct((parts, group, seg, cols), BF16)
    return pl.pallas_call(
        functools.partial(attend_kernel, cuts),
        grid_spec=grid_spec,
        out_shape=[
            jax.ShapeDtypeStruct((group, heads, queries, key_count), BF16),
            jax.ShapeDtypeStruct((group, heads, queries, DH), F32),
            small,
            small,
            small,
        ],
        compiler_params=pltpu.CompilerParams(
            dimension_semantics=("arbitrary", "arbitrary"), vmem_limit_bytes=50 * 2**20
        ),
        cost_estimate=cost(40),
        name="attend",
    )(query, content_shift, position_shift, keys, values, table_rev, info)


def pull_kernel(
    cuts, e_ref, inv_ref, o_ref, g_ref, cq_ref, pq_ref, k_ref, v_ref, t_ref,
    dq_ref, dk_ref, dv_ref, dt_ref, sums_ref,
    keys, values, grad, prob, part, score, lean, key_sum, value_sum,
):
    stream = pl.program_id(1)
    parts, seg, _ = g_ref.shape
    queries = parts * seg
    old = parts * (cuts[0] + cuts[1])
    in_place_order(k_ref, keys, cuts)
    in_place_order(v_ref, values, cuts)
    out_grad = g_ref[...].reshape(queries, DH).astype(F32)
    attended = o_ref[...].reshape(queries, DH).astype(F32)
    inv = inv_ref[...]
    grad[...] = (out_grad * inv).astype(BF16)
    dots = jnp.sum(out_grad * attended, axis=1, keepdims=True) * inv
    content_q = cq_ref[...].reshape(queries, DH)
    position_q = pq_ref[...].reshape(queries, DH)

    @pl.when(stream == 0)
    def _():
        dt_ref[...] = jnp.zeros_like(dt_ref)
        sums_ref[...] = jnp.zeros_like(sums_ref)

    key_sum[...] = jnp.zeros_like(key_sum)
    value_sum[...] = jnp.zeros_like(value_sum)
    content_total = jnp.zeros((1, DH), F32)
    position_total = jnp.zeros((1, DH), F32)
    query_total = jnp.zeros((1, DH), F32)
    flip = flip_matrix(BF16)
    flip_wide = flip_matrix(F32)
    turn = lambda rows: mm(flip, rows, NN).astype(BF16)
    for block in range(queries // BLOCK):
        row0 = block * BLOCK
        width = old + row0 + BLOCK
        skip = queries - BLOCK - row0
        rows = slice(row0, row0 + BLOCK)
        dots_back = lax.dot_general(
            flip_wide,
            jnp.broadcast_to(dots[rows], (BLOCK, DH)),
            (NN, ((), ())),
            precision=lax.Precision.HIGHEST,
            preferred_element_type=F32,
        )
        content_back = turn(content_q[rows])
        position_back = turn(position_q[rows])
        prob[:, :width] = mm(turn(grad[rows, :]), values[:width, :], NT)
        part[:, :width] = mm(flip, e_ref[rows, :width], NN)
        value_sum[:, :width] += mm(grad[rows, :], e_ref[rows, :width], TN)
        for chunk in range(BLOCK // CHUNK):
            r0 = chunk * CHUNK
            mean = dots_back[r0 : r0 + CHUNK, 0:1]
            change = part[r0 : r0 + CHUNK, :width] * (prob[r0 : r0 + CHUNK, :width] - mean)
            score[r0 : r0 + CHUNK, :width] = change.astype(BF16)
            lean[r0 : r0 + CHUNK, :width] = lean_right(change, r0).astype(BF16)
        content_grad = (mm(score[:, :width], keys[:width, :], NN) * SCALE).astype(BF16).astype(F32)
        position_grad = (
            (mm(lean[:, :width], t_ref[skip : skip + width, :], NN) * SCALE)
            .astype(BF16)
            .astype(F32)
        )
        query_grad = turn((content_grad + position_grad).astype(BF16))
        content_total += jnp.sum(content_grad, axis=0, keepdims=True)
        position_total += jnp.sum(position_grad, axis=0, keepdims=True)
        query_total += jnp.sum(query_grad.astype(F32), axis=0, keepdims=True)
        low = row0
        while low < row0 + BLOCK:
            part_at, part_row = low // seg, low % seg
            size = min(seg - part_row, row0 + BLOCK - low)
            dq_ref[part_at, part_row : part_row + size, :] = query_grad[
                low - row0 : low - row0 + size
            ]
            low += size
        key_sum[:, :width] += mm(content_back, score[:, :width], TN)
        dt_ref[:, skip : skip + width] += mm(position_back, lean[:, :width], TN) * SCALE
    key_rows = (key_sum[...] * SCALE).T.astype(BF16)
    value_rows = value_sum[...].T.astype(BF16)
    low, base = 0, 0
    for size in cuts:
        for at in range(parts):
            span = slice(base + at * size, base + (at + 1) * size)
            dk_ref[at, low : low + size, :] = key_rows[span]
            dv_ref[at, low : low + size, :] = value_rows[span]
        low += size
        base += parts * size
    key_total = jnp.sum(key_rows.astype(F32), axis=0, keepdims=True)
    value_total = jnp.sum(value_rows.astype(F32), axis=0, keepdims=True)
    sums_ref[...] += jnp.concatenate(
        [
            content_total,
            position_total,
            query_total,
            key_total,
            value_total,
            jnp.zeros((3, DH), F32),
        ],
        axis=0,
    )


def pull(weights, inverse, attended, out_grad, content_q, position_q, keys, values, table_rev, cuts):
    parts, group, seg, cols = out_grad.shape
    rows = keys.shape[2]
    queries, key_count, heads = parts * seg, parts * rows, cols // DH
    by_head = lambda size: pl.BlockSpec((parts, None, size, DH), lambda h, s: (0, s, 0, h))
    grid_spec = pl.GridSpec(
        grid=(heads, group),
        in_specs=[
            pl.BlockSpec((None, None, queries, key_count), lambda h, s: (s, h, 0, 0)),
            pl.BlockSpec((None, None, queries, DH), lambda h, s: (s, h, 0, 0)),
            by_head(seg),
            by_head(seg),
            by_head(seg),
            by_head(seg),
            by_head(rows),
            by_head(rows),
            pl.BlockSpec((key_count, DH), lambda h, s: (0, h)),
        ],
        out_specs=[
            by_head(seg),
            by_head(rows),
            by_head(rows),
            pl.BlockSpec((None, DH, key_count), lambda h, s: (h, 0, 0)),
            pl.BlockSpec((None, 8, DH), lambda h, s: (h, 0, 0)),
        ],
        scratch_shapes=[
            pltpu.VMEM((key_count, DH), BF16),
            pltpu.VMEM((key_count, DH), BF16),
            pltpu.VMEM((queries, DH), BF16),
            pltpu.VMEM((BLOCK, key_count), F32),
            pltpu.VMEM((BLOCK, key_count), F32),
            pltpu.VMEM((BLOCK, key_count), BF16),
            pltpu.VMEM((BLOCK, key_count), BF16),
            pltpu.VMEM((DH, key_count), F32),
            pltpu.VMEM((DH, key_count), F32),
        ],
    )
    return pl.pallas_call(
        functools.partial(pull_kernel, cuts),
        grid_spec=grid_spec,
        out_shape=[
            jax.ShapeDtypeStruct((parts, group, seg, cols), BF16),
            jax.ShapeDtypeStruct((parts, group, rows, cols), BF16),
            jax.ShapeDtypeStruct((parts, group, rows, cols), BF16),
            jax.ShapeDtypeStruct((heads, DH, key_count), F32),
            jax.ShapeDtypeStruct((heads, 8, DH), F32),
        ],
        compiler_params=pltpu.CompilerParams(
            dimension_semantics=("arbitrary", "arbitrary"), vmem_limit_bytes=50 * 2**20
        ),
        cost_estimate=cost(39),
        name="pull",
    )(weights, inverse, attended, out_grad, content_q, position_q, keys, values, table_rev)


def project_kernel(cut, rows_ref, gain_ref, shift_ref, w_ref, n_ref, ns_ref, q_ref, k_ref, v_ref):
    rows, width = rows_ref.shape
    cols = k_ref.shape[1]
    step = 64 if rows % 64 == 0 else 32
    for low in range(0, rows, step):
        wide = rows_ref[low : low + step, :].astype(F32)
        centred = wide - jnp.mean(wide, axis=1, keepdims=True)
        rate = lax.rsqrt(jnp.mean(centred * centred, axis=1, keepdims=True) + EPSILON)
        normed = (centred * rate * gain_ref[...] + shift_ref[...]).astype(BF16)
        n_ref[low : low + step, :] = normed
    ns_ref[...] = n_ref[cut:, :]
    q_ref[...] = mm(n_ref[cut:, :], w_ref[:, :cols], NN)
    k_ref[...] = mm(n_ref[...], w_ref[:, cols : 2 * cols], NN).astype(BF16)
    v_ref[...] = mm(n_ref[...], w_ref[:, 2 * cols : 3 * cols], NN).astype(BF16)


def project(rows_all, gain, shift, columns, cut):
    parts, group, each, width = rows_all.shape
    cols = columns.shape[1] // 4
    seg = each - cut
    block = lambda size, wide: pl.BlockSpec((None, None, size, wide), lambda p, s: (p, s, 0, 0))
    whole = lambda *shape: pl.BlockSpec(shape, lambda p, s: (0,) * len(shape))
    shape = lambda size, wide, kind: jax.ShapeDtypeStruct((parts, group, size, wide), kind)
    return pl.pallas_call(
        functools.partial(project_kernel, cut),
        grid_spec=pl.GridSpec(
            grid=(parts, group),
            in_specs=[
                block(each, width),
                whole(1, width),
                whole(1, width),
                whole(width, 4 * cols),
            ],
            out_specs=[
                block(each, width),
                block(seg, width),
                block(seg, cols),
                block(each, cols),
                block(each, cols),
            ],
        ),
        out_shape=[
            shape(each, width, BF16),
            shape(seg, width, BF16),
            shape(seg, cols, F32),
            shape(each, cols, BF16),
            shape(each, cols, BF16),
        ],
        compiler_params=pltpu.CompilerParams(
            dimension_semantics=("arbitrary", "arbitrary"), vmem_limit_bytes=40 * 2**20
        ),
        cost_estimate=cost(17),
        name="project",
    )(rows_all, gain, shift, columns)


def gelu_both(x):
    near = jnp.abs(x)
    t = 1.0 / (1.0 + (0.3275911 * math.sqrt(0.5)) * near)
    bell = jnp.exp2((x * x) * (-0.5 * LOG2E))
    tail = 0.5 * 1.061405429
    for factor in (-1.453152027, 1.421413741, -0.284496736, 0.254829592):
        tail = tail * t + 0.5 * factor
    tail = tail * t * bell
    below = jnp.where(x < 0.0, tail, 1.0 - tail)
    return x * below, below + x * bell * (1.0 / math.sqrt(2.0 * math.pi))


def forward_back_kernel(
    last, n_ref, c_ref, up_ref, down_ref, shift_ref, *rest,
):
    if last:
        part_in, grad_in, part_out, part_far, grad_out, grad_far, late_ref, sums_ref = rest[:8]
        pre, slope, hidden, act, up_out, down_out, sems, part_ref, grad_ref = rest[8:]
    else:
        part_ref, grad_ref, late_ref, sums_ref = rest[:4]
        pre, slope, hidden, act, up_out, down_out, sems = rest[4:]
    tile = pl.program_id(0)
    tiles = pl.num_programs(0)
    parts, cols, units = up_ref.shape
    width = parts * cols
    rows = n_ref.shape[0]
    slot = lax.rem(tile, 2)
    up_weight = up_ref[...].reshape(width, units)
    down_weight = down_ref[...]

    def copies(at, index):
        return (
            pltpu.make_async_copy(
                up_out.at[at],
                late_ref.at[:, pl.ds(0, cols), pl.ds(pl.multiple_of(index * units, units), units)],
                sems.at[at, 0],
            ),
            pltpu.make_async_copy(
                down_out.at[at], late_ref.at[index, pl.ds(cols, units), :], sems.at[at, 1]
            ),
        )

    @pl.when(tile == 0)
    def _():
        if last:
            part_ref[...] = part_in[...]
            grad_ref[...] = grad_in[...]
        else:
            part_ref[...] = jnp.zeros_like(part_ref)
            grad_ref[...] = jnp.zeros_like(grad_ref)

    pre[...] = mm(n_ref[...], up_weight, NN)
    slope[...] = mm(c_ref[...], down_weight, NT)
    step = 64
    for low in range(0, rows, step):
        value, change = gelu_both(pre[low : low + step, :] + shift_ref[...])
        hidden[low : low + step, :] = value.astype(BF16)
        act[low : low + step, :] = (change * slope[low : low + step, :]).astype(BF16)
    part_ref[...] += mm(hidden[...], down_weight, NN)
    grad_ref[...] += mm(act[...], up_weight, NT)
    sums_ref[...] = jnp.sum(act[...].astype(F32), axis=0, keepdims=True)

    @pl.when(tile >= 2)
    def _():
        for copy in copies(slot, tile - 2):
            copy.wait()

    up_out[slot] = mm(n_ref[...], act[...], TN).astype(BF16).reshape(parts, cols, units)
    down_out[slot] = mm(hidden[...], c_ref[...], TN).astype(BF16)
    for copy in copies(slot, tile):
        copy.start()

    @pl.when(tile == tiles - 1)
    def _():
        if last:
            part_out[...] = part_ref[: rows // 2, :]
            part_far[...] = part_ref[rows // 2 :, :].astype(BF16)
            grad_out[...] = grad_ref[: rows // 2, :]
            grad_far[...] = grad_ref[rows // 2 :, :].astype(BF16)
        for copy in copies(1 - slot, tile - 1) + copies(slot, tile):
            copy.wait()


def forward_back(normed, cot, gathered, shift, carry):
    parts, _, width = gathered.shape
    rows = normed.shape[0]
    cols = width // parts
    units = shift.shape[1] // parts
    last = len(carry) > 0
    one = pl.Buffered(1)
    whole = lambda *shape: pl.BlockSpec(shape, lambda t: (0,) * len(shape), pipeline_mode=one)
    if last:
        sums = [((rows // 2, width), F32), ((rows // 2, width), BF16)] * 2
    else:
        sums = [((rows, width), F32)] * 2
    return pl.pallas_call(
        functools.partial(forward_back_kernel, last),
        grid_spec=pl.GridSpec(
            grid=(parts,),
            in_specs=[
                whole(rows, width),
                whole(rows, width),
                pl.BlockSpec((parts, cols, units), lambda t: (0, 0, t)),
                pl.BlockSpec((None, units, width), lambda t: (t, cols // units, 0)),
                pl.BlockSpec((1, units), lambda t: (0, t)),
            ]
            + [whole(rows, width) for _ in carry],
            out_specs=[whole(*shape) for shape, _ in sums]
            + [
                pl.BlockSpec(memory_space=pl.ANY),
                pl.BlockSpec((1, units), lambda t: (0, t)),
            ],
            scratch_shapes=[
                pltpu.VMEM((rows, units), F32),
                pltpu.VMEM((rows, units), F32),
                pltpu.VMEM((rows, units), BF16),
                pltpu.VMEM((rows, units), BF16),
                pltpu.VMEM((2, parts, cols, units), BF16),
                pltpu.VMEM((2, units, width), BF16),
                pltpu.SemaphoreType.DMA((2, 2)),
            ]
            + [pltpu.VMEM((rows, width), F32) for _ in carry],
        ),
        out_shape=[jax.ShapeDtypeStruct(shape, kind) for shape, kind in sums]
        + [
            jax.ShapeDtypeStruct((parts, cols + units, width), BF16),
            jax.ShapeDtypeStruct((1, parts * units), F32),
        ],
        compiler_params=pltpu.CompilerParams(
            dimension_semantics=("arbitrary",), vmem_limit_bytes=56 * 2**20
        ),
        cost_estimate=cost(29),
        name="forward_back",
    )(normed, cot, gathered, gathered, shift, *carry)


def leave_kernel(a_ref, s_ref, w_ref, shift_ref, gain_ref, bias_ref, flat_ref, m_ref, n_ref):
    parts = a_ref.shape[0]
    flat_ref[...] = jnp.concatenate([a_ref[part] for part in range(parts)], axis=1)
    weight = w_ref[...].reshape(flat_ref.shape[1], flat_ref.shape[1])
    m_ref[...] = s_ref[...].astype(F32) + (mm(flat_ref[...], weight, NN) + shift_ref[...])
    step = 32
    for low in range(0, m_ref.shape[0], step):
        unit, _ = standardise(m_ref[low : low + step, :])
        n_ref[low : low + step, :] = (unit * gain_ref[...] + bias_ref[...]).astype(BF16)


def leave(mixed_heads, segment, base, gathered, shift, gain, bias):
    parts, group, seg, cols = mixed_heads.shape
    width = parts * cols
    at = gathered.shape[1] // cols - 1
    rows = lambda: pl.BlockSpec((None, seg, width), lambda s: (s, 0, 0))
    vector = lambda: pl.BlockSpec((1, width), lambda s: (0, 0))
    shape = lambda kind: jax.ShapeDtypeStruct((group, seg, width), kind)
    return pl.pallas_call(
        leave_kernel,
        grid_spec=pl.GridSpec(
            grid=(group,),
            in_specs=[
                pl.BlockSpec((parts, None, seg, cols), lambda s: (0, s, 0, 0)),
                pl.BlockSpec((None, seg, width), lambda s: (s + base, 0, 0)),
                pl.BlockSpec((parts, cols, width), lambda s: (0, at, 0)),
                vector(),
                vector(),
                vector(),
            ],
            out_specs=[rows(), rows(), rows()],
        ),
        out_shape=[shape(BF16), shape(F32), shape(BF16)],
        compiler_params=pltpu.CompilerParams(vmem_limit_bytes=32 * 2**20),
        cost_estimate=cost(6),
        name="leave",
    )(mixed_heads, segment, gathered, shift, gain, bias)


def enter_kernel(
    m_ref, g_ref, far_ref, c_ref, w_ref, gain_ref, mg_ref, b_ref, a_ref, sums_ref
):
    @pl.when(pl.program_id(0) == 0)
    def _():
        sums_ref[...] = jnp.zeros_like(sums_ref)

    parts = a_ref.shape[0]
    rows, width = m_ref.shape
    step = 32
    total = [jnp.zeros((1, width), F32) for _ in range(4)]
    for low in range(0, rows, step):
        at = slice(low, low + step)
        unit, rate = standardise(m_ref[at, :])
        grad = g_ref[at, :] + far_ref[at, :].astype(F32)
        cot = c_ref[at, :].astype(F32)
        middle_grad = cot + standardise_back(unit, rate, grad, gain_ref[...])
        branch = middle_grad.astype(BF16)
        mg_ref[at, :] = middle_grad
        b_ref[at, :] = branch
        for i, value in enumerate((branch.astype(F32), grad * unit, grad, cot)):
            total[i] = total[i] + jnp.sum(value, axis=0, keepdims=True)
    sums_ref[...] += jnp.concatenate(total + [jnp.zeros((4, width), F32)], axis=0)
    for part in range(parts):
        a_ref[part] = mm(b_ref[...], w_ref[part], NT).astype(BF16)


def enter(middle, grad, far, cot, base, gathered, gain):
    group, seg, width = middle.shape
    parts = gathered.shape[0]
    cols = width // parts
    at = gathered.shape[1] // cols - 1
    rows = lambda: pl.BlockSpec((None, seg, width), lambda s: (s, 0, 0))
    later = lambda: pl.BlockSpec((None, seg, width), lambda s: (s + base, 0, 0))
    shape = lambda kind: jax.ShapeDtypeStruct((group, seg, width), kind)
    return pl.pallas_call(
        enter_kernel,
        grid_spec=pl.GridSpec(
            grid=(group,),
            in_specs=[
                rows(),
                later(),
                later(),
                later(),
                pl.BlockSpec((parts, cols, width), lambda s: (0, at, 0)),
                pl.BlockSpec((1, width), lambda s: (0, 0)),
            ],
            out_specs=[
                rows(),
                rows(),
                pl.BlockSpec((parts, None, seg, cols), lambda s: (0, s, 0, 0)),
                pl.BlockSpec((8, width), lambda s: (0, 0)),
            ],
        ),
        out_shape=[
            shape(F32),
            shape(BF16),
            jax.ShapeDtypeStruct((parts, group, seg, cols), BF16),
            jax.ShapeDtypeStruct((8, width), F32),
        ],
        compiler_params=pltpu.CompilerParams(
            dimension_semantics=("arbitrary",), vmem_limit_bytes=32 * 2**20
        ),
        cost_estimate=cost(7),
        name="enter",
    )(middle, grad, far, cot, gathered, gain)


def compress_kernel(low, rows_ref, w_ref, shift_ref, out_ref, wide):
    count = out_ref.shape[0]
    cols = out_ref.shape[1]
    blocks = wide.shape[0]
    for at in range(blocks):
        wide[at] = rows_ref[low : low + 3 * count, at * LANES : (at + 1) * LANES].astype(F32)
    total = jnp.broadcast_to(shift_ref[...], (count, cols))
    for k in range(3):
        every = jnp.concatenate(
            [wide[at, pl.ds(k, count, stride=3), :] for at in range(blocks)], axis=1
        ).astype(BF16)
        total = total + mm(every, w_ref[:, k * cols : (k + 1) * cols], NN)
    out_ref[...] = total.astype(BF16)


def compress(rows_all, columns, shift, low, count):
    parts, group, each, width = rows_all.shape
    cols = columns.shape[1] // 3
    return pl.pallas_call(
        functools.partial(compress_kernel, low),
        grid_spec=pl.GridSpec(
            grid=(parts, group),
            in_specs=[
                pl.BlockSpec((None, None, each, width), lambda p, s: (p, s, 0, 0)),
                pl.BlockSpec((width, 3 * cols), lambda p, s: (0, 0)),
                pl.BlockSpec((1, cols), lambda p, s: (0, 0)),
            ],
            out_specs=pl.BlockSpec((None, None, count, cols), lambda p, s: (p, s, 0, 0)),
            scratch_shapes=[pltpu.VMEM((width // LANES, 3 * count, LANES), F32)],
        ),
        out_shape=jax.ShapeDtypeStruct((parts, group, count, cols), BF16),
        compiler_params=pltpu.CompilerParams(
            dimension_semantics=("arbitrary", "arbitrary"), vmem_limit_bytes=32 * 2**20
        ),
        cost_estimate=cost(6.5),
        name="compress",
    )(rows_all, columns, shift)


def lay_out_kernel(
    parts, unit_cols, core_ref, a_ref, b_ref, c_ref, d_ref, up_ref, down_ref
):
    flipped = core_ref[0] == 1
    for half, (mine_ref, far_ref) in enumerate(((a_ref, c_ref), (b_ref, d_ref))):
        mine, far = mine_ref[...].astype(F32), far_ref[...].astype(F32)
        for core, value in enumerate(
            (jnp.where(flipped, far, mine), jnp.where(flipped, mine, far))
        ):
            for part in range(parts):
                at = ((part * 2 + core) * 2 + half) * unit_cols
                up_ref[:, at : at + unit_cols] = value[
                    0, :, part * unit_cols : (part + 1) * unit_cols
                ]
            down_ref[2 * core + half] = value[1]


def lay_out(core, mine, far, parts):
    _, rows, width = mine[0].shape
    step = rows // 4 if rows % 64 == 0 else rows
    half = lambda: pl.BlockSpec((2, step, width), lambda r, *_: (0, r, 0))
    return pl.pallas_call(
        functools.partial(lay_out_kernel, parts, rows),
        grid_spec=pltpu.PrefetchScalarGridSpec(
            num_scalar_prefetch=1,
            grid=(rows // step,),
            in_specs=[half(), half(), half(), half()],
            out_specs=[
                pl.BlockSpec((step, 4 * width), lambda r, *_: (r, 0)),
                pl.BlockSpec((4, step, width), lambda r, *_: (0, r, 0)),
            ],
        ),
        out_shape=[
            jax.ShapeDtypeStruct((rows, 4 * width), F32),
            jax.ShapeDtypeStruct((4, rows, width), F32),
        ],
        compiler_params=pltpu.CompilerParams(vmem_limit_bytes=32 * 2**20),
        cost_estimate=cost(4),
        name="lay_out",
    )(core.reshape(1), *mine, *far)


def lay_squares_kernel(in_ref, *out_refs):
    parts = in_ref.shape[0]
    cols = in_ref.shape[2] // len(out_refs)
    for at, out_ref in enumerate(out_refs):
        for part in range(parts):
            out_ref[:, part * cols : (part + 1) * cols] = in_ref[
                part, :, at * cols : (at + 1) * cols
            ].astype(F32)


def lay_squares(summed, rows):
    parts, _, wide = summed.shape
    width = parts * wide // 4
    step = rows // 2
    return pl.pallas_call(
        lay_squares_kernel,
        grid_spec=pl.GridSpec(
            grid=(2,),
            in_specs=[pl.BlockSpec((parts, step, wide), lambda i: (0, i, 0))],
            out_specs=[pl.BlockSpec((step, width), lambda i: (i, 0)) for _ in range(4)],
        ),
        out_shape=[jax.ShapeDtypeStruct((rows, width), F32) for _ in range(4)],
        compiler_params=pltpu.CompilerParams(vmem_limit_bytes=32 * 2**20),
        cost_estimate=cost(2.5),
        name="lay_squares",
    )(summed)


def settle_kernel(
    cut, me_ref, n_ref, q_ref, k_ref, v_ref, w_ref, table_ref, dt_ref, sums_ref, gain_ref, shift_ref,
    small_ref, seg_ref, out_ref, total,
):
    part, stream = pl.program_id(0), pl.program_id(1)
    parts, rows, wide = out_ref.shape
    cols = wide // 4
    width = parts * cols

    @pl.when((part == 0) & (stream == 0))
    def _():
        total[...] = jnp.zeros_like(total)

    total[:, :cols] += mm(n_ref[cut:, :], q_ref[...], TN)
    pair = jnp.concatenate([k_ref[...], v_ref[...]], axis=1)
    total[:, cols : 3 * cols] += mm(n_ref[...], pair, TN)
    all_three = jnp.concatenate([q_ref[...], pair[cut:]], axis=1)
    seg_ref[...] = mm(all_three, w_ref[:, : 3 * cols], NT).astype(BF16)

    @pl.when((part == parts - 1) & (stream == pl.num_programs(1) - 1))
    def _():
        heads = dt_ref.shape[0]
        rel = [
            mm(dt_ref[head].astype(BF16), table_ref[...], NN).T.astype(BF16)
            for head in range(heads)
        ]
        rel = jnp.concatenate(rel, axis=1)
        line = lambda row: jnp.concatenate(
            [sums_ref[head, row : row + 1, :] for head in range(heads)], axis=1
        )
        exact = lambda left, right: lax.dot_general(
            left, right, (NT, ((), ())), precision=lax.Precision.HIGHEST, preferred_element_type=F32
        )
        weight = w_ref[:, : 3 * cols].astype(F32)
        row_sums = jnp.concatenate([line(2), line(3), line(4)], axis=1)
        shift_grad = exact(jnp.broadcast_to(row_sums, (8, 3 * cols)), weight)[0:1]
        along = exact(jnp.ones((8, 3 * cols), F32), weight * total[...])[0:1]
        gain_grad = (along - shift_ref[...] * shift_grad) / gain_ref[...]
        for at in range(parts):
            low, high = at * cols, (at + 1) * cols
            out_ref[at, :cols, : 3 * cols] = total[low:high, :].astype(BF16)
            out_ref[at, :cols, 3 * cols :] = rel[low:high]
            mine = (me_ref[0] == at).astype(F32)
            none = jnp.zeros((1, 2 * cols), F32)
            first = jnp.concatenate([gain_grad[:, low:high], shift_grad[:, low:high], none], axis=1)
            second = jnp.concatenate([none, mine * line(0), mine * line(1)], axis=1)
            added = jnp.concatenate([first, second, jnp.zeros((14, wide), F32)], axis=0)
            out_ref[at, cols:, :] = (small_ref[at] + added).astype(BF16)


def settle(me, normed, query_grad, key_grad, value_grad, columns, table, table_grad, sums, gain, shift, small):
    parts, group, each, width = normed.shape
    seg, cols = query_grad.shape[2:]
    cut, wide = each - seg, 4 * cols
    block = lambda size, columns: pl.BlockSpec((None, None, size, columns), lambda p, s, *_: (p, s, 0, 0))
    whole = lambda *shape: pl.BlockSpec(
        shape, lambda p, s, *_: (0,) * len(shape), pipeline_mode=pl.Buffered(1)
    )
    return pl.pallas_call(
        functools.partial(settle_kernel, cut),
        grid_spec=pltpu.PrefetchScalarGridSpec(
            num_scalar_prefetch=1,
            grid=(parts, group),
            in_specs=[
                block(each, width),
                block(seg, cols),
                block(each, cols),
                block(each, cols),
                whole(*columns.shape),
                whole(*table.shape),
                whole(*table_grad.shape),
                whole(*sums.shape),
                whole(1, width),
                whole(1, width),
                whole(*small.shape),
            ],
            out_specs=[block(seg, width), whole(parts, cols + 16, wide)],
            scratch_shapes=[pltpu.VMEM((width, 3 * cols), F32)],
        ),
        out_shape=[
            jax.ShapeDtypeStruct((parts, group, seg, width), BF16),
            jax.ShapeDtypeStruct((parts, cols + 16, wide), BF16),
        ],
        compiler_params=pltpu.CompilerParams(
            dimension_semantics=("arbitrary", "arbitrary"), vmem_limit_bytes=50 * 2**20
        ),
        cost_estimate=cost(20),
        name="settle",
    )(me.reshape(1), normed, query_grad, key_grad, value_grad, columns, table, table_grad, sums, gain, shift, small)


def standardise(rows):
    mean = jnp.mean(rows, axis=-1, keepdims=True)
    centred = rows - mean
    rate = lax.rsqrt(jnp.mean(centred * centred, axis=-1, keepdims=True) + EPSILON)
    return centred * rate, rate


def standardise_back(unit, rate, grad, gain):
    scaled = grad * gain
    mean = jnp.mean(scaled, axis=-1, keepdims=True)
    along = jnp.mean(scaled * unit, axis=-1, keepdims=True)
    return rate * (scaled - mean - unit * along)


def sinusoid_reversed(rows, width):
    positions = (rows - 1 - jnp.arange(rows, dtype=jnp.int32)).astype(F32)[:, None]
    frequency = jnp.exp(
        jnp.arange(width // 2, dtype=F32) * (-2.0 * math.log(10000.0) / width)
    )
    angles = positions * frequency[None, :]
    return jnp.concatenate([jnp.sin(angles), jnp.cos(angles)], axis=1).astype(BF16)


def dot(left, right):
    return mm(left, right, NN)


def swap(value):
    return lax.ppermute(value, "core", [(0, 1), (1, 0)])


def exchange(blocks, name, axis=0):
    count = lax.axis_size(name)
    me = lax.axis_index(name)
    block = lambda at: lax.dynamic_index_in_dim(blocks, at, axis, keepdims=False)
    return [block(me)] + [
        lax.ppermute(block(me ^ apart), name, [(i, i ^ apart) for i in range(count)])
        for apart in range(1, count)
    ]


def collect(block, name):
    count = lax.axis_size(name)
    me = lax.axis_index(name)
    found = jnp.stack(
        [block]
        + [
            lax.ppermute(block, name, [(i, i ^ apart) for i in range(count)])
            for apart in range(1, count)
        ]
    )
    return jnp.concatenate(
        [lax.dynamic_index_in_dim(found, me ^ i, 0, keepdims=False) for i in range(count)]
    )


def add_up(arrays, kind=BF16):
    total = arrays[0].astype(F32)
    for array in arrays[1:]:
        total = total + array.astype(F32)
    return total.astype(kind)


def body(
    segment, memory, compressed, eob, reset, ln1_gain, ln1_bias, w_query, w_key, w_value,
    w_out, out_bias, w_rel, bias_content, bias_position, ln2_gain, ln2_bias, w_up, up_bias,
    w_down, down_bias, conv_weight, conv_bias, cotangent,
):
    parts = lax.axis_size("seq")
    layers = lax.axis_size("z")
    core = lax.axis_index("core")
    me = lax.axis_index("seq")
    group, seg, width = segment.shape
    mem, old = memory.shape[1], compressed.shape[1]
    cuts = (old, mem, seg)
    each = old + mem + seg
    keys_in_all = parts * each
    cols = width // parts
    wide = 4 * cols
    own = group * seg
    unit_cols = w_up.shape[1] // (4 * parts)
    barrier = lax.optimization_barrier

    def by_columns(matrices):
        count = matrices.shape[0]
        sent = matrices.reshape(count, cols, parts, cols).transpose(2, 1, 0, 3)
        return sent.reshape(parts, cols, count * cols)

    up_bias_own = lax.dynamic_slice_in_dim(up_bias, core * 2 * unit_cols, 2 * unit_cols, 0)
    vectors = jnp.concatenate(
        [ln1_gain, ln1_bias, out_bias, ln2_gain, ln2_bias, down_bias, up_bias_own]
    )
    vectors = jnp.pad(vectors.reshape(2, wide), ((0, 14), (0, 0)))
    half = cols // 2
    sent = by_columns(jnp.stack([w_query, w_key, w_value, w_rel]))
    sent = lax.dynamic_slice_in_dim(sent, core * half, half, 1)
    sent = jnp.concatenate([sent, jnp.broadcast_to(vectors, (parts, 16, wide))], axis=1)
    got = lax.all_to_all(sent, "seq", 0, 0, tiled=True)
    spans = [(0, group)]
    local = [
        jnp.concatenate([compressed[low:high], memory[low:high], segment[low:high]], axis=1)
        for low, high in spans
    ]
    rows_all = [lax.all_gather(local[0], "seq")]
    mine = got[:, :half]
    far = swap(mine)
    columns = jnp.stack(
        [jnp.where(core == 0, mine, far), jnp.where(core == 0, far, mine)], axis=1
    ).reshape(width, wide)
    vectors = got[:, half : half + 2].reshape(parts, 2 * wide).astype(F32)
    gain_one, shift_one, out_shift, gain_two, shift_two, down_shift = (
        vectors[:, cols * i : cols * (i + 1)].reshape(1, width) for i in range(6)
    )
    up_shift = vectors[:, 6 * cols :].reshape(parts, 2, unit_cols).transpose(1, 0, 2)
    up_shift = up_shift.reshape(2, 1, parts * unit_cols)
    up_quarters = lax.dynamic_slice_in_dim(
        w_up.reshape(cols, parts, 2, 2, unit_cols), core, 1, 2
    ).reshape(cols, parts, 2, unit_cols)
    up_quarters = [up_quarters[:, :, i].reshape(cols, width) for i in range(2)]
    down_half = lax.dynamic_slice_in_dim(w_down, core * 2 * unit_cols, 2 * unit_cols, 0)
    down_quarters = [down_half[unit_cols * i : unit_cols * (i + 1)] for i in range(2)]
    first = jnp.concatenate([up_quarters[0], down_quarters[0], w_out], axis=0)
    second = jnp.concatenate([up_quarters[1], down_quarters[1]], axis=0)
    cot_own = cotangent.reshape(own, width)
    cot_both = jnp.concatenate([cot_own, swap(cot_own)], axis=0)

    table_rev = sinusoid_reversed(keys_in_all, width)
    proj_rev = dot(table_rev, columns[:, 3 * cols :]).astype(BF16)
    index = jnp.arange(eob.shape[1], dtype=jnp.int32)[None, :]
    opens = jnp.pad(eob, ((0, 0), (1, 0)))[:, :-1] == 1
    start = lax.cummax(jnp.where(opens, index, 0), axis=1)
    shade = jnp.where((start == 0) & (reset[:, None] == 0), 0.0, MASKED)
    info = jnp.stack([start.astype(F32), shade], axis=2)
    info = jnp.pad(info, ((0, 0), (0, 0), (0, LANES - 2)))
    rows_all[0], proj_rev, info, cot_both, table_rev, columns, *local = barrier(
        (rows_all[0], proj_rev, info, cot_both, table_rev, columns, *local)
    )
    rows_all = [rows_all[0]] + [lax.all_gather(rows, "seq") for rows in local[1:]]

    normed, normed_seg, kept, heads = [], [], [], []
    for batch, (low, high) in enumerate(spans):
        if batch == len(spans) - 1:
            rows_all[batch], first, *heads = barrier((rows_all[batch], first, *heads))
            first = lax.all_gather(first, "seq")
        normed_batch, seg_batch, query, keys, values = project(
            rows_all[batch], gain_one, shift_one, columns, old + mem
        )
        if batch == len(spans) - 1:
            conv_sent = by_columns(conv_weight)
            second, conv_sent, query = barrier((second, conv_sent, query))
            conv_columns = lax.all_to_all(conv_sent, "seq", 0, 0, tiled=True)
            second = lax.all_gather(second, "seq")
        weights, inverse, mixed_heads, content_q, position_q = attend(
            query,
            bias_content.astype(F32).reshape(1, cols),
            bias_position.astype(F32).reshape(1, cols),
            keys,
            values,
            proj_rev,
            info[low:high],
            cuts,
        )
        normed.append(normed_batch)
        normed_seg.append(seg_batch)
        kept.append((weights, inverse, mixed_heads, content_q, position_q, keys, values))
        heads.append(lax.all_to_all(mixed_heads, "seq", 0, 0, tiled=True))
    conv_columns, *heads = barrier((conv_columns, *heads))

    attended, middle, normed_two = [], [], []
    for (low, high), batch in zip(spans, heads):
        one, two, three = leave(batch, segment, low, first, out_shift, gain_two, shift_two)
        attended.append(one.reshape(-1, width))
        middle.append(two)
        normed_two.append(three.reshape(-1, width))
    both = jnp.concatenate(normed_two + [swap(rows) for rows in normed_two], axis=0)
    part, part_grad, late_one, unit_one = forward_back(both, cot_both, first, up_shift[0], ())
    late_one = lax.psum_scatter(
        late_one.reshape(-1, width), "seq", scatter_dimension=0, tiled=True
    )
    part, part_far, part_grad, grad_far, late_two, unit_two = forward_back(
        both, cot_both, second, up_shift[1], (part, part_grad)
    )
    late_two = exchange(late_two.reshape(parts, layers, -1, width), "z", 1)
    grad_far = swap(grad_far)
    by_stream = lambda rows: rows.reshape(group, seg, width)
    middle_grad, branch_grad, head_grad, sums_two = [], [], [], 0.0
    for (low, high), batch in zip(spans, middle):
        one, two, three, four = enter(
            batch, by_stream(part_grad), by_stream(grad_far), cotangent, low, first, gain_two
        )
        middle_grad.append(one)
        branch_grad.append(two.reshape(-1, width))
        three, part_grad = barrier((three, part_grad))
        head_grad.append(lax.all_to_all(three, "seq", 0, 0, tiled=True))
        sums_two = sums_two + four
    result = part + swap(part_far).astype(F32) + down_shift
    output = (jnp.concatenate(middle).reshape(own, width) + result).astype(BF16)
    output = output.reshape(group, seg, width)

    out_shift_grad, gain_two_grad, shift_two_grad, down_shift_grad = (
        sums_two[i].reshape(parts, cols) for i in range(4)
    )
    none = jnp.zeros((parts, 2 * cols), F32)
    unit_sums = jnp.stack(
        [unit_one.reshape(parts, unit_cols), unit_two.reshape(parts, unit_cols)], axis=1
    ).reshape(parts, 2 * unit_cols)
    small = jnp.stack(
        [
            jnp.concatenate([none, out_shift_grad, gain_two_grad], axis=1),
            jnp.concatenate([shift_two_grad, down_shift_grad, none], axis=1),
            jnp.concatenate(
                [jnp.where(core == 0, unit_sums, 0.0), jnp.where(core == 1, unit_sums, 0.0)], axis=1
            ),
        ],
        axis=1,
    )
    small = jnp.pad(small, ((0, 0), (0, 13), (0, 0)))
    weights, inverse, mixed_heads, content_q, position_q, keys, values = kept[0]
    out_grad = mm(jnp.concatenate(attended), jnp.concatenate(branch_grad), TN)
    out_grad = out_grad.astype(BF16).reshape(parts, cols, width)
    late_one, small, out_grad, head_grad = barrier((late_one, small, out_grad, head_grad[0]))
    ff = lax.psum(late_one, "z")
    out_grad = exchange(out_grad, "seq")
    query_grad, key_grad, value_grad, table_grad, sums = pull(
        weights, inverse, mixed_heads, head_grad, content_q, position_q, keys, values, proj_rev, cuts
    )
    late_two, query_grad = barrier((late_two, query_grad))
    late_two = exchange(add_up(late_two), "seq")
    seg_part, square_grads = settle(
        me, normed[0], query_grad, key_grad, value_grad, columns, table_rev, table_grad, sums,
        gain_one, shift_one, small,
    )
    summed = lax.all_to_all(square_grads, "seq", 0, 0, tiled=True)
    ff, late_two, square_grads = barrier((ff, late_two, square_grads))
    late_two = collect(add_up(late_two), "z")
    late_far = swap(late_two)
    summed = jnp.concatenate([summed.reshape(-1, wide), add_up(out_grad).reshape(-1, wide)], axis=0)
    ff, late_two, late_far, summed, seg_part, conv_columns = barrier(
        (ff, late_two, late_far, summed, seg_part, conv_columns)
    )
    summed = lax.psum(summed, ("z", "core"))
    squares = parts * (cols + 16)
    out_w = summed[squares:].reshape(cols, width).astype(F32)
    summed = summed[:squares].reshape(parts, cols + 16, wide)
    seg_grad = lax.all_to_all(seg_part, "seq", 0, 0, tiled=True).astype(F32)
    seg_grad = jnp.sum(seg_grad, axis=0).reshape(own, width)
    packed = [
        compress(
            rows, conv_columns.reshape(width, 3 * cols), conv_bias.astype(F32).reshape(1, cols),
            old, mem // 3,
        )
        for rows in rows_all
    ]
    packed = lax.all_to_all(jnp.concatenate(packed, axis=1), "seq", 0, 0, tiled=True)
    new_compressed = packed.transpose(1, 2, 0, 3).reshape(group, mem // 3, width)

    unit_seg, rate_seg = standardise(segment.reshape(own, width).astype(F32))
    rows_grad = standardise_back(unit_seg, rate_seg, seg_grad, gain_one)
    segment_grad = jnp.concatenate(middle_grad, axis=0) + by_stream(rows_grad)

    halves = lambda *rows: [each.reshape(2, unit_cols, width) for each in rows]
    up_w, down_w = lay_out(core, halves(ff, late_two), halves(swap(ff), late_far), parts)
    down_w = down_w.reshape(4 * unit_cols, width)
    query_w, key_w, value_w, rel_w = lay_squares(summed, cols)
    small = jnp.sum(summed[:, cols : cols + 3].astype(F32), axis=0)
    piece = lambda row, i: small[row, cols * i : cols * (i + 1)]
    return (
        output,
        segment_grad,
        piece(0, 0),
        piece(0, 1),
        query_w,
        key_w,
        value_w,
        out_w,
        piece(0, 2),
        rel_w,
        piece(1, 2),
        piece(1, 3),
        piece(0, 3),
        piece(1, 0),
        up_w,
        small[2],
        down_w,
        piece(1, 1),
        new_compressed,
    )


def solution(mesh):
    dp = mesh.shape["dp"]
    cores = jax.sharding.Mesh(
        mesh.devices.reshape(dp // 2, 2, mesh.shape["seq"]), ("z", "core", "seq")
    )
    rows = P(("z", "core"), "seq", None)
    shard, matrix = P("seq"), P("seq", None)
    return jax.shard_map(
        body,
        mesh=cores,
        in_specs=(
            rows, rows, rows, P(("z", "core"), None), P(("z", "core")), shard, shard, matrix,
            matrix, matrix, matrix, shard, matrix, shard, shard, shard, shard, matrix, shard,
            matrix, shard, P(None, "seq", None), shard, rows,
        ),
        out_specs=(
            rows, rows, shard, shard, matrix, matrix, matrix, matrix, shard, matrix, shard,
            shard, shard, shard, matrix, shard, matrix, shard, rows,
        ),
        check_vma=False,
    )
```

```python
import functools
import math

import jax
import jax.numpy as jnp
from jax import lax
from jax.experimental import pallas as pl
from jax.experimental.pallas import tpu as pltpu
from jax.sharding import PartitionSpec as P

HEADS = 8
DH = 128
EPSILON = 1e-05
MASKED = -1e30
LANES = 128
BLOCK = 256
CHUNK = 16
SCALE = 1.0 / math.sqrt(DH)
LOG2E = 1.4426950408889634
BF16 = jnp.bfloat16
F32 = jnp.float32


def cost(microseconds):
    return pl.CostEstimate(flops=int(microseconds * 1.15e7), bytes_accessed=0, transcendentals=0)


def mm(left, right, dims):
    return lax.dot_general(left, right, (dims, ((), ())), preferred_element_type=F32)


NN = ((1,), (0,))
NT = ((1,), (1,))
TN = ((0,), (0,))


def lean_left(block, first_row, fill_columns):
    columns = block.shape[1] // LANES
    far = BLOCK - 1 - first_row
    whole, part = far // LANES, far % LANES
    turned = [
        pltpu.roll(
            block[:, LANES * t : LANES * (t + 1)], LANES - part, 1, stride=1, stride_axis=0
        )
        for t in range(columns)
    ]
    rows = lax.broadcasted_iota(jnp.int32, (block.shape[0], LANES), 0)
    lanes = lax.broadcasted_iota(jnp.int32, (block.shape[0], LANES), 1)
    near = lanes - rows < LANES - part
    out = []
    for t in range(fill_columns):
        a = turned[(t + whole) % columns]
        b = turned[(t + whole + 1) % columns]
        out.append(jnp.where(near, a, b))
    return jnp.concatenate(out, axis=1)


def lean_right(block, first_row):
    columns = block.shape[1] // LANES
    whole, part = first_row // LANES, first_row % LANES
    turned = [
        pltpu.roll(block[:, LANES * t : LANES * (t + 1)], part, 1, stride=1, stride_axis=0)
        for t in range(columns)
    ]
    rows = lax.broadcasted_iota(jnp.int32, (block.shape[0], LANES), 0)
    lanes = lax.broadcasted_iota(jnp.int32, (block.shape[0], LANES), 1)
    wrapped = lanes - rows < part
    out = []
    for t in range(columns):
        a = turned[(t - whole) % columns]
        b = turned[(t - whole - 1) % columns]
        out.append(jnp.where(wrapped, b, a))
    return jnp.concatenate(out, axis=1)


def flip_matrix(kind):
    rows = lax.broadcasted_iota(jnp.int32, (BLOCK, BLOCK), 0)
    lanes = lax.broadcasted_iota(jnp.int32, (BLOCK, BLOCK), 1)
    return (rows + lanes == BLOCK - 1).astype(F32).astype(kind)


def in_place_order(parts_ref, out_ref, cuts):
    parts = parts_ref.shape[0]
    low, base = 0, 0
    for size in cuts:
        for part in range(parts):
            out_ref[base + part * size : base + (part + 1) * size, :] = parts_ref[
                part, low : low + size, :
            ]
        low += size
        base += parts * size


def attend_kernel(
    cuts, q_ref, cb_ref, pb_ref, k_ref, v_ref, t_ref, info_ref,
    e_ref, inv_ref, o_ref, cq_ref, pq_ref,
    keys, values, raw, lean, mix, tops, sums,
):
    parts, seg, _ = q_ref.shape
    queries = parts * seg
    old = parts * (cuts[0] + cuts[1])
    in_place_order(k_ref, keys, cuts)
    in_place_order(v_ref, values, cuts)
    q = q_ref[...].reshape(queries, DH)
    content_q = (q + cb_ref[...]).astype(BF16)
    position_q = (q + pb_ref[...]).astype(BF16)
    cq_ref[...] = content_q.reshape(parts, seg, DH)
    pq_ref[...] = position_q.reshape(parts, seg, DH)
    for block in range(queries // BLOCK):
        row0 = block * BLOCK
        width = old + row0 + BLOCK
        skip = queries - BLOCK - row0
        raw[:, :width] = mm(content_q[row0 : row0 + BLOCK], keys[:width, :], NT)
        lean[:, :width] = mm(position_q[row0 : row0 + BLOCK], t_ref[skip : skip + width, :], NT)
        for chunk in range(BLOCK // CHUNK):
            r0 = chunk * CHUNK
            rows = slice(r0, r0 + CHUNK)
            turned = lean_left(lean[rows, :width], r0, width // LANES)
            score = raw[rows, :width] + turned
            start = info_ref[row0 + r0 : row0 + r0 + CHUNK, 0:1].astype(jnp.int32)
            shade = info_ref[row0 + r0 : row0 + r0 + CHUNK, 1:2]
            past = score[:, :old] + shade
            place = lax.broadcasted_iota(jnp.int32, (CHUNK, row0 + BLOCK), 1)
            own = lax.broadcasted_iota(jnp.int32, (CHUNK, row0 + BLOCK), 0) + (row0 + r0)
            now = jnp.where((place <= own) & (place >= start), score[:, old:], MASKED)
            raw[rows, :old] = past
            raw[rows, old:width] = now
            top = past[:, :LANES]
            for low in range(LANES, old, LANES):
                top = jnp.maximum(top, past[:, low : low + LANES])
            for low in range(0, row0 + BLOCK, LANES):
                top = jnp.maximum(top, now[:, low : low + LANES])
            tops[rows, :] = top
        top = jnp.max(tops[...], axis=1, keepdims=True)
        tops[...] = jnp.broadcast_to(top, (BLOCK, LANES))
        for chunk in range(BLOCK // CHUNK):
            r0 = chunk * CHUNK
            rows = slice(r0, r0 + CHUNK)
            top = tops[rows, :]
            total = jnp.zeros((CHUNK, LANES), F32)
            for low in range(0, width, LANES):
                weight = jnp.exp2((raw[rows, low : low + LANES] - top) * (SCALE * LOG2E))
                total = total + weight
                e_ref[row0 + r0 : row0 + r0 + CHUNK, low : low + LANES] = weight.astype(BF16)
            sums[rows, :] = total
        total = jnp.sum(sums[...], axis=1, keepdims=True)
        inv_ref[row0 : row0 + BLOCK, :] = jnp.broadcast_to(1.0 / total, (BLOCK, DH))
        mix[row0 : row0 + BLOCK, :] = mm(
            e_ref[row0 : row0 + BLOCK, :width], values[:width, :], NN
        )
    o_ref[...] = (mix[...] * inv_ref[...]).astype(BF16).reshape(parts, seg, DH)


def attend(query, content_shift, position_shift, keys, values, table_rev, info, cuts):
    parts, group, seg, cols = query.shape
    rows = keys.shape[2]
    queries, key_count, heads = parts * seg, parts * rows, cols // DH
    by_head = lambda size: pl.BlockSpec((parts, None, size, DH), lambda s, h: (0, s, 0, h))
    grid_spec = pl.GridSpec(
        grid=(group, heads),
        in_specs=[
            by_head(seg),
            pl.BlockSpec((1, DH), lambda s, h: (0, h)),
            pl.BlockSpec((1, DH), lambda s, h: (0, h)),
            by_head(rows),
            by_head(rows),
            pl.BlockSpec((key_count, DH), lambda s, h: (0, h)),
            pl.BlockSpec((None, queries, LANES), lambda s, h: (s, 0, 0)),
        ],
        out_specs=[
            pl.BlockSpec((None, None, queries, key_count), lambda s, h: (s, h, 0, 0)),
            pl.BlockSpec((None, None, queries, DH), lambda s, h: (s, h, 0, 0)),
            by_head(seg),
            by_head(seg),
            by_head(seg),
        ],
        scratch_shapes=[
            pltpu.VMEM((key_count, DH), BF16),
            pltpu.VMEM((key_count, DH), BF16),
            pltpu.VMEM((BLOCK, key_count), F32),
            pltpu.VMEM((BLOCK, key_count), F32),
            pltpu.VMEM((queries, DH), F32),
            pltpu.VMEM((BLOCK, LANES), F32),
            pltpu.VMEM((BLOCK, LANES), F32),
        ],
    )
    small = jax.ShapeDtypeStruct((parts, group, seg, cols), BF16)
    return pl.pallas_call(
        functools.partial(attend_kernel, cuts),
        grid_spec=grid_spec,
        out_shape=[
            jax.ShapeDtypeStruct((group, heads, queries, key_count), BF16),
            jax.ShapeDtypeStruct((group, heads, queries, DH), F32),
            small,
            small,
            small,
        ],
        compiler_params=pltpu.CompilerParams(
            dimension_semantics=("arbitrary", "arbitrary"), vmem_limit_bytes=50 * 2**20
        ),
        cost_estimate=cost(40),
        name="attend",
    )(query, content_shift, position_shift, keys, values, table_rev, info)


def pull_kernel(
    cuts, e_ref, inv_ref, o_ref, g_ref, cq_ref, pq_ref, k_ref, v_ref, t_ref,
    dq_ref, dk_ref, dv_ref, ks_ref, vs_ref, dt_ref, sums_ref,
    keys, values, grad, prob, part, score, lean, key_sum, value_sum,
):
    stream = pl.program_id(1)
    parts, seg, _ = g_ref.shape
    queries = parts * seg
    old = parts * (cuts[0] + cuts[1])
    in_place_order(k_ref, keys, cuts)
    in_place_order(v_ref, values, cuts)
    out_grad = g_ref[...].reshape(queries, DH).astype(F32)
    attended = o_ref[...].reshape(queries, DH).astype(F32)
    inv = inv_ref[...]
    grad[...] = (out_grad * inv).astype(BF16)
    dots = jnp.sum(out_grad * attended, axis=1, keepdims=True) * inv
    content_q = cq_ref[...].reshape(queries, DH)
    position_q = pq_ref[...].reshape(queries, DH)

    @pl.when(stream == 0)
    def _():
        dt_ref[...] = jnp.zeros_like(dt_ref)
        sums_ref[...] = jnp.zeros_like(sums_ref)

    key_sum[...] = jnp.zeros_like(key_sum)
    value_sum[...] = jnp.zeros_like(value_sum)
    content_total = jnp.zeros((1, DH), F32)
    position_total = jnp.zeros((1, DH), F32)
    query_total = jnp.zeros((1, DH), F32)
    flip = flip_matrix(BF16)
    flip_wide = flip_matrix(F32)
    turn = lambda rows: mm(flip, rows, NN).astype(BF16)
    for block in range(queries // BLOCK):
        row0 = block * BLOCK
        width = old + row0 + BLOCK
        skip = queries - BLOCK - row0
        rows = slice(row0, row0 + BLOCK)
        dots_back = lax.dot_general(
            flip_wide,
            jnp.broadcast_to(dots[rows], (BLOCK, DH)),
            (NN, ((), ())),
            precision=lax.Precision.HIGHEST,
            preferred_element_type=F32,
        )
        content_back = turn(content_q[rows])
        position_back = turn(position_q[rows])
        prob[:, :width] = mm(turn(grad[rows, :]), values[:width, :], NT)
        part[:, :width] = mm(flip, e_ref[rows, :width], NN)
        value_sum[:, :width] += mm(grad[rows, :], e_ref[rows, :width], TN)
        for chunk in range(BLOCK // CHUNK):
            r0 = chunk * CHUNK
            mean = dots_back[r0 : r0 + CHUNK, 0:1]
            change = part[r0 : r0 + CHUNK, :width] * (prob[r0 : r0 + CHUNK, :width] - mean)
            score[r0 : r0 + CHUNK, :width] = change.astype(BF16)
            lean[r0 : r0 + CHUNK, :width] = lean_right(change, r0).astype(BF16)
        content_grad = (mm(score[:, :width], keys[:width, :], NN) * SCALE).astype(BF16).astype(F32)
        position_grad = (
            (mm(lean[:, :width], t_ref[skip : skip + width, :], NN) * SCALE)
            .astype(BF16)
            .astype(F32)
        )
        query_grad = turn((content_grad + position_grad).astype(BF16))
        content_total += jnp.sum(content_grad, axis=0, keepdims=True)
        position_total += jnp.sum(position_grad, axis=0, keepdims=True)
        query_total += jnp.sum(query_grad.astype(F32), axis=0, keepdims=True)
        dq_ref[rows, :] = query_grad
        key_sum[:, :width] += mm(content_back, score[:, :width], TN)
        dt_ref[:, skip : skip + width] += mm(position_back, lean[:, :width], TN) * SCALE
    key_cols = (key_sum[...] * SCALE).astype(BF16)
    value_cols = value_sum[...].astype(BF16)
    dk_ref[...] = key_cols
    dv_ref[...] = value_cols
    ks_ref[...] = (key_sum[:, old:] * SCALE).T.astype(BF16)
    vs_ref[...] = value_sum[:, old:].T.astype(BF16)
    ones = jnp.ones((8, key_cols.shape[1]), BF16)
    key_total = mm(ones, key_cols, NT)[0:1]
    value_total = mm(ones, value_cols, NT)[0:1]
    sums_ref[...] += jnp.concatenate(
        [
            content_total,
            position_total,
            query_total,
            key_total,
            value_total,
            jnp.zeros((3, DH), F32),
        ],
        axis=0,
    )


def pull(weights, inverse, attended, out_grad, content_q, position_q, keys, values, table_rev, cuts):
    parts, group, seg, cols = out_grad.shape
    rows = keys.shape[2]
    queries, key_count, heads = parts * seg, parts * rows, cols // DH
    by_head = lambda size: pl.BlockSpec((parts, None, size, DH), lambda h, s: (0, s, 0, h))
    by_row = lambda: pl.BlockSpec((None, queries, DH), lambda h, s: (s, 0, h))
    by_place = lambda: pl.BlockSpec((None, DH, key_count), lambda h, s: (s, h, 0))
    grid_spec = pl.GridSpec(
        grid=(heads, group),
        in_specs=[
            pl.BlockSpec((None, None, queries, key_count), lambda h, s: (s, h, 0, 0)),
            pl.BlockSpec((None, None, queries, DH), lambda h, s: (s, h, 0, 0)),
            by_head(seg),
            by_head(seg),
            by_head(seg),
            by_head(seg),
            by_head(rows),
            by_head(rows),
            pl.BlockSpec((key_count, DH), lambda h, s: (0, h)),
        ],
        out_specs=[
            by_row(),
            by_place(),
            by_place(),
            by_row(),
            by_row(),
            pl.BlockSpec((None, DH, key_count), lambda h, s: (h, 0, 0)),
            pl.BlockSpec((None, 8, DH), lambda h, s: (h, 0, 0)),
        ],
        scratch_shapes=[
            pltpu.VMEM((key_count, DH), BF16),
            pltpu.VMEM((key_count, DH), BF16),
            pltpu.VMEM((queries, DH), BF16),
            pltpu.VMEM((BLOCK, key_count), F32),
            pltpu.VMEM((BLOCK, key_count), F32),
            pltpu.VMEM((BLOCK, key_count), BF16),
            pltpu.VMEM((BLOCK, key_count), BF16),
            pltpu.VMEM((DH, key_count), F32),
            pltpu.VMEM((DH, key_count), F32),
        ],
    )
    return pl.pallas_call(
        functools.partial(pull_kernel, cuts),
        grid_spec=grid_spec,
        out_shape=[
            jax.ShapeDtypeStruct((group, queries, cols), BF16),
            jax.ShapeDtypeStruct((group, cols, key_count), BF16),
            jax.ShapeDtypeStruct((group, cols, key_count), BF16),
            jax.ShapeDtypeStruct((group, queries, cols), BF16),
            jax.ShapeDtypeStruct((group, queries, cols), BF16),
            jax.ShapeDtypeStruct((heads, DH, key_count), F32),
            jax.ShapeDtypeStruct((heads, 8, DH), F32),
        ],
        compiler_params=pltpu.CompilerParams(
            dimension_semantics=("arbitrary", "arbitrary"), vmem_limit_bytes=50 * 2**20
        ),
        cost_estimate=cost(39),
        name="pull",
    )(weights, inverse, attended, out_grad, content_q, position_q, keys, values, table_rev)


def project_kernel(
    cuts, rows_ref, gain_ref, shift_ref, w_ref, old_ref, mem_ref, seg_ref, q_ref, k_ref, v_ref, normed
):
    rows, width = rows_ref.shape
    cols = k_ref.shape[1]
    step = 64 if rows % 64 == 0 else 32
    for low in range(0, rows, step):
        wide = rows_ref[low : low + step, :].astype(F32)
        centred = wide - jnp.mean(wide, axis=1, keepdims=True)
        rate = lax.rsqrt(jnp.mean(centred * centred, axis=1, keepdims=True) + EPSILON)
        normed[low : low + step, :] = (centred * rate * gain_ref[...] + shift_ref[...]).astype(BF16)
    cut = cuts[0] + cuts[1]
    old_ref[...] = normed[: cuts[0], :]
    mem_ref[...] = normed[cuts[0] : cut, :]
    seg_ref[...] = normed[cut:, :]
    q_ref[...] = mm(normed[cut:, :], w_ref[:, :cols], NN)
    k_ref[...] = mm(normed[...], w_ref[:, cols : 2 * cols], NN).astype(BF16)
    v_ref[...] = mm(normed[...], w_ref[:, 2 * cols : 3 * cols], NN).astype(BF16)


def project(rows_all, gain, shift, columns, cuts):
    parts, group, each, width = rows_all.shape
    cols = columns.shape[1] // 4
    block = lambda size, wide: pl.BlockSpec((None, None, size, wide), lambda p, s: (p, s, 0, 0))
    placed = lambda size: pl.BlockSpec((None, size, width), lambda p, s: (s, p, 0))
    whole = lambda *shape: pl.BlockSpec(shape, lambda p, s: (0,) * len(shape))
    shape = lambda size, kind: jax.ShapeDtypeStruct((parts, group, size, cols), kind)
    return pl.pallas_call(
        functools.partial(project_kernel, cuts),
        grid_spec=pl.GridSpec(
            grid=(parts, group),
            in_specs=[
                block(each, width),
                whole(1, width),
                whole(1, width),
                whole(width, 4 * cols),
            ],
            out_specs=[placed(size) for size in cuts]
            + [block(cuts[2], cols), block(each, cols), block(each, cols)],
            scratch_shapes=[pltpu.VMEM((each, width), BF16)],
        ),
        out_shape=[jax.ShapeDtypeStruct((group, parts * size, width), BF16) for size in cuts]
        + [shape(cuts[2], F32), shape(each, BF16), shape(each, BF16)],
        compiler_params=pltpu.CompilerParams(
            dimension_semantics=("arbitrary", "arbitrary"), vmem_limit_bytes=40 * 2**20
        ),
        cost_estimate=cost(17),
        name="project",
    )(rows_all, gain, shift, columns)


def gelu_both(x):
    near = jnp.abs(x)
    t = 1.0 / (1.0 + (0.3275911 * math.sqrt(0.5)) * near)
    bell = jnp.exp2((x * x) * (-0.5 * LOG2E))
    tail = 0.5 * 1.061405429
    for factor in (-1.453152027, 1.421413741, -0.284496736, 0.254829592):
        tail = tail * t + 0.5 * factor
    tail = tail * t * bell
    below = jnp.where(x < 0.0, tail, 1.0 - tail)
    return x * below, below + x * bell * (1.0 / math.sqrt(2.0 * math.pi))


def forward_back_kernel(
    last, n_ref, c_ref, up_ref, down_ref, shift_ref, *rest,
):
    if last:
        part_in, grad_in, part_out, part_far, grad_out, grad_far, late_ref, sums_ref = rest[:8]
        pre, slope, hidden, act, up_out, down_out, sems, part_ref, grad_ref = rest[8:]
    else:
        part_ref, grad_ref, late_ref, sums_ref = rest[:4]
        pre, slope, hidden, act, up_out, down_out, sems = rest[4:]
    tile = pl.program_id(0)
    tiles = pl.num_programs(0)
    parts, cols, units = up_ref.shape
    pair, unit_cols, width = down_ref.shape
    rows = n_ref.shape[0]
    slot = lax.rem(tile, 2)
    up_weight = up_ref[...].reshape(width, units)
    down_weight = down_ref[...].reshape(units, width)

    def copies(at, index):
        return (
            pltpu.make_async_copy(
                up_out.at[at],
                late_ref.at[:, pl.ds(0, cols), pl.ds(pl.multiple_of(index * units, units), units)],
                sems.at[at, 0],
            ),
            pltpu.make_async_copy(
                down_out.at[at],
                late_ref.at[pl.ds(index * pair, pair), pl.ds(cols, unit_cols), :],
                sems.at[at, 1],
            ),
        )

    @pl.when(tile == 0)
    def _():
        if last:
            part_ref[...] = part_in[...]
            grad_ref[...] = grad_in[...]
        else:
            part_ref[...] = jnp.zeros_like(part_ref)
            grad_ref[...] = jnp.zeros_like(grad_ref)

    pre[...] = mm(n_ref[...], up_weight, NN)
    slope[...] = mm(c_ref[...], down_weight, NT)
    step = 64
    for low in range(0, rows, step):
        value, change = gelu_both(pre[low : low + step, :] + shift_ref[...])
        hidden[low : low + step, :] = value.astype(BF16)
        act[low : low + step, :] = (change * slope[low : low + step, :]).astype(BF16)
    part_ref[...] += mm(hidden[...], down_weight, NN)
    grad_ref[...] += mm(act[...], up_weight, NT)
    sums_ref[...] = jnp.sum(act[...].astype(F32), axis=0, keepdims=True)

    @pl.when(tile >= 2)
    def _():
        for copy in copies(slot, tile - 2):
            copy.wait()

    up_out[slot] = mm(n_ref[...], act[...], TN).astype(BF16).reshape(parts, cols, units)
    down_out[slot] = mm(hidden[...], c_ref[...], TN).astype(BF16).reshape(pair, unit_cols, width)
    for copy in copies(slot, tile):
        copy.start()

    @pl.when(tile == tiles - 1)
    def _():
        if last:
            part_out[...] = part_ref[: rows // 2, :]
            part_far[...] = part_ref[rows // 2 :, :].astype(BF16)
            grad_out[...] = grad_ref[: rows // 2, :]
            grad_far[...] = grad_ref[rows // 2 :, :].astype(BF16)
        for copy in (copies(1 - slot, tile - 1) if parts > pair else ()) + copies(slot, tile):
            copy.wait()


def forward_back(normed, cot, gathered, shift, carry):
    parts, _, width = gathered.shape
    rows = normed.shape[0]
    cols = width // parts
    unit_cols = shift.shape[1] // parts
    pair = 2
    units = pair * unit_cols
    last = len(carry) > 0
    one = pl.Buffered(1)
    whole = lambda *shape: pl.BlockSpec(shape, lambda t: (0,) * len(shape), pipeline_mode=one)
    if last:
        sums = [((rows // 2, width), F32), ((rows // 2, width), BF16)] * 2
    else:
        sums = [((rows, width), F32)] * 2
    return pl.pallas_call(
        functools.partial(forward_back_kernel, last),
        grid_spec=pl.GridSpec(
            grid=(parts // pair,),
            in_specs=[
                whole(rows, width),
                whole(rows, width),
                pl.BlockSpec((parts, cols, units), lambda t: (0, 0, t)),
                pl.BlockSpec((pair, unit_cols, width), lambda t: (t, cols // unit_cols, 0)),
                pl.BlockSpec((1, units), lambda t: (0, t)),
            ]
            + [whole(rows, width) for _ in carry],
            out_specs=[whole(*shape) for shape, _ in sums]
            + [
                pl.BlockSpec(memory_space=pl.ANY),
                pl.BlockSpec((1, units), lambda t: (0, t)),
            ],
            scratch_shapes=[
                pltpu.VMEM((rows, units), F32),
                pltpu.VMEM((rows, units), F32),
                pltpu.VMEM((rows, units), BF16),
                pltpu.VMEM((rows, units), BF16),
                pltpu.VMEM((2, parts, cols, units), BF16),
                pltpu.VMEM((2, pair, unit_cols, width), BF16),
                pltpu.SemaphoreType.DMA((2, 2)),
            ]
            + [pltpu.VMEM((rows, width), F32) for _ in carry],
        ),
        out_shape=[jax.ShapeDtypeStruct(shape, kind) for shape, kind in sums]
        + [
            jax.ShapeDtypeStruct((parts, cols + unit_cols, width), BF16),
            jax.ShapeDtypeStruct((1, parts * unit_cols), F32),
        ],
        compiler_params=pltpu.CompilerParams(
            dimension_semantics=("arbitrary",), vmem_limit_bytes=56 * 2**20
        ),
        cost_estimate=cost(29),
        name="forward_back",
    )(normed, cot, gathered, gathered, shift, *carry)


def leave_kernel(a_ref, s_ref, w_ref, shift_ref, gain_ref, bias_ref, flat_ref, m_ref, n_ref):
    parts = a_ref.shape[0]
    flat_ref[...] = jnp.concatenate([a_ref[part] for part in range(parts)], axis=1)
    weight = w_ref[...].reshape(flat_ref.shape[1], flat_ref.shape[1])
    m_ref[...] = s_ref[...].astype(F32) + (mm(flat_ref[...], weight, NN) + shift_ref[...])
    step = 32
    for low in range(0, m_ref.shape[0], step):
        unit, _ = standardise(m_ref[low : low + step, :])
        n_ref[low : low + step, :] = (unit * gain_ref[...] + bias_ref[...]).astype(BF16)


def leave(mixed_heads, segment, base, gathered, shift, gain, bias):
    parts, group, seg, cols = mixed_heads.shape
    width = parts * cols
    at = gathered.shape[1] // cols - 1
    rows = lambda: pl.BlockSpec((None, seg, width), lambda s: (s, 0, 0))
    vector = lambda: pl.BlockSpec((1, width), lambda s: (0, 0))
    shape = lambda kind: jax.ShapeDtypeStruct((group, seg, width), kind)
    return pl.pallas_call(
        leave_kernel,
        grid_spec=pl.GridSpec(
            grid=(group,),
            in_specs=[
                pl.BlockSpec((parts, None, seg, cols), lambda s: (0, s, 0, 0)),
                pl.BlockSpec((None, seg, width), lambda s: (s + base, 0, 0)),
                pl.BlockSpec((parts, cols, width), lambda s: (0, at, 0)),
                vector(),
                vector(),
                vector(),
            ],
            out_specs=[rows(), rows(), rows()],
        ),
        out_shape=[shape(BF16), shape(F32), shape(BF16)],
        compiler_params=pltpu.CompilerParams(vmem_limit_bytes=32 * 2**20),
        cost_estimate=cost(6),
        name="leave",
    )(mixed_heads, segment, gathered, shift, gain, bias)


def enter_kernel(
    m_ref, g_ref, far_ref, c_ref, w_ref, gain_ref, mg_ref, b_ref, a_ref, sums_ref
):
    @pl.when(pl.program_id(0) == 0)
    def _():
        sums_ref[...] = jnp.zeros_like(sums_ref)

    parts = a_ref.shape[0]
    rows, width = m_ref.shape
    step = 32
    total = [jnp.zeros((1, width), F32) for _ in range(4)]
    for low in range(0, rows, step):
        at = slice(low, low + step)
        unit, rate = standardise(m_ref[at, :])
        grad = g_ref[at, :] + far_ref[at, :].astype(F32)
        cot = c_ref[at, :].astype(F32)
        middle_grad = cot + standardise_back(unit, rate, grad, gain_ref[...])
        branch = middle_grad.astype(BF16)
        mg_ref[at, :] = middle_grad
        b_ref[at, :] = branch
        for i, value in enumerate((branch.astype(F32), grad * unit, grad, cot)):
            total[i] = total[i] + jnp.sum(value, axis=0, keepdims=True)
    sums_ref[...] += jnp.concatenate(total + [jnp.zeros((4, width), F32)], axis=0)
    for part in range(parts):
        a_ref[part] = mm(b_ref[...], w_ref[part], NT).astype(BF16)


def enter(middle, grad, far, cot, base, gathered, gain):
    group, seg, width = middle.shape
    parts = gathered.shape[0]
    cols = width // parts
    at = gathered.shape[1] // cols - 1
    rows = lambda: pl.BlockSpec((None, seg, width), lambda s: (s, 0, 0))
    later = lambda: pl.BlockSpec((None, seg, width), lambda s: (s + base, 0, 0))
    shape = lambda kind: jax.ShapeDtypeStruct((group, seg, width), kind)
    return pl.pallas_call(
        enter_kernel,
        grid_spec=pl.GridSpec(
            grid=(group,),
            in_specs=[
                rows(),
                later(),
                later(),
                later(),
                pl.BlockSpec((parts, cols, width), lambda s: (0, at, 0)),
                pl.BlockSpec((1, width), lambda s: (0, 0)),
            ],
            out_specs=[
                rows(),
                rows(),
                pl.BlockSpec((parts, None, seg, cols), lambda s: (0, s, 0, 0)),
                pl.BlockSpec((8, width), lambda s: (0, 0)),
            ],
        ),
        out_shape=[
            shape(F32),
            shape(BF16),
            jax.ShapeDtypeStruct((parts, group, seg, cols), BF16),
            jax.ShapeDtypeStruct((8, width), F32),
        ],
        compiler_params=pltpu.CompilerParams(
            dimension_semantics=("arbitrary",), vmem_limit_bytes=32 * 2**20
        ),
        cost_estimate=cost(7),
        name="enter",
    )(middle, grad, far, cot, gathered, gain)


def compress_kernel(low, rows_ref, w_ref, shift_ref, out_ref, wide):
    count = out_ref.shape[0]
    cols = out_ref.shape[1]
    blocks = wide.shape[0]
    for at in range(blocks):
        wide[at] = rows_ref[low : low + 3 * count, at * LANES : (at + 1) * LANES].astype(F32)
    total = jnp.broadcast_to(shift_ref[...], (count, cols))
    for k in range(3):
        every = jnp.concatenate(
            [wide[at, pl.ds(k, count, stride=3), :] for at in range(blocks)], axis=1
        ).astype(BF16)
        total = total + mm(every, w_ref[:, k * cols : (k + 1) * cols], NN)
    out_ref[...] = total.astype(BF16)


def compress(rows_all, columns, shift, low, count):
    parts, group, each, width = rows_all.shape
    cols = columns.shape[1] // 3
    return pl.pallas_call(
        functools.partial(compress_kernel, low),
        grid_spec=pl.GridSpec(
            grid=(parts, group),
            in_specs=[
                pl.BlockSpec((None, None, each, width), lambda p, s: (p, s, 0, 0)),
                pl.BlockSpec((width, 3 * cols), lambda p, s: (0, 0)),
                pl.BlockSpec((1, cols), lambda p, s: (0, 0)),
            ],
            out_specs=pl.BlockSpec((None, None, count, cols), lambda p, s: (p, s, 0, 0)),
            scratch_shapes=[pltpu.VMEM((width // LANES, 3 * count, LANES), F32)],
        ),
        out_shape=jax.ShapeDtypeStruct((parts, group, count, cols), BF16),
        compiler_params=pltpu.CompilerParams(
            dimension_semantics=("arbitrary", "arbitrary"), vmem_limit_bytes=32 * 2**20
        ),
        cost_estimate=cost(6.5),
        name="compress",
    )(rows_all, columns, shift)


def lay_out_kernel(
    parts, unit_cols, core_ref, a_ref, b_ref, c_ref, d_ref, up_ref, down_ref
):
    flipped = core_ref[0] == 1
    for half, (mine_ref, far_ref) in enumerate(((a_ref, c_ref), (b_ref, d_ref))):
        mine, far = mine_ref[...].astype(F32), far_ref[...].astype(F32)
        for core, value in enumerate(
            (jnp.where(flipped, far, mine), jnp.where(flipped, mine, far))
        ):
            for part in range(parts):
                at = ((part * 2 + core) * 2 + half) * unit_cols
                up_ref[:, at : at + unit_cols] = value[
                    0, :, part * unit_cols : (part + 1) * unit_cols
                ]
            down_ref[2 * core + half] = value[1]


def lay_out(core, mine, far, parts):
    _, rows, width = mine.shape
    step = rows // 4 if rows % 64 == 0 else rows
    half = lambda i: pl.BlockSpec((2, step, width), lambda r, *_: (i, r, 0))
    return pl.pallas_call(
        functools.partial(lay_out_kernel, parts, rows),
        grid_spec=pltpu.PrefetchScalarGridSpec(
            num_scalar_prefetch=1,
            grid=(rows // step,),
            in_specs=[half(0), half(1), half(0), half(1)],
            out_specs=[
                pl.BlockSpec((step, 4 * width), lambda r, *_: (r, 0)),
                pl.BlockSpec((4, step, width), lambda r, *_: (0, r, 0)),
            ],
        ),
        out_shape=[
            jax.ShapeDtypeStruct((rows, 4 * width), F32),
            jax.ShapeDtypeStruct((4, rows, width), F32),
        ],
        compiler_params=pltpu.CompilerParams(vmem_limit_bytes=32 * 2**20),
        cost_estimate=cost(4),
        name="lay_out",
    )(core.reshape(1), mine, mine, far, far)


def lay_squares_kernel(in_ref, *out_refs):
    parts = in_ref.shape[0]
    cols = in_ref.shape[2] // len(out_refs)
    for at, out_ref in enumerate(out_refs):
        for part in range(parts):
            out_ref[:, part * cols : (part + 1) * cols] = in_ref[
                part, :, at * cols : (at + 1) * cols
            ].astype(F32)


def lay_squares(summed, rows):
    parts, _, wide = summed.shape
    width = parts * wide // 4
    step = rows // 2
    return pl.pallas_call(
        lay_squares_kernel,
        grid_spec=pl.GridSpec(
            grid=(2,),
            in_specs=[pl.BlockSpec((parts, step, wide), lambda i: (0, i, 0))],
            out_specs=[pl.BlockSpec((step, width), lambda i: (i, 0)) for _ in range(4)],
        ),
        out_shape=[jax.ShapeDtypeStruct((rows, width), F32) for _ in range(4)],
        compiler_params=pltpu.CompilerParams(vmem_limit_bytes=32 * 2**20),
        cost_estimate=cost(2.5),
        name="lay_squares",
    )(summed)


def settle_kernel(
    me_ref, old_ref, mem_ref, seg_ref, q_ref, k_ref, v_ref, ks_ref, vs_ref, w_ref, table_ref, dt_ref,
    sums_ref, gain_ref, shift_ref, small_ref, part_ref, out_ref, total,
):
    stream = pl.program_id(0)
    parts, rows, wide = out_ref.shape
    cols = wide // 4
    width = parts * cols

    @pl.when(stream == 0)
    def _():
        total[...] = jnp.zeros_like(total)

    total[:cols, :] += mm(q_ref[...], seg_ref[...], TN)
    for at, grad in ((cols, k_ref), (2 * cols, v_ref)):
        low = 0
        for normed in (old_ref, mem_ref, seg_ref):
            high = low + normed.shape[0]
            total[at : at + cols, :] += mm(grad[:, low:high], normed[...], NN)
            low = high
    three = jnp.concatenate([q_ref[...], ks_ref[...], vs_ref[...]], axis=1)
    part = mm(three, w_ref[:, : 3 * cols], NT).astype(BF16)
    part_ref[...] = part.reshape(part_ref.shape)

    @pl.when(stream == pl.num_programs(0) - 1)
    def _():
        heads = dt_ref.shape[0]
        rel = jnp.concatenate(
            [mm(dt_ref[head].astype(BF16), table_ref[...], NN) for head in range(heads)], axis=0
        )
        line = lambda row: jnp.concatenate(
            [sums_ref[head, row : row + 1, :] for head in range(heads)], axis=1
        )
        row_sums = jnp.concatenate([line(2), line(3), line(4)], axis=1)
        weight = w_ref[:, : 3 * cols].astype(F32)
        shift_grad = lax.dot_general(
            jnp.broadcast_to(row_sums, (8, 3 * cols)),
            weight,
            (NT, ((), ())),
            precision=lax.Precision.HIGHEST,
            preferred_element_type=F32,
        )[0:1]
        along = jnp.sum(weight.T * total[...], axis=0, keepdims=True)
        gain_grad = (along - shift_ref[...] * shift_grad) / gain_ref[...]
        for at in range(parts):
            low, high = at * cols, (at + 1) * cols
            out_ref[at, :cols, : 3 * cols] = total[:, low:high].T.astype(BF16)
            out_ref[at, :cols, 3 * cols :] = rel[:, low:high].T.astype(BF16)
            mine = (me_ref[0] == at).astype(F32)
            none = jnp.zeros((1, 2 * cols), F32)
            first = jnp.concatenate([gain_grad[:, low:high], shift_grad[:, low:high], none], axis=1)
            second = jnp.concatenate([none, mine * line(0), mine * line(1)], axis=1)
            added = jnp.concatenate([first, second, jnp.zeros((14, wide), F32)], axis=0)
            out_ref[at, cols:, :] = (small_ref[at] + added).astype(BF16)


def settle(me, normed, grads, columns, table, table_grad, sums, gain, shift, small, parts):
    group, queries, width = normed[2].shape
    cols = width // parts
    wide = 4 * cols
    block = lambda array: pl.BlockSpec((None, *array.shape[1:]), lambda s, *_: (s, 0, 0))
    whole = lambda *shape: pl.BlockSpec(
        shape, lambda s, *_: (0,) * len(shape), pipeline_mode=pl.Buffered(1)
    )
    return pl.pallas_call(
        settle_kernel,
        grid_spec=pltpu.PrefetchScalarGridSpec(
            num_scalar_prefetch=1,
            grid=(group,),
            in_specs=[block(rows) for rows in normed]
            + [block(grad) for grad in grads]
            + [
                whole(*columns.shape),
                whole(*table.shape),
                whole(*table_grad.shape),
                whole(*sums.shape),
                whole(1, width),
                whole(1, width),
                whole(*small.shape),
            ],
            out_specs=[
                pl.BlockSpec((parts, None, queries // parts, width), lambda s, *_: (0, s, 0, 0)),
                whole(parts, cols + 16, wide),
            ],
            scratch_shapes=[pltpu.VMEM((3 * cols, width), F32)],
        ),
        out_shape=[
            jax.ShapeDtypeStruct((parts, group, queries // parts, width), BF16),
            jax.ShapeDtypeStruct((parts, cols + 16, wide), BF16),
        ],
        compiler_params=pltpu.CompilerParams(
            dimension_semantics=("arbitrary",), vmem_limit_bytes=56 * 2**20
        ),
        cost_estimate=cost(14),
        name="settle",
    )(me.reshape(1), *normed, *grads, columns, table, table_grad, sums, gain, shift, small)


def standardise(rows):
    mean = jnp.mean(rows, axis=-1, keepdims=True)
    centred = rows - mean
    rate = lax.rsqrt(jnp.mean(centred * centred, axis=-1, keepdims=True) + EPSILON)
    return centred * rate, rate


def standardise_back(unit, rate, grad, gain):
    scaled = grad * gain
    mean = jnp.mean(scaled, axis=-1, keepdims=True)
    along = jnp.mean(scaled * unit, axis=-1, keepdims=True)
    return rate * (scaled - mean - unit * along)


def sinusoid_reversed(rows, width):
    positions = (rows - 1 - jnp.arange(rows, dtype=jnp.int32)).astype(F32)[:, None]
    frequency = jnp.exp(
        jnp.arange(width // 2, dtype=F32) * (-2.0 * math.log(10000.0) / width)
    )
    angles = positions * frequency[None, :]
    return jnp.concatenate([jnp.sin(angles), jnp.cos(angles)], axis=1).astype(BF16)


def dot(left, right):
    return mm(left, right, NN)


def swap(value):
    return lax.ppermute(value, "core", [(0, 1), (1, 0)])


def exchange(blocks, name, axis=0):
    count = lax.axis_size(name)
    me = lax.axis_index(name)
    block = lambda at: lax.dynamic_index_in_dim(blocks, at, axis, keepdims=False)
    return [block(me)] + [
        lax.ppermute(block(me ^ apart), name, [(i, i ^ apart) for i in range(count)])
        for apart in range(1, count)
    ]


def add_up(arrays, kind=BF16):
    total = arrays[0].astype(F32)
    for array in arrays[1:]:
        total = total + array.astype(F32)
    return total.astype(kind)


def body(
    segment, memory, compressed, eob, reset, ln1_gain, ln1_bias, w_query, w_key, w_value,
    w_out, out_bias, w_rel, bias_content, bias_position, ln2_gain, ln2_bias, w_up, up_bias,
    w_down, down_bias, conv_weight, conv_bias, cotangent,
):
    parts = lax.axis_size("seq")
    core = lax.axis_index("core")
    me = lax.axis_index("seq")
    group, seg, width = segment.shape
    mem, old = memory.shape[1], compressed.shape[1]
    cuts = (old, mem, seg)
    each = old + mem + seg
    keys_in_all = parts * each
    cols = width // parts
    wide = 4 * cols
    own = group * seg
    unit_cols = w_up.shape[1] // (4 * parts)
    barrier = lax.optimization_barrier

    def by_columns(matrices):
        count = matrices.shape[0]
        sent = matrices.reshape(count, cols, parts, cols).transpose(2, 1, 0, 3)
        return sent.reshape(parts, cols, count * cols)

    up_bias_own = lax.dynamic_slice_in_dim(up_bias, core * 2 * unit_cols, 2 * unit_cols, 0)
    vectors = jnp.concatenate(
        [ln1_gain, ln1_bias, out_bias, ln2_gain, ln2_bias, down_bias, up_bias_own]
    )
    vectors = jnp.pad(vectors.reshape(2, wide), ((0, 14), (0, 0)))
    half = cols // 2
    sent = by_columns(jnp.concatenate([jnp.stack([w_query, w_key, w_value, w_rel]), conv_weight]))
    sent = lax.dynamic_slice_in_dim(sent, core * half, half, 1)
    vectors = jnp.pad(vectors, ((0, 0), (0, 3 * cols)))
    sent = jnp.concatenate([sent, jnp.broadcast_to(vectors, (parts, *vectors.shape))], axis=1)
    got = lax.all_to_all(sent, "seq", 0, 0, tiled=True)
    spans = [(0, group)]
    local = [
        jnp.concatenate([compressed[low:high], memory[low:high], segment[low:high]], axis=1)
        for low, high in spans
    ]
    rows_all = [lax.all_gather(local[0], "seq")]
    mine = got[:, :half]
    far = swap(mine)
    columns = jnp.stack(
        [jnp.where(core == 0, mine, far), jnp.where(core == 0, far, mine)], axis=1
    ).reshape(width, 7 * cols)
    columns, conv_columns = columns[:, :wide], columns[:, wide:]
    vectors = got[:, half : half + 2, :wide].reshape(parts, 2 * wide).astype(F32)
    gain_one, shift_one, out_shift, gain_two, shift_two, down_shift = (
        vectors[:, cols * i : cols * (i + 1)].reshape(1, width) for i in range(6)
    )
    up_shift = vectors[:, 6 * cols :].reshape(parts, 2, unit_cols).transpose(1, 0, 2)
    up_shift = up_shift.reshape(2, 1, parts * unit_cols)
    up_quarters = lax.dynamic_slice_in_dim(
        w_up.reshape(cols, parts, 2, 2, unit_cols), core, 1, 2
    ).reshape(cols, parts, 2, unit_cols)
    up_quarters = [up_quarters[:, :, i].reshape(cols, width) for i in range(2)]
    down_half = lax.dynamic_slice_in_dim(w_down, core * 2 * unit_cols, 2 * unit_cols, 0)
    down_quarters = [down_half[unit_cols * i : unit_cols * (i + 1)] for i in range(2)]
    first = jnp.concatenate([up_quarters[0], down_quarters[0], w_out], axis=0)
    second = jnp.concatenate([up_quarters[1], down_quarters[1]], axis=0)
    cot_own = cotangent.reshape(own, width)
    cot_both = jnp.concatenate([cot_own, swap(cot_own)], axis=0)

    table_rev = sinusoid_reversed(keys_in_all, width)
    proj_rev = dot(table_rev, columns[:, 3 * cols :]).astype(BF16)
    index = jnp.arange(eob.shape[1], dtype=jnp.int32)[None, :]
    opens = jnp.pad(eob, ((0, 0), (1, 0)))[:, :-1] == 1
    start = lax.cummax(jnp.where(opens, index, 0), axis=1)
    shade = jnp.where((start == 0) & (reset[:, None] == 0), 0.0, MASKED)
    info = jnp.stack([start.astype(F32), shade], axis=2)
    info = jnp.pad(info, ((0, 0), (0, 0), (0, LANES - 2)))
    rows_all[0], proj_rev, info, cot_both, table_rev, columns, conv_columns, *local = barrier(
        (rows_all[0], proj_rev, info, cot_both, table_rev, columns, conv_columns, *local)
    )
    rows_all = [rows_all[0]] + [lax.all_gather(rows, "seq") for rows in local[1:]]

    kept, heads = [], []
    for batch, (low, high) in enumerate(spans):
        if batch == len(spans) - 1:
            rows_all[batch], first, *heads = barrier((rows_all[batch], first, *heads))
            first = lax.all_gather(first, "seq")
        *normed, query, keys, values = project(rows_all[batch], gain_one, shift_one, columns, cuts)
        if batch == len(spans) - 1:
            second, query = barrier((second, query))
            second = lax.all_gather(second, "seq")
        weights, inverse, mixed_heads, content_q, position_q = attend(
            query,
            bias_content.astype(F32).reshape(1, cols),
            bias_position.astype(F32).reshape(1, cols),
            keys,
            values,
            proj_rev,
            info[low:high],
            cuts,
        )
        kept.append((weights, inverse, mixed_heads, content_q, position_q, keys, values))
        heads.append(lax.all_to_all(mixed_heads, "seq", 0, 0, tiled=True))

    attended, middle, normed_two = [], [], []
    for (low, high), batch in zip(spans, heads):
        one, two, three = leave(batch, segment, low, first, out_shift, gain_two, shift_two)
        attended.append(one.reshape(-1, width))
        middle.append(two)
        normed_two.append(three.reshape(-1, width))
    both = jnp.concatenate(normed_two + [swap(rows) for rows in normed_two], axis=0)
    part, part_grad, late_one, unit_one = forward_back(both, cot_both, first, up_shift[0], ())
    late_one = lax.psum_scatter(
        late_one.reshape(-1, width), "seq", scatter_dimension=0, tiled=True
    )
    part, part_far, part_grad, grad_far, late_two, unit_two = forward_back(
        both, cot_both, second, up_shift[1], (part, part_grad)
    )
    grad_far = swap(grad_far)
    by_stream = lambda rows: rows.reshape(group, seg, width)
    middle_grad, branch_grad, head_grad, sums_two = [], [], [], 0.0
    for (low, high), batch in zip(spans, middle):
        one, two, three, four = enter(
            batch, by_stream(part_grad), by_stream(grad_far), cotangent, low, first, gain_two
        )
        middle_grad.append(one)
        branch_grad.append(two.reshape(-1, width))
        three, part_grad = barrier((three, part_grad))
        head_grad.append(lax.all_to_all(three, "seq", 0, 0, tiled=True))
        sums_two = sums_two + four
    result = part + swap(part_far).astype(F32) + down_shift
    output = (jnp.concatenate(middle).reshape(own, width) + result).astype(BF16)
    output = output.reshape(group, seg, width)

    out_shift_grad, gain_two_grad, shift_two_grad, down_shift_grad = (
        sums_two[i].reshape(parts, cols) for i in range(4)
    )
    none = jnp.zeros((parts, 2 * cols), F32)
    unit_sums = jnp.stack(
        [unit_one.reshape(parts, unit_cols), unit_two.reshape(parts, unit_cols)], axis=1
    ).reshape(parts, 2 * unit_cols)
    small = jnp.stack(
        [
            jnp.concatenate([none, out_shift_grad, gain_two_grad], axis=1),
            jnp.concatenate([shift_two_grad, down_shift_grad, none], axis=1),
            jnp.concatenate(
                [jnp.where(core == 0, unit_sums, 0.0), jnp.where(core == 1, unit_sums, 0.0)], axis=1
            ),
        ],
        axis=1,
    )
    small = jnp.pad(small, ((0, 0), (0, 13), (0, 0)))
    weights, inverse, mixed_heads, content_q, position_q, keys, values = kept[0]
    out_grad = mm(jnp.concatenate(attended), jnp.concatenate(branch_grad), TN)
    out_grad = out_grad.astype(BF16).reshape(parts, cols, width)
    late_one, small, out_grad, late_two, head_grad = barrier(
        (late_one, small, out_grad, late_two, head_grad[0])
    )
    late_two = lax.psum_scatter(
        late_two.reshape(-1, width), "seq", scatter_dimension=0, tiled=True
    )
    query_grad, *key_grads, table_grad, sums = pull(
        weights, inverse, mixed_heads, head_grad, content_q, position_q, keys, values, proj_rev, cuts
    )
    late_two, out_grad, query_grad = barrier((late_two, out_grad, query_grad))
    ff = lax.psum(jnp.concatenate([late_one, late_two]), "z")
    out_grad = exchange(out_grad, "seq")
    seg_part, square_grads = settle(
        me, normed, (query_grad, *key_grads), columns, table_rev, table_grad, sums, gain_one,
        shift_one, small, parts,
    )
    summed = lax.all_to_all(square_grads, "seq", 0, 0, tiled=True)
    conv_columns, square_grads = barrier((conv_columns, square_grads))
    packed = compress(
        rows_all[0], conv_columns, conv_bias.astype(F32).reshape(1, cols), old, mem // 3
    )
    packed = lax.all_to_all(packed, "seq", 0, 0, tiled=True)
    new_compressed = packed.transpose(1, 2, 0, 3).reshape(group, mem // 3, width)
    summed = jnp.concatenate([summed.reshape(-1, wide), add_up(out_grad).reshape(-1, wide)], axis=0)
    ff, summed, seg_part, new_compressed = barrier((ff, summed, seg_part, new_compressed))
    summed = lax.psum(summed, ("z", "core"))
    squares = parts * (cols + 16)
    out_w = summed[squares:].reshape(cols, width).astype(F32)
    summed = summed[:squares].reshape(parts, cols + 16, wide)
    seg_grad = lax.all_to_all(seg_part, "seq", 0, 0, tiled=True).astype(F32)
    seg_grad = jnp.sum(seg_grad, axis=0).reshape(own, width)
    unit_seg, rate_seg = standardise(segment.reshape(own, width).astype(F32))
    rows_grad = standardise_back(unit_seg, rate_seg, seg_grad, gain_one)
    segment_grad = jnp.concatenate(middle_grad, axis=0) + by_stream(rows_grad)

    halves = lambda rows: rows.reshape(4, unit_cols, width)
    up_w, down_w = lay_out(core, halves(ff), halves(swap(ff)), parts)
    down_w = down_w.reshape(4 * unit_cols, width)
    query_w, key_w, value_w, rel_w = lay_squares(summed, cols)
    small = jnp.sum(summed[:, cols : cols + 3].astype(F32), axis=0)
    piece = lambda row, i: small[row, cols * i : cols * (i + 1)]
    return (
        output,
        segment_grad,
        piece(0, 0),
        piece(0, 1),
        query_w,
        key_w,
        value_w,
        out_w,
        piece(0, 2),
        rel_w,
        piece(1, 2),
        piece(1, 3),
        piece(0, 3),
        piece(1, 0),
        up_w,
        small[2],
        down_w,
        piece(1, 1),
        new_compressed,
    )


def solution(mesh):
    dp = mesh.shape["dp"]
    cores = jax.sharding.Mesh(
        mesh.devices.reshape(dp // 2, 2, mesh.shape["seq"]), ("z", "core", "seq")
    )
    rows = P(("z", "core"), "seq", None)
    shard, matrix = P("seq"), P("seq", None)
    return jax.shard_map(
        body,
        mesh=cores,
        in_specs=(
            rows, rows, rows, P(("z", "core"), None), P(("z", "core")), shard, shard, matrix,
            matrix, matrix, matrix, shard, matrix, shard, shard, shard, shard, matrix, shard,
            matrix, shard, P(None, "seq", None), shard, rows,
        ),
        out_specs=(
            rows, rows, shard, shard, matrix, matrix, matrix, matrix, shard, matrix, shard,
            shard, shard, shard, matrix, shard, matrix, shard, rows,
        ),
        check_vma=False,
    )
```

```python
import functools
import math

import jax
import jax.numpy as jnp
from jax import lax
from jax.experimental import pallas as pl
from jax.experimental.pallas import tpu as pltpu
from jax.sharding import PartitionSpec as P

HEADS = 8
DH = 128
EPSILON = 1e-05
MASKED = -1e30
LANES = 128
BLOCK = 256
CHUNK = 16
VMEM_LIMIT = 60 * 2**20
SCALE = 1.0 / math.sqrt(DH)
LOG2E = 1.4426950408889634
BF16 = jnp.bfloat16
F32 = jnp.float32


def cost(microseconds):
    return pl.CostEstimate(flops=int(microseconds * 1.15e7), bytes_accessed=0, transcendentals=0)


def mm(left, right, dims):
    return lax.dot_general(left, right, (dims, ((), ())), preferred_element_type=F32)


NN = ((1,), (0,))
NT = ((1,), (1,))
TN = ((0,), (0,))


def lean_left(block, first_row, fill_columns):
    columns = block.shape[1] // LANES
    far = BLOCK - 1 - first_row
    whole, part = far // LANES, far % LANES
    turned = [
        pltpu.roll(
            block[:, LANES * t : LANES * (t + 1)], LANES - part, 1, stride=1, stride_axis=0
        )
        for t in range(columns)
    ]
    rows = lax.broadcasted_iota(jnp.int32, (block.shape[0], LANES), 0)
    lanes = lax.broadcasted_iota(jnp.int32, (block.shape[0], LANES), 1)
    near = lanes - rows < LANES - part
    out = []
    for t in range(fill_columns):
        a = turned[(t + whole) % columns]
        b = turned[(t + whole + 1) % columns]
        out.append(jnp.where(near, a, b))
    return jnp.concatenate(out, axis=1)


def lean_right(block, first_row):
    columns = block.shape[1] // LANES
    whole, part = first_row // LANES, first_row % LANES
    turned = [
        pltpu.roll(block[:, LANES * t : LANES * (t + 1)], part, 1, stride=1, stride_axis=0)
        for t in range(columns)
    ]
    rows = lax.broadcasted_iota(jnp.int32, (block.shape[0], LANES), 0)
    lanes = lax.broadcasted_iota(jnp.int32, (block.shape[0], LANES), 1)
    wrapped = lanes - rows < part
    out = []
    for t in range(columns):
        a = turned[(t - whole) % columns]
        b = turned[(t - whole - 1) % columns]
        out.append(jnp.where(wrapped, b, a))
    return jnp.concatenate(out, axis=1)


def flip_matrix(kind):
    rows = lax.broadcasted_iota(jnp.int32, (BLOCK, BLOCK), 0)
    lanes = lax.broadcasted_iota(jnp.int32, (BLOCK, BLOCK), 1)
    return (rows + lanes == BLOCK - 1).astype(F32).astype(kind)


def in_place_order(parts_ref, out_ref, cuts):
    parts = parts_ref.shape[0]
    low, base = 0, 0
    for size in cuts:
        for part in range(parts):
            out_ref[base + part * size : base + (part + 1) * size, :] = parts_ref[
                part, low : low + size, :
            ]
        low += size
        base += parts * size


def attend_kernel(
    cuts, q_ref, cb_ref, pb_ref, k_ref, v_ref, t_ref, info_ref,
    e_ref, inv_ref, o_ref, cq_ref, pq_ref,
    keys, values, raw, lean, mix, tops, sums,
):
    parts, seg, _ = q_ref.shape
    queries = parts * seg
    old = parts * (cuts[0] + cuts[1])
    in_place_order(k_ref, keys, cuts)
    in_place_order(v_ref, values, cuts)
    q = q_ref[...].reshape(queries, DH)
    content_q = (q + cb_ref[...]).astype(BF16)
    position_q = (q + pb_ref[...]).astype(BF16)
    cq_ref[...] = content_q.reshape(parts, seg, DH)
    pq_ref[...] = position_q.reshape(parts, seg, DH)
    for block in range(queries // BLOCK):
        row0 = block * BLOCK
        width = old + row0 + BLOCK
        skip = queries - BLOCK - row0
        raw[:, :width] = mm(content_q[row0 : row0 + BLOCK], keys[:width, :], NT)
        lean[:, :width] = mm(position_q[row0 : row0 + BLOCK], t_ref[skip : skip + width, :], NT)
        for chunk in range(BLOCK // CHUNK):
            r0 = chunk * CHUNK
            rows = slice(r0, r0 + CHUNK)
            turned = lean_left(lean[rows, :width], r0, width // LANES)
            score = raw[rows, :width] + turned
            start = info_ref[row0 + r0 : row0 + r0 + CHUNK, 0:1].astype(jnp.int32)
            shade = info_ref[row0 + r0 : row0 + r0 + CHUNK, 1:2]
            past = score[:, :old] + shade
            place = lax.broadcasted_iota(jnp.int32, (CHUNK, row0 + BLOCK), 1)
            own = lax.broadcasted_iota(jnp.int32, (CHUNK, row0 + BLOCK), 0) + (row0 + r0)
            now = jnp.where((place <= own) & (place >= start), score[:, old:], MASKED)
            raw[rows, :old] = past
            raw[rows, old:width] = now
            top = past[:, :LANES]
            for low in range(LANES, old, LANES):
                top = jnp.maximum(top, past[:, low : low + LANES])
            for low in range(0, row0 + BLOCK, LANES):
                top = jnp.maximum(top, now[:, low : low + LANES])
            tops[rows, :] = top
        top = jnp.max(tops[...], axis=1, keepdims=True)
        tops[...] = jnp.broadcast_to(top, (BLOCK, LANES))
        for chunk in range(BLOCK // CHUNK):
            r0 = chunk * CHUNK
            rows = slice(r0, r0 + CHUNK)
            top = tops[rows, :]
            total = jnp.zeros((CHUNK, LANES), F32)
            for low in range(0, width, LANES):
                weight = jnp.exp2((raw[rows, low : low + LANES] - top) * (SCALE * LOG2E))
                total = total + weight
                e_ref[row0 + r0 : row0 + r0 + CHUNK, low : low + LANES] = weight.astype(BF16)
            sums[rows, :] = total
        total = jnp.sum(sums[...], axis=1, keepdims=True)
        inv_ref[row0 : row0 + BLOCK, :] = jnp.broadcast_to(1.0 / total, (BLOCK, DH))
        mix[row0 : row0 + BLOCK, :] = mm(
            e_ref[row0 : row0 + BLOCK, :width], values[:width, :], NN
        )
    o_ref[...] = (mix[...] * inv_ref[...]).astype(BF16).reshape(parts, seg, DH)


def attend(query, content_shift, position_shift, keys, values, table_rev, info, cuts):
    parts, group, seg, cols = query.shape
    rows = keys.shape[2]
    queries, key_count, heads = parts * seg, parts * rows, cols // DH
    by_head = lambda size: pl.BlockSpec((parts, None, size, DH), lambda s, h: (0, s, 0, h))
    grid_spec = pl.GridSpec(
        grid=(group, heads),
        in_specs=[
            by_head(seg),
            pl.BlockSpec((1, DH), lambda s, h: (0, h)),
            pl.BlockSpec((1, DH), lambda s, h: (0, h)),
            by_head(rows),
            by_head(rows),
            pl.BlockSpec((key_count, DH), lambda s, h: (0, h)),
            pl.BlockSpec((None, queries, LANES), lambda s, h: (s, 0, 0)),
        ],
        out_specs=[
            pl.BlockSpec((None, None, queries, key_count), lambda s, h: (s, h, 0, 0)),
            pl.BlockSpec((None, None, queries, DH), lambda s, h: (s, h, 0, 0)),
            by_head(seg),
            by_head(seg),
            by_head(seg),
        ],
        scratch_shapes=[
            pltpu.VMEM((key_count, DH), BF16),
            pltpu.VMEM((key_count, DH), BF16),
            pltpu.VMEM((BLOCK, key_count), F32),
            pltpu.VMEM((BLOCK, key_count), F32),
            pltpu.VMEM((queries, DH), F32),
            pltpu.VMEM((BLOCK, LANES), F32),
            pltpu.VMEM((BLOCK, LANES), F32),
        ],
    )
    small = jax.ShapeDtypeStruct((parts, group, seg, cols), BF16)
    return pl.pallas_call(
        functools.partial(attend_kernel, cuts),
        grid_spec=grid_spec,
        out_shape=[
            jax.ShapeDtypeStruct((group, heads, queries, key_count), BF16),
            jax.ShapeDtypeStruct((group, heads, queries, DH), F32),
            small,
            small,
            small,
        ],
        compiler_params=pltpu.CompilerParams(
            dimension_semantics=("arbitrary", "arbitrary"), vmem_limit_bytes=VMEM_LIMIT
        ),
        cost_estimate=cost(40),
        name="attend",
    )(query, content_shift, position_shift, keys, values, table_rev, info)


def pull_kernel(
    cuts, e_ref, inv_ref, o_ref, g_ref, cq_ref, pq_ref, k_ref, v_ref, t_ref,
    dq_ref, dk_ref, dv_ref, ks_ref, vs_ref, dt_ref, sums_ref,
    keys, values, grad, prob, part, score, lean, key_sum, value_sum,
):
    stream = pl.program_id(1)
    parts, seg, _ = g_ref.shape
    queries = parts * seg
    old = parts * (cuts[0] + cuts[1])
    in_place_order(k_ref, keys, cuts)
    in_place_order(v_ref, values, cuts)
    out_grad = g_ref[...].reshape(queries, DH).astype(F32)
    attended = o_ref[...].reshape(queries, DH).astype(F32)
    inv = inv_ref[...]
    grad[...] = (out_grad * inv).astype(BF16)
    dots = jnp.sum(out_grad * attended, axis=1, keepdims=True) * inv
    content_q = cq_ref[...].reshape(queries, DH)
    position_q = pq_ref[...].reshape(queries, DH)

    @pl.when(stream == 0)
    def _():
        dt_ref[...] = jnp.zeros_like(dt_ref)
        sums_ref[...] = jnp.zeros_like(sums_ref)

    key_sum[...] = jnp.zeros_like(key_sum)
    value_sum[...] = jnp.zeros_like(value_sum)
    content_total = jnp.zeros((1, DH), F32)
    position_total = jnp.zeros((1, DH), F32)
    query_total = jnp.zeros((1, DH), F32)
    flip = flip_matrix(BF16)
    flip_wide = flip_matrix(F32)
    turn = lambda rows: mm(flip, rows, NN).astype(BF16)
    for block in range(queries // BLOCK):
        row0 = block * BLOCK
        width = old + row0 + BLOCK
        skip = queries - BLOCK - row0
        rows = slice(row0, row0 + BLOCK)
        dots_back = lax.dot_general(
            flip_wide,
            jnp.broadcast_to(dots[rows], (BLOCK, DH)),
            (NN, ((), ())),
            precision=lax.Precision.HIGHEST,
            preferred_element_type=F32,
        )
        content_back = turn(content_q[rows])
        position_back = turn(position_q[rows])
        prob[:, :width] = mm(turn(grad[rows, :]), values[:width, :], NT)
        part[:, :width] = mm(flip, e_ref[rows, :width], NN)
        value_sum[:, :width] += mm(grad[rows, :], e_ref[rows, :width], TN)
        for chunk in range(BLOCK // CHUNK):
            r0 = chunk * CHUNK
            mean = dots_back[r0 : r0 + CHUNK, 0:1]
            change = part[r0 : r0 + CHUNK, :width] * (prob[r0 : r0 + CHUNK, :width] - mean)
            score[r0 : r0 + CHUNK, :width] = change.astype(BF16)
            lean[r0 : r0 + CHUNK, :width] = lean_right(change, r0).astype(BF16)
        content_grad = (mm(score[:, :width], keys[:width, :], NN) * SCALE).astype(BF16).astype(F32)
        position_grad = (
            (mm(lean[:, :width], t_ref[skip : skip + width, :], NN) * SCALE)
            .astype(BF16)
            .astype(F32)
        )
        query_grad = turn((content_grad + position_grad).astype(BF16))
        content_total += jnp.sum(content_grad, axis=0, keepdims=True)
        position_total += jnp.sum(position_grad, axis=0, keepdims=True)
        query_total += jnp.sum(query_grad.astype(F32), axis=0, keepdims=True)
        dq_ref[rows, :] = query_grad
        key_sum[:, :width] += mm(content_back, score[:, :width], TN)
        dt_ref[:, skip : skip + width] += mm(position_back, lean[:, :width], TN) * SCALE
    key_cols = (key_sum[...] * SCALE).astype(BF16)
    value_cols = value_sum[...].astype(BF16)
    dk_ref[...] = key_cols
    dv_ref[...] = value_cols
    ks_ref[...] = (key_sum[:, old:] * SCALE).T.astype(BF16)
    vs_ref[...] = value_sum[:, old:].T.astype(BF16)
    ones = jnp.ones((8, key_cols.shape[1]), BF16)
    key_total = mm(ones, key_cols, NT)[0:1]
    value_total = mm(ones, value_cols, NT)[0:1]
    sums_ref[...] += jnp.concatenate(
        [
            content_total,
            position_total,
            query_total,
            key_total,
            value_total,
            jnp.zeros((3, DH), F32),
        ],
        axis=0,
    )


def pull(weights, inverse, attended, out_grad, content_q, position_q, keys, values, table_rev, cuts):
    parts, group, seg, cols = out_grad.shape
    rows = keys.shape[2]
    queries, key_count, heads = parts * seg, parts * rows, cols // DH
    by_head = lambda size: pl.BlockSpec((parts, None, size, DH), lambda h, s: (0, s, 0, h))
    by_row = lambda: pl.BlockSpec((None, queries, DH), lambda h, s: (s, 0, h))
    by_place = lambda: pl.BlockSpec((None, DH, key_count), lambda h, s: (s, h, 0))
    grid_spec = pl.GridSpec(
        grid=(heads, group),
        in_specs=[
            pl.BlockSpec((None, None, queries, key_count), lambda h, s: (s, h, 0, 0)),
            pl.BlockSpec((None, None, queries, DH), lambda h, s: (s, h, 0, 0)),
            by_head(seg),
            by_head(seg),
            by_head(seg),
            by_head(seg),
            by_head(rows),
            by_head(rows),
            pl.BlockSpec((key_count, DH), lambda h, s: (0, h)),
        ],
        out_specs=[
            by_row(),
            by_place(),
            by_place(),
            by_row(),
            by_row(),
            pl.BlockSpec((None, DH, key_count), lambda h, s: (h, 0, 0)),
            pl.BlockSpec((None, 8, DH), lambda h, s: (h, 0, 0)),
        ],
        scratch_shapes=[
            pltpu.VMEM((key_count, DH), BF16),
            pltpu.VMEM((key_count, DH), BF16),
            pltpu.VMEM((queries, DH), BF16),
            pltpu.VMEM((BLOCK, key_count), F32),
            pltpu.VMEM((BLOCK, key_count), F32),
            pltpu.VMEM((BLOCK, key_count), BF16),
            pltpu.VMEM((BLOCK, key_count), BF16),
            pltpu.VMEM((DH, key_count), F32),
            pltpu.VMEM((DH, key_count), F32),
        ],
    )
    return pl.pallas_call(
        functools.partial(pull_kernel, cuts),
        grid_spec=grid_spec,
        out_shape=[
            jax.ShapeDtypeStruct((group, queries, cols), BF16),
            jax.ShapeDtypeStruct((group, cols, key_count), BF16),
            jax.ShapeDtypeStruct((group, cols, key_count), BF16),
            jax.ShapeDtypeStruct((group, queries, cols), BF16),
            jax.ShapeDtypeStruct((group, queries, cols), BF16),
            jax.ShapeDtypeStruct((heads, DH, key_count), F32),
            jax.ShapeDtypeStruct((heads, 8, DH), F32),
        ],
        compiler_params=pltpu.CompilerParams(
            dimension_semantics=("arbitrary", "arbitrary"), vmem_limit_bytes=VMEM_LIMIT
        ),
        cost_estimate=cost(39),
        name="pull",
    )(weights, inverse, attended, out_grad, content_q, position_q, keys, values, table_rev)


def project_kernel(
    cuts, rows_ref, gain_ref, shift_ref, w_ref, old_ref, mem_ref, seg_ref, q_ref, k_ref, v_ref, normed
):
    rows, width = rows_ref.shape
    cols = k_ref.shape[1]
    step = 64 if rows % 64 == 0 else 32
    for low in range(0, rows, step):
        wide = rows_ref[low : low + step, :].astype(F32)
        centred = wide - jnp.mean(wide, axis=1, keepdims=True)
        rate = lax.rsqrt(jnp.mean(centred * centred, axis=1, keepdims=True) + EPSILON)
        normed[low : low + step, :] = (centred * rate * gain_ref[...] + shift_ref[...]).astype(BF16)
    cut = cuts[0] + cuts[1]
    old_ref[...] = normed[: cuts[0], :]
    mem_ref[...] = normed[cuts[0] : cut, :]
    seg_ref[...] = normed[cut:, :]
    q_ref[...] = mm(normed[cut:, :], w_ref[:, :cols], NN)
    k_ref[...] = mm(normed[...], w_ref[:, cols : 2 * cols], NN).astype(BF16)
    v_ref[...] = mm(normed[...], w_ref[:, 2 * cols : 3 * cols], NN).astype(BF16)


def project(rows_all, gain, shift, columns, cuts):
    parts, group, each, width = rows_all.shape
    cols = columns.shape[1] // 4
    block = lambda size, wide: pl.BlockSpec((None, None, size, wide), lambda p, s: (p, s, 0, 0))
    placed = lambda size: pl.BlockSpec((None, size, width), lambda p, s: (s, p, 0))
    whole = lambda *shape: pl.BlockSpec(shape, lambda p, s: (0,) * len(shape))
    shape = lambda size, kind: jax.ShapeDtypeStruct((parts, group, size, cols), kind)
    return pl.pallas_call(
        functools.partial(project_kernel, cuts),
        grid_spec=pl.GridSpec(
            grid=(parts, group),
            in_specs=[
                block(each, width),
                whole(1, width),
                whole(1, width),
                whole(width, 4 * cols),
            ],
            out_specs=[placed(size) for size in cuts]
            + [block(cuts[2], cols), block(each, cols), block(each, cols)],
            scratch_shapes=[pltpu.VMEM((each, width), BF16)],
        ),
        out_shape=[jax.ShapeDtypeStruct((group, parts * size, width), BF16) for size in cuts]
        + [shape(cuts[2], F32), shape(each, BF16), shape(each, BF16)],
        compiler_params=pltpu.CompilerParams(
            dimension_semantics=("arbitrary", "arbitrary"), vmem_limit_bytes=VMEM_LIMIT
        ),
        cost_estimate=cost(17),
        name="project",
    )(rows_all, gain, shift, columns)


def gelu_both(x):
    near = jnp.abs(x)
    t = 1.0 / (1.0 + (0.3275911 * math.sqrt(0.5)) * near)
    bell = jnp.exp2((x * x) * (-0.5 * LOG2E))
    tail = 0.5 * 1.061405429
    for factor in (-1.453152027, 1.421413741, -0.284496736, 0.254829592):
        tail = tail * t + 0.5 * factor
    tail = tail * t * bell
    below = jnp.where(x < 0.0, tail, 1.0 - tail)
    return x * below, below + x * bell * (1.0 / math.sqrt(2.0 * math.pi))


def forward_back_kernel(
    last, parts, pair, me_ref, n_ref, c_ref, *rest,
):
    up_refs, down_refs, shift_ref = rest[:parts], rest[parts : parts + pair], rest[parts + pair]
    rest = rest[parts + pair + 1 :]
    if last:
        part_in, grad_in, part_out, part_far, grad_out, grad_far, late_ref, sums_ref = rest[:8]
        pre, slope, hidden, act, up_out, down_out, sems, part_ref, grad_ref = rest[8:]
    else:
        part_ref, grad_ref, late_ref, sums_ref = rest[:4]
        pre, slope, hidden, act, up_out, down_out, sems = rest[4:]
    tile = pl.program_id(0)
    tiles = pl.num_programs(0)
    cols, units = up_refs[0].shape
    unit_cols, width = down_refs[0].shape
    rows = n_ref.shape[0]
    slot = lax.rem(tile, 2)
    up_weight = jnp.concatenate([ref[...] for ref in up_refs], axis=0)
    down_weight = jnp.concatenate([ref[...] for ref in down_refs], axis=0)

    def copies(at, index):
        return (
            pltpu.make_async_copy(
                up_out.at[at],
                late_ref.at[:, pl.ds(0, cols), pl.ds(pl.multiple_of(index * units, units), units)],
                sems.at[at, 0],
            ),
            pltpu.make_async_copy(
                down_out.at[at],
                late_ref.at[pl.ds(index * pair, pair), pl.ds(cols, unit_cols), :],
                sems.at[at, 1],
            ),
        )

    @pl.when(tile == 0)
    def _():
        if last:
            part_ref[...] = part_in[...]
            grad_ref[...] = grad_in[...]
        else:
            part_ref[...] = jnp.zeros_like(part_ref)
            grad_ref[...] = jnp.zeros_like(grad_ref)

    pre[...] = mm(n_ref[...], up_weight, NN)
    slope[...] = mm(c_ref[...], down_weight, NT)
    step = 64
    for low in range(0, rows, step):
        value, change = gelu_both(pre[low : low + step, :] + shift_ref[...])
        hidden[low : low + step, :] = value.astype(BF16)
        act[low : low + step, :] = (change * slope[low : low + step, :]).astype(BF16)
    part_ref[...] += mm(hidden[...], down_weight, NN)
    grad_ref[...] += mm(act[...], up_weight, NT)
    sums_ref[...] = jnp.sum(act[...].astype(F32), axis=0, keepdims=True)

    @pl.when(tile >= 2)
    def _():
        for copy in copies(slot, tile - 2):
            copy.wait()

    up_out[slot] = mm(n_ref[...], act[...], TN).astype(BF16).reshape(parts, cols, units)
    down_out[slot] = mm(hidden[...], c_ref[...], TN).astype(BF16).reshape(pair, unit_cols, width)
    for copy in copies(slot, tile):
        copy.start()

    @pl.when(tile == tiles - 1)
    def _():
        if last:
            part_out[...] = part_ref[: rows // 2, :]
            part_far[...] = part_ref[rows // 2 :, :].astype(BF16)
            grad_out[...] = grad_ref[: rows // 2, :]
            grad_far[...] = grad_ref[rows // 2 :, :].astype(BF16)
        for copy in (copies(1 - slot, tile - 1) if parts > pair else ()) + copies(slot, tile):
            copy.wait()


def forward_back(me, normed, cot, gathered, shift, carry):
    parts, _, width = gathered.shape
    rows = normed.shape[0]
    cols = width // parts
    unit_cols = shift.shape[1] // parts
    pair = 2
    units = pair * unit_cols
    last = len(carry) > 0
    one = pl.Buffered(1)
    whole = lambda *shape: pl.BlockSpec(shape, lambda t, _: (0,) * len(shape), pipeline_mode=one)
    up = lambda p: pl.BlockSpec((None, cols, units), lambda t, m: (p ^ m[0], 0, t))
    down = lambda i: pl.BlockSpec(
        (None, unit_cols, width), lambda t, m: ((t * pair + i) ^ m[0], cols // unit_cols, 0)
    )
    if last:
        sums = [((rows // 2, width), F32), ((rows // 2, width), BF16)] * 2
    else:
        sums = [((rows, width), F32)] * 2
    return pl.pallas_call(
        functools.partial(forward_back_kernel, last, parts, pair),
        grid_spec=pltpu.PrefetchScalarGridSpec(
            num_scalar_prefetch=1,
            grid=(parts // pair,),
            in_specs=[
                whole(rows, width),
                whole(rows, width),
            ]
            + [up(p) for p in range(parts)]
            + [down(i) for i in range(pair)]
            + [pl.BlockSpec((1, units), lambda t, _: (0, t))]
            + [whole(rows, width) for _ in carry],
            out_specs=[whole(*shape) for shape, _ in sums]
            + [
                pl.BlockSpec(memory_space=pl.ANY),
                pl.BlockSpec((1, units), lambda t, _: (0, t)),
            ],
            scratch_shapes=[
                pltpu.VMEM((rows, units), F32),
                pltpu.VMEM((rows, units), F32),
                pltpu.VMEM((rows, units), BF16),
                pltpu.VMEM((rows, units), BF16),
                pltpu.VMEM((2, parts, cols, units), BF16),
                pltpu.VMEM((2, pair, unit_cols, width), BF16),
                pltpu.SemaphoreType.DMA((2, 2)),
            ]
            + [pltpu.VMEM((rows, width), F32) for _ in carry],
        ),
        out_shape=[jax.ShapeDtypeStruct(shape, kind) for shape, kind in sums]
        + [
            jax.ShapeDtypeStruct((parts, cols + unit_cols, width), BF16),
            jax.ShapeDtypeStruct((1, parts * unit_cols), F32),
        ],
        compiler_params=pltpu.CompilerParams(
            dimension_semantics=("arbitrary",), vmem_limit_bytes=VMEM_LIMIT
        ),
        cost_estimate=cost(29),
        name="forward_back",
    )(me.reshape(1), normed, cot, *[gathered] * (parts + pair), shift, *carry)


def leave_kernel(a_ref, s_ref, w_ref, shift_ref, gain_ref, bias_ref, flat_ref, m_ref, n_ref):
    parts = a_ref.shape[0]
    flat_ref[...] = jnp.concatenate([a_ref[part] for part in range(parts)], axis=1)
    weight = w_ref[...].reshape(flat_ref.shape[1], flat_ref.shape[1])
    m_ref[...] = s_ref[...].astype(F32) + (mm(flat_ref[...], weight, NN) + shift_ref[...])
    step = 32
    for low in range(0, m_ref.shape[0], step):
        unit, _ = standardise(m_ref[low : low + step, :])
        n_ref[low : low + step, :] = (unit * gain_ref[...] + bias_ref[...]).astype(BF16)


def leave(mixed_heads, segment, base, gathered, shift, gain, bias):
    parts, group, seg, cols = mixed_heads.shape
    width = parts * cols
    at = gathered.shape[1] // cols - 1
    rows = lambda: pl.BlockSpec((None, seg, width), lambda s: (s, 0, 0))
    vector = lambda: pl.BlockSpec((1, width), lambda s: (0, 0))
    shape = lambda kind: jax.ShapeDtypeStruct((group, seg, width), kind)
    return pl.pallas_call(
        leave_kernel,
        grid_spec=pl.GridSpec(
            grid=(group,),
            in_specs=[
                pl.BlockSpec((parts, None, seg, cols), lambda s: (0, s, 0, 0)),
                pl.BlockSpec((None, seg, width), lambda s: (s + base, 0, 0)),
                pl.BlockSpec((parts, cols, width), lambda s: (0, at, 0)),
                vector(),
                vector(),
                vector(),
            ],
            out_specs=[rows(), rows(), rows()],
        ),
        out_shape=[shape(BF16), shape(F32), shape(BF16)],
        compiler_params=pltpu.CompilerParams(vmem_limit_bytes=VMEM_LIMIT),
        cost_estimate=cost(6),
        name="leave",
    )(mixed_heads, segment, gathered, shift, gain, bias)


def enter_kernel(
    m_ref, g_ref, far_ref, c_ref, w_ref, gain_ref, mg_ref, b_ref, a_ref, sums_ref
):
    @pl.when(pl.program_id(0) == 0)
    def _():
        sums_ref[...] = jnp.zeros_like(sums_ref)

    parts = a_ref.shape[0]
    rows, width = m_ref.shape
    step = 32
    total = [jnp.zeros((1, width), F32) for _ in range(4)]
    for low in range(0, rows, step):
        at = slice(low, low + step)
        unit, rate = standardise(m_ref[at, :])
        grad = g_ref[at, :] + far_ref[at, :].astype(F32)
        cot = c_ref[at, :].astype(F32)
        middle_grad = cot + standardise_back(unit, rate, grad, gain_ref[...])
        branch = middle_grad.astype(BF16)
        mg_ref[at, :] = middle_grad
        b_ref[at, :] = branch
        for i, value in enumerate((branch.astype(F32), grad * unit, grad, cot)):
            total[i] = total[i] + jnp.sum(value, axis=0, keepdims=True)
    sums_ref[...] += jnp.concatenate(total + [jnp.zeros((4, width), F32)], axis=0)
    for part in range(parts):
        a_ref[part] = mm(b_ref[...], w_ref[part], NT).astype(BF16)


def enter(middle, grad, far, cot, base, gathered, gain):
    group, seg, width = middle.shape
    parts = gathered.shape[0]
    cols = width // parts
    at = gathered.shape[1] // cols - 1
    rows = lambda: pl.BlockSpec((None, seg, width), lambda s: (s, 0, 0))
    later = lambda: pl.BlockSpec((None, seg, width), lambda s: (s + base, 0, 0))
    shape = lambda kind: jax.ShapeDtypeStruct((group, seg, width), kind)
    return pl.pallas_call(
        enter_kernel,
        grid_spec=pl.GridSpec(
            grid=(group,),
            in_specs=[
                rows(),
                later(),
                later(),
                later(),
                pl.BlockSpec((parts, cols, width), lambda s: (0, at, 0)),
                pl.BlockSpec((1, width), lambda s: (0, 0)),
            ],
            out_specs=[
                rows(),
                rows(),
                pl.BlockSpec((parts, None, seg, cols), lambda s: (0, s, 0, 0)),
                pl.BlockSpec((8, width), lambda s: (0, 0)),
            ],
        ),
        out_shape=[
            shape(F32),
            shape(BF16),
            jax.ShapeDtypeStruct((parts, group, seg, cols), BF16),
            jax.ShapeDtypeStruct((8, width), F32),
        ],
        compiler_params=pltpu.CompilerParams(
            dimension_semantics=("arbitrary",), vmem_limit_bytes=VMEM_LIMIT
        ),
        cost_estimate=cost(7),
        name="enter",
    )(middle, grad, far, cot, gathered, gain)


def compress_kernel(low, rows_ref, w_ref, shift_ref, out_ref, wide):
    count = out_ref.shape[0]
    cols = out_ref.shape[1]
    blocks = wide.shape[0]
    for at in range(blocks):
        wide[at] = rows_ref[low : low + 3 * count, at * LANES : (at + 1) * LANES].astype(F32)
    total = jnp.broadcast_to(shift_ref[...], (count, cols))
    for k in range(3):
        every = jnp.concatenate(
            [wide[at, pl.ds(k, count, stride=3), :] for at in range(blocks)], axis=1
        ).astype(BF16)
        total = total + mm(every, w_ref[:, k * cols : (k + 1) * cols], NN)
    out_ref[...] = total.astype(BF16)


def compress(rows_all, columns, shift, low, count):
    parts, group, each, width = rows_all.shape
    cols = columns.shape[1] // 3
    return pl.pallas_call(
        functools.partial(compress_kernel, low),
        grid_spec=pl.GridSpec(
            grid=(parts, group),
            in_specs=[
                pl.BlockSpec((None, None, each, width), lambda p, s: (p, s, 0, 0)),
                pl.BlockSpec((width, 3 * cols), lambda p, s: (0, 0)),
                pl.BlockSpec((1, cols), lambda p, s: (0, 0)),
            ],
            out_specs=pl.BlockSpec((None, None, count, cols), lambda p, s: (p, s, 0, 0)),
            scratch_shapes=[pltpu.VMEM((width // LANES, 3 * count, LANES), F32)],
        ),
        out_shape=jax.ShapeDtypeStruct((parts, group, count, cols), BF16),
        compiler_params=pltpu.CompilerParams(
            dimension_semantics=("arbitrary", "arbitrary"), vmem_limit_bytes=VMEM_LIMIT
        ),
        cost_estimate=cost(6.5),
        name="compress",
    )(rows_all, columns, shift)


def lay_out_kernel(
    parts, unit_cols, core_ref, a_ref, b_ref, c_ref, d_ref, up_ref, down_ref
):
    flipped = core_ref[0] == 1
    for half, (mine_ref, far_ref) in enumerate(((a_ref, c_ref), (b_ref, d_ref))):
        mine, far = mine_ref[...].astype(F32), far_ref[...].astype(F32)
        for core, value in enumerate(
            (jnp.where(flipped, far, mine), jnp.where(flipped, mine, far))
        ):
            for part in range(parts):
                at = ((part * 2 + core) * 2 + half) * unit_cols
                up_ref[:, at : at + unit_cols] = value[
                    0, :, part * unit_cols : (part + 1) * unit_cols
                ]
            down_ref[2 * core + half] = value[1]


def lay_out(core, mine, far, parts):
    _, rows, width = mine.shape
    step = rows // 4 if rows % 64 == 0 else rows
    half = lambda i: pl.BlockSpec((2, step, width), lambda r, *_: (i, r, 0))
    return pl.pallas_call(
        functools.partial(lay_out_kernel, parts, rows),
        grid_spec=pltpu.PrefetchScalarGridSpec(
            num_scalar_prefetch=1,
            grid=(rows // step,),
            in_specs=[half(0), half(1), half(0), half(1)],
            out_specs=[
                pl.BlockSpec((step, 4 * width), lambda r, *_: (r, 0)),
                pl.BlockSpec((4, step, width), lambda r, *_: (0, r, 0)),
            ],
        ),
        out_shape=[
            jax.ShapeDtypeStruct((rows, 4 * width), F32),
            jax.ShapeDtypeStruct((4, rows, width), F32),
        ],
        compiler_params=pltpu.CompilerParams(vmem_limit_bytes=VMEM_LIMIT),
        cost_estimate=cost(4),
        name="lay_out",
    )(core.reshape(1), mine, mine, far, far)


def lay_squares_kernel(in_ref, *out_refs):
    parts = in_ref.shape[0]
    cols = in_ref.shape[2] // len(out_refs)
    for at, out_ref in enumerate(out_refs):
        for part in range(parts):
            out_ref[:, part * cols : (part + 1) * cols] = in_ref[
                part, :, at * cols : (at + 1) * cols
            ].astype(F32)


def lay_squares(summed, rows):
    parts, _, wide = summed.shape
    width = parts * wide // 4
    step = rows // 2
    return pl.pallas_call(
        lay_squares_kernel,
        grid_spec=pl.GridSpec(
            grid=(2,),
            in_specs=[pl.BlockSpec((parts, step, wide), lambda i: (0, i, 0))],
            out_specs=[pl.BlockSpec((step, width), lambda i: (i, 0)) for _ in range(4)],
        ),
        out_shape=[jax.ShapeDtypeStruct((rows, width), F32) for _ in range(4)],
        compiler_params=pltpu.CompilerParams(vmem_limit_bytes=VMEM_LIMIT),
        cost_estimate=cost(2.5),
        name="lay_squares",
    )(summed)


def settle_kernel(
    me_ref, old_ref, mem_ref, seg_ref, q_ref, k_ref, v_ref, ks_ref, vs_ref, w_ref, table_ref, dt_ref,
    sums_ref, gain_ref, shift_ref, small_ref, part_ref, out_ref, total,
):
    stream = pl.program_id(0)
    parts, rows, wide = out_ref.shape
    cols = wide // 4
    width = parts * cols

    @pl.when(stream == 0)
    def _():
        total[...] = jnp.zeros_like(total)

    total[:cols, :] += mm(q_ref[...], seg_ref[...], TN)
    for at, grad in ((cols, k_ref), (2 * cols, v_ref)):
        low = 0
        for normed in (old_ref, mem_ref, seg_ref):
            high = low + normed.shape[0]
            total[at : at + cols, :] += mm(grad[:, low:high], normed[...], NN)
            low = high
    three = jnp.concatenate([q_ref[...], ks_ref[...], vs_ref[...]], axis=1)
    part = mm(three, w_ref[:, : 3 * cols], NT).astype(BF16)
    part_ref[...] = part.reshape(part_ref.shape)

    @pl.when(stream == pl.num_programs(0) - 1)
    def _():
        heads = dt_ref.shape[0]
        rel = jnp.concatenate(
            [mm(dt_ref[head].astype(BF16), table_ref[...], NN) for head in range(heads)], axis=0
        )
        line = lambda row: jnp.concatenate(
            [sums_ref[head, row : row + 1, :] for head in range(heads)], axis=1
        )
        row_sums = jnp.concatenate([line(2), line(3), line(4)], axis=1)
        weight = w_ref[:, : 3 * cols].astype(F32)
        shift_grad = lax.dot_general(
            jnp.broadcast_to(row_sums, (8, 3 * cols)),
            weight,
            (NT, ((), ())),
            precision=lax.Precision.HIGHEST,
            preferred_element_type=F32,
        )[0:1]
        along = jnp.sum(weight.T * total[...], axis=0, keepdims=True)
        gain_grad = (along - shift_ref[...] * shift_grad) / gain_ref[...]
        for at in range(parts):
            low, high = at * cols, (at + 1) * cols
            out_ref[at, :cols, : 3 * cols] = total[:, low:high].T.astype(BF16)
            out_ref[at, :cols, 3 * cols :] = rel[:, low:high].T.astype(BF16)
            mine = (me_ref[0] == at).astype(F32)
            none = jnp.zeros((1, 2 * cols), F32)
            first = jnp.concatenate([gain_grad[:, low:high], shift_grad[:, low:high], none], axis=1)
            second = jnp.concatenate([none, mine * line(0), mine * line(1)], axis=1)
            added = jnp.concatenate([first, second, jnp.zeros((14, wide), F32)], axis=0)
            out_ref[at, cols:, :] = (small_ref[at] + added).astype(BF16)


def settle(me, normed, grads, columns, table, table_grad, sums, gain, shift, small, parts):
    group, queries, width = normed[2].shape
    cols = width // parts
    wide = 4 * cols
    block = lambda array: pl.BlockSpec((None, *array.shape[1:]), lambda s, *_: (s, 0, 0))
    whole = lambda *shape: pl.BlockSpec(
        shape, lambda s, *_: (0,) * len(shape), pipeline_mode=pl.Buffered(1)
    )
    return pl.pallas_call(
        settle_kernel,
        grid_spec=pltpu.PrefetchScalarGridSpec(
            num_scalar_prefetch=1,
            grid=(group,),
            in_specs=[block(rows) for rows in normed]
            + [block(grad) for grad in grads]
            + [
                whole(*columns.shape),
                whole(*table.shape),
                whole(*table_grad.shape),
                whole(*sums.shape),
                whole(1, width),
                whole(1, width),
                whole(*small.shape),
            ],
            out_specs=[
                pl.BlockSpec((parts, None, queries // parts, width), lambda s, *_: (0, s, 0, 0)),
                whole(parts, cols + 16, wide),
            ],
            scratch_shapes=[pltpu.VMEM((3 * cols, width), F32)],
        ),
        out_shape=[
            jax.ShapeDtypeStruct((parts, group, queries // parts, width), BF16),
            jax.ShapeDtypeStruct((parts, cols + 16, wide), BF16),
        ],
        compiler_params=pltpu.CompilerParams(
            dimension_semantics=("arbitrary",), vmem_limit_bytes=VMEM_LIMIT
        ),
        cost_estimate=cost(14),
        name="settle",
    )(me.reshape(1), *normed, *grads, columns, table, table_grad, sums, gain, shift, small)


def standardise(rows):
    mean = jnp.mean(rows, axis=-1, keepdims=True)
    centred = rows - mean
    rate = lax.rsqrt(jnp.mean(centred * centred, axis=-1, keepdims=True) + EPSILON)
    return centred * rate, rate


def standardise_back(unit, rate, grad, gain):
    scaled = grad * gain
    mean = jnp.mean(scaled, axis=-1, keepdims=True)
    along = jnp.mean(scaled * unit, axis=-1, keepdims=True)
    return rate * (scaled - mean - unit * along)


def sinusoid_reversed(rows, width):
    positions = (rows - 1 - jnp.arange(rows, dtype=jnp.int32)).astype(F32)[:, None]
    frequency = jnp.exp(
        jnp.arange(width // 2, dtype=F32) * (-2.0 * math.log(10000.0) / width)
    )
    angles = positions * frequency[None, :]
    return jnp.concatenate([jnp.sin(angles), jnp.cos(angles)], axis=1).astype(BF16)


def dot(left, right):
    return mm(left, right, NN)


def swap(value):
    return lax.ppermute(value, "core", [(0, 1), (1, 0)])


def exchange(blocks, name, axis=0):
    count = lax.axis_size(name)
    me = lax.axis_index(name)
    block = lambda at: lax.dynamic_index_in_dim(blocks, at, axis, keepdims=False)
    return [block(me)] + [
        lax.ppermute(block(me ^ apart), name, [(i, i ^ apart) for i in range(count)])
        for apart in range(1, count)
    ]


def add_up(arrays, kind=BF16):
    total = arrays[0].astype(F32)
    for array in arrays[1:]:
        total = total + array.astype(F32)
    return total.astype(kind)


def body(
    segment, memory, compressed, eob, reset, ln1_gain, ln1_bias, w_query, w_key, w_value,
    w_out, out_bias, w_rel, bias_content, bias_position, ln2_gain, ln2_bias, w_up, up_bias,
    w_down, down_bias, conv_weight, conv_bias, cotangent,
):
    parts = lax.axis_size("seq")
    core = lax.axis_index("core")
    me = lax.axis_index("seq")
    group, seg, width = segment.shape
    mem, old = memory.shape[1], compressed.shape[1]
    cuts = (old, mem, seg)
    each = old + mem + seg
    keys_in_all = parts * each
    cols = width // parts
    wide = 4 * cols
    own = group * seg
    unit_cols = w_up.shape[1] // (4 * parts)
    barrier = lax.optimization_barrier

    def by_columns(matrices):
        count = matrices.shape[0]
        sent = matrices.reshape(count, cols, parts, cols).transpose(2, 1, 0, 3)
        return sent.reshape(parts, cols, count * cols)

    up_bias_own = lax.dynamic_slice_in_dim(up_bias, core * 2 * unit_cols, 2 * unit_cols, 0)
    vectors = jnp.concatenate(
        [ln1_gain, ln1_bias, out_bias, ln2_gain, ln2_bias, down_bias, up_bias_own]
    )
    vectors = jnp.pad(vectors.reshape(2, wide), ((0, 14), (0, 0)))
    half = cols // 2
    sent = by_columns(jnp.concatenate([jnp.stack([w_query, w_key, w_value, w_rel]), conv_weight]))
    sent = lax.dynamic_slice_in_dim(sent, core * half, half, 1)
    vectors = jnp.pad(vectors, ((0, 0), (0, 3 * cols)))
    sent = jnp.concatenate([sent, jnp.broadcast_to(vectors, (parts, *vectors.shape))], axis=1)
    got = lax.all_to_all(sent, "seq", 0, 0, tiled=True)
    spans = [(0, group)]
    local = [
        jnp.concatenate([compressed[low:high], memory[low:high], segment[low:high]], axis=1)
        for low, high in spans
    ]
    rows_all = [lax.all_gather(local[0], "seq")]
    mine = got[:, :half]
    far = swap(mine)
    columns = jnp.stack(
        [jnp.where(core == 0, mine, far), jnp.where(core == 0, far, mine)], axis=1
    ).reshape(width, 7 * cols)
    columns, conv_columns = columns[:, :wide], columns[:, wide:]
    vectors = got[:, half : half + 2, :wide].reshape(parts, 2 * wide).astype(F32)
    gain_one, shift_one, out_shift, gain_two, shift_two, down_shift = (
        vectors[:, cols * i : cols * (i + 1)].reshape(1, width) for i in range(6)
    )
    up_shift = vectors[:, 6 * cols :].reshape(parts, 2, unit_cols).transpose(1, 0, 2)
    up_shift = up_shift.reshape(2, 1, parts * unit_cols)
    up_quarters = lax.dynamic_slice_in_dim(
        w_up.reshape(cols, parts, 2, 2, unit_cols), core, 1, 2
    ).reshape(cols, parts, 2, unit_cols)
    up_quarters = [up_quarters[:, :, i].reshape(cols, width) for i in range(2)]
    down_half = lax.dynamic_slice_in_dim(w_down, core * 2 * unit_cols, 2 * unit_cols, 0)
    down_quarters = [down_half[unit_cols * i : unit_cols * (i + 1)] for i in range(2)]
    first = jnp.concatenate([up_quarters[0], down_quarters[0], w_out], axis=0)
    second = jnp.concatenate([up_quarters[1], down_quarters[1]], axis=0)
    cot_own = cotangent.reshape(own, width)
    cot_both = jnp.concatenate([cot_own, swap(cot_own)], axis=0)

    table_rev = sinusoid_reversed(keys_in_all, width)
    proj_rev = dot(table_rev, columns[:, 3 * cols :]).astype(BF16)
    index = jnp.arange(eob.shape[1], dtype=jnp.int32)[None, :]
    opens = jnp.pad(eob, ((0, 0), (1, 0)))[:, :-1] == 1
    start = lax.cummax(jnp.where(opens, index, 0), axis=1)
    shade = jnp.where((start == 0) & (reset[:, None] == 0), 0.0, MASKED)
    info = jnp.stack([start.astype(F32), shade], axis=2)
    info = jnp.pad(info, ((0, 0), (0, 0), (0, LANES - 2)))
    rows_all[0], proj_rev, info, cot_both, table_rev, columns, conv_columns, *local = barrier(
        (rows_all[0], proj_rev, info, cot_both, table_rev, columns, conv_columns, *local)
    )
    rows_all = [rows_all[0]] + [lax.all_gather(rows, "seq") for rows in local[1:]]

    kept, heads = [], []
    for batch, (low, high) in enumerate(spans):
        if batch == len(spans) - 1:
            rows_all[batch], first, *heads = barrier((rows_all[batch], first, *heads))
            first = lax.all_gather(first, "seq")
        *normed, query, keys, values = project(rows_all[batch], gain_one, shift_one, columns, cuts)
        weights, inverse, mixed_heads, content_q, position_q = attend(
            query,
            bias_content.astype(F32).reshape(1, cols),
            bias_position.astype(F32).reshape(1, cols),
            keys,
            values,
            proj_rev,
            info[low:high],
            cuts,
        )
        kept.append((weights, inverse, mixed_heads, content_q, position_q, keys, values))
        heads.append(lax.all_to_all(mixed_heads, "seq", 0, 0, tiled=True))

    mixed_heads, conv_columns = barrier((mixed_heads, conv_columns))
    packed = compress(
        rows_all[0], conv_columns, conv_bias.astype(F32).reshape(1, cols), old, mem // 3
    )
    second, packed, *heads = barrier((second, packed, *heads))
    second = jnp.stack(
        [second]
        + [
            lax.ppermute(second, "seq", [(i, i ^ apart) for i in range(parts)])
            for apart in range(1, parts)
        ]
    )
    attended, middle, normed_two = [], [], []
    for (low, high), batch in zip(spans, heads):
        one, two, three = leave(batch, segment, low, first, out_shift, gain_two, shift_two)
        attended.append(one.reshape(-1, width))
        middle.append(two)
        normed_two.append(three.reshape(-1, width))
    both = jnp.concatenate(normed_two + [swap(rows) for rows in normed_two], axis=0)
    part, part_grad, late_one, unit_one = forward_back(
        jnp.zeros_like(me), both, cot_both, first, up_shift[0], ()
    )
    late_one = lax.psum_scatter(
        late_one.reshape(-1, width), "seq", scatter_dimension=0, tiled=True
    )
    part, part_far, part_grad, grad_far, late_two, unit_two = forward_back(
        me, both, cot_both, second, up_shift[1], (part, part_grad)
    )
    grad_far = swap(grad_far)
    by_stream = lambda rows: rows.reshape(group, seg, width)
    middle_grad, branch_grad, head_grad, sums_two = [], [], [], 0.0
    for (low, high), batch in zip(spans, middle):
        one, two, three, four = enter(
            batch, by_stream(part_grad), by_stream(grad_far), cotangent, low, first, gain_two
        )
        middle_grad.append(one)
        branch_grad.append(two.reshape(-1, width))
        three, part_grad = barrier((three, part_grad))
        head_grad.append(lax.all_to_all(three, "seq", 0, 0, tiled=True))
        sums_two = sums_two + four
    result = part + swap(part_far).astype(F32) + down_shift
    output = (jnp.concatenate(middle).reshape(own, width) + result).astype(BF16)
    output = output.reshape(group, seg, width)

    out_shift_grad, gain_two_grad, shift_two_grad, down_shift_grad = (
        sums_two[i].reshape(parts, cols) for i in range(4)
    )
    none = jnp.zeros((parts, 2 * cols), F32)
    unit_sums = jnp.stack(
        [unit_one.reshape(parts, unit_cols), unit_two.reshape(parts, unit_cols)], axis=1
    ).reshape(parts, 2 * unit_cols)
    small = jnp.stack(
        [
            jnp.concatenate([none, out_shift_grad, gain_two_grad], axis=1),
            jnp.concatenate([shift_two_grad, down_shift_grad, none], axis=1),
            jnp.concatenate(
                [jnp.where(core == 0, unit_sums, 0.0), jnp.where(core == 1, unit_sums, 0.0)], axis=1
            ),
        ],
        axis=1,
    )
    small = jnp.pad(small, ((0, 0), (0, 13), (0, 0)))
    weights, inverse, mixed_heads, content_q, position_q, keys, values = kept[0]
    out_grad = mm(jnp.concatenate(attended), jnp.concatenate(branch_grad), TN)
    out_grad = out_grad.astype(BF16).reshape(parts, cols, width)
    late_one, small, out_grad, late_two, head_grad = barrier(
        (late_one, small, out_grad, late_two, head_grad[0])
    )
    late_two = lax.psum_scatter(
        late_two.reshape(-1, width), "seq", scatter_dimension=0, tiled=True
    )
    out_sent = exchange(out_grad, "seq")
    query_grad, *key_grads, table_grad, sums = pull(
        weights, inverse, mixed_heads, head_grad, content_q, position_q, keys, values, proj_rev, cuts
    )
    late_two, out_sent, query_grad = barrier((late_two, out_sent, query_grad))
    ff = lax.psum(jnp.concatenate([late_one, late_two]), "z")
    seg_part, square_grads = settle(
        me, normed, (query_grad, *key_grads), columns, table_rev, table_grad, sums, gain_one,
        shift_one, small, parts,
    )
    summed = lax.all_to_all(square_grads, "seq", 0, 0, tiled=True)
    summed, seg_part = barrier((summed, seg_part))
    summed = jnp.concatenate([summed.reshape(-1, wide), add_up(out_sent).reshape(-1, wide)], axis=0)
    ff, summed, packed = barrier((ff, summed, packed))
    summed = lax.psum(summed, ("z", "core"))
    packed = lax.all_to_all(packed, "seq", 0, 0, tiled=True)
    new_compressed = packed.transpose(1, 2, 0, 3).reshape(group, mem // 3, width)
    squares = parts * (cols + 16)
    out_w = summed[squares:].reshape(cols, width).astype(F32)
    summed = summed[:squares].reshape(parts, cols + 16, wide)
    seg_grad = lax.all_to_all(seg_part, "seq", 0, 0, tiled=True).astype(F32)
    seg_grad = jnp.sum(seg_grad, axis=0).reshape(own, width)
    unit_seg, rate_seg = standardise(segment.reshape(own, width).astype(F32))
    rows_grad = standardise_back(unit_seg, rate_seg, seg_grad, gain_one)
    segment_grad = jnp.concatenate(middle_grad, axis=0) + by_stream(rows_grad)

    halves = lambda rows: rows.reshape(4, unit_cols, width)
    up_w, down_w = lay_out(core, halves(ff), halves(swap(ff)), parts)
    down_w = down_w.reshape(4 * unit_cols, width)
    query_w, key_w, value_w, rel_w = lay_squares(summed, cols)
    small = jnp.sum(summed[:, cols : cols + 3].astype(F32), axis=0)
    piece = lambda row, i: small[row, cols * i : cols * (i + 1)]
    return (
        output,
        segment_grad,
        piece(0, 0),
        piece(0, 1),
        query_w,
        key_w,
        value_w,
        out_w,
        piece(0, 2),
        rel_w,
        piece(1, 2),
        piece(1, 3),
        piece(0, 3),
        piece(1, 0),
        up_w,
        small[2],
        down_w,
        piece(1, 1),
        new_compressed,
    )


def solution(mesh):
    dp = mesh.shape["dp"]
    cores = jax.sharding.Mesh(
        mesh.devices.reshape(dp // 2, 2, mesh.shape["seq"]), ("z", "core", "seq")
    )
    rows = P(("z", "core"), "seq", None)
    shard, matrix = P("seq"), P("seq", None)
    return jax.shard_map(
        body,
        mesh=cores,
        in_specs=(
            rows, rows, rows, P(("z", "core"), None), P(("z", "core")), shard, shard, matrix,
            matrix, matrix, matrix, shard, matrix, shard, shard, shard, shard, matrix, shard,
            matrix, shard, P(None, "seq", None), shard, rows,
        ),
        out_specs=(
            rows, rows, shard, shard, matrix, matrix, matrix, matrix, shard, matrix, shard,
            shard, shard, shard, matrix, shard, matrix, shard, rows,
        ),
        check_vma=False,
    )
```

```python
import functools
import math

import jax
import jax.numpy as jnp
from jax import lax
from jax.experimental import pallas as pl
from jax.experimental.pallas import tpu as pltpu
from jax.sharding import PartitionSpec as P

HEADS = 8
DH = 128
EPSILON = 1e-05
MASKED = -1e30
LANES = 128
BLOCK = 256
CHUNK = 16
VMEM_LIMIT = 60 * 2**20
SCALE = 1.0 / math.sqrt(DH)
LOG2E = 1.4426950408889634
BF16 = jnp.bfloat16
F32 = jnp.float32


def cost(microseconds):
    return pl.CostEstimate(flops=int(microseconds * 1.15e7), bytes_accessed=0, transcendentals=0)


def mm(left, right, dims):
    return lax.dot_general(left, right, (dims, ((), ())), preferred_element_type=F32)


NN = ((1,), (0,))
NT = ((1,), (1,))
TN = ((0,), (0,))


def lean_left(block, first_row, fill_columns):
    columns = block.shape[1] // LANES
    far = BLOCK - 1 - first_row
    whole, part = far // LANES, far % LANES
    turned = [
        pltpu.roll(
            block[:, LANES * t : LANES * (t + 1)], LANES - part, 1, stride=1, stride_axis=0
        )
        for t in range(columns)
    ]
    rows = lax.broadcasted_iota(jnp.int32, (block.shape[0], LANES), 0)
    lanes = lax.broadcasted_iota(jnp.int32, (block.shape[0], LANES), 1)
    near = lanes - rows < LANES - part
    out = []
    for t in range(fill_columns):
        a = turned[(t + whole) % columns]
        b = turned[(t + whole + 1) % columns]
        out.append(jnp.where(near, a, b))
    return jnp.concatenate(out, axis=1)


def lean_right(block, first_row):
    columns = block.shape[1] // LANES
    whole, part = first_row // LANES, first_row % LANES
    turned = [
        pltpu.roll(block[:, LANES * t : LANES * (t + 1)], part, 1, stride=1, stride_axis=0)
        for t in range(columns)
    ]
    rows = lax.broadcasted_iota(jnp.int32, (block.shape[0], LANES), 0)
    lanes = lax.broadcasted_iota(jnp.int32, (block.shape[0], LANES), 1)
    wrapped = lanes - rows < part
    out = []
    for t in range(columns):
        a = turned[(t - whole) % columns]
        b = turned[(t - whole - 1) % columns]
        out.append(jnp.where(wrapped, b, a))
    return jnp.concatenate(out, axis=1)


def flip_matrix(kind):
    rows = lax.broadcasted_iota(jnp.int32, (BLOCK, BLOCK), 0)
    lanes = lax.broadcasted_iota(jnp.int32, (BLOCK, BLOCK), 1)
    return (rows + lanes == BLOCK - 1).astype(F32).astype(kind)


def in_place_order(parts_ref, out_ref, cuts):
    parts = parts_ref.shape[0]
    low, base = 0, 0
    for size in cuts:
        for part in range(parts):
            out_ref[base + part * size : base + (part + 1) * size, :] = parts_ref[
                part, low : low + size, :
            ]
        low += size
        base += parts * size


def attend_kernel(
    cuts, q_ref, cb_ref, pb_ref, k_ref, v_ref, t_ref, info_ref,
    e_ref, inv_ref, o_ref, cq_ref, pq_ref,
    keys, values, raw, lean, mix, tops, sums,
):
    parts, seg, _ = q_ref.shape
    queries = parts * seg
    old = parts * (cuts[0] + cuts[1])
    in_place_order(k_ref, keys, cuts)
    in_place_order(v_ref, values, cuts)
    q = q_ref[...].reshape(queries, DH)
    content_q = (q + cb_ref[...]).astype(BF16)
    position_q = (q + pb_ref[...]).astype(BF16)
    cq_ref[...] = content_q.reshape(parts, seg, DH)
    pq_ref[...] = position_q.reshape(parts, seg, DH)
    for block in range(queries // BLOCK):
        row0 = block * BLOCK
        width = old + row0 + BLOCK
        skip = queries - BLOCK - row0
        raw[:, :width] = mm(content_q[row0 : row0 + BLOCK], keys[:width, :], NT)
        lean[:, :width] = mm(position_q[row0 : row0 + BLOCK], t_ref[skip : skip + width, :], NT)
        for chunk in range(BLOCK // CHUNK):
            r0 = chunk * CHUNK
            rows = slice(r0, r0 + CHUNK)
            turned = lean_left(lean[rows, :width], r0, width // LANES)
            score = raw[rows, :width] + turned
            start = info_ref[row0 + r0 : row0 + r0 + CHUNK, 0:1].astype(jnp.int32)
            shade = info_ref[row0 + r0 : row0 + r0 + CHUNK, 1:2]
            past = score[:, :old] + shade
            place = lax.broadcasted_iota(jnp.int32, (CHUNK, row0 + BLOCK), 1)
            own = lax.broadcasted_iota(jnp.int32, (CHUNK, row0 + BLOCK), 0) + (row0 + r0)
            now = jnp.where((place <= own) & (place >= start), score[:, old:], MASKED)
            raw[rows, :old] = past
            raw[rows, old:width] = now
            top = past[:, :LANES]
            for low in range(LANES, old, LANES):
                top = jnp.maximum(top, past[:, low : low + LANES])
            for low in range(0, row0 + BLOCK, LANES):
                top = jnp.maximum(top, now[:, low : low + LANES])
            tops[rows, :] = top
        top = jnp.max(tops[...], axis=1, keepdims=True)
        tops[...] = jnp.broadcast_to(top, (BLOCK, LANES))
        for chunk in range(BLOCK // CHUNK):
            r0 = chunk * CHUNK
            rows = slice(r0, r0 + CHUNK)
            top = tops[rows, :]
            total = jnp.zeros((CHUNK, LANES), F32)
            for low in range(0, width, LANES):
                weight = jnp.exp2((raw[rows, low : low + LANES] - top) * (SCALE * LOG2E))
                total = total + weight
                e_ref[row0 + r0 : row0 + r0 + CHUNK, low : low + LANES] = weight.astype(BF16)
            sums[rows, :] = total
        total = jnp.sum(sums[...], axis=1, keepdims=True)
        inv_ref[row0 : row0 + BLOCK, :] = jnp.broadcast_to(1.0 / total, (BLOCK, DH))
        mix[row0 : row0 + BLOCK, :] = mm(
            e_ref[row0 : row0 + BLOCK, :width], values[:width, :], NN
        )
    o_ref[...] = (mix[...] * inv_ref[...]).astype(BF16).reshape(parts, seg, DH)


def attend(query, content_shift, position_shift, keys, values, table_rev, info, cuts):
    parts, group, seg, cols = query.shape
    rows = keys.shape[2]
    queries, key_count, heads = parts * seg, parts * rows, cols // DH
    by_head = lambda size: pl.BlockSpec((parts, None, size, DH), lambda s, h: (0, s, 0, h))
    grid_spec = pl.GridSpec(
        grid=(group, heads),
        in_specs=[
            by_head(seg),
            pl.BlockSpec((1, DH), lambda s, h: (0, h)),
            pl.BlockSpec((1, DH), lambda s, h: (0, h)),
            by_head(rows),
            by_head(rows),
            pl.BlockSpec((key_count, DH), lambda s, h: (0, h)),
            pl.BlockSpec((None, queries, LANES), lambda s, h: (s, 0, 0)),
        ],
        out_specs=[
            pl.BlockSpec((None, None, queries, key_count), lambda s, h: (s, h, 0, 0)),
            pl.BlockSpec((None, None, queries, DH), lambda s, h: (s, h, 0, 0)),
            by_head(seg),
            by_head(seg),
            by_head(seg),
        ],
        scratch_shapes=[
            pltpu.VMEM((key_count, DH), BF16),
            pltpu.VMEM((key_count, DH), BF16),
            pltpu.VMEM((BLOCK, key_count), F32),
            pltpu.VMEM((BLOCK, key_count), F32),
            pltpu.VMEM((queries, DH), F32),
            pltpu.VMEM((BLOCK, LANES), F32),
            pltpu.VMEM((BLOCK, LANES), F32),
        ],
    )
    small = jax.ShapeDtypeStruct((parts, group, seg, cols), BF16)
    return pl.pallas_call(
        functools.partial(attend_kernel, cuts),
        grid_spec=grid_spec,
        out_shape=[
            jax.ShapeDtypeStruct((group, heads, queries, key_count), BF16),
            jax.ShapeDtypeStruct((group, heads, queries, DH), F32),
            small,
            small,
            small,
        ],
        compiler_params=pltpu.CompilerParams(
            dimension_semantics=("arbitrary", "arbitrary"), vmem_limit_bytes=VMEM_LIMIT
        ),
        cost_estimate=cost(40),
        name="attend",
    )(query, content_shift, position_shift, keys, values, table_rev, info)


def pull_kernel(
    cuts, e_ref, inv_ref, o_ref, g_ref, cq_ref, pq_ref, k_ref, v_ref, t_ref,
    dq_ref, dk_ref, dv_ref, ks_ref, vs_ref, dt_ref, sums_ref,
    keys, values, grad, prob, part, score, lean, key_sum, value_sum,
):
    stream = pl.program_id(1)
    parts, seg, _ = g_ref.shape
    queries = parts * seg
    old = parts * (cuts[0] + cuts[1])
    in_place_order(k_ref, keys, cuts)
    in_place_order(v_ref, values, cuts)
    out_grad = g_ref[...].reshape(queries, DH).astype(F32)
    attended = o_ref[...].reshape(queries, DH).astype(F32)
    inv = inv_ref[...]
    grad[...] = (out_grad * inv).astype(BF16)
    dots = jnp.sum(out_grad * attended, axis=1, keepdims=True) * inv
    content_q = cq_ref[...].reshape(queries, DH)
    position_q = pq_ref[...].reshape(queries, DH)

    @pl.when(stream == 0)
    def _():
        dt_ref[...] = jnp.zeros_like(dt_ref)
        sums_ref[...] = jnp.zeros_like(sums_ref)

    key_sum[...] = jnp.zeros_like(key_sum)
    value_sum[...] = jnp.zeros_like(value_sum)
    content_total = jnp.zeros((1, DH), F32)
    position_total = jnp.zeros((1, DH), F32)
    query_total = jnp.zeros((1, DH), F32)
    flip = flip_matrix(BF16)
    flip_wide = flip_matrix(F32)
    turn = lambda rows: mm(flip, rows, NN).astype(BF16)
    for block in range(queries // BLOCK):
        row0 = block * BLOCK
        width = old + row0 + BLOCK
        skip = queries - BLOCK - row0
        rows = slice(row0, row0 + BLOCK)
        dots_back = lax.dot_general(
            flip_wide,
            jnp.broadcast_to(dots[rows], (BLOCK, DH)),
            (NN, ((), ())),
            precision=lax.Precision.HIGHEST,
            preferred_element_type=F32,
        )
        content_back = turn(content_q[rows])
        position_back = turn(position_q[rows])
        prob[:, :width] = mm(turn(grad[rows, :]), values[:width, :], NT)
        part[:, :width] = mm(flip, e_ref[rows, :width], NN)
        value_sum[:, :width] += mm(grad[rows, :], e_ref[rows, :width], TN)
        for chunk in range(BLOCK // CHUNK):
            r0 = chunk * CHUNK
            mean = dots_back[r0 : r0 + CHUNK, 0:1]
            change = part[r0 : r0 + CHUNK, :width] * (prob[r0 : r0 + CHUNK, :width] - mean)
            score[r0 : r0 + CHUNK, :width] = change.astype(BF16)
            lean[r0 : r0 + CHUNK, :width] = lean_right(change, r0).astype(BF16)
        content_grad = (mm(score[:, :width], keys[:width, :], NN) * SCALE).astype(BF16).astype(F32)
        position_grad = (
            (mm(lean[:, :width], t_ref[skip : skip + width, :], NN) * SCALE)
            .astype(BF16)
            .astype(F32)
        )
        query_grad = turn((content_grad + position_grad).astype(BF16))
        content_total += jnp.sum(content_grad, axis=0, keepdims=True)
        position_total += jnp.sum(position_grad, axis=0, keepdims=True)
        query_total += jnp.sum(query_grad.astype(F32), axis=0, keepdims=True)
        dq_ref[rows, :] = query_grad
        key_sum[:, :width] += mm(content_back, score[:, :width], TN)
        dt_ref[:, skip : skip + width] += mm(position_back, lean[:, :width], TN) * SCALE
    key_cols = (key_sum[...] * SCALE).astype(BF16)
    value_cols = value_sum[...].astype(BF16)
    dk_ref[...] = key_cols
    dv_ref[...] = value_cols
    ks_ref[...] = (key_sum[:, old:] * SCALE).T.astype(BF16)
    vs_ref[...] = value_sum[:, old:].T.astype(BF16)
    ones = jnp.ones((8, key_cols.shape[1]), BF16)
    key_total = mm(ones, key_cols, NT)[0:1]
    value_total = mm(ones, value_cols, NT)[0:1]
    sums_ref[...] += jnp.concatenate(
        [
            content_total,
            position_total,
            query_total,
            key_total,
            value_total,
            jnp.zeros((3, DH), F32),
        ],
        axis=0,
    )


def pull(weights, inverse, attended, out_grad, content_q, position_q, keys, values, table_rev, cuts):
    parts, group, seg, cols = out_grad.shape
    rows = keys.shape[2]
    queries, key_count, heads = parts * seg, parts * rows, cols // DH
    by_head = lambda size: pl.BlockSpec((parts, None, size, DH), lambda h, s: (0, s, 0, h))
    by_row = lambda: pl.BlockSpec((None, queries, DH), lambda h, s: (s, 0, h))
    by_place = lambda: pl.BlockSpec((None, DH, key_count), lambda h, s: (s, h, 0))
    grid_spec = pl.GridSpec(
        grid=(heads, group),
        in_specs=[
            pl.BlockSpec((None, None, queries, key_count), lambda h, s: (s, h, 0, 0)),
            pl.BlockSpec((None, None, queries, DH), lambda h, s: (s, h, 0, 0)),
            by_head(seg),
            by_head(seg),
            by_head(seg),
            by_head(seg),
            by_head(rows),
            by_head(rows),
            pl.BlockSpec((key_count, DH), lambda h, s: (0, h)),
        ],
        out_specs=[
            by_row(),
            by_place(),
            by_place(),
            by_row(),
            by_row(),
            pl.BlockSpec((None, DH, key_count), lambda h, s: (h, 0, 0)),
            pl.BlockSpec((None, 8, DH), lambda h, s: (h, 0, 0)),
        ],
        scratch_shapes=[
            pltpu.VMEM((key_count, DH), BF16),
            pltpu.VMEM((key_count, DH), BF16),
            pltpu.VMEM((queries, DH), BF16),
            pltpu.VMEM((BLOCK, key_count), F32),
            pltpu.VMEM((BLOCK, key_count), F32),
            pltpu.VMEM((BLOCK, key_count), BF16),
            pltpu.VMEM((BLOCK, key_count), BF16),
            pltpu.VMEM((DH, key_count), F32),
            pltpu.VMEM((DH, key_count), F32),
        ],
    )
    return pl.pallas_call(
        functools.partial(pull_kernel, cuts),
        grid_spec=grid_spec,
        out_shape=[
            jax.ShapeDtypeStruct((group, queries, cols), BF16),
            jax.ShapeDtypeStruct((group, cols, key_count), BF16),
            jax.ShapeDtypeStruct((group, cols, key_count), BF16),
            jax.ShapeDtypeStruct((group, queries, cols), BF16),
            jax.ShapeDtypeStruct((group, queries, cols), BF16),
            jax.ShapeDtypeStruct((heads, DH, key_count), F32),
            jax.ShapeDtypeStruct((heads, 8, DH), F32),
        ],
        compiler_params=pltpu.CompilerParams(
            dimension_semantics=("arbitrary", "arbitrary"), vmem_limit_bytes=VMEM_LIMIT
        ),
        cost_estimate=cost(39),
        name="pull",
    )(weights, inverse, attended, out_grad, content_q, position_q, keys, values, table_rev)


def project_kernel(
    cuts, rows_ref, gain_ref, shift_ref, w_ref, old_ref, mem_ref, seg_ref, q_ref, k_ref, v_ref, normed
):
    rows, width = rows_ref.shape
    cols = k_ref.shape[1]
    step = 64 if rows % 64 == 0 else 32
    for low in range(0, rows, step):
        wide = rows_ref[low : low + step, :].astype(F32)
        centred = wide - jnp.mean(wide, axis=1, keepdims=True)
        rate = lax.rsqrt(jnp.mean(centred * centred, axis=1, keepdims=True) + EPSILON)
        normed[low : low + step, :] = (centred * rate * gain_ref[...] + shift_ref[...]).astype(BF16)
    cut = cuts[0] + cuts[1]
    old_ref[...] = normed[: cuts[0], :]
    mem_ref[...] = normed[cuts[0] : cut, :]
    seg_ref[...] = normed[cut:, :]
    q_ref[...] = mm(normed[cut:, :], w_ref[:, :cols], NN)
    k_ref[...] = mm(normed[...], w_ref[:, cols : 2 * cols], NN).astype(BF16)
    v_ref[...] = mm(normed[...], w_ref[:, 2 * cols : 3 * cols], NN).astype(BF16)


def project(rows_all, gain, shift, columns, cuts):
    parts, group, each, width = rows_all.shape
    cols = columns.shape[1] // 4
    block = lambda size, wide: pl.BlockSpec((None, None, size, wide), lambda p, s: (p, s, 0, 0))
    placed = lambda size: pl.BlockSpec((None, size, width), lambda p, s: (s, p, 0))
    whole = lambda *shape: pl.BlockSpec(shape, lambda p, s: (0,) * len(shape))
    shape = lambda size, kind: jax.ShapeDtypeStruct((parts, group, size, cols), kind)
    return pl.pallas_call(
        functools.partial(project_kernel, cuts),
        grid_spec=pl.GridSpec(
            grid=(parts, group),
            in_specs=[
                block(each, width),
                whole(1, width),
                whole(1, width),
                whole(width, 4 * cols),
            ],
            out_specs=[placed(size) for size in cuts]
            + [block(cuts[2], cols), block(each, cols), block(each, cols)],
            scratch_shapes=[pltpu.VMEM((each, width), BF16)],
        ),
        out_shape=[jax.ShapeDtypeStruct((group, parts * size, width), BF16) for size in cuts]
        + [shape(cuts[2], F32), shape(each, BF16), shape(each, BF16)],
        compiler_params=pltpu.CompilerParams(
            dimension_semantics=("arbitrary", "arbitrary"), vmem_limit_bytes=VMEM_LIMIT
        ),
        cost_estimate=cost(17),
        name="project",
    )(rows_all, gain, shift, columns)


def gelu_both(x):
    near = jnp.abs(x)
    t = 1.0 / (1.0 + (0.3275911 * math.sqrt(0.5)) * near)
    bell = jnp.exp2((x * x) * (-0.5 * LOG2E))
    tail = 0.5 * 1.061405429
    for factor in (-1.453152027, 1.421413741, -0.284496736, 0.254829592):
        tail = tail * t + 0.5 * factor
    tail = tail * t * bell
    below = jnp.where(x < 0.0, tail, 1.0 - tail)
    return x * below, below + x * bell * (1.0 / math.sqrt(2.0 * math.pi))


def forward_back_kernel(
    last, parts, pair, n_ref, c_ref, *rest,
):
    up_refs, down_refs, shift_ref = rest[:parts], rest[parts : parts + pair], rest[parts + pair]
    rest = rest[parts + pair + 1 :]
    if last:
        part_in, grad_in, part_out, part_far, grad_out, grad_far, late_ref, sums_ref = rest[:8]
        pre, slope, hidden, act, up_out, down_out, sems, part_ref, grad_ref = rest[8:]
    else:
        part_ref, grad_ref, late_ref, sums_ref = rest[:4]
        pre, slope, hidden, act, up_out, down_out, sems = rest[4:]
    tile = pl.program_id(0)
    tiles = pl.num_programs(0)
    cols, units = up_refs[0].shape
    unit_cols, width = down_refs[0].shape
    rows = n_ref.shape[0]
    slot = lax.rem(tile, 2)
    up_weight = jnp.concatenate([ref[...] for ref in up_refs], axis=0)
    down_weight = jnp.concatenate([ref[...] for ref in down_refs], axis=0)

    def copies(at, index):
        return (
            pltpu.make_async_copy(
                up_out.at[at],
                late_ref.at[:, pl.ds(0, cols), pl.ds(pl.multiple_of(index * units, units), units)],
                sems.at[at, 0],
            ),
            pltpu.make_async_copy(
                down_out.at[at],
                late_ref.at[pl.ds(index * pair, pair), pl.ds(cols, unit_cols), :],
                sems.at[at, 1],
            ),
        )

    @pl.when(tile == 0)
    def _():
        if last:
            part_ref[...] = part_in[...]
            grad_ref[...] = grad_in[...]
        else:
            part_ref[...] = jnp.zeros_like(part_ref)
            grad_ref[...] = jnp.zeros_like(grad_ref)

    pre[...] = mm(n_ref[...], up_weight, NN)
    slope[...] = mm(c_ref[...], down_weight, NT)
    step = 64
    for low in range(0, rows, step):
        value, change = gelu_both(pre[low : low + step, :] + shift_ref[...])
        hidden[low : low + step, :] = value.astype(BF16)
        act[low : low + step, :] = (change * slope[low : low + step, :]).astype(BF16)
    part_ref[...] += mm(hidden[...], down_weight, NN)
    grad_ref[...] += mm(act[...], up_weight, NT)
    sums_ref[...] = jnp.sum(act[...].astype(F32), axis=0, keepdims=True)

    @pl.when(tile >= 2)
    def _():
        for copy in copies(slot, tile - 2):
            copy.wait()

    up_out[slot] = mm(n_ref[...], act[...], TN).astype(BF16).reshape(parts, cols, units)
    down_out[slot] = mm(hidden[...], c_ref[...], TN).astype(BF16).reshape(pair, unit_cols, width)
    for copy in copies(slot, tile):
        copy.start()

    @pl.when(tile == tiles - 1)
    def _():
        if last:
            part_out[...] = part_ref[: rows // 2, :]
            part_far[...] = part_ref[rows // 2 :, :].astype(BF16)
            grad_out[...] = grad_ref[: rows // 2, :]
            grad_far[...] = grad_ref[rows // 2 :, :].astype(BF16)
        for copy in (copies(1 - slot, tile - 1) if parts > pair else ()) + copies(slot, tile):
            copy.wait()


def forward_back(normed, cot, gathered, shift, carry):
    parts, _, width = gathered.shape
    rows = normed.shape[0]
    cols = width // parts
    unit_cols = shift.shape[1] // parts
    pair = 2
    units = pair * unit_cols
    last = len(carry) > 0
    one = pl.Buffered(1)
    whole = lambda *shape: pl.BlockSpec(shape, lambda t: (0,) * len(shape), pipeline_mode=one)
    up = lambda p: pl.BlockSpec((None, cols, units), lambda t: (p, 0, t))
    down = lambda i: pl.BlockSpec(
        (None, unit_cols, width), lambda t: (t * pair + i, cols // unit_cols, 0)
    )
    if last:
        sums = [((rows // 2, width), F32), ((rows // 2, width), BF16)] * 2
    else:
        sums = [((rows, width), F32)] * 2
    return pl.pallas_call(
        functools.partial(forward_back_kernel, last, parts, pair),
        grid_spec=pl.GridSpec(
            grid=(parts // pair,),
            in_specs=[
                whole(rows, width),
                whole(rows, width),
            ]
            + [up(p) for p in range(parts)]
            + [down(i) for i in range(pair)]
            + [pl.BlockSpec((1, units), lambda t: (0, t))]
            + [whole(rows, width) for _ in carry],
            out_specs=[whole(*shape) for shape, _ in sums]
            + [
                pl.BlockSpec(memory_space=pl.ANY),
                pl.BlockSpec((1, units), lambda t: (0, t)),
            ],
            scratch_shapes=[
                pltpu.VMEM((rows, units), F32),
                pltpu.VMEM((rows, units), F32),
                pltpu.VMEM((rows, units), BF16),
                pltpu.VMEM((rows, units), BF16),
                pltpu.VMEM((2, parts, cols, units), BF16),
                pltpu.VMEM((2, pair, unit_cols, width), BF16),
                pltpu.SemaphoreType.DMA((2, 2)),
            ]
            + [pltpu.VMEM((rows, width), F32) for _ in carry],
        ),
        out_shape=[jax.ShapeDtypeStruct(shape, kind) for shape, kind in sums]
        + [
            jax.ShapeDtypeStruct((parts, cols + unit_cols, width), BF16),
            jax.ShapeDtypeStruct((1, parts * unit_cols), F32),
        ],
        compiler_params=pltpu.CompilerParams(
            dimension_semantics=("arbitrary",), vmem_limit_bytes=VMEM_LIMIT
        ),
        cost_estimate=cost(29),
        name="forward_back",
    )(normed, cot, *[gathered] * (parts + pair), shift, *carry)


def leave_kernel(me_ref, a_ref, s_ref, shift_ref, gain_ref, bias_ref, *rest):
    parts = a_ref.shape[0]
    w_refs, (flat_ref, m_ref, n_ref) = rest[:parts], rest[parts:]
    flat_ref[...] = jnp.concatenate([a_ref[part] for part in range(parts)], axis=1)
    weight = jnp.concatenate([ref[...] for ref in w_refs], axis=0)
    m_ref[...] = s_ref[...].astype(F32) + (mm(flat_ref[...], weight, NN) + shift_ref[...])
    step = 32
    for low in range(0, m_ref.shape[0], step):
        unit, _ = standardise(m_ref[low : low + step, :])
        n_ref[low : low + step, :] = (unit * gain_ref[...] + bias_ref[...]).astype(BF16)


def leave(me, mixed_heads, segment, base, gathered, shift, gain, bias):
    parts, group, seg, cols = mixed_heads.shape
    width = parts * cols
    rows = lambda: pl.BlockSpec((None, seg, width), lambda s, _: (s, 0, 0))
    vector = lambda: pl.BlockSpec((1, width), lambda s, _: (0, 0))
    shape = lambda kind: jax.ShapeDtypeStruct((group, seg, width), kind)
    return pl.pallas_call(
        leave_kernel,
        grid_spec=pltpu.PrefetchScalarGridSpec(
            num_scalar_prefetch=1,
            grid=(group,),
            in_specs=[
                pl.BlockSpec((parts, None, seg, cols), lambda s, _: (0, s, 0, 0)),
                pl.BlockSpec((None, seg, width), lambda s, _: (s + base, 0, 0)),
                vector(),
                vector(),
                vector(),
            ]
            + [
                pl.BlockSpec((None, cols, width), lambda s, m, p=p: (p ^ m[0], 0, 0))
                for p in range(parts)
            ],
            out_specs=[rows(), rows(), rows()],
        ),
        out_shape=[shape(BF16), shape(F32), shape(BF16)],
        compiler_params=pltpu.CompilerParams(vmem_limit_bytes=VMEM_LIMIT),
        cost_estimate=cost(6),
        name="leave",
    )(me.reshape(1), mixed_heads, segment, shift, gain, bias, *[gathered] * parts)


def enter_kernel(me_ref, m_ref, g_ref, far_ref, c_ref, gain_ref, *rest):
    w_refs, (mg_ref, b_ref, a_ref, sums_ref) = rest[:-4], rest[-4:]

    @pl.when(pl.program_id(0) == 0)
    def _():
        sums_ref[...] = jnp.zeros_like(sums_ref)

    parts = a_ref.shape[0]
    rows, width = m_ref.shape
    step = 32
    total = [jnp.zeros((1, width), F32) for _ in range(4)]
    for low in range(0, rows, step):
        at = slice(low, low + step)
        unit, rate = standardise(m_ref[at, :])
        grad = g_ref[at, :] + far_ref[at, :].astype(F32)
        cot = c_ref[at, :].astype(F32)
        middle_grad = cot + standardise_back(unit, rate, grad, gain_ref[...])
        branch = middle_grad.astype(BF16)
        mg_ref[at, :] = middle_grad
        b_ref[at, :] = branch
        for i, value in enumerate((branch.astype(F32), grad * unit, grad, cot)):
            total[i] = total[i] + jnp.sum(value, axis=0, keepdims=True)
    sums_ref[...] += jnp.concatenate(total + [jnp.zeros((4, width), F32)], axis=0)
    for part in range(parts):
        a_ref[part] = mm(b_ref[...], w_refs[part][...], NT).astype(BF16)


def enter(me, middle, grad, far, cot, base, gathered, gain):
    group, seg, width = middle.shape
    parts = gathered.shape[0]
    cols = width // parts
    rows = lambda: pl.BlockSpec((None, seg, width), lambda s, _: (s, 0, 0))
    later = lambda: pl.BlockSpec((None, seg, width), lambda s, _: (s + base, 0, 0))
    shape = lambda kind: jax.ShapeDtypeStruct((group, seg, width), kind)
    return pl.pallas_call(
        enter_kernel,
        grid_spec=pltpu.PrefetchScalarGridSpec(
            num_scalar_prefetch=1,
            grid=(group,),
            in_specs=[
                rows(),
                later(),
                later(),
                later(),
                pl.BlockSpec((1, width), lambda s, _: (0, 0)),
            ]
            + [
                pl.BlockSpec((None, cols, width), lambda s, m, p=p: (p ^ m[0], 0, 0))
                for p in range(parts)
            ],
            out_specs=[
                rows(),
                rows(),
                pl.BlockSpec((parts, None, seg, cols), lambda s, _: (0, s, 0, 0)),
                pl.BlockSpec((8, width), lambda s, _: (0, 0)),
            ],
        ),
        out_shape=[
            shape(F32),
            shape(BF16),
            jax.ShapeDtypeStruct((parts, group, seg, cols), BF16),
            jax.ShapeDtypeStruct((8, width), F32),
        ],
        compiler_params=pltpu.CompilerParams(
            dimension_semantics=("arbitrary",), vmem_limit_bytes=VMEM_LIMIT
        ),
        cost_estimate=cost(7),
        name="enter",
    )(me.reshape(1), middle, grad, far, cot, gain, *[gathered] * parts)


def compress_kernel(low, rows_ref, w_ref, shift_ref, out_ref, wide):
    count = out_ref.shape[0]
    cols = out_ref.shape[1]
    blocks = wide.shape[0]
    for at in range(blocks):
        wide[at] = rows_ref[low : low + 3 * count, at * LANES : (at + 1) * LANES].astype(F32)
    total = jnp.broadcast_to(shift_ref[...], (count, cols))
    for k in range(3):
        every = jnp.concatenate(
            [wide[at, pl.ds(k, count, stride=3), :] for at in range(blocks)], axis=1
        ).astype(BF16)
        total = total + mm(every, w_ref[:, k * cols : (k + 1) * cols], NN)
    out_ref[...] = total.astype(BF16)


def compress(rows_all, columns, shift, low, count):
    parts, group, each, width = rows_all.shape
    cols = columns.shape[1] // 3
    return pl.pallas_call(
        functools.partial(compress_kernel, low),
        grid_spec=pl.GridSpec(
            grid=(parts, group),
            in_specs=[
                pl.BlockSpec((None, None, each, width), lambda p, s: (p, s, 0, 0)),
                pl.BlockSpec((width, 3 * cols), lambda p, s: (0, 0)),
                pl.BlockSpec((1, cols), lambda p, s: (0, 0)),
            ],
            out_specs=pl.BlockSpec((None, None, count, cols), lambda p, s: (p, s, 0, 0)),
            scratch_shapes=[pltpu.VMEM((width // LANES, 3 * count, LANES), F32)],
        ),
        out_shape=jax.ShapeDtypeStruct((parts, group, count, cols), BF16),
        compiler_params=pltpu.CompilerParams(
            dimension_semantics=("arbitrary", "arbitrary"), vmem_limit_bytes=VMEM_LIMIT
        ),
        cost_estimate=cost(6.5),
        name="compress",
    )(rows_all, columns, shift)


def lay_out_kernel(
    parts, unit_cols, core_ref, a_ref, b_ref, c_ref, d_ref, up_ref, down_ref
):
    flipped = core_ref[0] == 1
    for half, (mine_ref, far_ref) in enumerate(((a_ref, c_ref), (b_ref, d_ref))):
        mine, far = mine_ref[...].astype(F32), far_ref[...].astype(F32)
        for core, value in enumerate(
            (jnp.where(flipped, far, mine), jnp.where(flipped, mine, far))
        ):
            for part in range(parts):
                at = ((part * 2 + core) * 2 + half) * unit_cols
                up_ref[:, at : at + unit_cols] = value[
                    0, :, part * unit_cols : (part + 1) * unit_cols
                ]
            down_ref[2 * core + half] = value[1]


def lay_out(core, mine, far, parts):
    _, rows, width = mine[0].shape
    step = rows // 4 if rows % 64 == 0 else rows
    half = lambda: pl.BlockSpec((2, step, width), lambda r, *_: (0, r, 0))
    return pl.pallas_call(
        functools.partial(lay_out_kernel, parts, rows),
        grid_spec=pltpu.PrefetchScalarGridSpec(
            num_scalar_prefetch=1,
            grid=(rows // step,),
            in_specs=[half(), half(), half(), half()],
            out_specs=[
                pl.BlockSpec((step, 4 * width), lambda r, *_: (r, 0)),
                pl.BlockSpec((4, step, width), lambda r, *_: (0, r, 0)),
            ],
        ),
        out_shape=[
            jax.ShapeDtypeStruct((rows, 4 * width), F32),
            jax.ShapeDtypeStruct((4, rows, width), F32),
        ],
        compiler_params=pltpu.CompilerParams(vmem_limit_bytes=VMEM_LIMIT),
        cost_estimate=cost(4),
        name="lay_out",
    )(core.reshape(1), *mine, *far)


def lay_squares_kernel(in_ref, *out_refs):
    parts = in_ref.shape[0]
    cols = in_ref.shape[2] // len(out_refs)
    for at, out_ref in enumerate(out_refs):
        for part in range(parts):
            out_ref[:, part * cols : (part + 1) * cols] = in_ref[
                part, :, at * cols : (at + 1) * cols
            ].astype(F32)


def lay_squares(summed, rows):
    parts, _, wide = summed.shape
    width = parts * wide // 4
    step = rows // 2
    return pl.pallas_call(
        lay_squares_kernel,
        grid_spec=pl.GridSpec(
            grid=(2,),
            in_specs=[pl.BlockSpec((parts, step, wide), lambda i: (0, i, 0))],
            out_specs=[pl.BlockSpec((step, width), lambda i: (i, 0)) for _ in range(4)],
        ),
        out_shape=[jax.ShapeDtypeStruct((rows, width), F32) for _ in range(4)],
        compiler_params=pltpu.CompilerParams(vmem_limit_bytes=VMEM_LIMIT),
        cost_estimate=cost(2.5),
        name="lay_squares",
    )(summed)


def settle_kernel(
    me_ref, old_ref, mem_ref, seg_ref, q_ref, k_ref, v_ref, ks_ref, vs_ref, w_ref, table_ref, dt_ref,
    sums_ref, gain_ref, shift_ref, small_ref, part_ref, out_ref, total,
):
    stream = pl.program_id(0)
    parts, rows, wide = out_ref.shape
    cols = wide // 4
    width = parts * cols

    @pl.when(stream == 0)
    def _():
        total[...] = jnp.zeros_like(total)

    total[:cols, :] += mm(q_ref[...], seg_ref[...], TN)
    for at, grad in ((cols, k_ref), (2 * cols, v_ref)):
        low = 0
        for normed in (old_ref, mem_ref, seg_ref):
            high = low + normed.shape[0]
            total[at : at + cols, :] += mm(grad[:, low:high], normed[...], NN)
            low = high
    three = jnp.concatenate([q_ref[...], ks_ref[...], vs_ref[...]], axis=1)
    part = mm(three, w_ref[:, : 3 * cols], NT).astype(BF16)
    part_ref[...] = part.reshape(part_ref.shape)

    @pl.when(stream == pl.num_programs(0) - 1)
    def _():
        heads = dt_ref.shape[0]
        rel = jnp.concatenate(
            [mm(dt_ref[head].astype(BF16), table_ref[...], NN) for head in range(heads)], axis=0
        )
        line = lambda row: jnp.concatenate(
            [sums_ref[head, row : row + 1, :] for head in range(heads)], axis=1
        )
        row_sums = jnp.concatenate([line(2), line(3), line(4)], axis=1)
        weight = w_ref[:, : 3 * cols].astype(F32)
        shift_grad = lax.dot_general(
            jnp.broadcast_to(row_sums, (8, 3 * cols)),
            weight,
            (NT, ((), ())),
            precision=lax.Precision.HIGHEST,
            preferred_element_type=F32,
        )[0:1]
        along = jnp.sum(weight.T * total[...], axis=0, keepdims=True)
        gain_grad = (along - shift_ref[...] * shift_grad) / gain_ref[...]
        for at in range(parts):
            low, high = at * cols, (at + 1) * cols
            out_ref[at, :cols, : 3 * cols] = total[:, low:high].T.astype(BF16)
            out_ref[at, :cols, 3 * cols :] = rel[:, low:high].T.astype(BF16)
            mine = (me_ref[0] == at).astype(F32)
            none = jnp.zeros((1, 2 * cols), F32)
            first = jnp.concatenate([gain_grad[:, low:high], shift_grad[:, low:high], none], axis=1)
            second = jnp.concatenate([none, mine * line(0), mine * line(1)], axis=1)
            added = jnp.concatenate([first, second, jnp.zeros((14, wide), F32)], axis=0)
            out_ref[at, cols:, :] = (small_ref[at] + added).astype(BF16)


def settle(me, normed, grads, columns, table, table_grad, sums, gain, shift, small, parts):
    group, queries, width = normed[2].shape
    cols = width // parts
    wide = 4 * cols
    block = lambda array: pl.BlockSpec((None, *array.shape[1:]), lambda s, *_: (s, 0, 0))
    whole = lambda *shape: pl.BlockSpec(
        shape, lambda s, *_: (0,) * len(shape), pipeline_mode=pl.Buffered(1)
    )
    return pl.pallas_call(
        settle_kernel,
        grid_spec=pltpu.PrefetchScalarGridSpec(
            num_scalar_prefetch=1,
            grid=(group,),
            in_specs=[block(rows) for rows in normed]
            + [block(grad) for grad in grads]
            + [
                whole(*columns.shape),
                whole(*table.shape),
                whole(*table_grad.shape),
                whole(*sums.shape),
                whole(1, width),
                whole(1, width),
                whole(*small.shape),
            ],
            out_specs=[
                pl.BlockSpec((parts, None, queries // parts, width), lambda s, *_: (0, s, 0, 0)),
                whole(parts, cols + 16, wide),
            ],
            scratch_shapes=[pltpu.VMEM((3 * cols, width), F32)],
        ),
        out_shape=[
            jax.ShapeDtypeStruct((parts, group, queries // parts, width), BF16),
            jax.ShapeDtypeStruct((parts, cols + 16, wide), BF16),
        ],
        compiler_params=pltpu.CompilerParams(
            dimension_semantics=("arbitrary",), vmem_limit_bytes=VMEM_LIMIT
        ),
        cost_estimate=cost(14),
        name="settle",
    )(me.reshape(1), *normed, *grads, columns, table, table_grad, sums, gain, shift, small)


def standardise(rows):
    mean = jnp.mean(rows, axis=-1, keepdims=True)
    centred = rows - mean
    rate = lax.rsqrt(jnp.mean(centred * centred, axis=-1, keepdims=True) + EPSILON)
    return centred * rate, rate


def standardise_back(unit, rate, grad, gain):
    scaled = grad * gain
    mean = jnp.mean(scaled, axis=-1, keepdims=True)
    along = jnp.mean(scaled * unit, axis=-1, keepdims=True)
    return rate * (scaled - mean - unit * along)


def sinusoid_reversed(rows, width):
    positions = (rows - 1 - jnp.arange(rows, dtype=jnp.int32)).astype(F32)[:, None]
    frequency = jnp.exp(
        jnp.arange(width // 2, dtype=F32) * (-2.0 * math.log(10000.0) / width)
    )
    angles = positions * frequency[None, :]
    return jnp.concatenate([jnp.sin(angles), jnp.cos(angles)], axis=1).astype(BF16)


def dot(left, right):
    return mm(left, right, NN)


def swap(value):
    return lax.ppermute(value, "core", [(0, 1), (1, 0)])


def exchange(blocks, name, axis=0):
    count = lax.axis_size(name)
    me = lax.axis_index(name)
    block = lambda at: lax.dynamic_index_in_dim(blocks, at, axis, keepdims=False)
    return [block(me)] + [
        lax.ppermute(block(me ^ apart), name, [(i, i ^ apart) for i in range(count)])
        for apart in range(1, count)
    ]


def stack_up(block):
    parts = lax.axis_size("seq")
    return jnp.stack(
        [block]
        + [
            lax.ppermute(block, "seq", [(i, i ^ apart) for i in range(parts)])
            for apart in range(1, parts)
        ]
    )


def collect(block, name):
    count = lax.axis_size(name)
    me = lax.axis_index(name)
    found = jnp.stack(
        [block]
        + [
            lax.ppermute(block, name, [(i, i ^ apart) for i in range(count)])
            for apart in range(1, count)
        ]
    )
    return jnp.concatenate(
        [lax.dynamic_index_in_dim(found, me ^ i, 0, keepdims=False) for i in range(count)]
    )


def add_up(arrays, kind=BF16):
    total = arrays[0].astype(F32)
    for array in arrays[1:]:
        total = total + array.astype(F32)
    return total.astype(kind)


def body(
    segment, memory, compressed, eob, reset, ln1_gain, ln1_bias, w_query, w_key, w_value,
    w_out, out_bias, w_rel, bias_content, bias_position, ln2_gain, ln2_bias, w_up, up_bias,
    w_down, down_bias, conv_weight, conv_bias, cotangent,
):
    parts = lax.axis_size("seq")
    layers = lax.axis_size("z")
    core = lax.axis_index("core")
    me = lax.axis_index("seq")
    group, seg, width = segment.shape
    mem, old = memory.shape[1], compressed.shape[1]
    cuts = (old, mem, seg)
    each = old + mem + seg
    keys_in_all = parts * each
    cols = width // parts
    wide = 4 * cols
    own = group * seg
    unit_cols = w_up.shape[1] // (4 * parts)
    barrier = lax.optimization_barrier

    def by_columns(matrices):
        count = matrices.shape[0]
        sent = matrices.reshape(count, cols, parts, cols).transpose(2, 1, 0, 3)
        return sent.reshape(parts, cols, count * cols)

    up_bias_own = lax.dynamic_slice_in_dim(up_bias, core * 2 * unit_cols, 2 * unit_cols, 0)
    vectors = jnp.concatenate(
        [ln1_gain, ln1_bias, out_bias, ln2_gain, ln2_bias, down_bias, up_bias_own]
    )
    vectors = jnp.pad(vectors.reshape(2, wide), ((0, 14), (0, 0)))
    half = cols // 2
    sent = by_columns(jnp.concatenate([jnp.stack([w_query, w_key, w_value, w_rel]), conv_weight]))
    sent = lax.dynamic_slice_in_dim(sent, core * half, half, 1)
    vectors = jnp.pad(vectors, ((0, 0), (0, 3 * cols)))
    sent = jnp.concatenate([sent, jnp.broadcast_to(vectors, (parts, *vectors.shape))], axis=1)
    got = lax.all_to_all(sent, "seq", 0, 0, tiled=True)
    spans = [(0, group)]
    local = [
        jnp.concatenate([compressed[low:high], memory[low:high], segment[low:high]], axis=1)
        for low, high in spans
    ]
    rows_all = [lax.all_gather(local[0], "seq")]
    mine = got[:, :half]
    far = swap(mine)
    columns = jnp.stack(
        [jnp.where(core == 0, mine, far), jnp.where(core == 0, far, mine)], axis=1
    ).reshape(width, 7 * cols)
    columns, conv_columns = columns[:, :wide], columns[:, wide:]
    vectors = got[:, half : half + 2, :wide].reshape(parts, 2 * wide).astype(F32)
    gain_one, shift_one, out_shift, gain_two, shift_two, down_shift = (
        vectors[:, cols * i : cols * (i + 1)].reshape(1, width) for i in range(6)
    )
    up_shift = vectors[:, 6 * cols :].reshape(parts, 2, unit_cols).transpose(1, 0, 2)
    up_shift = up_shift.reshape(2, 1, parts * unit_cols)
    up_quarters = lax.dynamic_slice_in_dim(
        w_up.reshape(cols, parts, 2, 2, unit_cols), core, 1, 2
    ).reshape(cols, parts, 2, unit_cols)
    up_quarters = [up_quarters[:, :, i].reshape(cols, width) for i in range(2)]
    down_half = lax.dynamic_slice_in_dim(w_down, core * 2 * unit_cols, 2 * unit_cols, 0)
    down_quarters = [down_half[unit_cols * i : unit_cols * (i + 1)] for i in range(2)]
    first = jnp.concatenate([up_quarters[0], down_quarters[0]], axis=0)
    second = jnp.concatenate([up_quarters[1], down_quarters[1]], axis=0)
    cot_own = cotangent.reshape(own, width)
    cot_both = jnp.concatenate([cot_own, swap(cot_own)], axis=0)

    table_rev = sinusoid_reversed(keys_in_all, width)
    proj_rev = dot(table_rev, columns[:, 3 * cols :]).astype(BF16)
    index = jnp.arange(eob.shape[1], dtype=jnp.int32)[None, :]
    opens = jnp.pad(eob, ((0, 0), (1, 0)))[:, :-1] == 1
    start = lax.cummax(jnp.where(opens, index, 0), axis=1)
    shade = jnp.where((start == 0) & (reset[:, None] == 0), 0.0, MASKED)
    info = jnp.stack([start.astype(F32), shade], axis=2)
    info = jnp.pad(info, ((0, 0), (0, 0), (0, LANES - 2)))
    rows_all[0], proj_rev, info, cot_both, table_rev, columns, conv_columns, *local = barrier(
        (rows_all[0], proj_rev, info, cot_both, table_rev, columns, conv_columns, *local)
    )
    rows_all = [rows_all[0]] + [lax.all_gather(rows, "seq") for rows in local[1:]]

    kept, heads = [], []
    for batch, (low, high) in enumerate(spans):
        if batch == len(spans) - 1:
            rows_all[batch], first, *heads = barrier((rows_all[batch], first, *heads))
            first = lax.all_gather(first, "seq")
        *normed, query, keys, values = project(rows_all[batch], gain_one, shift_one, columns, cuts)
        second, out_rows, query = barrier((second, w_out, query))
        second = lax.all_gather(second, "seq")
        out_rows = stack_up(out_rows)
        weights, inverse, mixed_heads, content_q, position_q = attend(
            query,
            bias_content.astype(F32).reshape(1, cols),
            bias_position.astype(F32).reshape(1, cols),
            keys,
            values,
            proj_rev,
            info[low:high],
            cuts,
        )
        kept.append((weights, inverse, mixed_heads, content_q, position_q, keys, values))
        heads.append(lax.all_to_all(mixed_heads, "seq", 0, 0, tiled=True))

    mixed_heads, conv_columns = barrier((mixed_heads, conv_columns))
    packed = compress(
        rows_all[0], conv_columns, conv_bias.astype(F32).reshape(1, cols), old, mem // 3
    )
    packed, out_rows, *heads = barrier((packed, out_rows, *heads))

    attended, middle, normed_two = [], [], []
    for (low, high), batch in zip(spans, heads):
        one, two, three = leave(me, batch, segment, low, out_rows, out_shift, gain_two, shift_two)
        attended.append(one.reshape(-1, width))
        middle.append(two)
        normed_two.append(three.reshape(-1, width))
    both = jnp.concatenate(normed_two + [swap(rows) for rows in normed_two], axis=0)
    part, part_grad, late_one, unit_one = forward_back(both, cot_both, first, up_shift[0], ())
    late_one = lax.psum_scatter(
        late_one.reshape(-1, width), "seq", scatter_dimension=0, tiled=True
    )
    part, part_far, part_grad, grad_far, late_two, unit_two = forward_back(
        both, cot_both, second, up_shift[1], (part, part_grad)
    )
    grad_far = swap(grad_far)
    by_stream = lambda rows: rows.reshape(group, seg, width)
    middle_grad, branch_grad, head_grad, sums_two = [], [], [], 0.0
    for (low, high), batch in zip(spans, middle):
        one, two, three, four = enter(
            me, batch, by_stream(part_grad), by_stream(grad_far), cotangent, low, out_rows, gain_two
        )
        middle_grad.append(one)
        branch_grad.append(two.reshape(-1, width))
        three, part_grad = barrier((three, part_grad))
        head_grad.append(lax.all_to_all(three, "seq", 0, 0, tiled=True))
        sums_two = sums_two + four
    result = part + swap(part_far).astype(F32) + down_shift
    output = (jnp.concatenate(middle).reshape(own, width) + result).astype(BF16)
    output = output.reshape(group, seg, width)

    out_shift_grad, gain_two_grad, shift_two_grad, down_shift_grad = (
        sums_two[i].reshape(parts, cols) for i in range(4)
    )
    none = jnp.zeros((parts, 2 * cols), F32)
    unit_sums = jnp.stack(
        [unit_one.reshape(parts, unit_cols), unit_two.reshape(parts, unit_cols)], axis=1
    ).reshape(parts, 2 * unit_cols)
    small = jnp.stack(
        [
            jnp.concatenate([none, out_shift_grad, gain_two_grad], axis=1),
            jnp.concatenate([shift_two_grad, down_shift_grad, none], axis=1),
            jnp.concatenate(
                [jnp.where(core == 0, unit_sums, 0.0), jnp.where(core == 1, unit_sums, 0.0)], axis=1
            ),
        ],
        axis=1,
    )
    small = jnp.pad(small, ((0, 0), (0, 13), (0, 0)))
    weights, inverse, mixed_heads, content_q, position_q, keys, values = kept[0]
    out_grad = mm(jnp.concatenate(attended), jnp.concatenate(branch_grad), TN)
    out_grad = out_grad.astype(BF16).reshape(parts, cols, width)
    late_one, small, out_grad, late_two, head_grad = barrier(
        (late_one, small, out_grad, late_two, head_grad[0])
    )
    late_two = lax.psum_scatter(
        late_two.reshape(-1, width), "seq", scatter_dimension=0, tiled=True
    )
    late_one = exchange(late_one.reshape(layers, -1, width), "z")
    query_grad, *key_grads, table_grad, sums = pull(
        weights, inverse, mixed_heads, head_grad, content_q, position_q, keys, values, proj_rev, cuts
    )
    late_one, late_two, out_grad, query_grad = barrier((late_one, late_two, out_grad, query_grad))
    ff = lax.psum(late_two, "z")
    late_one = add_up(late_one)
    out_sent = exchange(out_grad, "seq")
    seg_part, square_grads = settle(
        me, normed, (query_grad, *key_grads), columns, table_rev, table_grad, sums, gain_one,
        shift_one, small, parts,
    )
    summed = lax.all_to_all(square_grads, "seq", 0, 0, tiled=True)
    ff, late_one, square_grads = barrier((ff, late_one, square_grads))
    late_one = collect(late_one, "z")
    summed, seg_part = barrier((summed, seg_part))
    summed = jnp.concatenate([summed.reshape(-1, wide), add_up(out_sent).reshape(-1, wide)], axis=0)
    ff, summed, packed = barrier((ff, summed, packed))
    summed = lax.psum(summed, ("z", "core"))
    packed = jnp.stack(exchange(packed, "seq"))
    new_compressed = jnp.concatenate(
        [lax.dynamic_index_in_dim(packed, p ^ me, 0, keepdims=False) for p in range(parts)], axis=2
    )
    squares = parts * (cols + 16)
    out_w = summed[squares:].reshape(cols, width).astype(F32)
    summed = summed[:squares].reshape(parts, cols + 16, wide)
    seg_grad = lax.all_to_all(seg_part, "seq", 0, 0, tiled=True).astype(F32)
    seg_grad = jnp.sum(seg_grad, axis=0).reshape(own, width)
    unit_seg, rate_seg = standardise(segment.reshape(own, width).astype(F32))
    rows_grad = standardise_back(unit_seg, rate_seg, seg_grad, gain_one)
    segment_grad = jnp.concatenate(middle_grad, axis=0) + by_stream(rows_grad)

    halves = lambda *rows: [each.reshape(2, unit_cols, width) for each in rows]
    up_w, down_w = lay_out(core, halves(late_one, ff), halves(swap(late_one), swap(ff)), parts)
    down_w = down_w.reshape(4 * unit_cols, width)
    query_w, key_w, value_w, rel_w = lay_squares(summed, cols)
    small = jnp.sum(summed[:, cols : cols + 3].astype(F32), axis=0)
    piece = lambda row, i: small[row, cols * i : cols * (i + 1)]
    return (
        output,
        segment_grad,
        piece(0, 0),
        piece(0, 1),
        query_w,
        key_w,
        value_w,
        out_w,
        piece(0, 2),
        rel_w,
        piece(1, 2),
        piece(1, 3),
        piece(0, 3),
        piece(1, 0),
        up_w,
        small[2],
        down_w,
        piece(1, 1),
        new_compressed,
    )


def solution(mesh):
    dp = mesh.shape["dp"]
    cores = jax.sharding.Mesh(
        mesh.devices.reshape(dp // 2, 2, mesh.shape["seq"]), ("z", "core", "seq")
    )
    rows = P(("z", "core"), "seq", None)
    shard, matrix = P("seq"), P("seq", None)
    return jax.shard_map(
        body,
        mesh=cores,
        in_specs=(
            rows, rows, rows, P(("z", "core"), None), P(("z", "core")), shard, shard, matrix,
            matrix, matrix, matrix, shard, matrix, shard, shard, shard, shard, matrix, shard,
            matrix, shard, P(None, "seq", None), shard, rows,
        ),
        out_specs=(
            rows, rows, shard, shard, matrix, matrix, matrix, matrix, shard, matrix, shard,
            shard, shard, shard, matrix, shard, matrix, shard, rows,
        ),
        check_vma=False,
    )
```

```python
import functools
import math

import jax
import jax.numpy as jnp
from jax import lax
from jax.experimental import pallas as pl
from jax.experimental.pallas import tpu as pltpu
from jax.sharding import PartitionSpec as P

HEADS = 8
DH = 128
EPSILON = 1e-05
MASKED = -1e30
LANES = 128
BLOCK = 256
CHUNK = 16
VMEM_LIMIT = 60 * 2**20
SCALE = 1.0 / math.sqrt(DH)
LOG2E = 1.4426950408889634
BF16 = jnp.bfloat16
F32 = jnp.float32


def cost(microseconds):
    return pl.CostEstimate(flops=int(microseconds * 1.15e7), bytes_accessed=0, transcendentals=0)


def mm(left, right, dims):
    return lax.dot_general(left, right, (dims, ((), ())), preferred_element_type=F32)


NN = ((1,), (0,))
NT = ((1,), (1,))
TN = ((0,), (0,))


def lean_left(block, first_row, fill_columns):
    columns = block.shape[1] // LANES
    far = BLOCK - 1 - first_row
    whole, part = far // LANES, far % LANES
    turned = [
        pltpu.roll(
            block[:, LANES * t : LANES * (t + 1)], LANES - part, 1, stride=1, stride_axis=0
        )
        for t in range(columns)
    ]
    rows = lax.broadcasted_iota(jnp.int32, (block.shape[0], LANES), 0)
    lanes = lax.broadcasted_iota(jnp.int32, (block.shape[0], LANES), 1)
    near = lanes - rows < LANES - part
    out = []
    for t in range(fill_columns):
        a = turned[(t + whole) % columns]
        b = turned[(t + whole + 1) % columns]
        out.append(jnp.where(near, a, b))
    return jnp.concatenate(out, axis=1)


def lean_right(block, first_row):
    columns = block.shape[1] // LANES
    whole, part = first_row // LANES, first_row % LANES
    turned = [
        pltpu.roll(block[:, LANES * t : LANES * (t + 1)], part, 1, stride=1, stride_axis=0)
        for t in range(columns)
    ]
    rows = lax.broadcasted_iota(jnp.int32, (block.shape[0], LANES), 0)
    lanes = lax.broadcasted_iota(jnp.int32, (block.shape[0], LANES), 1)
    wrapped = lanes - rows < part
    out = []
    for t in range(columns):
        a = turned[(t - whole) % columns]
        b = turned[(t - whole - 1) % columns]
        out.append(jnp.where(wrapped, b, a))
    return jnp.concatenate(out, axis=1)


def flip_matrix(kind):
    rows = lax.broadcasted_iota(jnp.int32, (BLOCK, BLOCK), 0)
    lanes = lax.broadcasted_iota(jnp.int32, (BLOCK, BLOCK), 1)
    return (rows + lanes == BLOCK - 1).astype(F32).astype(kind)


def in_place_order(parts_ref, out_ref, cuts):
    parts = parts_ref.shape[0]
    low, base = 0, 0
    for size in cuts:
        for part in range(parts):
            out_ref[base + part * size : base + (part + 1) * size, :] = parts_ref[
                part, low : low + size, :
            ]
        low += size
        base += parts * size


def attend_kernel(
    cuts, q_ref, cb_ref, pb_ref, k_ref, v_ref, t_ref, info_ref,
    e_ref, inv_ref, o_ref, cq_ref, pq_ref,
    keys, values, raw, lean, mix, tops, sums,
):
    parts, seg, _ = q_ref.shape
    queries = parts * seg
    old = parts * (cuts[0] + cuts[1])
    in_place_order(k_ref, keys, cuts)
    in_place_order(v_ref, values, cuts)
    q = q_ref[...].reshape(queries, DH)
    content_q = (q + cb_ref[...]).astype(BF16)
    position_q = (q + pb_ref[...]).astype(BF16)
    cq_ref[...] = content_q.reshape(parts, seg, DH)
    pq_ref[...] = position_q.reshape(parts, seg, DH)
    for block in range(queries // BLOCK):
        row0 = block * BLOCK
        width = old + row0 + BLOCK
        skip = queries - BLOCK - row0
        raw[:, :width] = mm(content_q[row0 : row0 + BLOCK], keys[:width, :], NT)
        lean[:, :width] = mm(position_q[row0 : row0 + BLOCK], t_ref[skip : skip + width, :], NT)
        for chunk in range(BLOCK // CHUNK):
            r0 = chunk * CHUNK
            rows = slice(r0, r0 + CHUNK)
            turned = lean_left(lean[rows, :width], r0, width // LANES)
            score = raw[rows, :width] + turned
            start = info_ref[row0 + r0 : row0 + r0 + CHUNK, 0:1].astype(jnp.int32)
            shade = info_ref[row0 + r0 : row0 + r0 + CHUNK, 1:2]
            past = score[:, :old] + shade
            place = lax.broadcasted_iota(jnp.int32, (CHUNK, row0 + BLOCK), 1)
            own = lax.broadcasted_iota(jnp.int32, (CHUNK, row0 + BLOCK), 0) + (row0 + r0)
            now = jnp.where((place <= own) & (place >= start), score[:, old:], MASKED)
            raw[rows, :old] = past
            raw[rows, old:width] = now
            top = past[:, :LANES]
            for low in range(LANES, old, LANES):
                top = jnp.maximum(top, past[:, low : low + LANES])
            for low in range(0, row0 + BLOCK, LANES):
                top = jnp.maximum(top, now[:, low : low + LANES])
            tops[rows, :] = top
        top = jnp.max(tops[...], axis=1, keepdims=True)
        tops[...] = jnp.broadcast_to(top, (BLOCK, LANES))
        for chunk in range(BLOCK // CHUNK):
            r0 = chunk * CHUNK
            rows = slice(r0, r0 + CHUNK)
            top = tops[rows, :]
            total = jnp.zeros((CHUNK, LANES), F32)
            for low in range(0, width, LANES):
                weight = jnp.exp2((raw[rows, low : low + LANES] - top) * (SCALE * LOG2E))
                total = total + weight
                e_ref[row0 + r0 : row0 + r0 + CHUNK, low : low + LANES] = weight.astype(BF16)
            sums[rows, :] = total
        total = jnp.sum(sums[...], axis=1, keepdims=True)
        inv_ref[row0 : row0 + BLOCK, :] = jnp.broadcast_to(1.0 / total, (BLOCK, DH))
        mix[row0 : row0 + BLOCK, :] = mm(
            e_ref[row0 : row0 + BLOCK, :width], values[:width, :], NN
        )
    o_ref[...] = (mix[...] * inv_ref[...]).astype(BF16).reshape(parts, seg, DH)


def attend(query, content_shift, position_shift, keys, values, table_rev, info, cuts):
    parts, group, seg, cols = query.shape
    rows = keys.shape[2]
    queries, key_count, heads = parts * seg, parts * rows, cols // DH
    by_head = lambda size: pl.BlockSpec((parts, None, size, DH), lambda s, h: (0, s, 0, h))
    grid_spec = pl.GridSpec(
        grid=(group, heads),
        in_specs=[
            by_head(seg),
            pl.BlockSpec((1, DH), lambda s, h: (0, h)),
            pl.BlockSpec((1, DH), lambda s, h: (0, h)),
            by_head(rows),
            by_head(rows),
            pl.BlockSpec((key_count, DH), lambda s, h: (0, h)),
            pl.BlockSpec((None, queries, LANES), lambda s, h: (s, 0, 0)),
        ],
        out_specs=[
            pl.BlockSpec((None, None, queries, key_count), lambda s, h: (s, h, 0, 0)),
            pl.BlockSpec((None, None, queries, DH), lambda s, h: (s, h, 0, 0)),
            by_head(seg),
            by_head(seg),
            by_head(seg),
        ],
        scratch_shapes=[
            pltpu.VMEM((key_count, DH), BF16),
            pltpu.VMEM((key_count, DH), BF16),
            pltpu.VMEM((BLOCK, key_count), F32),
            pltpu.VMEM((BLOCK, key_count), F32),
            pltpu.VMEM((queries, DH), F32),
            pltpu.VMEM((BLOCK, LANES), F32),
            pltpu.VMEM((BLOCK, LANES), F32),
        ],
    )
    small = jax.ShapeDtypeStruct((parts, group, seg, cols), BF16)
    return pl.pallas_call(
        functools.partial(attend_kernel, cuts),
        grid_spec=grid_spec,
        out_shape=[
            jax.ShapeDtypeStruct((group, heads, queries, key_count), BF16),
            jax.ShapeDtypeStruct((group, heads, queries, DH), F32),
            small,
            small,
            small,
        ],
        compiler_params=pltpu.CompilerParams(
            dimension_semantics=("arbitrary", "arbitrary"), vmem_limit_bytes=VMEM_LIMIT
        ),
        cost_estimate=cost(40),
        name="attend",
    )(query, content_shift, position_shift, keys, values, table_rev, info)


def pull_kernel(
    cuts, e_ref, inv_ref, o_ref, g_ref, cq_ref, pq_ref, k_ref, v_ref, t_ref,
    dq_ref, dk_ref, dv_ref, ks_ref, vs_ref, dt_ref, sums_ref,
    keys, values, grad, prob, part, score, lean, key_sum, value_sum,
):
    stream = pl.program_id(1)
    parts, seg, _ = g_ref.shape
    queries = parts * seg
    old = parts * (cuts[0] + cuts[1])
    in_place_order(k_ref, keys, cuts)
    in_place_order(v_ref, values, cuts)
    out_grad = g_ref[...].reshape(queries, DH).astype(F32)
    attended = o_ref[...].reshape(queries, DH).astype(F32)
    inv = inv_ref[...]
    grad[...] = (out_grad * inv).astype(BF16)
    dots = jnp.sum(out_grad * attended, axis=1, keepdims=True) * inv
    content_q = cq_ref[...].reshape(queries, DH)
    position_q = pq_ref[...].reshape(queries, DH)

    @pl.when(stream == 0)
    def _():
        dt_ref[...] = jnp.zeros_like(dt_ref)
        sums_ref[...] = jnp.zeros_like(sums_ref)

    key_sum[...] = jnp.zeros_like(key_sum)
    value_sum[...] = jnp.zeros_like(value_sum)
    content_total = jnp.zeros((1, DH), F32)
    position_total = jnp.zeros((1, DH), F32)
    query_total = jnp.zeros((1, DH), F32)
    flip = flip_matrix(BF16)
    flip_wide = flip_matrix(F32)
    turn = lambda rows: mm(flip, rows, NN).astype(BF16)
    for block in range(queries // BLOCK):
        row0 = block * BLOCK
        width = old + row0 + BLOCK
        skip = queries - BLOCK - row0
        rows = slice(row0, row0 + BLOCK)
        dots_back = lax.dot_general(
            flip_wide,
            jnp.broadcast_to(dots[rows], (BLOCK, DH)),
            (NN, ((), ())),
            precision=lax.Precision.HIGHEST,
            preferred_element_type=F32,
        )
        content_back = turn(content_q[rows])
        position_back = turn(position_q[rows])
        prob[:, :width] = mm(turn(grad[rows, :]), values[:width, :], NT)
        part[:, :width] = mm(flip, e_ref[rows, :width], NN)
        value_sum[:, :width] += mm(grad[rows, :], e_ref[rows, :width], TN)
        for chunk in range(BLOCK // CHUNK):
            r0 = chunk * CHUNK
            mean = dots_back[r0 : r0 + CHUNK, 0:1]
            change = part[r0 : r0 + CHUNK, :width] * (prob[r0 : r0 + CHUNK, :width] - mean)
            score[r0 : r0 + CHUNK, :width] = change.astype(BF16)
            lean[r0 : r0 + CHUNK, :width] = lean_right(change, r0).astype(BF16)
        content_grad = (mm(score[:, :width], keys[:width, :], NN) * SCALE).astype(BF16).astype(F32)
        position_grad = (
            (mm(lean[:, :width], t_ref[skip : skip + width, :], NN) * SCALE)
            .astype(BF16)
            .astype(F32)
        )
        query_grad = turn((content_grad + position_grad).astype(BF16))
        content_total += jnp.sum(content_grad, axis=0, keepdims=True)
        position_total += jnp.sum(position_grad, axis=0, keepdims=True)
        query_total += jnp.sum(query_grad.astype(F32), axis=0, keepdims=True)
        dq_ref[rows, :] = query_grad
        key_sum[:, :width] += mm(content_back, score[:, :width], TN)
        dt_ref[:, skip : skip + width] += mm(position_back, lean[:, :width], TN) * SCALE
    key_cols = (key_sum[...] * SCALE).astype(BF16)
    value_cols = value_sum[...].astype(BF16)
    dk_ref[...] = key_cols
    dv_ref[...] = value_cols
    ks_ref[...] = (key_sum[:, old:] * SCALE).T.astype(BF16)
    vs_ref[...] = value_sum[:, old:].T.astype(BF16)
    ones = jnp.ones((8, key_cols.shape[1]), BF16)
    key_total = mm(ones, key_cols, NT)[0:1]
    value_total = mm(ones, value_cols, NT)[0:1]
    sums_ref[...] += jnp.concatenate(
        [
            content_total,
            position_total,
            query_total,
            key_total,
            value_total,
            jnp.zeros((3, DH), F32),
        ],
        axis=0,
    )


def pull(weights, inverse, attended, out_grad, content_q, position_q, keys, values, table_rev, cuts):
    parts, group, seg, cols = out_grad.shape
    rows = keys.shape[2]
    queries, key_count, heads = parts * seg, parts * rows, cols // DH
    by_head = lambda size: pl.BlockSpec((parts, None, size, DH), lambda h, s: (0, s, 0, h))
    by_row = lambda: pl.BlockSpec((None, queries, DH), lambda h, s: (s, 0, h))
    by_place = lambda: pl.BlockSpec((None, DH, key_count), lambda h, s: (s, h, 0))
    grid_spec = pl.GridSpec(
        grid=(heads, group),
        in_specs=[
            pl.BlockSpec((None, None, queries, key_count), lambda h, s: (s, h, 0, 0)),
            pl.BlockSpec((None, None, queries, DH), lambda h, s: (s, h, 0, 0)),
            by_head(seg),
            by_head(seg),
            by_head(seg),
            by_head(seg),
            by_head(rows),
            by_head(rows),
            pl.BlockSpec((key_count, DH), lambda h, s: (0, h)),
        ],
        out_specs=[
            by_row(),
            by_place(),
            by_place(),
            by_row(),
            by_row(),
            pl.BlockSpec((None, DH, key_count), lambda h, s: (h, 0, 0)),
            pl.BlockSpec((None, 8, DH), lambda h, s: (h, 0, 0)),
        ],
        scratch_shapes=[
            pltpu.VMEM((key_count, DH), BF16),
            pltpu.VMEM((key_count, DH), BF16),
            pltpu.VMEM((queries, DH), BF16),
            pltpu.VMEM((BLOCK, key_count), F32),
            pltpu.VMEM((BLOCK, key_count), F32),
            pltpu.VMEM((BLOCK, key_count), BF16),
            pltpu.VMEM((BLOCK, key_count), BF16),
            pltpu.VMEM((DH, key_count), F32),
            pltpu.VMEM((DH, key_count), F32),
        ],
    )
    return pl.pallas_call(
        functools.partial(pull_kernel, cuts),
        grid_spec=grid_spec,
        out_shape=[
            jax.ShapeDtypeStruct((group, queries, cols), BF16),
            jax.ShapeDtypeStruct((group, cols, key_count), BF16),
            jax.ShapeDtypeStruct((group, cols, key_count), BF16),
            jax.ShapeDtypeStruct((group, queries, cols), BF16),
            jax.ShapeDtypeStruct((group, queries, cols), BF16),
            jax.ShapeDtypeStruct((heads, DH, key_count), F32),
            jax.ShapeDtypeStruct((heads, 8, DH), F32),
        ],
        compiler_params=pltpu.CompilerParams(
            dimension_semantics=("arbitrary", "arbitrary"), vmem_limit_bytes=VMEM_LIMIT
        ),
        cost_estimate=cost(39),
        name="pull",
    )(weights, inverse, attended, out_grad, content_q, position_q, keys, values, table_rev)


def project_kernel(
    cuts, rows_ref, gain_ref, shift_ref, w_ref, old_ref, mem_ref, seg_ref, q_ref, k_ref, v_ref, normed
):
    rows, width = rows_ref.shape
    cols = k_ref.shape[1]
    step = 64 if rows % 64 == 0 else 32
    for low in range(0, rows, step):
        wide = rows_ref[low : low + step, :].astype(F32)
        centred = wide - jnp.mean(wide, axis=1, keepdims=True)
        rate = lax.rsqrt(jnp.mean(centred * centred, axis=1, keepdims=True) + EPSILON)
        normed[low : low + step, :] = (centred * rate * gain_ref[...] + shift_ref[...]).astype(BF16)
    cut = cuts[0] + cuts[1]
    old_ref[...] = normed[: cuts[0], :]
    mem_ref[...] = normed[cuts[0] : cut, :]
    seg_ref[...] = normed[cut:, :]
    q_ref[...] = mm(normed[cut:, :], w_ref[:, :cols], NN)
    k_ref[...] = mm(normed[...], w_ref[:, cols : 2 * cols], NN).astype(BF16)
    v_ref[...] = mm(normed[...], w_ref[:, 2 * cols : 3 * cols], NN).astype(BF16)


def project(rows_all, gain, shift, columns, cuts):
    parts, group, each, width = rows_all.shape
    cols = columns.shape[1] // 4
    block = lambda size, wide: pl.BlockSpec((None, None, size, wide), lambda p, s: (p, s, 0, 0))
    placed = lambda size: pl.BlockSpec((None, size, width), lambda p, s: (s, p, 0))
    whole = lambda *shape: pl.BlockSpec(shape, lambda p, s: (0,) * len(shape))
    shape = lambda size, kind: jax.ShapeDtypeStruct((parts, group, size, cols), kind)
    return pl.pallas_call(
        functools.partial(project_kernel, cuts),
        grid_spec=pl.GridSpec(
            grid=(parts, group),
            in_specs=[
                block(each, width),
                whole(1, width),
                whole(1, width),
                whole(width, 4 * cols),
            ],
            out_specs=[placed(size) for size in cuts]
            + [block(cuts[2], cols), block(each, cols), block(each, cols)],
            scratch_shapes=[pltpu.VMEM((each, width), BF16)],
        ),
        out_shape=[jax.ShapeDtypeStruct((group, parts * size, width), BF16) for size in cuts]
        + [shape(cuts[2], F32), shape(each, BF16), shape(each, BF16)],
        compiler_params=pltpu.CompilerParams(
            dimension_semantics=("arbitrary", "arbitrary"), vmem_limit_bytes=VMEM_LIMIT
        ),
        cost_estimate=cost(17),
        name="project",
    )(rows_all, gain, shift, columns)


def gelu_both(x):
    near = jnp.abs(x)
    t = 1.0 / (1.0 + (0.3275911 * math.sqrt(0.5)) * near)
    bell = jnp.exp2((x * x) * (-0.5 * LOG2E))
    tail = 0.5 * 1.061405429
    for factor in (-1.453152027, 1.421413741, -0.284496736, 0.254829592):
        tail = tail * t + 0.5 * factor
    tail = tail * t * bell
    below = jnp.where(x < 0.0, tail, 1.0 - tail)
    return x * below, below + x * bell * (1.0 / math.sqrt(2.0 * math.pi))


def forward_back_kernel(
    last, parts, pair, n_ref, c_ref, *rest,
):
    up_refs, down_refs, shift_ref = rest[:parts], rest[parts : parts + pair], rest[parts + pair]
    rest = rest[parts + pair + 1 :]
    if last:
        part_in, grad_in, part_out, part_far, grad_out, grad_far, late_ref, sums_ref = rest[:8]
        pre, slope, hidden, act, up_out, down_out, sems, part_ref, grad_ref = rest[8:]
    else:
        part_ref, grad_ref, late_ref, sums_ref = rest[:4]
        pre, slope, hidden, act, up_out, down_out, sems = rest[4:]
    tile = pl.program_id(0)
    tiles = pl.num_programs(0)
    cols, units = up_refs[0].shape
    unit_cols, width = down_refs[0].shape
    rows = n_ref.shape[0]
    slot = lax.rem(tile, 2)
    up_weight = jnp.concatenate([ref[...] for ref in up_refs], axis=0)
    down_weight = jnp.concatenate([ref[...] for ref in down_refs], axis=0)

    def copies(at, index):
        return (
            pltpu.make_async_copy(
                up_out.at[at],
                late_ref.at[:, pl.ds(0, cols), pl.ds(pl.multiple_of(index * units, units), units)],
                sems.at[at, 0],
            ),
            pltpu.make_async_copy(
                down_out.at[at],
                late_ref.at[pl.ds(index * pair, pair), pl.ds(cols, unit_cols), :],
                sems.at[at, 1],
            ),
        )

    @pl.when(tile == 0)
    def _():
        if last:
            part_ref[...] = part_in[...]
            grad_ref[...] = grad_in[...]
        else:
            part_ref[...] = jnp.zeros_like(part_ref)
            grad_ref[...] = jnp.zeros_like(grad_ref)

    pre[...] = mm(n_ref[...], up_weight, NN)
    slope[...] = mm(c_ref[...], down_weight, NT)
    step = 64
    for low in range(0, rows, step):
        value, change = gelu_both(pre[low : low + step, :] + shift_ref[...])
        hidden[low : low + step, :] = value.astype(BF16)
        act[low : low + step, :] = (change * slope[low : low + step, :]).astype(BF16)
    part_ref[...] += mm(hidden[...], down_weight, NN)
    grad_ref[...] += mm(act[...], up_weight, NT)
    sums_ref[...] = jnp.sum(act[...].astype(F32), axis=0, keepdims=True)

    @pl.when(tile >= 2)
    def _():
        for copy in copies(slot, tile - 2):
            copy.wait()

    up_out[slot] = mm(n_ref[...], act[...], TN).astype(BF16).reshape(parts, cols, units)
    down_out[slot] = mm(hidden[...], c_ref[...], TN).astype(BF16).reshape(pair, unit_cols, width)
    for copy in copies(slot, tile):
        copy.start()

    @pl.when(tile == tiles - 1)
    def _():
        if last:
            part_out[...] = part_ref[: rows // 2, :]
            part_far[...] = part_ref[rows // 2 :, :].astype(BF16)
            grad_out[...] = grad_ref[: rows // 2, :]
            grad_far[...] = grad_ref[rows // 2 :, :].astype(BF16)
        for copy in (copies(1 - slot, tile - 1) if parts > pair else ()) + copies(slot, tile):
            copy.wait()


def forward_back(normed, cot, gathered, shift, carry):
    parts, _, width = gathered.shape
    rows = normed.shape[0]
    cols = width // parts
    unit_cols = shift.shape[1] // parts
    pair = 2
    units = pair * unit_cols
    last = len(carry) > 0
    one = pl.Buffered(1)
    whole = lambda *shape: pl.BlockSpec(shape, lambda t: (0,) * len(shape), pipeline_mode=one)
    up = lambda p: pl.BlockSpec((None, cols, units), lambda t: (p, 0, t))
    down = lambda i: pl.BlockSpec(
        (None, unit_cols, width), lambda t: (t * pair + i, cols // unit_cols, 0)
    )
    if last:
        sums = [((rows // 2, width), F32), ((rows // 2, width), BF16)] * 2
    else:
        sums = [((rows, width), F32)] * 2
    return pl.pallas_call(
        functools.partial(forward_back_kernel, last, parts, pair),
        grid_spec=pl.GridSpec(
            grid=(parts // pair,),
            in_specs=[
                whole(rows, width),
                whole(rows, width),
            ]
            + [up(p) for p in range(parts)]
            + [down(i) for i in range(pair)]
            + [pl.BlockSpec((1, units), lambda t: (0, t))]
            + [whole(rows, width) for _ in carry],
            out_specs=[whole(*shape) for shape, _ in sums]
            + [
                pl.BlockSpec(memory_space=pl.ANY),
                pl.BlockSpec((1, units), lambda t: (0, t)),
            ],
            scratch_shapes=[
                pltpu.VMEM((rows, units), F32),
                pltpu.VMEM((rows, units), F32),
                pltpu.VMEM((rows, units), BF16),
                pltpu.VMEM((rows, units), BF16),
                pltpu.VMEM((2, parts, cols, units), BF16),
                pltpu.VMEM((2, pair, unit_cols, width), BF16),
                pltpu.SemaphoreType.DMA((2, 2)),
            ]
            + [pltpu.VMEM((rows, width), F32) for _ in carry],
        ),
        out_shape=[jax.ShapeDtypeStruct(shape, kind) for shape, kind in sums]
        + [
            jax.ShapeDtypeStruct((parts, cols + unit_cols, width), BF16),
            jax.ShapeDtypeStruct((1, parts * unit_cols), F32),
        ],
        compiler_params=pltpu.CompilerParams(
            dimension_semantics=("arbitrary",), vmem_limit_bytes=VMEM_LIMIT
        ),
        cost_estimate=cost(29),
        name="forward_back",
    )(normed, cot, *[gathered] * (parts + pair), shift, *carry)


def leave_kernel(a_ref, s_ref, w_ref, shift_ref, gain_ref, bias_ref, flat_ref, m_ref, n_ref):
    parts = a_ref.shape[0]
    flat_ref[...] = jnp.concatenate([a_ref[part] for part in range(parts)], axis=1)
    m_ref[...] = s_ref[...].astype(F32) + (mm(flat_ref[...], w_ref[...], NN) + shift_ref[...])
    step = 32
    for low in range(0, m_ref.shape[0], step):
        unit, _ = standardise(m_ref[low : low + step, :])
        n_ref[low : low + step, :] = (unit * gain_ref[...] + bias_ref[...]).astype(BF16)


def leave(mixed_heads, segment, base, weight, shift, gain, bias):
    parts, group, seg, cols = mixed_heads.shape
    width = parts * cols
    rows = lambda: pl.BlockSpec((None, seg, width), lambda s: (s, 0, 0))
    vector = lambda: pl.BlockSpec((1, width), lambda s: (0, 0))
    shape = lambda kind: jax.ShapeDtypeStruct((group, seg, width), kind)
    return pl.pallas_call(
        leave_kernel,
        grid_spec=pl.GridSpec(
            grid=(group,),
            in_specs=[
                pl.BlockSpec((parts, None, seg, cols), lambda s: (0, s, 0, 0)),
                pl.BlockSpec((None, seg, width), lambda s: (s + base, 0, 0)),
                pl.BlockSpec((width, width), lambda s: (0, 0)),
                vector(),
                vector(),
                vector(),
            ],
            out_specs=[rows(), rows(), rows()],
        ),
        out_shape=[shape(BF16), shape(F32), shape(BF16)],
        compiler_params=pltpu.CompilerParams(vmem_limit_bytes=VMEM_LIMIT),
        cost_estimate=cost(6),
        name="leave",
    )(mixed_heads, segment, weight, shift, gain, bias)


def enter_kernel(
    m_ref, g_ref, far_ref, c_ref, w_ref, gain_ref, mg_ref, b_ref, a_ref, sums_ref
):
    @pl.when(pl.program_id(0) == 0)
    def _():
        sums_ref[...] = jnp.zeros_like(sums_ref)

    parts = a_ref.shape[0]
    rows, width = m_ref.shape
    step = 32
    total = [jnp.zeros((1, width), F32) for _ in range(4)]
    for low in range(0, rows, step):
        at = slice(low, low + step)
        unit, rate = standardise(m_ref[at, :])
        grad = g_ref[at, :] + far_ref[at, :].astype(F32)
        cot = c_ref[at, :].astype(F32)
        middle_grad = cot + standardise_back(unit, rate, grad, gain_ref[...])
        branch = middle_grad.astype(BF16)
        mg_ref[at, :] = middle_grad
        b_ref[at, :] = branch
        for i, value in enumerate((branch.astype(F32), grad * unit, grad, cot)):
            total[i] = total[i] + jnp.sum(value, axis=0, keepdims=True)
    sums_ref[...] += jnp.concatenate(total + [jnp.zeros((4, width), F32)], axis=0)
    for part in range(parts):
        low = part * a_ref.shape[2]
        weight = w_ref[low : low + a_ref.shape[2], :]
        a_ref[part] = mm(b_ref[...], weight, NT).astype(BF16)


def enter(middle, grad, far, cot, base, weight, gain, parts):
    group, seg, width = middle.shape
    cols = width // parts
    rows = lambda: pl.BlockSpec((None, seg, width), lambda s: (s, 0, 0))
    later = lambda: pl.BlockSpec((None, seg, width), lambda s: (s + base, 0, 0))
    shape = lambda kind: jax.ShapeDtypeStruct((group, seg, width), kind)
    return pl.pallas_call(
        enter_kernel,
        grid_spec=pl.GridSpec(
            grid=(group,),
            in_specs=[
                rows(),
                later(),
                later(),
                later(),
                pl.BlockSpec((width, width), lambda s: (0, 0)),
                pl.BlockSpec((1, width), lambda s: (0, 0)),
            ],
            out_specs=[
                rows(),
                rows(),
                pl.BlockSpec((parts, None, seg, cols), lambda s: (0, s, 0, 0)),
                pl.BlockSpec((8, width), lambda s: (0, 0)),
            ],
        ),
        out_shape=[
            shape(F32),
            shape(BF16),
            jax.ShapeDtypeStruct((parts, group, seg, cols), BF16),
            jax.ShapeDtypeStruct((8, width), F32),
        ],
        compiler_params=pltpu.CompilerParams(
            dimension_semantics=("arbitrary",), vmem_limit_bytes=VMEM_LIMIT
        ),
        cost_estimate=cost(7),
        name="enter",
    )(middle, grad, far, cot, weight, gain)


def compress_kernel(low, rows_ref, w_ref, shift_ref, out_ref, wide):
    count = out_ref.shape[0]
    cols = out_ref.shape[1]
    blocks = wide.shape[0]
    for at in range(blocks):
        wide[at] = rows_ref[low : low + 3 * count, at * LANES : (at + 1) * LANES].astype(F32)
    total = jnp.broadcast_to(shift_ref[...], (count, cols))
    for k in range(3):
        every = jnp.concatenate(
            [wide[at, pl.ds(k, count, stride=3), :] for at in range(blocks)], axis=1
        ).astype(BF16)
        total = total + mm(every, w_ref[:, k * cols : (k + 1) * cols], NN)
    out_ref[...] = total.astype(BF16)


def compress(rows_all, columns, shift, low, count):
    parts, group, each, width = rows_all.shape
    cols = columns.shape[1] // 3
    return pl.pallas_call(
        functools.partial(compress_kernel, low),
        grid_spec=pl.GridSpec(
            grid=(parts, group),
            in_specs=[
                pl.BlockSpec((None, None, each, width), lambda p, s: (p, s, 0, 0)),
                pl.BlockSpec((width, 3 * cols), lambda p, s: (0, 0)),
                pl.BlockSpec((1, cols), lambda p, s: (0, 0)),
            ],
            out_specs=pl.BlockSpec((None, None, count, cols), lambda p, s: (p, s, 0, 0)),
            scratch_shapes=[pltpu.VMEM((width // LANES, 3 * count, LANES), F32)],
        ),
        out_shape=jax.ShapeDtypeStruct((parts, group, count, cols), BF16),
        compiler_params=pltpu.CompilerParams(
            dimension_semantics=("arbitrary", "arbitrary"), vmem_limit_bytes=VMEM_LIMIT
        ),
        cost_estimate=cost(6.5),
        name="compress",
    )(rows_all, columns, shift)


def lay_out_kernel(
    parts, unit_cols, core_ref, a_ref, b_ref, c_ref, d_ref, up_ref, down_ref
):
    flipped = core_ref[0] == 1
    for half, (mine_ref, far_ref) in enumerate(((a_ref, c_ref), (b_ref, d_ref))):
        mine, far = mine_ref[...].astype(F32), far_ref[...].astype(F32)
        for core, value in enumerate(
            (jnp.where(flipped, far, mine), jnp.where(flipped, mine, far))
        ):
            for part in range(parts):
                at = ((part * 2 + core) * 2 + half) * unit_cols
                up_ref[:, at : at + unit_cols] = value[
                    0, :, part * unit_cols : (part + 1) * unit_cols
                ]
            down_ref[2 * core + half] = value[1]


def lay_out(core, mine, far, parts):
    _, rows, width = mine[0].shape
    step = rows // 4 if rows % 64 == 0 else rows
    half = lambda: pl.BlockSpec((2, step, width), lambda r, *_: (0, r, 0))
    return pl.pallas_call(
        functools.partial(lay_out_kernel, parts, rows),
        grid_spec=pltpu.PrefetchScalarGridSpec(
            num_scalar_prefetch=1,
            grid=(rows // step,),
            in_specs=[half(), half(), half(), half()],
            out_specs=[
                pl.BlockSpec((step, 4 * width), lambda r, *_: (r, 0)),
                pl.BlockSpec((4, step, width), lambda r, *_: (0, r, 0)),
            ],
        ),
        out_shape=[
            jax.ShapeDtypeStruct((rows, 4 * width), F32),
            jax.ShapeDtypeStruct((4, rows, width), F32),
        ],
        compiler_params=pltpu.CompilerParams(vmem_limit_bytes=VMEM_LIMIT),
        cost_estimate=cost(4),
        name="lay_out",
    )(core.reshape(1), *mine, *far)


def lay_squares_kernel(in_ref, *out_refs):
    parts = in_ref.shape[0]
    cols = in_ref.shape[2] // len(out_refs)
    for at, out_ref in enumerate(out_refs):
        for part in range(parts):
            out_ref[:, part * cols : (part + 1) * cols] = in_ref[
                part, :, at * cols : (at + 1) * cols
            ].astype(F32)


def lay_squares(summed, rows):
    parts, _, wide = summed.shape
    width = parts * wide // 4
    step = rows // 2
    return pl.pallas_call(
        lay_squares_kernel,
        grid_spec=pl.GridSpec(
            grid=(2,),
            in_specs=[pl.BlockSpec((parts, step, wide), lambda i: (0, i, 0))],
            out_specs=[pl.BlockSpec((step, width), lambda i: (i, 0)) for _ in range(4)],
        ),
        out_shape=[jax.ShapeDtypeStruct((rows, width), F32) for _ in range(4)],
        compiler_params=pltpu.CompilerParams(vmem_limit_bytes=VMEM_LIMIT),
        cost_estimate=cost(2.5),
        name="lay_squares",
    )(summed)


def settle_kernel(
    me_ref, old_ref, mem_ref, seg_ref, q_ref, k_ref, v_ref, ks_ref, vs_ref, w_ref, table_ref, dt_ref,
    sums_ref, gain_ref, shift_ref, small_ref, og_ref, part_ref, out_ref, total,
):
    stream = pl.program_id(0)
    parts, rows, wide = out_ref.shape
    cols = wide // 4
    width = parts * cols

    @pl.when(stream == 0)
    def _():
        total[...] = jnp.zeros_like(total)

    total[:cols, :] += mm(q_ref[...], seg_ref[...], TN)
    for at, grad in ((cols, k_ref), (2 * cols, v_ref)):
        low = 0
        for normed in (old_ref, mem_ref, seg_ref):
            high = low + normed.shape[0]
            total[at : at + cols, :] += mm(grad[:, low:high], normed[...], NN)
            low = high
    three = jnp.concatenate([q_ref[...], ks_ref[...], vs_ref[...]], axis=1)
    part = mm(three, w_ref[:, : 3 * cols], NT).astype(BF16)
    part_ref[...] = part.reshape(part_ref.shape)

    @pl.when(stream == pl.num_programs(0) - 1)
    def _():
        heads = dt_ref.shape[0]
        rel = jnp.concatenate(
            [mm(dt_ref[head].astype(BF16), table_ref[...], NN) for head in range(heads)], axis=0
        )
        line = lambda row: jnp.concatenate(
            [sums_ref[head, row : row + 1, :] for head in range(heads)], axis=1
        )
        row_sums = jnp.concatenate([line(2), line(3), line(4)], axis=1)
        weight = w_ref[:, : 3 * cols].astype(F32)
        shift_grad = lax.dot_general(
            jnp.broadcast_to(row_sums, (8, 3 * cols)),
            weight,
            (NT, ((), ())),
            precision=lax.Precision.HIGHEST,
            preferred_element_type=F32,
        )[0:1]
        along = jnp.sum(weight.T * total[...], axis=0, keepdims=True)
        gain_grad = (along - shift_ref[...] * shift_grad) / gain_ref[...]
        for at in range(parts):
            low, high = at * cols, (at + 1) * cols
            out_ref[at, :cols, : 3 * cols] = total[:, low:high].T.astype(BF16)
            out_ref[at, :cols, 3 * cols :] = rel[:, low:high].T.astype(BF16)
            mine = (me_ref[0] == at).astype(F32)
            none = jnp.zeros((1, 2 * cols), F32)
            first = jnp.concatenate([gain_grad[:, low:high], shift_grad[:, low:high], none], axis=1)
            second = jnp.concatenate([none, mine * line(0), mine * line(1)], axis=1)
            added = jnp.concatenate([first, second, jnp.zeros((14, wide), F32)], axis=0)
            out_ref[at, cols : cols + 16, :] = (small_ref[at] + added).astype(BF16)
            for i in range(width // wide):
                base = cols + 16 + i * cols
                out_ref[at, base : base + cols, :] = og_ref[at, :, i * wide : (i + 1) * wide]


def settle(me, normed, grads, columns, table, table_grad, sums, gain, shift, small, out_grad, parts):
    group, queries, width = normed[2].shape
    cols = width // parts
    wide = 4 * cols
    height = cols + 16 + cols * width // wide
    block = lambda array: pl.BlockSpec((None, *array.shape[1:]), lambda s, *_: (s, 0, 0))
    whole = lambda *shape: pl.BlockSpec(
        shape, lambda s, *_: (0,) * len(shape), pipeline_mode=pl.Buffered(1)
    )
    return pl.pallas_call(
        settle_kernel,
        grid_spec=pltpu.PrefetchScalarGridSpec(
            num_scalar_prefetch=1,
            grid=(group,),
            in_specs=[block(rows) for rows in normed]
            + [block(grad) for grad in grads]
            + [
                whole(*columns.shape),
                whole(*table.shape),
                whole(*table_grad.shape),
                whole(*sums.shape),
                whole(1, width),
                whole(1, width),
                whole(*small.shape),
                whole(*out_grad.shape),
            ],
            out_specs=[
                pl.BlockSpec((parts, None, queries // parts, width), lambda s, *_: (0, s, 0, 0)),
                whole(parts, height, wide),
            ],
            scratch_shapes=[pltpu.VMEM((3 * cols, width), F32)],
        ),
        out_shape=[
            jax.ShapeDtypeStruct((parts, group, queries // parts, width), BF16),
            jax.ShapeDtypeStruct((parts, height, wide), BF16),
        ],
        compiler_params=pltpu.CompilerParams(
            dimension_semantics=("arbitrary",), vmem_limit_bytes=VMEM_LIMIT
        ),
        cost_estimate=cost(14),
        name="settle",
    )(me.reshape(1), *normed, *grads, columns, table, table_grad, sums, gain, shift, small, out_grad)


def standardise(rows):
    mean = jnp.mean(rows, axis=-1, keepdims=True)
    centred = rows - mean
    rate = lax.rsqrt(jnp.mean(centred * centred, axis=-1, keepdims=True) + EPSILON)
    return centred * rate, rate


def standardise_back(unit, rate, grad, gain):
    scaled = grad * gain
    mean = jnp.mean(scaled, axis=-1, keepdims=True)
    along = jnp.mean(scaled * unit, axis=-1, keepdims=True)
    return rate * (scaled - mean - unit * along)


def sinusoid_reversed(rows, width):
    positions = (rows - 1 - jnp.arange(rows, dtype=jnp.int32)).astype(F32)[:, None]
    frequency = jnp.exp(
        jnp.arange(width // 2, dtype=F32) * (-2.0 * math.log(10000.0) / width)
    )
    angles = positions * frequency[None, :]
    return jnp.concatenate([jnp.sin(angles), jnp.cos(angles)], axis=1).astype(BF16)


def dot(left, right):
    return mm(left, right, NN)


def swap(value):
    return lax.ppermute(value, "core", [(0, 1), (1, 0)])


def exchange(blocks, name, axis=0):
    count = lax.axis_size(name)
    me = lax.axis_index(name)
    block = lambda at: lax.dynamic_index_in_dim(blocks, at, axis, keepdims=False)
    return [block(me)] + [
        lax.ppermute(block(me ^ apart), name, [(i, i ^ apart) for i in range(count)])
        for apart in range(1, count)
    ]


def collect(block, name):
    count = lax.axis_size(name)
    me = lax.axis_index(name)
    found = jnp.stack(
        [block]
        + [
            lax.ppermute(block, name, [(i, i ^ apart) for i in range(count)])
            for apart in range(1, count)
        ]
    )
    return jnp.concatenate(
        [lax.dynamic_index_in_dim(found, me ^ i, 0, keepdims=False) for i in range(count)]
    )


def add_up(arrays, kind=BF16):
    total = arrays[0].astype(F32)
    for array in arrays[1:]:
        total = total + array.astype(F32)
    return total.astype(kind)


def body(
    segment, memory, compressed, eob, reset, ln1_gain, ln1_bias, w_query, w_key, w_value,
    w_out, out_bias, w_rel, bias_content, bias_position, ln2_gain, ln2_bias, w_up, up_bias,
    w_down, down_bias, conv_weight, conv_bias, cotangent,
):
    parts = lax.axis_size("seq")
    layers = lax.axis_size("z")
    core = lax.axis_index("core")
    me = lax.axis_index("seq")
    group, seg, width = segment.shape
    mem, old = memory.shape[1], compressed.shape[1]
    cuts = (old, mem, seg)
    each = old + mem + seg
    keys_in_all = parts * each
    cols = width // parts
    wide = 4 * cols
    own = group * seg
    unit_cols = w_up.shape[1] // (4 * parts)
    barrier = lax.optimization_barrier

    def by_columns(matrices):
        count = matrices.shape[0]
        sent = matrices.reshape(count, cols, parts, cols).transpose(2, 1, 0, 3)
        return sent.reshape(parts, cols, count * cols)

    up_bias_own = lax.dynamic_slice_in_dim(up_bias, core * 2 * unit_cols, 2 * unit_cols, 0)
    vectors = jnp.concatenate(
        [ln1_gain, ln1_bias, out_bias, ln2_gain, ln2_bias, down_bias, up_bias_own]
    )
    vectors = jnp.pad(vectors.reshape(2, wide), ((0, 14), (0, 0)))
    half = cols // 2
    sent = by_columns(jnp.concatenate([jnp.stack([w_query, w_key, w_value, w_rel]), conv_weight]))
    sent = lax.dynamic_slice_in_dim(sent, core * half, half, 1)
    out_half = lax.dynamic_slice_in_dim(w_out, core * half, half, 0)
    sent = jnp.concatenate([sent, jnp.broadcast_to(out_half, (parts, half, width))], axis=2)
    vectors = jnp.pad(vectors, ((0, 0), (0, 3 * cols + width)))
    sent = jnp.concatenate([sent, jnp.broadcast_to(vectors, (parts, *vectors.shape))], axis=1)
    got = lax.all_to_all(sent, "seq", 0, 0, tiled=True)
    spans = [(0, group)]
    local = [
        jnp.concatenate([compressed[low:high], memory[low:high], segment[low:high]], axis=1)
        for low, high in spans
    ]
    rows_all = [lax.all_gather(local[0], "seq")]
    mine = got[:, :half]
    far = swap(mine)
    columns = jnp.stack(
        [jnp.where(core == 0, mine, far), jnp.where(core == 0, far, mine)], axis=1
    ).reshape(width, 7 * cols + width)
    columns, conv_columns, out_full = (
        columns[:, :wide],
        columns[:, wide : 7 * cols],
        columns[:, 7 * cols :],
    )
    vectors = got[:, half : half + 2, :wide].reshape(parts, 2 * wide).astype(F32)
    gain_one, shift_one, out_shift, gain_two, shift_two, down_shift = (
        vectors[:, cols * i : cols * (i + 1)].reshape(1, width) for i in range(6)
    )
    up_shift = vectors[:, 6 * cols :].reshape(parts, 2, unit_cols).transpose(1, 0, 2)
    up_shift = up_shift.reshape(2, 1, parts * unit_cols)
    up_quarters = lax.dynamic_slice_in_dim(
        w_up.reshape(cols, parts, 2, 2, unit_cols), core, 1, 2
    ).reshape(cols, parts, 2, unit_cols)
    up_quarters = [up_quarters[:, :, i].reshape(cols, width) for i in range(2)]
    down_half = lax.dynamic_slice_in_dim(w_down, core * 2 * unit_cols, 2 * unit_cols, 0)
    down_quarters = [down_half[unit_cols * i : unit_cols * (i + 1)] for i in range(2)]
    first = jnp.concatenate([up_quarters[0], down_quarters[0]], axis=0)
    second = jnp.concatenate([up_quarters[1], down_quarters[1]], axis=0)
    cot_own = cotangent.reshape(own, width)
    cot_both = jnp.concatenate([cot_own, swap(cot_own)], axis=0)

    table_rev = sinusoid_reversed(keys_in_all, width)
    proj_rev = dot(table_rev, columns[:, 3 * cols :]).astype(BF16)
    index = jnp.arange(eob.shape[1], dtype=jnp.int32)[None, :]
    opens = jnp.pad(eob, ((0, 0), (1, 0)))[:, :-1] == 1
    start = lax.cummax(jnp.where(opens, index, 0), axis=1)
    shade = jnp.where((start == 0) & (reset[:, None] == 0), 0.0, MASKED)
    info = jnp.stack([start.astype(F32), shade], axis=2)
    info = jnp.pad(info, ((0, 0), (0, 0), (0, LANES - 2)))
    rows_all[0], proj_rev, info, cot_both, table_rev, columns, conv_columns, out_full, *local = barrier(
        (rows_all[0], proj_rev, info, cot_both, table_rev, columns, conv_columns, out_full, *local)
    )
    rows_all = [rows_all[0]] + [lax.all_gather(rows, "seq") for rows in local[1:]]

    kept, heads = [], []
    for batch, (low, high) in enumerate(spans):
        if batch == len(spans) - 1:
            rows_all[batch], first, *heads = barrier((rows_all[batch], first, *heads))
            first = lax.all_gather(first, "seq")
        *normed, query, keys, values = project(rows_all[batch], gain_one, shift_one, columns, cuts)
        second, query = barrier((second, query))
        second = lax.all_gather(second, "seq")
        weights, inverse, mixed_heads, content_q, position_q = attend(
            query,
            bias_content.astype(F32).reshape(1, cols),
            bias_position.astype(F32).reshape(1, cols),
            keys,
            values,
            proj_rev,
            info[low:high],
            cuts,
        )
        kept.append((weights, inverse, mixed_heads, content_q, position_q, keys, values))
        heads.append(lax.all_to_all(mixed_heads, "seq", 0, 0, tiled=True))

    mixed_heads, conv_columns = barrier((mixed_heads, conv_columns))
    packed = compress(
        rows_all[0], conv_columns, conv_bias.astype(F32).reshape(1, cols), old, mem // 3
    )
    packed, *heads = barrier((packed, *heads))

    attended, middle, normed_two = [], [], []
    for (low, high), batch in zip(spans, heads):
        one, two, three = leave(batch, segment, low, out_full, out_shift, gain_two, shift_two)
        attended.append(one.reshape(-1, width))
        middle.append(two)
        normed_two.append(three.reshape(-1, width))
    both = jnp.concatenate(normed_two + [swap(rows) for rows in normed_two], axis=0)
    part, part_grad, late_one, unit_one = forward_back(both, cot_both, first, up_shift[0], ())
    late_one = lax.psum_scatter(
        late_one.reshape(-1, width), "seq", scatter_dimension=0, tiled=True
    )
    part, part_far, part_grad, grad_far, late_two, unit_two = forward_back(
        both, cot_both, second, up_shift[1], (part, part_grad)
    )
    grad_far = swap(grad_far)
    by_stream = lambda rows: rows.reshape(group, seg, width)
    middle_grad, branch_grad, head_grad, sums_two = [], [], [], 0.0
    for (low, high), batch in zip(spans, middle):
        one, two, three, four = enter(
            batch, by_stream(part_grad), by_stream(grad_far), cotangent, low, out_full, gain_two, parts
        )
        middle_grad.append(one)
        branch_grad.append(two.reshape(-1, width))
        three, part_grad = barrier((three, part_grad))
        head_grad.append(lax.all_to_all(three, "seq", 0, 0, tiled=True))
        sums_two = sums_two + four
    result = part + swap(part_far).astype(F32) + down_shift
    output = (jnp.concatenate(middle).reshape(own, width) + result).astype(BF16)
    output = output.reshape(group, seg, width)

    out_shift_grad, gain_two_grad, shift_two_grad, down_shift_grad = (
        sums_two[i].reshape(parts, cols) for i in range(4)
    )
    none = jnp.zeros((parts, 2 * cols), F32)
    unit_sums = jnp.stack(
        [unit_one.reshape(parts, unit_cols), unit_two.reshape(parts, unit_cols)], axis=1
    ).reshape(parts, 2 * unit_cols)
    small = jnp.stack(
        [
            jnp.concatenate([none, out_shift_grad, gain_two_grad], axis=1),
            jnp.concatenate([shift_two_grad, down_shift_grad, none], axis=1),
            jnp.concatenate(
                [jnp.where(core == 0, unit_sums, 0.0), jnp.where(core == 1, unit_sums, 0.0)], axis=1
            ),
        ],
        axis=1,
    )
    small = jnp.pad(small, ((0, 0), (0, 13), (0, 0)))
    weights, inverse, mixed_heads, content_q, position_q, keys, values = kept[0]
    out_grad = mm(jnp.concatenate(attended), jnp.concatenate(branch_grad), TN)
    out_grad = out_grad.astype(BF16).reshape(parts, cols, width)
    late_one, small, out_grad, late_two, head_grad = barrier(
        (late_one, small, out_grad, late_two, head_grad[0])
    )
    late_two = lax.psum_scatter(
        late_two.reshape(-1, width), "seq", scatter_dimension=0, tiled=True
    )
    late_one = exchange(late_one.reshape(layers, -1, width), "z")
    query_grad, *key_grads, table_grad, sums = pull(
        weights, inverse, mixed_heads, head_grad, content_q, position_q, keys, values, proj_rev, cuts
    )
    late_one, late_two, query_grad = barrier((late_one, late_two, query_grad))
    ff = lax.psum(late_two, "z")
    late_one = add_up(late_one)
    seg_part, square_grads = settle(
        me, normed, (query_grad, *key_grads), columns, table_rev, table_grad, sums, gain_one,
        shift_one, small, out_grad, parts,
    )
    summed = lax.all_to_all(square_grads, "seq", 0, 0, tiled=True)
    ff, late_one, square_grads = barrier((ff, late_one, square_grads))
    late_one = collect(late_one, "z")
    summed, seg_part = barrier((summed, seg_part))
    squares = parts * (cols + 16)
    out_sum = jnp.sum(summed[:, cols + 16 :].astype(F32), axis=0).astype(BF16)
    summed = jnp.concatenate([summed[:, : cols + 16].reshape(squares, wide), out_sum], axis=0)
    ff, summed, packed = barrier((ff, summed, packed))
    summed = lax.psum(summed, ("z", "core"))
    packed = jnp.stack(exchange(packed, "seq"))
    new_compressed = jnp.concatenate(
        [lax.dynamic_index_in_dim(packed, p ^ me, 0, keepdims=False) for p in range(parts)], axis=2
    )
    out_w = summed[squares:].reshape(width // wide, cols, wide).astype(F32)
    out_w = out_w.transpose(1, 0, 2).reshape(cols, width)
    summed = summed[:squares].reshape(parts, cols + 16, wide)
    seg_grad = lax.all_to_all(seg_part, "seq", 0, 0, tiled=True).astype(F32)
    seg_grad = jnp.sum(seg_grad, axis=0).reshape(own, width)
    unit_seg, rate_seg = standardise(segment.reshape(own, width).astype(F32))
    rows_grad = standardise_back(unit_seg, rate_seg, seg_grad, gain_one)
    segment_grad = jnp.concatenate(middle_grad, axis=0) + by_stream(rows_grad)

    halves = lambda *rows: [each.reshape(2, unit_cols, width) for each in rows]
    up_w, down_w = lay_out(core, halves(late_one, ff), halves(swap(late_one), swap(ff)), parts)
    down_w = down_w.reshape(4 * unit_cols, width)
    query_w, key_w, value_w, rel_w = lay_squares(summed, cols)
    small = jnp.sum(summed[:, cols : cols + 3].astype(F32), axis=0)
    piece = lambda row, i: small[row, cols * i : cols * (i + 1)]
    return (
        output,
        segment_grad,
        piece(0, 0),
        piece(0, 1),
        query_w,
        key_w,
        value_w,
        out_w,
        piece(0, 2),
        rel_w,
        piece(1, 2),
        piece(1, 3),
        piece(0, 3),
        piece(1, 0),
        up_w,
        small[2],
        down_w,
        piece(1, 1),
        new_compressed,
    )


def solution(mesh):
    dp = mesh.shape["dp"]
    cores = jax.sharding.Mesh(
        mesh.devices.reshape(dp // 2, 2, mesh.shape["seq"]), ("z", "core", "seq")
    )
    rows = P(("z", "core"), "seq", None)
    shard, matrix = P("seq"), P("seq", None)
    return jax.shard_map(
        body,
        mesh=cores,
        in_specs=(
            rows, rows, rows, P(("z", "core"), None), P(("z", "core")), shard, shard, matrix,
            matrix, matrix, matrix, shard, matrix, shard, shard, shard, shard, matrix, shard,
            matrix, shard, P(None, "seq", None), shard, rows,
        ),
        out_specs=(
            rows, rows, shard, shard, matrix, matrix, matrix, matrix, shard, matrix, shard,
            shard, shard, shard, matrix, shard, matrix, shard, rows,
        ),
        check_vma=False,
    )
```

```python
import functools
import math

import jax
import jax.numpy as jnp
from jax import lax
from jax.experimental import pallas as pl
from jax.experimental.pallas import tpu as pltpu
from jax.sharding import PartitionSpec as P

HEADS = 8
DH = 128
EPSILON = 1e-05
MASKED = -1e30
LANES = 128
BLOCK = 256
CHUNK = 16
VMEM_LIMIT = 60 * 2**20
SCALE = 1.0 / math.sqrt(DH)
LOG2E = 1.4426950408889634
BF16 = jnp.bfloat16
F32 = jnp.float32


def cost(microseconds):
    return pl.CostEstimate(flops=int(microseconds * 1.15e7), bytes_accessed=0, transcendentals=0)


def mm(left, right, dims):
    return lax.dot_general(left, right, (dims, ((), ())), preferred_element_type=F32)


NN = ((1,), (0,))
NT = ((1,), (1,))
TN = ((0,), (0,))


def lean_left(block, first_row, fill_columns):
    columns = block.shape[1] // LANES
    far = BLOCK - 1 - first_row
    whole, part = far // LANES, far % LANES
    turned = [
        pltpu.roll(
            block[:, LANES * t : LANES * (t + 1)], LANES - part, 1, stride=1, stride_axis=0
        )
        for t in range(columns)
    ]
    rows = lax.broadcasted_iota(jnp.int32, (block.shape[0], LANES), 0)
    lanes = lax.broadcasted_iota(jnp.int32, (block.shape[0], LANES), 1)
    near = lanes - rows < LANES - part
    out = []
    for t in range(fill_columns):
        a = turned[(t + whole) % columns]
        b = turned[(t + whole + 1) % columns]
        out.append(jnp.where(near, a, b))
    return jnp.concatenate(out, axis=1)


def lean_right(block, first_row):
    columns = block.shape[1] // LANES
    whole, part = first_row // LANES, first_row % LANES
    turned = [
        pltpu.roll(block[:, LANES * t : LANES * (t + 1)], part, 1, stride=1, stride_axis=0)
        for t in range(columns)
    ]
    rows = lax.broadcasted_iota(jnp.int32, (block.shape[0], LANES), 0)
    lanes = lax.broadcasted_iota(jnp.int32, (block.shape[0], LANES), 1)
    wrapped = lanes - rows < part
    out = []
    for t in range(columns):
        a = turned[(t - whole) % columns]
        b = turned[(t - whole - 1) % columns]
        out.append(jnp.where(wrapped, b, a))
    return jnp.concatenate(out, axis=1)


def flip_matrix(kind):
    rows = lax.broadcasted_iota(jnp.int32, (BLOCK, BLOCK), 0)
    lanes = lax.broadcasted_iota(jnp.int32, (BLOCK, BLOCK), 1)
    return (rows + lanes == BLOCK - 1).astype(F32).astype(kind)


def in_place_order(parts_ref, out_ref, cuts):
    parts = parts_ref.shape[0]
    low, base = 0, 0
    for size in cuts:
        for part in range(parts):
            out_ref[base + part * size : base + (part + 1) * size, :] = parts_ref[
                part, low : low + size, :
            ]
        low += size
        base += parts * size


def attend_kernel(
    cuts, q_ref, cb_ref, pb_ref, k_ref, v_ref, t_ref, info_ref,
    e_ref, inv_ref, o_ref, cq_ref, pq_ref,
    keys, values, raw, lean, mix, tops, sums,
):
    parts, seg, _ = q_ref.shape
    queries = parts * seg
    old = parts * (cuts[0] + cuts[1])
    in_place_order(k_ref, keys, cuts)
    in_place_order(v_ref, values, cuts)
    q = q_ref[...].reshape(queries, DH)
    content_q = (q + cb_ref[...]).astype(BF16)
    position_q = (q + pb_ref[...]).astype(BF16)
    cq_ref[...] = content_q.reshape(parts, seg, DH)
    pq_ref[...] = position_q.reshape(parts, seg, DH)
    for block in range(queries // BLOCK):
        row0 = block * BLOCK
        width = old + row0 + BLOCK
        skip = queries - BLOCK - row0
        raw[:, :width] = mm(content_q[row0 : row0 + BLOCK], keys[:width, :], NT)
        lean[:, :width] = mm(position_q[row0 : row0 + BLOCK], t_ref[skip : skip + width, :], NT)
        for chunk in range(BLOCK // CHUNK):
            r0 = chunk * CHUNK
            rows = slice(r0, r0 + CHUNK)
            turned = lean_left(lean[rows, :width], r0, width // LANES)
            score = raw[rows, :width] + turned
            start = info_ref[row0 + r0 : row0 + r0 + CHUNK, 0:1].astype(jnp.int32)
            shade = info_ref[row0 + r0 : row0 + r0 + CHUNK, 1:2]
            past = score[:, :old] + shade
            place = lax.broadcasted_iota(jnp.int32, (CHUNK, row0 + BLOCK), 1)
            own = lax.broadcasted_iota(jnp.int32, (CHUNK, row0 + BLOCK), 0) + (row0 + r0)
            now = jnp.where((place <= own) & (place >= start), score[:, old:], MASKED)
            raw[rows, :old] = past
            raw[rows, old:width] = now
            top = past[:, :LANES]
            for low in range(LANES, old, LANES):
                top = jnp.maximum(top, past[:, low : low + LANES])
            for low in range(0, row0 + BLOCK, LANES):
                top = jnp.maximum(top, now[:, low : low + LANES])
            tops[rows, :] = top
        top = jnp.max(tops[...], axis=1, keepdims=True)
        tops[...] = jnp.broadcast_to(top, (BLOCK, LANES))
        for chunk in range(BLOCK // CHUNK):
            r0 = chunk * CHUNK
            rows = slice(r0, r0 + CHUNK)
            top = tops[rows, :]
            total = jnp.zeros((CHUNK, LANES), F32)
            for low in range(0, width, LANES):
                weight = jnp.exp2((raw[rows, low : low + LANES] - top) * (SCALE * LOG2E))
                total = total + weight
                e_ref[row0 + r0 : row0 + r0 + CHUNK, low : low + LANES] = weight.astype(BF16)
            sums[rows, :] = total
        total = jnp.sum(sums[...], axis=1, keepdims=True)
        inv_ref[row0 : row0 + BLOCK, :] = jnp.broadcast_to(1.0 / total, (BLOCK, DH))
        mix[row0 : row0 + BLOCK, :] = mm(
            e_ref[row0 : row0 + BLOCK, :width], values[:width, :], NN
        )
    o_ref[...] = (mix[...] * inv_ref[...]).astype(BF16).reshape(parts, seg, DH)


def attend(query, content_shift, position_shift, keys, values, table_rev, info, cuts):
    parts, group, seg, cols = query.shape
    rows = keys.shape[2]
    queries, key_count, heads = parts * seg, parts * rows, cols // DH
    by_head = lambda size: pl.BlockSpec((parts, None, size, DH), lambda s, h: (0, s, 0, h))
    grid_spec = pl.GridSpec(
        grid=(group, heads),
        in_specs=[
            by_head(seg),
            pl.BlockSpec((1, DH), lambda s, h: (0, h)),
            pl.BlockSpec((1, DH), lambda s, h: (0, h)),
            by_head(rows),
            by_head(rows),
            pl.BlockSpec((key_count, DH), lambda s, h: (0, h)),
            pl.BlockSpec((None, queries, LANES), lambda s, h: (s, 0, 0)),
        ],
        out_specs=[
            pl.BlockSpec((None, None, queries, key_count), lambda s, h: (s, h, 0, 0)),
            pl.BlockSpec((None, None, queries, DH), lambda s, h: (s, h, 0, 0)),
            by_head(seg),
            by_head(seg),
            by_head(seg),
        ],
        scratch_shapes=[
            pltpu.VMEM((key_count, DH), BF16),
            pltpu.VMEM((key_count, DH), BF16),
            pltpu.VMEM((BLOCK, key_count), F32),
            pltpu.VMEM((BLOCK, key_count), F32),
            pltpu.VMEM((queries, DH), F32),
            pltpu.VMEM((BLOCK, LANES), F32),
            pltpu.VMEM((BLOCK, LANES), F32),
        ],
    )
    small = jax.ShapeDtypeStruct((parts, group, seg, cols), BF16)
    return pl.pallas_call(
        functools.partial(attend_kernel, cuts),
        grid_spec=grid_spec,
        out_shape=[
            jax.ShapeDtypeStruct((group, heads, queries, key_count), BF16),
            jax.ShapeDtypeStruct((group, heads, queries, DH), F32),
            small,
            small,
            small,
        ],
        compiler_params=pltpu.CompilerParams(
            dimension_semantics=("arbitrary", "arbitrary"), vmem_limit_bytes=VMEM_LIMIT
        ),
        cost_estimate=cost(40),
        name="attend",
    )(query, content_shift, position_shift, keys, values, table_rev, info)


def pull_kernel(
    cuts, e_ref, inv_ref, o_ref, g_ref, cq_ref, pq_ref, k_ref, v_ref, t_ref,
    dq_ref, dk_ref, dv_ref, ks_ref, vs_ref, dt_ref, sums_ref,
    keys, values, grad, prob, part, score, lean, key_sum, value_sum,
):
    stream = pl.program_id(1)
    parts, seg, _ = g_ref.shape
    queries = parts * seg
    old = parts * (cuts[0] + cuts[1])
    in_place_order(k_ref, keys, cuts)
    in_place_order(v_ref, values, cuts)
    grad[...] = (g_ref[...].reshape(queries, DH).astype(F32) * inv_ref[...]).astype(BF16)
    attended = o_ref[...].reshape(queries, DH)
    content_q = cq_ref[...].reshape(queries, DH)
    position_q = pq_ref[...].reshape(queries, DH)

    @pl.when(stream == 0)
    def _():
        dt_ref[...] = jnp.zeros_like(dt_ref)
        sums_ref[...] = jnp.zeros_like(sums_ref)

    key_sum[...] = jnp.zeros_like(key_sum)
    value_sum[...] = jnp.zeros_like(value_sum)
    content_total = jnp.zeros((1, DH), F32)
    position_total = jnp.zeros((1, DH), F32)
    query_total = jnp.zeros((1, DH), F32)
    flip = flip_matrix(BF16)
    turn = lambda rows: mm(flip, rows, NN).astype(BF16)
    for block in range(queries // BLOCK):
        row0 = block * BLOCK
        width = old + row0 + BLOCK
        skip = queries - BLOCK - row0
        rows = slice(row0, row0 + BLOCK)
        grad_back = turn(grad[rows, :])
        dots_back = jnp.sum(
            grad_back.astype(F32) * turn(attended[rows]).astype(F32), axis=1, keepdims=True
        )
        content_back = turn(content_q[rows])
        position_back = turn(position_q[rows])
        prob[:, :width] = mm(grad_back, values[:width, :], NT)
        both = mm(jnp.concatenate([flip, grad[rows, :].T], axis=0), e_ref[rows, :width], NN)
        part[:, :width] = both[:BLOCK]
        value_sum[:, :width] += both[BLOCK:]
        for chunk in range(BLOCK // CHUNK):
            r0 = chunk * CHUNK
            mean = dots_back[r0 : r0 + CHUNK, 0:1]
            change = part[r0 : r0 + CHUNK, :width] * (prob[r0 : r0 + CHUNK, :width] - mean)
            score[r0 : r0 + CHUNK, :width] = change.astype(BF16)
            lean[r0 : r0 + CHUNK, :width] = lean_right(change, r0).astype(BF16)
        content_grad = (mm(score[:, :width], keys[:width, :], NN) * SCALE).astype(BF16).astype(F32)
        position_grad = (
            (mm(lean[:, :width], t_ref[skip : skip + width, :], NN) * SCALE)
            .astype(BF16)
            .astype(F32)
        )
        query_grad = turn((content_grad + position_grad).astype(BF16))
        content_total += jnp.sum(content_grad, axis=0, keepdims=True)
        position_total += jnp.sum(position_grad, axis=0, keepdims=True)
        query_total += jnp.sum(query_grad.astype(F32), axis=0, keepdims=True)
        dq_ref[rows, :] = query_grad
        key_sum[:, :width] += mm(content_back, score[:, :width], TN)
        dt_ref[:, skip : skip + width] += mm(position_back, lean[:, :width], TN) * SCALE
    key_cols = (key_sum[...] * SCALE).astype(BF16)
    value_cols = value_sum[...].astype(BF16)
    dk_ref[...] = key_cols
    dv_ref[...] = value_cols
    ks_ref[...] = (key_sum[:, old:] * SCALE).T.astype(BF16)
    vs_ref[...] = value_sum[:, old:].T.astype(BF16)
    ones = jnp.ones((8, key_cols.shape[1]), BF16)
    key_total = mm(ones, key_cols, NT)[0:1]
    value_total = mm(ones, value_cols, NT)[0:1]
    sums_ref[...] += jnp.concatenate(
        [
            content_total,
            position_total,
            query_total,
            key_total,
            value_total,
            jnp.zeros((3, DH), F32),
        ],
        axis=0,
    )


def pull(weights, inverse, attended, out_grad, content_q, position_q, keys, values, table_rev, cuts):
    parts, group, seg, cols = out_grad.shape
    rows = keys.shape[2]
    queries, key_count, heads = parts * seg, parts * rows, cols // DH
    by_head = lambda size: pl.BlockSpec((parts, None, size, DH), lambda h, s: (0, s, 0, h))
    by_row = lambda: pl.BlockSpec((None, queries, DH), lambda h, s: (s, 0, h))
    by_place = lambda: pl.BlockSpec((None, DH, key_count), lambda h, s: (s, h, 0))
    grid_spec = pl.GridSpec(
        grid=(heads, group),
        in_specs=[
            pl.BlockSpec((None, None, queries, key_count), lambda h, s: (s, h, 0, 0)),
            pl.BlockSpec((None, None, queries, DH), lambda h, s: (s, h, 0, 0)),
            by_head(seg),
            by_head(seg),
            by_head(seg),
            by_head(seg),
            by_head(rows),
            by_head(rows),
            pl.BlockSpec((key_count, DH), lambda h, s: (0, h)),
        ],
        out_specs=[
            by_row(),
            by_place(),
            by_place(),
            by_row(),
            by_row(),
            pl.BlockSpec((None, DH, key_count), lambda h, s: (h, 0, 0)),
            pl.BlockSpec((None, 8, DH), lambda h, s: (h, 0, 0)),
        ],
        scratch_shapes=[
            pltpu.VMEM((key_count, DH), BF16),
            pltpu.VMEM((key_count, DH), BF16),
            pltpu.VMEM((queries, DH), BF16),
            pltpu.VMEM((BLOCK, key_count), F32),
            pltpu.VMEM((BLOCK, key_count), F32),
            pltpu.VMEM((BLOCK, key_count), BF16),
            pltpu.VMEM((BLOCK, key_count), BF16),
            pltpu.VMEM((DH, key_count), F32),
            pltpu.VMEM((DH, key_count), F32),
        ],
    )
    return pl.pallas_call(
        functools.partial(pull_kernel, cuts),
        grid_spec=grid_spec,
        out_shape=[
            jax.ShapeDtypeStruct((group, queries, cols), BF16),
            jax.ShapeDtypeStruct((group, cols, key_count), BF16),
            jax.ShapeDtypeStruct((group, cols, key_count), BF16),
            jax.ShapeDtypeStruct((group, queries, cols), BF16),
            jax.ShapeDtypeStruct((group, queries, cols), BF16),
            jax.ShapeDtypeStruct((heads, DH, key_count), F32),
            jax.ShapeDtypeStruct((heads, 8, DH), F32),
        ],
        compiler_params=pltpu.CompilerParams(
            dimension_semantics=("arbitrary", "arbitrary"), vmem_limit_bytes=VMEM_LIMIT
        ),
        cost_estimate=cost(39),
        name="pull",
    )(weights, inverse, attended, out_grad, content_q, position_q, keys, values, table_rev)


def project_kernel(
    cuts, rows_ref, gain_ref, shift_ref, w_ref, old_ref, mem_ref, seg_ref, q_ref, k_ref, v_ref, normed
):
    rows, width = rows_ref.shape
    cols = k_ref.shape[1]
    step = 64 if rows % 64 == 0 else 32
    for low in range(0, rows, step):
        wide = rows_ref[low : low + step, :].astype(F32)
        centred = wide - jnp.mean(wide, axis=1, keepdims=True)
        rate = lax.rsqrt(jnp.mean(centred * centred, axis=1, keepdims=True) + EPSILON)
        normed[low : low + step, :] = (centred * rate * gain_ref[...] + shift_ref[...]).astype(BF16)
    cut = cuts[0] + cuts[1]
    old_ref[...] = normed[: cuts[0], :]
    mem_ref[...] = normed[cuts[0] : cut, :]
    seg_ref[...] = normed[cut:, :]
    q_ref[...] = mm(normed[cut:, :], w_ref[:, :cols], NN)
    k_ref[...] = mm(normed[...], w_ref[:, cols : 2 * cols], NN).astype(BF16)
    v_ref[...] = mm(normed[...], w_ref[:, 2 * cols : 3 * cols], NN).astype(BF16)


def project(rows_all, gain, shift, columns, cuts):
    parts, group, each, width = rows_all.shape
    cols = columns.shape[1] // 4
    block = lambda size, wide: pl.BlockSpec((None, None, size, wide), lambda p, s: (p, s, 0, 0))
    placed = lambda size: pl.BlockSpec((None, size, width), lambda p, s: (s, p, 0))
    whole = lambda *shape: pl.BlockSpec(shape, lambda p, s: (0,) * len(shape))
    shape = lambda size, kind: jax.ShapeDtypeStruct((parts, group, size, cols), kind)
    return pl.pallas_call(
        functools.partial(project_kernel, cuts),
        grid_spec=pl.GridSpec(
            grid=(parts, group),
            in_specs=[
                block(each, width),
                whole(1, width),
                whole(1, width),
                whole(width, 4 * cols),
            ],
            out_specs=[placed(size) for size in cuts]
            + [block(cuts[2], cols), block(each, cols), block(each, cols)],
            scratch_shapes=[pltpu.VMEM((each, width), BF16)],
        ),
        out_shape=[jax.ShapeDtypeStruct((group, parts * size, width), BF16) for size in cuts]
        + [shape(cuts[2], F32), shape(each, BF16), shape(each, BF16)],
        compiler_params=pltpu.CompilerParams(
            dimension_semantics=("arbitrary", "arbitrary"), vmem_limit_bytes=VMEM_LIMIT
        ),
        cost_estimate=cost(17),
        name="project",
    )(rows_all, gain, shift, columns)


def gelu_both(x):
    near = jnp.abs(x)
    t = 1.0 / (1.0 + (0.3275911 * math.sqrt(0.5)) * near)
    bell = jnp.exp2((x * x) * (-0.5 * LOG2E))
    tail = 0.5 * 1.061405429
    for factor in (-1.453152027, 1.421413741, -0.284496736, 0.254829592):
        tail = tail * t + 0.5 * factor
    tail = tail * t * bell
    below = jnp.where(x < 0.0, tail, 1.0 - tail)
    return x * below, below + x * bell * (1.0 / math.sqrt(2.0 * math.pi))


def forward_back_kernel(
    last, parts, pair, n_ref, c_ref, *rest,
):
    up_refs, down_refs, shift_ref = rest[:parts], rest[parts : parts + pair], rest[parts + pair]
    rest = rest[parts + pair + 1 :]
    if last:
        part_in, grad_in, part_out, part_far, grad_out, grad_far, late_ref, sums_ref = rest[:8]
        pre, slope, hidden, act, up_out, down_out, sems, part_ref, grad_ref = rest[8:]
    else:
        part_ref, grad_ref, late_ref, sums_ref = rest[:4]
        pre, slope, hidden, act, up_out, down_out, sems = rest[4:]
    tile = pl.program_id(0)
    tiles = pl.num_programs(0)
    cols, units = up_refs[0].shape
    unit_cols, width = down_refs[0].shape
    rows = n_ref.shape[0]
    slot = lax.rem(tile, 2)
    up_weight = jnp.concatenate([ref[...] for ref in up_refs], axis=0)
    down_weight = jnp.concatenate([ref[...] for ref in down_refs], axis=0)

    def copies(at, index):
        return (
            pltpu.make_async_copy(
                up_out.at[at],
                late_ref.at[:, pl.ds(0, cols), pl.ds(pl.multiple_of(index * units, units), units)],
                sems.at[at, 0],
            ),
            pltpu.make_async_copy(
                down_out.at[at],
                late_ref.at[pl.ds(index * pair, pair), pl.ds(cols, unit_cols), :],
                sems.at[at, 1],
            ),
        )

    @pl.when(tile == 0)
    def _():
        if last:
            part_ref[...] = part_in[...]
            grad_ref[...] = grad_in[...]
        else:
            part_ref[...] = jnp.zeros_like(part_ref)
            grad_ref[...] = jnp.zeros_like(grad_ref)

    pre[...] = mm(n_ref[...], up_weight, NN)
    slope[...] = mm(c_ref[...], down_weight, NT)
    step = 64
    for low in range(0, rows, step):
        value, change = gelu_both(pre[low : low + step, :] + shift_ref[...])
        hidden[low : low + step, :] = value.astype(BF16)
        act[low : low + step, :] = (change * slope[low : low + step, :]).astype(BF16)
    part_ref[...] += mm(hidden[...], down_weight, NN)
    grad_ref[...] += mm(act[...], up_weight, NT)
    sums_ref[...] = jnp.sum(act[...].astype(F32), axis=0, keepdims=True)

    @pl.when(tile >= 2)
    def _():
        for copy in copies(slot, tile - 2):
            copy.wait()

    up_out[slot] = mm(n_ref[...], act[...], TN).astype(BF16).reshape(parts, cols, units)
    down_out[slot] = mm(hidden[...], c_ref[...], TN).astype(BF16).reshape(pair, unit_cols, width)
    for copy in copies(slot, tile):
        copy.start()

    @pl.when(tile == tiles - 1)
    def _():
        if last:
            part_out[...] = part_ref[: rows // 2, :]
            part_far[...] = part_ref[rows // 2 :, :].astype(BF16)
            grad_out[...] = grad_ref[: rows // 2, :]
            grad_far[...] = grad_ref[rows // 2 :, :].astype(BF16)
        for copy in (copies(1 - slot, tile - 1) if parts > pair else ()) + copies(slot, tile):
            copy.wait()


def forward_back(normed, cot, gathered, shift, carry):
    parts, _, width = gathered.shape
    rows = normed.shape[0]
    cols = width // parts
    unit_cols = shift.shape[1] // parts
    pair = 2
    units = pair * unit_cols
    last = len(carry) > 0
    one = pl.Buffered(1)
    whole = lambda *shape: pl.BlockSpec(shape, lambda t: (0,) * len(shape), pipeline_mode=one)
    up = lambda p: pl.BlockSpec((None, cols, units), lambda t: (p, 0, t))
    down = lambda i: pl.BlockSpec(
        (None, unit_cols, width), lambda t: (t * pair + i, cols // unit_cols, 0)
    )
    if last:
        sums = [((rows // 2, width), F32), ((rows // 2, width), BF16)] * 2
    else:
        sums = [((rows, width), F32)] * 2
    return pl.pallas_call(
        functools.partial(forward_back_kernel, last, parts, pair),
        grid_spec=pl.GridSpec(
            grid=(parts // pair,),
            in_specs=[
                whole(rows, width),
                whole(rows, width),
            ]
            + [up(p) for p in range(parts)]
            + [down(i) for i in range(pair)]
            + [pl.BlockSpec((1, units), lambda t: (0, t))]
            + [whole(rows, width) for _ in carry],
            out_specs=[whole(*shape) for shape, _ in sums]
            + [
                pl.BlockSpec(memory_space=pl.ANY),
                pl.BlockSpec((1, units), lambda t: (0, t)),
            ],
            scratch_shapes=[
                pltpu.VMEM((rows, units), F32),
                pltpu.VMEM((rows, units), F32),
                pltpu.VMEM((rows, units), BF16),
                pltpu.VMEM((rows, units), BF16),
                pltpu.VMEM((2, parts, cols, units), BF16),
                pltpu.VMEM((2, pair, unit_cols, width), BF16),
                pltpu.SemaphoreType.DMA((2, 2)),
            ]
            + [pltpu.VMEM((rows, width), F32) for _ in carry],
        ),
        out_shape=[jax.ShapeDtypeStruct(shape, kind) for shape, kind in sums]
        + [
            jax.ShapeDtypeStruct((parts, cols + unit_cols, width), BF16),
            jax.ShapeDtypeStruct((1, parts * unit_cols), F32),
        ],
        compiler_params=pltpu.CompilerParams(
            dimension_semantics=("arbitrary",), vmem_limit_bytes=VMEM_LIMIT
        ),
        cost_estimate=cost(29),
        name="forward_back",
    )(normed, cot, *[gathered] * (parts + pair), shift, *carry)


def leave_kernel(a_ref, s_ref, w_ref, shift_ref, gain_ref, bias_ref, flat_ref, m_ref, n_ref):
    parts = a_ref.shape[0]
    flat_ref[...] = jnp.concatenate([a_ref[part] for part in range(parts)], axis=1)
    m_ref[...] = s_ref[...].astype(F32) + (mm(flat_ref[...], w_ref[...], NN) + shift_ref[...])
    step = 32
    for low in range(0, m_ref.shape[0], step):
        unit, _ = standardise(m_ref[low : low + step, :])
        n_ref[low : low + step, :] = (unit * gain_ref[...] + bias_ref[...]).astype(BF16)


def leave(mixed_heads, segment, base, weight, shift, gain, bias):
    parts, group, seg, cols = mixed_heads.shape
    width = parts * cols
    rows = lambda: pl.BlockSpec((None, seg, width), lambda s: (s, 0, 0))
    vector = lambda: pl.BlockSpec((1, width), lambda s: (0, 0))
    shape = lambda kind: jax.ShapeDtypeStruct((group, seg, width), kind)
    return pl.pallas_call(
        leave_kernel,
        grid_spec=pl.GridSpec(
            grid=(group,),
            in_specs=[
                pl.BlockSpec((parts, None, seg, cols), lambda s: (0, s, 0, 0)),
                pl.BlockSpec((None, seg, width), lambda s: (s + base, 0, 0)),
                pl.BlockSpec((width, width), lambda s: (0, 0)),
                vector(),
                vector(),
                vector(),
            ],
            out_specs=[rows(), rows(), rows()],
        ),
        out_shape=[shape(BF16), shape(F32), shape(BF16)],
        compiler_params=pltpu.CompilerParams(vmem_limit_bytes=VMEM_LIMIT),
        cost_estimate=cost(6),
        name="leave",
    )(mixed_heads, segment, weight, shift, gain, bias)


def enter_kernel(
    m_ref, g_ref, far_ref, c_ref, w_ref, gain_ref, mg_ref, b_ref, a_ref, sums_ref
):
    @pl.when(pl.program_id(0) == 0)
    def _():
        sums_ref[...] = jnp.zeros_like(sums_ref)

    parts = a_ref.shape[0]
    rows, width = m_ref.shape
    step = 32
    total = [jnp.zeros((1, width), F32) for _ in range(4)]
    for low in range(0, rows, step):
        at = slice(low, low + step)
        unit, rate = standardise(m_ref[at, :])
        grad = g_ref[at, :] + far_ref[at, :].astype(F32)
        cot = c_ref[at, :].astype(F32)
        middle_grad = cot + standardise_back(unit, rate, grad, gain_ref[...])
        branch = middle_grad.astype(BF16)
        mg_ref[at, :] = middle_grad
        b_ref[at, :] = branch
        for i, value in enumerate((branch.astype(F32), grad * unit, grad, cot)):
            total[i] = total[i] + jnp.sum(value, axis=0, keepdims=True)
    sums_ref[...] += jnp.concatenate(total + [jnp.zeros((4, width), F32)], axis=0)
    for part in range(parts):
        low = part * a_ref.shape[2]
        weight = w_ref[low : low + a_ref.shape[2], :]
        a_ref[part] = mm(b_ref[...], weight, NT).astype(BF16)


def enter(middle, grad, far, cot, base, weight, gain, parts):
    group, seg, width = middle.shape
    cols = width // parts
    rows = lambda: pl.BlockSpec((None, seg, width), lambda s: (s, 0, 0))
    later = lambda: pl.BlockSpec((None, seg, width), lambda s: (s + base, 0, 0))
    shape = lambda kind: jax.ShapeDtypeStruct((group, seg, width), kind)
    return pl.pallas_call(
        enter_kernel,
        grid_spec=pl.GridSpec(
            grid=(group,),
            in_specs=[
                rows(),
                later(),
                later(),
                later(),
                pl.BlockSpec((width, width), lambda s: (0, 0)),
                pl.BlockSpec((1, width), lambda s: (0, 0)),
            ],
            out_specs=[
                rows(),
                rows(),
                pl.BlockSpec((parts, None, seg, cols), lambda s: (0, s, 0, 0)),
                pl.BlockSpec((8, width), lambda s: (0, 0)),
            ],
        ),
        out_shape=[
            shape(F32),
            shape(BF16),
            jax.ShapeDtypeStruct((parts, group, seg, cols), BF16),
            jax.ShapeDtypeStruct((8, width), F32),
        ],
        compiler_params=pltpu.CompilerParams(
            dimension_semantics=("arbitrary",), vmem_limit_bytes=VMEM_LIMIT
        ),
        cost_estimate=cost(7),
        name="enter",
    )(middle, grad, far, cot, weight, gain)


def compress_kernel(low, rows_ref, w_ref, shift_ref, out_ref, wide):
    count = out_ref.shape[0]
    cols = out_ref.shape[1]
    blocks = wide.shape[0]
    for at in range(blocks):
        wide[at] = rows_ref[low : low + 3 * count, at * LANES : (at + 1) * LANES].astype(F32)
    total = jnp.broadcast_to(shift_ref[...], (count, cols))
    for k in range(3):
        every = jnp.concatenate(
            [wide[at, pl.ds(k, count, stride=3), :] for at in range(blocks)], axis=1
        ).astype(BF16)
        total = total + mm(every, w_ref[:, k * cols : (k + 1) * cols], NN)
    out_ref[...] = total.astype(BF16)


def compress(rows_all, columns, shift, low, count):
    parts, group, each, width = rows_all.shape
    cols = columns.shape[1] // 3
    return pl.pallas_call(
        functools.partial(compress_kernel, low),
        grid_spec=pl.GridSpec(
            grid=(parts, group),
            in_specs=[
                pl.BlockSpec((None, None, each, width), lambda p, s: (p, s, 0, 0)),
                pl.BlockSpec((width, 3 * cols), lambda p, s: (0, 0)),
                pl.BlockSpec((1, cols), lambda p, s: (0, 0)),
            ],
            out_specs=pl.BlockSpec((None, None, count, cols), lambda p, s: (p, s, 0, 0)),
            scratch_shapes=[pltpu.VMEM((width // LANES, 3 * count, LANES), F32)],
        ),
        out_shape=jax.ShapeDtypeStruct((parts, group, count, cols), BF16),
        compiler_params=pltpu.CompilerParams(
            dimension_semantics=("arbitrary", "arbitrary"), vmem_limit_bytes=VMEM_LIMIT
        ),
        cost_estimate=cost(6.5),
        name="compress",
    )(rows_all, columns, shift)


def lay_out_kernel(
    parts, unit_cols, core_ref, a_ref, b_ref, c_ref, d_ref, up_ref, down_ref
):
    flipped = core_ref[0] == 1
    for half, (mine_ref, far_ref) in enumerate(((a_ref, c_ref), (b_ref, d_ref))):
        mine, far = mine_ref[...].astype(F32), far_ref[...].astype(F32)
        for core, value in enumerate(
            (jnp.where(flipped, far, mine), jnp.where(flipped, mine, far))
        ):
            for part in range(parts):
                at = ((part * 2 + core) * 2 + half) * unit_cols
                up_ref[:, at : at + unit_cols] = value[
                    0, :, part * unit_cols : (part + 1) * unit_cols
                ]
            down_ref[2 * core + half] = value[1]


def lay_out(core, mine, far, parts):
    _, rows, width = mine.shape
    step = rows // 4 if rows % 64 == 0 else rows
    half = lambda i: pl.BlockSpec((2, step, width), lambda r, *_: (i, r, 0))
    return pl.pallas_call(
        functools.partial(lay_out_kernel, parts, rows),
        grid_spec=pltpu.PrefetchScalarGridSpec(
            num_scalar_prefetch=1,
            grid=(rows // step,),
            in_specs=[half(0), half(1), half(0), half(1)],
            out_specs=[
                pl.BlockSpec((step, 4 * width), lambda r, *_: (r, 0)),
                pl.BlockSpec((4, step, width), lambda r, *_: (0, r, 0)),
            ],
        ),
        out_shape=[
            jax.ShapeDtypeStruct((rows, 4 * width), F32),
            jax.ShapeDtypeStruct((4, rows, width), F32),
        ],
        compiler_params=pltpu.CompilerParams(vmem_limit_bytes=VMEM_LIMIT),
        cost_estimate=cost(4),
        name="lay_out",
    )(core.reshape(1), mine, mine, far, far)


def lay_squares_kernel(in_ref, *out_refs):
    parts = in_ref.shape[0]
    cols = in_ref.shape[2] // len(out_refs)
    for at, out_ref in enumerate(out_refs):
        for part in range(parts):
            out_ref[:, part * cols : (part + 1) * cols] = in_ref[
                part, :, at * cols : (at + 1) * cols
            ].astype(F32)


def lay_squares(summed, rows):
    parts, _, wide = summed.shape
    width = parts * wide // 4
    step = rows // 2
    return pl.pallas_call(
        lay_squares_kernel,
        grid_spec=pl.GridSpec(
            grid=(2,),
            in_specs=[pl.BlockSpec((parts, step, wide), lambda i: (0, i, 0))],
            out_specs=[pl.BlockSpec((step, width), lambda i: (i, 0)) for _ in range(4)],
        ),
        out_shape=[jax.ShapeDtypeStruct((rows, width), F32) for _ in range(4)],
        compiler_params=pltpu.CompilerParams(vmem_limit_bytes=VMEM_LIMIT),
        cost_estimate=cost(2.5),
        name="lay_squares",
    )(summed)


def settle_kernel(
    me_ref, old_ref, mem_ref, seg_ref, q_ref, k_ref, v_ref, ks_ref, vs_ref, w_ref, table_ref, dt_ref,
    sums_ref, gain_ref, shift_ref, small_ref, part_ref, out_ref, total,
):
    stream = pl.program_id(0)
    parts, rows, wide = out_ref.shape
    cols = wide // 4
    width = parts * cols

    @pl.when(stream == 0)
    def _():
        total[...] = jnp.zeros_like(total)

    total[:cols, :] += mm(q_ref[...], seg_ref[...], TN)
    for at, grad in ((cols, k_ref), (2 * cols, v_ref)):
        low = 0
        for normed in (old_ref, mem_ref, seg_ref):
            high = low + normed.shape[0]
            total[at : at + cols, :] += mm(grad[:, low:high], normed[...], NN)
            low = high
    three = jnp.concatenate([q_ref[...], ks_ref[...], vs_ref[...]], axis=1)
    part = mm(three, w_ref[:, : 3 * cols], NT).astype(BF16)
    part_ref[...] = part.reshape(part_ref.shape)

    @pl.when(stream == pl.num_programs(0) - 1)
    def _():
        heads = dt_ref.shape[0]
        rel = jnp.concatenate(
            [mm(dt_ref[head].astype(BF16), table_ref[...], NN) for head in range(heads)], axis=0
        )
        line = lambda row: jnp.concatenate(
            [sums_ref[head, row : row + 1, :] for head in range(heads)], axis=1
        )
        row_sums = jnp.concatenate([line(2), line(3), line(4)], axis=1)
        weight = w_ref[:, : 3 * cols].astype(F32)
        shift_grad = lax.dot_general(
            jnp.broadcast_to(row_sums, (8, 3 * cols)),
            weight,
            (NT, ((), ())),
            precision=lax.Precision.HIGHEST,
            preferred_element_type=F32,
        )[0:1]
        along = jnp.sum(weight.T * total[...], axis=0, keepdims=True)
        gain_grad = (along - shift_ref[...] * shift_grad) / gain_ref[...]
        for at in range(parts):
            low, high = at * cols, (at + 1) * cols
            out_ref[at, :cols, : 3 * cols] = total[:, low:high].T.astype(BF16)
            out_ref[at, :cols, 3 * cols :] = rel[:, low:high].T.astype(BF16)
            mine = (me_ref[0] == at).astype(F32)
            none = jnp.zeros((1, 2 * cols), F32)
            first = jnp.concatenate([gain_grad[:, low:high], shift_grad[:, low:high], none], axis=1)
            second = jnp.concatenate([none, mine * line(0), mine * line(1)], axis=1)
            added = jnp.concatenate([first, second, jnp.zeros((14, wide), F32)], axis=0)
            out_ref[at, cols:, :] = (small_ref[at] + added).astype(BF16)


def settle(me, normed, grads, columns, table, table_grad, sums, gain, shift, small, parts):
    group, queries, width = normed[2].shape
    cols = width // parts
    wide = 4 * cols
    block = lambda array: pl.BlockSpec((None, *array.shape[1:]), lambda s, *_: (s, 0, 0))
    whole = lambda *shape: pl.BlockSpec(
        shape, lambda s, *_: (0,) * len(shape), pipeline_mode=pl.Buffered(1)
    )
    return pl.pallas_call(
        settle_kernel,
        grid_spec=pltpu.PrefetchScalarGridSpec(
            num_scalar_prefetch=1,
            grid=(group,),
            in_specs=[block(rows) for rows in normed]
            + [block(grad) for grad in grads]
            + [
                whole(*columns.shape),
                whole(*table.shape),
                whole(*table_grad.shape),
                whole(*sums.shape),
                whole(1, width),
                whole(1, width),
                whole(*small.shape),
            ],
            out_specs=[
                pl.BlockSpec((parts, None, queries // parts, width), lambda s, *_: (0, s, 0, 0)),
                whole(parts, cols + 16, wide),
            ],
            scratch_shapes=[pltpu.VMEM((3 * cols, width), F32)],
        ),
        out_shape=[
            jax.ShapeDtypeStruct((parts, group, queries // parts, width), BF16),
            jax.ShapeDtypeStruct((parts, cols + 16, wide), BF16),
        ],
        compiler_params=pltpu.CompilerParams(
            dimension_semantics=("arbitrary",), vmem_limit_bytes=VMEM_LIMIT
        ),
        cost_estimate=cost(14),
        name="settle",
    )(me.reshape(1), *normed, *grads, columns, table, table_grad, sums, gain, shift, small)


def standardise(rows):
    mean = jnp.mean(rows, axis=-1, keepdims=True)
    centred = rows - mean
    rate = lax.rsqrt(jnp.mean(centred * centred, axis=-1, keepdims=True) + EPSILON)
    return centred * rate, rate


def standardise_back(unit, rate, grad, gain):
    scaled = grad * gain
    mean = jnp.mean(scaled, axis=-1, keepdims=True)
    along = jnp.mean(scaled * unit, axis=-1, keepdims=True)
    return rate * (scaled - mean - unit * along)


def sinusoid_reversed(rows, width):
    positions = (rows - 1 - jnp.arange(rows, dtype=jnp.int32)).astype(F32)[:, None]
    frequency = jnp.exp(
        jnp.arange(width // 2, dtype=F32) * (-2.0 * math.log(10000.0) / width)
    )
    angles = positions * frequency[None, :]
    return jnp.concatenate([jnp.sin(angles), jnp.cos(angles)], axis=1).astype(BF16)


def dot(left, right):
    return mm(left, right, NN)


def swap(value):
    return lax.ppermute(value, "core", [(0, 1), (1, 0)])


def exchange(blocks, name, axis=0):
    count = lax.axis_size(name)
    me = lax.axis_index(name)
    block = lambda at: lax.dynamic_index_in_dim(blocks, at, axis, keepdims=False)
    return [block(me)] + [
        lax.ppermute(block(me ^ apart), name, [(i, i ^ apart) for i in range(count)])
        for apart in range(1, count)
    ]


def collect(block, name):
    count = lax.axis_size(name)
    me = lax.axis_index(name)
    found = jnp.stack(
        [block]
        + [
            lax.ppermute(block, name, [(i, i ^ apart) for i in range(count)])
            for apart in range(1, count)
        ]
    )
    return jnp.stack(
        [lax.dynamic_index_in_dim(found, me ^ i, 0, keepdims=False) for i in range(count)]
    )


def add_up(arrays, kind=BF16):
    total = arrays[0].astype(F32)
    for array in arrays[1:]:
        total = total + array.astype(F32)
    return total.astype(kind)


def body(
    segment, memory, compressed, eob, reset, ln1_gain, ln1_bias, w_query, w_key, w_value,
    w_out, out_bias, w_rel, bias_content, bias_position, ln2_gain, ln2_bias, w_up, up_bias,
    w_down, down_bias, conv_weight, conv_bias, cotangent,
):
    parts = lax.axis_size("seq")
    layers = lax.axis_size("z")
    core = lax.axis_index("core")
    me = lax.axis_index("seq")
    group, seg, width = segment.shape
    mem, old = memory.shape[1], compressed.shape[1]
    cuts = (old, mem, seg)
    each = old + mem + seg
    keys_in_all = parts * each
    cols = width // parts
    wide = 4 * cols
    own = group * seg
    unit_cols = w_up.shape[1] // (4 * parts)
    barrier = lax.optimization_barrier

    def by_columns(matrices):
        count = matrices.shape[0]
        sent = matrices.reshape(count, cols, parts, cols).transpose(2, 1, 0, 3)
        return sent.reshape(parts, cols, count * cols)

    up_bias_own = lax.dynamic_slice_in_dim(up_bias, core * 2 * unit_cols, 2 * unit_cols, 0)
    vectors = jnp.concatenate(
        [ln1_gain, ln1_bias, out_bias, ln2_gain, ln2_bias, down_bias, up_bias_own]
    )
    vectors = jnp.pad(vectors.reshape(2, wide), ((0, 14), (0, 0)))
    half = cols // 2
    sent = by_columns(jnp.concatenate([jnp.stack([w_query, w_key, w_value, w_rel]), conv_weight]))
    sent = lax.dynamic_slice_in_dim(sent, core * half, half, 1)
    out_half = lax.dynamic_slice_in_dim(w_out, core * half, half, 0)
    sent = jnp.concatenate([sent, jnp.broadcast_to(out_half, (parts, half, width))], axis=2)
    vectors = jnp.pad(vectors, ((0, 0), (0, 3 * cols + width)))
    sent = jnp.concatenate([sent, jnp.broadcast_to(vectors, (parts, *vectors.shape))], axis=1)
    got = lax.all_to_all(sent, "seq", 0, 0, tiled=True)
    spans = [(0, group)]
    local = [
        jnp.concatenate([compressed[low:high], memory[low:high], segment[low:high]], axis=1)
        for low, high in spans
    ]
    rows_all = [lax.all_gather(local[0], "seq")]
    mine = got[:, :half]
    far = swap(mine)
    columns = jnp.stack(
        [jnp.where(core == 0, mine, far), jnp.where(core == 0, far, mine)], axis=1
    ).reshape(width, 7 * cols + width)
    columns, conv_columns, out_full = (
        columns[:, :wide],
        columns[:, wide : 7 * cols],
        columns[:, 7 * cols :],
    )
    vectors = got[:, half : half + 2, :wide].reshape(parts, 2 * wide).astype(F32)
    gain_one, shift_one, out_shift, gain_two, shift_two, down_shift = (
        vectors[:, cols * i : cols * (i + 1)].reshape(1, width) for i in range(6)
    )
    up_shift = vectors[:, 6 * cols :].reshape(parts, 2, unit_cols).transpose(1, 0, 2)
    up_shift = up_shift.reshape(2, 1, parts * unit_cols)
    up_quarters = lax.dynamic_slice_in_dim(
        w_up.reshape(cols, parts, 2, 2, unit_cols), core, 1, 2
    ).reshape(cols, parts, 2, unit_cols)
    up_quarters = [up_quarters[:, :, i].reshape(cols, width) for i in range(2)]
    down_half = lax.dynamic_slice_in_dim(w_down, core * 2 * unit_cols, 2 * unit_cols, 0)
    down_quarters = [down_half[unit_cols * i : unit_cols * (i + 1)] for i in range(2)]
    first = jnp.concatenate([up_quarters[0], down_quarters[0]], axis=0)
    second = jnp.concatenate([up_quarters[1], down_quarters[1]], axis=0)
    cot_own = cotangent.reshape(own, width)
    cot_both = jnp.concatenate([cot_own, swap(cot_own)], axis=0)

    table_rev = sinusoid_reversed(keys_in_all, width)
    proj_rev = dot(table_rev, columns[:, 3 * cols :]).astype(BF16)
    index = jnp.arange(eob.shape[1], dtype=jnp.int32)[None, :]
    opens = jnp.pad(eob, ((0, 0), (1, 0)))[:, :-1] == 1
    start = lax.cummax(jnp.where(opens, index, 0), axis=1)
    shade = jnp.where((start == 0) & (reset[:, None] == 0), 0.0, MASKED)
    info = jnp.stack([start.astype(F32), shade], axis=2)
    info = jnp.pad(info, ((0, 0), (0, 0), (0, LANES - 2)))
    rows_all[0], proj_rev, info, cot_both, table_rev, columns, conv_columns, out_full, *local = barrier(
        (rows_all[0], proj_rev, info, cot_both, table_rev, columns, conv_columns, out_full, *local)
    )
    rows_all = [rows_all[0]] + [lax.all_gather(rows, "seq") for rows in local[1:]]

    kept, heads = [], []
    for batch, (low, high) in enumerate(spans):
        if batch == len(spans) - 1:
            rows_all[batch], first, *heads = barrier((rows_all[batch], first, *heads))
            first = lax.all_gather(first, "seq")
        *normed, query, keys, values = project(rows_all[batch], gain_one, shift_one, columns, cuts)
        second, query = barrier((second, query))
        second = lax.all_gather(second, "seq")
        weights, inverse, mixed_heads, content_q, position_q = attend(
            query,
            bias_content.astype(F32).reshape(1, cols),
            bias_position.astype(F32).reshape(1, cols),
            keys,
            values,
            proj_rev,
            info[low:high],
            cuts,
        )
        kept.append((weights, inverse, mixed_heads, content_q, position_q, keys, values))
        heads.append(lax.all_to_all(mixed_heads, "seq", 0, 0, tiled=True))

    mixed_heads, conv_columns = barrier((mixed_heads, conv_columns))
    packed = compress(
        rows_all[0], conv_columns, conv_bias.astype(F32).reshape(1, cols), old, mem // 3
    )
    packed, *heads = barrier((packed, *heads))

    attended, middle, normed_two = [], [], []
    for (low, high), batch in zip(spans, heads):
        one, two, three = leave(batch, segment, low, out_full, out_shift, gain_two, shift_two)
        attended.append(one.reshape(-1, width))
        middle.append(two)
        normed_two.append(three.reshape(-1, width))
    both = jnp.concatenate(normed_two + [swap(rows) for rows in normed_two], axis=0)
    part, part_grad, late_one, unit_one = forward_back(both, cot_both, first, up_shift[0], ())
    late_one = lax.psum_scatter(
        late_one.reshape(-1, width), "seq", scatter_dimension=0, tiled=True
    )
    part, part_far, part_grad, grad_far, late_two, unit_two = forward_back(
        both, cot_both, second, up_shift[1], (part, part_grad)
    )
    grad_far = swap(grad_far)
    by_stream = lambda rows: rows.reshape(group, seg, width)
    middle_grad, branch_grad, head_grad, sums_two = [], [], [], 0.0
    for (low, high), batch in zip(spans, middle):
        one, two, three, four = enter(
            batch, by_stream(part_grad), by_stream(grad_far), cotangent, low, out_full, gain_two, parts
        )
        middle_grad.append(one)
        branch_grad.append(two.reshape(-1, width))
        three, part_grad = barrier((three, part_grad))
        head_grad.append(lax.all_to_all(three, "seq", 0, 0, tiled=True))
        sums_two = sums_two + four
    result = part + swap(part_far).astype(F32) + down_shift
    output = (jnp.concatenate(middle).reshape(own, width) + result).astype(BF16)
    output = output.reshape(group, seg, width)

    out_shift_grad, gain_two_grad, shift_two_grad, down_shift_grad = (
        sums_two[i].reshape(parts, cols) for i in range(4)
    )
    none = jnp.zeros((parts, 2 * cols), F32)
    unit_sums = jnp.stack(
        [unit_one.reshape(parts, unit_cols), unit_two.reshape(parts, unit_cols)], axis=1
    ).reshape(parts, 2 * unit_cols)
    small = jnp.stack(
        [
            jnp.concatenate([none, out_shift_grad, gain_two_grad], axis=1),
            jnp.concatenate([shift_two_grad, down_shift_grad, none], axis=1),
            jnp.concatenate(
                [jnp.where(core == 0, unit_sums, 0.0), jnp.where(core == 1, unit_sums, 0.0)], axis=1
            ),
        ],
        axis=1,
    )
    small = jnp.pad(small, ((0, 0), (0, 13), (0, 0)))
    weights, inverse, mixed_heads, content_q, position_q, keys, values = kept[0]
    out_grad = mm(jnp.concatenate(attended), jnp.concatenate(branch_grad), TN)
    out_grad = out_grad.astype(BF16).reshape(parts, cols, width)
    late_one, small, out_grad, late_two, head_grad = barrier(
        (late_one, small, out_grad, late_two, head_grad[0])
    )
    late_two = lax.psum_scatter(
        late_two.reshape(-1, width), "seq", scatter_dimension=0, tiled=True
    )
    late_one = exchange(late_one.reshape(layers, -1, width), "z")
    query_grad, *key_grads, table_grad, sums = pull(
        weights, inverse, mixed_heads, head_grad, content_q, position_q, keys, values, proj_rev, cuts
    )
    late_one, late_two, out_grad, query_grad = barrier((late_one, late_two, out_grad, query_grad))
    late_two = exchange(late_two.reshape(layers, -1, width), "z")
    out_sent = exchange(out_grad, "seq")
    late_one = add_up(late_one)
    seg_part, square_grads = settle(
        me, normed, (query_grad, *key_grads), columns, table_rev, table_grad, sums, gain_one,
        shift_one, small, parts,
    )
    late_two, out_sent, square_grads = barrier((late_two, out_sent, square_grads))
    summed = lax.all_to_all(square_grads, "seq", 0, 0, tiled=True)
    late = collect(jnp.stack([late_one, add_up(late_two)]), "z")
    out_sent = add_up(out_sent)
    late, out_sent, summed, seg_part = barrier((late, out_sent, summed, seg_part))
    squares = parts * (cols + 16)
    summed = jnp.concatenate([summed.reshape(squares, wide), out_sent.reshape(-1, wide)], axis=0)
    summed, packed = barrier((summed, packed))
    summed = lax.psum(summed, ("z", "core"))
    packed = jnp.stack(exchange(packed, "seq"))
    new_compressed = jnp.concatenate(
        [lax.dynamic_index_in_dim(packed, p ^ me, 0, keepdims=False) for p in range(parts)], axis=2
    )
    seg_grad = lax.all_to_all(seg_part, "seq", 0, 0, tiled=True).astype(F32)
    seg_grad = jnp.sum(seg_grad, axis=0).reshape(own, width)
    unit_seg, rate_seg = standardise(segment.reshape(own, width).astype(F32))
    rows_grad = standardise_back(unit_seg, rate_seg, seg_grad, gain_one)
    segment_grad = jnp.concatenate(middle_grad, axis=0) + by_stream(rows_grad)

    late = late.reshape(layers, 2, -1, width).transpose(1, 0, 2, 3).reshape(4, unit_cols, width)
    up_w, down_w = lay_out(core, late, swap(late), parts)
    down_w = down_w.reshape(4 * unit_cols, width)
    summed, output, segment_grad, new_compressed, up_w, down_w = barrier(
        (summed, output, segment_grad, new_compressed, up_w, down_w)
    )
    out_w = summed[squares:].reshape(cols, width).astype(F32)
    summed = summed[:squares].reshape(parts, cols + 16, wide)
    query_w, key_w, value_w, rel_w = lay_squares(summed, cols)
    small = jnp.sum(summed[:, cols : cols + 3].astype(F32), axis=0)
    piece = lambda row, i: small[row, cols * i : cols * (i + 1)]
    return (
        output,
        segment_grad,
        piece(0, 0),
        piece(0, 1),
        query_w,
        key_w,
        value_w,
        out_w,
        piece(0, 2),
        rel_w,
        piece(1, 2),
        piece(1, 3),
        piece(0, 3),
        piece(1, 0),
        up_w,
        small[2],
        down_w,
        piece(1, 1),
        new_compressed,
    )


def solution(mesh):
    dp = mesh.shape["dp"]
    cores = jax.sharding.Mesh(
        mesh.devices.reshape(dp // 2, 2, mesh.shape["seq"]), ("z", "core", "seq")
    )
    rows = P(("z", "core"), "seq", None)
    shard, matrix = P("seq"), P("seq", None)
    return jax.shard_map(
        body,
        mesh=cores,
        in_specs=(
            rows, rows, rows, P(("z", "core"), None), P(("z", "core")), shard, shard, matrix,
            matrix, matrix, matrix, shard, matrix, shard, shard, shard, shard, matrix, shard,
            matrix, shard, P(None, "seq", None), shard, rows,
        ),
        out_specs=(
            rows, rows, shard, shard, matrix, matrix, matrix, matrix, shard, matrix, shard,
            shard, shard, shard, matrix, shard, matrix, shard, rows,
        ),
        check_vma=False,
    )
```

```python
import functools
import math

import jax
import jax.numpy as jnp
from jax import lax
from jax.experimental import pallas as pl
from jax.experimental.pallas import tpu as pltpu
from jax.sharding import PartitionSpec as P

HEADS = 8
DH = 128
EPSILON = 1e-05
MASKED = -1e30
LANES = 128
BLOCK = 256
CHUNK = 16
VMEM_LIMIT = 60 * 2**20
SCALE = 1.0 / math.sqrt(DH)
LOG2E = 1.4426950408889634
BF16 = jnp.bfloat16
F32 = jnp.float32


def cost(microseconds):
    return pl.CostEstimate(flops=int(microseconds * 1.15e7), bytes_accessed=0, transcendentals=0)


def mm(left, right, dims):
    return lax.dot_general(left, right, (dims, ((), ())), preferred_element_type=F32)


NN = ((1,), (0,))
NT = ((1,), (1,))
TN = ((0,), (0,))


def lean_left(block, first_row, fill_columns):
    columns = block.shape[1] // LANES
    far = BLOCK - 1 - first_row
    whole, part = far // LANES, far % LANES
    turned = [
        pltpu.roll(
            block[:, LANES * t : LANES * (t + 1)], LANES - part, 1, stride=1, stride_axis=0
        )
        for t in range(columns)
    ]
    rows = lax.broadcasted_iota(jnp.int32, (block.shape[0], LANES), 0)
    lanes = lax.broadcasted_iota(jnp.int32, (block.shape[0], LANES), 1)
    near = lanes - rows < LANES - part
    out = []
    for t in range(fill_columns):
        a = turned[(t + whole) % columns]
        b = turned[(t + whole + 1) % columns]
        out.append(jnp.where(near, a, b))
    return jnp.concatenate(out, axis=1)


def lean_right(block, first_row):
    columns = block.shape[1] // LANES
    whole, part = first_row // LANES, first_row % LANES
    turned = [
        pltpu.roll(block[:, LANES * t : LANES * (t + 1)], part, 1, stride=1, stride_axis=0)
        for t in range(columns)
    ]
    rows = lax.broadcasted_iota(jnp.int32, (block.shape[0], LANES), 0)
    lanes = lax.broadcasted_iota(jnp.int32, (block.shape[0], LANES), 1)
    wrapped = lanes - rows < part
    out = []
    for t in range(columns):
        a = turned[(t - whole) % columns]
        b = turned[(t - whole - 1) % columns]
        out.append(jnp.where(wrapped, b, a))
    return jnp.concatenate(out, axis=1)


def flip_matrix(kind):
    rows = lax.broadcasted_iota(jnp.int32, (BLOCK, BLOCK), 0)
    lanes = lax.broadcasted_iota(jnp.int32, (BLOCK, BLOCK), 1)
    return (rows + lanes == BLOCK - 1).astype(F32).astype(kind)


def in_place_order(parts_ref, out_ref, cuts):
    parts = parts_ref.shape[0]
    low, base = 0, 0
    for size in cuts:
        for part in range(parts):
            out_ref[base + part * size : base + (part + 1) * size, :] = parts_ref[
                part, low : low + size, :
            ]
        low += size
        base += parts * size


def attend_kernel(
    cuts, q_ref, cb_ref, pb_ref, k_ref, v_ref, t_ref, info_ref,
    e_ref, inv_ref, o_ref, cq_ref, pq_ref,
    keys, values, raw, lean, mix, tops, sums,
):
    parts, seg, _ = q_ref.shape
    queries = parts * seg
    old = parts * (cuts[0] + cuts[1])
    in_place_order(k_ref, keys, cuts)
    in_place_order(v_ref, values, cuts)
    q = q_ref[...].reshape(queries, DH)
    content_q = (q + cb_ref[...]).astype(BF16)
    position_q = (q + pb_ref[...]).astype(BF16)
    cq_ref[...] = content_q.reshape(parts, seg, DH)
    pq_ref[...] = position_q.reshape(parts, seg, DH)
    for block in range(queries // BLOCK):
        row0 = block * BLOCK
        width = old + row0 + BLOCK
        skip = queries - BLOCK - row0
        raw[:, :width] = mm(content_q[row0 : row0 + BLOCK], keys[:width, :], NT)
        lean[:, :width] = mm(position_q[row0 : row0 + BLOCK], t_ref[skip : skip + width, :], NT)
        for chunk in range(BLOCK // CHUNK):
            r0 = chunk * CHUNK
            rows = slice(r0, r0 + CHUNK)
            turned = lean_left(lean[rows, :width], r0, width // LANES)
            score = raw[rows, :width] + turned
            start = info_ref[row0 + r0 : row0 + r0 + CHUNK, 0:1].astype(jnp.int32)
            shade = info_ref[row0 + r0 : row0 + r0 + CHUNK, 1:2]
            past = score[:, :old] + shade
            place = lax.broadcasted_iota(jnp.int32, (CHUNK, row0 + BLOCK), 1)
            own = lax.broadcasted_iota(jnp.int32, (CHUNK, row0 + BLOCK), 0) + (row0 + r0)
            now = jnp.where((place <= own) & (place >= start), score[:, old:], MASKED)
            raw[rows, :old] = past
            raw[rows, old:width] = now
            top = past[:, :LANES]
            for low in range(LANES, old, LANES):
                top = jnp.maximum(top, past[:, low : low + LANES])
            for low in range(0, row0 + BLOCK, LANES):
                top = jnp.maximum(top, now[:, low : low + LANES])
            tops[rows, :] = top
        top = jnp.max(tops[...], axis=1, keepdims=True)
        tops[...] = jnp.broadcast_to(top, (BLOCK, LANES))
        for chunk in range(BLOCK // CHUNK):
            r0 = chunk * CHUNK
            rows = slice(r0, r0 + CHUNK)
            top = tops[rows, :]
            total = jnp.zeros((CHUNK, LANES), F32)
            for low in range(0, width, LANES):
                weight = jnp.exp2((raw[rows, low : low + LANES] - top) * (SCALE * LOG2E))
                total = total + weight
                e_ref[row0 + r0 : row0 + r0 + CHUNK, low : low + LANES] = weight.astype(BF16)
            sums[rows, :] = total
        total = jnp.sum(sums[...], axis=1, keepdims=True)
        inv_ref[row0 : row0 + BLOCK, :] = jnp.broadcast_to(1.0 / total, (BLOCK, DH))
        mix[row0 : row0 + BLOCK, :] = mm(
            e_ref[row0 : row0 + BLOCK, :width], values[:width, :], NN
        )
    o_ref[...] = (mix[...] * inv_ref[...]).astype(BF16).reshape(parts, seg, DH)


def attend(query, content_shift, position_shift, keys, values, table_rev, info, cuts):
    parts, group, seg, cols = query.shape
    rows = keys.shape[2]
    queries, key_count, heads = parts * seg, parts * rows, cols // DH
    by_head = lambda size: pl.BlockSpec((parts, None, size, DH), lambda s, h: (0, s, 0, h))
    grid_spec = pl.GridSpec(
        grid=(group, heads),
        in_specs=[
            by_head(seg),
            pl.BlockSpec((1, DH), lambda s, h: (0, h)),
            pl.BlockSpec((1, DH), lambda s, h: (0, h)),
            by_head(rows),
            by_head(rows),
            pl.BlockSpec((key_count, DH), lambda s, h: (0, h)),
            pl.BlockSpec((None, queries, LANES), lambda s, h: (s, 0, 0)),
        ],
        out_specs=[
            pl.BlockSpec((None, None, queries, key_count), lambda s, h: (s, h, 0, 0)),
            pl.BlockSpec((None, None, queries, DH), lambda s, h: (s, h, 0, 0)),
            by_head(seg),
            by_head(seg),
            by_head(seg),
        ],
        scratch_shapes=[
            pltpu.VMEM((key_count, DH), BF16),
            pltpu.VMEM((key_count, DH), BF16),
            pltpu.VMEM((BLOCK, key_count), F32),
            pltpu.VMEM((BLOCK, key_count), F32),
            pltpu.VMEM((queries, DH), F32),
            pltpu.VMEM((BLOCK, LANES), F32),
            pltpu.VMEM((BLOCK, LANES), F32),
        ],
    )
    small = jax.ShapeDtypeStruct((parts, group, seg, cols), BF16)
    return pl.pallas_call(
        functools.partial(attend_kernel, cuts),
        grid_spec=grid_spec,
        out_shape=[
            jax.ShapeDtypeStruct((group, heads, queries, key_count), BF16),
            jax.ShapeDtypeStruct((group, heads, queries, DH), F32),
            small,
            small,
            small,
        ],
        compiler_params=pltpu.CompilerParams(
            dimension_semantics=("arbitrary", "arbitrary"), vmem_limit_bytes=VMEM_LIMIT
        ),
        cost_estimate=cost(40),
        name="attend",
    )(query, content_shift, position_shift, keys, values, table_rev, info)


def pull_kernel(
    cuts, e_ref, inv_ref, o_ref, g_ref, cq_ref, pq_ref, k_ref, v_ref, t_ref,
    dq_ref, dk_ref, dv_ref, ks_ref, vs_ref, dt_ref, sums_ref,
    keys, values, grad, prob, part, score, lean, key_sum, value_sum,
):
    stream = pl.program_id(1)
    parts, seg, _ = g_ref.shape
    queries = parts * seg
    old = parts * (cuts[0] + cuts[1])
    in_place_order(k_ref, keys, cuts)
    in_place_order(v_ref, values, cuts)
    grad[...] = (g_ref[...].reshape(queries, DH).astype(F32) * inv_ref[...]).astype(BF16)
    attended = o_ref[...].reshape(queries, DH)
    content_q = cq_ref[...].reshape(queries, DH)
    position_q = pq_ref[...].reshape(queries, DH)

    @pl.when(stream == 0)
    def _():
        dt_ref[...] = jnp.zeros_like(dt_ref)
        sums_ref[...] = jnp.zeros_like(sums_ref)

    key_sum[...] = jnp.zeros_like(key_sum)
    value_sum[...] = jnp.zeros_like(value_sum)
    content_total = jnp.zeros((1, DH), F32)
    position_total = jnp.zeros((1, DH), F32)
    query_total = jnp.zeros((1, DH), F32)
    flip = flip_matrix(BF16)
    turn = lambda rows: mm(flip, rows, NN).astype(BF16)
    for block in range(queries // BLOCK):
        row0 = block * BLOCK
        width = old + row0 + BLOCK
        skip = queries - BLOCK - row0
        rows = slice(row0, row0 + BLOCK)
        grad_back = turn(grad[rows, :])
        dots_back = jnp.sum(
            grad_back.astype(F32) * turn(attended[rows]).astype(F32), axis=1, keepdims=True
        )
        content_back = turn(content_q[rows])
        position_back = turn(position_q[rows])
        prob[:, :width] = mm(grad_back, values[:width, :], NT)
        both = mm(jnp.concatenate([flip, grad[rows, :].T], axis=0), e_ref[rows, :width], NN)
        part[:, :width] = both[:BLOCK]
        value_sum[:, :width] += both[BLOCK:]
        for chunk in range(BLOCK // CHUNK):
            r0 = chunk * CHUNK
            mean = dots_back[r0 : r0 + CHUNK, 0:1]
            change = part[r0 : r0 + CHUNK, :width] * (prob[r0 : r0 + CHUNK, :width] - mean)
            score[r0 : r0 + CHUNK, :width] = change.astype(BF16)
            lean[r0 : r0 + CHUNK, :width] = lean_right(change, r0).astype(BF16)
        content_grad = (mm(score[:, :width], keys[:width, :], NN) * SCALE).astype(BF16).astype(F32)
        position_grad = (
            (mm(lean[:, :width], t_ref[skip : skip + width, :], NN) * SCALE)
            .astype(BF16)
            .astype(F32)
        )
        query_grad = turn((content_grad + position_grad).astype(BF16))
        content_total += jnp.sum(content_grad, axis=0, keepdims=True)
        position_total += jnp.sum(position_grad, axis=0, keepdims=True)
        query_total += jnp.sum(query_grad.astype(F32), axis=0, keepdims=True)
        dq_ref[rows, :] = query_grad
        key_sum[:, :width] += mm(content_back, score[:, :width], TN)
        dt_ref[:, skip : skip + width] += mm(position_back, lean[:, :width], TN) * SCALE
    key_cols = (key_sum[...] * SCALE).astype(BF16)
    value_cols = value_sum[...].astype(BF16)
    dk_ref[...] = key_cols
    dv_ref[...] = value_cols
    ks_ref[...] = (key_sum[:, old:] * SCALE).T.astype(BF16)
    vs_ref[...] = value_sum[:, old:].T.astype(BF16)
    ones = jnp.ones((8, key_cols.shape[1]), BF16)
    key_total = mm(ones, key_cols, NT)[0:1]
    value_total = mm(ones, value_cols, NT)[0:1]
    sums_ref[...] += jnp.concatenate(
        [
            content_total,
            position_total,
            query_total,
            key_total,
            value_total,
            jnp.zeros((3, DH), F32),
        ],
        axis=0,
    )


def pull(head, weights, inverse, attended, out_grad, content_q, position_q, keys, values, table_rev, cuts):
    parts, group, seg, cols = out_grad.shape
    rows = keys.shape[2]
    queries, key_count = parts * seg, parts * rows
    by_head = lambda size: pl.BlockSpec((parts, None, size, DH), lambda h, s: (0, s, 0, head))
    by_row = lambda: pl.BlockSpec((None, queries, DH), lambda h, s: (s, 0, h))
    by_place = lambda: pl.BlockSpec((None, DH, key_count), lambda h, s: (s, h, 0))
    grid_spec = pl.GridSpec(
        grid=(1, group),
        in_specs=[
            pl.BlockSpec((None, None, queries, key_count), lambda h, s: (s, head, 0, 0)),
            pl.BlockSpec((None, None, queries, DH), lambda h, s: (s, head, 0, 0)),
            by_head(seg),
            by_head(seg),
            by_head(seg),
            by_head(seg),
            by_head(rows),
            by_head(rows),
            pl.BlockSpec((key_count, DH), lambda h, s: (0, head)),
        ],
        out_specs=[
            by_row(),
            by_place(),
            by_place(),
            by_row(),
            by_row(),
            pl.BlockSpec((None, DH, key_count), lambda h, s: (h, 0, 0)),
            pl.BlockSpec((None, 8, DH), lambda h, s: (h, 0, 0)),
        ],
        scratch_shapes=[
            pltpu.VMEM((key_count, DH), BF16),
            pltpu.VMEM((key_count, DH), BF16),
            pltpu.VMEM((queries, DH), BF16),
            pltpu.VMEM((BLOCK, key_count), F32),
            pltpu.VMEM((BLOCK, key_count), F32),
            pltpu.VMEM((BLOCK, key_count), BF16),
            pltpu.VMEM((BLOCK, key_count), BF16),
            pltpu.VMEM((DH, key_count), F32),
            pltpu.VMEM((DH, key_count), F32),
        ],
    )
    return pl.pallas_call(
        functools.partial(pull_kernel, cuts),
        grid_spec=grid_spec,
        out_shape=[
            jax.ShapeDtypeStruct((group, queries, DH), BF16),
            jax.ShapeDtypeStruct((group, DH, key_count), BF16),
            jax.ShapeDtypeStruct((group, DH, key_count), BF16),
            jax.ShapeDtypeStruct((group, queries, DH), BF16),
            jax.ShapeDtypeStruct((group, queries, DH), BF16),
            jax.ShapeDtypeStruct((1, DH, key_count), F32),
            jax.ShapeDtypeStruct((1, 8, DH), F32),
        ],
        compiler_params=pltpu.CompilerParams(
            dimension_semantics=("arbitrary", "arbitrary"), vmem_limit_bytes=VMEM_LIMIT
        ),
        cost_estimate=cost(39),
        name="pull",
    )(weights, inverse, attended, out_grad, content_q, position_q, keys, values, table_rev)


def project_kernel(
    cuts, rows_ref, gain_ref, shift_ref, w_ref, old_ref, mem_ref, seg_ref, q_ref, k_ref, v_ref, normed
):
    rows, width = rows_ref.shape
    cols = k_ref.shape[1]
    step = 32
    for low in range(0, rows, step):
        wide = rows_ref[low : low + step, :].astype(F32)
        centred = wide - jnp.mean(wide, axis=1, keepdims=True)
        rate = lax.rsqrt(jnp.mean(centred * centred, axis=1, keepdims=True) + EPSILON)
        normed[low : low + step, :] = (centred * rate * gain_ref[...] + shift_ref[...]).astype(BF16)
    cut = cuts[0] + cuts[1]
    old_ref[...] = normed[: cuts[0], :]
    mem_ref[...] = normed[cuts[0] : cut, :]
    seg_ref[...] = normed[cut:, :]
    q_ref[...] = mm(normed[cut:, :], w_ref[:, :cols], NN)
    k_ref[...] = mm(normed[...], w_ref[:, cols : 2 * cols], NN).astype(BF16)
    v_ref[...] = mm(normed[...], w_ref[:, 2 * cols : 3 * cols], NN).astype(BF16)


def project(rows_all, gain, shift, columns, cuts):
    parts, group, each, width = rows_all.shape
    cols = columns.shape[1] // 4
    block = lambda size, wide: pl.BlockSpec((None, None, size, wide), lambda p, s: (p, s, 0, 0))
    placed = lambda size: pl.BlockSpec((None, size, width), lambda p, s: (s, p, 0))
    whole = lambda *shape: pl.BlockSpec(shape, lambda p, s: (0,) * len(shape))
    shape = lambda size, kind: jax.ShapeDtypeStruct((parts, group, size, cols), kind)
    return pl.pallas_call(
        functools.partial(project_kernel, cuts),
        grid_spec=pl.GridSpec(
            grid=(parts, group),
            in_specs=[
                block(each, width),
                whole(1, width),
                whole(1, width),
                whole(width, 4 * cols),
            ],
            out_specs=[placed(size) for size in cuts]
            + [block(cuts[2], cols), block(each, cols), block(each, cols)],
            scratch_shapes=[pltpu.VMEM((each, width), BF16)],
        ),
        out_shape=[jax.ShapeDtypeStruct((group, parts * size, width), BF16) for size in cuts]
        + [shape(cuts[2], F32), shape(each, BF16), shape(each, BF16)],
        compiler_params=pltpu.CompilerParams(
            dimension_semantics=("arbitrary", "arbitrary"), vmem_limit_bytes=VMEM_LIMIT
        ),
        cost_estimate=cost(17),
        name="project",
    )(rows_all, gain, shift, columns)


def gelu_both(x):
    near = jnp.abs(x)
    t = 1.0 / (1.0 + (0.3275911 * math.sqrt(0.5)) * near)
    bell = jnp.exp2((x * x) * (-0.5 * LOG2E))
    tail = 0.5 * 1.061405429
    for factor in (-1.453152027, 1.421413741, -0.284496736, 0.254829592):
        tail = tail * t + 0.5 * factor
    tail = tail * t * bell
    below = jnp.where(x < 0.0, tail, 1.0 - tail)
    return x * below, below + x * bell * (1.0 / math.sqrt(2.0 * math.pi))


def forward_back_kernel(
    last, parts, pair, n_ref, c_ref, *rest,
):
    up_refs, down_refs, shift_ref = rest[:parts], rest[parts : parts + pair], rest[parts + pair]
    rest = rest[parts + pair + 1 :]
    if last:
        part_in, grad_in, part_out, part_far, grad_out, grad_far, late_ref, sums_ref = rest[:8]
        pre, slope, hidden, act, up_out, down_out, sems, part_ref, grad_ref = rest[8:]
    else:
        part_ref, grad_ref, late_ref, sums_ref = rest[:4]
        pre, slope, hidden, act, up_out, down_out, sems = rest[4:]
    tile = pl.program_id(0)
    tiles = pl.num_programs(0)
    cols, units = up_refs[0].shape
    unit_cols, width = down_refs[0].shape
    rows = n_ref.shape[0]
    slot = lax.rem(tile, 2)
    up_weight = jnp.concatenate([ref[...] for ref in up_refs], axis=0)
    down_weight = jnp.concatenate([ref[...] for ref in down_refs], axis=0)

    def copies(at, index):
        return (
            pltpu.make_async_copy(
                up_out.at[at],
                late_ref.at[:, pl.ds(0, cols), pl.ds(pl.multiple_of(index * units, units), units)],
                sems.at[at, 0],
            ),
            pltpu.make_async_copy(
                down_out.at[at],
                late_ref.at[pl.ds(index * pair, pair), pl.ds(cols, unit_cols), :],
                sems.at[at, 1],
            ),
        )

    @pl.when(tile == 0)
    def _():
        if last:
            part_ref[...] = part_in[...]
            grad_ref[...] = grad_in[...]
        else:
            part_ref[...] = jnp.zeros_like(part_ref)
            grad_ref[...] = jnp.zeros_like(grad_ref)

    chunk = 288 if rows % 288 == 0 else rows
    for base in range(0, rows, chunk):
        at = slice(base, base + chunk)
        pre[at, :] = mm(n_ref[at, :], up_weight, NN)
        slope[at, :] = mm(c_ref[at, :], down_weight, NT)
        for low in range(base, base + chunk, 16):
            some = slice(low, low + 16)
            value, change = gelu_both(pre[some, :] + shift_ref[...])
            hidden[some, :] = value.astype(BF16)
            act[some, :] = (change * slope[some, :]).astype(BF16)
        part_ref[at, :] += mm(hidden[at, :], down_weight, NN)
        grad_ref[at, :] += mm(act[at, :], up_weight, NT)
    sums_ref[...] = jnp.sum(act[...].astype(F32), axis=0, keepdims=True)

    @pl.when(tile >= 2)
    def _():
        for copy in copies(slot, tile - 2):
            copy.wait()

    up_out[slot] = mm(n_ref[...], act[...], TN).astype(BF16).reshape(parts, cols, units)
    down_out[slot] = mm(hidden[...], c_ref[...], TN).astype(BF16).reshape(pair, unit_cols, width)
    for copy in copies(slot, tile):
        copy.start()

    @pl.when(tile == tiles - 1)
    def _():
        if last:
            part_out[...] = part_ref[: rows // 2, :]
            part_far[...] = part_ref[rows // 2 :, :].astype(BF16)
            grad_out[...] = grad_ref[: rows // 2, :]
            grad_far[...] = grad_ref[rows // 2 :, :].astype(BF16)
        for copy in (copies(1 - slot, tile - 1) if parts > pair else ()) + copies(slot, tile):
            copy.wait()


def forward_back(normed, cot, gathered, shift, carry):
    parts, _, width = gathered.shape
    rows = normed.shape[0]
    cols = width // parts
    unit_cols = shift.shape[1] // parts
    pair = 2
    units = pair * unit_cols
    last = len(carry) > 0
    one = pl.Buffered(1)
    whole = lambda *shape: pl.BlockSpec(shape, lambda t: (0,) * len(shape), pipeline_mode=one)
    up = lambda p: pl.BlockSpec((None, cols, units), lambda t: (p, 0, t))
    down = lambda i: pl.BlockSpec(
        (None, unit_cols, width), lambda t: (t * pair + i, cols // unit_cols, 0)
    )
    if last:
        sums = [((rows // 2, width), F32), ((rows // 2, width), BF16)] * 2
    else:
        sums = [((rows, width), F32)] * 2
    return pl.pallas_call(
        functools.partial(forward_back_kernel, last, parts, pair),
        grid_spec=pl.GridSpec(
            grid=(parts // pair,),
            in_specs=[
                whole(rows, width),
                whole(rows, width),
            ]
            + [up(p) for p in range(parts)]
            + [down(i) for i in range(pair)]
            + [pl.BlockSpec((1, units), lambda t: (0, t))]
            + [whole(rows, width) for _ in carry],
            out_specs=[whole(*shape) for shape, _ in sums]
            + [
                pl.BlockSpec(memory_space=pl.ANY),
                pl.BlockSpec((1, units), lambda t: (0, t)),
            ],
            scratch_shapes=[
                pltpu.VMEM((rows, units), F32),
                pltpu.VMEM((rows, units), F32),
                pltpu.VMEM((rows, units), BF16),
                pltpu.VMEM((rows, units), BF16),
                pltpu.VMEM((2, parts, cols, units), BF16),
                pltpu.VMEM((2, pair, unit_cols, width), BF16),
                pltpu.SemaphoreType.DMA((2, 2)),
            ]
            + [pltpu.VMEM((rows, width), F32) for _ in carry],
        ),
        out_shape=[jax.ShapeDtypeStruct(shape, kind) for shape, kind in sums]
        + [
            jax.ShapeDtypeStruct((parts, cols + unit_cols, width), BF16),
            jax.ShapeDtypeStruct((1, parts * unit_cols), F32),
        ],
        compiler_params=pltpu.CompilerParams(
            dimension_semantics=("arbitrary",), vmem_limit_bytes=VMEM_LIMIT
        ),
        cost_estimate=cost(29),
        name="forward_back",
    )(normed, cot, *[gathered] * (parts + pair), shift, *carry)


def leave_kernel(a_ref, s_ref, w_ref, shift_ref, gain_ref, bias_ref, flat_ref, m_ref, n_ref):
    parts = a_ref.shape[0]
    flat_ref[...] = jnp.concatenate([a_ref[part] for part in range(parts)], axis=1)
    m_ref[...] = s_ref[...].astype(F32) + (mm(flat_ref[...], w_ref[...], NN) + shift_ref[...])
    step = 16
    for low in range(0, m_ref.shape[0], step):
        unit, _ = standardise(m_ref[low : low + step, :])
        n_ref[low : low + step, :] = (unit * gain_ref[...] + bias_ref[...]).astype(BF16)


def leave(mixed_heads, segment, base, weight, shift, gain, bias):
    parts, group, seg, cols = mixed_heads.shape
    width = parts * cols
    rows = lambda: pl.BlockSpec((None, seg, width), lambda s: (s, 0, 0))
    vector = lambda: pl.BlockSpec((1, width), lambda s: (0, 0))
    shape = lambda kind: jax.ShapeDtypeStruct((group, seg, width), kind)
    return pl.pallas_call(
        leave_kernel,
        grid_spec=pl.GridSpec(
            grid=(group,),
            in_specs=[
                pl.BlockSpec((parts, None, seg, cols), lambda s: (0, s, 0, 0)),
                pl.BlockSpec((None, seg, width), lambda s: (s + base, 0, 0)),
                pl.BlockSpec((width, width), lambda s: (0, 0)),
                vector(),
                vector(),
                vector(),
            ],
            out_specs=[rows(), rows(), rows()],
        ),
        out_shape=[shape(BF16), shape(F32), shape(BF16)],
        compiler_params=pltpu.CompilerParams(vmem_limit_bytes=VMEM_LIMIT),
        cost_estimate=cost(6),
        name="leave",
    )(mixed_heads, segment, weight, shift, gain, bias)


def enter_kernel(
    m_ref, g_ref, far_ref, c_ref, w_ref, gain_ref, mg_ref, b_ref, a_ref, sums_ref
):
    @pl.when(pl.program_id(0) == 0)
    def _():
        sums_ref[...] = jnp.zeros_like(sums_ref)

    parts = a_ref.shape[0]
    rows, width = m_ref.shape
    step = 16
    total = [jnp.zeros((1, width), F32) for _ in range(4)]
    for low in range(0, rows, step):
        at = slice(low, low + step)
        unit, rate = standardise(m_ref[at, :])
        grad = g_ref[at, :] + far_ref[at, :].astype(F32)
        cot = c_ref[at, :].astype(F32)
        middle_grad = cot + standardise_back(unit, rate, grad, gain_ref[...])
        branch = middle_grad.astype(BF16)
        mg_ref[at, :] = middle_grad
        b_ref[at, :] = branch
        for i, value in enumerate((branch.astype(F32), grad * unit, grad, cot)):
            total[i] = total[i] + jnp.sum(value, axis=0, keepdims=True)
    sums_ref[...] += jnp.concatenate(total + [jnp.zeros((4, width), F32)], axis=0)
    for part in range(parts):
        low = part * a_ref.shape[2]
        weight = w_ref[low : low + a_ref.shape[2], :]
        a_ref[part] = mm(b_ref[...], weight, NT).astype(BF16)


def enter(middle, grad, far, cot, base, weight, gain, parts):
    group, seg, width = middle.shape
    cols = width // parts
    rows = lambda: pl.BlockSpec((None, seg, width), lambda s: (s, 0, 0))
    later = lambda: pl.BlockSpec((None, seg, width), lambda s: (s + base, 0, 0))
    shape = lambda kind: jax.ShapeDtypeStruct((group, seg, width), kind)
    return pl.pallas_call(
        enter_kernel,
        grid_spec=pl.GridSpec(
            grid=(group,),
            in_specs=[
                rows(),
                later(),
                later(),
                later(),
                pl.BlockSpec((width, width), lambda s: (0, 0)),
                pl.BlockSpec((1, width), lambda s: (0, 0)),
            ],
            out_specs=[
                rows(),
                rows(),
                pl.BlockSpec((parts, None, seg, cols), lambda s: (0, s, 0, 0)),
                pl.BlockSpec((8, width), lambda s: (0, 0)),
            ],
        ),
        out_shape=[
            shape(F32),
            shape(BF16),
            jax.ShapeDtypeStruct((parts, group, seg, cols), BF16),
            jax.ShapeDtypeStruct((8, width), F32),
        ],
        compiler_params=pltpu.CompilerParams(
            dimension_semantics=("arbitrary",), vmem_limit_bytes=VMEM_LIMIT
        ),
        cost_estimate=cost(7),
        name="enter",
    )(middle, grad, far, cot, weight, gain)


def compress_kernel(low, rows_ref, w_ref, shift_ref, out_ref, wide):
    count = out_ref.shape[0]
    cols = out_ref.shape[1]
    blocks = wide.shape[0]
    for at in range(blocks):
        wide[at] = rows_ref[low : low + 3 * count, at * LANES : (at + 1) * LANES].astype(F32)
    total = jnp.broadcast_to(shift_ref[...], (count, cols))
    for k in range(3):
        every = jnp.concatenate(
            [wide[at, pl.ds(k, count, stride=3), :] for at in range(blocks)], axis=1
        ).astype(BF16)
        total = total + mm(every, w_ref[:, k * cols : (k + 1) * cols], NN)
    out_ref[...] = total.astype(BF16)


def compress(rows_all, columns, shift, low, count):
    parts, group, each, width = rows_all.shape
    cols = columns.shape[1] // 3
    return pl.pallas_call(
        functools.partial(compress_kernel, low),
        grid_spec=pl.GridSpec(
            grid=(parts, group),
            in_specs=[
                pl.BlockSpec((None, None, each, width), lambda p, s: (p, s, 0, 0)),
                pl.BlockSpec((width, 3 * cols), lambda p, s: (0, 0)),
                pl.BlockSpec((1, cols), lambda p, s: (0, 0)),
            ],
            out_specs=pl.BlockSpec((None, None, count, cols), lambda p, s: (p, s, 0, 0)),
            scratch_shapes=[pltpu.VMEM((width // LANES, 3 * count, LANES), F32)],
        ),
        out_shape=jax.ShapeDtypeStruct((parts, group, count, cols), BF16),
        compiler_params=pltpu.CompilerParams(
            dimension_semantics=("arbitrary", "arbitrary"), vmem_limit_bytes=VMEM_LIMIT
        ),
        cost_estimate=cost(6.5),
        name="compress",
    )(rows_all, columns, shift)


def lay_out_kernel(
    parts, unit_cols, core_ref, a_ref, b_ref, c_ref, d_ref, up_ref, down_ref
):
    flipped = core_ref[0] == 1
    for half, (mine_ref, far_ref) in enumerate(((a_ref, c_ref), (b_ref, d_ref))):
        mine, far = mine_ref[...].astype(F32), far_ref[...].astype(F32)
        for core, value in enumerate(
            (jnp.where(flipped, far, mine), jnp.where(flipped, mine, far))
        ):
            for part in range(parts):
                at = ((part * 2 + core) * 2 + half) * unit_cols
                up_ref[:, at : at + unit_cols] = value[
                    0, :, part * unit_cols : (part + 1) * unit_cols
                ]
            down_ref[2 * core + half] = value[1]


def lay_out(core, mine, far, parts):
    _, rows, width = mine[0].shape
    step = rows // 4 if rows % 64 == 0 else rows
    half = lambda: pl.BlockSpec((2, step, width), lambda r, *_: (0, r, 0))
    return pl.pallas_call(
        functools.partial(lay_out_kernel, parts, rows),
        grid_spec=pltpu.PrefetchScalarGridSpec(
            num_scalar_prefetch=1,
            grid=(rows // step,),
            in_specs=[half(), half(), half(), half()],
            out_specs=[
                pl.BlockSpec((step, 4 * width), lambda r, *_: (r, 0)),
                pl.BlockSpec((4, step, width), lambda r, *_: (0, r, 0)),
            ],
        ),
        out_shape=[
            jax.ShapeDtypeStruct((rows, 4 * width), F32),
            jax.ShapeDtypeStruct((4, rows, width), F32),
        ],
        compiler_params=pltpu.CompilerParams(vmem_limit_bytes=VMEM_LIMIT),
        cost_estimate=cost(4),
        name="lay_out",
    )(core.reshape(1), *mine, *far)


def lay_squares_kernel(in_ref, *out_refs):
    parts = in_ref.shape[0]
    cols = in_ref.shape[2] // len(out_refs)
    for at, out_ref in enumerate(out_refs):
        for part in range(parts):
            out_ref[:, part * cols : (part + 1) * cols] = in_ref[
                part, :, at * cols : (at + 1) * cols
            ].astype(F32)


def lay_squares(summed, rows):
    parts, _, wide = summed.shape
    width = parts * wide // 4
    step = rows // 2
    return pl.pallas_call(
        lay_squares_kernel,
        grid_spec=pl.GridSpec(
            grid=(2,),
            in_specs=[pl.BlockSpec((parts, step, wide), lambda i: (0, i, 0))],
            out_specs=[pl.BlockSpec((step, width), lambda i: (i, 0)) for _ in range(4)],
        ),
        out_shape=[jax.ShapeDtypeStruct((rows, width), F32) for _ in range(4)],
        compiler_params=pltpu.CompilerParams(vmem_limit_bytes=VMEM_LIMIT),
        cost_estimate=cost(2.5),
        name="lay_squares",
    )(summed)


def settle_kernel(heads, me_ref, old_ref, mem_ref, seg_ref, *rest):
    q_refs, k_refs, v_refs, ks_refs, vs_refs, dt_refs, sums_refs = (
        rest[i * heads : (i + 1) * heads] for i in range(7)
    )
    w_ref, table_ref, gain_ref, shift_ref, small_ref, part_ref, out_ref, total = rest[7 * heads :]
    stream = pl.program_id(0)
    parts, rows, wide = out_ref.shape
    cols = wide // 4
    width = parts * cols

    @pl.when(stream == 0)
    def _():
        total[...] = jnp.zeros_like(total)

    low = old_ref.shape[0]
    high = low + mem_ref.shape[0]
    pair = lambda first, last: [ref[:, first:last] for ref in (*k_refs, *v_refs)]
    total[...] += mm(
        jnp.concatenate([ref[...].T for ref in q_refs] + pair(high, high + seg_ref.shape[0]), axis=0),
        seg_ref[...],
        NN,
    )
    total[cols:, :] += mm(jnp.concatenate(pair(low, high), axis=0), mem_ref[...], NN)
    total[cols:, :] += mm(jnp.concatenate(pair(0, low), axis=0), old_ref[...], NN)
    three = jnp.concatenate([ref[...] for ref in (*q_refs, *ks_refs, *vs_refs)], axis=1)
    part = mm(three, w_ref[:, : 3 * cols], NT).astype(BF16)
    part_ref[...] = part.reshape(part_ref.shape)

    @pl.when(stream == pl.num_programs(0) - 1)
    def _():
        places = jnp.concatenate([ref[0].astype(BF16) for ref in dt_refs], axis=0)
        rel = mm(places, table_ref[...], NN)
        line = lambda row: jnp.concatenate(
            [ref[0, row : row + 1, :] for ref in sums_refs], axis=1
        )
        row_sums = jnp.concatenate([line(2), line(3), line(4)], axis=1)
        pieces, rest = [], row_sums
        for _ in range(3):
            pieces.append(rest.astype(BF16))
            rest = rest - pieces[-1].astype(F32)
        pieces = jnp.concatenate(pieces + [jnp.zeros((13, 3 * cols), BF16)], axis=0)
        shift_grad = jnp.sum(mm(pieces, w_ref[:, : 3 * cols], NT), axis=0, keepdims=True)
        weight = w_ref[:, : 3 * cols].astype(F32)
        along = jnp.sum(weight.T * total[...], axis=0, keepdims=True)
        gain_grad = (along - shift_ref[...] * shift_grad) / gain_ref[...]
        for at in range(parts):
            low, high = at * cols, (at + 1) * cols
            out_ref[at, :cols, : 3 * cols] = total[:, low:high].T.astype(BF16)
            out_ref[at, :cols, 3 * cols :] = rel[:, low:high].T.astype(BF16)
            mine = (me_ref[0] == at).astype(F32)
            none = jnp.zeros((1, 2 * cols), F32)
            first = jnp.concatenate([gain_grad[:, low:high], shift_grad[:, low:high], none], axis=1)
            second = jnp.concatenate([none, mine * line(0), mine * line(1)], axis=1)
            added = jnp.concatenate([first, second, jnp.zeros((14, wide), F32)], axis=0)
            out_ref[at, cols:, :] = (small_ref[at] + added).astype(BF16)


def settle(me, normed, grads, columns, table, gain, shift, small, parts):
    group, queries, width = normed[2].shape
    cols = width // parts
    wide = 4 * cols
    by_kind = list(zip(*grads))
    block = lambda array: pl.BlockSpec((None, *array.shape[1:]), lambda s, *_: (s, 0, 0))
    whole = lambda *shape: pl.BlockSpec(
        shape, lambda s, *_: (0,) * len(shape), pipeline_mode=pl.Buffered(1)
    )
    return pl.pallas_call(
        functools.partial(settle_kernel, len(grads)),
        grid_spec=pltpu.PrefetchScalarGridSpec(
            num_scalar_prefetch=1,
            grid=(group,),
            in_specs=[block(rows) for rows in normed]
            + [block(each) for kind in by_kind[:5] for each in kind]
            + [whole(*each.shape) for kind in by_kind[5:] for each in kind]
            + [
                whole(*columns.shape),
                whole(*table.shape),
                whole(1, width),
                whole(1, width),
                whole(*small.shape),
            ],
            out_specs=[
                pl.BlockSpec((parts, None, queries // parts, width), lambda s, *_: (0, s, 0, 0)),
                whole(parts, cols + 16, wide),
            ],
            scratch_shapes=[pltpu.VMEM((3 * cols, width), F32)],
        ),
        out_shape=[
            jax.ShapeDtypeStruct((parts, group, queries // parts, width), BF16),
            jax.ShapeDtypeStruct((parts, cols + 16, wide), BF16),
        ],
        compiler_params=pltpu.CompilerParams(
            dimension_semantics=("arbitrary",), vmem_limit_bytes=VMEM_LIMIT
        ),
        cost_estimate=cost(14),
        name="settle",
    )(
        me.reshape(1), *normed, *[each for kind in by_kind for each in kind], columns, table, gain, shift,
        small,
    )


def standardise(rows):
    mean = jnp.mean(rows, axis=-1, keepdims=True)
    centred = rows - mean
    rate = lax.rsqrt(jnp.mean(centred * centred, axis=-1, keepdims=True) + EPSILON)
    return centred * rate, rate


def standardise_back(unit, rate, grad, gain):
    scaled = grad * gain
    mean = jnp.mean(scaled, axis=-1, keepdims=True)
    along = jnp.mean(scaled * unit, axis=-1, keepdims=True)
    return rate * (scaled - mean - unit * along)


def sinusoid_reversed(rows, width):
    positions = (rows - 1 - jnp.arange(rows, dtype=jnp.int32)).astype(F32)[:, None]
    frequency = jnp.exp(
        jnp.arange(width // 2, dtype=F32) * (-2.0 * math.log(10000.0) / width)
    )
    angles = positions * frequency[None, :]
    return jnp.concatenate([jnp.sin(angles), jnp.cos(angles)], axis=1).astype(BF16)


def dot(left, right):
    return mm(left, right, NN)


def swap(value):
    return lax.ppermute(value, "core", [(0, 1), (1, 0)])


def exchange(blocks, name, axis=0):
    count = lax.axis_size(name)
    me = lax.axis_index(name)
    block = lambda at: lax.dynamic_index_in_dim(blocks, at, axis, keepdims=False)
    return [block(me)] + [
        lax.ppermute(block(me ^ apart), name, [(i, i ^ apart) for i in range(count)])
        for apart in range(1, count)
    ]


def collect(block, name):
    count = lax.axis_size(name)
    me = lax.axis_index(name)
    found = jnp.stack(
        [block]
        + [
            lax.ppermute(block, name, [(i, i ^ apart) for i in range(count)])
            for apart in range(1, count)
        ]
    )
    return jnp.stack(
        [lax.dynamic_index_in_dim(found, me ^ i, 0, keepdims=False) for i in range(count)]
    )


def add_up(arrays, kind=BF16):
    total = arrays[0].astype(F32)
    for array in arrays[1:]:
        total = total + array.astype(F32)
    return total.astype(kind)


def body(
    segment, memory, compressed, eob, reset, ln1_gain, ln1_bias, w_query, w_key, w_value,
    w_out, out_bias, w_rel, bias_content, bias_position, ln2_gain, ln2_bias, w_up, up_bias,
    w_down, down_bias, conv_weight, conv_bias, cotangent,
):
    parts = lax.axis_size("seq")
    layers = lax.axis_size("z")
    core = lax.axis_index("core")
    me = lax.axis_index("seq")
    group, seg, width = segment.shape
    mem, old = memory.shape[1], compressed.shape[1]
    cuts = (old, mem, seg)
    each = old + mem + seg
    keys_in_all = parts * each
    cols = width // parts
    wide = 4 * cols
    own = group * seg
    unit_cols = w_up.shape[1] // (4 * parts)
    barrier = lax.optimization_barrier

    def by_columns(matrices):
        count = matrices.shape[0]
        sent = matrices.reshape(count, cols, parts, cols).transpose(2, 1, 0, 3)
        return sent.reshape(parts, cols, count * cols)

    up_bias_own = lax.dynamic_slice_in_dim(up_bias, core * 2 * unit_cols, 2 * unit_cols, 0)
    vectors = jnp.concatenate(
        [ln1_gain, ln1_bias, out_bias, ln2_gain, ln2_bias, down_bias, up_bias_own]
    )
    vectors = jnp.pad(vectors.reshape(2, wide), ((0, 14), (0, 0)))
    half = cols // 2
    sent = by_columns(jnp.concatenate([jnp.stack([w_query, w_key, w_value, w_rel]), conv_weight]))
    sent = lax.dynamic_slice_in_dim(sent, core * half, half, 1)
    out_half = lax.dynamic_slice_in_dim(w_out, core * half, half, 0)
    sent = jnp.concatenate([sent, jnp.broadcast_to(out_half, (parts, half, width))], axis=2)
    vectors = jnp.pad(vectors, ((0, 0), (0, 3 * cols + width)))
    sent = jnp.concatenate([sent, jnp.broadcast_to(vectors, (parts, *vectors.shape))], axis=1)
    got = lax.all_to_all(sent, "seq", 0, 0, tiled=True)
    spans = [(0, group)]
    local = [
        jnp.concatenate([compressed[low:high], memory[low:high], segment[low:high]], axis=1)
        for low, high in spans
    ]
    rows_all = [lax.all_gather(local[0], "seq")]
    mine = got[:, :half]
    far = swap(mine)
    columns = jnp.stack(
        [jnp.where(core == 0, mine, far), jnp.where(core == 0, far, mine)], axis=1
    ).reshape(width, 7 * cols + width)
    columns, conv_columns, out_full = (
        columns[:, :wide],
        columns[:, wide : 7 * cols],
        columns[:, 7 * cols :],
    )
    vectors = got[:, half : half + 2, :wide].reshape(parts, 2 * wide).astype(F32)
    gain_one, shift_one, out_shift, gain_two, shift_two, down_shift = (
        vectors[:, cols * i : cols * (i + 1)].reshape(1, width) for i in range(6)
    )
    up_shift = vectors[:, 6 * cols :].reshape(parts, 2, unit_cols).transpose(1, 0, 2)
    up_shift = up_shift.reshape(2, 1, parts * unit_cols)
    up_quarters = lax.dynamic_slice_in_dim(
        w_up.reshape(cols, parts, 2, 2, unit_cols), core, 1, 2
    ).reshape(cols, parts, 2, unit_cols)
    up_quarters = [up_quarters[:, :, i].reshape(cols, width) for i in range(2)]
    down_half = lax.dynamic_slice_in_dim(w_down, core * 2 * unit_cols, 2 * unit_cols, 0)
    down_quarters = [down_half[unit_cols * i : unit_cols * (i + 1)] for i in range(2)]
    first = jnp.concatenate([up_quarters[0], down_quarters[0]], axis=0)
    second = jnp.concatenate([up_quarters[1], down_quarters[1]], axis=0)
    cot_own = cotangent.reshape(own, width)
    cot_both = jnp.concatenate([cot_own, swap(cot_own)], axis=0)

    table_rev = sinusoid_reversed(keys_in_all, width)
    proj_rev = dot(table_rev, columns[:, 3 * cols :]).astype(BF16)
    index = jnp.arange(eob.shape[1], dtype=jnp.int32)[None, :]
    opens = jnp.pad(eob, ((0, 0), (1, 0)))[:, :-1] == 1
    start = lax.cummax(jnp.where(opens, index, 0), axis=1)
    shade = jnp.where((start == 0) & (reset[:, None] == 0), 0.0, MASKED)
    info = jnp.stack([start.astype(F32), shade], axis=2)
    info = jnp.pad(info, ((0, 0), (0, 0), (0, LANES - 2)))
    rows_all[0], proj_rev, info, cot_both, table_rev, columns, conv_columns, out_full, *local = barrier(
        (rows_all[0], proj_rev, info, cot_both, table_rev, columns, conv_columns, out_full, *local)
    )
    rows_all = [rows_all[0]] + [lax.all_gather(rows, "seq") for rows in local[1:]]

    kept, heads = [], []
    for batch, (low, high) in enumerate(spans):
        if batch == len(spans) - 1:
            rows_all[batch], first, *heads = barrier((rows_all[batch], first, *heads))
            first = lax.all_gather(first, "seq")
        *normed, query, keys, values = project(rows_all[batch], gain_one, shift_one, columns, cuts)
        second, query = barrier((second, query))
        second = lax.all_gather(second, "seq")
        weights, inverse, mixed_heads, content_q, position_q = attend(
            query,
            bias_content.astype(F32).reshape(1, cols),
            bias_position.astype(F32).reshape(1, cols),
            keys,
            values,
            proj_rev,
            info[low:high],
            cuts,
        )
        kept.append((weights, inverse, mixed_heads, content_q, position_q, keys, values))
        heads.append(lax.all_to_all(mixed_heads, "seq", 0, 0, tiled=True))

    mixed_heads, conv_columns = barrier((mixed_heads, conv_columns))
    packed = compress(
        rows_all[0], conv_columns, conv_bias.astype(F32).reshape(1, cols), old, mem // 3
    )
    packed, *heads = barrier((packed, *heads))

    attended, middle, normed_two = [], [], []
    for (low, high), batch in zip(spans, heads):
        one, two, three = leave(batch, segment, low, out_full, out_shift, gain_two, shift_two)
        attended.append(one.reshape(-1, width))
        middle.append(two)
        normed_two.append(three.reshape(-1, width))
    both = jnp.concatenate(normed_two + [swap(rows) for rows in normed_two], axis=0)
    part, part_grad, late_one, unit_one = forward_back(both, cot_both, first, up_shift[0], ())
    late_one = lax.psum_scatter(
        late_one.reshape(-1, width), "seq", scatter_dimension=0, tiled=True
    )
    part, part_far, part_grad, grad_far, late_two, unit_two = forward_back(
        both, cot_both, second, up_shift[1], (part, part_grad)
    )
    grad_far = swap(grad_far)
    by_stream = lambda rows: rows.reshape(group, seg, width)
    middle_grad, branch_grad, head_grad, sums_two = [], [], [], 0.0
    for (low, high), batch in zip(spans, middle):
        one, two, three, four = enter(
            batch, by_stream(part_grad), by_stream(grad_far), cotangent, low, out_full, gain_two, parts
        )
        middle_grad.append(one)
        branch_grad.append(two.reshape(-1, width))
        three, part_grad = barrier((three, part_grad))
        head_grad.append(lax.all_to_all(three, "seq", 0, 0, tiled=True))
        sums_two = sums_two + four
    result = part + swap(part_far).astype(F32) + down_shift
    output = (jnp.concatenate(middle).reshape(own, width) + result).astype(BF16)
    output = output.reshape(group, seg, width)

    out_shift_grad, gain_two_grad, shift_two_grad, down_shift_grad = (
        sums_two[i].reshape(parts, cols) for i in range(4)
    )
    none = jnp.zeros((parts, 2 * cols), F32)
    unit_sums = jnp.stack(
        [unit_one.reshape(parts, unit_cols), unit_two.reshape(parts, unit_cols)], axis=1
    ).reshape(parts, 2 * unit_cols)
    small = jnp.stack(
        [
            jnp.concatenate([none, out_shift_grad, gain_two_grad], axis=1),
            jnp.concatenate([shift_two_grad, down_shift_grad, none], axis=1),
            jnp.concatenate(
                [jnp.where(core == 0, unit_sums, 0.0), jnp.where(core == 1, unit_sums, 0.0)], axis=1
            ),
        ],
        axis=1,
    )
    small = jnp.pad(small, ((0, 0), (0, 13), (0, 0)))
    weights, inverse, mixed_heads, content_q, position_q, keys, values = kept[0]
    out_grad = mm(jnp.concatenate(attended), jnp.concatenate(branch_grad), TN)
    out_grad = out_grad.astype(BF16).reshape(parts, cols, width)
    late_one, small, out_grad, late_two, output, head_grad = barrier(
        (late_one, small, out_grad, late_two, output, head_grad[0])
    )
    late_two = lax.psum_scatter(
        late_two.reshape(-1, width), "seq", scatter_dimension=0, tiled=True
    )
    late_one = exchange(late_one.reshape(layers, -1, width), "z")
    grads = []
    for head in range(cols // DH):
        grads.append(
            list(
                pull(
                    head, weights, inverse, mixed_heads, head_grad, content_q, position_q, keys,
                    values, proj_rev, cuts,
                )
            )
        )
        if head == 0:
            late_one, head_grad, grads[0][0] = barrier((late_one, head_grad, grads[0][0]))
            late_one = collect(add_up(late_one), "z")
    late_one, late_two, out_grad, grads[-1][0] = barrier(
        (late_one, late_two, out_grad, grads[-1][0])
    )
    late_two = exchange(late_two.reshape(layers, -1, width), "z")
    out_sent = lax.all_to_all(out_grad, "seq", 0, 0, tiled=True)
    seg_part, square_grads = settle(
        me, normed, grads, columns, table_rev, gain_one, shift_one, small, parts
    )
    late_two, out_sent, square_grads = barrier((late_two, out_sent, square_grads))
    summed = lax.all_to_all(square_grads, "seq", 0, 0, tiled=True)
    late_two = collect(add_up(late_two), "z")
    out_sent = jnp.sum(out_sent.astype(F32), axis=0).astype(BF16)
    late_two, out_sent, summed, seg_part = barrier((late_two, out_sent, summed, seg_part))
    squares = parts * (cols + 16)
    summed = jnp.concatenate([summed.reshape(squares, wide), out_sent.reshape(-1, wide)], axis=0)
    summed, packed = barrier((summed, packed))
    summed = lax.psum(summed, ("z", "core"))
    packed = jnp.stack(exchange(packed, "seq"))
    new_compressed = jnp.concatenate(
        [lax.dynamic_index_in_dim(packed, p ^ me, 0, keepdims=False) for p in range(parts)], axis=2
    )
    seg_grad = lax.all_to_all(seg_part, "seq", 0, 0, tiled=True).astype(F32)
    seg_grad = jnp.sum(seg_grad, axis=0).reshape(own, width)
    unit_seg, rate_seg = standardise(segment.reshape(own, width).astype(F32))
    rows_grad = standardise_back(unit_seg, rate_seg, seg_grad, gain_one)
    segment_grad = jnp.concatenate(middle_grad, axis=0) + by_stream(rows_grad)

    halves = [late_one.reshape(2, unit_cols, width), late_two.reshape(2, unit_cols, width)]
    up_w, down_w = lay_out(core, halves, [swap(rows) for rows in halves], parts)
    down_w = down_w.reshape(4 * unit_cols, width)
    summed, output, segment_grad, new_compressed, up_w, down_w = barrier(
        (summed, output, segment_grad, new_compressed, up_w, down_w)
    )
    out_w = summed[squares:].reshape(cols, width).astype(F32)
    summed = summed[:squares].reshape(parts, cols + 16, wide)
    query_w, key_w, value_w, rel_w = lay_squares(summed, cols)
    small = jnp.sum(summed[:, cols : cols + 3].astype(F32), axis=0)
    piece = lambda row, i: small[row, cols * i : cols * (i + 1)]
    return (
        output,
        segment_grad,
        piece(0, 0),
        piece(0, 1),
        query_w,
        key_w,
        value_w,
        out_w,
        piece(0, 2),
        rel_w,
        piece(1, 2),
        piece(1, 3),
        piece(0, 3),
        piece(1, 0),
        up_w,
        small[2],
        down_w,
        piece(1, 1),
        new_compressed,
    )


def solution(mesh):
    dp = mesh.shape["dp"]
    cores = jax.sharding.Mesh(
        mesh.devices.reshape(dp // 2, 2, mesh.shape["seq"]), ("z", "core", "seq")
    )
    rows = P(("z", "core"), "seq", None)
    shard, matrix = P("seq"), P("seq", None)
    return jax.shard_map(
        body,
        mesh=cores,
        in_specs=(
            rows, rows, rows, P(("z", "core"), None), P(("z", "core")), shard, shard, matrix,
            matrix, matrix, matrix, shard, matrix, shard, shard, shard, shard, matrix, shard,
            matrix, shard, P(None, "seq", None), shard, rows,
        ),
        out_specs=(
            rows, rows, shard, shard, matrix, matrix, matrix, matrix, shard, matrix, shard,
            shard, shard, shard, matrix, shard, matrix, shard, rows,
        ),
        check_vma=False,
    )
```

```python
import functools
import math

import jax
import jax.numpy as jnp
from jax import lax
from jax.experimental import pallas as pl
from jax.experimental.pallas import tpu as pltpu
from jax.sharding import PartitionSpec as P

HEADS = 8
DH = 128
EPSILON = 1e-05
MASKED = -1e30
LANES = 128
BLOCK = 256
CHUNK = 16
VMEM_LIMIT = 60 * 2**20
SCALE = 1.0 / math.sqrt(DH)
LOG2E = 1.4426950408889634
BF16 = jnp.bfloat16
F32 = jnp.float32


def cost(microseconds):
    return pl.CostEstimate(flops=int(microseconds * 1.15e7), bytes_accessed=0, transcendentals=0)


def mm(left, right, dims):
    return lax.dot_general(left, right, (dims, ((), ())), preferred_element_type=F32)


NN = ((1,), (0,))
NT = ((1,), (1,))
TN = ((0,), (0,))


def lean_left(block, first_row, fill_columns):
    columns = block.shape[1] // LANES
    far = BLOCK - 1 - first_row
    whole, part = far // LANES, far % LANES
    turned = [
        pltpu.roll(
            block[:, LANES * t : LANES * (t + 1)], LANES - part, 1, stride=1, stride_axis=0
        )
        for t in range(columns)
    ]
    rows = lax.broadcasted_iota(jnp.int32, (block.shape[0], LANES), 0)
    lanes = lax.broadcasted_iota(jnp.int32, (block.shape[0], LANES), 1)
    near = lanes - rows < LANES - part
    out = []
    for t in range(fill_columns):
        a = turned[(t + whole) % columns]
        b = turned[(t + whole + 1) % columns]
        out.append(jnp.where(near, a, b))
    return jnp.concatenate(out, axis=1)


def lean_right(block, first_row):
    columns = block.shape[1] // LANES
    whole, part = first_row // LANES, first_row % LANES
    turned = [
        pltpu.roll(block[:, LANES * t : LANES * (t + 1)], part, 1, stride=1, stride_axis=0)
        for t in range(columns)
    ]
    rows = lax.broadcasted_iota(jnp.int32, (block.shape[0], LANES), 0)
    lanes = lax.broadcasted_iota(jnp.int32, (block.shape[0], LANES), 1)
    wrapped = lanes - rows < part
    out = []
    for t in range(columns):
        a = turned[(t - whole) % columns]
        b = turned[(t - whole - 1) % columns]
        out.append(jnp.where(wrapped, b, a))
    return jnp.concatenate(out, axis=1)


def flip_matrix(kind):
    rows = lax.broadcasted_iota(jnp.int32, (BLOCK, BLOCK), 0)
    lanes = lax.broadcasted_iota(jnp.int32, (BLOCK, BLOCK), 1)
    return (rows + lanes == BLOCK - 1).astype(F32).astype(kind)


def in_place_order(parts_ref, out_ref, cuts):
    parts = parts_ref.shape[0]
    low, base = 0, 0
    for size in cuts:
        for part in range(parts):
            out_ref[base + part * size : base + (part + 1) * size, :] = parts_ref[
                part, low : low + size, :
            ]
        low += size
        base += parts * size


def attend_kernel(
    cuts, q_ref, cb_ref, pb_ref, k_ref, v_ref, t_ref, info_ref,
    e_ref, inv_ref, o_ref, cq_ref, pq_ref,
    keys, values, raw, lean, mix, tops, sums,
):
    parts, seg, _ = q_ref.shape
    queries = parts * seg
    old = parts * (cuts[0] + cuts[1])
    in_place_order(k_ref, keys, cuts)
    in_place_order(v_ref, values, cuts)
    q = q_ref[...].reshape(queries, DH)
    content_q = (q + cb_ref[...]).astype(BF16)
    position_q = (q + pb_ref[...]).astype(BF16)
    cq_ref[...] = content_q.reshape(parts, seg, DH)
    pq_ref[...] = position_q.reshape(parts, seg, DH)
    for block in range(queries // BLOCK):
        row0 = block * BLOCK
        width = old + row0 + BLOCK
        skip = queries - BLOCK - row0
        raw[:, :width] = mm(content_q[row0 : row0 + BLOCK], keys[:width, :], NT)
        lean[:, :width] = mm(position_q[row0 : row0 + BLOCK], t_ref[skip : skip + width, :], NT)
        for chunk in range(BLOCK // CHUNK):
            r0 = chunk * CHUNK
            rows = slice(r0, r0 + CHUNK)
            turned = lean_left(lean[rows, :width], r0, width // LANES)
            score = raw[rows, :width] + turned
            start = info_ref[row0 + r0 : row0 + r0 + CHUNK, 0:1].astype(jnp.int32)
            shade = info_ref[row0 + r0 : row0 + r0 + CHUNK, 1:2]
            past = score[:, :old] + shade
            place = lax.broadcasted_iota(jnp.int32, (CHUNK, row0 + BLOCK), 1)
            own = lax.broadcasted_iota(jnp.int32, (CHUNK, row0 + BLOCK), 0) + (row0 + r0)
            now = jnp.where((place <= own) & (place >= start), score[:, old:], MASKED)
            raw[rows, :old] = past
            raw[rows, old:width] = now
            top = past[:, :LANES]
            for low in range(LANES, old, LANES):
                top = jnp.maximum(top, past[:, low : low + LANES])
            for low in range(0, row0 + BLOCK, LANES):
                top = jnp.maximum(top, now[:, low : low + LANES])
            tops[rows, :] = top
        top = jnp.max(tops[...], axis=1, keepdims=True)
        tops[...] = jnp.broadcast_to(top, (BLOCK, LANES))
        for chunk in range(BLOCK // CHUNK):
            r0 = chunk * CHUNK
            rows = slice(r0, r0 + CHUNK)
            top = tops[rows, :]
            total = jnp.zeros((CHUNK, LANES), F32)
            for low in range(0, width, LANES):
                weight = jnp.exp2((raw[rows, low : low + LANES] - top) * (SCALE * LOG2E))
                total = total + weight
                e_ref[row0 + r0 : row0 + r0 + CHUNK, low : low + LANES] = weight.astype(BF16)
            sums[rows, :] = total
        total = jnp.sum(sums[...], axis=1, keepdims=True)
        inv_ref[row0 : row0 + BLOCK, :] = jnp.broadcast_to(1.0 / total, (BLOCK, DH))
        mix[row0 : row0 + BLOCK, :] = mm(
            e_ref[row0 : row0 + BLOCK, :width], values[:width, :], NN
        )
    o_ref[...] = (mix[...] * inv_ref[...]).astype(BF16).reshape(parts, seg, DH)


def attend(query, content_shift, position_shift, keys, values, table_rev, info, cuts):
    parts, group, seg, cols = query.shape
    rows = keys.shape[2]
    queries, key_count, heads = parts * seg, parts * rows, cols // DH
    by_head = lambda size: pl.BlockSpec((parts, None, size, DH), lambda s, h: (0, s, 0, h))
    grid_spec = pl.GridSpec(
        grid=(group, heads),
        in_specs=[
            by_head(seg),
            pl.BlockSpec((1, DH), lambda s, h: (0, h)),
            pl.BlockSpec((1, DH), lambda s, h: (0, h)),
            by_head(rows),
            by_head(rows),
            pl.BlockSpec((key_count, DH), lambda s, h: (0, h)),
            pl.BlockSpec((None, queries, LANES), lambda s, h: (s, 0, 0)),
        ],
        out_specs=[
            pl.BlockSpec((None, None, queries, key_count), lambda s, h: (s, h, 0, 0)),
            pl.BlockSpec((None, None, queries, DH), lambda s, h: (s, h, 0, 0)),
            by_head(seg),
            by_head(seg),
            by_head(seg),
        ],
        scratch_shapes=[
            pltpu.VMEM((key_count, DH), BF16),
            pltpu.VMEM((key_count, DH), BF16),
            pltpu.VMEM((BLOCK, key_count), F32),
            pltpu.VMEM((BLOCK, key_count), F32),
            pltpu.VMEM((queries, DH), F32),
            pltpu.VMEM((BLOCK, LANES), F32),
            pltpu.VMEM((BLOCK, LANES), F32),
        ],
    )
    small = jax.ShapeDtypeStruct((parts, group, seg, cols), BF16)
    return pl.pallas_call(
        functools.partial(attend_kernel, cuts),
        grid_spec=grid_spec,
        out_shape=[
            jax.ShapeDtypeStruct((group, heads, queries, key_count), BF16),
            jax.ShapeDtypeStruct((group, heads, queries, DH), F32),
            small,
            small,
            small,
        ],
        compiler_params=pltpu.CompilerParams(
            dimension_semantics=("arbitrary", "arbitrary"), vmem_limit_bytes=VMEM_LIMIT
        ),
        cost_estimate=cost(40),
        name="attend",
    )(query, content_shift, position_shift, keys, values, table_rev, info)


def pull_kernel(
    cuts, e_ref, inv_ref, o_ref, g_ref, cq_ref, pq_ref, k_ref, v_ref, t_ref,
    dq_ref, dk_ref, dv_ref, ks_ref, vs_ref, dt_ref, sums_ref,
    keys, values, grad, prob, part, score, lean, key_sum, value_sum,
):
    stream = pl.program_id(1)
    parts, seg, _ = g_ref.shape
    queries = parts * seg
    old = parts * (cuts[0] + cuts[1])
    in_place_order(k_ref, keys, cuts)
    in_place_order(v_ref, values, cuts)
    grad[...] = (g_ref[...].reshape(queries, DH).astype(F32) * inv_ref[...]).astype(BF16)
    attended = o_ref[...].reshape(queries, DH)
    content_q = cq_ref[...].reshape(queries, DH)
    position_q = pq_ref[...].reshape(queries, DH)

    @pl.when(stream == 0)
    def _():
        dt_ref[...] = jnp.zeros_like(dt_ref)
        sums_ref[...] = jnp.zeros_like(sums_ref)

    key_sum[...] = jnp.zeros_like(key_sum)
    value_sum[...] = jnp.zeros_like(value_sum)
    content_total = jnp.zeros((1, DH), F32)
    position_total = jnp.zeros((1, DH), F32)
    query_total = jnp.zeros((1, DH), F32)
    flip = flip_matrix(BF16)
    turn = lambda rows: mm(flip, rows, NN).astype(BF16)
    for block in range(queries // BLOCK):
        row0 = block * BLOCK
        width = old + row0 + BLOCK
        skip = queries - BLOCK - row0
        rows = slice(row0, row0 + BLOCK)
        grad_back = turn(grad[rows, :])
        dots_back = jnp.sum(
            grad_back.astype(F32) * turn(attended[rows]).astype(F32), axis=1, keepdims=True
        )
        content_back = turn(content_q[rows])
        position_back = turn(position_q[rows])
        prob[:, :width] = mm(grad_back, values[:width, :], NT)
        both = mm(jnp.concatenate([flip, grad[rows, :].T], axis=0), e_ref[rows, :width], NN)
        part[:, :width] = both[:BLOCK]
        value_sum[:, :width] += both[BLOCK:]
        for chunk in range(BLOCK // CHUNK):
            r0 = chunk * CHUNK
            mean = dots_back[r0 : r0 + CHUNK, 0:1]
            change = part[r0 : r0 + CHUNK, :width] * (prob[r0 : r0 + CHUNK, :width] - mean)
            score[r0 : r0 + CHUNK, :width] = change.astype(BF16)
            lean[r0 : r0 + CHUNK, :width] = lean_right(change, r0).astype(BF16)
        content_grad = (mm(score[:, :width], keys[:width, :], NN) * SCALE).astype(BF16).astype(F32)
        position_grad = (
            (mm(lean[:, :width], t_ref[skip : skip + width, :], NN) * SCALE)
            .astype(BF16)
            .astype(F32)
        )
        query_grad = turn((content_grad + position_grad).astype(BF16))
        content_total += jnp.sum(content_grad, axis=0, keepdims=True)
        position_total += jnp.sum(position_grad, axis=0, keepdims=True)
        query_total += jnp.sum(query_grad.astype(F32), axis=0, keepdims=True)
        dq_ref[rows, :] = query_grad
        key_sum[:, :width] += mm(content_back, score[:, :width], TN)
        dt_ref[:, skip : skip + width] += mm(position_back, lean[:, :width], TN) * SCALE
    key_cols = (key_sum[...] * SCALE).astype(BF16)
    value_cols = value_sum[...].astype(BF16)
    dk_ref[...] = key_cols
    dv_ref[...] = value_cols
    ks_ref[...] = (key_sum[:, old:] * SCALE).T.astype(BF16)
    vs_ref[...] = value_sum[:, old:].T.astype(BF16)
    ones = jnp.ones((8, key_cols.shape[1]), BF16)
    key_total = mm(ones, key_cols, NT)[0:1]
    value_total = mm(ones, value_cols, NT)[0:1]
    sums_ref[...] += jnp.concatenate(
        [
            content_total,
            position_total,
            query_total,
            key_total,
            value_total,
            jnp.zeros((3, DH), F32),
        ],
        axis=0,
    )


def pull(head, weights, inverse, attended, out_grad, content_q, position_q, keys, values, table_rev, cuts):
    parts, group, seg, cols = out_grad.shape
    rows = keys.shape[2]
    queries, key_count = parts * seg, parts * rows
    by_head = lambda size: pl.BlockSpec((parts, None, size, DH), lambda h, s: (0, s, 0, head))
    by_row = lambda: pl.BlockSpec((None, queries, DH), lambda h, s: (s, 0, h))
    by_place = lambda: pl.BlockSpec((None, DH, key_count), lambda h, s: (s, h, 0))
    grid_spec = pl.GridSpec(
        grid=(1, group),
        in_specs=[
            pl.BlockSpec((None, None, queries, key_count), lambda h, s: (s, head, 0, 0)),
            pl.BlockSpec((None, None, queries, DH), lambda h, s: (s, head, 0, 0)),
            by_head(seg),
            by_head(seg),
            by_head(seg),
            by_head(seg),
            by_head(rows),
            by_head(rows),
            pl.BlockSpec((key_count, DH), lambda h, s: (0, head)),
        ],
        out_specs=[
            by_row(),
            by_place(),
            by_place(),
            by_row(),
            by_row(),
            pl.BlockSpec((None, DH, key_count), lambda h, s: (h, 0, 0)),
            pl.BlockSpec((None, 8, DH), lambda h, s: (h, 0, 0)),
        ],
        scratch_shapes=[
            pltpu.VMEM((key_count, DH), BF16),
            pltpu.VMEM((key_count, DH), BF16),
            pltpu.VMEM((queries, DH), BF16),
            pltpu.VMEM((BLOCK, key_count), F32),
            pltpu.VMEM((BLOCK, key_count), F32),
            pltpu.VMEM((BLOCK, key_count), BF16),
            pltpu.VMEM((BLOCK, key_count), BF16),
            pltpu.VMEM((DH, key_count), F32),
            pltpu.VMEM((DH, key_count), F32),
        ],
    )
    return pl.pallas_call(
        functools.partial(pull_kernel, cuts),
        grid_spec=grid_spec,
        out_shape=[
            jax.ShapeDtypeStruct((group, queries, DH), BF16),
            jax.ShapeDtypeStruct((group, DH, key_count), BF16),
            jax.ShapeDtypeStruct((group, DH, key_count), BF16),
            jax.ShapeDtypeStruct((group, queries, DH), BF16),
            jax.ShapeDtypeStruct((group, queries, DH), BF16),
            jax.ShapeDtypeStruct((1, DH, key_count), F32),
            jax.ShapeDtypeStruct((1, 8, DH), F32),
        ],
        compiler_params=pltpu.CompilerParams(
            dimension_semantics=("arbitrary", "arbitrary"), vmem_limit_bytes=VMEM_LIMIT
        ),
        cost_estimate=cost(39),
        name="pull",
    )(weights, inverse, attended, out_grad, content_q, position_q, keys, values, table_rev)


def project_kernel(
    cuts, rows_ref, gain_ref, shift_ref, w_ref, old_ref, mem_ref, seg_ref, q_ref, k_ref, v_ref, normed
):
    rows, width = rows_ref.shape
    cols = k_ref.shape[1]
    step = 32
    for low in range(0, rows, step):
        wide = rows_ref[low : low + step, :].astype(F32)
        centred = wide - jnp.mean(wide, axis=1, keepdims=True)
        rate = lax.rsqrt(jnp.mean(centred * centred, axis=1, keepdims=True) + EPSILON)
        normed[low : low + step, :] = (centred * rate * gain_ref[...] + shift_ref[...]).astype(BF16)
    cut = cuts[0] + cuts[1]
    old_ref[...] = normed[: cuts[0], :]
    mem_ref[...] = normed[cuts[0] : cut, :]
    seg_ref[...] = normed[cut:, :]
    q_ref[...] = mm(normed[cut:, :], w_ref[:, :cols], NN)
    k_ref[...] = mm(normed[...], w_ref[:, cols : 2 * cols], NN).astype(BF16)
    v_ref[...] = mm(normed[...], w_ref[:, 2 * cols : 3 * cols], NN).astype(BF16)


def project(rows_all, gain, shift, columns, cuts):
    parts, group, each, width = rows_all.shape
    cols = columns.shape[1] // 4
    block = lambda size, wide: pl.BlockSpec((None, None, size, wide), lambda p, s: (p, s, 0, 0))
    placed = lambda size: pl.BlockSpec((None, size, width), lambda p, s: (s, p, 0))
    whole = lambda *shape: pl.BlockSpec(shape, lambda p, s: (0,) * len(shape))
    shape = lambda size, kind: jax.ShapeDtypeStruct((parts, group, size, cols), kind)
    return pl.pallas_call(
        functools.partial(project_kernel, cuts),
        grid_spec=pl.GridSpec(
            grid=(parts, group),
            in_specs=[
                block(each, width),
                whole(1, width),
                whole(1, width),
                whole(width, 4 * cols),
            ],
            out_specs=[placed(size) for size in cuts]
            + [block(cuts[2], cols), block(each, cols), block(each, cols)],
            scratch_shapes=[pltpu.VMEM((each, width), BF16)],
        ),
        out_shape=[jax.ShapeDtypeStruct((group, parts * size, width), BF16) for size in cuts]
        + [shape(cuts[2], F32), shape(each, BF16), shape(each, BF16)],
        compiler_params=pltpu.CompilerParams(
            dimension_semantics=("arbitrary", "arbitrary"), vmem_limit_bytes=VMEM_LIMIT
        ),
        cost_estimate=cost(17),
        name="project",
    )(rows_all, gain, shift, columns)


def gelu_both(x):
    near = jnp.abs(x)
    t = 1.0 / (1.0 + (0.3275911 * math.sqrt(0.5)) * near)
    bell = jnp.exp2((x * x) * (-0.5 * LOG2E))
    tail = 0.5 * 1.061405429
    for factor in (-1.453152027, 1.421413741, -0.284496736, 0.254829592):
        tail = tail * t + 0.5 * factor
    tail = tail * t * bell
    below = jnp.where(x < 0.0, tail, 1.0 - tail)
    return x * below, below + x * bell * (1.0 / math.sqrt(2.0 * math.pi))


def forward_back_kernel(
    last, parts, pair, n_ref, c_ref, *rest,
):
    up_refs, down_refs, shift_ref = rest[:parts], rest[parts : parts + pair], rest[parts + pair]
    rest = rest[parts + pair + 1 :]
    if last:
        part_in, grad_in, part_out, part_far, grad_out, grad_far, late_ref, sums_ref = rest[:8]
        pre, slope, hidden, act, up_out, down_out, sems, part_ref, grad_ref = rest[8:]
    else:
        part_ref, grad_ref, late_ref, sums_ref = rest[:4]
        pre, slope, hidden, act, up_out, down_out, sems = rest[4:]
    tile = pl.program_id(0)
    tiles = pl.num_programs(0)
    cols, units = up_refs[0].shape
    unit_cols, width = down_refs[0].shape
    rows = n_ref.shape[0]
    slot = lax.rem(tile, 2)
    up_weight = jnp.concatenate([ref[...] for ref in up_refs], axis=0)
    down_weight = jnp.concatenate([ref[...] for ref in down_refs], axis=0)

    def copies(at, index):
        return (
            pltpu.make_async_copy(
                up_out.at[at],
                late_ref.at[:, pl.ds(0, cols), pl.ds(pl.multiple_of(index * units, units), units)],
                sems.at[at, 0],
            ),
            pltpu.make_async_copy(
                down_out.at[at],
                late_ref.at[pl.ds(index * pair, pair), pl.ds(cols, unit_cols), :],
                sems.at[at, 1],
            ),
        )

    @pl.when(tile == 0)
    def _():
        if last:
            part_ref[...] = part_in[...]
            grad_ref[...] = grad_in[...]
        else:
            part_ref[...] = jnp.zeros_like(part_ref)
            grad_ref[...] = jnp.zeros_like(grad_ref)

    pre[...] = mm(n_ref[...], up_weight, NN)
    slope[...] = mm(c_ref[...], down_weight, NT)
    for low in range(0, rows, 16):
        some = slice(low, low + 16)
        value, change = gelu_both(pre[some, :] + shift_ref[...])
        hidden[some, :] = value.astype(BF16)
        act[some, :] = (change * slope[some, :]).astype(BF16)
    part_ref[...] += mm(hidden[...], down_weight, NN)
    grad_ref[...] += mm(act[...], up_weight, NT)
    sums_ref[...] = jnp.sum(act[...].astype(F32), axis=0, keepdims=True)

    @pl.when(tile >= 2)
    def _():
        for copy in copies(slot, tile - 2):
            copy.wait()

    up_out[slot] = mm(n_ref[...], act[...], TN).astype(BF16).reshape(parts, cols, units)
    down_out[slot] = mm(hidden[...], c_ref[...], TN).astype(BF16).reshape(pair, unit_cols, width)
    for copy in copies(slot, tile):
        copy.start()

    @pl.when(tile == tiles - 1)
    def _():
        if last:
            part_out[...] = part_ref[: rows // 2, :]
            part_far[...] = part_ref[rows // 2 :, :].astype(BF16)
            grad_out[...] = grad_ref[: rows // 2, :]
            grad_far[...] = grad_ref[rows // 2 :, :].astype(BF16)
        for copy in (copies(1 - slot, tile - 1) if parts > pair else ()) + copies(slot, tile):
            copy.wait()


def forward_back(normed, cot, gathered, shift, carry):
    parts, _, width = gathered.shape
    rows = normed.shape[0]
    cols = width // parts
    unit_cols = shift.shape[1] // parts
    pair = 2
    units = pair * unit_cols
    last = len(carry) > 0
    one = pl.Buffered(1)
    whole = lambda *shape: pl.BlockSpec(shape, lambda t: (0,) * len(shape), pipeline_mode=one)
    up = lambda p: pl.BlockSpec((None, cols, units), lambda t: (p, 0, t))
    down = lambda i: pl.BlockSpec(
        (None, unit_cols, width), lambda t: (t * pair + i, cols // unit_cols, 0)
    )
    if last:
        sums = [((rows // 2, width), F32), ((rows // 2, width), BF16)] * 2
    else:
        sums = [((rows, width), F32)] * 2
    return pl.pallas_call(
        functools.partial(forward_back_kernel, last, parts, pair),
        grid_spec=pl.GridSpec(
            grid=(parts // pair,),
            in_specs=[
                whole(rows, width),
                whole(rows, width),
            ]
            + [up(p) for p in range(parts)]
            + [down(i) for i in range(pair)]
            + [pl.BlockSpec((1, units), lambda t: (0, t))]
            + [whole(rows, width) for _ in carry],
            out_specs=[whole(*shape) for shape, _ in sums]
            + [
                pl.BlockSpec(memory_space=pl.ANY),
                pl.BlockSpec((1, units), lambda t: (0, t)),
            ],
            scratch_shapes=[
                pltpu.VMEM((rows, units), F32),
                pltpu.VMEM((rows, units), F32),
                pltpu.VMEM((rows, units), BF16),
                pltpu.VMEM((rows, units), BF16),
                pltpu.VMEM((2, parts, cols, units), BF16),
                pltpu.VMEM((2, pair, unit_cols, width), BF16),
                pltpu.SemaphoreType.DMA((2, 2)),
            ]
            + [pltpu.VMEM((rows, width), F32) for _ in carry],
        ),
        out_shape=[jax.ShapeDtypeStruct(shape, kind) for shape, kind in sums]
        + [
            jax.ShapeDtypeStruct((parts, cols + unit_cols, width), BF16),
            jax.ShapeDtypeStruct((1, parts * unit_cols), F32),
        ],
        compiler_params=pltpu.CompilerParams(
            dimension_semantics=("arbitrary",), vmem_limit_bytes=VMEM_LIMIT
        ),
        cost_estimate=cost(29),
        name="forward_back",
    )(normed, cot, *[gathered] * (parts + pair), shift, *carry)


def leave_kernel(a_ref, s_ref, w_ref, shift_ref, gain_ref, bias_ref, flat_ref, m_ref, n_ref):
    parts = a_ref.shape[0]
    flat_ref[...] = jnp.concatenate([a_ref[part] for part in range(parts)], axis=1)
    m_ref[...] = s_ref[...].astype(F32) + (mm(flat_ref[...], w_ref[...], NN) + shift_ref[...])
    step = 16
    for low in range(0, m_ref.shape[0], step):
        unit, _ = standardise(m_ref[low : low + step, :])
        n_ref[low : low + step, :] = (unit * gain_ref[...] + bias_ref[...]).astype(BF16)


def leave(mixed_heads, segment, base, weight, shift, gain, bias):
    parts, group, seg, cols = mixed_heads.shape
    width = parts * cols
    rows = lambda: pl.BlockSpec((None, seg, width), lambda s: (s, 0, 0))
    vector = lambda: pl.BlockSpec((1, width), lambda s: (0, 0))
    shape = lambda kind: jax.ShapeDtypeStruct((group, seg, width), kind)
    return pl.pallas_call(
        leave_kernel,
        grid_spec=pl.GridSpec(
            grid=(group,),
            in_specs=[
                pl.BlockSpec((parts, None, seg, cols), lambda s: (0, s, 0, 0)),
                pl.BlockSpec((None, seg, width), lambda s: (s + base, 0, 0)),
                pl.BlockSpec((width, width), lambda s: (0, 0)),
                vector(),
                vector(),
                vector(),
            ],
            out_specs=[rows(), rows(), rows()],
        ),
        out_shape=[shape(BF16), shape(F32), shape(BF16)],
        compiler_params=pltpu.CompilerParams(vmem_limit_bytes=VMEM_LIMIT),
        cost_estimate=cost(6),
        name="leave",
    )(mixed_heads, segment, weight, shift, gain, bias)


def enter_kernel(
    m_ref, g_ref, far_ref, c_ref, w_ref, gain_ref, mg_ref, b_ref, a_ref, sums_ref
):
    @pl.when(pl.program_id(0) == 0)
    def _():
        sums_ref[...] = jnp.zeros_like(sums_ref)

    parts = a_ref.shape[0]
    rows, width = m_ref.shape
    step = 32
    total = [jnp.zeros((1, width), F32) for _ in range(4)]
    for low in range(0, rows, step):
        at = slice(low, low + step)
        unit, rate = standardise(m_ref[at, :])
        grad = g_ref[at, :] + far_ref[at, :].astype(F32)
        cot = c_ref[at, :].astype(F32)
        middle_grad = cot + standardise_back(unit, rate, grad, gain_ref[...])
        branch = middle_grad.astype(BF16)
        mg_ref[at, :] = middle_grad
        b_ref[at, :] = branch
        for i, value in enumerate((branch.astype(F32), grad * unit, grad, cot)):
            total[i] = total[i] + jnp.sum(value, axis=0, keepdims=True)
    sums_ref[...] += jnp.concatenate(total + [jnp.zeros((4, width), F32)], axis=0)
    for part in range(parts):
        low = part * a_ref.shape[2]
        weight = w_ref[low : low + a_ref.shape[2], :]
        a_ref[part] = mm(b_ref[...], weight, NT).astype(BF16)


def enter(middle, grad, far, cot, base, weight, gain, parts):
    group, seg, width = middle.shape
    cols = width // parts
    rows = lambda: pl.BlockSpec((None, seg, width), lambda s: (s, 0, 0))
    later = lambda: pl.BlockSpec((None, seg, width), lambda s: (s + base, 0, 0))
    shape = lambda kind: jax.ShapeDtypeStruct((group, seg, width), kind)
    return pl.pallas_call(
        enter_kernel,
        grid_spec=pl.GridSpec(
            grid=(group,),
            in_specs=[
                rows(),
                later(),
                later(),
                later(),
                pl.BlockSpec((width, width), lambda s: (0, 0)),
                pl.BlockSpec((1, width), lambda s: (0, 0)),
            ],
            out_specs=[
                rows(),
                rows(),
                pl.BlockSpec((parts, None, seg, cols), lambda s: (0, s, 0, 0)),
                pl.BlockSpec((8, width), lambda s: (0, 0)),
            ],
        ),
        out_shape=[
            shape(F32),
            shape(BF16),
            jax.ShapeDtypeStruct((parts, group, seg, cols), BF16),
            jax.ShapeDtypeStruct((8, width), F32),
        ],
        compiler_params=pltpu.CompilerParams(
            dimension_semantics=("arbitrary",), vmem_limit_bytes=VMEM_LIMIT
        ),
        cost_estimate=cost(7),
        name="enter",
    )(middle, grad, far, cot, weight, gain)


def compress_kernel(low, rows_ref, w_ref, shift_ref, out_ref, wide):
    count = out_ref.shape[0]
    cols = out_ref.shape[1]
    blocks = wide.shape[0]
    for at in range(blocks):
        wide[at] = rows_ref[low : low + 3 * count, at * LANES : (at + 1) * LANES].astype(F32)
    total = jnp.broadcast_to(shift_ref[...], (count, cols))
    for k in range(3):
        every = jnp.concatenate(
            [wide[at, pl.ds(k, count, stride=3), :] for at in range(blocks)], axis=1
        ).astype(BF16)
        total = total + mm(every, w_ref[:, k * cols : (k + 1) * cols], NN)
    out_ref[...] = total.astype(BF16)


def compress(rows_all, columns, shift, low, count):
    parts, group, each, width = rows_all.shape
    cols = columns.shape[1] // 3
    return pl.pallas_call(
        functools.partial(compress_kernel, low),
        grid_spec=pl.GridSpec(
            grid=(parts, group),
            in_specs=[
                pl.BlockSpec((None, None, each, width), lambda p, s: (p, s, 0, 0)),
                pl.BlockSpec((width, 3 * cols), lambda p, s: (0, 0)),
                pl.BlockSpec((1, cols), lambda p, s: (0, 0)),
            ],
            out_specs=pl.BlockSpec((None, None, count, cols), lambda p, s: (p, s, 0, 0)),
            scratch_shapes=[pltpu.VMEM((width // LANES, 3 * count, LANES), F32)],
        ),
        out_shape=jax.ShapeDtypeStruct((parts, group, count, cols), BF16),
        compiler_params=pltpu.CompilerParams(
            dimension_semantics=("arbitrary", "arbitrary"), vmem_limit_bytes=VMEM_LIMIT
        ),
        cost_estimate=cost(6.5),
        name="compress",
    )(rows_all, columns, shift)


def lay_out_kernel(
    parts, unit_cols, core_ref, a_ref, b_ref, c_ref, d_ref, up_ref, down_ref
):
    flipped = core_ref[0] == 1
    for half, (mine_ref, far_ref) in enumerate(((a_ref, c_ref), (b_ref, d_ref))):
        mine, far = mine_ref[...].astype(F32), far_ref[...].astype(F32)
        for core, value in enumerate(
            (jnp.where(flipped, far, mine), jnp.where(flipped, mine, far))
        ):
            for part in range(parts):
                at = ((part * 2 + core) * 2 + half) * unit_cols
                up_ref[:, at : at + unit_cols] = value[
                    0, :, part * unit_cols : (part + 1) * unit_cols
                ]
            down_ref[2 * core + half] = value[1]


def lay_out(core, mine, far, parts):
    _, rows, width = mine[0].shape
    step = rows // 4 if rows % 64 == 0 else rows
    half = lambda: pl.BlockSpec((2, step, width), lambda r, *_: (0, r, 0))
    return pl.pallas_call(
        functools.partial(lay_out_kernel, parts, rows),
        grid_spec=pltpu.PrefetchScalarGridSpec(
            num_scalar_prefetch=1,
            grid=(rows // step,),
            in_specs=[half(), half(), half(), half()],
            out_specs=[
                pl.BlockSpec((step, 4 * width), lambda r, *_: (r, 0)),
                pl.BlockSpec((4, step, width), lambda r, *_: (0, r, 0)),
            ],
        ),
        out_shape=[
            jax.ShapeDtypeStruct((rows, 4 * width), F32),
            jax.ShapeDtypeStruct((4, rows, width), F32),
        ],
        compiler_params=pltpu.CompilerParams(vmem_limit_bytes=VMEM_LIMIT),
        cost_estimate=cost(4),
        name="lay_out",
    )(core.reshape(1), *mine, *far)


def lay_squares_kernel(in_ref, *out_refs):
    parts = in_ref.shape[0]
    cols = in_ref.shape[2] // len(out_refs)
    for at, out_ref in enumerate(out_refs):
        for part in range(parts):
            out_ref[:, part * cols : (part + 1) * cols] = in_ref[
                part, :, at * cols : (at + 1) * cols
            ].astype(F32)


def lay_squares(summed, rows):
    parts, _, wide = summed.shape
    width = parts * wide // 4
    step = rows // 2
    return pl.pallas_call(
        lay_squares_kernel,
        grid_spec=pl.GridSpec(
            grid=(2,),
            in_specs=[pl.BlockSpec((parts, step, wide), lambda i: (0, i, 0))],
            out_specs=[pl.BlockSpec((step, width), lambda i: (i, 0)) for _ in range(4)],
        ),
        out_shape=[jax.ShapeDtypeStruct((rows, width), F32) for _ in range(4)],
        compiler_params=pltpu.CompilerParams(vmem_limit_bytes=VMEM_LIMIT),
        cost_estimate=cost(2.5),
        name="lay_squares",
    )(summed)


def settle_kernel(heads, me_ref, old_ref, mem_ref, seg_ref, *rest):
    q_refs, k_refs, v_refs, ks_refs, vs_refs, dt_refs, sums_refs = (
        rest[i * heads : (i + 1) * heads] for i in range(7)
    )
    w_ref, table_ref, gain_ref, shift_ref, small_ref, part_ref, out_ref, total = rest[7 * heads :]
    stream = pl.program_id(0)
    parts, rows, wide = out_ref.shape
    cols = wide // 4
    width = parts * cols

    @pl.when(stream == 0)
    def _():
        total[...] = jnp.zeros_like(total)

    low = old_ref.shape[0]
    high = low + mem_ref.shape[0]
    pair = lambda first, last: [ref[:, first:last] for ref in (*k_refs, *v_refs)]
    total[...] += mm(
        jnp.concatenate([ref[...].T for ref in q_refs] + pair(high, high + seg_ref.shape[0]), axis=0),
        seg_ref[...],
        NN,
    )
    total[cols:, :] += mm(jnp.concatenate(pair(low, high), axis=0), mem_ref[...], NN)
    total[cols:, :] += mm(jnp.concatenate(pair(0, low), axis=0), old_ref[...], NN)
    three = jnp.concatenate([ref[...] for ref in (*q_refs, *ks_refs, *vs_refs)], axis=1)
    part = mm(three, w_ref[:, : 3 * cols], NT).astype(BF16)
    part_ref[...] = part.reshape(part_ref.shape)

    @pl.when(stream == pl.num_programs(0) - 1)
    def _():
        places = jnp.concatenate([ref[0].astype(BF16) for ref in dt_refs], axis=0)
        rel = mm(places, table_ref[...], NN)
        line = lambda row: jnp.concatenate(
            [ref[0, row : row + 1, :] for ref in sums_refs], axis=1
        )
        row_sums = jnp.concatenate([line(2), line(3), line(4)], axis=1)
        pieces, rest = [], row_sums
        for _ in range(3):
            pieces.append(rest.astype(BF16))
            rest = rest - pieces[-1].astype(F32)
        pieces = jnp.concatenate(pieces + [jnp.zeros((13, 3 * cols), BF16)], axis=0)
        shift_grad = jnp.sum(mm(pieces, w_ref[:, : 3 * cols], NT), axis=0, keepdims=True)
        weight = w_ref[:, : 3 * cols].astype(F32)
        along = jnp.sum(weight.T * total[...], axis=0, keepdims=True)
        gain_grad = (along - shift_ref[...] * shift_grad) / gain_ref[...]
        for at in range(parts):
            low, high = at * cols, (at + 1) * cols
            out_ref[at, :cols, : 3 * cols] = total[:, low:high].T.astype(BF16)
            out_ref[at, :cols, 3 * cols :] = rel[:, low:high].T.astype(BF16)
            mine = (me_ref[0] == at).astype(F32)
            none = jnp.zeros((1, 2 * cols), F32)
            first = jnp.concatenate([gain_grad[:, low:high], shift_grad[:, low:high], none], axis=1)
            second = jnp.concatenate([none, mine * line(0), mine * line(1)], axis=1)
            added = jnp.concatenate([first, second, jnp.zeros((14, wide), F32)], axis=0)
            out_ref[at, cols:, :] = (small_ref[at] + added).astype(BF16)


def settle(me, normed, grads, columns, table, gain, shift, small, parts):
    group, queries, width = normed[2].shape
    cols = width // parts
    wide = 4 * cols
    by_kind = list(zip(*grads))
    block = lambda array: pl.BlockSpec((None, *array.shape[1:]), lambda s, *_: (s, 0, 0))
    whole = lambda *shape: pl.BlockSpec(
        shape, lambda s, *_: (0,) * len(shape), pipeline_mode=pl.Buffered(1)
    )
    return pl.pallas_call(
        functools.partial(settle_kernel, len(grads)),
        grid_spec=pltpu.PrefetchScalarGridSpec(
            num_scalar_prefetch=1,
            grid=(group,),
            in_specs=[block(rows) for rows in normed]
            + [block(each) for kind in by_kind[:5] for each in kind]
            + [whole(*each.shape) for kind in by_kind[5:] for each in kind]
            + [
                whole(*columns.shape),
                whole(*table.shape),
                whole(1, width),
                whole(1, width),
                whole(*small.shape),
            ],
            out_specs=[
                pl.BlockSpec((parts, None, queries // parts, width), lambda s, *_: (0, s, 0, 0)),
                whole(parts, cols + 16, wide),
            ],
            scratch_shapes=[pltpu.VMEM((3 * cols, width), F32)],
        ),
        out_shape=[
            jax.ShapeDtypeStruct((parts, group, queries // parts, width), BF16),
            jax.ShapeDtypeStruct((parts, cols + 16, wide), BF16),
        ],
        compiler_params=pltpu.CompilerParams(
            dimension_semantics=("arbitrary",), vmem_limit_bytes=VMEM_LIMIT
        ),
        cost_estimate=cost(14),
        name="settle",
    )(
        me.reshape(1), *normed, *[each for kind in by_kind for each in kind], columns, table, gain, shift,
        small,
    )


def standardise(rows):
    mean = jnp.mean(rows, axis=-1, keepdims=True)
    centred = rows - mean
    rate = lax.rsqrt(jnp.mean(centred * centred, axis=-1, keepdims=True) + EPSILON)
    return centred * rate, rate


def standardise_back(unit, rate, grad, gain):
    scaled = grad * gain
    mean = jnp.mean(scaled, axis=-1, keepdims=True)
    along = jnp.mean(scaled * unit, axis=-1, keepdims=True)
    return rate * (scaled - mean - unit * along)


def sinusoid_reversed(rows, width):
    positions = (rows - 1 - jnp.arange(rows, dtype=jnp.int32)).astype(F32)[:, None]
    frequency = jnp.exp(
        jnp.arange(width // 2, dtype=F32) * (-2.0 * math.log(10000.0) / width)
    )
    angles = positions * frequency[None, :]
    return jnp.concatenate([jnp.sin(angles), jnp.cos(angles)], axis=1).astype(BF16)


def dot(left, right):
    return mm(left, right, NN)


def swap(value):
    return lax.ppermute(value, "core", [(0, 1), (1, 0)])


def exchange(blocks, name, axis=0):
    count = lax.axis_size(name)
    me = lax.axis_index(name)
    block = lambda at: lax.dynamic_index_in_dim(blocks, at, axis, keepdims=False)
    return [block(me)] + [
        lax.ppermute(block(me ^ apart), name, [(i, i ^ apart) for i in range(count)])
        for apart in range(1, count)
    ]


def collect(block, name):
    count = lax.axis_size(name)
    me = lax.axis_index(name)
    found = jnp.stack(
        [block]
        + [
            lax.ppermute(block, name, [(i, i ^ apart) for i in range(count)])
            for apart in range(1, count)
        ]
    )
    return jnp.stack(
        [lax.dynamic_index_in_dim(found, me ^ i, 0, keepdims=False) for i in range(count)]
    )


def add_up(arrays, kind=BF16):
    total = arrays[0].astype(F32)
    for array in arrays[1:]:
        total = total + array.astype(F32)
    return total.astype(kind)


def body(
    segment, memory, compressed, eob, reset, ln1_gain, ln1_bias, w_query, w_key, w_value,
    w_out, out_bias, w_rel, bias_content, bias_position, ln2_gain, ln2_bias, w_up, up_bias,
    w_down, down_bias, conv_weight, conv_bias, cotangent,
):
    parts = lax.axis_size("seq")
    layers = lax.axis_size("z")
    core = lax.axis_index("core")
    me = lax.axis_index("seq")
    group, seg, width = segment.shape
    mem, old = memory.shape[1], compressed.shape[1]
    cuts = (old, mem, seg)
    each = old + mem + seg
    keys_in_all = parts * each
    cols = width // parts
    wide = 4 * cols
    own = group * seg
    unit_cols = w_up.shape[1] // (4 * parts)
    barrier = lax.optimization_barrier

    def by_columns(matrices):
        count = matrices.shape[0]
        sent = matrices.reshape(count, cols, parts, cols).transpose(2, 1, 0, 3)
        return sent.reshape(parts, cols, count * cols)

    up_bias_own = lax.dynamic_slice_in_dim(up_bias, core * 2 * unit_cols, 2 * unit_cols, 0)
    vectors = jnp.concatenate(
        [ln1_gain, ln1_bias, out_bias, ln2_gain, ln2_bias, down_bias, up_bias_own]
    )
    vectors = jnp.pad(vectors.reshape(2, wide), ((0, 14), (0, 0)))
    half = cols // 2

    def my_half(blocks):
        return lax.dynamic_slice_in_dim(blocks, core * half, half, 1)

    def join(mine):
        far = swap(mine)
        both = [jnp.where(core == 0, mine, far), jnp.where(core == 0, far, mine)]
        return jnp.stack(both, axis=1).reshape(width, mine.shape[2])

    sent = my_half(by_columns(jnp.stack([w_query, w_key, w_value, w_rel])))
    sent = jnp.concatenate([sent, jnp.broadcast_to(vectors, (parts, *vectors.shape))], axis=1)
    got = lax.all_to_all(sent, "seq", 0, 0, tiled=True)
    out_sent = jnp.broadcast_to(lax.dynamic_slice_in_dim(w_out, core * half, half, 0), (parts, half, width))
    others = jnp.concatenate([my_half(by_columns(conv_weight)), out_sent], axis=2)
    spans = [(0, group)]
    local = [
        jnp.concatenate([compressed[low:high], memory[low:high], segment[low:high]], axis=1)
        for low, high in spans
    ]
    rows_all = [lax.all_gather(local[0], "seq")]
    columns = join(got[:, :half])
    vectors = got[:, half : half + 2].reshape(parts, 2 * wide).astype(F32)
    gain_one, shift_one, out_shift, gain_two, shift_two, down_shift = (
        vectors[:, cols * i : cols * (i + 1)].reshape(1, width) for i in range(6)
    )
    up_shift = vectors[:, 6 * cols :].reshape(parts, 2, unit_cols).transpose(1, 0, 2)
    up_shift = up_shift.reshape(2, 1, parts * unit_cols)
    up_quarters = lax.dynamic_slice_in_dim(
        w_up.reshape(cols, parts, 2, 2, unit_cols), core, 1, 2
    ).reshape(cols, parts, 2, unit_cols)
    up_quarters = [up_quarters[:, :, i].reshape(cols, width) for i in range(2)]
    down_half = lax.dynamic_slice_in_dim(w_down, core * 2 * unit_cols, 2 * unit_cols, 0)
    down_quarters = [down_half[unit_cols * i : unit_cols * (i + 1)] for i in range(2)]
    first = jnp.concatenate([up_quarters[0], down_quarters[0]], axis=0)
    second = jnp.concatenate([up_quarters[1], down_quarters[1]], axis=0)
    cot_own = cotangent.reshape(own, width)
    cot_both = jnp.concatenate([cot_own, swap(cot_own)], axis=0)

    table_rev = sinusoid_reversed(keys_in_all, width)
    proj_rev = dot(table_rev, columns[:, 3 * cols :]).astype(BF16)
    index = jnp.arange(eob.shape[1], dtype=jnp.int32)[None, :]
    opens = jnp.pad(eob, ((0, 0), (1, 0)))[:, :-1] == 1
    start = lax.cummax(jnp.where(opens, index, 0), axis=1)
    shade = jnp.where((start == 0) & (reset[:, None] == 0), 0.0, MASKED)
    info = jnp.stack([start.astype(F32), shade], axis=2)
    info = jnp.pad(info, ((0, 0), (0, 0), (0, LANES - 2)))
    rows_all[0], proj_rev, info, cot_both, table_rev, columns, others, *local = barrier(
        (rows_all[0], proj_rev, info, cot_both, table_rev, columns, others, *local)
    )
    others = lax.all_to_all(others, "seq", 0, 0, tiled=True)
    rows_all = [rows_all[0]] + [lax.all_gather(rows, "seq") for rows in local[1:]]

    kept, heads = [], []
    for batch, (low, high) in enumerate(spans):
        if batch == len(spans) - 1:
            rows_all[batch], first, *heads = barrier((rows_all[batch], first, *heads))
            first = lax.all_gather(first, "seq")
        *normed, query, keys, values = project(rows_all[batch], gain_one, shift_one, columns, cuts)
        second, others, query = barrier((second, others, query))
        second = lax.all_gather(second, "seq")
        weights, inverse, mixed_heads, content_q, position_q = attend(
            query,
            bias_content.astype(F32).reshape(1, cols),
            bias_position.astype(F32).reshape(1, cols),
            keys,
            values,
            proj_rev,
            info[low:high],
            cuts,
        )
        kept.append((weights, inverse, mixed_heads, content_q, position_q, keys, values))
        heads.append(lax.all_to_all(mixed_heads, "seq", 0, 0, tiled=True))

    mixed_heads, others = barrier((mixed_heads, others))
    others = join(others)
    conv_columns, out_full = others[:, : 3 * cols], others[:, 3 * cols :]
    packed = compress(
        rows_all[0], conv_columns, conv_bias.astype(F32).reshape(1, cols), old, mem // 3
    )
    packed, *heads = barrier((packed, *heads))

    attended, middle, normed_two = [], [], []
    for (low, high), batch in zip(spans, heads):
        one, two, three = leave(batch, segment, low, out_full, out_shift, gain_two, shift_two)
        attended.append(one.reshape(-1, width))
        middle.append(two)
        normed_two.append(three.reshape(-1, width))
    both = jnp.concatenate(normed_two + [swap(rows) for rows in normed_two], axis=0)
    part, part_grad, late_one, unit_one = forward_back(both, cot_both, first, up_shift[0], ())
    late_one = lax.psum_scatter(
        late_one.reshape(-1, width), "seq", scatter_dimension=0, tiled=True
    )
    part, part_far, part_grad, grad_far, late_two, unit_two = forward_back(
        both, cot_both, second, up_shift[1], (part, part_grad)
    )
    grad_far = swap(grad_far)
    by_stream = lambda rows: rows.reshape(group, seg, width)
    middle_grad, branch_grad, head_grad, sums_two = [], [], [], 0.0
    for (low, high), batch in zip(spans, middle):
        one, two, three, four = enter(
            batch, by_stream(part_grad), by_stream(grad_far), cotangent, low, out_full, gain_two, parts
        )
        middle_grad.append(one)
        branch_grad.append(two.reshape(-1, width))
        three, part_grad = barrier((three, part_grad))
        head_grad.append(lax.all_to_all(three, "seq", 0, 0, tiled=True))
        sums_two = sums_two + four
    result = part + swap(part_far).astype(F32) + down_shift
    output = (jnp.concatenate(middle).reshape(own, width) + result).astype(BF16)
    output = output.reshape(group, seg, width)

    out_shift_grad, gain_two_grad, shift_two_grad, down_shift_grad = (
        sums_two[i].reshape(parts, cols) for i in range(4)
    )
    none = jnp.zeros((parts, 2 * cols), F32)
    unit_sums = jnp.stack(
        [unit_one.reshape(parts, unit_cols), unit_two.reshape(parts, unit_cols)], axis=1
    ).reshape(parts, 2 * unit_cols)
    small = jnp.stack(
        [
            jnp.concatenate([none, out_shift_grad, gain_two_grad], axis=1),
            jnp.concatenate([shift_two_grad, down_shift_grad, none], axis=1),
            jnp.concatenate(
                [jnp.where(core == 0, unit_sums, 0.0), jnp.where(core == 1, unit_sums, 0.0)], axis=1
            ),
        ],
        axis=1,
    )
    small = jnp.pad(small, ((0, 0), (0, 13), (0, 0)))
    weights, inverse, mixed_heads, content_q, position_q, keys, values = kept[0]
    out_grad = mm(jnp.concatenate(attended), jnp.concatenate(branch_grad), TN)
    out_grad = out_grad.astype(BF16).reshape(parts, cols, width)
    late_one, small, out_grad, late_two, output, head_grad = barrier(
        (late_one, small, out_grad, late_two, output, head_grad[0])
    )
    late_two = lax.psum_scatter(
        late_two.reshape(-1, width), "seq", scatter_dimension=0, tiled=True
    )
    late_one = exchange(late_one.reshape(layers, -1, width), "z")
    grads = []
    for head in range(cols // DH):
        grads.append(
            list(
                pull(
                    head, weights, inverse, mixed_heads, head_grad, content_q, position_q, keys,
                    values, proj_rev, cuts,
                )
            )
        )
        if head == 0:
            late_one, head_grad, grads[0][0] = barrier((late_one, head_grad, grads[0][0]))
            late_one = collect(add_up(late_one), "z")
    late_one, late_two, out_grad, grads[-1][0] = barrier(
        (late_one, late_two, out_grad, grads[-1][0])
    )
    late_two = exchange(late_two.reshape(layers, -1, width), "z")
    out_sent = lax.all_to_all(out_grad, "seq", 0, 0, tiled=True)
    seg_part, square_grads = settle(
        me, normed, grads, columns, table_rev, gain_one, shift_one, small, parts
    )
    summed = lax.psum(square_grads, ("z", "core"))
    late_two, out_sent, seg_part = barrier((late_two, out_sent, seg_part))
    late_two = collect(add_up(late_two), "z")
    out_sent = jnp.sum(out_sent.astype(F32), axis=0).astype(BF16)
    summed, out_sent, packed = barrier((summed, out_sent, packed))
    summed = lax.all_to_all(summed, "seq", 0, 0, tiled=True)
    out_w = lax.psum(out_sent, ("z", "core"))
    packed = jnp.stack(exchange(packed, "seq"))
    new_compressed = jnp.concatenate(
        [lax.dynamic_index_in_dim(packed, p ^ me, 0, keepdims=False) for p in range(parts)], axis=2
    )
    seg_grad = lax.all_to_all(seg_part, "seq", 0, 0, tiled=True).astype(F32)
    seg_grad = jnp.sum(seg_grad, axis=0).reshape(own, width)
    unit_seg, rate_seg = standardise(segment.reshape(own, width).astype(F32))
    rows_grad = standardise_back(unit_seg, rate_seg, seg_grad, gain_one)
    segment_grad = jnp.concatenate(middle_grad, axis=0) + by_stream(rows_grad)

    halves = [late_one.reshape(2, unit_cols, width), late_two.reshape(2, unit_cols, width)]
    up_w, down_w = lay_out(core, halves, [swap(rows) for rows in halves], parts)
    down_w = down_w.reshape(4 * unit_cols, width)
    summed, out_w, output, segment_grad, new_compressed, up_w, down_w = barrier(
        (summed, out_w, output, segment_grad, new_compressed, up_w, down_w)
    )
    out_w = out_w.astype(F32)
    query_w, key_w, value_w, rel_w = lay_squares(summed, cols)
    small = jnp.sum(summed[:, cols : cols + 3].astype(F32), axis=0)
    piece = lambda row, i: small[row, cols * i : cols * (i + 1)]
    return (
        output,
        segment_grad,
        piece(0, 0),
        piece(0, 1),
        query_w,
        key_w,
        value_w,
        out_w,
        piece(0, 2),
        rel_w,
        piece(1, 2),
        piece(1, 3),
        piece(0, 3),
        piece(1, 0),
        up_w,
        small[2],
        down_w,
        piece(1, 1),
        new_compressed,
    )


def solution(mesh):
    dp = mesh.shape["dp"]
    cores = jax.sharding.Mesh(
        mesh.devices.reshape(dp // 2, 2, mesh.shape["seq"]), ("z", "core", "seq")
    )
    rows = P(("z", "core"), "seq", None)
    shard, matrix = P("seq"), P("seq", None)
    return jax.shard_map(
        body,
        mesh=cores,
        in_specs=(
            rows, rows, rows, P(("z", "core"), None), P(("z", "core")), shard, shard, matrix,
            matrix, matrix, matrix, shard, matrix, shard, shard, shard, shard, matrix, shard,
            matrix, shard, P(None, "seq", None), shard, rows,
        ),
        out_specs=(
            rows, rows, shard, shard, matrix, matrix, matrix, matrix, shard, matrix, shard,
            shard, shard, shard, matrix, shard, matrix, shard, rows,
        ),
        check_vma=False,
    )
```

```python
import functools
import math

import jax
import jax.numpy as jnp
from jax import lax
from jax.experimental import pallas as pl
from jax.experimental.pallas import tpu as pltpu
from jax.sharding import PartitionSpec as P

HEADS = 8
DH = 128
EPSILON = 1e-05
MASKED = -1e30
LANES = 128
BLOCK = 256
CHUNK = 16
VMEM_LIMIT = 60 * 2**20
SCALE = 1.0 / math.sqrt(DH)
LOG2E = 1.4426950408889634
BF16 = jnp.bfloat16
F32 = jnp.float32


def cost(microseconds):
    return pl.CostEstimate(flops=int(microseconds * 1.15e7), bytes_accessed=0, transcendentals=0)


def mm(left, right, dims):
    return lax.dot_general(left, right, (dims, ((), ())), preferred_element_type=F32)


NN = ((1,), (0,))
NT = ((1,), (1,))
TN = ((0,), (0,))


def lean_left(block, first_row, fill_columns):
    columns = block.shape[1] // LANES
    far = BLOCK - 1 - first_row
    whole, part = far // LANES, far % LANES
    turned = [
        pltpu.roll(
            block[:, LANES * t : LANES * (t + 1)], LANES - part, 1, stride=1, stride_axis=0
        )
        for t in range(columns)
    ]
    rows = lax.broadcasted_iota(jnp.int32, (block.shape[0], LANES), 0)
    lanes = lax.broadcasted_iota(jnp.int32, (block.shape[0], LANES), 1)
    near = lanes - rows < LANES - part
    out = []
    for t in range(fill_columns):
        a = turned[(t + whole) % columns]
        b = turned[(t + whole + 1) % columns]
        out.append(jnp.where(near, a, b))
    return jnp.concatenate(out, axis=1)


def lean_right(block, first_row):
    columns = block.shape[1] // LANES
    whole, part = first_row // LANES, first_row % LANES
    turned = [
        pltpu.roll(block[:, LANES * t : LANES * (t + 1)], part, 1, stride=1, stride_axis=0)
        for t in range(columns)
    ]
    rows = lax.broadcasted_iota(jnp.int32, (block.shape[0], LANES), 0)
    lanes = lax.broadcasted_iota(jnp.int32, (block.shape[0], LANES), 1)
    wrapped = lanes - rows < part
    out = []
    for t in range(columns):
        a = turned[(t - whole) % columns]
        b = turned[(t - whole - 1) % columns]
        out.append(jnp.where(wrapped, b, a))
    return jnp.concatenate(out, axis=1)


def flip_matrix(kind):
    rows = lax.broadcasted_iota(jnp.int32, (BLOCK, BLOCK), 0)
    lanes = lax.broadcasted_iota(jnp.int32, (BLOCK, BLOCK), 1)
    return (rows + lanes == BLOCK - 1).astype(F32).astype(kind)


def in_place_order(parts_ref, out_ref, cuts):
    parts = parts_ref.shape[0]
    low, base = 0, 0
    for size in cuts:
        for part in range(parts):
            out_ref[base + part * size : base + (part + 1) * size, :] = parts_ref[
                part, low : low + size, :
            ]
        low += size
        base += parts * size


def attend_kernel(
    cuts, q_ref, cb_ref, pb_ref, k_ref, v_ref, t_ref, info_ref,
    e_ref, inv_ref, o_ref, cq_ref, pq_ref,
    keys, values, raw, lean, mix, tops, sums,
):
    parts, seg, _ = q_ref.shape
    queries = parts * seg
    old = parts * (cuts[0] + cuts[1])
    in_place_order(k_ref, keys, cuts)
    in_place_order(v_ref, values, cuts)
    q = q_ref[...].reshape(queries, DH)
    content_q = (q + cb_ref[...]).astype(BF16)
    position_q = (q + pb_ref[...]).astype(BF16)
    cq_ref[...] = content_q.reshape(parts, seg, DH)
    pq_ref[...] = position_q.reshape(parts, seg, DH)
    for block in range(queries // BLOCK):
        row0 = block * BLOCK
        width = old + row0 + BLOCK
        skip = queries - BLOCK - row0
        raw[:, :width] = mm(content_q[row0 : row0 + BLOCK], keys[:width, :], NT)
        lean[:, :width] = mm(position_q[row0 : row0 + BLOCK], t_ref[skip : skip + width, :], NT)
        for chunk in range(BLOCK // CHUNK):
            r0 = chunk * CHUNK
            rows = slice(r0, r0 + CHUNK)
            turned = lean_left(lean[rows, :width], r0, width // LANES)
            score = raw[rows, :width] + turned
            start = info_ref[row0 + r0 : row0 + r0 + CHUNK, 0:1].astype(jnp.int32)
            shade = info_ref[row0 + r0 : row0 + r0 + CHUNK, 1:2]
            past = score[:, :old] + shade
            place = lax.broadcasted_iota(jnp.int32, (CHUNK, row0 + BLOCK), 1)
            own = lax.broadcasted_iota(jnp.int32, (CHUNK, row0 + BLOCK), 0) + (row0 + r0)
            now = jnp.where((place <= own) & (place >= start), score[:, old:], MASKED)
            raw[rows, :old] = past
            raw[rows, old:width] = now
            top = past[:, :LANES]
            for low in range(LANES, old, LANES):
                top = jnp.maximum(top, past[:, low : low + LANES])
            for low in range(0, row0 + BLOCK, LANES):
                top = jnp.maximum(top, now[:, low : low + LANES])
            tops[rows, :] = top
        top = jnp.max(tops[...], axis=1, keepdims=True)
        tops[...] = jnp.broadcast_to(top, (BLOCK, LANES))
        for chunk in range(BLOCK // CHUNK):
            r0 = chunk * CHUNK
            rows = slice(r0, r0 + CHUNK)
            top = tops[rows, :]
            total = jnp.zeros((CHUNK, LANES), F32)
            for low in range(0, width, LANES):
                weight = jnp.exp2((raw[rows, low : low + LANES] - top) * (SCALE * LOG2E))
                total = total + weight
                e_ref[row0 + r0 : row0 + r0 + CHUNK, low : low + LANES] = weight.astype(BF16)
            sums[rows, :] = total
        total = jnp.sum(sums[...], axis=1, keepdims=True)
        inv_ref[row0 : row0 + BLOCK, :] = jnp.broadcast_to(1.0 / total, (BLOCK, DH))
        mix[row0 : row0 + BLOCK, :] = mm(
            e_ref[row0 : row0 + BLOCK, :width], values[:width, :], NN
        )
    o_ref[...] = (mix[...] * inv_ref[...]).astype(BF16).reshape(parts, seg, DH)


def attend(query, content_shift, position_shift, keys, values, table_rev, info, cuts):
    parts, group, seg, cols = query.shape
    rows = keys.shape[2]
    queries, key_count, heads = parts * seg, parts * rows, cols // DH
    by_head = lambda size: pl.BlockSpec((parts, None, size, DH), lambda s, h: (0, s, 0, h))
    grid_spec = pl.GridSpec(
        grid=(group, heads),
        in_specs=[
            by_head(seg),
            pl.BlockSpec((1, DH), lambda s, h: (0, h)),
            pl.BlockSpec((1, DH), lambda s, h: (0, h)),
            by_head(rows),
            by_head(rows),
            pl.BlockSpec((key_count, DH), lambda s, h: (0, h)),
            pl.BlockSpec((None, queries, LANES), lambda s, h: (s, 0, 0)),
        ],
        out_specs=[
            pl.BlockSpec((None, None, queries, key_count), lambda s, h: (s, h, 0, 0)),
            pl.BlockSpec((None, None, queries, DH), lambda s, h: (s, h, 0, 0)),
            by_head(seg),
            by_head(seg),
            by_head(seg),
        ],
        scratch_shapes=[
            pltpu.VMEM((key_count, DH), BF16),
            pltpu.VMEM((key_count, DH), BF16),
            pltpu.VMEM((BLOCK, key_count), F32),
            pltpu.VMEM((BLOCK, key_count), F32),
            pltpu.VMEM((queries, DH), F32),
            pltpu.VMEM((BLOCK, LANES), F32),
            pltpu.VMEM((BLOCK, LANES), F32),
        ],
    )
    small = jax.ShapeDtypeStruct((parts, group, seg, cols), BF16)
    return pl.pallas_call(
        functools.partial(attend_kernel, cuts),
        grid_spec=grid_spec,
        out_shape=[
            jax.ShapeDtypeStruct((group, heads, queries, key_count), BF16),
            jax.ShapeDtypeStruct((group, heads, queries, DH), F32),
            small,
            small,
            small,
        ],
        compiler_params=pltpu.CompilerParams(
            dimension_semantics=("arbitrary", "arbitrary"), vmem_limit_bytes=VMEM_LIMIT
        ),
        cost_estimate=cost(40),
        name="attend",
    )(query, content_shift, position_shift, keys, values, table_rev, info)


def pull_kernel(
    cuts, e_ref, inv_ref, o_ref, g_ref, cq_ref, pq_ref, k_ref, v_ref, t_ref,
    dq_ref, dk_ref, dv_ref, ks_ref, vs_ref, dt_ref, sums_ref,
    keys, values, grad, prob, part, score, lean, key_sum, value_sum,
):
    stream = pl.program_id(1)
    parts, seg, _ = g_ref.shape
    queries = parts * seg
    old = parts * (cuts[0] + cuts[1])
    in_place_order(k_ref, keys, cuts)
    in_place_order(v_ref, values, cuts)
    grad[...] = (g_ref[...].reshape(queries, DH).astype(F32) * inv_ref[...]).astype(BF16)
    attended = o_ref[...].reshape(queries, DH)
    content_q = cq_ref[...].reshape(queries, DH)
    position_q = pq_ref[...].reshape(queries, DH)

    @pl.when(stream == 0)
    def _():
        dt_ref[...] = jnp.zeros_like(dt_ref)
        sums_ref[...] = jnp.zeros_like(sums_ref)

    key_sum[...] = jnp.zeros_like(key_sum)
    value_sum[...] = jnp.zeros_like(value_sum)
    content_total = jnp.zeros((1, DH), F32)
    position_total = jnp.zeros((1, DH), F32)
    query_total = jnp.zeros((1, DH), F32)
    flip = flip_matrix(BF16)
    turn = lambda rows: mm(flip, rows, NN).astype(BF16)
    for block in range(queries // BLOCK):
        row0 = block * BLOCK
        width = old + row0 + BLOCK
        skip = queries - BLOCK - row0
        rows = slice(row0, row0 + BLOCK)
        grad_back = turn(grad[rows, :])
        dots_back = jnp.sum(
            grad_back.astype(F32) * turn(attended[rows]).astype(F32), axis=1, keepdims=True
        )
        content_back = turn(content_q[rows])
        position_back = turn(position_q[rows])
        prob[:, :width] = mm(grad_back, values[:width, :], NT)
        both = mm(jnp.concatenate([flip, grad[rows, :].T], axis=0), e_ref[rows, :width], NN)
        part[:, :width] = both[:BLOCK]
        value_sum[:, :width] += both[BLOCK:]
        for chunk in range(BLOCK // CHUNK):
            r0 = chunk * CHUNK
            mean = dots_back[r0 : r0 + CHUNK, 0:1]
            change = part[r0 : r0 + CHUNK, :width] * (prob[r0 : r0 + CHUNK, :width] - mean)
            score[r0 : r0 + CHUNK, :width] = change.astype(BF16)
            lean[r0 : r0 + CHUNK, :width] = lean_right(change, r0).astype(BF16)
        content_grad = (mm(score[:, :width], keys[:width, :], NN) * SCALE).astype(BF16).astype(F32)
        position_grad = (
            (mm(lean[:, :width], t_ref[skip : skip + width, :], NN) * SCALE)
            .astype(BF16)
            .astype(F32)
        )
        query_grad = turn((content_grad + position_grad).astype(BF16))
        content_total += jnp.sum(content_grad, axis=0, keepdims=True)
        position_total += jnp.sum(position_grad, axis=0, keepdims=True)
        query_total += jnp.sum(query_grad.astype(F32), axis=0, keepdims=True)
        dq_ref[rows, :] = query_grad
        key_sum[:, :width] += mm(content_back, score[:, :width], TN)
        dt_ref[:, skip : skip + width] += mm(position_back, lean[:, :width], TN) * SCALE
    key_cols = (key_sum[...] * SCALE).astype(BF16)
    value_cols = value_sum[...].astype(BF16)
    dk_ref[...] = key_cols
    dv_ref[...] = value_cols
    ks_ref[...] = (key_sum[:, old:] * SCALE).T.astype(BF16)
    vs_ref[...] = value_sum[:, old:].T.astype(BF16)
    ones = jnp.ones((8, key_cols.shape[1]), BF16)
    key_total = mm(ones, key_cols, NT)[0:1]
    value_total = mm(ones, value_cols, NT)[0:1]
    sums_ref[...] += jnp.concatenate(
        [
            content_total,
            position_total,
            query_total,
            key_total,
            value_total,
            jnp.zeros((3, DH), F32),
        ],
        axis=0,
    )


def pull(head, weights, inverse, attended, out_grad, content_q, position_q, keys, values, table_rev, cuts):
    parts, group, seg, cols = out_grad.shape
    rows = keys.shape[2]
    queries, key_count = parts * seg, parts * rows
    by_head = lambda size: pl.BlockSpec((parts, None, size, DH), lambda h, s: (0, s, 0, head))
    by_row = lambda: pl.BlockSpec((None, queries, DH), lambda h, s: (s, 0, h))
    by_place = lambda: pl.BlockSpec((None, DH, key_count), lambda h, s: (s, h, 0))
    grid_spec = pl.GridSpec(
        grid=(1, group),
        in_specs=[
            pl.BlockSpec((None, None, queries, key_count), lambda h, s: (s, head, 0, 0)),
            pl.BlockSpec((None, None, queries, DH), lambda h, s: (s, head, 0, 0)),
            by_head(seg),
            by_head(seg),
            by_head(seg),
            by_head(seg),
            by_head(rows),
            by_head(rows),
            pl.BlockSpec((key_count, DH), lambda h, s: (0, head)),
        ],
        out_specs=[
            by_row(),
            by_place(),
            by_place(),
            by_row(),
            by_row(),
            pl.BlockSpec((None, DH, key_count), lambda h, s: (h, 0, 0)),
            pl.BlockSpec((None, 8, DH), lambda h, s: (h, 0, 0)),
        ],
        scratch_shapes=[
            pltpu.VMEM((key_count, DH), BF16),
            pltpu.VMEM((key_count, DH), BF16),
            pltpu.VMEM((queries, DH), BF16),
            pltpu.VMEM((BLOCK, key_count), F32),
            pltpu.VMEM((BLOCK, key_count), F32),
            pltpu.VMEM((BLOCK, key_count), BF16),
            pltpu.VMEM((BLOCK, key_count), BF16),
            pltpu.VMEM((DH, key_count), F32),
            pltpu.VMEM((DH, key_count), F32),
        ],
    )
    return pl.pallas_call(
        functools.partial(pull_kernel, cuts),
        grid_spec=grid_spec,
        out_shape=[
            jax.ShapeDtypeStruct((group, queries, DH), BF16),
            jax.ShapeDtypeStruct((group, DH, key_count), BF16),
            jax.ShapeDtypeStruct((group, DH, key_count), BF16),
            jax.ShapeDtypeStruct((group, queries, DH), BF16),
            jax.ShapeDtypeStruct((group, queries, DH), BF16),
            jax.ShapeDtypeStruct((1, DH, key_count), F32),
            jax.ShapeDtypeStruct((1, 8, DH), F32),
        ],
        compiler_params=pltpu.CompilerParams(
            dimension_semantics=("arbitrary", "arbitrary"), vmem_limit_bytes=VMEM_LIMIT
        ),
        cost_estimate=cost(39),
        name="pull",
    )(weights, inverse, attended, out_grad, content_q, position_q, keys, values, table_rev)


def project_kernel(
    cuts, rows_ref, gain_ref, shift_ref, w_ref, old_ref, mem_ref, seg_ref, q_ref, k_ref, v_ref, normed
):
    rows, width = rows_ref.shape
    cols = k_ref.shape[1]
    step = 32
    for low in range(0, rows, step):
        wide = rows_ref[low : low + step, :].astype(F32)
        centred = wide - jnp.mean(wide, axis=1, keepdims=True)
        rate = lax.rsqrt(jnp.mean(centred * centred, axis=1, keepdims=True) + EPSILON)
        normed[low : low + step, :] = (centred * rate * gain_ref[...] + shift_ref[...]).astype(BF16)
    cut = cuts[0] + cuts[1]
    old_ref[...] = normed[: cuts[0], :]
    mem_ref[...] = normed[cuts[0] : cut, :]
    seg_ref[...] = normed[cut:, :]
    q_ref[...] = mm(normed[cut:, :], w_ref[:, :cols], NN)
    k_ref[...] = mm(normed[...], w_ref[:, cols : 2 * cols], NN).astype(BF16)
    v_ref[...] = mm(normed[...], w_ref[:, 2 * cols : 3 * cols], NN).astype(BF16)


def project(rows_all, gain, shift, columns, cuts):
    parts, group, each, width = rows_all.shape
    cols = columns.shape[1] // 4
    block = lambda size, wide: pl.BlockSpec((None, None, size, wide), lambda p, s: (p, s, 0, 0))
    placed = lambda size: pl.BlockSpec((None, size, width), lambda p, s: (s, p, 0))
    whole = lambda *shape: pl.BlockSpec(shape, lambda p, s: (0,) * len(shape))
    shape = lambda size, kind: jax.ShapeDtypeStruct((parts, group, size, cols), kind)
    return pl.pallas_call(
        functools.partial(project_kernel, cuts),
        grid_spec=pl.GridSpec(
            grid=(parts, group),
            in_specs=[
                block(each, width),
                whole(1, width),
                whole(1, width),
                whole(width, 4 * cols),
            ],
            out_specs=[placed(size) for size in cuts]
            + [block(cuts[2], cols), block(each, cols), block(each, cols)],
            scratch_shapes=[pltpu.VMEM((each, width), BF16)],
        ),
        out_shape=[jax.ShapeDtypeStruct((group, parts * size, width), BF16) for size in cuts]
        + [shape(cuts[2], F32), shape(each, BF16), shape(each, BF16)],
        compiler_params=pltpu.CompilerParams(
            dimension_semantics=("arbitrary", "arbitrary"), vmem_limit_bytes=VMEM_LIMIT
        ),
        cost_estimate=cost(17),
        name="project",
    )(rows_all, gain, shift, columns)


def gelu_both(x):
    near = jnp.abs(x)
    t = 1.0 / (1.0 + (0.3275911 * math.sqrt(0.5)) * near)
    bell = jnp.exp2((x * x) * (-0.5 * LOG2E))
    tail = 0.5 * 1.061405429
    for factor in (-1.453152027, 1.421413741, -0.284496736, 0.254829592):
        tail = tail * t + 0.5 * factor
    tail = tail * t * bell
    below = jnp.where(x < 0.0, tail, 1.0 - tail)
    return x * below, below + x * bell * (1.0 / math.sqrt(2.0 * math.pi))


def forward_back_kernel(
    last, parts, pair, n_ref, c_ref, *rest,
):
    up_refs, down_refs, shift_ref = rest[:parts], rest[parts : parts + pair], rest[parts + pair]
    rest = rest[parts + pair + 1 :]
    if last:
        part_in, grad_in, part_out, part_far, grad_out, grad_far, late_ref, sums_ref = rest[:8]
        pre, slope, hidden, act, up_out, down_out, sems, part_ref, grad_ref = rest[8:]
    else:
        part_ref, grad_ref, late_ref, sums_ref = rest[:4]
        pre, slope, hidden, act, up_out, down_out, sems = rest[4:]
    tile = pl.program_id(0)
    tiles = pl.num_programs(0)
    cols, units = up_refs[0].shape
    unit_cols, width = down_refs[0].shape
    rows = n_ref.shape[0]
    slot = lax.rem(tile, 2)
    up_weight = jnp.concatenate([ref[...] for ref in up_refs], axis=0)
    down_weight = jnp.concatenate([ref[...] for ref in down_refs], axis=0)

    def copies(at, index):
        return (
            pltpu.make_async_copy(
                up_out.at[at],
                late_ref.at[:, pl.ds(0, cols), pl.ds(pl.multiple_of(index * units, units), units)],
                sems.at[at, 0],
            ),
            pltpu.make_async_copy(
                down_out.at[at],
                late_ref.at[pl.ds(index * pair, pair), pl.ds(cols, unit_cols), :],
                sems.at[at, 1],
            ),
        )

    @pl.when(tile == 0)
    def _():
        if last:
            part_ref[...] = part_in[...]
            grad_ref[...] = grad_in[...]
        else:
            part_ref[...] = jnp.zeros_like(part_ref)
            grad_ref[...] = jnp.zeros_like(grad_ref)

    pre[...] = mm(n_ref[...], up_weight, NN)
    slope[...] = mm(c_ref[...], down_weight, NT)
    for low in range(0, rows, 16):
        some = slice(low, low + 16)
        value, change = gelu_both(pre[some, :] + shift_ref[...])
        hidden[some, :] = value.astype(BF16)
        act[some, :] = (change * slope[some, :]).astype(BF16)
    part_ref[...] += mm(hidden[...], down_weight, NN)
    grad_ref[...] += mm(act[...], up_weight, NT)
    sums_ref[...] = jnp.sum(act[...].astype(F32), axis=0, keepdims=True)

    @pl.when(tile >= 2)
    def _():
        for copy in copies(slot, tile - 2):
            copy.wait()

    up_out[slot] = mm(n_ref[...], act[...], TN).astype(BF16).reshape(parts, cols, units)
    down_out[slot] = mm(hidden[...], c_ref[...], TN).astype(BF16).reshape(pair, unit_cols, width)
    for copy in copies(slot, tile):
        copy.start()

    @pl.when(tile == tiles - 1)
    def _():
        if last:
            part_out[...] = part_ref[: rows // 2, :]
            part_far[...] = part_ref[rows // 2 :, :].astype(BF16)
            grad_out[...] = grad_ref[: rows // 2, :]
            grad_far[...] = grad_ref[rows // 2 :, :].astype(BF16)
        for copy in (copies(1 - slot, tile - 1) if parts > pair else ()) + copies(slot, tile):
            copy.wait()


def forward_back(normed, cot, gathered, shift, carry):
    parts, _, width = gathered.shape
    rows = normed.shape[0]
    cols = width // parts
    unit_cols = shift.shape[1] // parts
    pair = 2
    units = pair * unit_cols
    last = len(carry) > 0
    one = pl.Buffered(1)
    whole = lambda *shape: pl.BlockSpec(shape, lambda t: (0,) * len(shape), pipeline_mode=one)
    up = lambda p: pl.BlockSpec((None, cols, units), lambda t: (p, 0, t))
    down = lambda i: pl.BlockSpec(
        (None, unit_cols, width), lambda t: (t * pair + i, cols // unit_cols, 0)
    )
    if last:
        sums = [((rows // 2, width), F32), ((rows // 2, width), BF16)] * 2
    else:
        sums = [((rows, width), F32)] * 2
    return pl.pallas_call(
        functools.partial(forward_back_kernel, last, parts, pair),
        grid_spec=pl.GridSpec(
            grid=(parts // pair,),
            in_specs=[
                whole(rows, width),
                whole(rows, width),
            ]
            + [up(p) for p in range(parts)]
            + [down(i) for i in range(pair)]
            + [pl.BlockSpec((1, units), lambda t: (0, t))]
            + [whole(rows, width) for _ in carry],
            out_specs=[whole(*shape) for shape, _ in sums]
            + [
                pl.BlockSpec(memory_space=pl.ANY),
                pl.BlockSpec((1, units), lambda t: (0, t)),
            ],
            scratch_shapes=[
                pltpu.VMEM((rows, units), F32),
                pltpu.VMEM((rows, units), F32),
                pltpu.VMEM((rows, units), BF16),
                pltpu.VMEM((rows, units), BF16),
                pltpu.VMEM((2, parts, cols, units), BF16),
                pltpu.VMEM((2, pair, unit_cols, width), BF16),
                pltpu.SemaphoreType.DMA((2, 2)),
            ]
            + [pltpu.VMEM((rows, width), F32) for _ in carry],
        ),
        out_shape=[jax.ShapeDtypeStruct(shape, kind) for shape, kind in sums]
        + [
            jax.ShapeDtypeStruct((parts, cols + unit_cols, width), BF16),
            jax.ShapeDtypeStruct((1, parts * unit_cols), F32),
        ],
        compiler_params=pltpu.CompilerParams(
            dimension_semantics=("arbitrary",), vmem_limit_bytes=VMEM_LIMIT
        ),
        cost_estimate=cost(29),
        name="forward_back",
    )(normed, cot, *[gathered] * (parts + pair), shift, *carry)


def leave_kernel(a_ref, s_ref, w_ref, shift_ref, gain_ref, bias_ref, flat_ref, m_ref, n_ref):
    parts = a_ref.shape[0]
    flat_ref[...] = jnp.concatenate([a_ref[part] for part in range(parts)], axis=1)
    m_ref[...] = s_ref[...].astype(F32) + (mm(flat_ref[...], w_ref[...], NN) + shift_ref[...])
    step = 16
    for low in range(0, m_ref.shape[0], step):
        unit, _ = standardise(m_ref[low : low + step, :])
        n_ref[low : low + step, :] = (unit * gain_ref[...] + bias_ref[...]).astype(BF16)


def leave(mixed_heads, segment, base, weight, shift, gain, bias):
    parts, group, seg, cols = mixed_heads.shape
    width = parts * cols
    rows = lambda: pl.BlockSpec((None, seg, width), lambda s: (s, 0, 0))
    vector = lambda: pl.BlockSpec((1, width), lambda s: (0, 0))
    shape = lambda kind: jax.ShapeDtypeStruct((group, seg, width), kind)
    return pl.pallas_call(
        leave_kernel,
        grid_spec=pl.GridSpec(
            grid=(group,),
            in_specs=[
                pl.BlockSpec((parts, None, seg, cols), lambda s: (0, s, 0, 0)),
                pl.BlockSpec((None, seg, width), lambda s: (s + base, 0, 0)),
                pl.BlockSpec((width, width), lambda s: (0, 0)),
                vector(),
                vector(),
                vector(),
            ],
            out_specs=[rows(), rows(), rows()],
        ),
        out_shape=[shape(BF16), shape(F32), shape(BF16)],
        compiler_params=pltpu.CompilerParams(vmem_limit_bytes=VMEM_LIMIT),
        cost_estimate=cost(6),
        name="leave",
    )(mixed_heads, segment, weight, shift, gain, bias)


def enter_kernel(
    m_ref, g_ref, far_ref, c_ref, w_ref, gain_ref, mg_ref, b_ref, a_ref, sums_ref
):
    @pl.when(pl.program_id(0) == 0)
    def _():
        sums_ref[...] = jnp.zeros_like(sums_ref)

    parts = a_ref.shape[0]
    rows, width = m_ref.shape
    step = 32
    total = [jnp.zeros((1, width), F32) for _ in range(4)]
    for low in range(0, rows, step):
        at = slice(low, low + step)
        unit, rate = standardise(m_ref[at, :])
        grad = g_ref[at, :] + far_ref[at, :].astype(F32)
        cot = c_ref[at, :].astype(F32)
        middle_grad = cot + standardise_back(unit, rate, grad, gain_ref[...])
        branch = middle_grad.astype(BF16)
        mg_ref[at, :] = middle_grad
        b_ref[at, :] = branch
        for i, value in enumerate((branch.astype(F32), grad * unit, grad, cot)):
            total[i] = total[i] + jnp.sum(value, axis=0, keepdims=True)
    sums_ref[...] += jnp.concatenate(total + [jnp.zeros((4, width), F32)], axis=0)
    for part in range(parts):
        low = part * a_ref.shape[2]
        weight = w_ref[low : low + a_ref.shape[2], :]
        a_ref[part] = mm(b_ref[...], weight, NT).astype(BF16)


def enter(middle, grad, far, cot, base, weight, gain, parts):
    group, seg, width = middle.shape
    cols = width // parts
    rows = lambda: pl.BlockSpec((None, seg, width), lambda s: (s, 0, 0))
    later = lambda: pl.BlockSpec((None, seg, width), lambda s: (s + base, 0, 0))
    shape = lambda kind: jax.ShapeDtypeStruct((group, seg, width), kind)
    return pl.pallas_call(
        enter_kernel,
        grid_spec=pl.GridSpec(
            grid=(group,),
            in_specs=[
                rows(),
                later(),
                later(),
                later(),
                pl.BlockSpec((width, width), lambda s: (0, 0)),
                pl.BlockSpec((1, width), lambda s: (0, 0)),
            ],
            out_specs=[
                rows(),
                rows(),
                pl.BlockSpec((parts, None, seg, cols), lambda s: (0, s, 0, 0)),
                pl.BlockSpec((8, width), lambda s: (0, 0)),
            ],
        ),
        out_shape=[
            shape(F32),
            shape(BF16),
            jax.ShapeDtypeStruct((parts, group, seg, cols), BF16),
            jax.ShapeDtypeStruct((8, width), F32),
        ],
        compiler_params=pltpu.CompilerParams(
            dimension_semantics=("arbitrary",), vmem_limit_bytes=VMEM_LIMIT
        ),
        cost_estimate=cost(7),
        name="enter",
    )(middle, grad, far, cot, weight, gain)


def compress_kernel(low, rows_ref, w_ref, shift_ref, out_ref, wide):
    count = out_ref.shape[0]
    cols = out_ref.shape[1]
    blocks = wide.shape[0]
    for at in range(blocks):
        wide[at] = rows_ref[low : low + 3 * count, at * LANES : (at + 1) * LANES].astype(F32)
    total = jnp.broadcast_to(shift_ref[...], (count, cols))
    for k in range(3):
        every = jnp.concatenate(
            [wide[at, pl.ds(k, count, stride=3), :] for at in range(blocks)], axis=1
        ).astype(BF16)
        total = total + mm(every, w_ref[:, k * cols : (k + 1) * cols], NN)
    out_ref[...] = total.astype(BF16)


def compress(rows_all, columns, shift, low, count):
    parts, group, each, width = rows_all.shape
    cols = columns.shape[1] // 3
    return pl.pallas_call(
        functools.partial(compress_kernel, low),
        grid_spec=pl.GridSpec(
            grid=(parts, group),
            in_specs=[
                pl.BlockSpec((None, None, each, width), lambda p, s: (p, s, 0, 0)),
                pl.BlockSpec((width, 3 * cols), lambda p, s: (0, 0)),
                pl.BlockSpec((1, cols), lambda p, s: (0, 0)),
            ],
            out_specs=pl.BlockSpec((None, None, count, cols), lambda p, s: (p, s, 0, 0)),
            scratch_shapes=[pltpu.VMEM((width // LANES, 3 * count, LANES), F32)],
        ),
        out_shape=jax.ShapeDtypeStruct((parts, group, count, cols), BF16),
        compiler_params=pltpu.CompilerParams(
            dimension_semantics=("arbitrary", "arbitrary"), vmem_limit_bytes=VMEM_LIMIT
        ),
        cost_estimate=cost(6.5),
        name="compress",
    )(rows_all, columns, shift)


def lay_out_kernel(
    parts, unit_cols, core_ref, a_ref, b_ref, c_ref, d_ref, up_ref, down_ref
):
    flipped = core_ref[0] == 1
    for half, (mine_ref, far_ref) in enumerate(((a_ref, c_ref), (b_ref, d_ref))):
        mine, far = mine_ref[...].astype(F32), far_ref[...].astype(F32)
        for core, value in enumerate(
            (jnp.where(flipped, far, mine), jnp.where(flipped, mine, far))
        ):
            for part in range(parts):
                at = ((part * 2 + core) * 2 + half) * unit_cols
                up_ref[:, at : at + unit_cols] = value[
                    0, :, part * unit_cols : (part + 1) * unit_cols
                ]
            down_ref[2 * core + half] = value[1]


def lay_out(core, mine, far, parts):
    _, rows, width = mine[0].shape
    step = rows // 4 if rows % 64 == 0 else rows
    half = lambda: pl.BlockSpec((2, step, width), lambda r, *_: (0, r, 0))
    return pl.pallas_call(
        functools.partial(lay_out_kernel, parts, rows),
        grid_spec=pltpu.PrefetchScalarGridSpec(
            num_scalar_prefetch=1,
            grid=(rows // step,),
            in_specs=[half(), half(), half(), half()],
            out_specs=[
                pl.BlockSpec((step, 4 * width), lambda r, *_: (r, 0)),
                pl.BlockSpec((4, step, width), lambda r, *_: (0, r, 0)),
            ],
        ),
        out_shape=[
            jax.ShapeDtypeStruct((rows, 4 * width), F32),
            jax.ShapeDtypeStruct((4, rows, width), F32),
        ],
        compiler_params=pltpu.CompilerParams(vmem_limit_bytes=VMEM_LIMIT),
        cost_estimate=cost(4),
        name="lay_out",
    )(core.reshape(1), *mine, *far)


def lay_squares_kernel(where_ref, mine_ref, far_ref, *out_refs):
    parts = mine_ref.shape[0]
    cols = mine_ref.shape[2] // len(out_refs)
    own = pl.program_id(0) == where_ref[0]
    for part in range(parts):
        value = jnp.where(own, mine_ref[part].astype(F32), far_ref[part].astype(F32))
        for at, out_ref in enumerate(out_refs):
            out_ref[:, part * cols : (part + 1) * cols] = value[:, at * cols : (at + 1) * cols]


def lay_squares(where, mine, far):
    layers, parts, rows, wide = mine.shape
    width = parts * wide // 4
    pieces = pl.BlockSpec((None, parts, rows, wide), lambda c, z, at: (z ^ at[1], 0, 0, 0))
    return pl.pallas_call(
        lay_squares_kernel,
        grid_spec=pltpu.PrefetchScalarGridSpec(
            num_scalar_prefetch=1,
            grid=(2, layers),
            in_specs=[pieces, pieces],
            out_specs=[
                pl.BlockSpec((rows, width), lambda c, z, at: (c * layers + z, 0)) for _ in range(4)
            ],
        ),
        out_shape=[jax.ShapeDtypeStruct((2 * layers * rows, width), F32) for _ in range(4)],
        compiler_params=pltpu.CompilerParams(vmem_limit_bytes=VMEM_LIMIT),
        cost_estimate=cost(2.5),
        name="lay_squares",
    )(where, mine, far)


def settle_kernel(heads, me_ref, old_ref, mem_ref, seg_ref, *rest):
    q_refs, k_refs, v_refs, ks_refs, vs_refs, dt_refs, sums_refs = (
        rest[i * heads : (i + 1) * heads] for i in range(7)
    )
    w_ref, table_ref, gain_ref, shift_ref, small_ref, part_ref, out_ref, row_ref, total = rest[
        7 * heads :
    ]
    stream = pl.program_id(0)
    parts, rows, wide = out_ref.shape
    cols = wide // 4
    width = parts * cols

    @pl.when(stream == 0)
    def _():
        total[...] = jnp.zeros_like(total)

    low = old_ref.shape[0]
    high = low + mem_ref.shape[0]
    pair = lambda first, last: [ref[:, first:last] for ref in (*k_refs, *v_refs)]
    total[...] += mm(
        jnp.concatenate([ref[...].T for ref in q_refs] + pair(high, high + seg_ref.shape[0]), axis=0),
        seg_ref[...],
        NN,
    )
    total[cols:, :] += mm(jnp.concatenate(pair(low, high), axis=0), mem_ref[...], NN)
    total[cols:, :] += mm(jnp.concatenate(pair(0, low), axis=0), old_ref[...], NN)
    three = jnp.concatenate([ref[...] for ref in (*q_refs, *ks_refs, *vs_refs)], axis=1)
    part = mm(three, w_ref[:, : 3 * cols], NT).astype(BF16)
    part_ref[...] = part.reshape(part_ref.shape)

    @pl.when(stream == pl.num_programs(0) - 1)
    def _():
        places = jnp.concatenate([ref[0].astype(BF16) for ref in dt_refs], axis=0)
        rel = mm(places, table_ref[...], NN)
        line = lambda row: jnp.concatenate(
            [ref[0, row : row + 1, :] for ref in sums_refs], axis=1
        )
        row_sums = jnp.concatenate([line(2), line(3), line(4)], axis=1)
        pieces, rest = [], row_sums
        for _ in range(3):
            pieces.append(rest.astype(BF16))
            rest = rest - pieces[-1].astype(F32)
        pieces = jnp.concatenate(pieces + [jnp.zeros((13, 3 * cols), BF16)], axis=0)
        shift_grad = jnp.sum(mm(pieces, w_ref[:, : 3 * cols], NT), axis=0, keepdims=True)
        weight = w_ref[:, : 3 * cols].astype(F32)
        along = jnp.sum(weight.T * total[...], axis=0, keepdims=True)
        gain_grad = (along - shift_ref[...] * shift_grad) / gain_ref[...]
        for at in range(parts):
            low, high = at * cols, (at + 1) * cols
            out_ref[at, :, : 3 * cols] = total[:, low:high].T.astype(BF16)
            out_ref[at, :, 3 * cols :] = rel[:, low:high].T.astype(BF16)
            mine = (me_ref[0] == at).astype(F32)
            none = jnp.zeros((1, 2 * cols), F32)
            first = jnp.concatenate([gain_grad[:, low:high], shift_grad[:, low:high], none], axis=1)
            second = jnp.concatenate([none, mine * line(0), mine * line(1)], axis=1)
            added = jnp.concatenate([first, second, jnp.zeros((14, wide), F32)], axis=0)
            row_ref[at] = (small_ref[at] + added).astype(BF16)


def settle(me, normed, grads, columns, table, gain, shift, small, parts):
    group, queries, width = normed[2].shape
    cols = width // parts
    wide = 4 * cols
    by_kind = list(zip(*grads))
    block = lambda array: pl.BlockSpec((None, *array.shape[1:]), lambda s, *_: (s, 0, 0))
    whole = lambda *shape: pl.BlockSpec(
        shape, lambda s, *_: (0,) * len(shape), pipeline_mode=pl.Buffered(1)
    )
    return pl.pallas_call(
        functools.partial(settle_kernel, len(grads)),
        grid_spec=pltpu.PrefetchScalarGridSpec(
            num_scalar_prefetch=1,
            grid=(group,),
            in_specs=[block(rows) for rows in normed]
            + [block(each) for kind in by_kind[:5] for each in kind]
            + [whole(*each.shape) for kind in by_kind[5:] for each in kind]
            + [
                whole(*columns.shape),
                whole(*table.shape),
                whole(1, width),
                whole(1, width),
                whole(*small.shape),
            ],
            out_specs=[
                pl.BlockSpec((parts, None, queries // parts, width), lambda s, *_: (0, s, 0, 0)),
                whole(parts, cols, wide),
                whole(parts, 16, wide),
            ],
            scratch_shapes=[pltpu.VMEM((3 * cols, width), F32)],
        ),
        out_shape=[
            jax.ShapeDtypeStruct((parts, group, queries // parts, width), BF16),
            jax.ShapeDtypeStruct((parts, cols, wide), BF16),
            jax.ShapeDtypeStruct((parts, 16, wide), BF16),
        ],
        compiler_params=pltpu.CompilerParams(
            dimension_semantics=("arbitrary",), vmem_limit_bytes=VMEM_LIMIT
        ),
        cost_estimate=cost(14),
        name="settle",
    )(
        me.reshape(1), *normed, *[each for kind in by_kind for each in kind], columns, table, gain, shift,
        small,
    )


def standardise(rows):
    mean = jnp.mean(rows, axis=-1, keepdims=True)
    centred = rows - mean
    rate = lax.rsqrt(jnp.mean(centred * centred, axis=-1, keepdims=True) + EPSILON)
    return centred * rate, rate


def standardise_back(unit, rate, grad, gain):
    scaled = grad * gain
    mean = jnp.mean(scaled, axis=-1, keepdims=True)
    along = jnp.mean(scaled * unit, axis=-1, keepdims=True)
    return rate * (scaled - mean - unit * along)


def sinusoid_reversed(rows, width):
    positions = (rows - 1 - jnp.arange(rows, dtype=jnp.int32)).astype(F32)[:, None]
    frequency = jnp.exp(
        jnp.arange(width // 2, dtype=F32) * (-2.0 * math.log(10000.0) / width)
    )
    angles = positions * frequency[None, :]
    return jnp.concatenate([jnp.sin(angles), jnp.cos(angles)], axis=1).astype(BF16)


def dot(left, right):
    return mm(left, right, NN)


def swap(value):
    return lax.ppermute(value, "core", [(0, 1), (1, 0)])


def exchange(blocks, name, axis=0):
    count = lax.axis_size(name)
    me = lax.axis_index(name)
    block = lambda at: lax.dynamic_index_in_dim(blocks, at, axis, keepdims=False)
    return [block(me)] + [
        lax.ppermute(block(me ^ apart), name, [(i, i ^ apart) for i in range(count)])
        for apart in range(1, count)
    ]


def spread(block, name):
    count = lax.axis_size(name)
    return jnp.stack(
        [block]
        + [
            lax.ppermute(block, name, [(i, i ^ apart) for i in range(count)])
            for apart in range(1, count)
        ]
    )


def collect(block, name):
    count = lax.axis_size(name)
    me = lax.axis_index(name)
    found = spread(block, name)
    return jnp.stack(
        [lax.dynamic_index_in_dim(found, me ^ i, 0, keepdims=False) for i in range(count)]
    )


def add_up(arrays, kind=BF16):
    total = arrays[0].astype(F32)
    for array in arrays[1:]:
        total = total + array.astype(F32)
    return total.astype(kind)


def body(
    segment, memory, compressed, eob, reset, ln1_gain, ln1_bias, w_query, w_key, w_value,
    w_out, out_bias, w_rel, bias_content, bias_position, ln2_gain, ln2_bias, w_up, up_bias,
    w_down, down_bias, conv_weight, conv_bias, cotangent,
):
    parts = lax.axis_size("seq")
    layers = lax.axis_size("z")
    core = lax.axis_index("core")
    layer = lax.axis_index("z")
    me = lax.axis_index("seq")
    group, seg, width = segment.shape
    mem, old = memory.shape[1], compressed.shape[1]
    cuts = (old, mem, seg)
    each = old + mem + seg
    keys_in_all = parts * each
    cols = width // parts
    wide = 4 * cols
    own = group * seg
    unit_cols = w_up.shape[1] // (4 * parts)
    barrier = lax.optimization_barrier

    def by_columns(matrices):
        count = matrices.shape[0]
        sent = matrices.reshape(count, cols, parts, cols).transpose(2, 1, 0, 3)
        return sent.reshape(parts, cols, count * cols)

    up_bias_own = lax.dynamic_slice_in_dim(up_bias, core * 2 * unit_cols, 2 * unit_cols, 0)
    vectors = jnp.concatenate(
        [ln1_gain, ln1_bias, out_bias, ln2_gain, ln2_bias, down_bias, up_bias_own]
    )
    vectors = jnp.pad(vectors.reshape(2, wide), ((0, 14), (0, 0)))
    half = cols // 2
    sent = by_columns(jnp.concatenate([jnp.stack([w_query, w_key, w_value, w_rel]), conv_weight]))
    sent = lax.dynamic_slice_in_dim(sent, core * half, half, 1)
    out_half = lax.dynamic_slice_in_dim(w_out, core * half, half, 0)
    sent = jnp.concatenate([sent, jnp.broadcast_to(out_half, (parts, half, width))], axis=2)
    vectors = jnp.pad(vectors, ((0, 0), (0, 3 * cols + width)))
    sent = jnp.concatenate([sent, jnp.broadcast_to(vectors, (parts, *vectors.shape))], axis=1)
    got = lax.all_to_all(sent, "seq", 0, 0, tiled=True)
    spans = [(0, group)]
    local = [
        jnp.concatenate([compressed[low:high], memory[low:high], segment[low:high]], axis=1)
        for low, high in spans
    ]
    rows_all = [lax.all_gather(local[0], "seq")]
    mine = got[:, :half]
    far = swap(mine)
    columns = jnp.stack(
        [jnp.where(core == 0, mine, far), jnp.where(core == 0, far, mine)], axis=1
    ).reshape(width, 7 * cols + width)
    columns, conv_columns, out_full = (
        columns[:, :wide],
        columns[:, wide : 7 * cols],
        columns[:, 7 * cols :],
    )
    vectors = got[:, half : half + 2, :wide].reshape(parts, 2 * wide).astype(F32)
    gain_one, shift_one, out_shift, gain_two, shift_two, down_shift = (
        vectors[:, cols * i : cols * (i + 1)].reshape(1, width) for i in range(6)
    )
    up_shift = vectors[:, 6 * cols :].reshape(parts, 2, unit_cols).transpose(1, 0, 2)
    up_shift = up_shift.reshape(2, 1, parts * unit_cols)
    up_quarters = lax.dynamic_slice_in_dim(
        w_up.reshape(cols, parts, 2, 2, unit_cols), core, 1, 2
    ).reshape(cols, parts, 2, unit_cols)
    up_quarters = [up_quarters[:, :, i].reshape(cols, width) for i in range(2)]
    down_half = lax.dynamic_slice_in_dim(w_down, core * 2 * unit_cols, 2 * unit_cols, 0)
    down_quarters = [down_half[unit_cols * i : unit_cols * (i + 1)] for i in range(2)]
    first = jnp.concatenate([up_quarters[0], down_quarters[0]], axis=0)
    second = jnp.concatenate([up_quarters[1], down_quarters[1]], axis=0)
    cot_own = cotangent.reshape(own, width)
    cot_both = jnp.concatenate([cot_own, swap(cot_own)], axis=0)

    table_rev = sinusoid_reversed(keys_in_all, width)
    proj_rev = dot(table_rev, columns[:, 3 * cols :]).astype(BF16)
    index = jnp.arange(eob.shape[1], dtype=jnp.int32)[None, :]
    opens = jnp.pad(eob, ((0, 0), (1, 0)))[:, :-1] == 1
    start = lax.cummax(jnp.where(opens, index, 0), axis=1)
    shade = jnp.where((start == 0) & (reset[:, None] == 0), 0.0, MASKED)
    info = jnp.stack([start.astype(F32), shade], axis=2)
    info = jnp.pad(info, ((0, 0), (0, 0), (0, LANES - 2)))
    rows_all[0], proj_rev, info, cot_both, table_rev, columns, conv_columns, out_full, *local = barrier(
        (rows_all[0], proj_rev, info, cot_both, table_rev, columns, conv_columns, out_full, *local)
    )
    rows_all = [rows_all[0]] + [lax.all_gather(rows, "seq") for rows in local[1:]]

    kept, heads = [], []
    for batch, (low, high) in enumerate(spans):
        if batch == len(spans) - 1:
            rows_all[batch], first, *heads = barrier((rows_all[batch], first, *heads))
            first = lax.all_gather(first, "seq")
        *normed, query, keys, values = project(rows_all[batch], gain_one, shift_one, columns, cuts)
        second, query = barrier((second, query))
        second = lax.all_gather(second, "seq")
        weights, inverse, mixed_heads, content_q, position_q = attend(
            query,
            bias_content.astype(F32).reshape(1, cols),
            bias_position.astype(F32).reshape(1, cols),
            keys,
            values,
            proj_rev,
            info[low:high],
            cuts,
        )
        kept.append((weights, inverse, mixed_heads, content_q, position_q, keys, values))
        heads.append(lax.all_to_all(mixed_heads, "seq", 0, 0, tiled=True))

    mixed_heads, conv_columns = barrier((mixed_heads, conv_columns))
    packed = compress(
        rows_all[0], conv_columns, conv_bias.astype(F32).reshape(1, cols), old, mem // 3
    )
    packed, *heads = barrier((packed, *heads))

    attended, middle, normed_two = [], [], []
    for (low, high), batch in zip(spans, heads):
        one, two, three = leave(batch, segment, low, out_full, out_shift, gain_two, shift_two)
        attended.append(one.reshape(-1, width))
        middle.append(two)
        normed_two.append(three.reshape(-1, width))
    both = jnp.concatenate(normed_two + [swap(rows) for rows in normed_two], axis=0)
    part, part_grad, late_one, unit_one = forward_back(both, cot_both, first, up_shift[0], ())
    late_one = lax.psum_scatter(
        late_one.reshape(-1, width), "seq", scatter_dimension=0, tiled=True
    )
    part, part_far, part_grad, grad_far, late_two, unit_two = forward_back(
        both, cot_both, second, up_shift[1], (part, part_grad)
    )
    grad_far = swap(grad_far)
    by_stream = lambda rows: rows.reshape(group, seg, width)
    middle_grad, branch_grad, head_grad, sums_two = [], [], [], 0.0
    for (low, high), batch in zip(spans, middle):
        one, two, three, four = enter(
            batch, by_stream(part_grad), by_stream(grad_far), cotangent, low, out_full, gain_two, parts
        )
        middle_grad.append(one)
        branch_grad.append(two.reshape(-1, width))
        three, part_grad = barrier((three, part_grad))
        head_grad.append(lax.all_to_all(three, "seq", 0, 0, tiled=True))
        sums_two = sums_two + four
    result = part + swap(part_far).astype(F32) + down_shift
    output = (jnp.concatenate(middle).reshape(own, width) + result).astype(BF16)
    output = output.reshape(group, seg, width)

    out_shift_grad, gain_two_grad, shift_two_grad, down_shift_grad = (
        sums_two[i].reshape(parts, cols) for i in range(4)
    )
    none = jnp.zeros((parts, 2 * cols), F32)
    unit_sums = jnp.stack(
        [unit_one.reshape(parts, unit_cols), unit_two.reshape(parts, unit_cols)], axis=1
    ).reshape(parts, 2 * unit_cols)
    small = jnp.stack(
        [
            jnp.concatenate([none, out_shift_grad, gain_two_grad], axis=1),
            jnp.concatenate([shift_two_grad, down_shift_grad, none], axis=1),
            jnp.concatenate(
                [jnp.where(core == 0, unit_sums, 0.0), jnp.where(core == 1, unit_sums, 0.0)], axis=1
            ),
        ],
        axis=1,
    )
    small = jnp.pad(small, ((0, 0), (0, 13), (0, 0)))
    weights, inverse, mixed_heads, content_q, position_q, keys, values = kept[0]
    out_grad = mm(jnp.concatenate(attended), jnp.concatenate(branch_grad), TN)
    out_grad = out_grad.astype(BF16).reshape(parts, cols, width)
    late_one, small, out_grad, late_two, output, head_grad = barrier(
        (late_one, small, out_grad, late_two, output, head_grad[0])
    )
    late_two = lax.psum_scatter(
        late_two.reshape(-1, width), "seq", scatter_dimension=0, tiled=True
    )
    late_one = exchange(late_one.reshape(layers, -1, width), "z")
    grads = []
    for head in range(cols // DH):
        grads.append(
            list(
                pull(
                    head, weights, inverse, mixed_heads, head_grad, content_q, position_q, keys,
                    values, proj_rev, cuts,
                )
            )
        )
        if head == 0:
            late_one, head_grad, grads[0][0] = barrier((late_one, head_grad, grads[0][0]))
            late_one = collect(add_up(late_one), "z")
    late_one, late_two, out_grad, grads[-1][0] = barrier(
        (late_one, late_two, out_grad, grads[-1][0])
    )
    late_two = exchange(late_two.reshape(layers, -1, width), "z")
    out_sent = lax.all_to_all(out_grad, "seq", 0, 0, tiled=True)
    seg_part, squares, vectors = settle(
        me, normed, grads, columns, table_rev, gain_one, shift_one, small, parts
    )
    late_two, out_sent, squares = barrier((late_two, out_sent, squares))
    halves = squares.reshape(parts, 2, cols // 2, wide)
    half = lambda at: lax.dynamic_index_in_dim(halves, at, 1, keepdims=False)
    squares = add_up([half(core), swap(half(1 - core))])
    squares, seg_part, vectors, late_two, packed = barrier(
        (squares, seg_part, vectors, late_two, packed)
    )
    squares = exchange(squares.reshape(parts, layers, -1, wide), "z", 1)
    squares = lax.all_to_all(add_up(squares), "seq", 0, 0, tiled=True)
    squares = spread(squares, "z")
    squares_far = swap(squares)
    vectors = lax.all_to_all(vectors, "seq", 0, 0, tiled=True)
    vectors = jnp.sum(vectors.astype(F32), axis=0).astype(BF16)
    out_sent = jnp.sum(out_sent.astype(F32), axis=0).astype(BF16)
    summed = jnp.concatenate([out_sent.reshape(-1, wide), vectors], axis=0)
    summed = lax.psum(summed, ("z", "core")).astype(F32)
    out_w = summed[: cols * width // wide].reshape(cols, width)
    small = summed[cols * width // wide :]
    late_two = collect(add_up(late_two), "z")
    packed = jnp.stack(exchange(packed, "seq"))
    new_compressed = jnp.concatenate(
        [lax.dynamic_index_in_dim(packed, p ^ me, 0, keepdims=False) for p in range(parts)], axis=2
    )
    seg_grad = lax.all_to_all(seg_part, "seq", 0, 0, tiled=True).astype(F32)
    seg_grad = jnp.sum(seg_grad, axis=0).reshape(own, width)
    unit_seg, rate_seg = standardise(segment.reshape(own, width).astype(F32))
    rows_grad = standardise_back(unit_seg, rate_seg, seg_grad, gain_one)
    segment_grad = jnp.concatenate(middle_grad, axis=0) + by_stream(rows_grad)

    halves = [late_one.reshape(2, unit_cols, width), late_two.reshape(2, unit_cols, width)]
    up_w, down_w = lay_out(core, halves, [swap(rows) for rows in halves], parts)
    down_w = down_w.reshape(4 * unit_cols, width)
    squares, squares_far, out_w, small, output, segment_grad, new_compressed, up_w, down_w = barrier(
        (squares, squares_far, out_w, small, output, segment_grad, new_compressed, up_w, down_w)
    )
    query_w, key_w, value_w, rel_w = lay_squares(jnp.stack([core, layer]), squares, squares_far)
    piece = lambda row, i: small[row, cols * i : cols * (i + 1)]
    return (
        output,
        segment_grad,
        piece(0, 0),
        piece(0, 1),
        query_w,
        key_w,
        value_w,
        out_w,
        piece(0, 2),
        rel_w,
        piece(1, 2),
        piece(1, 3),
        piece(0, 3),
        piece(1, 0),
        up_w,
        small[2],
        down_w,
        piece(1, 1),
        new_compressed,
    )


def solution(mesh):
    dp = mesh.shape["dp"]
    cores = jax.sharding.Mesh(
        mesh.devices.reshape(dp // 2, 2, mesh.shape["seq"]), ("z", "core", "seq")
    )
    rows = P(("z", "core"), "seq", None)
    shard, matrix = P("seq"), P("seq", None)
    return jax.shard_map(
        body,
        mesh=cores,
        in_specs=(
            rows, rows, rows, P(("z", "core"), None), P(("z", "core")), shard, shard, matrix,
            matrix, matrix, matrix, shard, matrix, shard, shard, shard, shard, matrix, shard,
            matrix, shard, P(None, "seq", None), shard, rows,
        ),
        out_specs=(
            rows, rows, shard, shard, matrix, matrix, matrix, matrix, shard, matrix, shard,
            shard, shard, shard, matrix, shard, matrix, shard, rows,
        ),
        check_vma=False,
    )
```

```python
import functools
import math

import jax
import jax.numpy as jnp
from jax import lax
from jax.experimental import pallas as pl
from jax.experimental.pallas import tpu as pltpu
from jax.sharding import PartitionSpec as P

HEADS = 8
DH = 128
EPSILON = 1e-05
MASKED = -1e30
LANES = 128
BLOCK = 256
CHUNK = 16
VMEM_LIMIT = 60 * 2**20
SCALE = 1.0 / math.sqrt(DH)
LOG2E = 1.4426950408889634
BF16 = jnp.bfloat16
F32 = jnp.float32


def cost(microseconds):
    return pl.CostEstimate(flops=int(microseconds * 1.15e7), bytes_accessed=0, transcendentals=0)


def mm(left, right, dims):
    return lax.dot_general(left, right, (dims, ((), ())), preferred_element_type=F32)


NN = ((1,), (0,))
NT = ((1,), (1,))
TN = ((0,), (0,))


def lean_left(block, first_row, fill_columns):
    columns = block.shape[1] // LANES
    far = BLOCK - 1 - first_row
    whole, part = far // LANES, far % LANES
    turned = [
        pltpu.roll(
            block[:, LANES * t : LANES * (t + 1)], LANES - part, 1, stride=1, stride_axis=0
        )
        for t in range(columns)
    ]
    rows = lax.broadcasted_iota(jnp.int32, (block.shape[0], LANES), 0)
    lanes = lax.broadcasted_iota(jnp.int32, (block.shape[0], LANES), 1)
    near = lanes - rows < LANES - part
    out = []
    for t in range(fill_columns):
        a = turned[(t + whole) % columns]
        b = turned[(t + whole + 1) % columns]
        out.append(jnp.where(near, a, b))
    return jnp.concatenate(out, axis=1)


def lean_right(block, first_row):
    columns = block.shape[1] // LANES
    whole, part = first_row // LANES, first_row % LANES
    turned = [
        pltpu.roll(block[:, LANES * t : LANES * (t + 1)], part, 1, stride=1, stride_axis=0)
        for t in range(columns)
    ]
    rows = lax.broadcasted_iota(jnp.int32, (block.shape[0], LANES), 0)
    lanes = lax.broadcasted_iota(jnp.int32, (block.shape[0], LANES), 1)
    wrapped = lanes - rows < part
    out = []
    for t in range(columns):
        a = turned[(t - whole) % columns]
        b = turned[(t - whole - 1) % columns]
        out.append(jnp.where(wrapped, b, a))
    return jnp.concatenate(out, axis=1)


def flip_matrix(kind):
    rows = lax.broadcasted_iota(jnp.int32, (BLOCK, BLOCK), 0)
    lanes = lax.broadcasted_iota(jnp.int32, (BLOCK, BLOCK), 1)
    return (rows + lanes == BLOCK - 1).astype(F32).astype(kind)


def in_place_order(parts_ref, out_ref, cuts):
    parts = parts_ref.shape[0]
    low, base = 0, 0
    for size in cuts:
        for part in range(parts):
            out_ref[base + part * size : base + (part + 1) * size, :] = parts_ref[
                part, low : low + size, :
            ]
        low += size
        base += parts * size


def attend_kernel(
    cuts, q_ref, cb_ref, pb_ref, k_ref, v_ref, t_ref, info_ref,
    e_ref, inv_ref, o_ref, cq_ref, pq_ref,
    keys, values, raw, lean, mix, tops, sums,
):
    parts, seg, _ = q_ref.shape
    queries = parts * seg
    old = parts * (cuts[0] + cuts[1])
    in_place_order(k_ref, keys, cuts)
    in_place_order(v_ref, values, cuts)
    q = q_ref[...].reshape(queries, DH)
    content_q = (q + cb_ref[...]).astype(BF16)
    position_q = (q + pb_ref[...]).astype(BF16)
    cq_ref[...] = content_q.reshape(parts, seg, DH)
    pq_ref[...] = position_q.reshape(parts, seg, DH)
    for block in range(queries // BLOCK):
        row0 = block * BLOCK
        width = old + row0 + BLOCK
        skip = queries - BLOCK - row0
        raw[:, :width] = mm(content_q[row0 : row0 + BLOCK], keys[:width, :], NT)
        lean[:, :width] = mm(position_q[row0 : row0 + BLOCK], t_ref[skip : skip + width, :], NT)
        for chunk in range(BLOCK // CHUNK):
            r0 = chunk * CHUNK
            rows = slice(r0, r0 + CHUNK)
            turned = lean_left(lean[rows, :width], r0, width // LANES)
            score = raw[rows, :width] + turned
            start = info_ref[row0 + r0 : row0 + r0 + CHUNK, 0:1].astype(jnp.int32)
            shade = info_ref[row0 + r0 : row0 + r0 + CHUNK, 1:2]
            past = score[:, :old] + shade
            place = lax.broadcasted_iota(jnp.int32, (CHUNK, row0 + BLOCK), 1)
            own = lax.broadcasted_iota(jnp.int32, (CHUNK, row0 + BLOCK), 0) + (row0 + r0)
            now = jnp.where((place <= own) & (place >= start), score[:, old:], MASKED)
            raw[rows, :old] = past
            raw[rows, old:width] = now
            top = past[:, :LANES]
            for low in range(LANES, old, LANES):
                top = jnp.maximum(top, past[:, low : low + LANES])
            for low in range(0, row0 + BLOCK, LANES):
                top = jnp.maximum(top, now[:, low : low + LANES])
            tops[rows, :] = top
        top = jnp.max(tops[...], axis=1, keepdims=True)
        tops[...] = jnp.broadcast_to(top, (BLOCK, LANES))
        for chunk in range(BLOCK // CHUNK):
            r0 = chunk * CHUNK
            rows = slice(r0, r0 + CHUNK)
            top = tops[rows, :]
            total = jnp.zeros((CHUNK, LANES), F32)
            for low in range(0, width, LANES):
                weight = jnp.exp2((raw[rows, low : low + LANES] - top) * (SCALE * LOG2E))
                total = total + weight
                e_ref[row0 + r0 : row0 + r0 + CHUNK, low : low + LANES] = weight.astype(BF16)
            sums[rows, :] = total
        total = jnp.sum(sums[...], axis=1, keepdims=True)
        inv_ref[row0 : row0 + BLOCK, :] = jnp.broadcast_to(1.0 / total, (BLOCK, DH))
        mix[row0 : row0 + BLOCK, :] = mm(
            e_ref[row0 : row0 + BLOCK, :width], values[:width, :], NN
        )
    o_ref[...] = (mix[...] * inv_ref[...]).astype(BF16).reshape(parts, seg, DH)


def attend(query, content_shift, position_shift, keys, values, table_rev, info, cuts):
    parts, group, seg, cols = query.shape
    rows = keys.shape[2]
    queries, key_count, heads = parts * seg, parts * rows, cols // DH
    by_head = lambda size: pl.BlockSpec((parts, None, size, DH), lambda s, h: (0, s, 0, h))
    grid_spec = pl.GridSpec(
        grid=(group, heads),
        in_specs=[
            by_head(seg),
            pl.BlockSpec((1, DH), lambda s, h: (0, h)),
            pl.BlockSpec((1, DH), lambda s, h: (0, h)),
            by_head(rows),
            by_head(rows),
            pl.BlockSpec((key_count, DH), lambda s, h: (0, h)),
            pl.BlockSpec((None, queries, LANES), lambda s, h: (s, 0, 0)),
        ],
        out_specs=[
            pl.BlockSpec((None, None, queries, key_count), lambda s, h: (s, h, 0, 0)),
            pl.BlockSpec((None, None, queries, DH), lambda s, h: (s, h, 0, 0)),
            by_head(seg),
            by_head(seg),
            by_head(seg),
        ],
        scratch_shapes=[
            pltpu.VMEM((key_count, DH), BF16),
            pltpu.VMEM((key_count, DH), BF16),
            pltpu.VMEM((BLOCK, key_count), F32),
            pltpu.VMEM((BLOCK, key_count), F32),
            pltpu.VMEM((queries, DH), F32),
            pltpu.VMEM((BLOCK, LANES), F32),
            pltpu.VMEM((BLOCK, LANES), F32),
        ],
    )
    small = jax.ShapeDtypeStruct((parts, group, seg, cols), BF16)
    return pl.pallas_call(
        functools.partial(attend_kernel, cuts),
        grid_spec=grid_spec,
        out_shape=[
            jax.ShapeDtypeStruct((group, heads, queries, key_count), BF16),
            jax.ShapeDtypeStruct((group, heads, queries, DH), F32),
            small,
            small,
            small,
        ],
        compiler_params=pltpu.CompilerParams(
            dimension_semantics=("arbitrary", "arbitrary"), vmem_limit_bytes=VMEM_LIMIT
        ),
        cost_estimate=cost(40),
        name="attend",
    )(query, content_shift, position_shift, keys, values, table_rev, info)


def pull_kernel(
    cuts, e_ref, inv_ref, o_ref, g_ref, cq_ref, pq_ref, k_ref, v_ref, t_ref,
    dq_ref, dk_ref, dv_ref, ks_ref, vs_ref, dt_ref, sums_ref,
    keys, values, grad, prob, part, score, lean, key_sum, value_sum,
):
    stream = pl.program_id(1)
    parts, seg, _ = g_ref.shape
    queries = parts * seg
    old = parts * (cuts[0] + cuts[1])
    in_place_order(k_ref, keys, cuts)
    in_place_order(v_ref, values, cuts)
    grad[...] = (g_ref[...].reshape(queries, DH).astype(F32) * inv_ref[...]).astype(BF16)
    attended = o_ref[...].reshape(queries, DH)
    content_q = cq_ref[...].reshape(queries, DH)
    position_q = pq_ref[...].reshape(queries, DH)

    @pl.when(stream == 0)
    def _():
        dt_ref[...] = jnp.zeros_like(dt_ref)
        sums_ref[...] = jnp.zeros_like(sums_ref)

    key_sum[...] = jnp.zeros_like(key_sum)
    value_sum[...] = jnp.zeros_like(value_sum)
    content_total = jnp.zeros((1, DH), F32)
    position_total = jnp.zeros((1, DH), F32)
    query_total = jnp.zeros((1, DH), F32)
    flip = flip_matrix(BF16)
    turn = lambda rows: mm(flip, rows, NN).astype(BF16)
    for block in range(queries // BLOCK):
        row0 = block * BLOCK
        width = old + row0 + BLOCK
        skip = queries - BLOCK - row0
        rows = slice(row0, row0 + BLOCK)
        grad_back = turn(grad[rows, :])
        dots_back = jnp.sum(
            grad_back.astype(F32) * turn(attended[rows]).astype(F32), axis=1, keepdims=True
        )
        content_back = turn(content_q[rows])
        position_back = turn(position_q[rows])
        prob[:, :width] = mm(grad_back, values[:width, :], NT)
        both = mm(jnp.concatenate([flip, grad[rows, :].T], axis=0), e_ref[rows, :width], NN)
        part[:, :width] = both[:BLOCK]
        value_sum[:, :width] += both[BLOCK:]
        for chunk in range(BLOCK // CHUNK):
            r0 = chunk * CHUNK
            mean = dots_back[r0 : r0 + CHUNK, 0:1]
            change = part[r0 : r0 + CHUNK, :width] * (prob[r0 : r0 + CHUNK, :width] - mean)
            score[r0 : r0 + CHUNK, :width] = change.astype(BF16)
            lean[r0 : r0 + CHUNK, :width] = lean_right(change, r0).astype(BF16)
        content_grad = (mm(score[:, :width], keys[:width, :], NN) * SCALE).astype(BF16).astype(F32)
        position_grad = (
            (mm(lean[:, :width], t_ref[skip : skip + width, :], NN) * SCALE)
            .astype(BF16)
            .astype(F32)
        )
        query_grad = turn((content_grad + position_grad).astype(BF16))
        content_total += jnp.sum(content_grad, axis=0, keepdims=True)
        position_total += jnp.sum(position_grad, axis=0, keepdims=True)
        query_total += jnp.sum(query_grad.astype(F32), axis=0, keepdims=True)
        dq_ref[rows, :] = query_grad
        key_sum[:, :width] += mm(content_back, score[:, :width], TN)
        dt_ref[:, skip : skip + width] += mm(position_back, lean[:, :width], TN) * SCALE
    key_cols = (key_sum[...] * SCALE).astype(BF16)
    value_cols = value_sum[...].astype(BF16)
    dk_ref[...] = key_cols
    dv_ref[...] = value_cols
    ks_ref[...] = (key_sum[:, old:] * SCALE).T.astype(BF16)
    vs_ref[...] = value_sum[:, old:].T.astype(BF16)
    ones = jnp.ones((8, key_cols.shape[1]), BF16)
    key_total = mm(ones, key_cols, NT)[0:1]
    value_total = mm(ones, value_cols, NT)[0:1]
    sums_ref[...] += jnp.concatenate(
        [
            content_total,
            position_total,
            query_total,
            key_total,
            value_total,
            jnp.zeros((3, DH), F32),
        ],
        axis=0,
    )


def pull(head, weights, inverse, attended, out_grad, content_q, position_q, keys, values, table_rev, cuts):
    parts, group, seg, cols = out_grad.shape
    rows = keys.shape[2]
    queries, key_count = parts * seg, parts * rows
    by_head = lambda size: pl.BlockSpec((parts, None, size, DH), lambda h, s: (0, s, 0, head))
    by_row = lambda: pl.BlockSpec((None, queries, DH), lambda h, s: (s, 0, h))
    by_place = lambda: pl.BlockSpec((None, DH, key_count), lambda h, s: (s, h, 0))
    grid_spec = pl.GridSpec(
        grid=(1, group),
        in_specs=[
            pl.BlockSpec((None, None, queries, key_count), lambda h, s: (s, head, 0, 0)),
            pl.BlockSpec((None, None, queries, DH), lambda h, s: (s, head, 0, 0)),
            by_head(seg),
            by_head(seg),
            by_head(seg),
            by_head(seg),
            by_head(rows),
            by_head(rows),
            pl.BlockSpec((key_count, DH), lambda h, s: (0, head)),
        ],
        out_specs=[
            by_row(),
            by_place(),
            by_place(),
            by_row(),
            by_row(),
            pl.BlockSpec((None, DH, key_count), lambda h, s: (h, 0, 0)),
            pl.BlockSpec((None, 8, DH), lambda h, s: (h, 0, 0)),
        ],
        scratch_shapes=[
            pltpu.VMEM((key_count, DH), BF16),
            pltpu.VMEM((key_count, DH), BF16),
            pltpu.VMEM((queries, DH), BF16),
            pltpu.VMEM((BLOCK, key_count), F32),
            pltpu.VMEM((BLOCK, key_count), F32),
            pltpu.VMEM((BLOCK, key_count), BF16),
            pltpu.VMEM((BLOCK, key_count), BF16),
            pltpu.VMEM((DH, key_count), F32),
            pltpu.VMEM((DH, key_count), F32),
        ],
    )
    return pl.pallas_call(
        functools.partial(pull_kernel, cuts),
        grid_spec=grid_spec,
        out_shape=[
            jax.ShapeDtypeStruct((group, queries, DH), BF16),
            jax.ShapeDtypeStruct((group, DH, key_count), BF16),
            jax.ShapeDtypeStruct((group, DH, key_count), BF16),
            jax.ShapeDtypeStruct((group, queries, DH), BF16),
            jax.ShapeDtypeStruct((group, queries, DH), BF16),
            jax.ShapeDtypeStruct((1, DH, key_count), F32),
            jax.ShapeDtypeStruct((1, 8, DH), F32),
        ],
        compiler_params=pltpu.CompilerParams(
            dimension_semantics=("arbitrary", "arbitrary"), vmem_limit_bytes=VMEM_LIMIT
        ),
        cost_estimate=cost(39),
        name="pull",
    )(weights, inverse, attended, out_grad, content_q, position_q, keys, values, table_rev)


def project_kernel(
    cuts, rows_ref, gain_ref, shift_ref, w_ref, old_ref, mem_ref, seg_ref, q_ref, k_ref, v_ref, normed
):
    rows, width = rows_ref.shape
    cols = k_ref.shape[1]
    step = 32
    for low in range(0, rows, step):
        wide = rows_ref[low : low + step, :].astype(F32)
        centred = wide - jnp.mean(wide, axis=1, keepdims=True)
        rate = lax.rsqrt(jnp.mean(centred * centred, axis=1, keepdims=True) + EPSILON)
        normed[low : low + step, :] = (centred * rate * gain_ref[...] + shift_ref[...]).astype(BF16)
    cut = cuts[0] + cuts[1]
    old_ref[...] = normed[: cuts[0], :]
    mem_ref[...] = normed[cuts[0] : cut, :]
    seg_ref[...] = normed[cut:, :]
    q_ref[...] = mm(normed[cut:, :], w_ref[:, :cols], NN)
    k_ref[...] = mm(normed[...], w_ref[:, cols : 2 * cols], NN).astype(BF16)
    v_ref[...] = mm(normed[...], w_ref[:, 2 * cols : 3 * cols], NN).astype(BF16)


def project(rows_all, gain, shift, columns, cuts):
    parts, group, each, width = rows_all.shape
    cols = columns.shape[1] // 4
    block = lambda size, wide: pl.BlockSpec((None, None, size, wide), lambda p, s: (p, s, 0, 0))
    placed = lambda size: pl.BlockSpec((None, size, width), lambda p, s: (s, p, 0))
    whole = lambda *shape: pl.BlockSpec(shape, lambda p, s: (0,) * len(shape))
    shape = lambda size, kind: jax.ShapeDtypeStruct((parts, group, size, cols), kind)
    return pl.pallas_call(
        functools.partial(project_kernel, cuts),
        grid_spec=pl.GridSpec(
            grid=(parts, group),
            in_specs=[
                block(each, width),
                whole(1, width),
                whole(1, width),
                whole(width, 4 * cols),
            ],
            out_specs=[placed(size) for size in cuts]
            + [block(cuts[2], cols), block(each, cols), block(each, cols)],
            scratch_shapes=[pltpu.VMEM((each, width), BF16)],
        ),
        out_shape=[jax.ShapeDtypeStruct((group, parts * size, width), BF16) for size in cuts]
        + [shape(cuts[2], F32), shape(each, BF16), shape(each, BF16)],
        compiler_params=pltpu.CompilerParams(
            dimension_semantics=("arbitrary", "arbitrary"), vmem_limit_bytes=VMEM_LIMIT
        ),
        cost_estimate=cost(17),
        name="project",
    )(rows_all, gain, shift, columns)


def gelu_both(x):
    near = jnp.abs(x)
    t = 1.0 / (1.0 + (0.3275911 * math.sqrt(0.5)) * near)
    bell = jnp.exp2((x * x) * (-0.5 * LOG2E))
    tail = 0.5 * 1.061405429
    for factor in (-1.453152027, 1.421413741, -0.284496736, 0.254829592):
        tail = tail * t + 0.5 * factor
    tail = tail * t * bell
    below = jnp.where(x < 0.0, tail, 1.0 - tail)
    return x * below, below + x * bell * (1.0 / math.sqrt(2.0 * math.pi))


def forward_back_kernel(
    last, parts, pair, n_ref, c_ref, *rest,
):
    up_refs, down_refs, shift_ref = rest[:parts], rest[parts : parts + pair], rest[parts + pair]
    rest = rest[parts + pair + 1 :]
    if last:
        part_in, grad_in, part_out, part_far, grad_out, grad_far, late_ref, sums_ref = rest[:8]
        pre, slope, hidden, act, up_out, down_out, sems, part_ref, grad_ref = rest[8:]
    else:
        part_ref, grad_ref, late_ref, sums_ref = rest[:4]
        pre, slope, hidden, act, up_out, down_out, sems = rest[4:]
    tile = pl.program_id(0)
    tiles = pl.num_programs(0)
    cols, units = up_refs[0].shape
    unit_cols, width = down_refs[0].shape
    rows = n_ref.shape[0]
    slot = lax.rem(tile, 2)
    up_weight = jnp.concatenate([ref[...] for ref in up_refs], axis=0)
    down_weight = jnp.concatenate([ref[...] for ref in down_refs], axis=0)

    def copies(at, index):
        return (
            pltpu.make_async_copy(
                up_out.at[at],
                late_ref.at[:, pl.ds(0, cols), pl.ds(pl.multiple_of(index * units, units), units)],
                sems.at[at, 0],
            ),
            pltpu.make_async_copy(
                down_out.at[at],
                late_ref.at[pl.ds(index * pair, pair), pl.ds(cols, unit_cols), :],
                sems.at[at, 1],
            ),
        )

    @pl.when(tile == 0)
    def _():
        if last:
            part_ref[...] = part_in[...]
            grad_ref[...] = grad_in[...]
        else:
            part_ref[...] = jnp.zeros_like(part_ref)
            grad_ref[...] = jnp.zeros_like(grad_ref)

    pre[...] = mm(n_ref[...], up_weight, NN)
    slope[...] = mm(c_ref[...], down_weight, NT)
    for low in range(0, rows, 16):
        some = slice(low, low + 16)
        value, change = gelu_both(pre[some, :] + shift_ref[...])
        hidden[some, :] = value.astype(BF16)
        act[some, :] = (change * slope[some, :]).astype(BF16)
    part_ref[...] += mm(hidden[...], down_weight, NN)
    grad_ref[...] += mm(act[...], up_weight, NT)
    sums_ref[...] = jnp.sum(act[...].astype(F32), axis=0, keepdims=True)

    @pl.when(tile >= 2)
    def _():
        for copy in copies(slot, tile - 2):
            copy.wait()

    up_out[slot] = mm(n_ref[...], act[...], TN).astype(BF16).reshape(parts, cols, units)
    down_out[slot] = mm(hidden[...], c_ref[...], TN).astype(BF16).reshape(pair, unit_cols, width)
    for copy in copies(slot, tile):
        copy.start()

    @pl.when(tile == tiles - 1)
    def _():
        if last:
            part_out[...] = part_ref[: rows // 2, :]
            part_far[...] = part_ref[rows // 2 :, :].astype(BF16)
            grad_out[...] = grad_ref[: rows // 2, :]
            grad_far[...] = grad_ref[rows // 2 :, :].astype(BF16)
        for copy in (copies(1 - slot, tile - 1) if parts > pair else ()) + copies(slot, tile):
            copy.wait()


def forward_back(normed, cot, gathered, shift, carry):
    parts, _, width = gathered.shape
    rows = normed.shape[0]
    cols = width // parts
    unit_cols = shift.shape[1] // parts
    pair = 2
    units = pair * unit_cols
    last = len(carry) > 0
    one = pl.Buffered(1)
    whole = lambda *shape: pl.BlockSpec(shape, lambda t: (0,) * len(shape), pipeline_mode=one)
    up = lambda p: pl.BlockSpec((None, cols, units), lambda t: (p, 0, t))
    down = lambda i: pl.BlockSpec(
        (None, unit_cols, width), lambda t: (t * pair + i, cols // unit_cols, 0)
    )
    if last:
        sums = [((rows // 2, width), F32), ((rows // 2, width), BF16)] * 2
    else:
        sums = [((rows, width), F32)] * 2
    return pl.pallas_call(
        functools.partial(forward_back_kernel, last, parts, pair),
        grid_spec=pl.GridSpec(
            grid=(parts // pair,),
            in_specs=[
                whole(rows, width),
                whole(rows, width),
            ]
            + [up(p) for p in range(parts)]
            + [down(i) for i in range(pair)]
            + [pl.BlockSpec((1, units), lambda t: (0, t))]
            + [whole(rows, width) for _ in carry],
            out_specs=[whole(*shape) for shape, _ in sums]
            + [
                pl.BlockSpec(memory_space=pl.ANY),
                pl.BlockSpec((1, units), lambda t: (0, t)),
            ],
            scratch_shapes=[
                pltpu.VMEM((rows, units), F32),
                pltpu.VMEM((rows, units), F32),
                pltpu.VMEM((rows, units), BF16),
                pltpu.VMEM((rows, units), BF16),
                pltpu.VMEM((2, parts, cols, units), BF16),
                pltpu.VMEM((2, pair, unit_cols, width), BF16),
                pltpu.SemaphoreType.DMA((2, 2)),
            ]
            + [pltpu.VMEM((rows, width), F32) for _ in carry],
        ),
        out_shape=[jax.ShapeDtypeStruct(shape, kind) for shape, kind in sums]
        + [
            jax.ShapeDtypeStruct((parts, cols + unit_cols, width), BF16),
            jax.ShapeDtypeStruct((1, parts * unit_cols), F32),
        ],
        compiler_params=pltpu.CompilerParams(
            dimension_semantics=("arbitrary",), vmem_limit_bytes=VMEM_LIMIT
        ),
        cost_estimate=cost(29),
        name="forward_back",
    )(normed, cot, *[gathered] * (parts + pair), shift, *carry)


def leave_kernel(a_ref, s_ref, w_ref, shift_ref, gain_ref, bias_ref, flat_ref, m_ref, n_ref):
    parts = a_ref.shape[0]
    flat_ref[...] = jnp.concatenate([a_ref[part] for part in range(parts)], axis=1)
    m_ref[...] = s_ref[...].astype(F32) + (mm(flat_ref[...], w_ref[...], NN) + shift_ref[...])
    step = 16
    for low in range(0, m_ref.shape[0], step):
        unit, _ = standardise(m_ref[low : low + step, :])
        n_ref[low : low + step, :] = (unit * gain_ref[...] + bias_ref[...]).astype(BF16)


def leave(mixed_heads, segment, base, weight, shift, gain, bias):
    parts, group, seg, cols = mixed_heads.shape
    width = parts * cols
    rows = lambda: pl.BlockSpec((None, seg, width), lambda s: (s, 0, 0))
    vector = lambda: pl.BlockSpec((1, width), lambda s: (0, 0))
    shape = lambda kind: jax.ShapeDtypeStruct((group, seg, width), kind)
    return pl.pallas_call(
        leave_kernel,
        grid_spec=pl.GridSpec(
            grid=(group,),
            in_specs=[
                pl.BlockSpec((parts, None, seg, cols), lambda s: (0, s, 0, 0)),
                pl.BlockSpec((None, seg, width), lambda s: (s + base, 0, 0)),
                pl.BlockSpec((width, width), lambda s: (0, 0)),
                vector(),
                vector(),
                vector(),
            ],
            out_specs=[rows(), rows(), rows()],
        ),
        out_shape=[shape(BF16), shape(F32), shape(BF16)],
        compiler_params=pltpu.CompilerParams(vmem_limit_bytes=VMEM_LIMIT),
        cost_estimate=cost(6),
        name="leave",
    )(mixed_heads, segment, weight, shift, gain, bias)


def enter_kernel(
    m_ref, g_ref, far_ref, c_ref, w_ref, gain_ref, mg_ref, b_ref, a_ref, sums_ref
):
    @pl.when(pl.program_id(0) == 0)
    def _():
        sums_ref[...] = jnp.zeros_like(sums_ref)

    parts = a_ref.shape[0]
    rows, width = m_ref.shape
    step = 32
    total = [jnp.zeros((1, width), F32) for _ in range(4)]
    for low in range(0, rows, step):
        at = slice(low, low + step)
        unit, rate = standardise(m_ref[at, :])
        grad = g_ref[at, :] + far_ref[at, :].astype(F32)
        cot = c_ref[at, :].astype(F32)
        middle_grad = cot + standardise_back(unit, rate, grad, gain_ref[...])
        branch = middle_grad.astype(BF16)
        mg_ref[at, :] = middle_grad
        b_ref[at, :] = branch
        for i, value in enumerate((branch.astype(F32), grad * unit, grad, cot)):
            total[i] = total[i] + jnp.sum(value, axis=0, keepdims=True)
    sums_ref[...] += jnp.concatenate(total + [jnp.zeros((4, width), F32)], axis=0)
    for part in range(parts):
        low = part * a_ref.shape[2]
        weight = w_ref[low : low + a_ref.shape[2], :]
        a_ref[part] = mm(b_ref[...], weight, NT).astype(BF16)


def enter(middle, grad, far, cot, base, weight, gain, parts):
    group, seg, width = middle.shape
    cols = width // parts
    rows = lambda: pl.BlockSpec((None, seg, width), lambda s: (s, 0, 0))
    later = lambda: pl.BlockSpec((None, seg, width), lambda s: (s + base, 0, 0))
    shape = lambda kind: jax.ShapeDtypeStruct((group, seg, width), kind)
    return pl.pallas_call(
        enter_kernel,
        grid_spec=pl.GridSpec(
            grid=(group,),
            in_specs=[
                rows(),
                later(),
                later(),
                later(),
                pl.BlockSpec((width, width), lambda s: (0, 0)),
                pl.BlockSpec((1, width), lambda s: (0, 0)),
            ],
            out_specs=[
                rows(),
                rows(),
                pl.BlockSpec((parts, None, seg, cols), lambda s: (0, s, 0, 0)),
                pl.BlockSpec((8, width), lambda s: (0, 0)),
            ],
        ),
        out_shape=[
            shape(F32),
            shape(BF16),
            jax.ShapeDtypeStruct((parts, group, seg, cols), BF16),
            jax.ShapeDtypeStruct((8, width), F32),
        ],
        compiler_params=pltpu.CompilerParams(
            dimension_semantics=("arbitrary",), vmem_limit_bytes=VMEM_LIMIT
        ),
        cost_estimate=cost(7),
        name="enter",
    )(middle, grad, far, cot, weight, gain)


def compress_kernel(low, rows_ref, w_ref, shift_ref, out_ref, wide):
    count = out_ref.shape[0]
    cols = out_ref.shape[1]
    blocks = wide.shape[0]
    for at in range(blocks):
        wide[at] = rows_ref[low : low + 3 * count, at * LANES : (at + 1) * LANES].astype(F32)
    total = jnp.broadcast_to(shift_ref[...], (count, cols))
    for k in range(3):
        every = jnp.concatenate(
            [wide[at, pl.ds(k, count, stride=3), :] for at in range(blocks)], axis=1
        ).astype(BF16)
        total = total + mm(every, w_ref[:, k * cols : (k + 1) * cols], NN)
    out_ref[...] = total.astype(BF16)


def compress(rows_all, columns, shift, low, count):
    parts, group, each, width = rows_all.shape
    cols = columns.shape[1] // 3
    return pl.pallas_call(
        functools.partial(compress_kernel, low),
        grid_spec=pl.GridSpec(
            grid=(parts, group),
            in_specs=[
                pl.BlockSpec((None, None, each, width), lambda p, s: (p, s, 0, 0)),
                pl.BlockSpec((width, 3 * cols), lambda p, s: (0, 0)),
                pl.BlockSpec((1, cols), lambda p, s: (0, 0)),
            ],
            out_specs=pl.BlockSpec((None, None, count, cols), lambda p, s: (p, s, 0, 0)),
            scratch_shapes=[pltpu.VMEM((width // LANES, 3 * count, LANES), F32)],
        ),
        out_shape=jax.ShapeDtypeStruct((parts, group, count, cols), BF16),
        compiler_params=pltpu.CompilerParams(
            dimension_semantics=("arbitrary", "arbitrary"), vmem_limit_bytes=VMEM_LIMIT
        ),
        cost_estimate=cost(6.5),
        name="compress",
    )(rows_all, columns, shift)


def lay_out_kernel(
    parts, unit_cols, core_ref, a_ref, b_ref, c_ref, d_ref, up_ref, down_ref
):
    flipped = core_ref[0] == 1
    for half, (mine_ref, far_ref) in enumerate(((a_ref, c_ref), (b_ref, d_ref))):
        mine, far = mine_ref[...].astype(F32), far_ref[...].astype(F32)
        for core, value in enumerate(
            (jnp.where(flipped, far, mine), jnp.where(flipped, mine, far))
        ):
            for part in range(parts):
                at = ((part * 2 + core) * 2 + half) * unit_cols
                up_ref[:, at : at + unit_cols] = value[
                    0, :, part * unit_cols : (part + 1) * unit_cols
                ]
            down_ref[2 * core + half] = value[1]


def lay_out(core, mine, far, parts):
    _, rows, width = mine[0].shape
    step = rows // 4 if rows % 64 == 0 else rows
    half = lambda: pl.BlockSpec((2, step, width), lambda r, *_: (0, r, 0))
    return pl.pallas_call(
        functools.partial(lay_out_kernel, parts, rows),
        grid_spec=pltpu.PrefetchScalarGridSpec(
            num_scalar_prefetch=1,
            grid=(rows // step,),
            in_specs=[half(), half(), half(), half()],
            out_specs=[
                pl.BlockSpec((step, 4 * width), lambda r, *_: (r, 0)),
                pl.BlockSpec((4, step, width), lambda r, *_: (0, r, 0)),
            ],
        ),
        out_shape=[
            jax.ShapeDtypeStruct((rows, 4 * width), F32),
            jax.ShapeDtypeStruct((4, rows, width), F32),
        ],
        compiler_params=pltpu.CompilerParams(vmem_limit_bytes=VMEM_LIMIT),
        cost_estimate=cost(4),
        name="lay_out",
    )(core.reshape(1), *mine, *far)


def lay_squares_kernel(in_ref, *out_refs):
    parts = in_ref.shape[0]
    cols = in_ref.shape[2] // len(out_refs)
    for at, out_ref in enumerate(out_refs):
        for part in range(parts):
            out_ref[:, part * cols : (part + 1) * cols] = in_ref[
                part, :, at * cols : (at + 1) * cols
            ].astype(F32)


def lay_squares(summed, rows):
    parts, _, wide = summed.shape
    width = parts * wide // 4
    step = rows // 2
    return pl.pallas_call(
        lay_squares_kernel,
        grid_spec=pl.GridSpec(
            grid=(2,),
            in_specs=[pl.BlockSpec((parts, step, wide), lambda i: (0, i, 0))],
            out_specs=[pl.BlockSpec((step, width), lambda i: (i, 0)) for _ in range(4)],
        ),
        out_shape=[jax.ShapeDtypeStruct((rows, width), F32) for _ in range(4)],
        compiler_params=pltpu.CompilerParams(vmem_limit_bytes=VMEM_LIMIT),
        cost_estimate=cost(2.5),
        name="lay_squares",
    )(summed)


def settle_kernel(heads, me_ref, old_ref, mem_ref, seg_ref, *rest):
    q_refs, k_refs, v_refs, ks_refs, vs_refs, dt_refs, sums_refs = (
        rest[i * heads : (i + 1) * heads] for i in range(7)
    )
    w_ref, table_ref, gain_ref, shift_ref, small_ref, part_ref, out_ref, total = rest[7 * heads :]
    stream = pl.program_id(0)
    parts, rows, wide = out_ref.shape
    cols = wide // 4
    width = parts * cols

    @pl.when(stream == 0)
    def _():
        total[...] = jnp.zeros_like(total)

    low = old_ref.shape[0]
    high = low + mem_ref.shape[0]
    pair = lambda first, last: [ref[:, first:last] for ref in (*k_refs, *v_refs)]
    total[...] += mm(
        jnp.concatenate([ref[...].T for ref in q_refs] + pair(high, high + seg_ref.shape[0]), axis=0),
        seg_ref[...],
        NN,
    )
    total[cols:, :] += mm(jnp.concatenate(pair(low, high), axis=0), mem_ref[...], NN)
    total[cols:, :] += mm(jnp.concatenate(pair(0, low), axis=0), old_ref[...], NN)
    three = jnp.concatenate([ref[...] for ref in (*q_refs, *ks_refs, *vs_refs)], axis=1)
    part = mm(three, w_ref[:, : 3 * cols], NT).astype(BF16)
    part_ref[...] = part.reshape(part_ref.shape)

    @pl.when(stream == pl.num_programs(0) - 1)
    def _():
        places = jnp.concatenate([ref[0].astype(BF16) for ref in dt_refs], axis=0)
        rel = mm(places, table_ref[...], NN)
        line = lambda row: jnp.concatenate(
            [ref[0, row : row + 1, :] for ref in sums_refs], axis=1
        )
        row_sums = jnp.concatenate([line(2), line(3), line(4)], axis=1)
        pieces, rest = [], row_sums
        for _ in range(3):
            pieces.append(rest.astype(BF16))
            rest = rest - pieces[-1].astype(F32)
        pieces = jnp.concatenate(pieces + [jnp.zeros((13, 3 * cols), BF16)], axis=0)
        shift_grad = jnp.sum(mm(pieces, w_ref[:, : 3 * cols], NT), axis=0, keepdims=True)
        weight = w_ref[:, : 3 * cols].astype(F32)
        along = jnp.sum(weight.T * total[...], axis=0, keepdims=True)
        gain_grad = (along - shift_ref[...] * shift_grad) / gain_ref[...]
        for at in range(parts):
            low, high = at * cols, (at + 1) * cols
            out_ref[at, :cols, : 3 * cols] = total[:, low:high].T.astype(BF16)
            out_ref[at, :cols, 3 * cols :] = rel[:, low:high].T.astype(BF16)
            mine = (me_ref[0] == at).astype(F32)
            none = jnp.zeros((1, 2 * cols), F32)
            first = jnp.concatenate([gain_grad[:, low:high], shift_grad[:, low:high], none], axis=1)
            second = jnp.concatenate([none, mine * line(0), mine * line(1)], axis=1)
            added = jnp.concatenate([first, second, jnp.zeros((14, wide), F32)], axis=0)
            out_ref[at, cols:, :] = (small_ref[at] + added).astype(BF16)


def settle(me, normed, grads, columns, table, gain, shift, small, parts):
    group, queries, width = normed[2].shape
    cols = width // parts
    wide = 4 * cols
    by_kind = list(zip(*grads))
    block = lambda array: pl.BlockSpec((None, *array.shape[1:]), lambda s, *_: (s, 0, 0))
    whole = lambda *shape: pl.BlockSpec(
        shape, lambda s, *_: (0,) * len(shape), pipeline_mode=pl.Buffered(1)
    )
    return pl.pallas_call(
        functools.partial(settle_kernel, len(grads)),
        grid_spec=pltpu.PrefetchScalarGridSpec(
            num_scalar_prefetch=1,
            grid=(group,),
            in_specs=[block(rows) for rows in normed]
            + [block(each) for kind in by_kind[:5] for each in kind]
            + [whole(*each.shape) for kind in by_kind[5:] for each in kind]
            + [
                whole(*columns.shape),
                whole(*table.shape),
                whole(1, width),
                whole(1, width),
                whole(*small.shape),
            ],
            out_specs=[
                pl.BlockSpec((parts, None, queries // parts, width), lambda s, *_: (0, s, 0, 0)),
                whole(parts, cols + 16, wide),
            ],
            scratch_shapes=[pltpu.VMEM((3 * cols, width), F32)],
        ),
        out_shape=[
            jax.ShapeDtypeStruct((parts, group, queries // parts, width), BF16),
            jax.ShapeDtypeStruct((parts, cols + 16, wide), BF16),
        ],
        compiler_params=pltpu.CompilerParams(
            dimension_semantics=("arbitrary",), vmem_limit_bytes=VMEM_LIMIT
        ),
        cost_estimate=cost(14),
        name="settle",
    )(
        me.reshape(1), *normed, *[each for kind in by_kind for each in kind], columns, table, gain, shift,
        small,
    )


def standardise(rows):
    mean = jnp.mean(rows, axis=-1, keepdims=True)
    centred = rows - mean
    rate = lax.rsqrt(jnp.mean(centred * centred, axis=-1, keepdims=True) + EPSILON)
    return centred * rate, rate


def standardise_back(unit, rate, grad, gain):
    scaled = grad * gain
    mean = jnp.mean(scaled, axis=-1, keepdims=True)
    along = jnp.mean(scaled * unit, axis=-1, keepdims=True)
    return rate * (scaled - mean - unit * along)


def sinusoid_reversed(rows, width):
    positions = (rows - 1 - jnp.arange(rows, dtype=jnp.int32)).astype(F32)[:, None]
    frequency = jnp.exp(
        jnp.arange(width // 2, dtype=F32) * (-2.0 * math.log(10000.0) / width)
    )
    angles = positions * frequency[None, :]
    return jnp.concatenate([jnp.sin(angles), jnp.cos(angles)], axis=1).astype(BF16)


def dot(left, right):
    return mm(left, right, NN)


def swap(value):
    return lax.ppermute(value, "core", [(0, 1), (1, 0)])


def exchange(blocks, name, axis=0):
    count = lax.axis_size(name)
    me = lax.axis_index(name)
    block = lambda at: lax.dynamic_index_in_dim(blocks, at, axis, keepdims=False)
    return [block(me)] + [
        lax.ppermute(block(me ^ apart), name, [(i, i ^ apart) for i in range(count)])
        for apart in range(1, count)
    ]


def collect(block, name):
    count = lax.axis_size(name)
    me = lax.axis_index(name)
    found = jnp.stack(
        [block]
        + [
            lax.ppermute(block, name, [(i, i ^ apart) for i in range(count)])
            for apart in range(1, count)
        ]
    )
    return jnp.stack(
        [lax.dynamic_index_in_dim(found, me ^ i, 0, keepdims=False) for i in range(count)]
    )


def add_up(arrays, kind=BF16):
    total = arrays[0].astype(F32)
    for array in arrays[1:]:
        total = total + array.astype(F32)
    return total.astype(kind)


def body(
    segment, memory, compressed, eob, reset, ln1_gain, ln1_bias, w_query, w_key, w_value,
    w_out, out_bias, w_rel, bias_content, bias_position, ln2_gain, ln2_bias, w_up, up_bias,
    w_down, down_bias, conv_weight, conv_bias, cotangent,
):
    parts = lax.axis_size("seq")
    layers = lax.axis_size("z")
    core = lax.axis_index("core")
    me = lax.axis_index("seq")
    group, seg, width = segment.shape
    mem, old = memory.shape[1], compressed.shape[1]
    cuts = (old, mem, seg)
    each = old + mem + seg
    keys_in_all = parts * each
    cols = width // parts
    wide = 4 * cols
    own = group * seg
    unit_cols = w_up.shape[1] // (4 * parts)
    barrier = lax.optimization_barrier

    def by_columns(matrices):
        count = matrices.shape[0]
        sent = matrices.reshape(count, cols, parts, cols).transpose(2, 1, 0, 3)
        return sent.reshape(parts, cols, count * cols)

    up_bias_own = lax.dynamic_slice_in_dim(up_bias, core * 2 * unit_cols, 2 * unit_cols, 0)
    vectors = jnp.concatenate(
        [ln1_gain, ln1_bias, out_bias, ln2_gain, ln2_bias, down_bias, up_bias_own]
    )
    vectors = jnp.pad(vectors.reshape(2, wide), ((0, 14), (0, 0)))
    half = cols // 2
    sent = by_columns(jnp.concatenate([jnp.stack([w_query, w_key, w_value, w_rel]), conv_weight]))
    sent = lax.dynamic_slice_in_dim(sent, core * half, half, 1)
    out_half = lax.dynamic_slice_in_dim(w_out, core * half, half, 0)
    sent = jnp.concatenate([sent, jnp.broadcast_to(out_half, (parts, half, width))], axis=2)
    vectors = jnp.pad(vectors, ((0, 0), (0, 3 * cols + width)))
    sent = jnp.concatenate([sent, jnp.broadcast_to(vectors, (parts, *vectors.shape))], axis=1)
    got = lax.all_to_all(sent, "seq", 0, 0, tiled=True)
    spans = [(0, group)]
    local = [
        jnp.concatenate([compressed[low:high], memory[low:high], segment[low:high]], axis=1)
        for low, high in spans
    ]
    rows_all = [lax.all_gather(local[0], "seq")]
    mine = got[:, :half]
    far = swap(mine)
    columns = jnp.stack(
        [jnp.where(core == 0, mine, far), jnp.where(core == 0, far, mine)], axis=1
    ).reshape(width, 7 * cols + width)
    columns, conv_columns, out_full = (
        columns[:, :wide],
        columns[:, wide : 7 * cols],
        columns[:, 7 * cols :],
    )
    vectors = got[:, half : half + 2, :wide].reshape(parts, 2 * wide).astype(F32)
    gain_one, shift_one, out_shift, gain_two, shift_two, down_shift = (
        vectors[:, cols * i : cols * (i + 1)].reshape(1, width) for i in range(6)
    )
    up_shift = vectors[:, 6 * cols :].reshape(parts, 2, unit_cols).transpose(1, 0, 2)
    up_shift = up_shift.reshape(2, 1, parts * unit_cols)
    up_quarters = lax.dynamic_slice_in_dim(
        w_up.reshape(cols, parts, 2, 2, unit_cols), core, 1, 2
    ).reshape(cols, parts, 2, unit_cols)
    up_quarters = [up_quarters[:, :, i].reshape(cols, width) for i in range(2)]
    down_half = lax.dynamic_slice_in_dim(w_down, core * 2 * unit_cols, 2 * unit_cols, 0)
    down_quarters = [down_half[unit_cols * i : unit_cols * (i + 1)] for i in range(2)]
    first = jnp.concatenate([up_quarters[0], down_quarters[0]], axis=0)
    second = jnp.concatenate([up_quarters[1], down_quarters[1]], axis=0)
    cot_own = cotangent.reshape(own, width)
    cot_both = jnp.concatenate([cot_own, swap(cot_own)], axis=0)

    table_rev = sinusoid_reversed(keys_in_all, width)
    proj_rev = dot(table_rev, columns[:, 3 * cols :]).astype(BF16)
    index = jnp.arange(eob.shape[1], dtype=jnp.int32)[None, :]
    opens = jnp.pad(eob, ((0, 0), (1, 0)))[:, :-1] == 1
    start = lax.cummax(jnp.where(opens, index, 0), axis=1)
    shade = jnp.where((start == 0) & (reset[:, None] == 0), 0.0, MASKED)
    info = jnp.stack([start.astype(F32), shade], axis=2)
    info = jnp.pad(info, ((0, 0), (0, 0), (0, LANES - 2)))
    rows_all[0], proj_rev, info, cot_both, table_rev, columns, conv_columns, out_full, *local = barrier(
        (rows_all[0], proj_rev, info, cot_both, table_rev, columns, conv_columns, out_full, *local)
    )
    rows_all = [rows_all[0]] + [lax.all_gather(rows, "seq") for rows in local[1:]]

    kept, heads = [], []
    for batch, (low, high) in enumerate(spans):
        if batch == len(spans) - 1:
            rows_all[batch], first, *heads = barrier((rows_all[batch], first, *heads))
            first = lax.all_gather(first, "seq")
        *normed, query, keys, values = project(rows_all[batch], gain_one, shift_one, columns, cuts)
        second, query = barrier((second, query))
        second = lax.all_gather(second, "seq")
        weights, inverse, mixed_heads, content_q, position_q = attend(
            query,
            bias_content.astype(F32).reshape(1, cols),
            bias_position.astype(F32).reshape(1, cols),
            keys,
            values,
            proj_rev,
            info[low:high],
            cuts,
        )
        kept.append((weights, inverse, mixed_heads, content_q, position_q, keys, values))
        heads.append(lax.all_to_all(mixed_heads, "seq", 0, 0, tiled=True))

    mixed_heads, conv_columns = barrier((mixed_heads, conv_columns))
    packed = compress(
        rows_all[0], conv_columns, conv_bias.astype(F32).reshape(1, cols), old, mem // 3
    )
    packed, *heads = barrier((packed, *heads))

    attended, middle, normed_two = [], [], []
    for (low, high), batch in zip(spans, heads):
        one, two, three = leave(batch, segment, low, out_full, out_shift, gain_two, shift_two)
        attended.append(one.reshape(-1, width))
        middle.append(two)
        normed_two.append(three.reshape(-1, width))
    both = jnp.concatenate(normed_two + [swap(rows) for rows in normed_two], axis=0)
    part, part_grad, late_one, unit_one = forward_back(both, cot_both, first, up_shift[0], ())
    late_one = lax.psum_scatter(
        late_one.reshape(-1, width), "seq", scatter_dimension=0, tiled=True
    )
    part, part_far, part_grad, grad_far, late_two, unit_two = forward_back(
        both, cot_both, second, up_shift[1], (part, part_grad)
    )
    grad_far = swap(grad_far)
    by_stream = lambda rows: rows.reshape(group, seg, width)
    middle_grad, branch_grad, head_grad, sums_two = [], [], [], 0.0
    for (low, high), batch in zip(spans, middle):
        one, two, three, four = enter(
            batch, by_stream(part_grad), by_stream(grad_far), cotangent, low, out_full, gain_two, parts
        )
        middle_grad.append(one)
        branch_grad.append(two.reshape(-1, width))
        three, part_grad = barrier((three, part_grad))
        head_grad.append(lax.all_to_all(three, "seq", 0, 0, tiled=True))
        sums_two = sums_two + four
    result = part + swap(part_far).astype(F32) + down_shift
    output = (jnp.concatenate(middle).reshape(own, width) + result).astype(BF16)
    output = output.reshape(group, seg, width)

    out_shift_grad, gain_two_grad, shift_two_grad, down_shift_grad = (
        sums_two[i].reshape(parts, cols) for i in range(4)
    )
    none = jnp.zeros((parts, 2 * cols), F32)
    unit_sums = jnp.stack(
        [unit_one.reshape(parts, unit_cols), unit_two.reshape(parts, unit_cols)], axis=1
    ).reshape(parts, 2 * unit_cols)
    small = jnp.stack(
        [
            jnp.concatenate([none, out_shift_grad, gain_two_grad], axis=1),
            jnp.concatenate([shift_two_grad, down_shift_grad, none], axis=1),
            jnp.concatenate(
                [jnp.where(core == 0, unit_sums, 0.0), jnp.where(core == 1, unit_sums, 0.0)], axis=1
            ),
        ],
        axis=1,
    )
    small = jnp.pad(small, ((0, 0), (0, 13), (0, 0)))
    weights, inverse, mixed_heads, content_q, position_q, keys, values = kept[0]
    out_grad = mm(jnp.concatenate(attended), jnp.concatenate(branch_grad), TN)
    out_grad = out_grad.astype(BF16).reshape(parts, cols, width)
    late_one, small, out_grad, late_two, output, head_grad = barrier(
        (late_one, small, out_grad, late_two, output, head_grad[0])
    )
    late_two = lax.psum_scatter(
        late_two.reshape(-1, width), "seq", scatter_dimension=0, tiled=True
    )
    late_one = exchange(late_one.reshape(layers, -1, width), "z")
    grads = []
    for head in range(cols // DH):
        grads.append(
            list(
                pull(
                    head, weights, inverse, mixed_heads, head_grad, content_q, position_q, keys,
                    values, proj_rev, cuts,
                )
            )
        )
        if head == 0:
            late_one, head_grad, grads[0][0] = barrier((late_one, head_grad, grads[0][0]))
            late_one = collect(add_up(late_one), "z")
    late_one, late_two, out_grad, grads[-1][0] = barrier(
        (late_one, late_two, out_grad, grads[-1][0])
    )
    out_sent = lax.all_to_all(out_grad, "seq", 0, 0, tiled=True)
    seg_part, square_grads = settle(
        me, normed, grads, columns, table_rev, gain_one, shift_one, small, parts
    )
    out_sent, late_two, square_grads = barrier((out_sent, late_two, square_grads))
    late_two = exchange(late_two.reshape(layers, -1, width), "z")
    summed = lax.all_to_all(square_grads, "seq", 0, 0, tiled=True)
    late_two, packed = barrier((add_up(late_two), packed))
    late_two = collect(late_two, "z")
    packed = exchange(packed, "seq")
    out_sent = jnp.sum(out_sent.astype(F32), axis=0).astype(BF16)
    out_sent, summed, seg_part = barrier((out_sent, summed, seg_part))
    squares = parts * (cols + 16)
    summed = jnp.concatenate([summed.reshape(squares, wide), out_sent.reshape(-1, wide)], axis=0)
    summed = lax.psum(summed, ("z", "core"))
    packed = jnp.stack(packed)
    new_compressed = jnp.concatenate(
        [lax.dynamic_index_in_dim(packed, p ^ me, 0, keepdims=False) for p in range(parts)], axis=2
    )
    seg_grad = lax.all_to_all(seg_part, "seq", 0, 0, tiled=True).astype(F32)
    seg_grad = jnp.sum(seg_grad, axis=0).reshape(own, width)
    unit_seg, rate_seg = standardise(segment.reshape(own, width).astype(F32))
    rows_grad = standardise_back(unit_seg, rate_seg, seg_grad, gain_one)
    segment_grad = jnp.concatenate(middle_grad, axis=0) + by_stream(rows_grad)

    halves = [late_one.reshape(2, unit_cols, width), late_two.reshape(2, unit_cols, width)]
    up_w, down_w = lay_out(core, halves, [swap(rows) for rows in halves], parts)
    down_w = down_w.reshape(4 * unit_cols, width)
    summed, output, segment_grad, new_compressed, up_w, down_w = barrier(
        (summed, output, segment_grad, new_compressed, up_w, down_w)
    )
    out_w = summed[squares:].reshape(cols, width).astype(F32)
    summed = summed[:squares].reshape(parts, cols + 16, wide)
    query_w, key_w, value_w, rel_w = lay_squares(summed, cols)
    small = jnp.sum(summed[:, cols : cols + 3].astype(F32), axis=0)
    piece = lambda row, i: small[row, cols * i : cols * (i + 1)]
    return (
        output,
        segment_grad,
        piece(0, 0),
        piece(0, 1),
        query_w,
        key_w,
        value_w,
        out_w,
        piece(0, 2),
        rel_w,
        piece(1, 2),
        piece(1, 3),
        piece(0, 3),
        piece(1, 0),
        up_w,
        small[2],
        down_w,
        piece(1, 1),
        new_compressed,
    )


def solution(mesh):
    dp = mesh.shape["dp"]
    cores = jax.sharding.Mesh(
        mesh.devices.reshape(dp // 2, 2, mesh.shape["seq"]), ("z", "core", "seq")
    )
    rows = P(("z", "core"), "seq", None)
    shard, matrix = P("seq"), P("seq", None)
    return jax.shard_map(
        body,
        mesh=cores,
        in_specs=(
            rows, rows, rows, P(("z", "core"), None), P(("z", "core")), shard, shard, matrix,
            matrix, matrix, matrix, shard, matrix, shard, shard, shard, shard, matrix, shard,
            matrix, shard, P(None, "seq", None), shard, rows,
        ),
        out_specs=(
            rows, rows, shard, shard, matrix, matrix, matrix, matrix, shard, matrix, shard,
            shard, shard, shard, matrix, shard, matrix, shard, rows,
        ),
        check_vma=False,
    )
```

```python
import functools
import math

import jax
import jax.numpy as jnp
from jax import lax
from jax.experimental import pallas as pl
from jax.experimental.pallas import tpu as pltpu
from jax.sharding import PartitionSpec as P

HEADS = 8
DH = 128
EPSILON = 1e-05
MASKED = -1e30
LANES = 128
BLOCK = 256
CHUNK = 16
VMEM_LIMIT = 60 * 2**20
SCALE = 1.0 / math.sqrt(DH)
LOG2E = 1.4426950408889634
BF16 = jnp.bfloat16
F32 = jnp.float32


def cost(microseconds):
    return pl.CostEstimate(flops=int(microseconds * 1.15e7), bytes_accessed=0, transcendentals=0)


def mm(left, right, dims):
    return lax.dot_general(left, right, (dims, ((), ())), preferred_element_type=F32)


NN = ((1,), (0,))
NT = ((1,), (1,))
TN = ((0,), (0,))


def flip_matrix(kind):
    rows = lax.broadcasted_iota(jnp.int32, (BLOCK, BLOCK), 0)
    lanes = lax.broadcasted_iota(jnp.int32, (BLOCK, BLOCK), 1)
    return (rows + lanes == BLOCK - 1).astype(F32).astype(kind)


def in_place_order(parts_ref, out_ref, cuts):
    parts = parts_ref.shape[0]
    low, base = 0, 0
    for size in cuts:
        for part in range(parts):
            out_ref[base + part * size : base + (part + 1) * size, :] = parts_ref[
                part, low : low + size, :
            ]
        low += size
        base += parts * size


def attend_kernel(
    cuts, q_ref, cb_ref, pb_ref, k_ref, v_ref, t_ref, info_ref,
    e_ref, inv_ref, o_ref, cq_ref, pq_ref,
    keys, values, raw, lean, mix, tops, sums,
):
    parts, seg, _ = q_ref.shape
    queries = parts * seg
    old = parts * (cuts[0] + cuts[1])
    in_place_order(k_ref, keys, cuts)
    in_place_order(v_ref, values, cuts)
    q = q_ref[...].reshape(queries, DH)
    content_q = (q + cb_ref[...]).astype(BF16)
    position_q = (q + pb_ref[...]).astype(BF16)
    cq_ref[...] = content_q.reshape(parts, seg, DH)
    pq_ref[...] = position_q.reshape(parts, seg, DH)
    for block in range(queries // BLOCK):
        row0 = block * BLOCK
        width = old + row0 + BLOCK
        skip = queries - BLOCK - row0
        raw[:, :width] = mm(content_q[row0 : row0 + BLOCK], keys[:width, :], NT)
        lean[:, :width] = mm(position_q[row0 : row0 + BLOCK], t_ref[skip : skip + width, :], NT)
        for chunk in range(BLOCK // CHUNK):
            r0 = chunk * CHUNK
            rows = slice(r0, r0 + CHUNK)
            columns = width // LANES
            whole, part = (BLOCK - 1 - r0) // LANES, (BLOCK - 1 - r0) % LANES
            lane = lax.broadcasted_iota(jnp.int32, (CHUNK, LANES), 1)
            row = lax.broadcasted_iota(jnp.int32, (CHUNK, LANES), 0)
            near = lane - row < LANES - part
            own = row + (row0 + r0)
            info = info_ref[row0 + r0 : row0 + r0 + CHUNK, 0:2]
            start = jnp.broadcast_to(info[:, 0:1].astype(jnp.int32), (CHUNK, LANES))
            shade = jnp.broadcast_to(info[:, 1:2], (CHUNK, LANES))

            def turned(t):
                low = (t % columns) * LANES
                return pltpu.roll(
                    lean[rows, low : low + LANES], LANES - part, 1, stride=1, stride_axis=0
                )

            top, this = None, turned(whole)
            for t in range(columns):
                after = turned(t + whole + 1)
                at = slice(t * LANES, (t + 1) * LANES)
                score = raw[rows, at] + jnp.where(near, this, after)
                this = after
                if t * LANES < old:
                    score = score + shade
                else:
                    place = lane + (t * LANES - old)
                    seen = place >= start
                    if (t + 1) * LANES - old > row0:
                        seen = seen & (place <= own)
                    score = jnp.where(seen, score, MASKED)
                raw[rows, at] = score
                top = score if top is None else jnp.maximum(top, score)
            tops[rows, :] = top
        top = jnp.max(tops[...], axis=1, keepdims=True)
        tops[...] = jnp.broadcast_to(top, (BLOCK, LANES))
        for chunk in range(BLOCK // CHUNK):
            r0 = chunk * CHUNK
            rows = slice(r0, r0 + CHUNK)
            top = tops[rows, :]
            total = jnp.zeros((CHUNK, LANES), F32)
            for low in range(0, width, LANES):
                weight = jnp.exp2((raw[rows, low : low + LANES] - top) * (SCALE * LOG2E))
                total = total + weight
                e_ref[row0 + r0 : row0 + r0 + CHUNK, low : low + LANES] = weight.astype(BF16)
            sums[rows, :] = total
        total = jnp.sum(sums[...], axis=1, keepdims=True)
        inv_ref[row0 : row0 + BLOCK, :] = jnp.broadcast_to(1.0 / total, (BLOCK, DH))
        mix[row0 : row0 + BLOCK, :] = mm(
            e_ref[row0 : row0 + BLOCK, :width], values[:width, :], NN
        )
    o_ref[...] = (mix[...] * inv_ref[...]).astype(BF16).reshape(parts, seg, DH)


def attend(query, content_shift, position_shift, keys, values, table_rev, info, cuts):
    parts, group, seg, cols = query.shape
    rows = keys.shape[2]
    queries, key_count, heads = parts * seg, parts * rows, cols // DH
    by_head = lambda size: pl.BlockSpec((parts, None, size, DH), lambda s, h: (0, s, 0, h))
    grid_spec = pl.GridSpec(
        grid=(group, heads),
        in_specs=[
            by_head(seg),
            pl.BlockSpec((1, DH), lambda s, h: (0, h)),
            pl.BlockSpec((1, DH), lambda s, h: (0, h)),
            by_head(rows),
            by_head(rows),
            pl.BlockSpec((key_count, DH), lambda s, h: (0, h)),
            pl.BlockSpec((None, queries, LANES), lambda s, h: (s, 0, 0)),
        ],
        out_specs=[
            pl.BlockSpec((None, None, queries, key_count), lambda s, h: (s, h, 0, 0)),
            pl.BlockSpec((None, None, queries, DH), lambda s, h: (s, h, 0, 0)),
            by_head(seg),
            by_head(seg),
            by_head(seg),
        ],
        scratch_shapes=[
            pltpu.VMEM((key_count, DH), BF16),
            pltpu.VMEM((key_count, DH), BF16),
            pltpu.VMEM((BLOCK, key_count), F32),
            pltpu.VMEM((BLOCK, key_count), F32),
            pltpu.VMEM((queries, DH), F32),
            pltpu.VMEM((BLOCK, LANES), F32),
            pltpu.VMEM((BLOCK, LANES), F32),
        ],
    )
    small = jax.ShapeDtypeStruct((parts, group, seg, cols), BF16)
    return pl.pallas_call(
        functools.partial(attend_kernel, cuts),
        grid_spec=grid_spec,
        out_shape=[
            jax.ShapeDtypeStruct((group, heads, queries, key_count), BF16),
            jax.ShapeDtypeStruct((group, heads, queries, DH), F32),
            small,
            small,
            small,
        ],
        compiler_params=pltpu.CompilerParams(
            dimension_semantics=("arbitrary", "arbitrary"), vmem_limit_bytes=VMEM_LIMIT
        ),
        cost_estimate=cost(40),
        name="attend",
    )(query, content_shift, position_shift, keys, values, table_rev, info)


def pull_kernel(
    cuts, e_ref, inv_ref, o_ref, g_ref, cq_ref, pq_ref, k_ref, v_ref, t_ref,
    dq_ref, dk_ref, dv_ref, ks_ref, vs_ref, dt_ref, sums_ref,
    keys, values, grad, prob, part, score, lean, key_sum, value_sum,
):
    stream = pl.program_id(1)
    parts, seg, _ = g_ref.shape
    queries = parts * seg
    old = parts * (cuts[0] + cuts[1])
    in_place_order(k_ref, keys, cuts)
    in_place_order(v_ref, values, cuts)
    grad[...] = (g_ref[...].reshape(queries, DH).astype(F32) * inv_ref[...]).astype(BF16)
    attended = o_ref[...].reshape(queries, DH)
    content_q = cq_ref[...].reshape(queries, DH)
    position_q = pq_ref[...].reshape(queries, DH)

    @pl.when(stream == 0)
    def _():
        dt_ref[...] = jnp.zeros_like(dt_ref)
        sums_ref[...] = jnp.zeros_like(sums_ref)

    key_sum[...] = jnp.zeros_like(key_sum)
    value_sum[...] = jnp.zeros_like(value_sum)
    content_total = jnp.zeros((1, DH), F32)
    position_total = jnp.zeros((1, DH), F32)
    query_total = jnp.zeros((1, DH), F32)
    flip = flip_matrix(BF16)
    turn = lambda rows: mm(flip, rows, NN).astype(BF16)
    for block in range(queries // BLOCK):
        row0 = block * BLOCK
        width = old + row0 + BLOCK
        skip = queries - BLOCK - row0
        rows = slice(row0, row0 + BLOCK)
        grad_back = turn(grad[rows, :])
        dots_back = jnp.sum(
            grad_back.astype(F32) * turn(attended[rows]).astype(F32), axis=1, keepdims=True
        )
        content_back = turn(content_q[rows])
        position_back = turn(position_q[rows])
        prob[:, :width] = mm(grad_back, values[:width, :], NT)
        both = mm(jnp.concatenate([flip, grad[rows, :].T], axis=0), e_ref[rows, :width], NN)
        part[:, :width] = both[:BLOCK]
        value_sum[:, :width] += both[BLOCK:]
        for chunk in range(BLOCK // CHUNK):
            r0 = chunk * CHUNK
            rows_here = slice(r0, r0 + CHUNK)
            columns = width // LANES
            whole, part_shift = r0 // LANES, r0 % LANES
            lane = lax.broadcasted_iota(jnp.int32, (CHUNK, LANES), 1)
            row = lax.broadcasted_iota(jnp.int32, (CHUNK, LANES), 0)
            wrapped = lane - row < part_shift
            mean = jnp.broadcast_to(dots_back[rows_here], (CHUNK, LANES))
            before = jnp.zeros((CHUNK, LANES), F32)
            for t in range(whole):
                lean[rows_here, t * LANES : (t + 1) * LANES] = before.astype(BF16)
            for t in range(columns):
                at = slice(t * LANES, (t + 1) * LANES)
                change = part[rows_here, at] * (prob[rows_here, at] - mean)
                score[rows_here, at] = change.astype(BF16)
                if t + whole < columns:
                    turned = pltpu.roll(change, part_shift, 1, stride=1, stride_axis=0)
                    lean[rows_here, (t + whole) * LANES : (t + whole + 1) * LANES] = jnp.where(
                        wrapped, before, turned
                    ).astype(BF16)
                    before = turned
        content_grad = (mm(score[:, :width], keys[:width, :], NN) * SCALE).astype(BF16).astype(F32)
        position_grad = (
            (mm(lean[:, :width], t_ref[skip : skip + width, :], NN) * SCALE)
            .astype(BF16)
            .astype(F32)
        )
        query_grad = turn((content_grad + position_grad).astype(BF16))
        content_total += jnp.sum(content_grad, axis=0, keepdims=True)
        position_total += jnp.sum(position_grad, axis=0, keepdims=True)
        query_total += jnp.sum(query_grad.astype(F32), axis=0, keepdims=True)
        dq_ref[rows, :] = query_grad
        key_sum[:, :width] += mm(content_back, score[:, :width], TN)
        dt_ref[:, skip : skip + width] += mm(position_back, lean[:, :width], TN) * SCALE
    key_cols = (key_sum[...] * SCALE).astype(BF16)
    value_cols = value_sum[...].astype(BF16)
    dk_ref[...] = key_cols
    dv_ref[...] = value_cols
    ks_ref[...] = (key_sum[:, old:] * SCALE).T.astype(BF16)
    vs_ref[...] = value_sum[:, old:].T.astype(BF16)
    ones = jnp.ones((8, key_cols.shape[1]), BF16)
    key_total = mm(ones, key_cols, NT)[0:1]
    value_total = mm(ones, value_cols, NT)[0:1]
    sums_ref[...] += jnp.concatenate(
        [
            content_total,
            position_total,
            query_total,
            key_total,
            value_total,
            jnp.zeros((3, DH), F32),
        ],
        axis=0,
    )


def pull(head, weights, inverse, attended, out_grad, content_q, position_q, keys, values, table_rev, cuts):
    parts, group, seg, cols = out_grad.shape
    rows = keys.shape[2]
    queries, key_count = parts * seg, parts * rows
    by_head = lambda size: pl.BlockSpec((parts, None, size, DH), lambda h, s: (0, s, 0, head))
    by_row = lambda: pl.BlockSpec((None, queries, DH), lambda h, s: (s, 0, h))
    by_place = lambda: pl.BlockSpec((None, DH, key_count), lambda h, s: (s, h, 0))
    grid_spec = pl.GridSpec(
        grid=(1, group),
        in_specs=[
            pl.BlockSpec((None, None, queries, key_count), lambda h, s: (s, head, 0, 0)),
            pl.BlockSpec((None, None, queries, DH), lambda h, s: (s, head, 0, 0)),
            by_head(seg),
            by_head(seg),
            by_head(seg),
            by_head(seg),
            by_head(rows),
            by_head(rows),
            pl.BlockSpec((key_count, DH), lambda h, s: (0, head)),
        ],
        out_specs=[
            by_row(),
            by_place(),
            by_place(),
            by_row(),
            by_row(),
            pl.BlockSpec((None, DH, key_count), lambda h, s: (h, 0, 0)),
            pl.BlockSpec((None, 8, DH), lambda h, s: (h, 0, 0)),
        ],
        scratch_shapes=[
            pltpu.VMEM((key_count, DH), BF16),
            pltpu.VMEM((key_count, DH), BF16),
            pltpu.VMEM((queries, DH), BF16),
            pltpu.VMEM((BLOCK, key_count), F32),
            pltpu.VMEM((BLOCK, key_count), F32),
            pltpu.VMEM((BLOCK, key_count), BF16),
            pltpu.VMEM((BLOCK, key_count), BF16),
            pltpu.VMEM((DH, key_count), F32),
            pltpu.VMEM((DH, key_count), F32),
        ],
    )
    return pl.pallas_call(
        functools.partial(pull_kernel, cuts),
        grid_spec=grid_spec,
        out_shape=[
            jax.ShapeDtypeStruct((group, queries, DH), BF16),
            jax.ShapeDtypeStruct((group, DH, key_count), BF16),
            jax.ShapeDtypeStruct((group, DH, key_count), BF16),
            jax.ShapeDtypeStruct((group, queries, DH), BF16),
            jax.ShapeDtypeStruct((group, queries, DH), BF16),
            jax.ShapeDtypeStruct((1, DH, key_count), F32),
            jax.ShapeDtypeStruct((1, 8, DH), F32),
        ],
        compiler_params=pltpu.CompilerParams(
            dimension_semantics=("arbitrary", "arbitrary"), vmem_limit_bytes=VMEM_LIMIT
        ),
        cost_estimate=cost(39),
        name="pull",
    )(weights, inverse, attended, out_grad, content_q, position_q, keys, values, table_rev)


def project_kernel(
    cuts, rows_ref, gain_ref, shift_ref, w_ref, old_ref, mem_ref, seg_ref, q_ref, k_ref, v_ref, normed
):
    rows, width = rows_ref.shape
    cols = k_ref.shape[1]
    step = 32
    for low in range(0, rows, step):
        wide = rows_ref[low : low + step, :].astype(F32)
        centred = wide - jnp.mean(wide, axis=1, keepdims=True)
        rate = lax.rsqrt(jnp.mean(centred * centred, axis=1, keepdims=True) + EPSILON)
        normed[low : low + step, :] = (centred * rate * gain_ref[...] + shift_ref[...]).astype(BF16)
    cut = cuts[0] + cuts[1]
    old_ref[...] = normed[: cuts[0], :]
    mem_ref[...] = normed[cuts[0] : cut, :]
    seg_ref[...] = normed[cut:, :]
    q_ref[...] = mm(normed[cut:, :], w_ref[:, :cols], NN)
    k_ref[...] = mm(normed[...], w_ref[:, cols : 2 * cols], NN).astype(BF16)
    v_ref[...] = mm(normed[...], w_ref[:, 2 * cols : 3 * cols], NN).astype(BF16)


def project(rows_all, gain, shift, columns, cuts):
    parts, group, each, width = rows_all.shape
    cols = columns.shape[1] // 4
    block = lambda size, wide: pl.BlockSpec((None, None, size, wide), lambda p, s: (p, s, 0, 0))
    placed = lambda size: pl.BlockSpec((None, size, width), lambda p, s: (s, p, 0))
    whole = lambda *shape: pl.BlockSpec(shape, lambda p, s: (0,) * len(shape))
    shape = lambda size, kind: jax.ShapeDtypeStruct((parts, group, size, cols), kind)
    return pl.pallas_call(
        functools.partial(project_kernel, cuts),
        grid_spec=pl.GridSpec(
            grid=(parts, group),
            in_specs=[
                block(each, width),
                whole(1, width),
                whole(1, width),
                whole(width, 4 * cols),
            ],
            out_specs=[placed(size) for size in cuts]
            + [block(cuts[2], cols), block(each, cols), block(each, cols)],
            scratch_shapes=[pltpu.VMEM((each, width), BF16)],
        ),
        out_shape=[jax.ShapeDtypeStruct((group, parts * size, width), BF16) for size in cuts]
        + [shape(cuts[2], F32), shape(each, BF16), shape(each, BF16)],
        compiler_params=pltpu.CompilerParams(
            dimension_semantics=("arbitrary", "arbitrary"), vmem_limit_bytes=VMEM_LIMIT
        ),
        cost_estimate=cost(17),
        name="project",
    )(rows_all, gain, shift, columns)


def gelu_both(x):
    near = jnp.abs(x)
    t = 1.0 / (1.0 + (0.3275911 * math.sqrt(0.5)) * near)
    bell = jnp.exp2((x * x) * (-0.5 * LOG2E))
    tail = 0.5 * 1.061405429
    for factor in (-1.453152027, 1.421413741, -0.284496736, 0.254829592):
        tail = tail * t + 0.5 * factor
    tail = tail * t * bell
    below = jnp.where(x < 0.0, tail, 1.0 - tail)
    return x * below, below + x * bell * (1.0 / math.sqrt(2.0 * math.pi))


def forward_back_kernel(
    last, parts, pair, n_ref, c_ref, *rest,
):
    up_refs, down_refs, shift_ref = rest[:parts], rest[parts : parts + pair], rest[parts + pair]
    rest = rest[parts + pair + 1 :]
    if last:
        part_in, grad_in, part_out, part_far, grad_out, grad_far, late_ref, sums_ref = rest[:8]
        pre, slope, hidden, act, up_out, down_out, sems, part_ref, grad_ref = rest[8:]
    else:
        part_ref, grad_ref, late_ref, sums_ref = rest[:4]
        pre, slope, hidden, act, up_out, down_out, sems = rest[4:]
    tile = pl.program_id(0)
    tiles = pl.num_programs(0)
    cols, units = up_refs[0].shape
    unit_cols, width = down_refs[0].shape
    rows = n_ref.shape[0]
    slot = lax.rem(tile, 2)
    up_weight = jnp.concatenate([ref[...] for ref in up_refs], axis=0)
    down_weight = jnp.concatenate([ref[...] for ref in down_refs], axis=0)

    def copies(at, index):
        return (
            pltpu.make_async_copy(
                up_out.at[at],
                late_ref.at[:, pl.ds(0, cols), pl.ds(pl.multiple_of(index * units, units), units)],
                sems.at[at, 0],
            ),
            pltpu.make_async_copy(
                down_out.at[at],
                late_ref.at[pl.ds(index * pair, pair), pl.ds(cols, unit_cols), :],
                sems.at[at, 1],
            ),
        )

    @pl.when(tile == 0)
    def _():
        if last:
            part_ref[...] = part_in[...]
            grad_ref[...] = grad_in[...]
        else:
            part_ref[...] = jnp.zeros_like(part_ref)
            grad_ref[...] = jnp.zeros_like(grad_ref)

    pre[...] = mm(n_ref[...], up_weight, NN)
    slope[...] = mm(c_ref[...], down_weight, NT)
    for low in range(0, rows, 16):
        some = slice(low, low + 16)
        value, change = gelu_both(pre[some, :] + shift_ref[...])
        hidden[some, :] = value.astype(BF16)
        act[some, :] = (change * slope[some, :]).astype(BF16)
    part_ref[...] += mm(hidden[...], down_weight, NN)
    grad_ref[...] += mm(act[...], up_weight, NT)
    sums_ref[...] = jnp.sum(act[...].astype(F32), axis=0, keepdims=True)

    @pl.when(tile >= 2)
    def _():
        for copy in copies(slot, tile - 2):
            copy.wait()

    up_out[slot] = mm(n_ref[...], act[...], TN).astype(BF16).reshape(parts, cols, units)
    down_out[slot] = mm(hidden[...], c_ref[...], TN).astype(BF16).reshape(pair, unit_cols, width)
    for copy in copies(slot, tile):
        copy.start()

    @pl.when(tile == tiles - 1)
    def _():
        if last:
            part_out[...] = part_ref[: rows // 2, :]
            part_far[...] = part_ref[rows // 2 :, :].astype(BF16)
            grad_out[...] = grad_ref[: rows // 2, :]
            grad_far[...] = grad_ref[rows // 2 :, :].astype(BF16)
        for copy in (copies(1 - slot, tile - 1) if parts > pair else ()) + copies(slot, tile):
            copy.wait()


def forward_back(normed, cot, gathered, shift, carry):
    parts, _, width = gathered.shape
    rows = normed.shape[0]
    cols = width // parts
    unit_cols = shift.shape[1] // parts
    pair = 2
    units = pair * unit_cols
    last = len(carry) > 0
    one = pl.Buffered(1)
    whole = lambda *shape: pl.BlockSpec(shape, lambda t: (0,) * len(shape), pipeline_mode=one)
    up = lambda p: pl.BlockSpec((None, cols, units), lambda t: (p, 0, t))
    down = lambda i: pl.BlockSpec(
        (None, unit_cols, width), lambda t: (t * pair + i, cols // unit_cols, 0)
    )
    if last:
        sums = [((rows // 2, width), F32), ((rows // 2, width), BF16)] * 2
    else:
        sums = [((rows, width), F32)] * 2
    return pl.pallas_call(
        functools.partial(forward_back_kernel, last, parts, pair),
        grid_spec=pl.GridSpec(
            grid=(parts // pair,),
            in_specs=[
                whole(rows, width),
                whole(rows, width),
            ]
            + [up(p) for p in range(parts)]
            + [down(i) for i in range(pair)]
            + [pl.BlockSpec((1, units), lambda t: (0, t))]
            + [whole(rows, width) for _ in carry],
            out_specs=[whole(*shape) for shape, _ in sums]
            + [
                pl.BlockSpec(memory_space=pl.ANY),
                pl.BlockSpec((1, units), lambda t: (0, t)),
            ],
            scratch_shapes=[
                pltpu.VMEM((rows, units), F32),
                pltpu.VMEM((rows, units), F32),
                pltpu.VMEM((rows, units), BF16),
                pltpu.VMEM((rows, units), BF16),
                pltpu.VMEM((2, parts, cols, units), BF16),
                pltpu.VMEM((2, pair, unit_cols, width), BF16),
                pltpu.SemaphoreType.DMA((2, 2)),
            ]
            + [pltpu.VMEM((rows, width), F32) for _ in carry],
        ),
        out_shape=[jax.ShapeDtypeStruct(shape, kind) for shape, kind in sums]
        + [
            jax.ShapeDtypeStruct((parts, cols + unit_cols, width), BF16),
            jax.ShapeDtypeStruct((1, parts * unit_cols), F32),
        ],
        compiler_params=pltpu.CompilerParams(
            dimension_semantics=("arbitrary",), vmem_limit_bytes=VMEM_LIMIT
        ),
        cost_estimate=cost(29),
        name="forward_back",
    )(normed, cot, *[gathered] * (parts + pair), shift, *carry)


def leave_kernel(a_ref, s_ref, w_ref, shift_ref, gain_ref, bias_ref, flat_ref, m_ref, n_ref):
    parts = a_ref.shape[0]
    flat_ref[...] = jnp.concatenate([a_ref[part] for part in range(parts)], axis=1)
    m_ref[...] = s_ref[...].astype(F32) + (mm(flat_ref[...], w_ref[...], NN) + shift_ref[...])
    step = 16
    for low in range(0, m_ref.shape[0], step):
        unit, _ = standardise(m_ref[low : low + step, :])
        n_ref[low : low + step, :] = (unit * gain_ref[...] + bias_ref[...]).astype(BF16)


def leave(mixed_heads, segment, base, weight, shift, gain, bias):
    parts, group, seg, cols = mixed_heads.shape
    width = parts * cols
    rows = lambda: pl.BlockSpec((None, seg, width), lambda s: (s, 0, 0))
    vector = lambda: pl.BlockSpec((1, width), lambda s: (0, 0))
    shape = lambda kind: jax.ShapeDtypeStruct((group, seg, width), kind)
    return pl.pallas_call(
        leave_kernel,
        grid_spec=pl.GridSpec(
            grid=(group,),
            in_specs=[
                pl.BlockSpec((parts, None, seg, cols), lambda s: (0, s, 0, 0)),
                pl.BlockSpec((None, seg, width), lambda s: (s + base, 0, 0)),
                pl.BlockSpec((width, width), lambda s: (0, 0)),
                vector(),
                vector(),
                vector(),
            ],
            out_specs=[rows(), rows(), rows()],
        ),
        out_shape=[shape(BF16), shape(F32), shape(BF16)],
        compiler_params=pltpu.CompilerParams(vmem_limit_bytes=VMEM_LIMIT),
        cost_estimate=cost(6),
        name="leave",
    )(mixed_heads, segment, weight, shift, gain, bias)


def enter_kernel(
    m_ref, g_ref, far_ref, c_ref, w_ref, gain_ref, mg_ref, b_ref, a_ref, sums_ref
):
    @pl.when(pl.program_id(0) == 0)
    def _():
        sums_ref[...] = jnp.zeros_like(sums_ref)

    parts = a_ref.shape[0]
    rows, width = m_ref.shape
    step = 32
    total = [jnp.zeros((1, width), F32) for _ in range(4)]
    for low in range(0, rows, step):
        at = slice(low, low + step)
        unit, rate = standardise(m_ref[at, :])
        grad = g_ref[at, :] + far_ref[at, :].astype(F32)
        cot = c_ref[at, :].astype(F32)
        middle_grad = cot + standardise_back(unit, rate, grad, gain_ref[...])
        branch = middle_grad.astype(BF16)
        mg_ref[at, :] = middle_grad
        b_ref[at, :] = branch
        for i, value in enumerate((branch.astype(F32), grad * unit, grad, cot)):
            total[i] = total[i] + jnp.sum(value, axis=0, keepdims=True)
    sums_ref[...] += jnp.concatenate(total + [jnp.zeros((4, width), F32)], axis=0)
    for part in range(parts):
        low = part * a_ref.shape[2]
        weight = w_ref[low : low + a_ref.shape[2], :]
        a_ref[part] = mm(b_ref[...], weight, NT).astype(BF16)


def enter(middle, grad, far, cot, base, weight, gain, parts):
    group, seg, width = middle.shape
    cols = width // parts
    rows = lambda: pl.BlockSpec((None, seg, width), lambda s: (s, 0, 0))
    later = lambda: pl.BlockSpec((None, seg, width), lambda s: (s + base, 0, 0))
    shape = lambda kind: jax.ShapeDtypeStruct((group, seg, width), kind)
    return pl.pallas_call(
        enter_kernel,
        grid_spec=pl.GridSpec(
            grid=(group,),
            in_specs=[
                rows(),
                later(),
                later(),
                later(),
                pl.BlockSpec((width, width), lambda s: (0, 0)),
                pl.BlockSpec((1, width), lambda s: (0, 0)),
            ],
            out_specs=[
                rows(),
                rows(),
                pl.BlockSpec((parts, None, seg, cols), lambda s: (0, s, 0, 0)),
                pl.BlockSpec((8, width), lambda s: (0, 0)),
            ],
        ),
        out_shape=[
            shape(F32),
            shape(BF16),
            jax.ShapeDtypeStruct((parts, group, seg, cols), BF16),
            jax.ShapeDtypeStruct((8, width), F32),
        ],
        compiler_params=pltpu.CompilerParams(
            dimension_semantics=("arbitrary",), vmem_limit_bytes=VMEM_LIMIT
        ),
        cost_estimate=cost(7),
        name="enter",
    )(middle, grad, far, cot, weight, gain)


def compress_kernel(low, rows_ref, w_ref, shift_ref, out_ref, wide):
    count = out_ref.shape[0]
    cols = out_ref.shape[1]
    blocks = wide.shape[0]
    for at in range(blocks):
        wide[at] = rows_ref[low : low + 3 * count, at * LANES : (at + 1) * LANES].astype(F32)
    total = jnp.broadcast_to(shift_ref[...], (count, cols))
    for k in range(3):
        every = jnp.concatenate(
            [wide[at, pl.ds(k, count, stride=3), :] for at in range(blocks)], axis=1
        ).astype(BF16)
        total = total + mm(every, w_ref[:, k * cols : (k + 1) * cols], NN)
    out_ref[...] = total.astype(BF16)


def compress(rows_all, columns, shift, low, count):
    parts, group, each, width = rows_all.shape
    cols = columns.shape[1] // 3
    return pl.pallas_call(
        functools.partial(compress_kernel, low),
        grid_spec=pl.GridSpec(
            grid=(parts, group),
            in_specs=[
                pl.BlockSpec((None, None, each, width), lambda p, s: (p, s, 0, 0)),
                pl.BlockSpec((width, 3 * cols), lambda p, s: (0, 0)),
                pl.BlockSpec((1, cols), lambda p, s: (0, 0)),
            ],
            out_specs=pl.BlockSpec((None, None, count, cols), lambda p, s: (p, s, 0, 0)),
            scratch_shapes=[pltpu.VMEM((width // LANES, 3 * count, LANES), F32)],
        ),
        out_shape=jax.ShapeDtypeStruct((parts, group, count, cols), BF16),
        compiler_params=pltpu.CompilerParams(
            dimension_semantics=("arbitrary", "arbitrary"), vmem_limit_bytes=VMEM_LIMIT
        ),
        cost_estimate=cost(6.5),
        name="compress",
    )(rows_all, columns, shift)


def lay_out_kernel(
    parts, unit_cols, core_ref, a_ref, b_ref, c_ref, d_ref, up_ref, down_ref
):
    flipped = core_ref[0] == 1
    for half, (mine_ref, far_ref) in enumerate(((a_ref, c_ref), (b_ref, d_ref))):
        mine, far = mine_ref[...].astype(F32), far_ref[...].astype(F32)
        for core, value in enumerate(
            (jnp.where(flipped, far, mine), jnp.where(flipped, mine, far))
        ):
            for part in range(parts):
                at = ((part * 2 + core) * 2 + half) * unit_cols
                up_ref[:, at : at + unit_cols] = value[
                    0, :, part * unit_cols : (part + 1) * unit_cols
                ]
            down_ref[2 * core + half] = value[1]


def lay_out(core, mine, far, parts):
    _, rows, width = mine[0].shape
    step = rows // 4 if rows % 64 == 0 else rows
    half = lambda: pl.BlockSpec((2, step, width), lambda r, *_: (0, r, 0))
    return pl.pallas_call(
        functools.partial(lay_out_kernel, parts, rows),
        grid_spec=pltpu.PrefetchScalarGridSpec(
            num_scalar_prefetch=1,
            grid=(rows // step,),
            in_specs=[half(), half(), half(), half()],
            out_specs=[
                pl.BlockSpec((step, 4 * width), lambda r, *_: (r, 0)),
                pl.BlockSpec((4, step, width), lambda r, *_: (0, r, 0)),
            ],
        ),
        out_shape=[
            jax.ShapeDtypeStruct((rows, 4 * width), F32),
            jax.ShapeDtypeStruct((4, rows, width), F32),
        ],
        compiler_params=pltpu.CompilerParams(vmem_limit_bytes=VMEM_LIMIT),
        cost_estimate=cost(4),
        name="lay_out",
    )(core.reshape(1), *mine, *far)


def lay_squares_kernel(in_ref, *out_refs):
    parts = in_ref.shape[0]
    cols = in_ref.shape[2] // len(out_refs)
    for at, out_ref in enumerate(out_refs):
        for part in range(parts):
            out_ref[:, part * cols : (part + 1) * cols] = in_ref[
                part, :, at * cols : (at + 1) * cols
            ].astype(F32)


def lay_squares(summed, rows):
    parts, _, wide = summed.shape
    width = parts * wide // 4
    step = rows // 2
    return pl.pallas_call(
        lay_squares_kernel,
        grid_spec=pl.GridSpec(
            grid=(2,),
            in_specs=[pl.BlockSpec((parts, step, wide), lambda i: (0, i, 0))],
            out_specs=[pl.BlockSpec((step, width), lambda i: (i, 0)) for _ in range(4)],
        ),
        out_shape=[jax.ShapeDtypeStruct((rows, width), F32) for _ in range(4)],
        compiler_params=pltpu.CompilerParams(vmem_limit_bytes=VMEM_LIMIT),
        cost_estimate=cost(2.5),
        name="lay_squares",
    )(summed)


def settle_kernel(heads, me_ref, old_ref, mem_ref, seg_ref, *rest):
    q_refs, k_refs, v_refs, ks_refs, vs_refs, dt_refs, sums_refs = (
        rest[i * heads : (i + 1) * heads] for i in range(7)
    )
    w_ref, table_ref, gain_ref, shift_ref, small_ref, part_ref, out_ref, total = rest[7 * heads :]
    stream = pl.program_id(0)
    parts, rows, wide = out_ref.shape
    cols = wide // 4
    width = parts * cols

    @pl.when(stream == 0)
    def _():
        total[...] = jnp.zeros_like(total)

    low = old_ref.shape[0]
    high = low + mem_ref.shape[0]
    pair = lambda first, last: [ref[:, first:last] for ref in (*k_refs, *v_refs)]
    total[...] += mm(
        jnp.concatenate([ref[...].T for ref in q_refs] + pair(high, high + seg_ref.shape[0]), axis=0),
        seg_ref[...],
        NN,
    )
    total[cols:, :] += mm(jnp.concatenate(pair(low, high), axis=0), mem_ref[...], NN)
    total[cols:, :] += mm(jnp.concatenate(pair(0, low), axis=0), old_ref[...], NN)
    three = jnp.concatenate([ref[...] for ref in (*q_refs, *ks_refs, *vs_refs)], axis=1)
    part = mm(three, w_ref[:, : 3 * cols], NT).astype(BF16)
    part_ref[...] = part.reshape(part_ref.shape)

    @pl.when(stream == pl.num_programs(0) - 1)
    def _():
        places = jnp.concatenate([ref[0].astype(BF16) for ref in dt_refs], axis=0)
        rel = mm(places, table_ref[...], NN)
        line = lambda row: jnp.concatenate(
            [ref[0, row : row + 1, :] for ref in sums_refs], axis=1
        )
        row_sums = jnp.concatenate([line(2), line(3), line(4)], axis=1)
        pieces, rest = [], row_sums
        for _ in range(3):
            pieces.append(rest.astype(BF16))
            rest = rest - pieces[-1].astype(F32)
        pieces = jnp.concatenate(pieces + [jnp.zeros((13, 3 * cols), BF16)], axis=0)
        shift_grad = jnp.sum(mm(pieces, w_ref[:, : 3 * cols], NT), axis=0, keepdims=True)
        weight = w_ref[:, : 3 * cols].astype(F32)
        along = jnp.sum(weight.T * total[...], axis=0, keepdims=True)
        gain_grad = (along - shift_ref[...] * shift_grad) / gain_ref[...]
        for at in range(parts):
            low, high = at * cols, (at + 1) * cols
            out_ref[at, :cols, : 3 * cols] = total[:, low:high].T.astype(BF16)
            out_ref[at, :cols, 3 * cols :] = rel[:, low:high].T.astype(BF16)
            mine = (me_ref[0] == at).astype(F32)
            none = jnp.zeros((1, 2 * cols), F32)
            first = jnp.concatenate([gain_grad[:, low:high], shift_grad[:, low:high], none], axis=1)
            second = jnp.concatenate([none, mine * line(0), mine * line(1)], axis=1)
            added = jnp.concatenate([first, second, jnp.zeros((14, wide), F32)], axis=0)
            out_ref[at, cols:, :] = (small_ref[at] + added).astype(BF16)


def settle(me, normed, grads, columns, table, gain, shift, small, parts):
    group, queries, width = normed[2].shape
    cols = width // parts
    wide = 4 * cols
    by_kind = list(zip(*grads))
    block = lambda array: pl.BlockSpec((None, *array.shape[1:]), lambda s, *_: (s, 0, 0))
    whole = lambda *shape: pl.BlockSpec(
        shape, lambda s, *_: (0,) * len(shape), pipeline_mode=pl.Buffered(1)
    )
    return pl.pallas_call(
        functools.partial(settle_kernel, len(grads)),
        grid_spec=pltpu.PrefetchScalarGridSpec(
            num_scalar_prefetch=1,
            grid=(group,),
            in_specs=[block(rows) for rows in normed]
            + [block(each) for kind in by_kind[:5] for each in kind]
            + [whole(*each.shape) for kind in by_kind[5:] for each in kind]
            + [
                whole(*columns.shape),
                whole(*table.shape),
                whole(1, width),
                whole(1, width),
                whole(*small.shape),
            ],
            out_specs=[
                pl.BlockSpec((parts, None, queries // parts, width), lambda s, *_: (0, s, 0, 0)),
                whole(parts, cols + 16, wide),
            ],
            scratch_shapes=[pltpu.VMEM((3 * cols, width), F32)],
        ),
        out_shape=[
            jax.ShapeDtypeStruct((parts, group, queries // parts, width), BF16),
            jax.ShapeDtypeStruct((parts, cols + 16, wide), BF16),
        ],
        compiler_params=pltpu.CompilerParams(
            dimension_semantics=("arbitrary",), vmem_limit_bytes=VMEM_LIMIT
        ),
        cost_estimate=cost(14),
        name="settle",
    )(
        me.reshape(1), *normed, *[each for kind in by_kind for each in kind], columns, table, gain, shift,
        small,
    )


def standardise(rows):
    mean = jnp.mean(rows, axis=-1, keepdims=True)
    centred = rows - mean
    rate = lax.rsqrt(jnp.mean(centred * centred, axis=-1, keepdims=True) + EPSILON)
    return centred * rate, rate


def standardise_back(unit, rate, grad, gain):
    scaled = grad * gain
    mean = jnp.mean(scaled, axis=-1, keepdims=True)
    along = jnp.mean(scaled * unit, axis=-1, keepdims=True)
    return rate * (scaled - mean - unit * along)


def sinusoid_reversed(rows, width):
    positions = (rows - 1 - jnp.arange(rows, dtype=jnp.int32)).astype(F32)[:, None]
    frequency = jnp.exp(
        jnp.arange(width // 2, dtype=F32) * (-2.0 * math.log(10000.0) / width)
    )
    angles = positions * frequency[None, :]
    return jnp.concatenate([jnp.sin(angles), jnp.cos(angles)], axis=1).astype(BF16)


def dot(left, right):
    return mm(left, right, NN)


def swap(value):
    return lax.ppermute(value, "core", [(0, 1), (1, 0)])


def exchange(blocks, name, axis=0):
    count = lax.axis_size(name)
    me = lax.axis_index(name)
    block = lambda at: lax.dynamic_index_in_dim(blocks, at, axis, keepdims=False)
    return [block(me)] + [
        lax.ppermute(block(me ^ apart), name, [(i, i ^ apart) for i in range(count)])
        for apart in range(1, count)
    ]


def collect(block, name):
    count = lax.axis_size(name)
    me = lax.axis_index(name)
    found = jnp.stack(
        [block]
        + [
            lax.ppermute(block, name, [(i, i ^ apart) for i in range(count)])
            for apart in range(1, count)
        ]
    )
    return jnp.stack(
        [lax.dynamic_index_in_dim(found, me ^ i, 0, keepdims=False) for i in range(count)]
    )


def add_up(arrays, kind=BF16):
    total = arrays[0].astype(F32)
    for array in arrays[1:]:
        total = total + array.astype(F32)
    return total.astype(kind)


def body(
    segment, memory, compressed, eob, reset, ln1_gain, ln1_bias, w_query, w_key, w_value,
    w_out, out_bias, w_rel, bias_content, bias_position, ln2_gain, ln2_bias, w_up, up_bias,
    w_down, down_bias, conv_weight, conv_bias, cotangent,
):
    parts = lax.axis_size("seq")
    layers = lax.axis_size("z")
    core = lax.axis_index("core")
    me = lax.axis_index("seq")
    group, seg, width = segment.shape
    mem, old = memory.shape[1], compressed.shape[1]
    cuts = (old, mem, seg)
    each = old + mem + seg
    keys_in_all = parts * each
    cols = width // parts
    wide = 4 * cols
    own = group * seg
    unit_cols = w_up.shape[1] // (4 * parts)
    barrier = lax.optimization_barrier

    def by_columns(matrices):
        count = matrices.shape[0]
        sent = matrices.reshape(count, cols, parts, cols).transpose(2, 1, 0, 3)
        return sent.reshape(parts, cols, count * cols)

    up_bias_own = lax.dynamic_slice_in_dim(up_bias, core * 2 * unit_cols, 2 * unit_cols, 0)
    vectors = jnp.concatenate(
        [ln1_gain, ln1_bias, out_bias, ln2_gain, ln2_bias, down_bias, up_bias_own]
    )
    vectors = jnp.pad(vectors.reshape(2, wide), ((0, 14), (0, 0)))
    half = cols // 2
    sent = by_columns(jnp.concatenate([jnp.stack([w_query, w_key, w_value, w_rel]), conv_weight]))
    sent = lax.dynamic_slice_in_dim(sent, core * half, half, 1)
    out_half = lax.dynamic_slice_in_dim(w_out, core * half, half, 0)
    sent = jnp.concatenate([sent, jnp.broadcast_to(out_half, (parts, half, width))], axis=2)
    vectors = jnp.pad(vectors, ((0, 0), (0, 3 * cols + width)))
    sent = jnp.concatenate([sent, jnp.broadcast_to(vectors, (parts, *vectors.shape))], axis=1)
    got = lax.all_to_all(sent, "seq", 0, 0, tiled=True)
    spans = [(0, group)]
    local = [
        jnp.concatenate([compressed[low:high], memory[low:high], segment[low:high]], axis=1)
        for low, high in spans
    ]
    rows_all = [lax.all_gather(local[0], "seq")]
    mine = got[:, :half]
    far = swap(mine)
    columns = jnp.stack(
        [jnp.where(core == 0, mine, far), jnp.where(core == 0, far, mine)], axis=1
    ).reshape(width, 7 * cols + width)
    columns, conv_columns, out_full = (
        columns[:, :wide],
        columns[:, wide : 7 * cols],
        columns[:, 7 * cols :],
    )
    vectors = got[:, half : half + 2, :wide].reshape(parts, 2 * wide).astype(F32)
    gain_one, shift_one, out_shift, gain_two, shift_two, down_shift = (
        vectors[:, cols * i : cols * (i + 1)].reshape(1, width) for i in range(6)
    )
    up_shift = vectors[:, 6 * cols :].reshape(parts, 2, unit_cols).transpose(1, 0, 2)
    up_shift = up_shift.reshape(2, 1, parts * unit_cols)
    up_quarters = lax.dynamic_slice_in_dim(
        w_up.reshape(cols, parts, 2, 2, unit_cols), core, 1, 2
    ).reshape(cols, parts, 2, unit_cols)
    up_quarters = [up_quarters[:, :, i].reshape(cols, width) for i in range(2)]
    down_half = lax.dynamic_slice_in_dim(w_down, core * 2 * unit_cols, 2 * unit_cols, 0)
    down_quarters = [down_half[unit_cols * i : unit_cols * (i + 1)] for i in range(2)]
    first = jnp.concatenate([up_quarters[0], down_quarters[0]], axis=0)
    second = jnp.concatenate([up_quarters[1], down_quarters[1]], axis=0)
    cot_own = cotangent.reshape(own, width)
    cot_both = jnp.concatenate([cot_own, swap(cot_own)], axis=0)

    table_rev = sinusoid_reversed(keys_in_all, width)
    proj_rev = dot(table_rev, columns[:, 3 * cols :]).astype(BF16)
    index = jnp.arange(eob.shape[1], dtype=jnp.int32)[None, :]
    opens = jnp.pad(eob, ((0, 0), (1, 0)))[:, :-1] == 1
    start = lax.cummax(jnp.where(opens, index, 0), axis=1)
    shade = jnp.where((start == 0) & (reset[:, None] == 0), 0.0, MASKED)
    info = jnp.stack([start.astype(F32), shade], axis=2)
    info = jnp.pad(info, ((0, 0), (0, 0), (0, LANES - 2)))
    rows_all[0], proj_rev, info, cot_both, table_rev, columns, conv_columns, out_full, *local = barrier(
        (rows_all[0], proj_rev, info, cot_both, table_rev, columns, conv_columns, out_full, *local)
    )
    rows_all = [rows_all[0]] + [lax.all_gather(rows, "seq") for rows in local[1:]]

    kept, heads = [], []
    for batch, (low, high) in enumerate(spans):
        if batch == len(spans) - 1:
            rows_all[batch], first, *heads = barrier((rows_all[batch], first, *heads))
            first = lax.all_gather(first, "seq")
        *normed, query, keys, values = project(rows_all[batch], gain_one, shift_one, columns, cuts)
        second, query = barrier((second, query))
        second = lax.all_gather(second, "seq")
        weights, inverse, mixed_heads, content_q, position_q = attend(
            query,
            bias_content.astype(F32).reshape(1, cols),
            bias_position.astype(F32).reshape(1, cols),
            keys,
            values,
            proj_rev,
            info[low:high],
            cuts,
        )
        kept.append((weights, inverse, mixed_heads, content_q, position_q, keys, values))
        heads.append(lax.all_to_all(mixed_heads, "seq", 0, 0, tiled=True))

    mixed_heads, conv_columns = barrier((mixed_heads, conv_columns))
    packed = compress(
        rows_all[0], conv_columns, conv_bias.astype(F32).reshape(1, cols), old, mem // 3
    )
    packed, *heads = barrier((packed, *heads))

    attended, middle, normed_two = [], [], []
    for (low, high), batch in zip(spans, heads):
        one, two, three = leave(batch, segment, low, out_full, out_shift, gain_two, shift_two)
        attended.append(one.reshape(-1, width))
        middle.append(two)
        normed_two.append(three.reshape(-1, width))
    both = jnp.concatenate(normed_two + [swap(rows) for rows in normed_two], axis=0)
    part, part_grad, late_one, unit_one = forward_back(both, cot_both, first, up_shift[0], ())
    late_one = lax.psum_scatter(
        late_one.reshape(-1, width), "seq", scatter_dimension=0, tiled=True
    )
    part, part_far, part_grad, grad_far, late_two, unit_two = forward_back(
        both, cot_both, second, up_shift[1], (part, part_grad)
    )
    grad_far = swap(grad_far)
    by_stream = lambda rows: rows.reshape(group, seg, width)
    middle_grad, branch_grad, head_grad, sums_two = [], [], [], 0.0
    for (low, high), batch in zip(spans, middle):
        one, two, three, four = enter(
            batch, by_stream(part_grad), by_stream(grad_far), cotangent, low, out_full, gain_two, parts
        )
        middle_grad.append(one)
        branch_grad.append(two.reshape(-1, width))
        three, part_grad = barrier((three, part_grad))
        head_grad.append(lax.all_to_all(three, "seq", 0, 0, tiled=True))
        sums_two = sums_two + four
    result = part + swap(part_far).astype(F32) + down_shift
    output = (jnp.concatenate(middle).reshape(own, width) + result).astype(BF16)
    output = output.reshape(group, seg, width)

    out_shift_grad, gain_two_grad, shift_two_grad, down_shift_grad = (
        sums_two[i].reshape(parts, cols) for i in range(4)
    )
    none = jnp.zeros((parts, 2 * cols), F32)
    unit_sums = jnp.stack(
        [unit_one.reshape(parts, unit_cols), unit_two.reshape(parts, unit_cols)], axis=1
    ).reshape(parts, 2 * unit_cols)
    small = jnp.stack(
        [
            jnp.concatenate([none, out_shift_grad, gain_two_grad], axis=1),
            jnp.concatenate([shift_two_grad, down_shift_grad, none], axis=1),
            jnp.concatenate(
                [jnp.where(core == 0, unit_sums, 0.0), jnp.where(core == 1, unit_sums, 0.0)], axis=1
            ),
        ],
        axis=1,
    )
    small = jnp.pad(small, ((0, 0), (0, 13), (0, 0)))
    weights, inverse, mixed_heads, content_q, position_q, keys, values = kept[0]
    out_grad = mm(jnp.concatenate(attended), jnp.concatenate(branch_grad), TN)
    out_grad = out_grad.astype(BF16).reshape(parts, cols, width)
    packed = exchange(packed, "seq")
    late_one, small, out_grad, late_two, output, packed, head_grad = barrier(
        (late_one, small, out_grad, late_two, output, packed, head_grad[0])
    )
    late_two = lax.psum_scatter(
        late_two.reshape(-1, width), "seq", scatter_dimension=0, tiled=True
    )
    late_one = exchange(late_one.reshape(layers, -1, width), "z")
    grads = []
    for head in range(cols // DH):
        grads.append(
            list(
                pull(
                    head, weights, inverse, mixed_heads, head_grad, content_q, position_q, keys,
                    values, proj_rev, cuts,
                )
            )
        )
        if head == 0:
            late_one, head_grad, grads[0][0] = barrier((late_one, head_grad, grads[0][0]))
            late_one = collect(add_up(late_one), "z")
    late_one, late_two, out_grad, grads[-1][0] = barrier(
        (late_one, late_two, out_grad, grads[-1][0])
    )
    late_two = exchange(late_two.reshape(layers, -1, width), "z")
    out_sent = lax.all_to_all(out_grad, "seq", 0, 0, tiled=True)
    seg_part, square_grads = settle(
        me, normed, grads, columns, table_rev, gain_one, shift_one, small, parts
    )
    late_two, out_sent, square_grads = barrier((late_two, out_sent, square_grads))
    summed = lax.all_to_all(square_grads, "seq", 0, 0, tiled=True)
    late_two = collect(add_up(late_two), "z")
    out_sent = jnp.sum(out_sent.astype(F32), axis=0).astype(BF16)
    late_two, out_sent, summed, seg_part = barrier((late_two, out_sent, summed, seg_part))
    squares = parts * (cols + 16)
    summed = jnp.concatenate([summed.reshape(squares, wide), out_sent.reshape(-1, wide)], axis=0)
    summed = lax.psum(summed, ("z", "core"))
    packed = jnp.stack(packed)
    new_compressed = jnp.concatenate(
        [lax.dynamic_index_in_dim(packed, p ^ me, 0, keepdims=False) for p in range(parts)], axis=2
    )
    seg_grad = lax.all_to_all(seg_part, "seq", 0, 0, tiled=True).astype(F32)
    seg_grad = jnp.sum(seg_grad, axis=0).reshape(own, width)
    unit_seg, rate_seg = standardise(segment.reshape(own, width).astype(F32))
    rows_grad = standardise_back(unit_seg, rate_seg, seg_grad, gain_one)
    segment_grad = jnp.concatenate(middle_grad, axis=0) + by_stream(rows_grad)

    halves = [late_one.reshape(2, unit_cols, width), late_two.reshape(2, unit_cols, width)]
    up_w, down_w = lay_out(core, halves, [swap(rows) for rows in halves], parts)
    down_w = down_w.reshape(4 * unit_cols, width)
    summed, output, segment_grad, new_compressed, up_w, down_w = barrier(
        (summed, output, segment_grad, new_compressed, up_w, down_w)
    )
    out_w = summed[squares:].reshape(cols, width).astype(F32)
    summed = summed[:squares].reshape(parts, cols + 16, wide)
    query_w, key_w, value_w, rel_w = lay_squares(summed, cols)
    small = jnp.sum(summed[:, cols : cols + 3].astype(F32), axis=0)
    piece = lambda row, i: small[row, cols * i : cols * (i + 1)]
    return (
        output,
        segment_grad,
        piece(0, 0),
        piece(0, 1),
        query_w,
        key_w,
        value_w,
        out_w,
        piece(0, 2),
        rel_w,
        piece(1, 2),
        piece(1, 3),
        piece(0, 3),
        piece(1, 0),
        up_w,
        small[2],
        down_w,
        piece(1, 1),
        new_compressed,
    )


def solution(mesh):
    dp = mesh.shape["dp"]
    cores = jax.sharding.Mesh(
        mesh.devices.reshape(dp // 2, 2, mesh.shape["seq"]), ("z", "core", "seq")
    )
    rows = P(("z", "core"), "seq", None)
    shard, matrix = P("seq"), P("seq", None)
    return jax.shard_map(
        body,
        mesh=cores,
        in_specs=(
            rows, rows, rows, P(("z", "core"), None), P(("z", "core")), shard, shard, matrix,
            matrix, matrix, matrix, shard, matrix, shard, shard, shard, shard, matrix, shard,
            matrix, shard, P(None, "seq", None), shard, rows,
        ),
        out_specs=(
            rows, rows, shard, shard, matrix, matrix, matrix, matrix, shard, matrix, shard,
            shard, shard, shard, matrix, shard, matrix, shard, rows,
        ),
        check_vma=False,
    )
```

```python
import functools
import math

import jax
import jax.numpy as jnp
from jax import lax
from jax.experimental import pallas as pl
from jax.experimental.pallas import tpu as pltpu
from jax.sharding import PartitionSpec as P

HEADS = 8
DH = 128
EPSILON = 1e-05
MASKED = -1e30
LANES = 128
BLOCK = 256
CHUNK = 16
VMEM_LIMIT = 60 * 2**20
SCALE = 1.0 / math.sqrt(DH)
LOG2E = 1.4426950408889634
BF16 = jnp.bfloat16
F32 = jnp.float32


def cost(microseconds):
    return pl.CostEstimate(flops=int(microseconds * 1.15e7), bytes_accessed=0, transcendentals=0)


def mm(left, right, dims):
    return lax.dot_general(left, right, (dims, ((), ())), preferred_element_type=F32)


NN = ((1,), (0,))
NT = ((1,), (1,))
TN = ((0,), (0,))


def lean_left(block, first_row, fill_columns):
    columns = block.shape[1] // LANES
    far = BLOCK - 1 - first_row
    whole, part = far // LANES, far % LANES
    turned = [
        pltpu.roll(
            block[:, LANES * t : LANES * (t + 1)], LANES - part, 1, stride=1, stride_axis=0
        )
        for t in range(columns)
    ]
    rows = lax.broadcasted_iota(jnp.int32, (block.shape[0], LANES), 0)
    lanes = lax.broadcasted_iota(jnp.int32, (block.shape[0], LANES), 1)
    near = lanes - rows < LANES - part
    out = []
    for t in range(fill_columns):
        a = turned[(t + whole) % columns]
        b = turned[(t + whole + 1) % columns]
        out.append(jnp.where(near, a, b))
    return jnp.concatenate(out, axis=1)


def lean_right(block, first_row):
    columns = block.shape[1] // LANES
    whole, part = first_row // LANES, first_row % LANES
    turned = [
        pltpu.roll(block[:, LANES * t : LANES * (t + 1)], part, 1, stride=1, stride_axis=0)
        for t in range(columns)
    ]
    rows = lax.broadcasted_iota(jnp.int32, (block.shape[0], LANES), 0)
    lanes = lax.broadcasted_iota(jnp.int32, (block.shape[0], LANES), 1)
    wrapped = lanes - rows < part
    out = []
    for t in range(columns):
        a = turned[(t - whole) % columns]
        b = turned[(t - whole - 1) % columns]
        out.append(jnp.where(wrapped, b, a))
    return jnp.concatenate(out, axis=1)


def flip_matrix(kind):
    rows = lax.broadcasted_iota(jnp.int32, (BLOCK, BLOCK), 0)
    lanes = lax.broadcasted_iota(jnp.int32, (BLOCK, BLOCK), 1)
    return (rows + lanes == BLOCK - 1).astype(F32).astype(kind)


def in_place_order(parts_ref, out_ref, cuts):
    parts = parts_ref.shape[0]
    low, base = 0, 0
    for size in cuts:
        for part in range(parts):
            out_ref[base + part * size : base + (part + 1) * size, :] = parts_ref[
                part, low : low + size, :
            ]
        low += size
        base += parts * size


def attend_kernel(
    cuts, q_ref, cb_ref, pb_ref, k_ref, v_ref, t_ref, info_ref,
    e_ref, inv_ref, o_ref, cq_ref, pq_ref,
    keys, values, raw, lean, mix, tops, sums,
):
    parts, seg, _ = q_ref.shape
    queries = parts * seg
    old = parts * (cuts[0] + cuts[1])
    in_place_order(k_ref, keys, cuts)
    in_place_order(v_ref, values, cuts)
    q = q_ref[...].reshape(queries, DH)
    content_q = (q + cb_ref[...]).astype(BF16)
    position_q = (q + pb_ref[...]).astype(BF16)
    cq_ref[...] = content_q.reshape(parts, seg, DH)
    pq_ref[...] = position_q.reshape(parts, seg, DH)
    for block in range(queries // BLOCK):
        row0 = block * BLOCK
        width = old + row0 + BLOCK
        skip = queries - BLOCK - row0
        raw[:, :width] = mm(content_q[row0 : row0 + BLOCK], keys[:width, :], NT)
        lean[:, :width] = mm(position_q[row0 : row0 + BLOCK], t_ref[skip : skip + width, :], NT)
        for chunk in range(BLOCK // CHUNK):
            r0 = chunk * CHUNK
            rows = slice(r0, r0 + CHUNK)
            turned = lean_left(lean[rows, :width], r0, width // LANES)
            score = raw[rows, :width] + turned
            start = info_ref[row0 + r0 : row0 + r0 + CHUNK, 0:1].astype(jnp.int32)
            shade = info_ref[row0 + r0 : row0 + r0 + CHUNK, 1:2]
            past = score[:, :old] + shade
            place = lax.broadcasted_iota(jnp.int32, (CHUNK, row0 + BLOCK), 1)
            own = lax.broadcasted_iota(jnp.int32, (CHUNK, row0 + BLOCK), 0) + (row0 + r0)
            now = jnp.where((place <= own) & (place >= start), score[:, old:], MASKED)
            raw[rows, :old] = past
            raw[rows, old:width] = now
            top = past[:, :LANES]
            for low in range(LANES, old, LANES):
                top = jnp.maximum(top, past[:, low : low + LANES])
            for low in range(0, row0 + BLOCK, LANES):
                top = jnp.maximum(top, now[:, low : low + LANES])
            tops[rows, :] = top
        top = jnp.max(tops[...], axis=1, keepdims=True)
        tops[...] = jnp.broadcast_to(top, (BLOCK, LANES))
        for chunk in range(BLOCK // CHUNK):
            r0 = chunk * CHUNK
            rows = slice(r0, r0 + CHUNK)
            top = tops[rows, :]
            total = jnp.zeros((CHUNK, LANES), F32)
            for low in range(0, width, LANES):
                weight = jnp.exp2((raw[rows, low : low + LANES] - top) * (SCALE * LOG2E))
                total = total + weight
                e_ref[row0 + r0 : row0 + r0 + CHUNK, low : low + LANES] = weight.astype(BF16)
            sums[rows, :] = total
        total = jnp.sum(sums[...], axis=1, keepdims=True)
        inv_ref[row0 : row0 + BLOCK, :] = jnp.broadcast_to(1.0 / total, (BLOCK, DH))
        mix[row0 : row0 + BLOCK, :] = mm(
            e_ref[row0 : row0 + BLOCK, :width], values[:width, :], NN
        )
    o_ref[...] = (mix[...] * inv_ref[...]).astype(BF16).reshape(parts, seg, DH)


def attend(query, content_shift, position_shift, keys, values, table_rev, info, cuts):
    parts, group, seg, cols = query.shape
    rows = keys.shape[2]
    queries, key_count, heads = parts * seg, parts * rows, cols // DH
    by_head = lambda size: pl.BlockSpec((parts, None, size, DH), lambda s, h: (0, s, 0, h))
    grid_spec = pl.GridSpec(
        grid=(group, heads),
        in_specs=[
            by_head(seg),
            pl.BlockSpec((1, DH), lambda s, h: (0, h)),
            pl.BlockSpec((1, DH), lambda s, h: (0, h)),
            by_head(rows),
            by_head(rows),
            pl.BlockSpec((key_count, DH), lambda s, h: (0, h)),
            pl.BlockSpec((None, queries, LANES), lambda s, h: (s, 0, 0)),
        ],
        out_specs=[
            pl.BlockSpec((None, None, queries, key_count), lambda s, h: (s, h, 0, 0)),
            pl.BlockSpec((None, None, queries, DH), lambda s, h: (s, h, 0, 0)),
            by_head(seg),
            by_head(seg),
            by_head(seg),
        ],
        scratch_shapes=[
            pltpu.VMEM((key_count, DH), BF16),
            pltpu.VMEM((key_count, DH), BF16),
            pltpu.VMEM((BLOCK, key_count), F32),
            pltpu.VMEM((BLOCK, key_count), F32),
            pltpu.VMEM((queries, DH), F32),
            pltpu.VMEM((BLOCK, LANES), F32),
            pltpu.VMEM((BLOCK, LANES), F32),
        ],
    )
    small = jax.ShapeDtypeStruct((parts, group, seg, cols), BF16)
    return pl.pallas_call(
        functools.partial(attend_kernel, cuts),
        grid_spec=grid_spec,
        out_shape=[
            jax.ShapeDtypeStruct((group, heads, queries, key_count), BF16),
            jax.ShapeDtypeStruct((group, heads, queries, DH), F32),
            small,
            small,
            small,
        ],
        compiler_params=pltpu.CompilerParams(
            dimension_semantics=("arbitrary", "arbitrary"), vmem_limit_bytes=VMEM_LIMIT
        ),
        cost_estimate=cost(40),
        name="attend",
    )(query, content_shift, position_shift, keys, values, table_rev, info)


def pull_kernel(
    cuts, e_ref, inv_ref, o_ref, g_ref, cq_ref, pq_ref, k_ref, v_ref, t_ref,
    dq_ref, dk_ref, dv_ref, ks_ref, vs_ref, dt_ref, sums_ref,
    keys, values, grad, prob, part, score, lean, key_sum, value_sum,
):
    stream = pl.program_id(1)
    parts, seg, _ = g_ref.shape
    queries = parts * seg
    old = parts * (cuts[0] + cuts[1])
    in_place_order(k_ref, keys, cuts)
    in_place_order(v_ref, values, cuts)
    grad[...] = (g_ref[...].reshape(queries, DH).astype(F32) * inv_ref[...]).astype(BF16)
    attended = o_ref[...].reshape(queries, DH)
    content_q = cq_ref[...].reshape(queries, DH)
    position_q = pq_ref[...].reshape(queries, DH)

    @pl.when(stream == 0)
    def _():
        dt_ref[...] = jnp.zeros_like(dt_ref)
        sums_ref[...] = jnp.zeros_like(sums_ref)

    key_sum[...] = jnp.zeros_like(key_sum)
    value_sum[...] = jnp.zeros_like(value_sum)
    content_total = jnp.zeros((1, DH), F32)
    position_total = jnp.zeros((1, DH), F32)
    query_total = jnp.zeros((1, DH), F32)
    flip = flip_matrix(BF16)
    turn = lambda rows: mm(flip, rows, NN).astype(BF16)
    for block in range(queries // BLOCK):
        row0 = block * BLOCK
        width = old + row0 + BLOCK
        skip = queries - BLOCK - row0
        rows = slice(row0, row0 + BLOCK)
        grad_back = turn(grad[rows, :])
        dots_back = jnp.sum(
            grad_back.astype(F32) * turn(attended[rows]).astype(F32), axis=1, keepdims=True
        )
        content_back = turn(content_q[rows])
        position_back = turn(position_q[rows])
        prob[:, :width] = mm(grad_back, values[:width, :], NT)
        both = mm(jnp.concatenate([flip, grad[rows, :].T], axis=0), e_ref[rows, :width], NN)
        part[:, :width] = both[:BLOCK]
        value_sum[:, :width] += both[BLOCK:]
        for chunk in range(BLOCK // CHUNK):
            r0 = chunk * CHUNK
            mean = dots_back[r0 : r0 + CHUNK, 0:1]
            change = part[r0 : r0 + CHUNK, :width] * (prob[r0 : r0 + CHUNK, :width] - mean)
            score[r0 : r0 + CHUNK, :width] = change.astype(BF16)
            lean[r0 : r0 + CHUNK, :width] = lean_right(change, r0).astype(BF16)
        content_grad = (mm(score[:, :width], keys[:width, :], NN) * SCALE).astype(BF16).astype(F32)
        position_grad = (
            (mm(lean[:, :width], t_ref[skip : skip + width, :], NN) * SCALE)
            .astype(BF16)
            .astype(F32)
        )
        query_grad = turn((content_grad + position_grad).astype(BF16))
        content_total += jnp.sum(content_grad, axis=0, keepdims=True)
        position_total += jnp.sum(position_grad, axis=0, keepdims=True)
        query_total += jnp.sum(query_grad.astype(F32), axis=0, keepdims=True)
        dq_ref[rows, :] = query_grad
        key_sum[:, :width] += mm(content_back, score[:, :width], TN)
        dt_ref[:, skip : skip + width] += mm(position_back, lean[:, :width], TN) * SCALE
    key_cols = (key_sum[...] * SCALE).astype(BF16)
    value_cols = value_sum[...].astype(BF16)
    dk_ref[...] = key_cols
    dv_ref[...] = value_cols
    ks_ref[...] = (key_sum[:, old:] * SCALE).T.astype(BF16)
    vs_ref[...] = value_sum[:, old:].T.astype(BF16)
    ones = jnp.ones((8, key_cols.shape[1]), BF16)
    key_total = mm(ones, key_cols, NT)[0:1]
    value_total = mm(ones, value_cols, NT)[0:1]
    sums_ref[...] += jnp.concatenate(
        [
            content_total,
            position_total,
            query_total,
            key_total,
            value_total,
            jnp.zeros((3, DH), F32),
        ],
        axis=0,
    )


def pull(head, weights, inverse, attended, out_grad, content_q, position_q, keys, values, table_rev, cuts):
    parts, group, seg, cols = out_grad.shape
    rows = keys.shape[2]
    queries, key_count = parts * seg, parts * rows
    by_head = lambda size: pl.BlockSpec((parts, None, size, DH), lambda h, s: (0, s, 0, head))
    by_row = lambda: pl.BlockSpec((None, queries, DH), lambda h, s: (s, 0, h))
    by_place = lambda: pl.BlockSpec((None, DH, key_count), lambda h, s: (s, h, 0))
    grid_spec = pl.GridSpec(
        grid=(1, group),
        in_specs=[
            pl.BlockSpec((None, None, queries, key_count), lambda h, s: (s, head, 0, 0)),
            pl.BlockSpec((None, None, queries, DH), lambda h, s: (s, head, 0, 0)),
            by_head(seg),
            by_head(seg),
            by_head(seg),
            by_head(seg),
            by_head(rows),
            by_head(rows),
            pl.BlockSpec((key_count, DH), lambda h, s: (0, head)),
        ],
        out_specs=[
            by_row(),
            by_place(),
            by_place(),
            by_row(),
            by_row(),
            pl.BlockSpec((None, DH, key_count), lambda h, s: (h, 0, 0)),
            pl.BlockSpec((None, 8, DH), lambda h, s: (h, 0, 0)),
        ],
        scratch_shapes=[
            pltpu.VMEM((key_count, DH), BF16),
            pltpu.VMEM((key_count, DH), BF16),
            pltpu.VMEM((queries, DH), BF16),
            pltpu.VMEM((BLOCK, key_count), F32),
            pltpu.VMEM((BLOCK, key_count), F32),
            pltpu.VMEM((BLOCK, key_count), BF16),
            pltpu.VMEM((BLOCK, key_count), BF16),
            pltpu.VMEM((DH, key_count), F32),
            pltpu.VMEM((DH, key_count), F32),
        ],
    )
    return pl.pallas_call(
        functools.partial(pull_kernel, cuts),
        grid_spec=grid_spec,
        out_shape=[
            jax.ShapeDtypeStruct((group, queries, DH), BF16),
            jax.ShapeDtypeStruct((group, DH, key_count), BF16),
            jax.ShapeDtypeStruct((group, DH, key_count), BF16),
            jax.ShapeDtypeStruct((group, queries, DH), BF16),
            jax.ShapeDtypeStruct((group, queries, DH), BF16),
            jax.ShapeDtypeStruct((1, DH, key_count), F32),
            jax.ShapeDtypeStruct((1, 8, DH), F32),
        ],
        compiler_params=pltpu.CompilerParams(
            dimension_semantics=("arbitrary", "arbitrary"), vmem_limit_bytes=VMEM_LIMIT
        ),
        cost_estimate=cost(39),
        name="pull",
    )(weights, inverse, attended, out_grad, content_q, position_q, keys, values, table_rev)


def project_kernel(
    cuts, rows_ref, gain_ref, shift_ref, w_ref, old_ref, mem_ref, seg_ref, q_ref, k_ref, v_ref, normed
):
    rows, width = rows_ref.shape
    cols = k_ref.shape[1]
    step = 32
    for low in range(0, rows, step):
        wide = rows_ref[low : low + step, :].astype(F32)
        centred = wide - jnp.mean(wide, axis=1, keepdims=True)
        rate = lax.rsqrt(jnp.mean(centred * centred, axis=1, keepdims=True) + EPSILON)
        normed[low : low + step, :] = (centred * rate * gain_ref[...] + shift_ref[...]).astype(BF16)
    cut = cuts[0] + cuts[1]
    old_ref[...] = normed[: cuts[0], :]
    mem_ref[...] = normed[cuts[0] : cut, :]
    seg_ref[...] = normed[cut:, :]
    q_ref[...] = mm(normed[cut:, :], w_ref[:, :cols], NN)
    k_ref[...] = mm(normed[...], w_ref[:, cols : 2 * cols], NN).astype(BF16)
    v_ref[...] = mm(normed[...], w_ref[:, 2 * cols : 3 * cols], NN).astype(BF16)


def project(rows_all, gain, shift, columns, cuts):
    parts, group, each, width = rows_all.shape
    cols = columns.shape[1] // 4
    block = lambda size, wide: pl.BlockSpec((None, None, size, wide), lambda p, s: (p, s, 0, 0))
    placed = lambda size: pl.BlockSpec((None, size, width), lambda p, s: (s, p, 0))
    whole = lambda *shape: pl.BlockSpec(shape, lambda p, s: (0,) * len(shape))
    shape = lambda size, kind: jax.ShapeDtypeStruct((parts, group, size, cols), kind)
    return pl.pallas_call(
        functools.partial(project_kernel, cuts),
        grid_spec=pl.GridSpec(
            grid=(parts, group),
            in_specs=[
                block(each, width),
                whole(1, width),
                whole(1, width),
                whole(width, 4 * cols),
            ],
            out_specs=[placed(size) for size in cuts]
            + [block(cuts[2], cols), block(each, cols), block(each, cols)],
            scratch_shapes=[pltpu.VMEM((each, width), BF16)],
        ),
        out_shape=[jax.ShapeDtypeStruct((group, parts * size, width), BF16) for size in cuts]
        + [shape(cuts[2], F32), shape(each, BF16), shape(each, BF16)],
        compiler_params=pltpu.CompilerParams(
            dimension_semantics=("arbitrary", "arbitrary"), vmem_limit_bytes=VMEM_LIMIT
        ),
        cost_estimate=cost(17),
        name="project",
    )(rows_all, gain, shift, columns)


def gelu_both(x):
    near = jnp.abs(x)
    t = 1.0 / (1.0 + (0.3275911 * math.sqrt(0.5)) * near)
    bell = jnp.exp2((x * x) * (-0.5 * LOG2E))
    tail = 0.5 * 1.061405429
    for factor in (-1.453152027, 1.421413741, -0.284496736, 0.254829592):
        tail = tail * t + 0.5 * factor
    tail = tail * t * bell
    below = jnp.where(x < 0.0, tail, 1.0 - tail)
    return x * below, below + x * bell * (1.0 / math.sqrt(2.0 * math.pi))


def forward_back_kernel(
    last, parts, pair, n_ref, c_ref, *rest,
):
    up_refs, down_refs, shift_ref = rest[:parts], rest[parts : parts + pair], rest[parts + pair]
    rest = rest[parts + pair + 1 :]
    if last:
        part_in, grad_in, part_out, part_far, grad_out, grad_far, late_ref, sums_ref = rest[:8]
        pre, slope, hidden, act, up_out, down_out, sems, part_ref, grad_ref = rest[8:]
    else:
        part_ref, grad_ref, late_ref, sums_ref = rest[:4]
        pre, slope, hidden, act, up_out, down_out, sems = rest[4:]
    tile = pl.program_id(0)
    tiles = pl.num_programs(0)
    cols, units = up_refs[0].shape
    unit_cols, width = down_refs[0].shape
    rows = n_ref.shape[0]
    slot = lax.rem(tile, 2)
    up_weight = jnp.concatenate([ref[...] for ref in up_refs], axis=0)
    down_weight = jnp.concatenate([ref[...] for ref in down_refs], axis=0)

    def copies(at, index):
        return (
            pltpu.make_async_copy(
                up_out.at[at],
                late_ref.at[:, pl.ds(0, cols), pl.ds(pl.multiple_of(index * units, units), units)],
                sems.at[at, 0],
            ),
            pltpu.make_async_copy(
                down_out.at[at],
                late_ref.at[pl.ds(index * pair, pair), pl.ds(cols, unit_cols), :],
                sems.at[at, 1],
            ),
        )

    @pl.when(tile == 0)
    def _():
        if last:
            part_ref[...] = part_in[...]
            grad_ref[...] = grad_in[...]
        else:
            part_ref[...] = jnp.zeros_like(part_ref)
            grad_ref[...] = jnp.zeros_like(grad_ref)

    pre[...] = mm(n_ref[...], up_weight, NN)
    slope[...] = mm(c_ref[...], down_weight, NT)
    for low in range(0, rows, 16):
        some = slice(low, low + 16)
        value, change = gelu_both(pre[some, :] + shift_ref[...])
        hidden[some, :] = value.astype(BF16)
        act[some, :] = (change * slope[some, :]).astype(BF16)
    part_ref[...] += mm(hidden[...], down_weight, NN)
    grad_ref[...] += mm(act[...], up_weight, NT)
    sums_ref[...] = jnp.sum(act[...].astype(F32), axis=0, keepdims=True)

    @pl.when(tile >= 2)
    def _():
        for copy in copies(slot, tile - 2):
            copy.wait()

    up_out[slot] = mm(n_ref[...], act[...], TN).astype(BF16).reshape(parts, cols, units)
    down_out[slot] = mm(hidden[...], c_ref[...], TN).astype(BF16).reshape(pair, unit_cols, width)
    for copy in copies(slot, tile):
        copy.start()

    @pl.when(tile == tiles - 1)
    def _():
        if last:
            part_out[...] = part_ref[: rows // 2, :]
            part_far[...] = part_ref[rows // 2 :, :].astype(BF16)
            grad_out[...] = grad_ref[: rows // 2, :]
            grad_far[...] = grad_ref[rows // 2 :, :].astype(BF16)
        for copy in (copies(1 - slot, tile - 1) if parts > pair else ()) + copies(slot, tile):
            copy.wait()


def forward_back(normed, cot, gathered, shift, carry):
    parts, _, width = gathered.shape
    rows = normed.shape[0]
    cols = width // parts
    unit_cols = shift.shape[1] // parts
    pair = 2
    units = pair * unit_cols
    last = len(carry) > 0
    one = pl.Buffered(1)
    whole = lambda *shape: pl.BlockSpec(shape, lambda t: (0,) * len(shape), pipeline_mode=one)
    up = lambda p: pl.BlockSpec((None, cols, units), lambda t: (p, 0, t))
    down = lambda i: pl.BlockSpec(
        (None, unit_cols, width), lambda t: (t * pair + i, cols // unit_cols, 0)
    )
    if last:
        sums = [((rows // 2, width), F32), ((rows // 2, width), BF16)] * 2
    else:
        sums = [((rows, width), F32)] * 2
    return pl.pallas_call(
        functools.partial(forward_back_kernel, last, parts, pair),
        grid_spec=pl.GridSpec(
            grid=(parts // pair,),
            in_specs=[
                whole(rows, width),
                whole(rows, width),
            ]
            + [up(p) for p in range(parts)]
            + [down(i) for i in range(pair)]
            + [pl.BlockSpec((1, units), lambda t: (0, t))]
            + [whole(rows, width) for _ in carry],
            out_specs=[whole(*shape) for shape, _ in sums]
            + [
                pl.BlockSpec(memory_space=pl.ANY),
                pl.BlockSpec((1, units), lambda t: (0, t)),
            ],
            scratch_shapes=[
                pltpu.VMEM((rows, units), F32),
                pltpu.VMEM((rows, units), F32),
                pltpu.VMEM((rows, units), BF16),
                pltpu.VMEM((rows, units), BF16),
                pltpu.VMEM((2, parts, cols, units), BF16),
                pltpu.VMEM((2, pair, unit_cols, width), BF16),
                pltpu.SemaphoreType.DMA((2, 2)),
            ]
            + [pltpu.VMEM((rows, width), F32) for _ in carry],
        ),
        out_shape=[jax.ShapeDtypeStruct(shape, kind) for shape, kind in sums]
        + [
            jax.ShapeDtypeStruct((parts, cols + unit_cols, width), BF16),
            jax.ShapeDtypeStruct((1, parts * unit_cols), F32),
        ],
        compiler_params=pltpu.CompilerParams(
            dimension_semantics=("arbitrary",), vmem_limit_bytes=VMEM_LIMIT
        ),
        cost_estimate=cost(29),
        name="forward_back",
    )(normed, cot, *[gathered] * (parts + pair), shift, *carry)


def leave_kernel(a_ref, s_ref, w_ref, shift_ref, gain_ref, bias_ref, flat_ref, m_ref, n_ref):
    parts = a_ref.shape[0]
    flat_ref[...] = jnp.concatenate([a_ref[part] for part in range(parts)], axis=1)
    m_ref[...] = s_ref[...].astype(F32) + (mm(flat_ref[...], w_ref[...], NN) + shift_ref[...])
    step = 16
    for low in range(0, m_ref.shape[0], step):
        unit, _ = standardise(m_ref[low : low + step, :])
        n_ref[low : low + step, :] = (unit * gain_ref[...] + bias_ref[...]).astype(BF16)


def leave(mixed_heads, segment, base, weight, shift, gain, bias):
    parts, group, seg, cols = mixed_heads.shape
    width = parts * cols
    rows = lambda: pl.BlockSpec((None, seg, width), lambda s: (s, 0, 0))
    vector = lambda: pl.BlockSpec((1, width), lambda s: (0, 0))
    shape = lambda kind: jax.ShapeDtypeStruct((group, seg, width), kind)
    return pl.pallas_call(
        leave_kernel,
        grid_spec=pl.GridSpec(
            grid=(group,),
            in_specs=[
                pl.BlockSpec((parts, None, seg, cols), lambda s: (0, s, 0, 0)),
                pl.BlockSpec((None, seg, width), lambda s: (s + base, 0, 0)),
                pl.BlockSpec((width, width), lambda s: (0, 0)),
                vector(),
                vector(),
                vector(),
            ],
            out_specs=[rows(), rows(), rows()],
        ),
        out_shape=[shape(BF16), shape(F32), shape(BF16)],
        compiler_params=pltpu.CompilerParams(vmem_limit_bytes=VMEM_LIMIT),
        cost_estimate=cost(6),
        name="leave",
    )(mixed_heads, segment, weight, shift, gain, bias)


def enter_kernel(
    m_ref, g_ref, far_ref, c_ref, w_ref, gain_ref, mg_ref, b_ref, a_ref, sums_ref
):
    @pl.when(pl.program_id(0) == 0)
    def _():
        sums_ref[...] = jnp.zeros_like(sums_ref)

    parts = a_ref.shape[0]
    rows, width = m_ref.shape
    step = 32
    total = [jnp.zeros((1, width), F32) for _ in range(4)]
    for low in range(0, rows, step):
        at = slice(low, low + step)
        unit, rate = standardise(m_ref[at, :])
        grad = g_ref[at, :] + far_ref[at, :].astype(F32)
        cot = c_ref[at, :].astype(F32)
        middle_grad = cot + standardise_back(unit, rate, grad, gain_ref[...])
        branch = middle_grad.astype(BF16)
        mg_ref[at, :] = middle_grad
        b_ref[at, :] = branch
        for i, value in enumerate((branch.astype(F32), grad * unit, grad, cot)):
            total[i] = total[i] + jnp.sum(value, axis=0, keepdims=True)
    sums_ref[...] += jnp.concatenate(total + [jnp.zeros((4, width), F32)], axis=0)
    for part in range(parts):
        low = part * a_ref.shape[2]
        weight = w_ref[low : low + a_ref.shape[2], :]
        a_ref[part] = mm(b_ref[...], weight, NT).astype(BF16)


def enter(middle, grad, far, cot, base, weight, gain, parts):
    group, seg, width = middle.shape
    cols = width // parts
    rows = lambda: pl.BlockSpec((None, seg, width), lambda s: (s, 0, 0))
    later = lambda: pl.BlockSpec((None, seg, width), lambda s: (s + base, 0, 0))
    shape = lambda kind: jax.ShapeDtypeStruct((group, seg, width), kind)
    return pl.pallas_call(
        enter_kernel,
        grid_spec=pl.GridSpec(
            grid=(group,),
            in_specs=[
                rows(),
                later(),
                later(),
                later(),
                pl.BlockSpec((width, width), lambda s: (0, 0)),
                pl.BlockSpec((1, width), lambda s: (0, 0)),
            ],
            out_specs=[
                rows(),
                rows(),
                pl.BlockSpec((parts, None, seg, cols), lambda s: (0, s, 0, 0)),
                pl.BlockSpec((8, width), lambda s: (0, 0)),
            ],
        ),
        out_shape=[
            shape(F32),
            shape(BF16),
            jax.ShapeDtypeStruct((parts, group, seg, cols), BF16),
            jax.ShapeDtypeStruct((8, width), F32),
        ],
        compiler_params=pltpu.CompilerParams(
            dimension_semantics=("arbitrary",), vmem_limit_bytes=VMEM_LIMIT
        ),
        cost_estimate=cost(7),
        name="enter",
    )(middle, grad, far, cot, weight, gain)


def compress_kernel(low, rows_ref, w_ref, shift_ref, out_ref, wide):
    count = out_ref.shape[0]
    cols = out_ref.shape[1]
    blocks = wide.shape[0]
    for at in range(blocks):
        wide[at] = rows_ref[low : low + 3 * count, at * LANES : (at + 1) * LANES].astype(F32)
    total = jnp.broadcast_to(shift_ref[...], (count, cols))
    for k in range(3):
        every = jnp.concatenate(
            [wide[at, pl.ds(k, count, stride=3), :] for at in range(blocks)], axis=1
        ).astype(BF16)
        total = total + mm(every, w_ref[:, k * cols : (k + 1) * cols], NN)
    out_ref[...] = total.astype(BF16)


def compress(rows_all, columns, shift, low, count):
    parts, group, each, width = rows_all.shape
    cols = columns.shape[1] // 3
    return pl.pallas_call(
        functools.partial(compress_kernel, low),
        grid_spec=pl.GridSpec(
            grid=(parts, group),
            in_specs=[
                pl.BlockSpec((None, None, each, width), lambda p, s: (p, s, 0, 0)),
                pl.BlockSpec((width, 3 * cols), lambda p, s: (0, 0)),
                pl.BlockSpec((1, cols), lambda p, s: (0, 0)),
            ],
            out_specs=pl.BlockSpec((None, None, count, cols), lambda p, s: (p, s, 0, 0)),
            scratch_shapes=[pltpu.VMEM((width // LANES, 3 * count, LANES), F32)],
        ),
        out_shape=jax.ShapeDtypeStruct((parts, group, count, cols), BF16),
        compiler_params=pltpu.CompilerParams(
            dimension_semantics=("arbitrary", "arbitrary"), vmem_limit_bytes=VMEM_LIMIT
        ),
        cost_estimate=cost(6.5),
        name="compress",
    )(rows_all, columns, shift)


def lay_out_kernel(
    parts, unit_cols, core_ref, a_ref, b_ref, c_ref, d_ref, up_ref, down_ref
):
    flipped = core_ref[0] == 1
    for half, (mine_ref, far_ref) in enumerate(((a_ref, c_ref), (b_ref, d_ref))):
        mine, far = mine_ref[...].astype(F32), far_ref[...].astype(F32)
        for core, value in enumerate(
            (jnp.where(flipped, far, mine), jnp.where(flipped, mine, far))
        ):
            for part in range(parts):
                at = ((part * 2 + core) * 2 + half) * unit_cols
                up_ref[:, at : at + unit_cols] = value[
                    0, :, part * unit_cols : (part + 1) * unit_cols
                ]
            down_ref[2 * core + half] = value[1]


def lay_out(core, mine, far, parts):
    _, rows, width = mine[0].shape
    step = rows // 4 if rows % 64 == 0 else rows
    half = lambda: pl.BlockSpec((2, step, width), lambda r, *_: (0, r, 0))
    return pl.pallas_call(
        functools.partial(lay_out_kernel, parts, rows),
        grid_spec=pltpu.PrefetchScalarGridSpec(
            num_scalar_prefetch=1,
            grid=(rows // step,),
            in_specs=[half(), half(), half(), half()],
            out_specs=[
                pl.BlockSpec((step, 4 * width), lambda r, *_: (r, 0)),
                pl.BlockSpec((4, step, width), lambda r, *_: (0, r, 0)),
            ],
        ),
        out_shape=[
            jax.ShapeDtypeStruct((rows, 4 * width), F32),
            jax.ShapeDtypeStruct((4, rows, width), F32),
        ],
        compiler_params=pltpu.CompilerParams(vmem_limit_bytes=VMEM_LIMIT),
        cost_estimate=cost(4),
        name="lay_out",
    )(core.reshape(1), *mine, *far)


def lay_squares_kernel(in_ref, *out_refs):
    parts = in_ref.shape[0]
    cols = in_ref.shape[2] // len(out_refs)
    for at, out_ref in enumerate(out_refs):
        for part in range(parts):
            out_ref[:, part * cols : (part + 1) * cols] = in_ref[
                part, :, at * cols : (at + 1) * cols
            ].astype(F32)


def lay_squares(summed, rows):
    parts, _, wide = summed.shape
    width = parts * wide // 4
    step = rows // 2
    return pl.pallas_call(
        lay_squares_kernel,
        grid_spec=pl.GridSpec(
            grid=(2,),
            in_specs=[pl.BlockSpec((parts, step, wide), lambda i: (0, i, 0))],
            out_specs=[pl.BlockSpec((step, width), lambda i: (i, 0)) for _ in range(4)],
        ),
        out_shape=[jax.ShapeDtypeStruct((rows, width), F32) for _ in range(4)],
        compiler_params=pltpu.CompilerParams(vmem_limit_bytes=VMEM_LIMIT),
        cost_estimate=cost(2.5),
        name="lay_squares",
    )(summed)


def settle_kernel(heads, me_ref, old_ref, mem_ref, seg_ref, *rest):
    q_refs, k_refs, v_refs, ks_refs, vs_refs, dt_refs, sums_refs = (
        rest[i * heads : (i + 1) * heads] for i in range(7)
    )
    w_ref, table_ref, gain_ref, shift_ref, small_ref, part_ref, out_ref, total = rest[7 * heads :]
    stream = pl.program_id(0)
    parts, rows, wide = out_ref.shape
    cols = wide // 4
    width = parts * cols

    @pl.when(stream == 0)
    def _():
        total[...] = jnp.zeros_like(total)

    low = old_ref.shape[0]
    high = low + mem_ref.shape[0]
    pair = lambda first, last: [ref[:, first:last] for ref in (*k_refs, *v_refs)]
    total[...] += mm(
        jnp.concatenate([ref[...].T for ref in q_refs] + pair(high, high + seg_ref.shape[0]), axis=0),
        seg_ref[...],
        NN,
    )
    total[cols:, :] += mm(jnp.concatenate(pair(low, high), axis=0), mem_ref[...], NN)
    total[cols:, :] += mm(jnp.concatenate(pair(0, low), axis=0), old_ref[...], NN)
    three = jnp.concatenate([ref[...] for ref in (*q_refs, *ks_refs, *vs_refs)], axis=1)
    part = mm(three, w_ref[:, : 3 * cols], NT).astype(BF16)
    part_ref[...] = part.reshape(part_ref.shape)

    @pl.when(stream == pl.num_programs(0) - 1)
    def _():
        places = jnp.concatenate([ref[0].astype(BF16) for ref in dt_refs], axis=0)
        rel = mm(places, table_ref[...], NN)
        line = lambda row: jnp.concatenate(
            [ref[0, row : row + 1, :] for ref in sums_refs], axis=1
        )
        row_sums = jnp.concatenate([line(2), line(3), line(4)], axis=1)
        pieces, rest = [], row_sums
        for _ in range(3):
            pieces.append(rest.astype(BF16))
            rest = rest - pieces[-1].astype(F32)
        pieces = jnp.concatenate(pieces + [jnp.zeros((13, 3 * cols), BF16)], axis=0)
        shift_grad = jnp.sum(mm(pieces, w_ref[:, : 3 * cols], NT), axis=0, keepdims=True)
        weight = w_ref[:, : 3 * cols].astype(F32)
        along = jnp.sum(weight.T * total[...], axis=0, keepdims=True)
        gain_grad = (along - shift_ref[...] * shift_grad) / gain_ref[...]
        for at in range(parts):
            low, high = at * cols, (at + 1) * cols
            out_ref[at, :cols, : 3 * cols] = total[:, low:high].T.astype(BF16)
            out_ref[at, :cols, 3 * cols :] = rel[:, low:high].T.astype(BF16)
            mine = (me_ref[0] == at).astype(F32)
            none = jnp.zeros((1, 2 * cols), F32)
            first = jnp.concatenate([gain_grad[:, low:high], shift_grad[:, low:high], none], axis=1)
            second = jnp.concatenate([none, mine * line(0), mine * line(1)], axis=1)
            added = jnp.concatenate([first, second, jnp.zeros((14, wide), F32)], axis=0)
            out_ref[at, cols:, :] = (small_ref[at] + added).astype(BF16)


def settle(me, normed, grads, columns, table, gain, shift, small, parts):
    group, queries, width = normed[2].shape
    cols = width // parts
    wide = 4 * cols
    by_kind = list(zip(*grads))
    block = lambda array: pl.BlockSpec((None, *array.shape[1:]), lambda s, *_: (s, 0, 0))
    whole = lambda *shape: pl.BlockSpec(
        shape, lambda s, *_: (0,) * len(shape), pipeline_mode=pl.Buffered(1)
    )
    return pl.pallas_call(
        functools.partial(settle_kernel, len(grads)),
        grid_spec=pltpu.PrefetchScalarGridSpec(
            num_scalar_prefetch=1,
            grid=(group,),
            in_specs=[block(rows) for rows in normed]
            + [block(each) for kind in by_kind[:5] for each in kind]
            + [whole(*each.shape) for kind in by_kind[5:] for each in kind]
            + [
                whole(*columns.shape),
                whole(*table.shape),
                whole(1, width),
                whole(1, width),
                whole(*small.shape),
            ],
            out_specs=[
                pl.BlockSpec((parts, None, queries // parts, width), lambda s, *_: (0, s, 0, 0)),
                whole(parts, cols + 16, wide),
            ],
            scratch_shapes=[pltpu.VMEM((3 * cols, width), F32)],
        ),
        out_shape=[
            jax.ShapeDtypeStruct((parts, group, queries // parts, width), BF16),
            jax.ShapeDtypeStruct((parts, cols + 16, wide), BF16),
        ],
        compiler_params=pltpu.CompilerParams(
            dimension_semantics=("arbitrary",), vmem_limit_bytes=VMEM_LIMIT
        ),
        cost_estimate=cost(14),
        name="settle",
    )(
        me.reshape(1), *normed, *[each for kind in by_kind for each in kind], columns, table, gain, shift,
        small,
    )


def standardise(rows):
    mean = jnp.mean(rows, axis=-1, keepdims=True)
    centred = rows - mean
    rate = lax.rsqrt(jnp.mean(centred * centred, axis=-1, keepdims=True) + EPSILON)
    return centred * rate, rate


def standardise_back(unit, rate, grad, gain):
    scaled = grad * gain
    mean = jnp.mean(scaled, axis=-1, keepdims=True)
    along = jnp.mean(scaled * unit, axis=-1, keepdims=True)
    return rate * (scaled - mean - unit * along)


def sinusoid_reversed(rows, width):
    positions = (rows - 1 - jnp.arange(rows, dtype=jnp.int32)).astype(F32)[:, None]
    frequency = jnp.exp(
        jnp.arange(width // 2, dtype=F32) * (-2.0 * math.log(10000.0) / width)
    )
    angles = positions * frequency[None, :]
    return jnp.concatenate([jnp.sin(angles), jnp.cos(angles)], axis=1).astype(BF16)


def dot(left, right):
    return mm(left, right, NN)


def swap(value):
    return lax.ppermute(value, "core", [(0, 1), (1, 0)])


def exchange(blocks, name, axis=0):
    count = lax.axis_size(name)
    me = lax.axis_index(name)
    block = lambda at: lax.dynamic_index_in_dim(blocks, at, axis, keepdims=False)
    return [block(me)] + [
        lax.ppermute(block(me ^ apart), name, [(i, i ^ apart) for i in range(count)])
        for apart in range(1, count)
    ]


def spread(block, name):
    count = lax.axis_size(name)
    return [block] + [
        lax.ppermute(block, name, [(i, i ^ apart) for i in range(count)])
        for apart in range(1, count)
    ]


def in_order(pieces, name):
    me = lax.axis_index(name)
    found = jnp.stack(pieces)
    return jnp.stack(
        [lax.dynamic_index_in_dim(found, me ^ i, 0, keepdims=False) for i in range(len(pieces))]
    )


def add_up(arrays, kind=BF16):
    total = arrays[0].astype(F32)
    for array in arrays[1:]:
        total = total + array.astype(F32)
    return total.astype(kind)


def body(
    segment, memory, compressed, eob, reset, ln1_gain, ln1_bias, w_query, w_key, w_value,
    w_out, out_bias, w_rel, bias_content, bias_position, ln2_gain, ln2_bias, w_up, up_bias,
    w_down, down_bias, conv_weight, conv_bias, cotangent,
):
    parts = lax.axis_size("seq")
    layers = lax.axis_size("z")
    core = lax.axis_index("core")
    me = lax.axis_index("seq")
    group, seg, width = segment.shape
    mem, old = memory.shape[1], compressed.shape[1]
    cuts = (old, mem, seg)
    each = old + mem + seg
    keys_in_all = parts * each
    cols = width // parts
    wide = 4 * cols
    own = group * seg
    unit_cols = w_up.shape[1] // (4 * parts)
    barrier = lax.optimization_barrier

    def by_columns(matrices):
        count = matrices.shape[0]
        sent = matrices.reshape(count, cols, parts, cols).transpose(2, 1, 0, 3)
        return sent.reshape(parts, cols, count * cols)

    up_bias_own = lax.dynamic_slice_in_dim(up_bias, core * 2 * unit_cols, 2 * unit_cols, 0)
    vectors = jnp.concatenate(
        [ln1_gain, ln1_bias, out_bias, ln2_gain, ln2_bias, down_bias, up_bias_own]
    )
    vectors = jnp.pad(vectors.reshape(2, wide), ((0, 14), (0, 0)))
    half = cols // 2
    sent = by_columns(jnp.concatenate([jnp.stack([w_query, w_key, w_value, w_rel]), conv_weight]))
    sent = lax.dynamic_slice_in_dim(sent, core * half, half, 1)
    out_half = lax.dynamic_slice_in_dim(w_out, core * half, half, 0)
    sent = jnp.concatenate([sent, jnp.broadcast_to(out_half, (parts, half, width))], axis=2)
    vectors = jnp.pad(vectors, ((0, 0), (0, 3 * cols + width)))
    sent = jnp.concatenate([sent, jnp.broadcast_to(vectors, (parts, *vectors.shape))], axis=1)
    got = lax.all_to_all(sent, "seq", 0, 0, tiled=True)
    spans = [(0, group)]
    local = [
        jnp.concatenate([compressed[low:high], memory[low:high], segment[low:high]], axis=1)
        for low, high in spans
    ]
    rows_all = [lax.all_gather(local[0], "seq")]
    mine = got[:, :half]
    far = swap(mine)
    columns = jnp.stack(
        [jnp.where(core == 0, mine, far), jnp.where(core == 0, far, mine)], axis=1
    ).reshape(width, 7 * cols + width)
    columns, conv_columns, out_full = (
        columns[:, :wide],
        columns[:, wide : 7 * cols],
        columns[:, 7 * cols :],
    )
    vectors = got[:, half : half + 2, :wide].reshape(parts, 2 * wide).astype(F32)
    gain_one, shift_one, out_shift, gain_two, shift_two, down_shift = (
        vectors[:, cols * i : cols * (i + 1)].reshape(1, width) for i in range(6)
    )
    up_shift = vectors[:, 6 * cols :].reshape(parts, 2, unit_cols).transpose(1, 0, 2)
    up_shift = up_shift.reshape(2, 1, parts * unit_cols)
    up_quarters = lax.dynamic_slice_in_dim(
        w_up.reshape(cols, parts, 2, 2, unit_cols), core, 1, 2
    ).reshape(cols, parts, 2, unit_cols)
    up_quarters = [up_quarters[:, :, i].reshape(cols, width) for i in range(2)]
    down_half = lax.dynamic_slice_in_dim(w_down, core * 2 * unit_cols, 2 * unit_cols, 0)
    down_quarters = [down_half[unit_cols * i : unit_cols * (i + 1)] for i in range(2)]
    first = jnp.concatenate([up_quarters[0], down_quarters[0]], axis=0)
    second = jnp.concatenate([up_quarters[1], down_quarters[1]], axis=0)
    cot_own = cotangent.reshape(own, width)
    cot_both = jnp.concatenate([cot_own, swap(cot_own)], axis=0)

    table_rev = sinusoid_reversed(keys_in_all, width)
    proj_rev = dot(table_rev, columns[:, 3 * cols :]).astype(BF16)
    index = jnp.arange(eob.shape[1], dtype=jnp.int32)[None, :]
    opens = jnp.pad(eob, ((0, 0), (1, 0)))[:, :-1] == 1
    start = lax.cummax(jnp.where(opens, index, 0), axis=1)
    shade = jnp.where((start == 0) & (reset[:, None] == 0), 0.0, MASKED)
    info = jnp.stack([start.astype(F32), shade], axis=2)
    info = jnp.pad(info, ((0, 0), (0, 0), (0, LANES - 2)))
    rows_all[0], proj_rev, info, cot_both, table_rev, columns, conv_columns, out_full, *local = barrier(
        (rows_all[0], proj_rev, info, cot_both, table_rev, columns, conv_columns, out_full, *local)
    )
    rows_all = [rows_all[0]] + [lax.all_gather(rows, "seq") for rows in local[1:]]

    kept, heads = [], []
    for batch, (low, high) in enumerate(spans):
        if batch == len(spans) - 1:
            rows_all[batch], first, *heads = barrier((rows_all[batch], first, *heads))
            first = lax.all_gather(first, "seq")
        *normed, query, keys, values = project(rows_all[batch], gain_one, shift_one, columns, cuts)
        second, query = barrier((second, query))
        second = lax.all_gather(second, "seq")
        weights, inverse, mixed_heads, content_q, position_q = attend(
            query,
            bias_content.astype(F32).reshape(1, cols),
            bias_position.astype(F32).reshape(1, cols),
            keys,
            values,
            proj_rev,
            info[low:high],
            cuts,
        )
        kept.append((weights, inverse, mixed_heads, content_q, position_q, keys, values))
        heads.append(lax.all_to_all(mixed_heads, "seq", 0, 0, tiled=True))

    mixed_heads, conv_columns = barrier((mixed_heads, conv_columns))
    packed = compress(
        rows_all[0], conv_columns, conv_bias.astype(F32).reshape(1, cols), old, mem // 3
    )
    packed, *heads = barrier((packed, *heads))

    attended, middle, normed_two = [], [], []
    for (low, high), batch in zip(spans, heads):
        one, two, three = leave(batch, segment, low, out_full, out_shift, gain_two, shift_two)
        attended.append(one.reshape(-1, width))
        middle.append(two)
        normed_two.append(three.reshape(-1, width))
    both = jnp.concatenate(normed_two + [swap(rows) for rows in normed_two], axis=0)
    part, part_grad, late_one, unit_one = forward_back(both, cot_both, first, up_shift[0], ())
    late_one = lax.psum_scatter(
        late_one.reshape(-1, width), "seq", scatter_dimension=0, tiled=True
    )
    part, part_far, part_grad, grad_far, late_two, unit_two = forward_back(
        both, cot_both, second, up_shift[1], (part, part_grad)
    )
    grad_far = swap(grad_far)
    by_stream = lambda rows: rows.reshape(group, seg, width)
    middle_grad, branch_grad, head_grad, sums_two = [], [], [], 0.0
    for (low, high), batch in zip(spans, middle):
        one, two, three, four = enter(
            batch, by_stream(part_grad), by_stream(grad_far), cotangent, low, out_full, gain_two, parts
        )
        middle_grad.append(one)
        branch_grad.append(two.reshape(-1, width))
        three, part_grad = barrier((three, part_grad))
        head_grad.append(lax.all_to_all(three, "seq", 0, 0, tiled=True))
        sums_two = sums_two + four
    result = part + swap(part_far).astype(F32) + down_shift
    output = (jnp.concatenate(middle).reshape(own, width) + result).astype(BF16)
    output = output.reshape(group, seg, width)

    out_shift_grad, gain_two_grad, shift_two_grad, down_shift_grad = (
        sums_two[i].reshape(parts, cols) for i in range(4)
    )
    none = jnp.zeros((parts, 2 * cols), F32)
    unit_sums = jnp.stack(
        [unit_one.reshape(parts, unit_cols), unit_two.reshape(parts, unit_cols)], axis=1
    ).reshape(parts, 2 * unit_cols)
    small = jnp.stack(
        [
            jnp.concatenate([none, out_shift_grad, gain_two_grad], axis=1),
            jnp.concatenate([shift_two_grad, down_shift_grad, none], axis=1),
            jnp.concatenate(
                [jnp.where(core == 0, unit_sums, 0.0), jnp.where(core == 1, unit_sums, 0.0)], axis=1
            ),
        ],
        axis=1,
    )
    small = jnp.pad(small, ((0, 0), (0, 13), (0, 0)))
    weights, inverse, mixed_heads, content_q, position_q, keys, values = kept[0]
    out_grad = mm(jnp.concatenate(attended), jnp.concatenate(branch_grad), TN)
    out_grad = out_grad.astype(BF16).reshape(parts, cols, width)
    late_one, small, out_grad, late_two, output, head_grad = barrier(
        (late_one, small, out_grad, late_two, output, head_grad[0])
    )
    late_two = lax.psum_scatter(
        late_two.reshape(-1, width), "seq", scatter_dimension=0, tiled=True
    )
    late_one = exchange(late_one.reshape(layers, -1, width), "z")
    grads = []
    for head in range(cols // DH):
        grads.append(
            list(
                pull(
                    head, weights, inverse, mixed_heads, head_grad, content_q, position_q, keys,
                    values, proj_rev, cuts,
                )
            )
        )
        if head == 0:
            late_one, head_grad, grads[0][0] = barrier((late_one, head_grad, grads[0][0]))
            late_one = spread(add_up(late_one), "z")
    late_one, late_two, out_grad, grads[-1][0] = barrier(
        (late_one, late_two, out_grad, grads[-1][0])
    )
    late_two = exchange(late_two.reshape(layers, -1, width), "z")
    out_sent = lax.all_to_all(out_grad, "seq", 0, 0, tiled=True)
    seg_part, square_grads = settle(
        me, normed, grads, columns, table_rev, gain_one, shift_one, small, parts
    )
    late_one, late_two, out_sent, packed, square_grads = barrier(
        (late_one, late_two, out_sent, packed, square_grads)
    )
    packed = exchange(packed, "seq")
    summed = lax.all_to_all(square_grads, "seq", 0, 0, tiled=True)
    late_two = spread(add_up(late_two), "z")
    out_sent = jnp.sum(out_sent.astype(F32), axis=0).astype(BF16)
    late_one, late_two, packed, out_sent, summed, seg_part = barrier(
        (late_one, late_two, packed, out_sent, summed, seg_part)
    )
    squares = parts * (cols + 16)
    summed = jnp.concatenate([summed.reshape(squares, wide), out_sent.reshape(-1, wide)], axis=0)
    summed = lax.psum(summed, ("z", "core"))
    packed = jnp.stack(packed)
    new_compressed = jnp.concatenate(
        [lax.dynamic_index_in_dim(packed, p ^ me, 0, keepdims=False) for p in range(parts)], axis=2
    )
    seg_grad = lax.all_to_all(seg_part, "seq", 0, 0, tiled=True).astype(F32)
    seg_grad = jnp.sum(seg_grad, axis=0).reshape(own, width)
    unit_seg, rate_seg = standardise(segment.reshape(own, width).astype(F32))
    rows_grad = standardise_back(unit_seg, rate_seg, seg_grad, gain_one)
    segment_grad = jnp.concatenate(middle_grad, axis=0) + by_stream(rows_grad)

    halves = [
        in_order(pieces, "z").reshape(2, unit_cols, width) for pieces in (late_one, late_two)
    ]
    up_w, down_w = lay_out(core, halves, [swap(rows) for rows in halves], parts)
    down_w = down_w.reshape(4 * unit_cols, width)
    summed, output, segment_grad, new_compressed, up_w, down_w = barrier(
        (summed, output, segment_grad, new_compressed, up_w, down_w)
    )
    out_w = summed[squares:].reshape(cols, width).astype(F32)
    summed = summed[:squares].reshape(parts, cols + 16, wide)
    query_w, key_w, value_w, rel_w = lay_squares(summed, cols)
    small = jnp.sum(summed[:, cols : cols + 3].astype(F32), axis=0)
    piece = lambda row, i: small[row, cols * i : cols * (i + 1)]
    return (
        output,
        segment_grad,
        piece(0, 0),
        piece(0, 1),
        query_w,
        key_w,
        value_w,
        out_w,
        piece(0, 2),
        rel_w,
        piece(1, 2),
        piece(1, 3),
        piece(0, 3),
        piece(1, 0),
        up_w,
        small[2],
        down_w,
        piece(1, 1),
        new_compressed,
    )


def solution(mesh):
    dp = mesh.shape["dp"]
    cores = jax.sharding.Mesh(
        mesh.devices.reshape(dp // 2, 2, mesh.shape["seq"]), ("z", "core", "seq")
    )
    rows = P(("z", "core"), "seq", None)
    shard, matrix = P("seq"), P("seq", None)
    return jax.shard_map(
        body,
        mesh=cores,
        in_specs=(
            rows, rows, rows, P(("z", "core"), None), P(("z", "core")), shard, shard, matrix,
            matrix, matrix, matrix, shard, matrix, shard, shard, shard, shard, matrix, shard,
            matrix, shard, P(None, "seq", None), shard, rows,
        ),
        out_specs=(
            rows, rows, shard, shard, matrix, matrix, matrix, matrix, shard, matrix, shard,
            shard, shard, shard, matrix, shard, matrix, shard, rows,
        ),
        check_vma=False,
    )
```

```python
import functools
import math

import jax
import jax.numpy as jnp
from jax import lax
from jax.experimental import pallas as pl
from jax.experimental.pallas import tpu as pltpu
from jax.sharding import PartitionSpec as P

HEADS = 8
DH = 128
EPSILON = 1e-05
MASKED = -1e30
LANES = 128
BLOCK = 256
CHUNK = 16
VMEM_LIMIT = 60 * 2**20
SCALE = 1.0 / math.sqrt(DH)
LOG2E = 1.4426950408889634
BF16 = jnp.bfloat16
F32 = jnp.float32


def cost(microseconds):
    return pl.CostEstimate(flops=int(microseconds * 1.15e7), bytes_accessed=0, transcendentals=0)


def mm(left, right, dims):
    return lax.dot_general(left, right, (dims, ((), ())), preferred_element_type=F32)


NN = ((1,), (0,))
NT = ((1,), (1,))
TN = ((0,), (0,))


def lean_left(block, first_row, fill_columns):
    columns = block.shape[1] // LANES
    far = BLOCK - 1 - first_row
    whole, part = far // LANES, far % LANES
    turned = [
        pltpu.roll(
            block[:, LANES * t : LANES * (t + 1)], LANES - part, 1, stride=1, stride_axis=0
        )
        for t in range(columns)
    ]
    rows = lax.broadcasted_iota(jnp.int32, (block.shape[0], LANES), 0)
    lanes = lax.broadcasted_iota(jnp.int32, (block.shape[0], LANES), 1)
    near = lanes - rows < LANES - part
    out = []
    for t in range(fill_columns):
        a = turned[(t + whole) % columns]
        b = turned[(t + whole + 1) % columns]
        out.append(jnp.where(near, a, b))
    return jnp.concatenate(out, axis=1)


def lean_right(block, first_row):
    columns = block.shape[1] // LANES
    whole, part = first_row // LANES, first_row % LANES
    turned = [
        pltpu.roll(block[:, LANES * t : LANES * (t + 1)], part, 1, stride=1, stride_axis=0)
        for t in range(columns)
    ]
    rows = lax.broadcasted_iota(jnp.int32, (block.shape[0], LANES), 0)
    lanes = lax.broadcasted_iota(jnp.int32, (block.shape[0], LANES), 1)
    wrapped = lanes - rows < part
    out = []
    for t in range(columns):
        a = turned[(t - whole) % columns]
        b = turned[(t - whole - 1) % columns]
        out.append(jnp.where(wrapped, b, a))
    return jnp.concatenate(out, axis=1)


def flip_matrix(kind):
    rows = lax.broadcasted_iota(jnp.int32, (BLOCK, BLOCK), 0)
    lanes = lax.broadcasted_iota(jnp.int32, (BLOCK, BLOCK), 1)
    return (rows + lanes == BLOCK - 1).astype(F32).astype(kind)


def in_place_order(parts_ref, out_ref, cuts):
    parts = parts_ref.shape[0]
    low, base = 0, 0
    for size in cuts:
        for part in range(parts):
            out_ref[base + part * size : base + (part + 1) * size, :] = parts_ref[
                part, low : low + size, :
            ]
        low += size
        base += parts * size


def attend_kernel(
    cuts, q_ref, cb_ref, pb_ref, k_ref, v_ref, t_ref, info_ref,
    e_ref, inv_ref, o_ref, cq_ref, pq_ref,
    keys, values, raw, lean, mix, tops, sums,
):
    parts, seg, _ = q_ref.shape
    queries = parts * seg
    old = parts * (cuts[0] + cuts[1])
    in_place_order(k_ref, keys, cuts)
    in_place_order(v_ref, values, cuts)
    q = q_ref[...].reshape(queries, DH)
    content_q = (q + cb_ref[...]).astype(BF16)
    position_q = (q + pb_ref[...]).astype(BF16)
    cq_ref[...] = content_q.reshape(parts, seg, DH)
    pq_ref[...] = position_q.reshape(parts, seg, DH)
    for block in range(queries // BLOCK):
        row0 = block * BLOCK
        width = old + row0 + BLOCK
        skip = queries - BLOCK - row0
        raw[:, :width] = mm(content_q[row0 : row0 + BLOCK], keys[:width, :], NT)
        lean[:, :width] = mm(position_q[row0 : row0 + BLOCK], t_ref[skip : skip + width, :], NT)
        for chunk in range(BLOCK // CHUNK):
            r0 = chunk * CHUNK
            rows = slice(r0, r0 + CHUNK)
            turned = lean_left(lean[rows, :width], r0, width // LANES)
            score = raw[rows, :width] + turned
            start = info_ref[row0 + r0 : row0 + r0 + CHUNK, 0:1].astype(jnp.int32)
            shade = info_ref[row0 + r0 : row0 + r0 + CHUNK, 1:2]
            past = score[:, :old] + shade
            place = lax.broadcasted_iota(jnp.int32, (CHUNK, row0 + BLOCK), 1)
            own = lax.broadcasted_iota(jnp.int32, (CHUNK, row0 + BLOCK), 0) + (row0 + r0)
            now = jnp.where((place <= own) & (place >= start), score[:, old:], MASKED)
            raw[rows, :old] = past
            raw[rows, old:width] = now
            top = past[:, :LANES]
            for low in range(LANES, old, LANES):
                top = jnp.maximum(top, past[:, low : low + LANES])
            for low in range(0, row0 + BLOCK, LANES):
                top = jnp.maximum(top, now[:, low : low + LANES])
            tops[rows, :] = top
        top = jnp.max(tops[...], axis=1, keepdims=True)
        tops[...] = jnp.broadcast_to(top, (BLOCK, LANES))
        for chunk in range(BLOCK // CHUNK):
            r0 = chunk * CHUNK
            rows = slice(r0, r0 + CHUNK)
            top = tops[rows, :]
            total = jnp.zeros((CHUNK, LANES), F32)
            for low in range(0, width, LANES):
                weight = jnp.exp2((raw[rows, low : low + LANES] - top) * (SCALE * LOG2E))
                total = total + weight
                e_ref[row0 + r0 : row0 + r0 + CHUNK, low : low + LANES] = weight.astype(BF16)
            sums[rows, :] = total
        total = jnp.sum(sums[...], axis=1, keepdims=True)
        inv_ref[row0 : row0 + BLOCK, :] = jnp.broadcast_to(1.0 / total, (BLOCK, DH))
        mix[row0 : row0 + BLOCK, :] = mm(
            e_ref[row0 : row0 + BLOCK, :width], values[:width, :], NN
        )
    o_ref[...] = (mix[...] * inv_ref[...]).astype(BF16).reshape(parts, seg, DH)


def attend(query, content_shift, position_shift, keys, values, table_rev, info, cuts):
    parts, group, seg, cols = query.shape
    rows = keys.shape[2]
    queries, key_count, heads = parts * seg, parts * rows, cols // DH
    by_head = lambda size: pl.BlockSpec((parts, None, size, DH), lambda s, h: (0, s, 0, h))
    grid_spec = pl.GridSpec(
        grid=(group, heads),
        in_specs=[
            by_head(seg),
            pl.BlockSpec((1, DH), lambda s, h: (0, h)),
            pl.BlockSpec((1, DH), lambda s, h: (0, h)),
            by_head(rows),
            by_head(rows),
            pl.BlockSpec((key_count, DH), lambda s, h: (0, h)),
            pl.BlockSpec((None, queries, LANES), lambda s, h: (s, 0, 0)),
        ],
        out_specs=[
            pl.BlockSpec((None, None, queries, key_count), lambda s, h: (s, h, 0, 0)),
            pl.BlockSpec((None, None, queries, DH), lambda s, h: (s, h, 0, 0)),
            by_head(seg),
            by_head(seg),
            by_head(seg),
        ],
        scratch_shapes=[
            pltpu.VMEM((key_count, DH), BF16),
            pltpu.VMEM((key_count, DH), BF16),
            pltpu.VMEM((BLOCK, key_count), F32),
            pltpu.VMEM((BLOCK, key_count), F32),
            pltpu.VMEM((queries, DH), F32),
            pltpu.VMEM((BLOCK, LANES), F32),
            pltpu.VMEM((BLOCK, LANES), F32),
        ],
    )
    small = jax.ShapeDtypeStruct((parts, group, seg, cols), BF16)
    return pl.pallas_call(
        functools.partial(attend_kernel, cuts),
        grid_spec=grid_spec,
        out_shape=[
            jax.ShapeDtypeStruct((group, heads, queries, key_count), BF16),
            jax.ShapeDtypeStruct((group, heads, queries, DH), F32),
            small,
            small,
            small,
        ],
        compiler_params=pltpu.CompilerParams(
            dimension_semantics=("arbitrary", "arbitrary"), vmem_limit_bytes=VMEM_LIMIT
        ),
        cost_estimate=cost(40),
        name="attend",
    )(query, content_shift, position_shift, keys, values, table_rev, info)


def pull_kernel(
    cuts, e_ref, inv_ref, o_ref, g_ref, cq_ref, pq_ref, k_ref, v_ref, t_ref,
    dq_ref, dk_ref, dv_ref, ks_ref, vs_ref, dt_ref, sums_ref,
    keys, values, grad, prob, part, score, lean, key_sum, value_sum,
):
    stream = pl.program_id(1)
    parts, seg, _ = g_ref.shape
    queries = parts * seg
    old = parts * (cuts[0] + cuts[1])
    in_place_order(k_ref, keys, cuts)
    in_place_order(v_ref, values, cuts)
    grad[...] = (g_ref[...].reshape(queries, DH).astype(F32) * inv_ref[...]).astype(BF16)
    attended = o_ref[...].reshape(queries, DH)
    content_q = cq_ref[...].reshape(queries, DH)
    position_q = pq_ref[...].reshape(queries, DH)

    @pl.when(stream == 0)
    def _():
        dt_ref[...] = jnp.zeros_like(dt_ref)
        sums_ref[...] = jnp.zeros_like(sums_ref)

    key_sum[...] = jnp.zeros_like(key_sum)
    value_sum[...] = jnp.zeros_like(value_sum)
    content_total = jnp.zeros((1, DH), F32)
    position_total = jnp.zeros((1, DH), F32)
    query_total = jnp.zeros((1, DH), F32)
    flip = flip_matrix(BF16)
    turn = lambda rows: mm(flip, rows, NN).astype(BF16)
    for block in range(queries // BLOCK):
        row0 = block * BLOCK
        width = old + row0 + BLOCK
        skip = queries - BLOCK - row0
        rows = slice(row0, row0 + BLOCK)
        grad_back = turn(grad[rows, :])
        dots_back = jnp.sum(
            grad_back.astype(F32) * turn(attended[rows]).astype(F32), axis=1, keepdims=True
        )
        content_back = turn(content_q[rows])
        position_back = turn(position_q[rows])
        prob[:, :width] = mm(grad_back, values[:width, :], NT)
        both = mm(jnp.concatenate([flip, grad[rows, :].T], axis=0), e_ref[rows, :width], NN)
        part[:, :width] = both[:BLOCK]
        value_sum[:, :width] += both[BLOCK:]
        for chunk in range(BLOCK // CHUNK):
            r0 = chunk * CHUNK
            mean = dots_back[r0 : r0 + CHUNK, 0:1]
            change = part[r0 : r0 + CHUNK, :width] * (prob[r0 : r0 + CHUNK, :width] - mean)
            score[r0 : r0 + CHUNK, :width] = change.astype(BF16)
            lean[r0 : r0 + CHUNK, :width] = lean_right(change, r0).astype(BF16)
        content_grad = (mm(score[:, :width], keys[:width, :], NN) * SCALE).astype(BF16).astype(F32)
        position_grad = (
            (mm(lean[:, :width], t_ref[skip : skip + width, :], NN) * SCALE)
            .astype(BF16)
            .astype(F32)
        )
        query_grad = turn((content_grad + position_grad).astype(BF16))
        content_total += jnp.sum(content_grad, axis=0, keepdims=True)
        position_total += jnp.sum(position_grad, axis=0, keepdims=True)
        query_total += jnp.sum(query_grad.astype(F32), axis=0, keepdims=True)
        dq_ref[rows, :] = query_grad
        key_sum[:, :width] += mm(content_back, score[:, :width], TN)
        dt_ref[:, skip : skip + width] += mm(position_back, lean[:, :width], TN) * SCALE
    key_cols = (key_sum[...] * SCALE).astype(BF16)
    value_cols = value_sum[...].astype(BF16)
    dk_ref[...] = key_cols
    dv_ref[...] = value_cols
    ks_ref[...] = (key_sum[:, old:] * SCALE).T.astype(BF16)
    vs_ref[...] = value_sum[:, old:].T.astype(BF16)
    ones = jnp.ones((8, key_cols.shape[1]), BF16)
    key_total = mm(ones, key_cols, NT)[0:1]
    value_total = mm(ones, value_cols, NT)[0:1]
    sums_ref[...] += jnp.concatenate(
        [
            content_total,
            position_total,
            query_total,
            key_total,
            value_total,
            jnp.zeros((3, DH), F32),
        ],
        axis=0,
    )


def pull(head, weights, inverse, attended, out_grad, content_q, position_q, keys, values, table_rev, cuts):
    parts, group, seg, cols = out_grad.shape
    rows = keys.shape[2]
    queries, key_count = parts * seg, parts * rows
    by_head = lambda size: pl.BlockSpec((parts, None, size, DH), lambda h, s: (0, s, 0, head))
    by_row = lambda: pl.BlockSpec((None, queries, DH), lambda h, s: (s, 0, h))
    by_place = lambda: pl.BlockSpec((None, DH, key_count), lambda h, s: (s, h, 0))
    grid_spec = pl.GridSpec(
        grid=(1, group),
        in_specs=[
            pl.BlockSpec((None, None, queries, key_count), lambda h, s: (s, head, 0, 0)),
            pl.BlockSpec((None, None, queries, DH), lambda h, s: (s, head, 0, 0)),
            by_head(seg),
            by_head(seg),
            by_head(seg),
            by_head(seg),
            by_head(rows),
            by_head(rows),
            pl.BlockSpec((key_count, DH), lambda h, s: (0, head)),
        ],
        out_specs=[
            by_row(),
            by_place(),
            by_place(),
            by_row(),
            by_row(),
            pl.BlockSpec((None, DH, key_count), lambda h, s: (h, 0, 0)),
            pl.BlockSpec((None, 8, DH), lambda h, s: (h, 0, 0)),
        ],
        scratch_shapes=[
            pltpu.VMEM((key_count, DH), BF16),
            pltpu.VMEM((key_count, DH), BF16),
            pltpu.VMEM((queries, DH), BF16),
            pltpu.VMEM((BLOCK, key_count), F32),
            pltpu.VMEM((BLOCK, key_count), F32),
            pltpu.VMEM((BLOCK, key_count), BF16),
            pltpu.VMEM((BLOCK, key_count), BF16),
            pltpu.VMEM((DH, key_count), F32),
            pltpu.VMEM((DH, key_count), F32),
        ],
    )
    return pl.pallas_call(
        functools.partial(pull_kernel, cuts),
        grid_spec=grid_spec,
        out_shape=[
            jax.ShapeDtypeStruct((group, queries, DH), BF16),
            jax.ShapeDtypeStruct((group, DH, key_count), BF16),
            jax.ShapeDtypeStruct((group, DH, key_count), BF16),
            jax.ShapeDtypeStruct((group, queries, DH), BF16),
            jax.ShapeDtypeStruct((group, queries, DH), BF16),
            jax.ShapeDtypeStruct((1, DH, key_count), F32),
            jax.ShapeDtypeStruct((1, 8, DH), F32),
        ],
        compiler_params=pltpu.CompilerParams(
            dimension_semantics=("arbitrary", "arbitrary"), vmem_limit_bytes=VMEM_LIMIT
        ),
        cost_estimate=cost(39),
        name="pull",
    )(weights, inverse, attended, out_grad, content_q, position_q, keys, values, table_rev)


def project_kernel(
    cuts, rows_ref, gain_ref, shift_ref, w_ref, old_ref, mem_ref, seg_ref, q_ref, k_ref, v_ref, normed
):
    rows, width = rows_ref.shape
    cols = k_ref.shape[1]
    step = 32
    for low in range(0, rows, step):
        wide = rows_ref[low : low + step, :].astype(F32)
        centred = wide - jnp.mean(wide, axis=1, keepdims=True)
        rate = lax.rsqrt(jnp.mean(centred * centred, axis=1, keepdims=True) + EPSILON)
        normed[low : low + step, :] = (centred * rate * gain_ref[...] + shift_ref[...]).astype(BF16)
    cut = cuts[0] + cuts[1]
    old_ref[...] = normed[: cuts[0], :]
    mem_ref[...] = normed[cuts[0] : cut, :]
    seg_ref[...] = normed[cut:, :]
    q_ref[...] = mm(normed[cut:, :], w_ref[:, :cols], NN)
    k_ref[...] = mm(normed[...], w_ref[:, cols : 2 * cols], NN).astype(BF16)
    v_ref[...] = mm(normed[...], w_ref[:, 2 * cols : 3 * cols], NN).astype(BF16)


def project(rows_all, gain, shift, columns, cuts):
    parts, group, each, width = rows_all.shape
    cols = columns.shape[1] // 4
    block = lambda size, wide: pl.BlockSpec((None, None, size, wide), lambda p, s: (p, s, 0, 0))
    placed = lambda size: pl.BlockSpec((None, size, width), lambda p, s: (s, p, 0))
    whole = lambda *shape: pl.BlockSpec(shape, lambda p, s: (0,) * len(shape))
    shape = lambda size, kind: jax.ShapeDtypeStruct((parts, group, size, cols), kind)
    return pl.pallas_call(
        functools.partial(project_kernel, cuts),
        grid_spec=pl.GridSpec(
            grid=(parts, group),
            in_specs=[
                block(each, width),
                whole(1, width),
                whole(1, width),
                whole(width, 4 * cols),
            ],
            out_specs=[placed(size) for size in cuts]
            + [block(cuts[2], cols), block(each, cols), block(each, cols)],
            scratch_shapes=[pltpu.VMEM((each, width), BF16)],
        ),
        out_shape=[jax.ShapeDtypeStruct((group, parts * size, width), BF16) for size in cuts]
        + [shape(cuts[2], F32), shape(each, BF16), shape(each, BF16)],
        compiler_params=pltpu.CompilerParams(
            dimension_semantics=("arbitrary", "arbitrary"), vmem_limit_bytes=VMEM_LIMIT
        ),
        cost_estimate=cost(17),
        name="project",
    )(rows_all, gain, shift, columns)


def gelu_both(x):
    near = jnp.abs(x)
    t = 1.0 / (1.0 + (0.3275911 * math.sqrt(0.5)) * near)
    bell = jnp.exp2((x * x) * (-0.5 * LOG2E))
    tail = 0.5 * 1.061405429
    for factor in (-1.453152027, 1.421413741, -0.284496736, 0.254829592):
        tail = tail * t + 0.5 * factor
    tail = tail * t * bell
    below = jnp.where(x < 0.0, tail, 1.0 - tail)
    return x * below, below + x * bell * (1.0 / math.sqrt(2.0 * math.pi))


def forward_back_kernel(
    last, parts, pair, n_ref, c_ref, *rest,
):
    up_refs, down_refs, shift_ref = rest[:parts], rest[parts : parts + pair], rest[parts + pair]
    rest = rest[parts + pair + 1 :]
    if last:
        part_in, grad_in, part_out, part_far, grad_out, grad_far, late_ref, sums_ref = rest[:8]
        pre, slope, hidden, act, up_out, down_out, sems, part_ref, grad_ref = rest[8:]
    else:
        part_ref, grad_ref, late_ref, sums_ref = rest[:4]
        pre, slope, hidden, act, up_out, down_out, sems = rest[4:]
    tile = pl.program_id(0)
    tiles = pl.num_programs(0)
    cols, units = up_refs[0].shape
    unit_cols, width = down_refs[0].shape
    rows = n_ref.shape[0]
    slot = lax.rem(tile, 2)
    up_weight = jnp.concatenate([ref[...] for ref in up_refs], axis=0)
    down_weight = jnp.concatenate([ref[...] for ref in down_refs], axis=0)

    def copies(at, index):
        return (
            pltpu.make_async_copy(
                up_out.at[at],
                late_ref.at[:, pl.ds(0, cols), pl.ds(pl.multiple_of(index * units, units), units)],
                sems.at[at, 0],
            ),
            pltpu.make_async_copy(
                down_out.at[at],
                late_ref.at[pl.ds(index * pair, pair), pl.ds(cols, unit_cols), :],
                sems.at[at, 1],
            ),
        )

    @pl.when(tile == 0)
    def _():
        if last:
            part_ref[...] = part_in[...]
            grad_ref[...] = grad_in[...]
        else:
            part_ref[...] = jnp.zeros_like(part_ref)
            grad_ref[...] = jnp.zeros_like(grad_ref)

    pre[...] = mm(n_ref[...], up_weight, NN)
    slope[...] = mm(c_ref[...], down_weight, NT)
    for low in range(0, rows, 16):
        some = slice(low, low + 16)
        value, change = gelu_both(pre[some, :] + shift_ref[...])
        hidden[some, :] = value.astype(BF16)
        act[some, :] = (change * slope[some, :]).astype(BF16)
    part_ref[...] += mm(hidden[...], down_weight, NN)
    grad_ref[...] += mm(act[...], up_weight, NT)
    sums_ref[...] = jnp.sum(act[...].astype(F32), axis=0, keepdims=True)

    @pl.when(tile >= 2)
    def _():
        for copy in copies(slot, tile - 2):
            copy.wait()

    up_out[slot] = mm(n_ref[...], act[...], TN).astype(BF16).reshape(parts, cols, units)
    down_out[slot] = mm(hidden[...], c_ref[...], TN).astype(BF16).reshape(pair, unit_cols, width)
    for copy in copies(slot, tile):
        copy.start()

    @pl.when(tile == tiles - 1)
    def _():
        if last:
            part_out[...] = part_ref[: rows // 2, :]
            part_far[...] = part_ref[rows // 2 :, :].astype(BF16)
            grad_out[...] = grad_ref[: rows // 2, :]
            grad_far[...] = grad_ref[rows // 2 :, :].astype(BF16)
        for copy in (copies(1 - slot, tile - 1) if parts > pair else ()) + copies(slot, tile):
            copy.wait()


def forward_back(normed, cot, gathered, shift, carry):
    parts, _, width = gathered.shape
    rows = normed.shape[0]
    cols = width // parts
    unit_cols = shift.shape[1] // parts
    pair = 2
    units = pair * unit_cols
    last = len(carry) > 0
    one = pl.Buffered(1)
    whole = lambda *shape: pl.BlockSpec(shape, lambda t: (0,) * len(shape), pipeline_mode=one)
    up = lambda p: pl.BlockSpec((None, cols, units), lambda t: (p, 0, t))
    down = lambda i: pl.BlockSpec(
        (None, unit_cols, width), lambda t: (t * pair + i, cols // unit_cols, 0)
    )
    if last:
        sums = [((rows // 2, width), F32), ((rows // 2, width), BF16)] * 2
    else:
        sums = [((rows, width), F32)] * 2
    return pl.pallas_call(
        functools.partial(forward_back_kernel, last, parts, pair),
        grid_spec=pl.GridSpec(
            grid=(parts // pair,),
            in_specs=[
                whole(rows, width),
                whole(rows, width),
            ]
            + [up(p) for p in range(parts)]
            + [down(i) for i in range(pair)]
            + [pl.BlockSpec((1, units), lambda t: (0, t))]
            + [whole(rows, width) for _ in carry],
            out_specs=[whole(*shape) for shape, _ in sums]
            + [
                pl.BlockSpec(memory_space=pl.ANY),
                pl.BlockSpec((1, units), lambda t: (0, t)),
            ],
            scratch_shapes=[
                pltpu.VMEM((rows, units), F32),
                pltpu.VMEM((rows, units), F32),
                pltpu.VMEM((rows, units), BF16),
                pltpu.VMEM((rows, units), BF16),
                pltpu.VMEM((2, parts, cols, units), BF16),
                pltpu.VMEM((2, pair, unit_cols, width), BF16),
                pltpu.SemaphoreType.DMA((2, 2)),
            ]
            + [pltpu.VMEM((rows, width), F32) for _ in carry],
        ),
        out_shape=[jax.ShapeDtypeStruct(shape, kind) for shape, kind in sums]
        + [
            jax.ShapeDtypeStruct((parts, cols + unit_cols, width), BF16),
            jax.ShapeDtypeStruct((1, parts * unit_cols), F32),
        ],
        compiler_params=pltpu.CompilerParams(
            dimension_semantics=("arbitrary",), vmem_limit_bytes=VMEM_LIMIT
        ),
        cost_estimate=cost(29),
        name="forward_back",
    )(normed, cot, *[gathered] * (parts + pair), shift, *carry)


def leave_kernel(a_ref, s_ref, w_ref, shift_ref, gain_ref, bias_ref, flat_ref, m_ref, n_ref):
    parts = a_ref.shape[0]
    flat_ref[...] = jnp.concatenate([a_ref[part] for part in range(parts)], axis=1)
    m_ref[...] = s_ref[...].astype(F32) + (mm(flat_ref[...], w_ref[...], NN) + shift_ref[...])
    step = 16
    for low in range(0, m_ref.shape[0], step):
        unit, _ = standardise(m_ref[low : low + step, :])
        n_ref[low : low + step, :] = (unit * gain_ref[...] + bias_ref[...]).astype(BF16)


def leave(mixed_heads, segment, base, weight, shift, gain, bias):
    parts, group, seg, cols = mixed_heads.shape
    width = parts * cols
    rows = lambda: pl.BlockSpec((None, seg, width), lambda s: (s, 0, 0))
    vector = lambda: pl.BlockSpec((1, width), lambda s: (0, 0))
    shape = lambda kind: jax.ShapeDtypeStruct((group, seg, width), kind)
    return pl.pallas_call(
        leave_kernel,
        grid_spec=pl.GridSpec(
            grid=(group,),
            in_specs=[
                pl.BlockSpec((parts, None, seg, cols), lambda s: (0, s, 0, 0)),
                pl.BlockSpec((None, seg, width), lambda s: (s + base, 0, 0)),
                pl.BlockSpec((width, width), lambda s: (0, 0)),
                vector(),
                vector(),
                vector(),
            ],
            out_specs=[rows(), rows(), rows()],
        ),
        out_shape=[shape(BF16), shape(F32), shape(BF16)],
        compiler_params=pltpu.CompilerParams(vmem_limit_bytes=VMEM_LIMIT),
        cost_estimate=cost(6),
        name="leave",
    )(mixed_heads, segment, weight, shift, gain, bias)


def enter_kernel(
    m_ref, g_ref, far_ref, c_ref, w_ref, gain_ref, mg_ref, b_ref, a_ref, sums_ref
):
    @pl.when(pl.program_id(0) == 0)
    def _():
        sums_ref[...] = jnp.zeros_like(sums_ref)

    parts = a_ref.shape[0]
    rows, width = m_ref.shape
    step = 32
    total = [jnp.zeros((1, width), F32) for _ in range(4)]
    for low in range(0, rows, step):
        at = slice(low, low + step)
        unit, rate = standardise(m_ref[at, :])
        grad = g_ref[at, :] + far_ref[at, :].astype(F32)
        cot = c_ref[at, :].astype(F32)
        middle_grad = cot + standardise_back(unit, rate, grad, gain_ref[...])
        branch = middle_grad.astype(BF16)
        mg_ref[at, :] = middle_grad
        b_ref[at, :] = branch
        for i, value in enumerate((branch.astype(F32), grad * unit, grad, cot)):
            total[i] = total[i] + jnp.sum(value, axis=0, keepdims=True)
    sums_ref[...] += jnp.concatenate(total + [jnp.zeros((4, width), F32)], axis=0)
    for part in range(parts):
        low = part * a_ref.shape[2]
        weight = w_ref[low : low + a_ref.shape[2], :]
        a_ref[part] = mm(b_ref[...], weight, NT).astype(BF16)


def enter(middle, grad, far, cot, base, weight, gain, parts):
    group, seg, width = middle.shape
    cols = width // parts
    rows = lambda: pl.BlockSpec((None, seg, width), lambda s: (s, 0, 0))
    later = lambda: pl.BlockSpec((None, seg, width), lambda s: (s + base, 0, 0))
    shape = lambda kind: jax.ShapeDtypeStruct((group, seg, width), kind)
    return pl.pallas_call(
        enter_kernel,
        grid_spec=pl.GridSpec(
            grid=(group,),
            in_specs=[
                rows(),
                later(),
                later(),
                later(),
                pl.BlockSpec((width, width), lambda s: (0, 0)),
                pl.BlockSpec((1, width), lambda s: (0, 0)),
            ],
            out_specs=[
                rows(),
                rows(),
                pl.BlockSpec((parts, None, seg, cols), lambda s: (0, s, 0, 0)),
                pl.BlockSpec((8, width), lambda s: (0, 0)),
            ],
        ),
        out_shape=[
            shape(F32),
            shape(BF16),
            jax.ShapeDtypeStruct((parts, group, seg, cols), BF16),
            jax.ShapeDtypeStruct((8, width), F32),
        ],
        compiler_params=pltpu.CompilerParams(
            dimension_semantics=("arbitrary",), vmem_limit_bytes=VMEM_LIMIT
        ),
        cost_estimate=cost(7),
        name="enter",
    )(middle, grad, far, cot, weight, gain)


def compress_kernel(low, rows_ref, w_ref, shift_ref, out_ref, wide):
    count = out_ref.shape[0]
    cols = out_ref.shape[1]
    blocks = wide.shape[0]
    for at in range(blocks):
        wide[at, : 3 * count] = rows_ref[
            low : low + 3 * count, at * LANES : (at + 1) * LANES
        ].astype(F32)
    total = jnp.broadcast_to(shift_ref[...], (count, cols))
    for k in range(3):
        every = jnp.concatenate(
            [wide[at, pl.ds(k, count, stride=3), :] for at in range(blocks)], axis=1
        ).astype(BF16)
        total = total + mm(every, w_ref[:, k * cols : (k + 1) * cols], NN)
    out_ref[...] = total.astype(BF16)


def compress(rows_all, columns, shift, low, count):
    parts, group, each, width = rows_all.shape
    cols = columns.shape[1] // 3
    return pl.pallas_call(
        functools.partial(compress_kernel, low),
        grid_spec=pl.GridSpec(
            grid=(parts, group),
            in_specs=[
                pl.BlockSpec((None, None, each, width), lambda p, s: (p, s, 0, 0)),
                pl.BlockSpec((width, 3 * cols), lambda p, s: (0, 0)),
                pl.BlockSpec((1, cols), lambda p, s: (0, 0)),
            ],
            out_specs=pl.BlockSpec((None, None, count, cols), lambda p, s: (p, s, 0, 0)),
            scratch_shapes=[pltpu.VMEM((width // LANES, 3 * count + 8, LANES), F32)],
        ),
        out_shape=jax.ShapeDtypeStruct((parts, group, count, cols), BF16),
        compiler_params=pltpu.CompilerParams(
            dimension_semantics=("arbitrary", "arbitrary"), vmem_limit_bytes=VMEM_LIMIT
        ),
        cost_estimate=cost(6.5),
        name="compress",
    )(rows_all, columns, shift)


def lay_out_kernel(
    parts, unit_cols, core_ref, a_ref, b_ref, c_ref, d_ref, up_ref, down_ref
):
    flipped = core_ref[0] == 1
    for half, (mine_ref, far_ref) in enumerate(((a_ref, c_ref), (b_ref, d_ref))):
        mine, far = mine_ref[...].astype(F32), far_ref[...].astype(F32)
        for core, value in enumerate(
            (jnp.where(flipped, far, mine), jnp.where(flipped, mine, far))
        ):
            for part in range(parts):
                at = ((part * 2 + core) * 2 + half) * unit_cols
                up_ref[:, at : at + unit_cols] = value[
                    0, :, part * unit_cols : (part + 1) * unit_cols
                ]
            down_ref[2 * core + half] = value[1]


def lay_out(core, mine, far, parts):
    _, rows, width = mine[0].shape
    step = rows // 4 if rows % 64 == 0 else rows
    half = lambda: pl.BlockSpec((2, step, width), lambda r, *_: (0, r, 0))
    return pl.pallas_call(
        functools.partial(lay_out_kernel, parts, rows),
        grid_spec=pltpu.PrefetchScalarGridSpec(
            num_scalar_prefetch=1,
            grid=(rows // step,),
            in_specs=[half(), half(), half(), half()],
            out_specs=[
                pl.BlockSpec((step, 4 * width), lambda r, *_: (r, 0)),
                pl.BlockSpec((4, step, width), lambda r, *_: (0, r, 0)),
            ],
        ),
        out_shape=[
            jax.ShapeDtypeStruct((rows, 4 * width), F32),
            jax.ShapeDtypeStruct((4, rows, width), F32),
        ],
        compiler_params=pltpu.CompilerParams(vmem_limit_bytes=VMEM_LIMIT),
        cost_estimate=cost(4),
        name="lay_out",
    )(core.reshape(1), *mine, *far)


def lay_squares_kernel(in_ref, *out_refs):
    parts = in_ref.shape[0]
    cols = in_ref.shape[2] // len(out_refs)
    for at, out_ref in enumerate(out_refs):
        for part in range(parts):
            out_ref[:, part * cols : (part + 1) * cols] = in_ref[
                part, :, at * cols : (at + 1) * cols
            ].astype(F32)


def lay_squares(summed, rows):
    parts, _, wide = summed.shape
    width = parts * wide // 4
    step = rows // 2
    return pl.pallas_call(
        lay_squares_kernel,
        grid_spec=pl.GridSpec(
            grid=(2,),
            in_specs=[pl.BlockSpec((parts, step, wide), lambda i: (0, i, 0))],
            out_specs=[pl.BlockSpec((step, width), lambda i: (i, 0)) for _ in range(4)],
        ),
        out_shape=[jax.ShapeDtypeStruct((rows, width), F32) for _ in range(4)],
        compiler_params=pltpu.CompilerParams(vmem_limit_bytes=VMEM_LIMIT),
        cost_estimate=cost(2.5),
        name="lay_squares",
    )(summed)


def settle_kernel(heads, me_ref, old_ref, mem_ref, seg_ref, *rest):
    q_refs, k_refs, v_refs, ks_refs, vs_refs, dt_refs, sums_refs = (
        rest[i * heads : (i + 1) * heads] for i in range(7)
    )
    w_ref, table_ref, gain_ref, shift_ref, small_ref, part_ref, out_ref, total = rest[7 * heads :]
    stream = pl.program_id(0)
    parts, rows, wide = out_ref.shape
    cols = wide // 4
    width = parts * cols

    @pl.when(stream == 0)
    def _():
        total[...] = jnp.zeros_like(total)

    low = old_ref.shape[0]
    high = low + mem_ref.shape[0]
    pair = lambda first, last: [ref[:, first:last] for ref in (*k_refs, *v_refs)]
    total[...] += mm(
        jnp.concatenate([ref[...].T for ref in q_refs] + pair(high, high + seg_ref.shape[0]), axis=0),
        seg_ref[...],
        NN,
    )
    total[cols:, :] += mm(jnp.concatenate(pair(low, high), axis=0), mem_ref[...], NN)
    total[cols:, :] += mm(jnp.concatenate(pair(0, low), axis=0), old_ref[...], NN)
    three = jnp.concatenate([ref[...] for ref in (*q_refs, *ks_refs, *vs_refs)], axis=1)
    part = mm(three, w_ref[:, : 3 * cols], NT).astype(BF16)
    part_ref[...] = part.reshape(part_ref.shape)

    @pl.when(stream == pl.num_programs(0) - 1)
    def _():
        places = jnp.concatenate([ref[0].astype(BF16) for ref in dt_refs], axis=0)
        rel = mm(places, table_ref[...], NN)
        line = lambda row: jnp.concatenate(
            [ref[0, row : row + 1, :] for ref in sums_refs], axis=1
        )
        row_sums = jnp.concatenate([line(2), line(3), line(4)], axis=1)
        pieces, rest = [], row_sums
        for _ in range(3):
            pieces.append(rest.astype(BF16))
            rest = rest - pieces[-1].astype(F32)
        pieces = jnp.concatenate(pieces + [jnp.zeros((13, 3 * cols), BF16)], axis=0)
        shift_grad = jnp.sum(mm(pieces, w_ref[:, : 3 * cols], NT), axis=0, keepdims=True)
        weight = w_ref[:, : 3 * cols].astype(F32)
        along = jnp.sum(weight.T * total[...], axis=0, keepdims=True)
        gain_grad = (along - shift_ref[...] * shift_grad) / gain_ref[...]
        for at in range(parts):
            low, high = at * cols, (at + 1) * cols
            out_ref[at, :cols, : 3 * cols] = total[:, low:high].T.astype(BF16)
            out_ref[at, :cols, 3 * cols :] = rel[:, low:high].T.astype(BF16)
            mine = (me_ref[0] == at).astype(F32)
            none = jnp.zeros((1, 2 * cols), F32)
            first = jnp.concatenate([gain_grad[:, low:high], shift_grad[:, low:high], none], axis=1)
            second = jnp.concatenate([none, mine * line(0), mine * line(1)], axis=1)
            added = jnp.concatenate([first, second, jnp.zeros((14, wide), F32)], axis=0)
            out_ref[at, cols:, :] = (small_ref[at] + added).astype(BF16)


def settle(me, normed, grads, columns, table, gain, shift, small, parts):
    group, queries, width = normed[2].shape
    cols = width // parts
    wide = 4 * cols
    by_kind = list(zip(*grads))
    block = lambda array: pl.BlockSpec((None, *array.shape[1:]), lambda s, *_: (s, 0, 0))
    whole = lambda *shape: pl.BlockSpec(
        shape, lambda s, *_: (0,) * len(shape), pipeline_mode=pl.Buffered(1)
    )
    return pl.pallas_call(
        functools.partial(settle_kernel, len(grads)),
        grid_spec=pltpu.PrefetchScalarGridSpec(
            num_scalar_prefetch=1,
            grid=(group,),
            in_specs=[block(rows) for rows in normed]
            + [block(each) for kind in by_kind[:5] for each in kind]
            + [whole(*each.shape) for kind in by_kind[5:] for each in kind]
            + [
                whole(*columns.shape),
                whole(*table.shape),
                whole(1, width),
                whole(1, width),
                whole(*small.shape),
            ],
            out_specs=[
                pl.BlockSpec((parts, None, queries // parts, width), lambda s, *_: (0, s, 0, 0)),
                whole(parts, cols + 16, wide),
            ],
            scratch_shapes=[pltpu.VMEM((3 * cols, width), F32)],
        ),
        out_shape=[
            jax.ShapeDtypeStruct((parts, group, queries // parts, width), BF16),
            jax.ShapeDtypeStruct((parts, cols + 16, wide), BF16),
        ],
        compiler_params=pltpu.CompilerParams(
            dimension_semantics=("arbitrary",), vmem_limit_bytes=VMEM_LIMIT
        ),
        cost_estimate=cost(14),
        name="settle",
    )(
        me.reshape(1), *normed, *[each for kind in by_kind for each in kind], columns, table, gain, shift,
        small,
    )


def standardise(rows):
    mean = jnp.mean(rows, axis=-1, keepdims=True)
    centred = rows - mean
    rate = lax.rsqrt(jnp.mean(centred * centred, axis=-1, keepdims=True) + EPSILON)
    return centred * rate, rate


def standardise_back(unit, rate, grad, gain):
    scaled = grad * gain
    mean = jnp.mean(scaled, axis=-1, keepdims=True)
    along = jnp.mean(scaled * unit, axis=-1, keepdims=True)
    return rate * (scaled - mean - unit * along)


def sinusoid_reversed(rows, width):
    positions = (rows - 1 - jnp.arange(rows, dtype=jnp.int32)).astype(F32)[:, None]
    frequency = jnp.exp(
        jnp.arange(width // 2, dtype=F32) * (-2.0 * math.log(10000.0) / width)
    )
    angles = positions * frequency[None, :]
    return jnp.concatenate([jnp.sin(angles), jnp.cos(angles)], axis=1).astype(BF16)


def dot(left, right):
    return mm(left, right, NN)


def swap(value):
    return lax.ppermute(value, "core", [(0, 1), (1, 0)])


def exchange(blocks, name, axis=0):
    count = lax.axis_size(name)
    me = lax.axis_index(name)
    block = lambda at: lax.dynamic_index_in_dim(blocks, at, axis, keepdims=False)
    return [block(me)] + [
        lax.ppermute(block(me ^ apart), name, [(i, i ^ apart) for i in range(count)])
        for apart in range(1, count)
    ]


def collect(block, name):
    count = lax.axis_size(name)
    me = lax.axis_index(name)
    found = jnp.stack(
        [block]
        + [
            lax.ppermute(block, name, [(i, i ^ apart) for i in range(count)])
            for apart in range(1, count)
        ]
    )
    return jnp.stack(
        [lax.dynamic_index_in_dim(found, me ^ i, 0, keepdims=False) for i in range(count)]
    )


def add_up(arrays, kind=BF16):
    total = arrays[0].astype(F32)
    for array in arrays[1:]:
        total = total + array.astype(F32)
    return total.astype(kind)


def body(
    segment, memory, compressed, eob, reset, ln1_gain, ln1_bias, w_query, w_key, w_value,
    w_out, out_bias, w_rel, bias_content, bias_position, ln2_gain, ln2_bias, w_up, up_bias,
    w_down, down_bias, conv_weight, conv_bias, cotangent,
):
    parts = lax.axis_size("seq")
    layers = lax.axis_size("z")
    core = lax.axis_index("core")
    me = lax.axis_index("seq")
    group, seg, width = segment.shape
    mem, old = memory.shape[1], compressed.shape[1]
    cuts = (old, mem, seg)
    each = old + mem + seg
    keys_in_all = parts * each
    cols = width // parts
    wide = 4 * cols
    own = group * seg
    unit_cols = w_up.shape[1] // (4 * parts)
    barrier = lax.optimization_barrier

    def by_columns(matrices):
        count = matrices.shape[0]
        sent = matrices.reshape(count, cols, parts, cols).transpose(2, 1, 0, 3)
        return sent.reshape(parts, cols, count * cols)

    up_bias_own = lax.dynamic_slice_in_dim(up_bias, core * 2 * unit_cols, 2 * unit_cols, 0)
    vectors = jnp.concatenate(
        [ln1_gain, ln1_bias, out_bias, ln2_gain, ln2_bias, down_bias, up_bias_own]
    )
    vectors = jnp.pad(vectors.reshape(2, wide), ((0, 14), (0, 0)))
    half = cols // 2
    sent = by_columns(jnp.concatenate([jnp.stack([w_query, w_key, w_value, w_rel]), conv_weight]))
    sent = lax.dynamic_slice_in_dim(sent, core * half, half, 1)
    out_half = lax.dynamic_slice_in_dim(w_out, core * half, half, 0)
    sent = jnp.concatenate([sent, jnp.broadcast_to(out_half, (parts, half, width))], axis=2)
    vectors = jnp.pad(vectors, ((0, 0), (0, 3 * cols + width)))
    sent = jnp.concatenate([sent, jnp.broadcast_to(vectors, (parts, *vectors.shape))], axis=1)
    got = lax.all_to_all(sent, "seq", 0, 0, tiled=True)
    spans = [(0, group)]
    local = [
        jnp.concatenate([compressed[low:high], memory[low:high], segment[low:high]], axis=1)
        for low, high in spans
    ]
    rows_all = [lax.all_gather(local[0], "seq")]
    mine = got[:, :half]
    far = swap(mine)
    columns = jnp.stack(
        [jnp.where(core == 0, mine, far), jnp.where(core == 0, far, mine)], axis=1
    ).reshape(width, 7 * cols + width)
    columns, conv_columns, out_full = (
        columns[:, :wide],
        columns[:, wide : 7 * cols],
        columns[:, 7 * cols :],
    )
    vectors = got[:, half : half + 2, :wide].reshape(parts, 2 * wide).astype(F32)
    gain_one, shift_one, out_shift, gain_two, shift_two, down_shift = (
        vectors[:, cols * i : cols * (i + 1)].reshape(1, width) for i in range(6)
    )
    up_shift = vectors[:, 6 * cols :].reshape(parts, 2, unit_cols).transpose(1, 0, 2)
    up_shift = up_shift.reshape(2, 1, parts * unit_cols)
    up_quarters = lax.dynamic_slice_in_dim(
        w_up.reshape(cols, parts, 2, 2, unit_cols), core, 1, 2
    ).reshape(cols, parts, 2, unit_cols)
    up_quarters = [up_quarters[:, :, i].reshape(cols, width) for i in range(2)]
    down_half = lax.dynamic_slice_in_dim(w_down, core * 2 * unit_cols, 2 * unit_cols, 0)
    down_quarters = [down_half[unit_cols * i : unit_cols * (i + 1)] for i in range(2)]
    first = jnp.concatenate([up_quarters[0], down_quarters[0]], axis=0)
    second = jnp.concatenate([up_quarters[1], down_quarters[1]], axis=0)
    cot_own = cotangent.reshape(own, width)
    cot_both = jnp.concatenate([cot_own, swap(cot_own)], axis=0)

    table_rev = sinusoid_reversed(keys_in_all, width)
    proj_rev = dot(table_rev, columns[:, 3 * cols :]).astype(BF16)
    index = jnp.arange(eob.shape[1], dtype=jnp.int32)[None, :]
    opens = jnp.pad(eob, ((0, 0), (1, 0)))[:, :-1] == 1
    start = lax.cummax(jnp.where(opens, index, 0), axis=1)
    shade = jnp.where((start == 0) & (reset[:, None] == 0), 0.0, MASKED)
    info = jnp.stack([start.astype(F32), shade], axis=2)
    info = jnp.pad(info, ((0, 0), (0, 0), (0, LANES - 2)))
    rows_all[0], proj_rev, info, cot_both, table_rev, columns, conv_columns, out_full, *local = barrier(
        (rows_all[0], proj_rev, info, cot_both, table_rev, columns, conv_columns, out_full, *local)
    )
    rows_all = [rows_all[0]] + [lax.all_gather(rows, "seq") for rows in local[1:]]

    kept, heads = [], []
    for batch, (low, high) in enumerate(spans):
        if batch == len(spans) - 1:
            rows_all[batch], first, *heads = barrier((rows_all[batch], first, *heads))
            first = lax.all_gather(first, "seq")
        *normed, query, keys, values = project(rows_all[batch], gain_one, shift_one, columns, cuts)
        second, query = barrier((second, query))
        second = lax.all_gather(second, "seq")
        weights, inverse, mixed_heads, content_q, position_q = attend(
            query,
            bias_content.astype(F32).reshape(1, cols),
            bias_position.astype(F32).reshape(1, cols),
            keys,
            values,
            proj_rev,
            info[low:high],
            cuts,
        )
        kept.append((weights, inverse, mixed_heads, content_q, position_q, keys, values))
        heads.append(lax.all_to_all(mixed_heads, "seq", 0, 0, tiled=True))

    mixed_heads, conv_columns = barrier((mixed_heads, conv_columns))
    packed = compress(
        rows_all[0], conv_columns, conv_bias.astype(F32).reshape(1, cols), old, mem // 3
    )
    packed, *heads = barrier((packed, *heads))

    attended, middle, normed_two = [], [], []
    for (low, high), batch in zip(spans, heads):
        one, two, three = leave(batch, segment, low, out_full, out_shift, gain_two, shift_two)
        attended.append(one.reshape(-1, width))
        middle.append(two)
        normed_two.append(three.reshape(-1, width))
    both = jnp.concatenate(normed_two + [swap(rows) for rows in normed_two], axis=0)
    part, part_grad, late_one, unit_one = forward_back(both, cot_both, first, up_shift[0], ())
    late_one = lax.psum_scatter(
        late_one.reshape(-1, width), "seq", scatter_dimension=0, tiled=True
    )
    part, part_far, part_grad, grad_far, late_two, unit_two = forward_back(
        both, cot_both, second, up_shift[1], (part, part_grad)
    )
    grad_far = swap(grad_far)
    by_stream = lambda rows: rows.reshape(group, seg, width)
    middle_grad, branch_grad, head_grad, sums_two = [], [], [], 0.0
    for (low, high), batch in zip(spans, middle):
        one, two, three, four = enter(
            batch, by_stream(part_grad), by_stream(grad_far), cotangent, low, out_full, gain_two, parts
        )
        middle_grad.append(one)
        branch_grad.append(two.reshape(-1, width))
        three, part_grad = barrier((three, part_grad))
        head_grad.append(lax.all_to_all(three, "seq", 0, 0, tiled=True))
        sums_two = sums_two + four
    result = part + swap(part_far).astype(F32) + down_shift
    output = (jnp.concatenate(middle).reshape(own, width) + result).astype(BF16)
    output = output.reshape(group, seg, width)

    out_shift_grad, gain_two_grad, shift_two_grad, down_shift_grad = (
        sums_two[i].reshape(parts, cols) for i in range(4)
    )
    none = jnp.zeros((parts, 2 * cols), F32)
    unit_sums = jnp.stack(
        [unit_one.reshape(parts, unit_cols), unit_two.reshape(parts, unit_cols)], axis=1
    ).reshape(parts, 2 * unit_cols)
    small = jnp.stack(
        [
            jnp.concatenate([none, out_shift_grad, gain_two_grad], axis=1),
            jnp.concatenate([shift_two_grad, down_shift_grad, none], axis=1),
            jnp.concatenate(
                [jnp.where(core == 0, unit_sums, 0.0), jnp.where(core == 1, unit_sums, 0.0)], axis=1
            ),
        ],
        axis=1,
    )
    small = jnp.pad(small, ((0, 0), (0, 13), (0, 0)))
    weights, inverse, mixed_heads, content_q, position_q, keys, values = kept[0]
    out_grad = mm(jnp.concatenate(attended), jnp.concatenate(branch_grad), TN)
    out_grad = out_grad.astype(BF16).reshape(parts, cols, width)
    packed = exchange(packed, "seq")
    late_one, small, out_grad, late_two, output, packed, head_grad = barrier(
        (late_one, small, out_grad, late_two, output, packed, head_grad[0])
    )
    late_two = lax.psum_scatter(
        late_two.reshape(-1, width), "seq", scatter_dimension=0, tiled=True
    )
    late_one = exchange(late_one.reshape(layers, -1, width), "z")
    grads = []
    for head in range(cols // DH):
        grads.append(
            list(
                pull(
                    head, weights, inverse, mixed_heads, head_grad, content_q, position_q, keys,
                    values, proj_rev, cuts,
                )
            )
        )
        if head == 0:
            late_one, head_grad, grads[0][0] = barrier((late_one, head_grad, grads[0][0]))
            late_one = collect(add_up(late_one), "z")
    late_one, late_two, out_grad, grads[-1][0] = barrier(
        (late_one, late_two, out_grad, grads[-1][0])
    )
    late_two = exchange(late_two.reshape(layers, -1, width), "z")
    out_sent = lax.all_to_all(out_grad, "seq", 0, 0, tiled=True)
    seg_part, square_grads = settle(
        me, normed, grads, columns, table_rev, gain_one, shift_one, small, parts
    )
    late_two, out_sent, square_grads = barrier((late_two, out_sent, square_grads))
    summed = lax.all_to_all(square_grads, "seq", 0, 0, tiled=True)
    late_two = collect(add_up(late_two), "z")
    out_sent = jnp.sum(out_sent.astype(F32), axis=0).astype(BF16)
    late_two, out_sent, summed, seg_part = barrier((late_two, out_sent, summed, seg_part))
    squares = parts * (cols + 16)
    summed = jnp.concatenate([summed.reshape(squares, wide), out_sent.reshape(-1, wide)], axis=0)
    summed = lax.psum(summed, ("z", "core"))
    packed = jnp.stack(packed)
    new_compressed = jnp.concatenate(
        [lax.dynamic_index_in_dim(packed, p ^ me, 0, keepdims=False) for p in range(parts)], axis=2
    )
    seg_grad = lax.all_to_all(seg_part, "seq", 0, 0, tiled=True).astype(F32)
    seg_grad = jnp.sum(seg_grad, axis=0).reshape(own, width)
    unit_seg, rate_seg = standardise(segment.reshape(own, width).astype(F32))
    rows_grad = standardise_back(unit_seg, rate_seg, seg_grad, gain_one)
    segment_grad = jnp.concatenate(middle_grad, axis=0) + by_stream(rows_grad)

    halves = [late_one.reshape(2, unit_cols, width), late_two.reshape(2, unit_cols, width)]
    up_w, down_w = lay_out(core, halves, [swap(rows) for rows in halves], parts)
    down_w = down_w.reshape(4 * unit_cols, width)
    summed, output, segment_grad, new_compressed, up_w, down_w = barrier(
        (summed, output, segment_grad, new_compressed, up_w, down_w)
    )
    out_w = summed[squares:].reshape(cols, width).astype(F32)
    summed = summed[:squares].reshape(parts, cols + 16, wide)
    query_w, key_w, value_w, rel_w = lay_squares(summed, cols)
    small = jnp.sum(summed[:, cols : cols + 3].astype(F32), axis=0)
    piece = lambda row, i: small[row, cols * i : cols * (i + 1)]
    return (
        output,
        segment_grad,
        piece(0, 0),
        piece(0, 1),
        query_w,
        key_w,
        value_w,
        out_w,
        piece(0, 2),
        rel_w,
        piece(1, 2),
        piece(1, 3),
        piece(0, 3),
        piece(1, 0),
        up_w,
        small[2],
        down_w,
        piece(1, 1),
        new_compressed,
    )


def solution(mesh):
    dp = mesh.shape["dp"]
    cores = jax.sharding.Mesh(
        mesh.devices.reshape(dp // 2, 2, mesh.shape["seq"]), ("z", "core", "seq")
    )
    rows = P(("z", "core"), "seq", None)
    shard, matrix = P("seq"), P("seq", None)
    return jax.shard_map(
        body,
        mesh=cores,
        in_specs=(
            rows, rows, rows, P(("z", "core"), None), P(("z", "core")), shard, shard, matrix,
            matrix, matrix, matrix, shard, matrix, shard, shard, shard, shard, matrix, shard,
            matrix, shard, P(None, "seq", None), shard, rows,
        ),
        out_specs=(
            rows, rows, shard, shard, matrix, matrix, matrix, matrix, shard, matrix, shard,
            shard, shard, shard, matrix, shard, matrix, shard, rows,
        ),
        check_vma=False,
    )
```
